32 devices in a mesh: dp: 16 (over z, y, x), mp: 2 (over core).
Axes of the slice: x: 2, y: 2, z: 4, core: 2. Of those that a mesh axis runs over, the one named last changes fastest.
Arguments:
- hidden_in: float32 [6144, 960], P(('dp', 'mp')), may hold values from -6 to 6
- sel_one: int32 [32, 192], P(('dp', 'mp')), may hold values from 0 to 192, as said below
- sel_two: int32 [32, 160], P(('dp', 'mp')), may hold values from 0 to 192, as said below
- sel_three: int32 [32, 128], P(('dp', 'mp')), may hold values from 0 to 192, as said below
- segment_ids: int32 [32, 192], P(('dp', 'mp')), may hold values from 0 to 5, never falling along the last dimension, each value on 1 to 96 neighbouring positions
- pad_mask: int32 [32, 192], P(('dp', 'mp')), may hold values from 0 to 1, as said below
- qkv_weight: bfloat16 [960, 1600], replicated, may hold values from -0.1875 to 0.1875
- out_weight: bfloat16 [960, 960], replicated, may hold values from -0.375 to 0.375
- gate_weight: bfloat16 [960, 2560], P(None, 'mp'), may hold values from -0.1875 to 0.1875
- up_weight: bfloat16 [960, 2560], P(None, 'mp'), may hold values from -0.1875 to 0.1875
- down_weight: bfloat16 [960, 2560], P(None, 'mp'), may hold values from -0.125 to 0.125
- norm_one: float32 [960], replicated, may hold values from 0.5 to 1.5
- norm_two: float32 [960], replicated, may hold values from 0.5 to 1.5
- router_weight: float32 [3, 960], replicated, may hold values from -0.125 to 0.125
- d_hidden: float32 [6144, 960], P(('dp', 'mp')), may hold values from -6 to 6
Outputs:
- hidden_out: float32 [6144, 960], P(('dp', 'mp'))
- d_input: float32 [6144, 960], P(('dp', 'mp'))
- attn_weight_grads: float32 [2457600], P(('dp', 'mp'))
- ffn_weight_grads: float32 [2, 3686400], P('mp', 'dp')
- norm_one_grad: float32 [960], replicated
- norm_two_grad: float32 [960], replicated
- router_grad: float32 [3, 960], replicated
The draws below stay inside these ranges and needn't reach their ends.
Inputs may be any that keep to these rules, and one draw needn't show every extreme that they name: `sel_one`: row s lists the positions active in recursion one for sequence s in increasing order, followed by 192 in every empty entry. Some row has no empty entry. Over the sequences placed on one index of mp, the active counts add up to 96 times the devices of dp. `sel_two`: as for sel_one, for recursion two, with 80 in place of 96. `sel_three`: as for sel_one, for recursion three, with 64 in place of 96. `pad_mask`: each row is ones followed by zeros. `segment_ids`: ids never fall along a row.
All inputs are finite; a program needn't handle non-finite values.
Results may differ from the reference program's by a relative error of at most 0.025.
Values may be sent and summed in bfloat16 or wider, within the bound.
No kernel may reach another device: no remote copies, remote signals or barrier semaphores. Data moves between devices by JAX's collectives and lax.ppermute only.
A program may use at most 256 MiB of HBM per device.

```python
import math
import jax
import jax.numpy as jnp
import numpy as np
from jax import lax

MODEL_WIDTH = 960
HEADS = 15
KV_HEADS = 5
HEAD_DIM = 64
FF = 2560
RECURSIONS = 3
SEQ = 192
QKV = 1600
MEAN_ONE = 96
MEAN_TWO = 80
MEAN_THREE = 64
MOST_ONE = 192
PEAK_SECOND_LOOP = 160
MOST_THREE = 128
SEQS = 32
TOKENS = 6144
N_DP = 16
N_MP = 2


def device_counts(key, most_rows, mean_rows):
    heavy_count = N_DP // 4
    light_count = N_DP - heavy_count
    spare_rows = N_DP * mean_rows - heavy_count * most_rows
    base_rows = spare_rows // light_count
    extra_rows = spare_rows % light_count
    columns = []
    for member in range(N_MP):
        member_key = jax.random.fold_in(key, member)
        ranking = jax.random.permutation(jax.random.fold_in(member_key, 1), N_DP)
        shifts = jax.random.randint(jax.random.fold_in(member_key, 2), (light_count // 2,), 0, base_rows // 2 + 1)
        light_rank = jnp.maximum(ranking - heavy_count, 0)
        row_count = base_rows + (light_rank < extra_rows).astype(jnp.int32)
        pair_shift = jnp.take(shifts, light_rank // 2)
        row_count = row_count + jnp.where(light_rank % 2 == 0, pair_shift, -pair_shift)
        columns.append(jnp.where(ranking < heavy_count, most_rows, row_count))
    return jnp.stack(columns, axis=1).reshape(-1).astype(jnp.int32)


def selection(key, most_rows, mean_rows):
    counts = device_counts(jax.random.fold_in(key, 5), most_rows, mean_rows)
    row_keys = jax.random.split(jax.random.fold_in(key, 6), N_DP * N_MP)
    chosen = jax.vmap(lambda row_key: jax.random.permutation(row_key, SEQ)[:most_rows])(row_keys)
    ordinal = jnp.arange(most_rows, dtype=jnp.int32)
    chosen = jnp.where(ordinal[None, :] < counts[:, None], chosen, SEQ)
    return jnp.sort(chosen, axis=1).astype(jnp.int32)


def draw_sel_one(key, part):
    key = jax.random.fold_in(key, 11)
    return selection(key, MOST_ONE, MEAN_ONE)


def draw_sel_two(key, part):
    key = jax.random.fold_in(key, 12)
    return selection(key, PEAK_SECOND_LOOP, MEAN_TWO)


def draw_sel_three(key, part):
    key = jax.random.fold_in(key, 13)
    return selection(key, MOST_THREE, MEAN_THREE)


def draw_pad_mask(key, part):
    key = jax.random.fold_in(key, 14)
    trims = jax.random.randint(key, (SEQS,), 0, SEQ // 8 + 1)
    positions = jnp.arange(SEQ, dtype=jnp.int32)
    return (positions[None, :] < SEQ - trims[:, None]).astype(jnp.int32)


def block_levels(own_key, dims, cuts, smallest, high):
    def one(dim, shards_of):
        draws = jax.random.uniform(jax.random.fold_in(jax.random.fold_in(own_key, 6), dim), (shards_of,), jnp.float32, smallest / len(cuts), high / len(cuts))
        return jnp.repeat(jnp.exp(draws), dims[dim] // shards_of).reshape((-1,) + (1,) * (len(dims) - dim - 1))

    level = one(*cuts[0])
    for cut in cuts[1:]:
        level = level * one(*cut)
    return level


def split_up(amount, total, bound, skew):
    weights = [(1 << 20) // math.isqrt(rank ** skew) + 1 for rank in range(2, amount + 1)]
    surplus, given = total - bound - (amount - 1), [1] * (amount - 1)
    while surplus > 0:
        movable = [i for i in range(amount - 1) if given[i] < bound]
        pool, left = sum([weights[i] for i in movable]), surplus
        for i in movable:
            extra = min(bound - given[i], max(1, left * weights[i] // pool), surplus)
            given[i] = given[i] + extra
            surplus = surplus - extra
    return np.array([bound] + given)


def ragged_sizes(key, count, total, reach, lean):
    if count == 2:
        one = jax.random.randint(key, (), max(1, total - reach), min(reach, total - 1) + 1)
        return jnp.stack([one, total - one])
    tallies = jnp.asarray(split_up(count, total, reach, lean), jnp.int32)
    pairs = (count - 1) // 2
    giver, sink = tallies[1:1 + 2 * pairs:2], tallies[2:2 + 2 * pairs:2]
    margin = jnp.minimum(giver - 1, reach - sink)
    shifted = jax.random.randint(jax.random.fold_in(key, 1), (pairs,), 0, 1 << 20) % (margin + 1)
    tallies = tallies.at[1:1 + 2 * pairs:2].set(giver - shifted).at[2:2 + 2 * pairs:2].set(sink + shifted)
    return tallies[jax.random.permutation(jax.random.fold_in(key, 2), count)]


def gaussian(rng, extent, width, reach, pieces=(), held_as=jnp.bfloat16):
    array = width * jax.random.normal(rng, extent, jnp.float32)
    if pieces:
        array = array * block_levels(rng, extent, pieces, -0.22, 0.18)
    return jnp.clip(array, -reach, reach).astype(held_as)


def setup_inputs(seed: int = 0) -> dict:
    key_of = jax.random.split(jax.random.key(seed), 16)
    return {
        "hidden_in": gaussian(key_of[0], (TOKENS, MODEL_WIDTH), 1.0, 6.0, ((0, 32),), jnp.float32),
        "sel_one": draw_sel_one(jax.random.fold_in(key_of[15], 71), 0),
        "sel_two": draw_sel_two(jax.random.fold_in(key_of[15], 71), 0),
        "sel_three": draw_sel_three(jax.random.fold_in(key_of[15], 71), 0),
        "segment_ids": jax.vmap(lambda own: jnp.searchsorted(jnp.cumsum(ragged_sizes(own, 6, SEQ, SEQ // 2, 2)), jnp.arange(SEQ), side="right"))(jax.random.split(key_of[4], SEQS)).reshape((SEQS, SEQ)).astype(jnp.int32),
        "pad_mask": draw_pad_mask(jax.random.fold_in(key_of[15], 71), 0),
        "qkv_weight": gaussian(key_of[6], (MODEL_WIDTH, QKV), MODEL_WIDTH ** -0.5, 0.1875),
        "out_weight": gaussian(key_of[7], (MODEL_WIDTH, MODEL_WIDTH), (MODEL_WIDTH // 4) ** -0.5, 0.375),
        "gate_weight": gaussian(key_of[8], (MODEL_WIDTH, FF), MODEL_WIDTH ** -0.5, 0.1875, ((1, 2),)),
        "up_weight": gaussian(key_of[9], (MODEL_WIDTH, FF), MODEL_WIDTH ** -0.5, 0.1875, ((1, 2),)),
        "down_weight": gaussian(key_of[10], (MODEL_WIDTH, FF), FF ** -0.5, 0.125, ((1, 2),)),
        "norm_one": jnp.clip(1.0 + 0.1 * jax.random.normal(key_of[11], (MODEL_WIDTH,), jnp.float32), 0.5, 1.5),
        "norm_two": jnp.clip(1.0 + 0.1 * jax.random.normal(key_of[12], (MODEL_WIDTH,), jnp.float32), 0.5, 1.5),
        "router_weight": gaussian(key_of[13], (RECURSIONS, MODEL_WIDTH), (2 * MODEL_WIDTH) ** -0.5, 0.125, (), jnp.float32),
        "d_hidden": gaussian(key_of[14], (TOKENS, MODEL_WIDTH), 1.0, 6.0, ((0, 32),), jnp.float32),
    }


@jax.custom_vjp
def low(v):
    return lax.optimization_barrier(v.astype(jnp.bfloat16)).astype(jnp.float32)

@jax.custom_vjp
def low_back(v):
    return v

def bottom_retained(v):
    return (low(v), None)

def low_pass(kept, grad):
    return (grad,)

def back_keep(v):
    return (v, None)

def back_low(kept, grad):
    return (low(grad),)
low.defvjp(bottom_retained, low_pass)
low_back.defvjp(back_keep, back_low)

def precise(left, right):
    return jnp.dot(left, right, precision=lax.Precision.HIGHEST)

def rms_norm(values_in, gain_vec):
    return values_in * lax.rsqrt(lax.optimization_barrier(jnp.mean(values_in * values_in, axis=-1, keepdims=True)) + 1e-05) * gain_vec

def rotary(values_in, positions):
    half_dim = values_in.shape[-1] // 2
    frequency = 100000.0 ** (-2.0 * jnp.arange(half_dim, dtype=jnp.float32) / values_in.shape[-1])
    angles = positions[:, None, None] * frequency
    cosine = jnp.cos(angles)
    sine_part = jnp.sin(angles)
    first_half = values_in[..., :half_dim]
    second_half = values_in[..., half_dim:]
    return jnp.concatenate([first_half * cosine - second_half * sine_part, second_half * cosine + first_half * sine_part], axis=-1)

def attention_mask(clipped, is_valid, segment, padding):
    seg_rows = jnp.take(segment, clipped)
    pad_rows = jnp.take(padding, clipped)
    earlier = clipped[None, :] <= clipped[:, None]
    same_doc = seg_rows[None, :] == seg_rows[:, None]
    usable = is_valid & (pad_rows == 1)
    diagonal = jnp.eye(clipped.shape[0], dtype=bool)
    return earlier & same_doc & (usable[None, :] | diagonal)

def recursion_step(states, select, recursion_index, segment, padding, params):
    qkv_matrix, out_matrix, gate_matrix, up_matrix, down_matrix, gain_one, gain_two, router_matrix = params
    active_tokens = select.shape[0]
    kv_cols = KV_HEADS * HEAD_DIM
    is_valid = select < SEQ
    clipped = jnp.minimum(select, SEQ - 1)
    active_in = states[clipped]
    router_gate = jax.nn.sigmoid(precise(active_in, router_matrix[recursion_index]))
    normed_one = low(rms_norm(active_in, gain_one))
    projected = low_back(precise(normed_one, qkv_matrix))
    positions = clipped.astype(jnp.float32)
    question_vectors = low(rotary(projected[:, :MODEL_WIDTH].reshape(active_tokens, HEADS, HEAD_DIM), positions))
    question_vectors = question_vectors.reshape(active_tokens, KV_HEADS, HEADS // KV_HEADS, HEAD_DIM)
    routed_key_rows = low(rotary(projected[:, MODEL_WIDTH:MODEL_WIDTH + kv_cols].reshape(active_tokens, KV_HEADS, HEAD_DIM), positions))
    routed_value_rows = low(projected[:, MODEL_WIDTH + kv_cols:].reshape(active_tokens, KV_HEADS, HEAD_DIM))
    attention_scores = jnp.einsum('rwlq,ywq->wlry', question_vectors, routed_key_rows, precision=lax.Precision.HIGHEST)
    attention_scores = low_back(attention_scores * (1.0 / math.sqrt(HEAD_DIM)))
    masked = jnp.where(attention_mask(clipped, is_valid, segment, padding), attention_scores, -1e+30)
    row_max = lax.optimization_barrier(jnp.max(masked, axis=-1, keepdims=True))
    exponent = jnp.exp(masked - row_max)
    attend_tokens = low(exponent / lax.optimization_barrier(jnp.sum(exponent, axis=-1, keepdims=True)))
    heads_mixed_output = jnp.einsum('xzpm,mxe->pxze', attend_tokens, routed_value_rows, precision=lax.Precision.HIGHEST).reshape(active_tokens, MODEL_WIDTH)
    heads_mixed_output = low(low_back(heads_mixed_output))
    attn_out = low_back(precise(heads_mixed_output, out_matrix))
    normed_two = low(low_back(rms_norm(active_in + attn_out, gain_two)))
    gate_proj = low_back(precise(normed_two, gate_matrix))
    up_proj = low_back(precise(normed_two, up_matrix))
    hidden = low(jax.nn.silu(gate_proj) * up_proj)
    ffn_out = low(low_back(precise(hidden, down_matrix.T)))
    new_rows = active_in + router_gate[:, None] * (attn_out + ffn_out)
    return states.at[select].set(new_rows, mode='drop')

def reference(hidden_in, sel_one, sel_two, sel_three, segment_ids, pad_mask, qkv_weight, out_weight, gate_weight, up_weight, down_weight, norm_one, norm_two, router_weight, d_hidden):
    real_numbers = tuple((argument.astype(jnp.float32) for argument in (hidden_in, qkv_weight, out_weight, gate_weight, up_weight, down_weight, norm_one, norm_two, router_weight)))

    def grouped(tensor):
        return tensor.reshape((-1, 8) + tensor.shape[1:])

    def forward(states, *params):

        def one_sequence(seq_states, chosen_one, chosen_two, chosen_three, segment, padding):
            for recursion_index, select in enumerate((chosen_one, chosen_two, chosen_three)):
                seq_states = recursion_step(seq_states, select, recursion_index, segment, padding, params)
            return seq_states
        batched = jax.checkpoint(jax.vmap(one_sequence))
        result = lax.map(lambda bundle: batched(*bundle), (grouped(states.reshape(-1, SEQ, MODEL_WIDTH)), grouped(sel_one), grouped(sel_two), grouped(sel_three), grouped(segment_ids), grouped(pad_mask)))
        return result.reshape(-1, MODEL_WIDTH)
    outputs, pullback = jax.vjp(forward, *real_numbers)
    gradients = pullback(d_hidden.astype(jnp.float32))
    grad_states, grad_qkv, grad_out, grad_gate, lift_matrix_slope, grad_down, grad_one, grad_two, grad_router = gradients
    attn_flat = jnp.concatenate([grad_qkv.reshape(-1), grad_out.reshape(-1)])
    half_units = FF // N_MP

    def halves(matrix):
        return matrix.reshape(MODEL_WIDTH, N_MP, half_units).transpose(1, 0, 2).reshape(N_MP, MODEL_WIDTH * half_units)
    ffn_flat = jnp.concatenate([halves(grad_gate), halves(lift_matrix_slope), halves(grad_down)], axis=1)
    return (outputs, grad_states, attn_flat, ffn_flat, grad_one, grad_two, grad_router)
```

```python
import math

import jax
import jax.numpy as jnp
import numpy as np
from jax import lax
from jax.sharding import PartitionSpec as P

HEADS = 15
KV_HEADS = 5
HEAD_DIM = 64
RECURSIONS = 3
GROUPS = HEADS // KV_HEADS
EPS = 1e-05
BF = jnp.bfloat16
F32 = jnp.float32


def rotary_tables(seq_len):
    half = HEAD_DIM // 2
    frequency = np.float32(100000.0) ** (
        np.float32(-2.0) * np.arange(half, dtype=np.float32) / np.float32(HEAD_DIM)
    )
    angles = np.arange(seq_len, dtype=np.float32)[:, None] * frequency.astype(np.float32)
    return jnp.asarray(np.cos(angles), F32), jnp.asarray(np.sin(angles), F32)


def turn(values_in, cosine, sine):
    half = HEAD_DIM // 2
    first, second = values_in[..., :half], values_in[..., half:]
    c, s = cosine[:, None, :], sine[:, None, :]
    return jnp.concatenate([first * c - second * s, second * c + first * s], axis=-1)


def contract_rows(left, right):
    return lax.dot_general(left, right, (((0,), (0,)), ((), ())), preferred_element_type=F32)


def contract_last(left, right):
    return lax.dot_general(left, right, (((1,), (1,)), ((), ())), preferred_element_type=F32)


def plain(left, right):
    return jnp.dot(left, right, preferred_element_type=F32)


def inverse_rms(rows):
    return lax.rsqrt(jnp.mean(rows * rows, axis=-1, keepdims=True) + EPS)


def norm_back(rows, gain, d_out):
    inv = inverse_rms(rows)
    scaled = d_out * gain
    inner = jnp.mean(scaled * rows, axis=-1, keepdims=True)
    d_rows = inv * scaled - rows * (inv * inv * inv * inner)
    return d_rows, jnp.sum(d_out * rows * inv, axis=0)


def swap_dp(values_in, bit, n_dp):
    return lax.ppermute(values_in, "dp", [(i, i ^ (1 << bit)) for i in range(n_dp)])


def swap_mp(values_in):
    return lax.ppermute(values_in, "mp", [(0, 1), (1, 0)])


def halving(parts, order, n_dp, index):
    bits = n_dp.bit_length() - 1
    left = list(range(bits - 1, -1, -1))
    shape = parts.shape[1:]
    held = parts.reshape((2,) * bits + shape)
    for step, bit in enumerate(order):
        at = left.index(bit)
        upper = ((index >> bit) & 1) == 1
        low = lax.index_in_dim(held, 0, at, keepdims=False)
        high = lax.index_in_dim(held, 1, at, keepdims=False)
        keep, send = jnp.where(upper, high, low), jnp.where(upper, low, high)
        got = swap_dp(send, bit, n_dp)
        last = step == bits - 1
        total = keep.astype(F32) + got.astype(F32)
        held = total if last else total.astype(BF)
        left.remove(bit)
    return held


def orders_of(bits):
    rest = list(range(3, bits))
    if bits < 3:
        return [list(range(bits))] * 3
    return [[0, 1, 2] + rest, [1, 0, 2] + rest, [2, 0, 1] + rest]


def on_device(
    hidden_in,
    sel_one,
    sel_two,
    sel_three,
    segment_ids,
    pad_mask,
    qkv_weight,
    out_weight,
    gate_weight,
    up_weight,
    down_weight,
    norm_one,
    norm_two,
    router_weight,
    d_hidden,
):
    seq_len, width = hidden_in.shape
    n_dp, n_mp = lax.axis_size("dp"), lax.axis_size("mp")
    dp_index, mp_index = lax.axis_index("dp"), lax.axis_index("mp")
    kv_cols = KV_HEADS * HEAD_DIM
    scale = 1.0 / math.sqrt(HEAD_DIM)
    segment, padding = segment_ids[0], pad_mask[0]
    cosine, sine = rotary_tables(seq_len)
    positions = jnp.arange(seq_len, dtype=jnp.int32)
    weights = [(gate_weight, up_weight, down_weight)]
    weights.append(tuple(swap_mp(w) for w in weights[0]))
    causal = positions[None, :] <= positions[:, None]
    same_doc = segment[None, :] == segment[:, None]
    diagonal = positions[None, :] == positions[:, None]

    state = hidden_in
    saved = []
    for recursion, select in enumerate((sel_one[0], sel_two[0], sel_three[0])):
        active = jnp.any(select[:, None] == positions[None, :], axis=0)
        usable = active & (padding == 1)
        allowed = causal & same_doc & (usable[None, :] | diagonal)
        rows = state
        gate = jax.nn.sigmoid(jnp.sum(rows * router_weight[recursion], axis=-1, keepdims=True))
        normed_one = (rows * inverse_rms(rows) * norm_one).astype(BF)
        projected = plain(normed_one, qkv_weight)
        queries = turn(projected[:, :width].reshape(seq_len, HEADS, HEAD_DIM), cosine, sine)
        queries = queries.astype(BF).reshape(seq_len, KV_HEADS, GROUPS, HEAD_DIM)
        keys = turn(
            projected[:, width : width + kv_cols].reshape(seq_len, KV_HEADS, HEAD_DIM), cosine, sine
        ).astype(BF)
        values = projected[:, width + kv_cols :].reshape(seq_len, KV_HEADS, HEAD_DIM).astype(BF)
        scores = (
            jnp.einsum("rwlq,ywq->wlry", queries, keys, preferred_element_type=F32) * scale
        )
        masked = jnp.where(allowed, scores, -1e30)
        top = jnp.max(masked, axis=-1, keepdims=True)
        exponent = jnp.exp(masked - top)
        attend = exponent / jnp.sum(exponent, axis=-1, keepdims=True)
        attend = attend.astype(BF)
        mixed = jnp.einsum("xzpm,mxe->pxze", attend, values, preferred_element_type=F32)
        mixed = mixed.reshape(seq_len, width).astype(BF)
        attn = plain(mixed, out_weight)
        after = rows + attn
        normed_two = (after * inverse_rms(after) * norm_two).astype(BF)
        total, units = 0.0, []
        for gate_w, up_w, down_w in weights:
            g, u = plain(normed_two, gate_w), plain(normed_two, up_w)
            s = jax.nn.sigmoid(g)
            hidden = (g * s * u).astype(BF)
            total = total + contract_last(hidden, down_w)
            units.append((hidden, (u * s * (1.0 + g * (1.0 - s))).astype(BF), (g * s).astype(BF)))
        branch = attn + total.astype(BF).astype(F32)
        state = jnp.where(active[:, None], rows + gate * branch, rows)
        saved.append(
            (active, rows, gate, normed_one, queries, keys, values, attend, mixed, after, branch, normed_two, units)
        )

    grad_state = d_hidden
    gains_one, gains_two, router_rows = 0.0, 0.0, [None] * RECURSIONS
    factors = []
    for recursion in reversed(range(RECURSIONS)):
        (active, rows, gate, normed_one, queries, keys, values, attend, mixed, after, branch, normed_two, units) = saved[recursion]
        d_new = jnp.where(active[:, None], grad_state, 0.0)
        d_gate = jnp.sum(d_new * branch, axis=-1, keepdims=True)
        d_logit = d_gate * gate * (1.0 - gate)
        router_rows[recursion] = jnp.sum(d_logit * rows, axis=0)
        d_branch = gate * d_new
        d_feed = d_branch.astype(BF)
        d_two, d_units = 0.0, []
        for (gate_w, up_w, down_w), (hidden, slope, silu) in zip(weights, units):
            d_hid = plain(d_feed, down_w)
            d_g = (d_hid * slope.astype(F32)).astype(BF)
            d_u = (d_hid * silu.astype(F32)).astype(BF)
            d_two = d_two + contract_last(d_g, gate_w) + contract_last(d_u, up_w)
            d_units.append((d_g, d_u, hidden))
        d_after, gain = norm_back(after, norm_two, d_two.astype(BF).astype(F32))
        gains_two = gains_two + gain
        d_attn = (d_branch + d_after).astype(BF)
        d_mixed = contract_last(d_attn, out_weight).astype(BF)
        d_mixed = d_mixed.reshape(seq_len, KV_HEADS, GROUPS, HEAD_DIM)
        d_values = jnp.einsum("wlmk,mwld->kwd", attend, d_mixed, preferred_element_type=F32)
        d_attend = jnp.einsum("mwld,kwd->wlmk", d_mixed, values, preferred_element_type=F32)
        soft = attend.astype(F32)
        d_scores = (soft * (d_attend - jnp.sum(soft * d_attend, axis=-1, keepdims=True))).astype(BF)
        d_queries = jnp.einsum("wlmk,kwd->mwld", d_scores, keys, preferred_element_type=F32) * scale
        d_keys = jnp.einsum("wlmk,mwld->kwd", d_scores, queries, preferred_element_type=F32) * scale
        d_projected = jnp.concatenate(
            [
                turn(d_queries.reshape(seq_len, HEADS, HEAD_DIM), cosine, -sine).reshape(seq_len, width),
                turn(d_keys, cosine, -sine).reshape(seq_len, kv_cols),
                d_values.reshape(seq_len, kv_cols),
            ],
            axis=1,
        ).astype(BF)
        d_one = contract_last(d_projected, qkv_weight)
        d_rows, gain = norm_back(rows, norm_one, d_one)
        gains_one = gains_one + gain
        d_rows = d_new + d_logit * router_weight[recursion] + d_after + d_rows
        grad_state = jnp.where(active[:, None], d_rows, grad_state)
        factors.append((normed_one, d_projected, mixed, d_attn, normed_two, d_feed, d_units))

    def stacked(pick):
        return jnp.concatenate([pick(f) for f in factors], axis=0)

    two, feed = stacked(lambda f: f[4]), stacked(lambda f: f[5])
    units = gate_weight.shape[1]
    bits = n_dp.bit_length() - 1

    def ffn_terms(side, columns):
        return jnp.concatenate(
            [
                contract_rows(left, stacked(lambda f: f[6][side][which])[:, columns]).astype(BF)
                for which, left in enumerate((two, two, feed))
            ],
            axis=0,
        )

    orders = orders_of(bits)
    if 3 * width % n_dp == 0 and units % 1280 == 0:
        fifth = units // 5
        streams = [(orders[i], slice(j * fifth, (j + 1) * fifth)) for i, j in ((0, 0), (1, 1), (2, 2), (0, 3), (1, 4))]
        done = []
        for order, columns in streams:
            terms = ffn_terms(0, columns).astype(F32) + swap_mp(ffn_terms(1, columns)).astype(F32)
            done.append(halving(terms.astype(BF).reshape(n_dp, 3 * width // n_dp, fifth), order, n_dp, dp_index))
        ffn_flat = jnp.concatenate(done, axis=1).reshape(1, -1)
    else:
        terms = ffn_terms(0, slice(None)).astype(F32) + swap_mp(ffn_terms(1, slice(None))).astype(F32)
        terms = terms.astype(BF).reshape(n_dp, 3 * width * units // n_dp // 128, 128)
        ffn_flat = halving(terms, orders[0], n_dp, dp_index).reshape(1, -1)

    grad_qkv = contract_rows(stacked(lambda f: f[0]), stacked(lambda f: f[1])).astype(BF)
    grad_out = contract_rows(stacked(lambda f: f[2]), stacked(lambda f: f[3])).astype(BF)
    share = (grad_qkv.size + grad_out.size) // (n_dp * n_mp)
    attn = jnp.concatenate([grad_qkv.reshape(-1), grad_out.reshape(-1)]).reshape(n_dp, 2, share // 128, 128)
    keep = jnp.where(mp_index == 0, attn[:, 0], attn[:, 1])
    send = jnp.where(mp_index == 0, attn[:, 1], attn[:, 0])
    attn = (keep.astype(F32) + swap_mp(send).astype(F32)).astype(BF)
    cuts = [0, (share // 128) // 24 * 8, (share // 128) // 12 * 8, share // 128]
    attn_flat = jnp.concatenate(
        [halving(attn[:, a:b], order, n_dp, dp_index) for a, b, order in zip(cuts, cuts[1:], orders)], axis=0
    ).reshape(-1)

    small = jnp.stack([gains_one, gains_two, *router_rows])
    small = small + swap_mp(small)
    for bit in range(bits):
        small = small + swap_dp(small, bit, n_dp)
    return (state, grad_state, attn_flat, ffn_flat, small[0], small[1], small[2:])


def solution(mesh):
    both = P(("dp", "mp"), None)
    in_specs = (
        both,
        both,
        both,
        both,
        both,
        both,
        P(),
        P(),
        P(None, "mp"),
        P(None, "mp"),
        P(None, "mp"),
        P(),
        P(),
        P(),
        both,
    )
    out_specs = (both, both, P(("dp", "mp")), P("mp", "dp"), P(), P(), P())
    return jax.shard_map(
        on_device, mesh=mesh, in_specs=in_specs, out_specs=out_specs, check_vma=False
    )
```

```python
import math

import jax
import jax.numpy as jnp
import numpy as np
from jax import lax
from jax.experimental import pallas as pl
from jax.experimental.pallas import tpu as pltpu
from jax.sharding import PartitionSpec as P

HEADS = 15
KV_HEADS = 5
HEAD_DIM = 64
RECURSIONS = 3
GROUPS = HEADS // KV_HEADS
EPS = 1e-05
BF = jnp.bfloat16
F32 = jnp.float32


LANES = 128
CHUNKS = -(-HEADS * HEAD_DIM // LANES)
ROWS = 32
MIB = 1 << 20


def rotary_tables(seq_len):
    half = HEAD_DIM // 2
    frequency = np.float32(100000.0) ** (
        np.float32(-2.0) * np.arange(half, dtype=np.float32) / np.float32(HEAD_DIM)
    )
    angles = np.arange(seq_len, dtype=np.float32)[:, None] * frequency.astype(np.float32)
    cosine, sine = np.cos(angles), np.sin(angles)
    return (
        jnp.asarray(np.concatenate([cosine] * 4, axis=1), F32),
        jnp.asarray(np.concatenate([-sine, sine] * 2, axis=1), F32),
    )


def contract_rows(left, right):
    return lax.dot_general(left, right, (((0,), (0,)), ((), ())), preferred_element_type=F32)


def contract_last(left, right):
    return lax.dot_general(left, right, (((1,), (1,)), ((), ())), preferred_element_type=F32)


def plain(left, right):
    return jnp.dot(left, right, preferred_element_type=F32)


def inverse_rms(rows):
    return lax.rsqrt(jnp.mean(rows * rows, axis=-1, keepdims=True) + EPS)


def norm_back(rows, gain, d_out):
    inv = inverse_rms(rows)
    scaled = d_out * gain
    inner = jnp.mean(scaled * rows, axis=-1, keepdims=True)
    d_rows = inv * scaled - rows * (inv * inv * inv * inner)
    return d_rows, jnp.sum(d_out * rows * inv, axis=0, keepdims=True)


def lane_of(rows):
    return lax.broadcasted_iota(jnp.int32, (rows, LANES), 1)


def swapped(chunk):
    first = lane_of(chunk.shape[0]) % HEAD_DIM < HEAD_DIM // 2
    return jnp.where(first, pltpu.roll(chunk, LANES - 32, 1), pltpu.roll(chunk, 32, 1))


def other_half(chunk):
    return pltpu.roll(chunk, HEAD_DIM, 1)


def over_rows(count, body):
    def lap(i, carry):
        body(pl.ds(pl.multiple_of(i * ROWS, ROWS), ROWS))
        return carry

    lax.fori_loop(0, count // ROWS, lap, 0)


def attention_forward(x_ref, bias_ref, cos_ref, sin_ref, gain, qkv_w, n1_ref, q_ref, kz_ref, vz_ref, p_ref, o_ref):
    seq_len, width = x_ref.shape
    scale = 1.0 / math.sqrt(HEAD_DIM)

    def norm(rows):
        x = x_ref[rows, :]
        n1_ref[rows, :] = (x * inverse_rms(x) * gain).astype(BF)

    over_rows(seq_len, norm)
    lower = lane_of(seq_len) < HEAD_DIM
    n1 = n1_ref[...]

    def spread(ref, head, chunk, upper):
        flipped = other_half(chunk)
        here, there = (flipped, chunk) if upper else (chunk, flipped)
        ref[2 * head] = jnp.where(lower, here, 0.0).astype(BF)
        ref[2 * head + 1] = jnp.where(lower, 0.0, there).astype(BF)

    columns = qkv_w.shape[1]
    for start in range(0, columns, 2 * LANES):
        wide = plain(n1, qkv_w[:, start : min(start + 2 * LANES, columns)])
        for part in range(0, wide.shape[1], LANES):
            chunk = wide[:, part : part + LANES]
            if chunk.shape[1] < LANES:
                chunk = jnp.concatenate([chunk, jnp.zeros_like(chunk)], axis=1)
            at = (start + part) // LANES
            heads = (2 * at, 2 * at + 1)
            if heads[0] < HEADS + KV_HEADS:
                chunk = chunk * cos_ref[...] + swapped(chunk) * sin_ref[...]
                if heads[0] < HEADS:
                    q_ref[:, at * LANES : (at + 1) * LANES] = chunk.astype(BF)
            for upper, head in enumerate(heads):
                if HEADS <= head < HEADS + KV_HEADS:
                    spread(kz_ref, head - HEADS, chunk, upper)
                elif HEADS + KV_HEADS <= head < HEADS + 2 * KV_HEADS:
                    spread(vz_ref, head - HEADS - KV_HEADS, chunk, upper)

    for at in range(CHUNKS):
        query = q_ref[:, at * LANES : (at + 1) * LANES]
        total = None
        for upper in range(2):
            head = 2 * at + upper
            if head < HEADS:
                key = 2 * (head // GROUPS) + upper
                scores = contract_last(query, kz_ref[key]) * scale + bias_ref[...]
                top = jnp.max(scores, axis=-1, keepdims=True)
                exponent = jnp.exp(scores - top)
                share = pl.reciprocal(jnp.sum(exponent, axis=-1, keepdims=True))
                attend = (exponent * share).astype(BF)
                p_ref[head] = attend
                mixed = plain(attend, vz_ref[key])
                total = mixed if total is None else total + mixed
        stop = min(width, (at + 1) * LANES)
        o_ref[:, at * LANES : stop] = total[:, : stop - at * LANES].astype(BF)


def attention_out(x_ref, o_ref, out_w, gain, attn_ref, n2_ref):
    attn_ref[...] = plain(o_ref[...], out_w[...])

    def norm(rows):
        after = x_ref[rows, :] + attn_ref[rows, :]
        n2_ref[rows, :] = (after * inverse_rms(after) * gain).astype(BF)

    over_rows(x_ref.shape[0], norm)


def feed_forward(n2_ref, sides, f_ref):
    n2 = n2_ref[...]
    for side, (gate_w, up_w, down_w, m_ref, slope_ref, silu_ref) in enumerate(sides):

        def lap(i, carry, gate_w=gate_w, up_w=up_w, m_ref=m_ref, slope_ref=slope_ref, silu_ref=silu_ref):
            at = pl.ds(pl.multiple_of(i * 256, 256), 256)
            g, u = plain(n2, gate_w[:, at]), plain(n2, up_w[:, at])
            s = jax.nn.sigmoid(g)
            silu = g * s
            m_ref[:, at] = (silu * u).astype(BF)
            slope_ref[:, at] = (u * s * (1.0 + g * (1.0 - s))).astype(BF)
            silu_ref[:, at] = silu.astype(BF)
            return carry

        lax.fori_loop(0, gate_w.shape[1] // 256, lap, 0)
        part = contract_last(m_ref[...], down_w[...])
        f_ref[...] = part if side == 0 else f_ref[...] + part


def feed_backward(df_ref, sides, d_two_ref):
    d_feed = df_ref[...]
    for side, (gate_w, up_w, down_w, slope_ref, silu_ref, dg_ref, du_ref) in enumerate(sides):

        def lap(i, carry, down_w=down_w, slope_ref=slope_ref, silu_ref=silu_ref, dg_ref=dg_ref, du_ref=du_ref):
            at = pl.ds(pl.multiple_of(i * 256, 256), 256)
            d_hidden = plain(d_feed, down_w[:, at])
            dg_ref[:, at] = (d_hidden * slope_ref[:, at].astype(F32)).astype(BF)
            du_ref[:, at] = (d_hidden * silu_ref[:, at].astype(F32)).astype(BF)
            return carry

        lax.fori_loop(0, gate_w.shape[1] // 256, lap, 0)
        part = contract_last(dg_ref[...], gate_w[...]) + contract_last(du_ref[...], up_w[...])
        d_two_ref[...] = part if side == 0 else d_two_ref[...] + part


def attention_backward(d_attn_ref, out_w, qkv_w, cos_ref, sin_ref, q_ref, kz_ref, vz_ref, p_ref, do_ref, du_ref):
    seq_len, width = d_attn_ref.shape
    scale = 1.0 / math.sqrt(HEAD_DIM)
    do_ref[:, :width] = contract_last(d_attn_ref[...], out_w[...]).astype(BF)
    do_ref[:, width:] = jnp.zeros((seq_len, do_ref.shape[1] - width), BF)
    lower = lane_of(seq_len) < HEAD_DIM
    cosine, sine = cos_ref[...], sin_ref[...]

    def back(chunk):
        chunk = chunk * scale
        return chunk * cosine - swapped(chunk) * sine

    waiting, d_k, d_v = None, {}, {}
    sums = [[None, None], [None, None]]
    for at in range(CHUNKS):
        query, d_mixed = (ref[:, at * LANES : (at + 1) * LANES] for ref in (q_ref, do_ref))
        d_query = None
        for upper in range(2):
            head = 2 * at + upper
            if head >= HEADS:
                continue
            group = head // GROUPS
            key = 2 * group + upper
            attend = p_ref[head]
            d_attend = contract_last(d_mixed, vz_ref[key])
            soft = attend.astype(F32)
            weighted = soft * d_attend
            inner = jnp.sum(weighted, axis=-1, keepdims=True)
            d_scores = (weighted - soft * inner).astype(BF)
            part = plain(d_scores, kz_ref[key])
            d_query = part if d_query is None else d_query + part
            for which, term in ((0, contract_rows(d_scores, query)), (1, contract_rows(attend, d_mixed))):
                old = sums[which][upper]
                sums[which][upper] = term if old is None else old + term
            if head % GROUPS == GROUPS - 1:
                for which, store in ((0, d_k), (1, d_v)):
                    both = jnp.where(lower, sums[which][0], sums[which][1])
                    store[group] = both + other_half(both)
                sums = [[None, None], [None, None]]
        if at < CHUNKS - 1:
            du_ref[:, at * LANES : (at + 1) * LANES] = back(d_query).astype(BF)
        else:
            waiting = d_query
    tail = jnp.where(lower, waiting, d_k[0])
    du_ref[:, (CHUNKS - 1) * LANES : CHUNKS * LANES] = back(tail).astype(BF)
    for i in range(2):
        at = CHUNKS + i
        du_ref[:, at * LANES : (at + 1) * LANES] = back(jnp.where(lower, d_k[1 + 2 * i], d_k[2 + 2 * i])).astype(BF)
        at = CHUNKS + 2 + i
        du_ref[:, at * LANES : (at + 1) * LANES] = jnp.where(lower, d_v[2 * i], d_v[2 * i + 1]).astype(BF)
    at = CHUNKS + 4
    du_ref[:, at * LANES :] = d_v[4][:, : du_ref.shape[1] - at * LANES].astype(BF)


def router_gate(x, router_row):
    return jax.nn.sigmoid(jnp.sum(x * router_row, axis=-1, keepdims=True))


def first_attention(x_ref, bias_ref, cos_ref, sin_ref, gain_one, gain_two, qkv_w, out_w,
                    n1_ref, q_ref, kz_ref, vz_ref, p_ref, o_ref, attn_ref, n2_ref):
    n1, o = n1_ref.at[0], o_ref.at[0]
    attention_forward(x_ref, bias_ref.at[0], cos_ref, sin_ref, gain_one[...], qkv_w, n1, q_ref, kz_ref, vz_ref, p_ref, o)
    attention_out(x_ref, o, out_w, gain_two[...], attn_ref, n2_ref)


def load_all(pairs, sems):
    copies = [pltpu.make_async_copy(src, dst, sems.at[i]) for i, (src, dst) in enumerate(pairs)]
    return copies


def forward_steps(x0_ref, attn0_ref, n20_ref, bias_ref, active_ref, router_ref, cos_ref, sin_ref, gain_one, gain_two,
                  n1_in, o_in, qkv_hbm, out_hbm, *rest):
    feed_hbm, rest = rest[:6], rest[6:]
    (n1_ref, o_ref, q_ref, kz_ref, vz_ref, p_ref, x_ref, a_ref, branch_ref, n2_ref,
     m0, m1, slope0, slope1, silu0, silu1, final_ref), rest = rest[:17], rest[17:]
    qkv_w, out_w, w0, w1, w2, w3, w4, w5, state, attn, n2, total, sems = rest
    step = pl.program_id(0)
    copies = load_all(list(zip((*feed_hbm, qkv_hbm, out_hbm), (w0, w1, w2, w3, w4, w5, qkv_w, out_w))), sems)

    @pl.when(step == 0)
    def _():
        for copy in copies:
            copy.start()
        state[...] = x0_ref[...]
        attn[...] = attn0_ref[...]
        n2[...] = n20_ref[...]
        for copy in copies[:6]:
            copy.wait()

    n2_ref[0] = n2[...]
    feed_forward(n2, ((w0, w1, w2, m0.at[0], slope0.at[0], silu0.at[0]), (w3, w4, w5, m1.at[0], slope1.at[0], silu1.at[0])), total)
    router_row = router_ref[0]

    def finish(rows):
        x, attn_rows = state[rows, :], attn[rows, :]
        x_ref[0, rows, :] = x
        a_ref[0, rows, :] = x + attn_rows
        branch = attn_rows + total[rows, :].astype(BF).astype(F32)
        branch_ref[0, rows, :] = branch
        new = jnp.where(active_ref[0, rows, :] > 0, x + router_gate(x, router_row) * branch, x)
        state[rows, :] = new
        final_ref[rows, :] = new

    over_rows(state.shape[0], finish)

    @pl.when(step == 0)
    def _():
        for copy in copies[6:]:
            copy.wait()

    @pl.when(step < RECURSIONS - 1)
    def _():
        attention_forward(state, bias_ref.at[0], cos_ref, sin_ref, gain_one[...], qkv_w,
                          n1_ref.at[0], q_ref.at[0], kz_ref.at[0], vz_ref.at[0], p_ref.at[0], o_ref.at[0])
        attention_out(state, o_ref.at[0], out_w, gain_two[...], attn, n2)


def finish_attention_backward(x_ref, gain, active_ref, du_ref, qkv_w, base, state, total, out_ref):
    total[...] = contract_last(du_ref[...], qkv_w[...])
    terms = jnp.zeros((1, state.shape[1]), F32)

    def lap(i, terms):
        rows = pl.ds(pl.multiple_of(i * ROWS, ROWS), ROWS)
        d_rows, term = norm_back(x_ref[rows, :], gain, total[rows, :])
        new = jnp.where(active_ref[rows, :] > 0, base[rows, :] + d_rows, state[rows, :])
        out_ref[rows, :] = new
        return terms + term

    return lax.fori_loop(0, state.shape[0] // ROWS, lap, terms)


def backward_steps(d_hidden_ref, active_ref, router_ref, cos_ref, sin_ref, gain_one, gain_two,
                   x_ref, a_ref, branch_ref, slope0, slope1, silu0, silu1, q_ref, kz_ref, vz_ref, p_ref,
                   qkv_hbm, out_hbm, *rest):
    feed_hbm, rest = rest[:6], rest[6:]
    (df_ref, dg0, dg1, dw0, dw1, d_attn_ref, du_ref, base_ref, state_ref, small_ref), rest = rest[:10], rest[10:]
    qkv_w, out_w, w0, w1, w2, w3, w4, w5, d_branch, total, do_ref, sems = rest
    step = pl.program_id(0)
    copies = load_all(list(zip(
        (feed_hbm[2], feed_hbm[0], feed_hbm[1], feed_hbm[5], feed_hbm[3], feed_hbm[4], out_hbm, qkv_hbm),
        (w2, w0, w1, w5, w3, w4, out_w, qkv_w))), sems)

    @pl.when(step == 0)
    def _():
        for copy in copies:
            copy.start()
        state_ref[...] = d_hidden_ref[...]
        small_ref[...] = jnp.zeros(small_ref.shape, F32)

    router_row = router_ref[0]
    width = state_ref.shape[1]
    laps = state_ref.shape[0] // ROWS

    def enter(i, terms):
        rows = pl.ds(pl.multiple_of(i * ROWS, ROWS), ROWS)
        x = x_ref[0, rows, :]
        d_new = jnp.where(active_ref[0, rows, :] > 0, state_ref[rows, :], 0.0)
        gate = router_gate(x, router_row)
        d_gate = jnp.sum(d_new * branch_ref[0, rows, :], axis=-1, keepdims=True)
        d_logit = d_gate * gate * (1.0 - gate)
        spread = gate * d_new
        d_branch[rows, :] = spread
        df_ref[0, rows, :] = spread.astype(BF)
        base_ref[rows, :] = d_new + d_logit * router_row
        return terms + jnp.sum(d_logit * x, axis=0, keepdims=True)

    small_ref[pl.ds(2 + RECURSIONS - 1 - step, 1), :] = lax.fori_loop(0, laps, enter, jnp.zeros((1, width), F32))

    @pl.when(step == 0)
    def _():
        for copy in copies[:6]:
            copy.wait()

    feed_backward(df_ref.at[0], ((w0, w1, w2, slope0.at[0], silu0.at[0], dg0.at[0], dw0.at[0]),
                                 (w3, w4, w5, slope1.at[0], silu1.at[0], dg1.at[0], dw1.at[0])), total)

    def leave(i, terms):
        rows = pl.ds(pl.multiple_of(i * ROWS, ROWS), ROWS)
        d_after, term = norm_back(a_ref[0, rows, :], gain_two[...], total[rows, :].astype(BF).astype(F32))
        d_attn_ref[0, rows, :] = (d_branch[rows, :] + d_after).astype(BF)
        base_ref[rows, :] = base_ref[rows, :] + d_after
        return terms + term

    small_ref[1:2, :] = small_ref[1:2, :] + lax.fori_loop(0, laps, leave, jnp.zeros((1, width), F32))

    @pl.when(step == 0)
    def _():
        for copy in copies[6:]:
            copy.wait()

    @pl.when(step < RECURSIONS - 1)
    def _():
        attention_backward(d_attn_ref.at[0], out_w, qkv_w, cos_ref, sin_ref, q_ref.at[0], kz_ref.at[0], vz_ref.at[0],
                           p_ref.at[0], do_ref, du_ref.at[0])
        term = finish_attention_backward(x_ref.at[0], gain_one[...], active_ref.at[0], du_ref.at[0], qkv_w, base_ref, state_ref, total, state_ref)
        small_ref[0:1, :] = small_ref[0:1, :] + term


def last_attention(x_ref, active_ref, cos_ref, sin_ref, gain_one, q_ref, kz_ref, vz_ref, p_ref, d_attn_ref,
                   base_ref, state_ref, small_in, du_in, qkv_w, out_w, du_ref, d_input_ref, small_ref, do_ref, total):
    attention_backward(d_attn_ref.at[0], out_w, qkv_w, cos_ref, sin_ref, q_ref, kz_ref, vz_ref, p_ref, do_ref, du_ref.at[0])
    term = finish_attention_backward(x_ref.at[0], gain_one[...], active_ref.at[0], du_ref.at[0], qkv_w, base_ref, state_ref, total, d_input_ref)
    small_ref[...] = small_in[...]
    small_ref[0:1, :] = small_in[0:1, :] + term


def swap_dp(values_in, bit, n_dp):
    return lax.ppermute(values_in, "dp", [(i, i ^ (1 << bit)) for i in range(n_dp)])


def swap_mp(values_in):
    return lax.ppermute(values_in, "mp", [(0, 1), (1, 0)])


def halving(parts, order, n_dp, index):
    bits = n_dp.bit_length() - 1
    left = list(range(bits - 1, -1, -1))
    shape = parts.shape[1:]
    held = parts.reshape((2,) * bits + shape)
    for step, bit in enumerate(order):
        at = left.index(bit)
        upper = ((index >> bit) & 1) == 1
        low = lax.index_in_dim(held, 0, at, keepdims=False)
        high = lax.index_in_dim(held, 1, at, keepdims=False)
        keep, send = jnp.where(upper, high, low), jnp.where(upper, low, high)
        got = swap_dp(send, bit, n_dp)
        last = step == bits - 1
        total = keep.astype(F32) + got.astype(F32)
        held = total if last else total.astype(BF)
        left.remove(bit)
    return held


def orders_of(bits):
    rest = list(range(3, bits))
    if bits < 3:
        return [list(range(bits))] * 3
    return [[0, 1, 2] + rest, [1, 0, 2] + rest, [2, 0, 1] + rest]


def on_device(
    hidden_in,
    sel_one,
    sel_two,
    sel_three,
    segment_ids,
    pad_mask,
    qkv_weight,
    out_weight,
    gate_weight,
    up_weight,
    down_weight,
    norm_one,
    norm_two,
    router_weight,
    d_hidden,
):
    seq_len, width = hidden_in.shape
    n_dp, n_mp = lax.axis_size("dp"), lax.axis_size("mp")
    dp_index, mp_index = lax.axis_index("dp"), lax.axis_index("mp")
    segment, padding = segment_ids[0], pad_mask[0]
    cosine, sine = rotary_tables(seq_len)
    positions = jnp.arange(seq_len, dtype=jnp.int32)
    weights = [(gate_weight, up_weight, down_weight)]
    weights.append(tuple(swap_mp(w) for w in weights[0]))
    causal = positions[None, :] <= positions[:, None]
    same_doc = segment[None, :] == segment[:, None]
    diagonal = positions[None, :] == positions[:, None]

    selections = (sel_one[0], sel_two[0], sel_three[0])
    active = jnp.stack([jnp.any(select[:, None] == positions[None, :], axis=0) for select in selections])
    usable = active & (padding == 1)[None, :]
    allowed = (causal & same_doc)[None] & (usable[:, None, :] | diagonal[None])
    bias = jnp.where(allowed, 0.0, -1e30).astype(F32)
    active = jnp.broadcast_to(active[:, :, None], (RECURSIONS, seq_len, 1)).astype(F32)
    gain_one, gain_two = norm_one.reshape(1, width), norm_two.reshape(1, width)
    router = router_weight.reshape(RECURSIONS, 1, width)
    padded = CHUNKS * LANES
    units = gate_weight.shape[1]
    feed_weights = (*weights[0], *weights[1])

    def shape(*dims, dtype=BF):
        return jax.ShapeDtypeStruct(dims, dtype)

    def whole(*dims, **kw):
        return pl.BlockSpec(dims, lambda *_: (0,) * len(dims), **kw)

    anywhere = pl.BlockSpec(memory_space=pl.ANY)
    one = pl.Buffered(1)
    stack = RECURSIONS, seq_len
    heads = (2 * KV_HEADS, seq_len, LANES)
    square = (HEADS, seq_len, seq_len)
    n1, q, kz, vz, p, o, attn, n2 = pl.pallas_call(
        first_attention,
        grid=(1,),
        in_specs=[
            whole(seq_len, width), whole(1, seq_len, seq_len), whole(seq_len, LANES), whole(seq_len, LANES),
            whole(1, width), whole(1, width), whole(*qkv_weight.shape), whole(*out_weight.shape),
        ],
        out_specs=[
            whole(1, seq_len, width), whole(seq_len, padded), whole(*heads), whole(*heads), whole(*square),
            whole(1, seq_len, width), whole(seq_len, width), whole(seq_len, width),
        ],
        out_shape=[
            shape(*stack, width), shape(seq_len, padded), shape(*heads), shape(*heads), shape(*square),
            shape(*stack, width), shape(seq_len, width, dtype=F32), shape(seq_len, width),
        ],
        compiler_params=pltpu.CompilerParams(vmem_limit_bytes=30 * MIB),
        cost_estimate=pl.CostEstimate(flops=2 * 10**9, bytes_accessed=12 * 10**6, transcendentals=600000),
        name="first_attention",
    )(hidden_in, bias, cosine, sine, gain_one, gain_two, qkv_weight, out_weight)
    attention_0 = (q, kz, vz, p)

    def at_step(*dims):
        return pl.BlockSpec((1, *dims), lambda r: (r,) + (0,) * len(dims))

    def next_step(*dims):
        return pl.BlockSpec((1, *dims), lambda r: (jnp.minimum(r + 1, RECURSIONS - 1),) + (0,) * len(dims))

    def next_pair(*dims):
        return pl.BlockSpec((1, *dims), lambda r: (jnp.minimum(r, RECURSIONS - 2),) + (0,) * len(dims))

    weight_scratch = [pltpu.VMEM(w.shape, BF) for w in (qkv_weight, out_weight, *feed_weights)]
    results = pl.pallas_call(
        forward_steps,
        grid=(RECURSIONS,),
        in_specs=[
            whole(seq_len, width, pipeline_mode=one), whole(seq_len, width, pipeline_mode=one), whole(seq_len, width, pipeline_mode=one),
            next_step(seq_len, seq_len), at_step(seq_len, 1), at_step(1, width),
            whole(seq_len, LANES), whole(seq_len, LANES), whole(1, width), whole(1, width),
            anywhere, anywhere, *[anywhere] * 8,
        ],
        out_specs=[
            next_step(seq_len, width), next_step(seq_len, width), next_pair(seq_len, padded), next_pair(*heads), next_pair(*heads),
            next_pair(*square), *[at_step(seq_len, width)] * 4, *[at_step(seq_len, units)] * 6, whole(seq_len, width),
        ],
        out_shape=[
            shape(*stack, width), shape(*stack, width), shape(RECURSIONS - 1, seq_len, padded), shape(RECURSIONS - 1, *heads), shape(RECURSIONS - 1, *heads),
            shape(RECURSIONS - 1, *square), *[shape(*stack, width, dtype=F32)] * 3, shape(*stack, width), *[shape(*stack, units)] * 6,
            shape(seq_len, width, dtype=F32),
        ],
        scratch_shapes=[
            *weight_scratch,
            pltpu.VMEM((seq_len, width), F32), pltpu.VMEM((seq_len, width), F32), pltpu.VMEM((seq_len, width), BF), pltpu.VMEM((seq_len, width), F32),
            pltpu.SemaphoreType.DMA((8,)),
        ],
        input_output_aliases={10: 0, 11: 1},
        compiler_params=pltpu.CompilerParams(vmem_limit_bytes=58 * MIB),
        cost_estimate=pl.CostEstimate(flops=12 * 10**9, bytes_accessed=50 * 10**6, transcendentals=4 * 10**6),
        name="forward_steps",
    )(hidden_in, attn, n2, bias, active, router, cosine, sine, gain_one, gain_two, n1, o, qkv_weight, out_weight, *feed_weights)
    n1, o, q, kz, vz, p, x, a, branch, n2, m0, m1, slope0, slope1, silu0, silu1, state = results

    def back_step(*dims):
        return pl.BlockSpec((1, *dims), lambda i: (RECURSIONS - 1 - i,) + (0,) * len(dims))

    def back_pair(*dims):
        return pl.BlockSpec((1, *dims), lambda i: (jnp.maximum(RECURSIONS - 2 - i, 0),) + (0,) * len(dims))

    def back_next(*dims):
        return pl.BlockSpec((1, *dims), lambda i: (jnp.maximum(RECURSIONS - 1 - i, 1),) + (0,) * len(dims))

    results = pl.pallas_call(
        backward_steps,
        grid=(RECURSIONS,),
        in_specs=[
            whole(seq_len, width, pipeline_mode=one), back_step(seq_len, 1), back_step(1, width),
            whole(seq_len, LANES), whole(seq_len, LANES), whole(1, width), whole(1, width),
            *[back_step(seq_len, width)] * 3, *[back_step(seq_len, units)] * 4,
            back_pair(seq_len, padded), back_pair(*heads), back_pair(*heads), back_pair(*square),
            *[anywhere] * 8,
        ],
        out_specs=[
            back_step(seq_len, width), *[back_step(seq_len, units)] * 4, back_step(seq_len, width), back_next(seq_len, qkv_weight.shape[1]),
            whole(seq_len, width), whole(seq_len, width), whole(8, width),
        ],
        out_shape=[
            shape(*stack, width), *[shape(*stack, units)] * 4, shape(*stack, width), shape(*stack, qkv_weight.shape[1]),
            shape(seq_len, width, dtype=F32), shape(seq_len, width, dtype=F32), shape(8, width, dtype=F32),
        ],
        scratch_shapes=[
            *weight_scratch,
            pltpu.VMEM((seq_len, width), F32), pltpu.VMEM((seq_len, width), F32), pltpu.VMEM((seq_len, padded), BF),
            pltpu.SemaphoreType.DMA((8,)),
        ],
        compiler_params=pltpu.CompilerParams(vmem_limit_bytes=60 * MIB),
        cost_estimate=pl.CostEstimate(flops=11 * 10**9, bytes_accessed=50 * 10**6, transcendentals=4 * 10**6),
        name="backward_steps",
    )(d_hidden, active, router, cosine, sine, gain_one, gain_two, x, a, branch, slope0, slope1, silu0, silu1, q, kz, vz, p,
      qkv_weight, out_weight, *feed_weights)
    d_feed, dg0, dg1, dw0, dw1, d_attn, du, base, grad_state, small = results

    du, grad_state, small = pl.pallas_call(
        last_attention,
        grid=(1,),
        in_specs=[
            whole(1, seq_len, width), whole(1, seq_len, 1), whole(seq_len, LANES), whole(seq_len, LANES), whole(1, width),
            whole(seq_len, padded), whole(*heads), whole(*heads), whole(*square), whole(1, seq_len, width),
            whole(seq_len, width), whole(seq_len, width), whole(8, width), anywhere, whole(*qkv_weight.shape), whole(*out_weight.shape),
        ],
        out_specs=[whole(1, seq_len, qkv_weight.shape[1]), whole(seq_len, width), whole(8, width)],
        out_shape=[shape(*stack, qkv_weight.shape[1]), shape(seq_len, width, dtype=F32), shape(8, width, dtype=F32)],
        scratch_shapes=[pltpu.VMEM((seq_len, padded), BF), pltpu.VMEM((seq_len, width), F32)],
        input_output_aliases={13: 0},
        compiler_params=pltpu.CompilerParams(vmem_limit_bytes=30 * MIB),
        cost_estimate=pl.CostEstimate(flops=3 * 10**9, bytes_accessed=14 * 10**6, transcendentals=10**5),
        name="last_attention",
    )(x, active, cosine, sine, gain_one, *attention_0, d_attn, base, grad_state, small, du, qkv_weight, out_weight)

    def rows_of(stacked):
        return stacked.reshape(-1, stacked.shape[-1])

    two, feed = rows_of(n2), rows_of(d_feed)
    sides = ((dg0, dw0, m0), (dg1, dw1, m1))
    bits = n_dp.bit_length() - 1

    def ffn_terms(side, columns):
        return jnp.concatenate(
            [
                contract_rows(left, rows_of(sides[side][which])[:, columns]).astype(BF)
                for which, left in enumerate((two, two, feed))
            ],
            axis=0,
        )

    orders = orders_of(bits)
    if 3 * width % n_dp == 0 and units % 1280 == 0:
        fifth = units // 5
        streams = [(orders[i], slice(j * fifth, (j + 1) * fifth)) for i, j in ((0, 0), (1, 1), (2, 2), (0, 3), (1, 4))]
        done = []
        for order, columns in streams:
            terms = ffn_terms(0, columns).astype(F32) + swap_mp(ffn_terms(1, columns)).astype(F32)
            done.append(halving(terms.astype(BF).reshape(n_dp, 3 * width // n_dp, fifth), order, n_dp, dp_index))
        ffn_flat = jnp.concatenate(done, axis=1).reshape(1, -1)
    else:
        terms = ffn_terms(0, slice(None)).astype(F32) + swap_mp(ffn_terms(1, slice(None))).astype(F32)
        terms = terms.astype(BF).reshape(n_dp, 3 * width * units // n_dp // 128, 128)
        ffn_flat = halving(terms, orders[0], n_dp, dp_index).reshape(1, -1)

    grad_qkv = contract_rows(rows_of(n1), rows_of(du)).astype(BF)
    grad_out = contract_rows(rows_of(o), rows_of(d_attn)).astype(BF)
    share = (grad_qkv.size + grad_out.size) // (n_dp * n_mp)
    attn = jnp.concatenate([grad_qkv.reshape(-1), grad_out.reshape(-1)]).reshape(n_dp, 2, share // 128, 128)
    keep = jnp.where(mp_index == 0, attn[:, 0], attn[:, 1])
    send = jnp.where(mp_index == 0, attn[:, 1], attn[:, 0])
    attn = (keep.astype(F32) + swap_mp(send).astype(F32)).astype(BF)
    cuts = [0, (share // 128) // 24 * 8, (share // 128) // 12 * 8, share // 128]
    attn_flat = jnp.concatenate(
        [halving(attn[:, a:b], order, n_dp, dp_index) for a, b, order in zip(cuts, cuts[1:], orders)], axis=0
    ).reshape(-1)

    small = small + swap_mp(small)
    for bit in range(bits):
        small = small + swap_dp(small, bit, n_dp)
    return (state, grad_state, attn_flat, ffn_flat, small[0], small[1], small[2 : 2 + RECURSIONS])


def solution(mesh):
    both = P(("dp", "mp"), None)
    in_specs = (
        both,
        both,
        both,
        both,
        both,
        both,
        P(),
        P(),
        P(None, "mp"),
        P(None, "mp"),
        P(None, "mp"),
        P(),
        P(),
        P(),
        both,
    )
    out_specs = (both, both, P(("dp", "mp")), P("mp", "dp"), P(), P(), P())
    return jax.shard_map(
        on_device, mesh=mesh, in_specs=in_specs, out_specs=out_specs, check_vma=False
    )
```

```python
import math

import jax
import jax.numpy as jnp
import numpy as np
from jax import lax
from jax.experimental import pallas as pl
from jax.experimental.pallas import tpu as pltpu
from jax.sharding import PartitionSpec as P

HEADS = 15
KV_HEADS = 5
HEAD_DIM = 64
RECURSIONS = 3
GROUPS = HEADS // KV_HEADS
EPS = 1e-05
BF = jnp.bfloat16
F32 = jnp.float32


LANES = 128
CHUNKS = -(-HEADS * HEAD_DIM // LANES)
ROWS = 32
BLOCK = 256
MIB = 1 << 20


def rotary_tables(seq_len):
    half = HEAD_DIM // 2
    frequency = np.float32(100000.0) ** (
        np.float32(-2.0) * np.arange(half, dtype=np.float32) / np.float32(HEAD_DIM)
    )
    angles = np.arange(seq_len, dtype=np.float32)[:, None] * frequency.astype(np.float32)
    cosine, sine = np.cos(angles), np.sin(angles)
    return (
        jnp.asarray(np.concatenate([cosine] * 4, axis=1), F32),
        jnp.asarray(np.concatenate([-sine, sine] * 2, axis=1), F32),
    )


def contract_rows(left, right):
    return lax.dot_general(left, right, (((0,), (0,)), ((), ())), preferred_element_type=F32)


def contract_last(left, right):
    return lax.dot_general(left, right, (((1,), (1,)), ((), ())), preferred_element_type=F32)


def plain(left, right):
    return jnp.dot(left, right, preferred_element_type=F32)


def inverse_rms(rows):
    return lax.rsqrt(jnp.mean(rows * rows, axis=-1, keepdims=True) + EPS)


def norm_back(rows, gain, d_out):
    inv = inverse_rms(rows)
    scaled = d_out * gain
    inner = jnp.mean(scaled * rows, axis=-1, keepdims=True)
    d_rows = inv * scaled - rows * (inv * inv * inv * inner)
    return d_rows, jnp.sum(d_out * rows * inv, axis=0, keepdims=True)


def lane_of(rows):
    return lax.broadcasted_iota(jnp.int32, (rows, LANES), 1)


def swapped(chunk):
    first = lane_of(chunk.shape[0]) % HEAD_DIM < HEAD_DIM // 2
    return jnp.where(first, pltpu.roll(chunk, LANES - 32, 1), pltpu.roll(chunk, 32, 1))


def other_half(chunk):
    return pltpu.roll(chunk, HEAD_DIM, 1)


def over_rows(count, body):
    def lap(i, carry):
        body(pl.ds(pl.multiple_of(i * ROWS, ROWS), ROWS))
        return carry

    lax.fori_loop(0, count // ROWS, lap, 0)


def attention_forward(x_ref, bias_ref, cos_ref, sin_ref, gain, qkv_w, n1_ref, q_ref, kz_ref, vz_ref, p_ref, o_ref):
    seq_len, width = x_ref.shape
    scale = 1.0 / math.sqrt(HEAD_DIM)

    def norm(rows):
        x = x_ref[rows, :]
        n1_ref[rows, :] = (x * inverse_rms(x) * gain).astype(BF)

    over_rows(seq_len, norm)
    lower = lane_of(seq_len) < HEAD_DIM
    n1 = n1_ref[...]

    def spread(ref, head, chunk, upper):
        flipped = other_half(chunk)
        here, there = (flipped, chunk) if upper else (chunk, flipped)
        ref[2 * head] = jnp.where(lower, here, 0.0).astype(BF)
        ref[2 * head + 1] = jnp.where(lower, 0.0, there).astype(BF)

    columns = qkv_w.shape[1]
    for start in range(0, columns, 2 * LANES):
        wide = plain(n1, qkv_w[:, start : min(start + 2 * LANES, columns)])
        for part in range(0, wide.shape[1], LANES):
            chunk = wide[:, part : part + LANES]
            if chunk.shape[1] < LANES:
                chunk = jnp.concatenate([chunk, jnp.zeros_like(chunk)], axis=1)
            at = (start + part) // LANES
            heads = (2 * at, 2 * at + 1)
            if heads[0] < HEADS + KV_HEADS:
                chunk = chunk * cos_ref[...] + swapped(chunk) * sin_ref[...]
                if heads[0] < HEADS:
                    q_ref[:, at * LANES : (at + 1) * LANES] = chunk.astype(BF)
            for upper, head in enumerate(heads):
                if HEADS <= head < HEADS + KV_HEADS:
                    spread(kz_ref, head - HEADS, chunk, upper)
                elif HEADS + KV_HEADS <= head < HEADS + 2 * KV_HEADS:
                    spread(vz_ref, head - HEADS - KV_HEADS, chunk, upper)

    for at in range(CHUNKS):
        query = q_ref[:, at * LANES : (at + 1) * LANES]
        total = None
        for upper in range(2):
            head = 2 * at + upper
            if head < HEADS:
                key = 2 * (head // GROUPS) + upper
                scores = contract_last(query, kz_ref[key]) * scale + bias_ref[...]
                top = jnp.max(scores, axis=-1, keepdims=True)
                exponent = jnp.exp(scores - top)
                share = pl.reciprocal(jnp.sum(exponent, axis=-1, keepdims=True))
                attend = (exponent * share).astype(BF)
                p_ref[head] = attend
                mixed = plain(attend, vz_ref[key])
                total = mixed if total is None else total + mixed
        stop = min(width, (at + 1) * LANES)
        o_ref[:, at * LANES : stop] = total[:, : stop - at * LANES].astype(BF)


def attention_out(x_ref, o_ref, out_w, gain, attn_ref, n2_ref):
    attn_ref[...] = plain(o_ref[...], out_w[...])

    def norm(rows):
        after = x_ref[rows, :] + attn_ref[rows, :]
        n2_ref[rows, :] = (after * inverse_rms(after) * gain).astype(BF)

    over_rows(x_ref.shape[0], norm)


def feed_forward(n2_ref, sides, f_ref):
    n2 = n2_ref[...]
    for side, (gate_w, up_w, down_w, m_ref, slope_ref, silu_ref) in enumerate(sides):
        for start in range(0, gate_w.shape[1], BLOCK):
            at = slice(start, start + BLOCK)
            g, u = plain(n2, gate_w[:, at]), plain(n2, up_w[:, at])
            s = jax.nn.sigmoid(g)
            silu = g * s
            m_ref[:, at] = (silu * u).astype(BF)
            slope_ref[:, at] = (u * s * (1.0 + g * (1.0 - s))).astype(BF)
            silu_ref[:, at] = silu.astype(BF)
        part = contract_last(m_ref[...], down_w[...])
        f_ref[...] = part if side == 0 else f_ref[...] + part


def feed_backward(df_ref, sides, d_two_ref):
    d_feed = df_ref[...]
    for side, (gate_w, up_w, down_w, slope_ref, silu_ref, dg_ref, du_ref) in enumerate(sides):
        for start in range(0, gate_w.shape[1], BLOCK):
            at = slice(start, start + BLOCK)
            d_hidden = plain(d_feed, down_w[:, at])
            dg_ref[:, at] = (d_hidden * slope_ref[:, at].astype(F32)).astype(BF)
            du_ref[:, at] = (d_hidden * silu_ref[:, at].astype(F32)).astype(BF)
        part = contract_last(dg_ref[...], gate_w[...]) + contract_last(du_ref[...], up_w[...])
        d_two_ref[...] = part if side == 0 else d_two_ref[...] + part


def attention_backward(d_attn_ref, out_w, qkv_w, cos_ref, sin_ref, q_ref, kz_ref, vz_ref, p_ref, do_ref, du_ref):
    seq_len, width = d_attn_ref.shape
    scale = 1.0 / math.sqrt(HEAD_DIM)
    do_ref[:, :width] = contract_last(d_attn_ref[...], out_w[...]).astype(BF)
    do_ref[:, width:] = jnp.zeros((seq_len, do_ref.shape[1] - width), BF)
    lower = lane_of(seq_len) < HEAD_DIM
    cosine, sine = cos_ref[...], sin_ref[...]

    def back(chunk):
        chunk = chunk * scale
        return chunk * cosine - swapped(chunk) * sine

    waiting, d_k, d_v = None, {}, {}
    sums = [[None, None], [None, None]]
    for at in range(CHUNKS):
        query, d_mixed = (ref[:, at * LANES : (at + 1) * LANES] for ref in (q_ref, do_ref))
        d_query = None
        for upper in range(2):
            head = 2 * at + upper
            if head >= HEADS:
                continue
            group = head // GROUPS
            key = 2 * group + upper
            attend = p_ref[head]
            d_attend = contract_last(d_mixed, vz_ref[key])
            soft = attend.astype(F32)
            weighted = soft * d_attend
            inner = jnp.sum(weighted, axis=-1, keepdims=True)
            d_scores = (weighted - soft * inner).astype(BF)
            part = plain(d_scores, kz_ref[key])
            d_query = part if d_query is None else d_query + part
            for which, term in ((0, contract_rows(d_scores, query)), (1, contract_rows(attend, d_mixed))):
                old = sums[which][upper]
                sums[which][upper] = term if old is None else old + term
            if head % GROUPS == GROUPS - 1:
                for which, store in ((0, d_k), (1, d_v)):
                    both = jnp.where(lower, sums[which][0], sums[which][1])
                    store[group] = both + other_half(both)
                sums = [[None, None], [None, None]]
        if at < CHUNKS - 1:
            du_ref[:, at * LANES : (at + 1) * LANES] = back(d_query).astype(BF)
        else:
            waiting = d_query
    tail = jnp.where(lower, waiting, d_k[0])
    du_ref[:, (CHUNKS - 1) * LANES : CHUNKS * LANES] = back(tail).astype(BF)
    for i in range(2):
        at = CHUNKS + i
        du_ref[:, at * LANES : (at + 1) * LANES] = back(jnp.where(lower, d_k[1 + 2 * i], d_k[2 + 2 * i])).astype(BF)
        at = CHUNKS + 2 + i
        du_ref[:, at * LANES : (at + 1) * LANES] = jnp.where(lower, d_v[2 * i], d_v[2 * i + 1]).astype(BF)
    at = CHUNKS + 4
    du_ref[:, at * LANES :] = d_v[4][:, : du_ref.shape[1] - at * LANES].astype(BF)


def router_gate(x, router_row):
    return jax.nn.sigmoid(jnp.sum(x * router_row, axis=-1, keepdims=True))


def masks(select_refs, segment_ref, pad_ref, bias_ref, active_ref):
    seq_len = segment_ref.shape[1]
    square = (seq_len, seq_len)
    query, key = (lax.broadcasted_iota(jnp.int32, square, axis) for axis in (0, 1))
    diagonal = query == key
    segment = segment_ref[...].astype(F32)
    own = jnp.sum(jnp.where(diagonal, segment, 0.0), axis=1, keepdims=True)
    near = (key <= query) & (segment == own)
    real = pad_ref[...] == 1
    for recursion, ref in enumerate(select_refs):
        place = lax.broadcasted_iota(jnp.int32, (seq_len, ref.shape[1]), 0)
        active = jnp.max(jnp.where(ref[...] == place, 1.0, 0.0), axis=1, keepdims=True)
        active_ref[recursion] = active
        along = jnp.sum(jnp.where(diagonal, active, 0.0), axis=0, keepdims=True)
        usable = (along > 0.0) & real
        bias_ref[recursion] = jnp.where(near & (usable | diagonal), 0.0, -1e30)


def first_attention(x_ref, sel_one, sel_two, sel_three, segment_ref, pad_ref, cos_ref, sin_ref, gain_one, gain_two, qkv_w, out_w,
                    n1_ref, q_ref, kz_ref, vz_ref, p_ref, o_ref, attn_ref, n2_ref, bias_ref, active_ref):
    n1, o = n1_ref.at[0], o_ref.at[0]
    masks((sel_one, sel_two, sel_three), segment_ref, pad_ref, bias_ref, active_ref)
    attention_forward(x_ref, bias_ref.at[0], cos_ref, sin_ref, gain_one[...], qkv_w, n1, q_ref, kz_ref, vz_ref, p_ref, o)
    attention_out(x_ref, o, out_w, gain_two[...], attn_ref, n2_ref)


def load_all(pairs, sems):
    copies = [pltpu.make_async_copy(src, dst, sems.at[i]) for i, (src, dst) in enumerate(pairs)]
    return copies


def forward_steps(x0_ref, attn0_ref, n20_ref, bias_ref, active_ref, router_ref, cos_ref, sin_ref, gain_one, gain_two,
                  n1_in, o_in, qkv_hbm, out_hbm, *rest):
    feed_hbm, rest = rest[:6], rest[6:]
    (n1_ref, o_ref, q_ref, kz_ref, vz_ref, p_ref, x_ref, a_ref, branch_ref, n2_ref,
     m0, m1, slope0, slope1, silu0, silu1, final_ref), rest = rest[:17], rest[17:]
    qkv_w, out_w, w0, w1, w2, w3, w4, w5, state, attn, n2, total, sems = rest
    step = pl.program_id(0)
    copies = load_all(list(zip((*feed_hbm, qkv_hbm, out_hbm), (w0, w1, w2, w3, w4, w5, qkv_w, out_w))), sems)

    @pl.when(step == 0)
    def _():
        for copy in copies:
            copy.start()
        state[...] = x0_ref[...]
        attn[...] = attn0_ref[...]
        n2[...] = n20_ref[...]
        for copy in copies[:6]:
            copy.wait()

    n2_ref[0] = n2[...]
    feed_forward(n2, ((w0, w1, w2, m0.at[0], slope0.at[0], silu0.at[0]), (w3, w4, w5, m1.at[0], slope1.at[0], silu1.at[0])), total)
    router_row = router_ref[pl.ds(step, 1), :]

    def finish(rows):
        x, attn_rows = state[rows, :], attn[rows, :]
        x_ref[0, rows, :] = x
        a_ref[0, rows, :] = x + attn_rows
        branch = attn_rows + total[rows, :].astype(BF).astype(F32)
        branch_ref[0, rows, :] = branch
        new = jnp.where(active_ref[0, rows, :] > 0, x + router_gate(x, router_row) * branch, x)
        state[rows, :] = new
        final_ref[rows, :] = new

    over_rows(state.shape[0], finish)

    @pl.when(step == 0)
    def _():
        for copy in copies[6:]:
            copy.wait()

    @pl.when(step < RECURSIONS - 1)
    def _():
        attention_forward(state, bias_ref.at[0], cos_ref, sin_ref, gain_one[...], qkv_w,
                          n1_ref.at[0], q_ref.at[0], kz_ref.at[0], vz_ref.at[0], p_ref.at[0], o_ref.at[0])
        attention_out(state, o_ref.at[0], out_w, gain_two[...], attn, n2)


def finish_attention_backward(x_ref, gain, active_ref, du_ref, qkv_w, base, state, total, out_ref):
    total[...] = contract_last(du_ref[...], qkv_w[...])
    terms = jnp.zeros((1, state.shape[1]), F32)

    def lap(i, terms):
        rows = pl.ds(pl.multiple_of(i * ROWS, ROWS), ROWS)
        d_rows, term = norm_back(x_ref[rows, :], gain, total[rows, :])
        new = jnp.where(active_ref[rows, :] > 0, base[rows, :] + d_rows, state[rows, :])
        out_ref[rows, :] = new
        return terms + term

    return lax.fori_loop(0, state.shape[0] // ROWS, lap, terms)


def backward_steps(d_hidden_ref, active_ref, router_ref, cos_ref, sin_ref, gain_one, gain_two,
                   x_ref, a_ref, branch_ref, slope0, slope1, silu0, silu1, q_ref, kz_ref, vz_ref, p_ref,
                   qkv_hbm, out_hbm, *rest):
    feed_hbm, rest = rest[:6], rest[6:]
    (df_ref, dg0, dg1, dw0, dw1, d_attn_ref, du_ref, base_ref, state_ref, small_ref), rest = rest[:10], rest[10:]
    qkv_w, out_w, w0, w1, w2, w3, w4, w5, d_branch, total, do_ref, sems = rest
    step = pl.program_id(0)
    copies = load_all(list(zip(
        (feed_hbm[2], feed_hbm[0], feed_hbm[1], feed_hbm[5], feed_hbm[3], feed_hbm[4], out_hbm, qkv_hbm),
        (w2, w0, w1, w5, w3, w4, out_w, qkv_w))), sems)

    @pl.when(step == 0)
    def _():
        for copy in copies:
            copy.start()
        state_ref[...] = d_hidden_ref[...]
        small_ref[...] = jnp.zeros(small_ref.shape, F32)

    router_row = router_ref[pl.ds(RECURSIONS - 1 - step, 1), :]
    width = state_ref.shape[1]
    laps = state_ref.shape[0] // ROWS

    def enter(i, terms):
        rows = pl.ds(pl.multiple_of(i * ROWS, ROWS), ROWS)
        x = x_ref[0, rows, :]
        d_new = jnp.where(active_ref[0, rows, :] > 0, state_ref[rows, :], 0.0)
        gate = router_gate(x, router_row)
        d_gate = jnp.sum(d_new * branch_ref[0, rows, :], axis=-1, keepdims=True)
        d_logit = d_gate * gate * (1.0 - gate)
        spread = gate * d_new
        d_branch[rows, :] = spread
        df_ref[0, rows, :] = spread.astype(BF)
        base_ref[rows, :] = d_new + d_logit * router_row
        return terms + jnp.sum(d_logit * x, axis=0, keepdims=True)

    small_ref[pl.ds(2 + RECURSIONS - 1 - step, 1), :] = lax.fori_loop(0, laps, enter, jnp.zeros((1, width), F32))

    @pl.when(step == 0)
    def _():
        for copy in copies[:6]:
            copy.wait()

    feed_backward(df_ref.at[0], ((w0, w1, w2, slope0.at[0], silu0.at[0], dg0.at[0], dw0.at[0]),
                                 (w3, w4, w5, slope1.at[0], silu1.at[0], dg1.at[0], dw1.at[0])), total)

    def leave(i, terms):
        rows = pl.ds(pl.multiple_of(i * ROWS, ROWS), ROWS)
        d_after, term = norm_back(a_ref[0, rows, :], gain_two[...], total[rows, :].astype(BF).astype(F32))
        d_attn_ref[0, rows, :] = (d_branch[rows, :] + d_after).astype(BF)
        base_ref[rows, :] = base_ref[rows, :] + d_after
        return terms + term

    small_ref[1:2, :] = small_ref[1:2, :] + lax.fori_loop(0, laps, leave, jnp.zeros((1, width), F32))

    @pl.when(step == 0)
    def _():
        for copy in copies[6:]:
            copy.wait()

    @pl.when(step < RECURSIONS - 1)
    def _():
        attention_backward(d_attn_ref.at[0], out_w, qkv_w, cos_ref, sin_ref, q_ref.at[0], kz_ref.at[0], vz_ref.at[0],
                           p_ref.at[0], do_ref, du_ref.at[0])
        term = finish_attention_backward(x_ref.at[0], gain_one[...], active_ref.at[0], du_ref.at[0], qkv_w, base_ref, state_ref, total, state_ref)
        small_ref[0:1, :] = small_ref[0:1, :] + term


def last_attention(x_ref, active_ref, cos_ref, sin_ref, gain_one, q_ref, kz_ref, vz_ref, p_ref, d_attn_ref,
                   base_ref, state_ref, small_in, du_in, qkv_w, out_w, du_ref, d_input_ref, small_ref, do_ref, total):
    attention_backward(d_attn_ref.at[0], out_w, qkv_w, cos_ref, sin_ref, q_ref, kz_ref, vz_ref, p_ref, do_ref, du_ref.at[0])
    term = finish_attention_backward(x_ref.at[0], gain_one[...], active_ref.at[0], du_ref.at[0], qkv_w, base_ref, state_ref, total, d_input_ref)
    small_ref[...] = small_in[...]
    small_ref[0:1, :] = small_in[0:1, :] + term


def swap_dp(values_in, bit, n_dp):
    return lax.ppermute(values_in, "dp", [(i, i ^ (1 << bit)) for i in range(n_dp)])


def swap_mp(values_in):
    return lax.ppermute(values_in, "mp", [(0, 1), (1, 0)])


def halving(parts, order, n_dp, index):
    bits = n_dp.bit_length() - 1
    left = list(range(bits - 1, -1, -1))
    shape = parts.shape[1:]
    held = parts.reshape((2,) * bits + shape)
    for step, bit in enumerate(order):
        at = left.index(bit)
        upper = ((index >> bit) & 1) == 1
        low = lax.index_in_dim(held, 0, at, keepdims=False)
        high = lax.index_in_dim(held, 1, at, keepdims=False)
        keep, send = jnp.where(upper, high, low), jnp.where(upper, low, high)
        got = swap_dp(send, bit, n_dp)
        last = step == bits - 1
        total = keep.astype(F32) + got.astype(F32)
        held = total if last else total.astype(BF)
        left.remove(bit)
    return held


def orders_of(bits):
    rest = list(range(3, bits))
    if bits < 3:
        return [list(range(bits))] * 3
    return [[0, 1, 2] + rest, [1, 0, 2] + rest, [2, 0, 1] + rest]


def on_device(
    hidden_in,
    sel_one,
    sel_two,
    sel_three,
    segment_ids,
    pad_mask,
    qkv_weight,
    out_weight,
    gate_weight,
    up_weight,
    down_weight,
    norm_one,
    norm_two,
    router_weight,
    d_hidden,
):
    seq_len, width = hidden_in.shape
    n_dp, n_mp = lax.axis_size("dp"), lax.axis_size("mp")
    dp_index, mp_index = lax.axis_index("dp"), lax.axis_index("mp")
    cosine, sine = rotary_tables(seq_len)
    weights = [(gate_weight, up_weight, down_weight)]
    weights.append(tuple(swap_mp(w) for w in weights[0]))
    gain_one, gain_two = norm_one.reshape(1, width), norm_two.reshape(1, width)
    padded = CHUNKS * LANES
    units = gate_weight.shape[1]
    feed_weights = (*weights[0], *weights[1])

    def shape(*dims, dtype=BF):
        return jax.ShapeDtypeStruct(dims, dtype)

    def whole(*dims, **kw):
        return pl.BlockSpec(dims, lambda *_: (0,) * len(dims), **kw)

    anywhere = pl.BlockSpec(memory_space=pl.ANY)
    one = pl.Buffered(1)
    stack = RECURSIONS, seq_len
    heads = (2 * KV_HEADS, seq_len, LANES)
    square = (HEADS, seq_len, seq_len)
    n1, q, kz, vz, p, o, attn, n2, bias, active = pl.pallas_call(
        first_attention,
        grid=(1,),
        in_specs=[
            whole(seq_len, width), *[whole(*ref.shape) for ref in (sel_one, sel_two, sel_three, segment_ids, pad_mask)],
            whole(seq_len, LANES), whole(seq_len, LANES), whole(1, width), whole(1, width), whole(*qkv_weight.shape), whole(*out_weight.shape),
        ],
        out_specs=[
            whole(1, seq_len, width), whole(seq_len, padded), whole(*heads), whole(*heads), whole(*square),
            whole(1, seq_len, width), whole(seq_len, width), whole(seq_len, width), whole(RECURSIONS, seq_len, seq_len), whole(*stack, 1),
        ],
        out_shape=[
            shape(*stack, width), shape(seq_len, padded), shape(*heads), shape(*heads), shape(*square),
            shape(*stack, width), shape(seq_len, width, dtype=F32), shape(seq_len, width),
            shape(*stack, seq_len, dtype=F32), shape(*stack, 1, dtype=F32),
        ],
        compiler_params=pltpu.CompilerParams(vmem_limit_bytes=60 * MIB),
        cost_estimate=pl.CostEstimate(flops=2 * 10**9, bytes_accessed=12 * 10**6, transcendentals=600000),
        name="first_attention",
    )(hidden_in, sel_one, sel_two, sel_three, segment_ids, pad_mask, cosine, sine, gain_one, gain_two, qkv_weight, out_weight)
    attention_0 = (q, kz, vz, p)

    def at_step(*dims):
        return pl.BlockSpec((1, *dims), lambda r: (r,) + (0,) * len(dims))

    def next_step(*dims):
        return pl.BlockSpec((1, *dims), lambda r: (jnp.minimum(r + 1, RECURSIONS - 1),) + (0,) * len(dims))

    def next_pair(*dims):
        return pl.BlockSpec((1, *dims), lambda r: (jnp.minimum(r, RECURSIONS - 2),) + (0,) * len(dims))

    weight_scratch = [pltpu.VMEM(w.shape, BF) for w in (qkv_weight, out_weight, *feed_weights)]
    results = pl.pallas_call(
        forward_steps,
        grid=(RECURSIONS,),
        in_specs=[
            whole(seq_len, width, pipeline_mode=one), whole(seq_len, width, pipeline_mode=one), whole(seq_len, width, pipeline_mode=one),
            next_step(seq_len, seq_len), at_step(seq_len, 1), whole(RECURSIONS, width),
            whole(seq_len, LANES), whole(seq_len, LANES), whole(1, width), whole(1, width),
            anywhere, anywhere, *[anywhere] * 8,
        ],
        out_specs=[
            next_step(seq_len, width), next_step(seq_len, width), next_pair(seq_len, padded), next_pair(*heads), next_pair(*heads),
            next_pair(*square), *[at_step(seq_len, width)] * 4, *[at_step(seq_len, units)] * 6, whole(seq_len, width),
        ],
        out_shape=[
            shape(*stack, width), shape(*stack, width), shape(RECURSIONS - 1, seq_len, padded), shape(RECURSIONS - 1, *heads), shape(RECURSIONS - 1, *heads),
            shape(RECURSIONS - 1, *square), *[shape(*stack, width, dtype=F32)] * 3, shape(*stack, width), *[shape(*stack, units)] * 6,
            shape(seq_len, width, dtype=F32),
        ],
        scratch_shapes=[
            *weight_scratch,
            pltpu.VMEM((seq_len, width), F32), pltpu.VMEM((seq_len, width), F32), pltpu.VMEM((seq_len, width), BF), pltpu.VMEM((seq_len, width), F32),
            pltpu.SemaphoreType.DMA((8,)),
        ],
        input_output_aliases={10: 0, 11: 1},
        compiler_params=pltpu.CompilerParams(vmem_limit_bytes=60 * MIB),
        cost_estimate=pl.CostEstimate(flops=12 * 10**9, bytes_accessed=50 * 10**6, transcendentals=4 * 10**6),
        name="forward_steps",
    )(hidden_in, attn, n2, bias, active, router_weight, cosine, sine, gain_one, gain_two, n1, o, qkv_weight, out_weight, *feed_weights)
    n1, o, q, kz, vz, p, x, a, branch, n2, m0, m1, slope0, slope1, silu0, silu1, state = results

    def back_step(*dims):
        return pl.BlockSpec((1, *dims), lambda i: (RECURSIONS - 1 - i,) + (0,) * len(dims))

    def back_pair(*dims):
        return pl.BlockSpec((1, *dims), lambda i: (jnp.maximum(RECURSIONS - 2 - i, 0),) + (0,) * len(dims))

    def back_next(*dims):
        return pl.BlockSpec((1, *dims), lambda i: (jnp.maximum(RECURSIONS - 1 - i, 1),) + (0,) * len(dims))

    results = pl.pallas_call(
        backward_steps,
        grid=(RECURSIONS,),
        in_specs=[
            whole(seq_len, width, pipeline_mode=one), back_step(seq_len, 1), whole(RECURSIONS, width),
            whole(seq_len, LANES), whole(seq_len, LANES), whole(1, width), whole(1, width),
            *[back_step(seq_len, width)] * 3, *[back_step(seq_len, units)] * 4,
            back_pair(seq_len, padded), back_pair(*heads), back_pair(*heads), back_pair(*square),
            *[anywhere] * 8,
        ],
        out_specs=[
            back_step(seq_len, width), *[back_step(seq_len, units)] * 4, back_step(seq_len, width), back_next(seq_len, qkv_weight.shape[1]),
            whole(seq_len, width), whole(seq_len, width), whole(8, width),
        ],
        out_shape=[
            shape(*stack, width), *[shape(*stack, units)] * 4, shape(*stack, width), shape(*stack, qkv_weight.shape[1]),
            shape(seq_len, width, dtype=F32), shape(seq_len, width, dtype=F32), shape(8, width, dtype=F32),
        ],
        scratch_shapes=[
            *weight_scratch,
            pltpu.VMEM((seq_len, width), F32), pltpu.VMEM((seq_len, width), F32), pltpu.VMEM((seq_len, padded), BF),
            pltpu.SemaphoreType.DMA((8,)),
        ],
        compiler_params=pltpu.CompilerParams(vmem_limit_bytes=60 * MIB),
        cost_estimate=pl.CostEstimate(flops=11 * 10**9, bytes_accessed=50 * 10**6, transcendentals=4 * 10**6),
        name="backward_steps",
    )(d_hidden, active, router_weight, cosine, sine, gain_one, gain_two, x, a, branch, slope0, slope1, silu0, silu1, q, kz, vz, p,
      qkv_weight, out_weight, *feed_weights)
    d_feed, dg0, dg1, dw0, dw1, d_attn, du, base, grad_state, small = results

    du, grad_state, small = pl.pallas_call(
        last_attention,
        grid=(1,),
        in_specs=[
            whole(1, seq_len, width), whole(1, seq_len, 1), whole(seq_len, LANES), whole(seq_len, LANES), whole(1, width),
            whole(seq_len, padded), whole(*heads), whole(*heads), whole(*square), whole(1, seq_len, width),
            whole(seq_len, width), whole(seq_len, width), whole(8, width), anywhere, whole(*qkv_weight.shape), whole(*out_weight.shape),
        ],
        out_specs=[whole(1, seq_len, qkv_weight.shape[1]), whole(seq_len, width), whole(8, width)],
        out_shape=[shape(*stack, qkv_weight.shape[1]), shape(seq_len, width, dtype=F32), shape(8, width, dtype=F32)],
        scratch_shapes=[pltpu.VMEM((seq_len, padded), BF), pltpu.VMEM((seq_len, width), F32)],
        input_output_aliases={13: 0},
        compiler_params=pltpu.CompilerParams(vmem_limit_bytes=60 * MIB),
        cost_estimate=pl.CostEstimate(flops=3 * 10**9, bytes_accessed=14 * 10**6, transcendentals=10**5),
        name="last_attention",
    )(x, active, cosine, sine, gain_one, *attention_0, d_attn, base, grad_state, small, du, qkv_weight, out_weight)

    def rows_of(stacked):
        return stacked.reshape(-1, stacked.shape[-1])

    two, feed = rows_of(n2), rows_of(d_feed)
    sides = ((dg0, dw0, m0), (dg1, dw1, m1))
    bits = n_dp.bit_length() - 1

    def ffn_terms(side, columns):
        return jnp.concatenate(
            [
                contract_rows(left, rows_of(sides[side][which])[:, columns]).astype(BF)
                for which, left in enumerate((two, two, feed))
            ],
            axis=0,
        )

    orders = orders_of(bits)
    if 3 * width % n_dp == 0 and units % 1280 == 0:
        fifth = units // 5
        streams = [(orders[i], slice(j * fifth, (j + 1) * fifth)) for i, j in ((0, 0), (1, 1), (2, 2), (0, 3), (1, 4))]
        done = []
        for order, columns in streams:
            terms = ffn_terms(0, columns).astype(F32) + swap_mp(ffn_terms(1, columns)).astype(F32)
            done.append(halving(terms.astype(BF).reshape(n_dp, 3 * width // n_dp, fifth), order, n_dp, dp_index))
        ffn_flat = jnp.concatenate(done, axis=1).reshape(1, -1)
    else:
        terms = ffn_terms(0, slice(None)).astype(F32) + swap_mp(ffn_terms(1, slice(None))).astype(F32)
        terms = terms.astype(BF).reshape(n_dp, 3 * width * units // n_dp // 128, 128)
        ffn_flat = halving(terms, orders[0], n_dp, dp_index).reshape(1, -1)

    grad_qkv = contract_rows(rows_of(n1), rows_of(du)).astype(BF)
    grad_out = contract_rows(rows_of(o), rows_of(d_attn)).astype(BF)
    share = (grad_qkv.size + grad_out.size) // (n_dp * n_mp)
    attn = jnp.concatenate([grad_qkv.reshape(-1), grad_out.reshape(-1)]).reshape(n_dp, 2, share // 128, 128)
    keep = jnp.where(mp_index == 0, attn[:, 0], attn[:, 1])
    send = jnp.where(mp_index == 0, attn[:, 1], attn[:, 0])
    attn = (keep.astype(F32) + swap_mp(send).astype(F32)).astype(BF)
    cuts = [0, (share // 128) // 24 * 8, (share // 128) // 12 * 8, share // 128]
    attn_flat = jnp.concatenate(
        [halving(attn[:, a:b], order, n_dp, dp_index) for a, b, order in zip(cuts, cuts[1:], orders)], axis=0
    ).reshape(-1)

    small = small + swap_mp(small)
    for bit in range(bits):
        small = small + swap_dp(small, bit, n_dp)
    return (state, grad_state, attn_flat, ffn_flat, small[0], small[1], small[2 : 2 + RECURSIONS])


def solution(mesh):
    both = P(("dp", "mp"), None)
    in_specs = (
        both,
        both,
        both,
        both,
        both,
        both,
        P(),
        P(),
        P(None, "mp"),
        P(None, "mp"),
        P(None, "mp"),
        P(),
        P(),
        P(),
        both,
    )
    out_specs = (both, both, P(("dp", "mp")), P("mp", "dp"), P(), P(), P())
    return jax.shard_map(
        on_device, mesh=mesh, in_specs=in_specs, out_specs=out_specs, check_vma=False
    )
```

```python
import functools
import math

import jax
import jax.numpy as jnp
import numpy as np
from jax import lax
from jax.experimental import pallas as pl
from jax.experimental.pallas import tpu as pltpu
from jax.sharding import PartitionSpec as P

HEADS = 15
KV_HEADS = 5
HEAD_DIM = 64
RECURSIONS = 3
GROUPS = HEADS // KV_HEADS
EPS = 1e-05
BF = jnp.bfloat16
F32 = jnp.float32


LANES = 128
CHUNKS = -(-HEADS * HEAD_DIM // LANES)
ROWS = 32
BLOCK = 256
MIB = 1 << 20


def rotary_tables(seq_len):
    half = HEAD_DIM // 2
    frequency = np.float32(100000.0) ** (
        np.float32(-2.0) * np.arange(half, dtype=np.float32) / np.float32(HEAD_DIM)
    )
    angles = np.arange(seq_len, dtype=np.float32)[:, None] * frequency.astype(np.float32)
    cosine, sine = np.cos(angles), np.sin(angles)
    return (
        jnp.asarray(np.concatenate([cosine] * 4, axis=1), F32),
        jnp.asarray(np.concatenate([-sine, sine] * 2, axis=1), F32),
    )


def contract_rows(left, right):
    return lax.dot_general(left, right, (((0,), (0,)), ((), ())), preferred_element_type=F32)


def contract_last(left, right):
    return lax.dot_general(left, right, (((1,), (1,)), ((), ())), preferred_element_type=F32)


def plain(left, right):
    return jnp.dot(left, right, preferred_element_type=F32)


def inverse_rms(rows):
    return lax.rsqrt(jnp.mean(rows * rows, axis=-1, keepdims=True) + EPS)


def norm_back(rows, gain, d_out):
    inv = inverse_rms(rows)
    scaled = d_out * gain
    inner = jnp.mean(scaled * rows, axis=-1, keepdims=True)
    d_rows = inv * scaled - rows * (inv * inv * inv * inner)
    return d_rows, jnp.sum(d_out * rows * inv, axis=0, keepdims=True)


def lane_of(rows):
    return lax.broadcasted_iota(jnp.int32, (rows, LANES), 1)


def swapped(chunk):
    first = lane_of(chunk.shape[0]) % HEAD_DIM < HEAD_DIM // 2
    return jnp.where(first, pltpu.roll(chunk, LANES - 32, 1), pltpu.roll(chunk, 32, 1))


def other_half(chunk):
    return pltpu.roll(chunk, HEAD_DIM, 1)


def over_rows(count, body):
    def lap(i, carry):
        body(pl.ds(pl.multiple_of(i * ROWS, ROWS), ROWS))
        return carry

    lax.fori_loop(0, count // ROWS, lap, 0)


def attention_forward(x_ref, bias_ref, cos_ref, sin_ref, gain, qkv_w, n1_ref, q_ref, kz_ref, vz_ref, p_ref, o_ref):
    seq_len, width = x_ref.shape
    scale = 1.0 / math.sqrt(HEAD_DIM)

    def norm(rows):
        x = x_ref[rows, :]
        n1_ref[rows, :] = (x * inverse_rms(x) * gain).astype(BF)

    over_rows(seq_len, norm)
    lower = lane_of(seq_len) < HEAD_DIM
    n1 = n1_ref[...]

    def spread(ref, head, chunk, upper):
        flipped = other_half(chunk)
        here, there = (flipped, chunk) if upper else (chunk, flipped)
        ref[2 * head] = jnp.where(lower, here, 0.0).astype(BF)
        ref[2 * head + 1] = jnp.where(lower, 0.0, there).astype(BF)

    columns = qkv_w.shape[1]
    for start in range(0, columns, 2 * LANES):
        wide = plain(n1, qkv_w[:, start : min(start + 2 * LANES, columns)])
        for part in range(0, wide.shape[1], LANES):
            chunk = wide[:, part : part + LANES]
            if chunk.shape[1] < LANES:
                chunk = jnp.concatenate([chunk, jnp.zeros_like(chunk)], axis=1)
            at = (start + part) // LANES
            heads = (2 * at, 2 * at + 1)
            if heads[0] < HEADS + KV_HEADS:
                chunk = chunk * cos_ref[...] + swapped(chunk) * sin_ref[...]
                if heads[0] < HEADS:
                    q_ref[:, at * LANES : (at + 1) * LANES] = chunk.astype(BF)
            for upper, head in enumerate(heads):
                if HEADS <= head < HEADS + KV_HEADS:
                    spread(kz_ref, head - HEADS, chunk, upper)
                elif HEADS + KV_HEADS <= head < HEADS + 2 * KV_HEADS:
                    spread(vz_ref, head - HEADS - KV_HEADS, chunk, upper)

    for at in range(CHUNKS):
        query = q_ref[:, at * LANES : (at + 1) * LANES]
        total = None
        for upper in range(2):
            head = 2 * at + upper
            if head < HEADS:
                key = 2 * (head // GROUPS) + upper
                scores = contract_last(query, kz_ref[key]) * scale + bias_ref[...]
                top = jnp.max(scores, axis=-1, keepdims=True)
                exponent = jnp.exp(scores - top)
                share = pl.reciprocal(jnp.sum(exponent, axis=-1, keepdims=True))
                attend = (exponent * share).astype(BF)
                p_ref[head] = attend
                mixed = plain(attend, vz_ref[key])
                total = mixed if total is None else total + mixed
        stop = min(width, (at + 1) * LANES)
        o_ref[:, at * LANES : stop] = total[:, : stop - at * LANES].astype(BF)


def attention_out(x_ref, o_ref, out_w, gain, attn_ref, n2_ref):
    attn_ref[...] = plain(o_ref[...], out_w[...])

    def norm(rows):
        after = x_ref[rows, :] + attn_ref[rows, :]
        n2_ref[rows, :] = (after * inverse_rms(after) * gain).astype(BF)

    over_rows(x_ref.shape[0], norm)


def feed_forward(n2_ref, sides, f_ref):
    n2 = n2_ref[...]
    for side, (gate_w, up_w, down_w, m_ref, slope_ref, silu_ref) in enumerate(sides):
        for start in range(0, gate_w.shape[1], BLOCK):
            at = slice(start, start + BLOCK)
            g, u = plain(n2, gate_w[:, at]), plain(n2, up_w[:, at])
            s = jax.nn.sigmoid(g)
            silu = g * s
            m_ref[:, at] = (silu * u).astype(BF)
            slope_ref[:, at] = (u * s * (1.0 + g * (1.0 - s))).astype(BF)
            silu_ref[:, at] = silu.astype(BF)
        part = contract_last(m_ref[...], down_w[...])
        f_ref[...] = part if side == 0 else f_ref[...] + part


def feed_backward(df_ref, sides, d_two_ref):
    d_feed = df_ref[...]
    for side, (gate_w, up_w, down_w, slope_ref, silu_ref, dg_ref, du_ref) in enumerate(sides):
        for start in range(0, gate_w.shape[1], BLOCK):
            at = slice(start, start + BLOCK)
            d_hidden = plain(d_feed, down_w[:, at])
            dg_ref[:, at] = (d_hidden * slope_ref[:, at].astype(F32)).astype(BF)
            du_ref[:, at] = (d_hidden * silu_ref[:, at].astype(F32)).astype(BF)
        part = contract_last(dg_ref[...], gate_w[...]) + contract_last(du_ref[...], up_w[...])
        d_two_ref[...] = part if side == 0 else d_two_ref[...] + part


def attention_backward(d_attn_ref, out_w, qkv_w, cos_ref, sin_ref, q_ref, kz_ref, vz_ref, p_ref, do_ref, du_ref):
    seq_len, width = d_attn_ref.shape
    scale = 1.0 / math.sqrt(HEAD_DIM)
    do_ref[:, :width] = contract_last(d_attn_ref[...], out_w[...]).astype(BF)
    do_ref[:, width:] = jnp.zeros((seq_len, do_ref.shape[1] - width), BF)
    lower = lane_of(seq_len) < HEAD_DIM
    cosine, sine = cos_ref[...], sin_ref[...]

    def back(chunk):
        chunk = chunk * scale
        return chunk * cosine - swapped(chunk) * sine

    waiting, d_k, d_v = None, {}, {}
    sums = [[None, None], [None, None]]
    for at in range(CHUNKS):
        query, d_mixed = (ref[:, at * LANES : (at + 1) * LANES] for ref in (q_ref, do_ref))
        d_query = None
        for upper in range(2):
            head = 2 * at + upper
            if head >= HEADS:
                continue
            group = head // GROUPS
            key = 2 * group + upper
            attend = p_ref[head]
            d_attend = contract_last(d_mixed, vz_ref[key])
            soft = attend.astype(F32)
            weighted = soft * d_attend
            inner = jnp.sum(weighted, axis=-1, keepdims=True)
            d_scores = (weighted - soft * inner).astype(BF)
            part = plain(d_scores, kz_ref[key])
            d_query = part if d_query is None else d_query + part
            for which, term in ((0, contract_rows(d_scores, query)), (1, contract_rows(attend, d_mixed))):
                old = sums[which][upper]
                sums[which][upper] = term if old is None else old + term
            if head % GROUPS == GROUPS - 1:
                for which, store in ((0, d_k), (1, d_v)):
                    both = jnp.where(lower, sums[which][0], sums[which][1])
                    store[group] = both + other_half(both)
                sums = [[None, None], [None, None]]
        if at < CHUNKS - 1:
            du_ref[:, at * LANES : (at + 1) * LANES] = back(d_query).astype(BF)
        else:
            waiting = d_query
    tail = jnp.where(lower, waiting, d_k[0])
    du_ref[:, (CHUNKS - 1) * LANES : CHUNKS * LANES] = back(tail).astype(BF)
    for i in range(2):
        at = CHUNKS + i
        du_ref[:, at * LANES : (at + 1) * LANES] = back(jnp.where(lower, d_k[1 + 2 * i], d_k[2 + 2 * i])).astype(BF)
        at = CHUNKS + 2 + i
        du_ref[:, at * LANES : (at + 1) * LANES] = jnp.where(lower, d_v[2 * i], d_v[2 * i + 1]).astype(BF)
    at = CHUNKS + 4
    du_ref[:, at * LANES :] = d_v[4][:, : du_ref.shape[1] - at * LANES].astype(BF)


def router_gate(x, router_row):
    return jax.nn.sigmoid(jnp.sum(x * router_row, axis=-1, keepdims=True))


def masks(select_refs, segment_ref, pad_ref, bias_ref, active_ref):
    seq_len = segment_ref.shape[1]
    square = (seq_len, seq_len)
    query, key = (lax.broadcasted_iota(jnp.int32, square, axis) for axis in (0, 1))
    diagonal = query == key
    segment = segment_ref[...].astype(F32)
    own = jnp.sum(jnp.where(diagonal, segment, 0.0), axis=1, keepdims=True)
    near = (key <= query) & (segment == own)
    real = pad_ref[...] == 1
    for recursion, ref in enumerate(select_refs):
        place = lax.broadcasted_iota(jnp.int32, (seq_len, ref.shape[1]), 0)
        active = jnp.max(jnp.where(ref[...] == place, 1.0, 0.0), axis=1, keepdims=True)
        active_ref[recursion] = active
        along = jnp.sum(jnp.where(diagonal, active, 0.0), axis=0, keepdims=True)
        usable = (along > 0.0) & real
        bias_ref[recursion] = jnp.where(near & (usable | diagonal), 0.0, -1e30)


def first_attention(x_ref, sel_one, sel_two, sel_three, segment_ref, pad_ref, cos_ref, sin_ref, gain_one, gain_two, qkv_w, out_w,
                    n1_ref, q_ref, kz_ref, vz_ref, p_ref, o_ref, attn_ref, n2_ref, bias_ref, active_ref):
    n1, o = n1_ref.at[0], o_ref.at[0]
    masks((sel_one, sel_two, sel_three), segment_ref, pad_ref, bias_ref, active_ref)
    attention_forward(x_ref, bias_ref.at[0], cos_ref, sin_ref, gain_one[...], qkv_w, n1, q_ref, kz_ref, vz_ref, p_ref, o)
    attention_out(x_ref, o, out_w, gain_two[...], attn_ref, n2_ref)


def load_all(pairs, sems):
    copies = [pltpu.make_async_copy(src, dst, sems.at[i]) for i, (src, dst) in enumerate(pairs)]
    return copies


def forward_steps(x0_ref, attn0_ref, n20_ref, bias_ref, active_ref, router_ref, cos_ref, sin_ref, gain_one, gain_two,
                  n1_in, o_in, qkv_hbm, out_hbm, *rest):
    feed_hbm, rest = rest[:6], rest[6:]
    (n1_ref, o_ref, q_ref, kz_ref, vz_ref, p_ref, x_ref, a_ref, branch_ref, n2_ref,
     m0, m1, slope0, slope1, silu0, silu1, final_ref), rest = rest[:17], rest[17:]
    qkv_w, out_w, w0, w1, w2, w3, w4, w5, state, attn, n2, total, sems = rest
    step = pl.program_id(0)
    copies = load_all(list(zip((*feed_hbm, qkv_hbm, out_hbm), (w0, w1, w2, w3, w4, w5, qkv_w, out_w))), sems)

    @pl.when(step == 0)
    def _():
        for copy in copies:
            copy.start()
        state[...] = x0_ref[...]
        attn[...] = attn0_ref[...]
        n2[...] = n20_ref[...]
        for copy in copies[:6]:
            copy.wait()

    n2_ref[0] = n2[...]
    feed_forward(n2, ((w0, w1, w2, m0.at[0], slope0.at[0], silu0.at[0]), (w3, w4, w5, m1.at[0], slope1.at[0], silu1.at[0])), total)
    router_row = router_ref[pl.ds(step, 1), :]

    def finish(rows):
        x, attn_rows = state[rows, :], attn[rows, :]
        x_ref[0, rows, :] = x
        a_ref[0, rows, :] = x + attn_rows
        branch = attn_rows + total[rows, :].astype(BF).astype(F32)
        branch_ref[0, rows, :] = branch
        new = jnp.where(active_ref[0, rows, :] > 0, x + router_gate(x, router_row) * branch, x)
        state[rows, :] = new
        final_ref[rows, :] = new

    over_rows(state.shape[0], finish)

    @pl.when(step == 0)
    def _():
        for copy in copies[6:]:
            copy.wait()

    @pl.when(step < RECURSIONS - 1)
    def _():
        attention_forward(state, bias_ref.at[0], cos_ref, sin_ref, gain_one[...], qkv_w,
                          n1_ref.at[0], q_ref.at[0], kz_ref.at[0], vz_ref.at[0], p_ref.at[0], o_ref.at[0])
        attention_out(state, o_ref.at[0], out_w, gain_two[...], attn, n2)


def finish_attention_backward(x_ref, gain, active_ref, du_ref, qkv_w, base, state, total, out_ref):
    total[...] = contract_last(du_ref[...], qkv_w[...])
    terms = jnp.zeros((1, state.shape[1]), F32)

    def lap(i, terms):
        rows = pl.ds(pl.multiple_of(i * ROWS, ROWS), ROWS)
        d_rows, term = norm_back(x_ref[rows, :], gain, total[rows, :])
        new = jnp.where(active_ref[rows, :] > 0, base[rows, :] + d_rows, state[rows, :])
        out_ref[rows, :] = new
        return terms + term

    return lax.fori_loop(0, state.shape[0] // ROWS, lap, terms)


def backward_steps(d_hidden_ref, active_ref, router_ref, cos_ref, sin_ref, gain_one, gain_two,
                   x_ref, a_ref, branch_ref, slope0, slope1, silu0, silu1, q_ref, kz_ref, vz_ref, p_ref,
                   qkv_hbm, out_hbm, *rest):
    feed_hbm, rest = rest[:6], rest[6:]
    (df_ref, dg0, dg1, dw0, dw1, d_attn_ref, du_ref, base_ref, state_ref, small_ref), rest = rest[:10], rest[10:]
    qkv_w, out_w, w0, w1, w2, w3, w4, w5, d_branch, total, do_ref, sems = rest
    step = pl.program_id(0)
    copies = load_all(list(zip(
        (feed_hbm[2], feed_hbm[0], feed_hbm[1], feed_hbm[5], feed_hbm[3], feed_hbm[4], out_hbm, qkv_hbm),
        (w2, w0, w1, w5, w3, w4, out_w, qkv_w))), sems)

    @pl.when(step == 0)
    def _():
        for copy in copies:
            copy.start()
        state_ref[...] = d_hidden_ref[...]
        small_ref[...] = jnp.zeros(small_ref.shape, F32)

    router_row = router_ref[pl.ds(RECURSIONS - 1 - step, 1), :]
    width = state_ref.shape[1]
    laps = state_ref.shape[0] // ROWS

    def enter(i, terms):
        rows = pl.ds(pl.multiple_of(i * ROWS, ROWS), ROWS)
        x = x_ref[0, rows, :]
        d_new = jnp.where(active_ref[0, rows, :] > 0, state_ref[rows, :], 0.0)
        gate = router_gate(x, router_row)
        d_gate = jnp.sum(d_new * branch_ref[0, rows, :], axis=-1, keepdims=True)
        d_logit = d_gate * gate * (1.0 - gate)
        spread = gate * d_new
        d_branch[rows, :] = spread
        df_ref[0, rows, :] = spread.astype(BF)
        base_ref[rows, :] = d_new + d_logit * router_row
        return terms + jnp.sum(d_logit * x, axis=0, keepdims=True)

    small_ref[pl.ds(2 + RECURSIONS - 1 - step, 1), :] = lax.fori_loop(0, laps, enter, jnp.zeros((1, width), F32))

    @pl.when(step == 0)
    def _():
        for copy in copies[:6]:
            copy.wait()

    feed_backward(df_ref.at[0], ((w0, w1, w2, slope0.at[0], silu0.at[0], dg0.at[0], dw0.at[0]),
                                 (w3, w4, w5, slope1.at[0], silu1.at[0], dg1.at[0], dw1.at[0])), total)

    def leave(i, terms):
        rows = pl.ds(pl.multiple_of(i * ROWS, ROWS), ROWS)
        d_after, term = norm_back(a_ref[0, rows, :], gain_two[...], total[rows, :].astype(BF).astype(F32))
        d_attn_ref[0, rows, :] = (d_branch[rows, :] + d_after).astype(BF)
        base_ref[rows, :] = base_ref[rows, :] + d_after
        return terms + term

    small_ref[1:2, :] = small_ref[1:2, :] + lax.fori_loop(0, laps, leave, jnp.zeros((1, width), F32))

    @pl.when(step == 0)
    def _():
        for copy in copies[6:]:
            copy.wait()

    @pl.when(step < RECURSIONS - 1)
    def _():
        attention_backward(d_attn_ref.at[0], out_w, qkv_w, cos_ref, sin_ref, q_ref.at[0], kz_ref.at[0], vz_ref.at[0],
                           p_ref.at[0], do_ref, du_ref.at[0])
        term = finish_attention_backward(x_ref.at[0], gain_one[...], active_ref.at[0], du_ref.at[0], qkv_w, base_ref, state_ref, total, state_ref)
        small_ref[0:1, :] = small_ref[0:1, :] + term


def last_attention(x_ref, active_ref, cos_ref, sin_ref, gain_one, q_ref, kz_ref, vz_ref, p_ref, d_attn_ref,
                   base_ref, state_ref, small_in, du_in, qkv_w, out_w, token, du_ref, d_input_ref, small_ref, do_ref, total):
    attention_backward(d_attn_ref.at[0], out_w, qkv_w, cos_ref, sin_ref, q_ref, kz_ref, vz_ref, p_ref, do_ref, du_ref.at[0])
    term = finish_attention_backward(x_ref.at[0], gain_one[...], active_ref.at[0], du_ref.at[0], qkv_w, base_ref, state_ref, total, d_input_ref)
    small_ref[...] = small_in[...]
    small_ref[0:1, :] = small_in[0:1, :] + term


def swap_dp(values_in, bit, n_dp):
    return lax.ppermute(values_in, "dp", [(i, i ^ (1 << bit)) for i in range(n_dp)])


def swap_mp(values_in):
    return lax.ppermute(values_in, "mp", [(0, 1), (1, 0)])


def halving(parts, order, n_dp, index):
    bits = n_dp.bit_length() - 1
    left = list(range(bits - 1, -1, -1))
    shape = parts.shape[1:]
    held = parts.reshape((2,) * bits + shape)
    for step, bit in enumerate(order):
        at = left.index(bit)
        upper = ((index >> bit) & 1) == 1
        low = lax.index_in_dim(held, 0, at, keepdims=False)
        high = lax.index_in_dim(held, 1, at, keepdims=False)
        keep, send = jnp.where(upper, high, low), jnp.where(upper, low, high)
        got = swap_dp(send, bit, n_dp)
        last = step == bits - 1
        total = keep.astype(F32) + got.astype(F32)
        held = total if last else total.astype(BF)
        left.remove(bit)
    return held


def orders_of(bits):
    rest = list(range(3, bits))
    if bits < 3:
        return [list(range(bits))] * 3
    return [[0, 1, 2] + rest, [1, 0, 2] + rest, [2, 0, 1] + rest]


PART = 2 * LANES
FFN_ORDERS = ((0, 2, 3, 1), (1, 0, 2, 3), (0, 2, 3, 1), (2, 0, 1, 3), (1, 2, 3, 0))
ATTN_ORDERS = ((1, 0, 2, 3), (0, 1, 2, 3))
SCHEDULE = (
    "T0", "T1", "T2", "F0", "F1", "T3", "F2", "T4", "F3", "L", "F0", "F1",
    "F4", "A", "F2", "F3", "F0", "F1", "B", "F4", "F2", "F3", "F0", "F1",
    "A0", "A1", "F4", "F3", "F2", "A0", "A1", "F4", "A0", "A1",
)


def ffn_terms(n2_ref, df_ref, dg0, dg1, dw0, dw1, m0, m1, token, own_ref, far_ref, flat):
    rows = n2_ref.shape[1]
    wide = jnp.concatenate([dg0[...], dg1[...], dw0[...], dw1[...]], axis=1)
    first = contract_rows(n2_ref[...], wide)
    second = contract_rows(df_ref[...], jnp.concatenate([m0[...], m1[...]], axis=1))
    for side, out in ((0, own_ref), (1, far_ref)):
        for matrix, (terms, at) in enumerate(((first, side), (first, 2 + side), (second, side))):
            for c in range(2):
                start = at * PART + c * LANES
                flat[pl.ds(2 * rows * matrix + c, rows, stride=2), :] = terms[:, start : start + LANES]
        out[...] = flat[...].astype(BF)


def attn_terms(n1_ref, du_ref, o_ref, da_ref, token, own_ref, far_ref, terms, flat):
    width = n1_ref.shape[1]
    base = 0
    lower = lane_of(width // 2) < HEAD_DIM
    for left, right in ((n1_ref, du_ref), (o_ref, da_ref)):
        columns = right.shape[1]
        half = columns // LANES
        for start in range(0, columns, PART):
            stop = min(columns, start + PART)
            block = contract_rows(left[...], right[:, start:stop])
            if stop - start < PART:
                block = jnp.concatenate([block, jnp.zeros((width, PART - (stop - start)), F32)], axis=1)
            for part in range(0, stop - start, LANES):
                terms[(start + part) // LANES] = block[:, part : part + LANES]
        step = 2 * columns // LANES
        count = width // 2
        after = None
        for c in range(half + 1):
            even = terms[c, pl.ds(0, count, stride=2), :]
            odd = other_half(terms[c, pl.ds(1, count, stride=2), :])
            if c < half:
                flat[pl.ds(base + c, count, stride=step), :] = even
            else:
                flat[pl.ds(base + c, count, stride=step), :] = jnp.where(lower, even, first_odd)
            if c == 0:
                first_odd = odd
            else:
                flat[pl.ds(base + half + c, count, stride=step), :] = jnp.where(lower, after, odd)
            after = odd
        base += width * columns // LANES
    n_dp, share = own_ref.shape[0], own_ref.shape[1]
    mine = lax.axis_index("mp")
    for d in range(n_dp):
        own_ref[d] = flat[pl.ds(pl.multiple_of((2 * d + mine) * share, 8), share), :].astype(BF)
        far_ref[d] = flat[pl.ds(pl.multiple_of((2 * d + 1 - mine) * share, 8), share), :].astype(BF)


def fold(bit, with_small, *refs):
    kept, got, refs = refs[0], refs[1], refs[2:]
    if with_small:
        refs, small_out = refs[:-1], refs[-1]
        small_out[...] = refs[0][...] + refs[1][...]
    keep, send = refs[-2:]
    mine = (lax.axis_index("dp") >> bit) & 1
    for p in range(kept.shape[0]):
        for q in range(kept.shape[2]):
            keep[p, q] = (kept[p, mine, q].astype(F32) + got[p, mine, q].astype(F32)).astype(BF)
            send[p, q] = (kept[p, 1 - mine, q].astype(F32) + got[p, 1 - mine, q].astype(F32)).astype(BF)


def split_pair(bits, cut, own, far, small_own, small_got, token, keep0, send0, keep1, send1, small_out):
    small_out[...] = small_own[...] + small_got[...]
    index = lax.axis_index("dp")
    for bit, keep, send, at in ((bits[0], keep0, send0, 0), (bits[1], keep1, send1, 1)):
        mine = (index >> bit) & 1
        inner = 1 << bit
        for p in range(keep.shape[0]):
            for q in range(inner):
                for out, which in ((keep, mine), (send, 1 - mine)):
                    shard = p * 2 * inner + which * inner + q
                    total = own[shard].astype(F32) + far[shard].astype(F32)
                    out[p, q] = (total[:cut] if at == 0 else total[cut:]).astype(BF)


def finish_streams(count, *refs):
    feeds, refs = refs[: 2 * count], refs[2 * count :]
    attn, refs = refs[:4], refs[4:]
    small_a, small_b, ffn_out, attn_out, small_out, flat = refs
    rows = ffn_out.shape[0] // (2 * count)
    for i in range(count):
        flat[...] = feeds[2 * i][...].astype(F32) + feeds[2 * i + 1][...].astype(F32)
        for c in range(2):
            ffn_out[pl.ds(2 * i + c, rows, stride=2 * count), :] = flat[pl.ds(c, rows, stride=2), :]
    cut = attn[0].shape[0]
    attn_out[:cut, :] = attn[0][...].astype(F32) + attn[1][...].astype(F32)
    attn_out[cut:, :] = attn[2][...].astype(F32) + attn[3][...].astype(F32)
    small_out[...] = small_a[...] + small_b[...]


class Stream:
    def __init__(self, order, bits):
        self.order, self.left, self.done = order, list(range(bits - 1, -1, -1)), 0
        self.kept = self.got = None

    def shape_for(self, array):
        at = self.left.index(self.order[self.done])
        rows, lanes = array.shape[-2:]
        return (1 << at, 2, 1 << (len(self.left) - 1 - at), rows, lanes)

    def sent(self, kept, send, n_dp):
        bit = self.order[self.done]
        self.kept, self.got = kept, swap_dp(send, bit, n_dp)
        self.left.remove(bit)
        self.done += 1


def on_device(
    hidden_in,
    sel_one,
    sel_two,
    sel_three,
    segment_ids,
    pad_mask,
    qkv_weight,
    out_weight,
    gate_weight,
    up_weight,
    down_weight,
    norm_one,
    norm_two,
    router_weight,
    d_hidden,
):
    seq_len, width = hidden_in.shape
    n_dp, n_mp = lax.axis_size("dp"), lax.axis_size("mp")
    dp_index, mp_index = lax.axis_index("dp"), lax.axis_index("mp")
    cosine, sine = rotary_tables(seq_len)
    weights = [(gate_weight, up_weight, down_weight)]
    weights.append(tuple(swap_mp(w) for w in weights[0]))
    gain_one, gain_two = norm_one.reshape(1, width), norm_two.reshape(1, width)
    padded = CHUNKS * LANES
    units = gate_weight.shape[1]
    feed_weights = (*weights[0], *weights[1])

    def shape(*dims, dtype=BF):
        return jax.ShapeDtypeStruct(dims, dtype)

    def whole(*dims, **kw):
        return pl.BlockSpec(dims, lambda *_: (0,) * len(dims), **kw)

    anywhere = pl.BlockSpec(memory_space=pl.ANY)
    one = pl.Buffered(1)
    stack = RECURSIONS, seq_len
    heads = (2 * KV_HEADS, seq_len, LANES)
    square = (HEADS, seq_len, seq_len)
    n1, q, kz, vz, p, o, attn, n2, bias, active = pl.pallas_call(
        first_attention,
        grid=(1,),
        in_specs=[
            whole(seq_len, width), *[whole(*ref.shape) for ref in (sel_one, sel_two, sel_three, segment_ids, pad_mask)],
            whole(seq_len, LANES), whole(seq_len, LANES), whole(1, width), whole(1, width), whole(*qkv_weight.shape), whole(*out_weight.shape),
        ],
        out_specs=[
            whole(1, seq_len, width), whole(seq_len, padded), whole(*heads), whole(*heads), whole(*square),
            whole(1, seq_len, width), whole(seq_len, width), whole(seq_len, width), whole(RECURSIONS, seq_len, seq_len), whole(*stack, 1),
        ],
        out_shape=[
            shape(*stack, width), shape(seq_len, padded), shape(*heads), shape(*heads), shape(*square),
            shape(*stack, width), shape(seq_len, width, dtype=F32), shape(seq_len, width),
            shape(*stack, seq_len, dtype=F32), shape(*stack, 1, dtype=F32),
        ],
        compiler_params=pltpu.CompilerParams(vmem_limit_bytes=60 * MIB),
        cost_estimate=pl.CostEstimate(flops=2 * 10**9, bytes_accessed=12 * 10**6, transcendentals=600000),
        name="first_attention",
    )(hidden_in, sel_one, sel_two, sel_three, segment_ids, pad_mask, cosine, sine, gain_one, gain_two, qkv_weight, out_weight)
    attention_0 = (q, kz, vz, p)

    def at_step(*dims):
        return pl.BlockSpec((1, *dims), lambda r: (r,) + (0,) * len(dims))

    def next_step(*dims):
        return pl.BlockSpec((1, *dims), lambda r: (jnp.minimum(r + 1, RECURSIONS - 1),) + (0,) * len(dims))

    def next_pair(*dims):
        return pl.BlockSpec((1, *dims), lambda r: (jnp.minimum(r, RECURSIONS - 2),) + (0,) * len(dims))

    weight_scratch = [pltpu.VMEM(w.shape, BF) for w in (qkv_weight, out_weight, *feed_weights)]
    results = pl.pallas_call(
        forward_steps,
        grid=(RECURSIONS,),
        in_specs=[
            whole(seq_len, width, pipeline_mode=one), whole(seq_len, width, pipeline_mode=one), whole(seq_len, width, pipeline_mode=one),
            next_step(seq_len, seq_len), at_step(seq_len, 1), whole(RECURSIONS, width),
            whole(seq_len, LANES), whole(seq_len, LANES), whole(1, width), whole(1, width),
            anywhere, anywhere, *[anywhere] * 8,
        ],
        out_specs=[
            next_step(seq_len, width), next_step(seq_len, width), next_pair(seq_len, padded), next_pair(*heads), next_pair(*heads),
            next_pair(*square), *[at_step(seq_len, width)] * 4, *[at_step(seq_len, units)] * 6, whole(seq_len, width),
        ],
        out_shape=[
            shape(*stack, width), shape(*stack, width), shape(RECURSIONS - 1, seq_len, padded), shape(RECURSIONS - 1, *heads), shape(RECURSIONS - 1, *heads),
            shape(RECURSIONS - 1, *square), *[shape(*stack, width, dtype=F32)] * 3, shape(*stack, width), *[shape(*stack, units)] * 6,
            shape(seq_len, width, dtype=F32),
        ],
        scratch_shapes=[
            *weight_scratch,
            pltpu.VMEM((seq_len, width), F32), pltpu.VMEM((seq_len, width), F32), pltpu.VMEM((seq_len, width), BF), pltpu.VMEM((seq_len, width), F32),
            pltpu.SemaphoreType.DMA((8,)),
        ],
        input_output_aliases={10: 0, 11: 1},
        compiler_params=pltpu.CompilerParams(vmem_limit_bytes=60 * MIB),
        cost_estimate=pl.CostEstimate(flops=12 * 10**9, bytes_accessed=50 * 10**6, transcendentals=4 * 10**6),
        name="forward_steps",
    )(hidden_in, attn, n2, bias, active, router_weight, cosine, sine, gain_one, gain_two, n1, o, qkv_weight, out_weight, *feed_weights)
    n1, o, q, kz, vz, p, x, a, branch, n2, m0, m1, slope0, slope1, silu0, silu1, state = results

    def back_step(*dims):
        return pl.BlockSpec((1, *dims), lambda i: (RECURSIONS - 1 - i,) + (0,) * len(dims))

    def back_pair(*dims):
        return pl.BlockSpec((1, *dims), lambda i: (jnp.maximum(RECURSIONS - 2 - i, 0),) + (0,) * len(dims))

    def back_next(*dims):
        return pl.BlockSpec((1, *dims), lambda i: (jnp.maximum(RECURSIONS - 1 - i, 1),) + (0,) * len(dims))

    results = pl.pallas_call(
        backward_steps,
        grid=(RECURSIONS,),
        in_specs=[
            whole(seq_len, width, pipeline_mode=one), back_step(seq_len, 1), whole(RECURSIONS, width),
            whole(seq_len, LANES), whole(seq_len, LANES), whole(1, width), whole(1, width),
            *[back_step(seq_len, width)] * 3, *[back_step(seq_len, units)] * 4,
            back_pair(seq_len, padded), back_pair(*heads), back_pair(*heads), back_pair(*square),
            *[anywhere] * 8,
        ],
        out_specs=[
            back_step(seq_len, width), *[back_step(seq_len, units)] * 4, back_step(seq_len, width), back_next(seq_len, qkv_weight.shape[1]),
            whole(seq_len, width), whole(seq_len, width), whole(8, width),
        ],
        out_shape=[
            shape(*stack, width), *[shape(*stack, units)] * 4, shape(*stack, width), shape(*stack, qkv_weight.shape[1]),
            shape(seq_len, width, dtype=F32), shape(seq_len, width, dtype=F32), shape(8, width, dtype=F32),
        ],
        scratch_shapes=[
            *weight_scratch,
            pltpu.VMEM((seq_len, width), F32), pltpu.VMEM((seq_len, width), F32), pltpu.VMEM((seq_len, padded), BF),
            pltpu.SemaphoreType.DMA((8,)),
        ],
        compiler_params=pltpu.CompilerParams(vmem_limit_bytes=60 * MIB),
        cost_estimate=pl.CostEstimate(flops=11 * 10**9, bytes_accessed=50 * 10**6, transcendentals=4 * 10**6),
        name="backward_steps",
    )(d_hidden, active, router_weight, cosine, sine, gain_one, gain_two, x, a, branch, slope0, slope1, silu0, silu1, q, kz, vz, p,
      qkv_weight, out_weight, *feed_weights)
    d_feed, dg0, dg1, dw0, dw1, d_attn, du, base, grad_state, small = results

    def run_last(token):
        return pl.pallas_call(
            last_attention,
            grid=(1,),
            in_specs=[
                whole(1, seq_len, width), whole(1, seq_len, 1), whole(seq_len, LANES), whole(seq_len, LANES), whole(1, width),
                whole(seq_len, padded), whole(*heads), whole(*heads), whole(*square), whole(1, seq_len, width),
                whole(seq_len, width), whole(seq_len, width), whole(8, width), anywhere, whole(*qkv_weight.shape), whole(*out_weight.shape), anywhere,
            ],
            out_specs=[whole(1, seq_len, qkv_weight.shape[1]), whole(seq_len, width), whole(8, width)],
            out_shape=[shape(*stack, qkv_weight.shape[1]), shape(seq_len, width, dtype=F32), shape(8, width, dtype=F32)],
            scratch_shapes=[pltpu.VMEM((seq_len, padded), BF), pltpu.VMEM((seq_len, width), F32)],
            input_output_aliases={13: 0},
            compiler_params=pltpu.CompilerParams(vmem_limit_bytes=60 * MIB),
            cost_estimate=pl.CostEstimate(flops=1, bytes_accessed=1, transcendentals=0),
            name="last_attention",
        )(x, active, cosine, sine, gain_one, *attention_0, d_attn, base, grad_state, small, du, qkv_weight, out_weight, token)

    def rows_of(stacked):
        return stacked.reshape(-1, stacked.shape[-1])

    two, feed = rows_of(n2), rows_of(d_feed)
    sides = ((dg0, dw0, m0), (dg1, dw1, m1))
    bits = n_dp.bit_length() - 1
    share = (qkv_weight.size + out_weight.size) // (n_dp * n_mp)
    if bits == 4 and 3 * width % n_dp == 0 and units == len(FFN_ORDERS) * PART and share % (8 * LANES) == 0:
        factors = [rows_of(t) for t in (n2, d_feed, dg0, dg1, dw0, dw1, m0, m1)]
        streams = [Stream(order, bits) for order in FFN_ORDERS]
        pair = [Stream(order, bits) for order in ATTN_ORDERS]
        flat_rows = 3 * width * 2
        cut = share // LANES // 2 // 16 * 16
        params = pltpu.CompilerParams(vmem_limit_bytes=60 * MIB)
        short = pl.CostEstimate(flops=1, bytes_accessed=1, transcendentals=0)

        def terms_of(j, token):
            stream = streams[j]
            own, far = pl.pallas_call(
                ffn_terms,
                grid=(1,),
                in_specs=[whole(*factors[0].shape), whole(*factors[1].shape),
                          *[pl.BlockSpec((t.shape[0], PART), lambda i: (0, j)) for t in factors[2:]], anywhere],
                out_specs=[whole(flat_rows, LANES)] * 2,
                out_shape=[shape(flat_rows, LANES)] * 2,
                scratch_shapes=[pltpu.VMEM((flat_rows, LANES), F32)],
                compiler_params=params,
                cost_estimate=short,
                name=f"ffn_terms_{j}",
            )(*factors, token)
            stream.kept = own.reshape(n_dp, flat_rows // n_dp, LANES)
            stream.got = swap_mp(far).reshape(stream.kept.shape)
            return own

        def fold_stream(stream, token, smalls=()):
            bit = stream.order[stream.done]
            dims = stream.shape_for(stream.kept)
            halves = (dims[0], *dims[2:])
            outs = pl.pallas_call(
                functools.partial(fold, bit, bool(smalls)),
                grid=(1,),
                in_specs=[whole(*dims), whole(*dims), *[whole(*t.shape) for t in smalls], anywhere],
                out_specs=[whole(*halves)] * 2 + [whole(*t.shape) for t in smalls[:1]],
                out_shape=[shape(*halves)] * 2 + [shape(*t.shape, dtype=F32) for t in smalls[:1]],
                compiler_params=params,
                cost_estimate=short,
                name="fold_terms",
            )(stream.kept.reshape(dims), stream.got.reshape(dims), *smalls, token)
            stream.sent(outs[0], outs[1], n_dp)
            return outs

        token = small
        small_own = small_got = attn_own = attn_got = None
        for item in SCHEDULE:
            if item[0] == "T":
                token = terms_of(int(item[1:]), token)
            elif item[0] == "F":
                stream = streams[int(item[1:])]
                if stream.done < bits:
                    token = fold_stream(stream, token)[0]
            elif item == "L":
                du, grad_state, small = run_last(token)
                small_own, small_got = small, swap_mp(small)
                token = small
            elif item == "A":
                parts = (n_dp, share // LANES, LANES)
                attn_own, attn_far = pl.pallas_call(
                    attn_terms,
                    grid=(1,),
                    in_specs=[whole(*rows_of(t).shape) for t in (n1, du, o, d_attn)] + [anywhere],
                    out_specs=[whole(*parts)] * 2,
                    out_shape=[shape(*parts)] * 2,
                    scratch_shapes=[pltpu.VMEM((-(-du.shape[-1] // PART) * 2, width, LANES), F32),
                                    pltpu.VMEM((n_dp * 2 * parts[1], LANES), F32)],
                    compiler_params=pltpu.CompilerParams(vmem_limit_bytes=60 * MIB),
                    cost_estimate=short,
                    name="attn_terms",
                )(*[rows_of(t) for t in (n1, du, o, d_attn)], token)
                attn_got = swap_mp(attn_far)
                token = attn_own
            elif item == "B":
                dims = [(1 << (bits - 1 - t.order[0]), 1 << t.order[0], rows, LANES)
                        for t, rows in zip(pair, (cut, share // LANES - cut))]
                outs = pl.pallas_call(
                    functools.partial(split_pair, tuple(t.order[0] for t in pair), cut),
                    grid=(1,),
                    in_specs=[whole(*attn_own.shape)] * 2 + [whole(*small.shape)] * 2 + [anywhere],
                    out_specs=[whole(*dims[0])] * 2 + [whole(*dims[1])] * 2 + [whole(*small.shape)],
                    out_shape=[shape(*dims[0])] * 2 + [shape(*dims[1])] * 2 + [shape(*small.shape, dtype=F32)],
                    compiler_params=params,
                    cost_estimate=short,
                    name="split_attn",
                )(attn_own, attn_got, small_own, small_got, token)
                pair[0].sent(outs[0], outs[1], n_dp)
                pair[1].sent(outs[2], outs[3], n_dp)
                small_own, small_got = outs[4], swap_dp(outs[4], pair[0].order[0], n_dp)
                token = outs[4]
            else:
                which = int(item[1:])
                stream = pair[which]
                if which == 0:
                    bit = stream.order[stream.done]
                    outs = fold_stream(stream, token, (small_own, small_got))
                    small_own, small_got = outs[2], swap_dp(outs[2], bit, n_dp)
                else:
                    outs = fold_stream(stream, token)
                token = outs[0]
        ends = [t.reshape(t.shape[-2:]) for stream in (*streams, *pair) for t in (stream.kept, stream.got)]
        ffn_rows = flat_rows // n_dp * len(streams)
        ffn_flat, attn_flat, small = pl.pallas_call(
            functools.partial(finish_streams, len(streams)),
            grid=(1,),
            in_specs=[whole(*t.shape) for t in (*ends, small_own, small_got)],
            out_specs=[whole(ffn_rows, LANES), whole(share // LANES, LANES), whole(*small.shape)],
            out_shape=[shape(ffn_rows, LANES, dtype=F32), shape(share // LANES, LANES, dtype=F32), shape(*small.shape, dtype=F32)],
            scratch_shapes=[pltpu.VMEM((flat_rows // n_dp, LANES), F32)],
            compiler_params=params,
            cost_estimate=short,
            name="finish_streams",
        )(*ends, small_own, small_got)
        return (state, grad_state, attn_flat.reshape(-1), ffn_flat.reshape(1, -1), small[0], small[1], small[2 : 2 + RECURSIONS])

    du, grad_state, small = run_last(small)

    def side_terms(side, columns):
        return jnp.concatenate(
            [
                contract_rows(left, rows_of(sides[side][which])[:, columns]).astype(BF)
                for which, left in enumerate((two, two, feed))
            ],
            axis=0,
        )

    orders = orders_of(bits)
    if 3 * width % n_dp == 0 and units % 1280 == 0:
        fifth = units // 5
        streams = [(orders[i], slice(j * fifth, (j + 1) * fifth)) for i, j in ((0, 0), (1, 1), (2, 2), (0, 3), (1, 4))]
        done = []
        for order, columns in streams:
            terms = side_terms(0, columns).astype(F32) + swap_mp(side_terms(1, columns)).astype(F32)
            done.append(halving(terms.astype(BF).reshape(n_dp, 3 * width // n_dp, fifth), order, n_dp, dp_index))
        ffn_flat = jnp.concatenate(done, axis=1).reshape(1, -1)
    else:
        terms = side_terms(0, slice(None)).astype(F32) + swap_mp(side_terms(1, slice(None))).astype(F32)
        terms = terms.astype(BF).reshape(n_dp, 3 * width * units // n_dp // 128, 128)
        ffn_flat = halving(terms, orders[0], n_dp, dp_index).reshape(1, -1)

    grad_qkv = contract_rows(rows_of(n1), rows_of(du)).astype(BF)
    grad_out = contract_rows(rows_of(o), rows_of(d_attn)).astype(BF)
    attn = jnp.concatenate([grad_qkv.reshape(-1), grad_out.reshape(-1)]).reshape(n_dp, 2, share // 128, 128)
    keep = jnp.where(mp_index == 0, attn[:, 0], attn[:, 1])
    send = jnp.where(mp_index == 0, attn[:, 1], attn[:, 0])
    attn = (keep.astype(F32) + swap_mp(send).astype(F32)).astype(BF)
    cuts = [0, (share // 128) // 24 * 8, (share // 128) // 12 * 8, share // 128]
    attn_flat = jnp.concatenate(
        [halving(attn[:, a:b], order, n_dp, dp_index) for a, b, order in zip(cuts, cuts[1:], orders)], axis=0
    ).reshape(-1)

    small = small + swap_mp(small)
    for bit in range(bits):
        small = small + swap_dp(small, bit, n_dp)
    return (state, grad_state, attn_flat, ffn_flat, small[0], small[1], small[2 : 2 + RECURSIONS])


def solution(mesh):
    both = P(("dp", "mp"), None)
    in_specs = (
        both,
        both,
        both,
        both,
        both,
        both,
        P(),
        P(),
        P(None, "mp"),
        P(None, "mp"),
        P(None, "mp"),
        P(),
        P(),
        P(),
        both,
    )
    out_specs = (both, both, P(("dp", "mp")), P("mp", "dp"), P(), P(), P())
    return jax.shard_map(
        on_device, mesh=mesh, in_specs=in_specs, out_specs=out_specs, check_vma=False
    )
```

```python
import functools
import math

import jax
import jax.numpy as jnp
import numpy as np
from jax import lax
from jax.experimental import pallas as pl
from jax.experimental.pallas import tpu as pltpu
from jax.sharding import PartitionSpec as P

HEADS = 15
KV_HEADS = 5
HEAD_DIM = 64
RECURSIONS = 3
GROUPS = HEADS // KV_HEADS
EPS = 1e-05
BF = jnp.bfloat16
F32 = jnp.float32


LANES = 128
CHUNKS = -(-HEADS * HEAD_DIM // LANES)
ROWS = 32
BLOCK = 256
MIB = 1 << 20
VMEM_MIB = 63


def rotary_tables(seq_len):
    half = HEAD_DIM // 2
    frequency = np.float32(100000.0) ** (
        np.float32(-2.0) * np.arange(half, dtype=np.float32) / np.float32(HEAD_DIM)
    )
    angles = np.arange(seq_len, dtype=np.float32)[:, None] * frequency.astype(np.float32)
    cosine, sine = np.cos(angles), np.sin(angles)
    return (
        jnp.asarray(np.concatenate([cosine] * 4, axis=1), F32),
        jnp.asarray(np.concatenate([-sine, sine] * 2, axis=1), F32),
    )


def contract_rows(left, right):
    return lax.dot_general(left, right, (((0,), (0,)), ((), ())), preferred_element_type=F32)


def contract_last(left, right):
    return lax.dot_general(left, right, (((1,), (1,)), ((), ())), preferred_element_type=F32)


def plain(left, right):
    return jnp.dot(left, right, preferred_element_type=F32)


def inverse_rms(rows):
    return lax.rsqrt(jnp.mean(rows * rows, axis=-1, keepdims=True) + EPS)


def norm_back(rows, gain, d_out):
    inv = inverse_rms(rows)
    scaled = d_out * gain
    inner = jnp.mean(scaled * rows, axis=-1, keepdims=True)
    d_rows = inv * scaled - rows * (inv * inv * inv * inner)
    return d_rows, jnp.sum(d_out * rows * inv, axis=0, keepdims=True)


def lane_of(rows):
    return lax.broadcasted_iota(jnp.int32, (rows, LANES), 1)


def swapped(chunk):
    first = lane_of(chunk.shape[0]) % HEAD_DIM < HEAD_DIM // 2
    return jnp.where(first, pltpu.roll(chunk, LANES - 32, 1), pltpu.roll(chunk, 32, 1))


def other_half(chunk):
    return pltpu.roll(chunk, HEAD_DIM, 1)


def over_rows(count, body):
    def lap(i, carry):
        body(pl.ds(pl.multiple_of(i * ROWS, ROWS), ROWS))
        return carry

    lax.fori_loop(0, count // ROWS, lap, 0)


def attention_forward(x_ref, bias_ref, cos_ref, sin_ref, gain, qkv_w, n1_ref, q_ref, kz_ref, vz_ref, p_ref, o_ref):
    seq_len, width = x_ref.shape
    scale = 1.0 / math.sqrt(HEAD_DIM)

    def norm(rows):
        x = x_ref[rows, :]
        n1_ref[rows, :] = (x * inverse_rms(x) * gain).astype(BF)

    over_rows(seq_len, norm)
    lower = lane_of(seq_len) < HEAD_DIM
    n1 = n1_ref[...]

    def spread(ref, head, chunk, upper):
        flipped = other_half(chunk)
        here, there = (flipped, chunk) if upper else (chunk, flipped)
        ref[2 * head] = jnp.where(lower, here, 0.0).astype(BF)
        ref[2 * head + 1] = jnp.where(lower, 0.0, there).astype(BF)

    columns = qkv_w.shape[1]
    for start in range(0, columns, 2 * LANES):
        wide = plain(n1, qkv_w[:, start : min(start + 2 * LANES, columns)])
        for part in range(0, wide.shape[1], LANES):
            chunk = wide[:, part : part + LANES]
            if chunk.shape[1] < LANES:
                chunk = jnp.concatenate([chunk, jnp.zeros_like(chunk)], axis=1)
            at = (start + part) // LANES
            heads = (2 * at, 2 * at + 1)
            if heads[0] < HEADS + KV_HEADS:
                chunk = chunk * cos_ref[...] + swapped(chunk) * sin_ref[...]
                if heads[0] < HEADS:
                    q_ref[:, at * LANES : (at + 1) * LANES] = chunk.astype(BF)
            for upper, head in enumerate(heads):
                if HEADS <= head < HEADS + KV_HEADS:
                    spread(kz_ref, head - HEADS, chunk, upper)
                elif HEADS + KV_HEADS <= head < HEADS + 2 * KV_HEADS:
                    spread(vz_ref, head - HEADS - KV_HEADS, chunk, upper)

    for at in range(CHUNKS):
        query = q_ref[:, at * LANES : (at + 1) * LANES]
        total = None
        for upper in range(2):
            head = 2 * at + upper
            if head < HEADS:
                key = 2 * (head // GROUPS) + upper
                scores = contract_last(query, kz_ref[key]) * scale + bias_ref[...]
                top = jnp.max(scores, axis=-1, keepdims=True)
                exponent = jnp.exp(scores - top)
                share = pl.reciprocal(jnp.sum(exponent, axis=-1, keepdims=True))
                attend = (exponent * share).astype(BF)
                p_ref[head] = attend
                mixed = plain(attend, vz_ref[key])
                total = mixed if total is None else total + mixed
        stop = min(width, (at + 1) * LANES)
        o_ref[:, at * LANES : stop] = total[:, : stop - at * LANES].astype(BF)


def attention_out(x_ref, o_ref, out_w, gain, attn_ref, n2_ref):
    attn_ref[...] = plain(o_ref[...], out_w[...])

    def norm(rows):
        after = x_ref[rows, :] + attn_ref[rows, :]
        n2_ref[rows, :] = (after * inverse_rms(after) * gain).astype(BF)

    over_rows(x_ref.shape[0], norm)


def feed_forward(n2_ref, sides, f_ref):
    n2 = n2_ref[...]
    for side, (gate_w, up_w, down_w, m_ref, slope_ref, silu_ref) in enumerate(sides):
        for start in range(0, gate_w.shape[1], BLOCK):
            at = slice(start, start + BLOCK)
            g, u = plain(n2, gate_w[:, at]), plain(n2, up_w[:, at])
            s = jax.nn.sigmoid(g)
            silu = g * s
            m_ref[:, at] = (silu * u).astype(BF)
            slope_ref[:, at] = (u * s * (1.0 + g * (1.0 - s))).astype(BF)
            silu_ref[:, at] = silu.astype(BF)
        part = contract_last(m_ref[...], down_w[...])
        f_ref[...] = part if side == 0 else f_ref[...] + part


def feed_backward(df_ref, sides, d_two_ref):
    d_feed = df_ref[...]
    for side, (gate_w, up_w, down_w, slope_ref, silu_ref, dg_ref, du_ref) in enumerate(sides):
        for start in range(0, gate_w.shape[1], BLOCK):
            at = slice(start, start + BLOCK)
            d_hidden = plain(d_feed, down_w[:, at])
            dg_ref[:, at] = (d_hidden * slope_ref[:, at].astype(F32)).astype(BF)
            du_ref[:, at] = (d_hidden * silu_ref[:, at].astype(F32)).astype(BF)
        part = contract_last(dg_ref[...], gate_w[...]) + contract_last(du_ref[...], up_w[...])
        d_two_ref[...] = part if side == 0 else d_two_ref[...] + part


def attention_backward(d_attn_ref, out_w, qkv_w, cos_ref, sin_ref, q_ref, kz_ref, vz_ref, p_ref, do_ref, du_ref):
    seq_len, width = d_attn_ref.shape
    scale = 1.0 / math.sqrt(HEAD_DIM)
    do_ref[:, :width] = contract_last(d_attn_ref[...], out_w[...]).astype(BF)
    do_ref[:, width:] = jnp.zeros((seq_len, do_ref.shape[1] - width), BF)
    lower = lane_of(seq_len) < HEAD_DIM
    cosine, sine = cos_ref[...], sin_ref[...]

    def back(chunk):
        chunk = chunk * scale
        return chunk * cosine - swapped(chunk) * sine

    waiting, d_k, d_v = None, {}, {}
    sums = [[None, None], [None, None]]
    for at in range(CHUNKS):
        query, d_mixed = (ref[:, at * LANES : (at + 1) * LANES] for ref in (q_ref, do_ref))
        d_query = None
        for upper in range(2):
            head = 2 * at + upper
            if head >= HEADS:
                continue
            group = head // GROUPS
            key = 2 * group + upper
            attend = p_ref[head]
            d_attend = contract_last(d_mixed, vz_ref[key])
            soft = attend.astype(F32)
            weighted = soft * d_attend
            inner = jnp.sum(weighted, axis=-1, keepdims=True)
            d_scores = (weighted - soft * inner).astype(BF)
            part = plain(d_scores, kz_ref[key])
            d_query = part if d_query is None else d_query + part
            for which, term in ((0, contract_rows(d_scores, query)), (1, contract_rows(attend, d_mixed))):
                old = sums[which][upper]
                sums[which][upper] = term if old is None else old + term
            if head % GROUPS == GROUPS - 1:
                for which, store in ((0, d_k), (1, d_v)):
                    both = jnp.where(lower, sums[which][0], sums[which][1])
                    store[group] = both + other_half(both)
                sums = [[None, None], [None, None]]
        if at < CHUNKS - 1:
            du_ref[:, at * LANES : (at + 1) * LANES] = back(d_query).astype(BF)
        else:
            waiting = d_query
    tail = jnp.where(lower, waiting, d_k[0])
    du_ref[:, (CHUNKS - 1) * LANES : CHUNKS * LANES] = back(tail).astype(BF)
    for i in range(2):
        at = CHUNKS + i
        du_ref[:, at * LANES : (at + 1) * LANES] = back(jnp.where(lower, d_k[1 + 2 * i], d_k[2 + 2 * i])).astype(BF)
        at = CHUNKS + 2 + i
        du_ref[:, at * LANES : (at + 1) * LANES] = jnp.where(lower, d_v[2 * i], d_v[2 * i + 1]).astype(BF)
    at = CHUNKS + 4
    du_ref[:, at * LANES :] = d_v[4][:, : du_ref.shape[1] - at * LANES].astype(BF)


def router_gate(x, router_row):
    return jax.nn.sigmoid(jnp.sum(x * router_row, axis=-1, keepdims=True))


def masks(select_refs, segment_ref, pad_ref, bias_ref, active_ref):
    seq_len = segment_ref.shape[1]
    square = (seq_len, seq_len)
    query, key = (lax.broadcasted_iota(jnp.int32, square, axis) for axis in (0, 1))
    diagonal = query == key
    segment = segment_ref[...].astype(F32)
    own = jnp.sum(jnp.where(diagonal, segment, 0.0), axis=1, keepdims=True)
    near = (key <= query) & (segment == own)
    real = pad_ref[...] == 1
    for recursion, ref in enumerate(select_refs):
        place = lax.broadcasted_iota(jnp.int32, (seq_len, ref.shape[1]), 0)
        active = jnp.max(jnp.where(ref[...] == place, 1.0, 0.0), axis=1, keepdims=True)
        active_ref[recursion] = active
        along = jnp.sum(jnp.where(diagonal, active, 0.0), axis=0, keepdims=True)
        usable = (along > 0.0) & real
        bias_ref[recursion] = jnp.where(near & (usable | diagonal), 0.0, -1e30)


def first_attention(x_ref, sel_one, sel_two, sel_three, segment_ref, pad_ref, cos_ref, sin_ref, gain_one, gain_two, qkv_w, out_w,
                    n1_ref, q_ref, kz_ref, vz_ref, p_ref, o_ref, attn_ref, n2_ref, bias_ref, active_ref):
    n1, o = n1_ref.at[0], o_ref.at[0]
    masks((sel_one, sel_two, sel_three), segment_ref, pad_ref, bias_ref, active_ref)
    attention_forward(x_ref, bias_ref.at[0], cos_ref, sin_ref, gain_one[...], qkv_w, n1, q_ref, kz_ref, vz_ref, p_ref, o)
    attention_out(x_ref, o, out_w, gain_two[...], attn_ref, n2_ref)


def load_all(pairs, sems):
    copies = [pltpu.make_async_copy(src, dst, sems.at[i]) for i, (src, dst) in enumerate(pairs)]
    return copies


def forward_steps(x0_ref, attn0_ref, n20_ref, bias_ref, active_ref, router_ref, cos_ref, sin_ref, gain_one, gain_two,
                  n1_in, o_in, qkv_hbm, out_hbm, *rest):
    feed_hbm, rest = rest[:6], rest[6:]
    (n1_ref, o_ref, q_ref, kz_ref, vz_ref, p_ref, x_ref, a_ref, branch_ref, n2_ref,
     m0, m1, slope0, slope1, silu0, silu1, final_ref), rest = rest[:17], rest[17:]
    qkv_w, out_w, w0, w1, w2, w3, w4, w5, state, attn, n2, total, sems = rest
    step = pl.program_id(0)
    copies = load_all(list(zip((*feed_hbm, qkv_hbm, out_hbm), (w0, w1, w2, w3, w4, w5, qkv_w, out_w))), sems)

    @pl.when(step == 0)
    def _():
        for copy in copies:
            copy.start()
        state[...] = x0_ref[...]
        attn[...] = attn0_ref[...]
        n2[...] = n20_ref[...]
        for copy in copies[:6]:
            copy.wait()

    n2_ref[0] = n2[...]
    feed_forward(n2, ((w0, w1, w2, m0.at[0], slope0.at[0], silu0.at[0]), (w3, w4, w5, m1.at[0], slope1.at[0], silu1.at[0])), total)
    router_row = router_ref[pl.ds(step, 1), :]

    def finish(rows):
        x, attn_rows = state[rows, :], attn[rows, :]
        x_ref[0, rows, :] = x
        a_ref[0, rows, :] = x + attn_rows
        branch = attn_rows + total[rows, :].astype(BF).astype(F32)
        branch_ref[0, rows, :] = branch
        new = jnp.where(active_ref[0, rows, :] > 0, x + router_gate(x, router_row) * branch, x)
        state[rows, :] = new
        final_ref[rows, :] = new

    over_rows(state.shape[0], finish)

    @pl.when(step == 0)
    def _():
        for copy in copies[6:]:
            copy.wait()

    @pl.when(step < RECURSIONS - 1)
    def _():
        attention_forward(state, bias_ref.at[0], cos_ref, sin_ref, gain_one[...], qkv_w,
                          n1_ref.at[0], q_ref.at[0], kz_ref.at[0], vz_ref.at[0], p_ref.at[0], o_ref.at[0])
        attention_out(state, o_ref.at[0], out_w, gain_two[...], attn, n2)


def finish_attention_backward(x_ref, gain, active_ref, du_ref, qkv_w, base, state, total, out_ref):
    total[...] = contract_last(du_ref[...], qkv_w[...])
    terms = jnp.zeros((1, state.shape[1]), F32)

    def lap(i, terms):
        rows = pl.ds(pl.multiple_of(i * ROWS, ROWS), ROWS)
        d_rows, term = norm_back(x_ref[rows, :], gain, total[rows, :])
        new = jnp.where(active_ref[rows, :] > 0, base[rows, :] + d_rows, state[rows, :])
        out_ref[rows, :] = new
        return terms + term

    return lax.fori_loop(0, state.shape[0] // ROWS, lap, terms)


def backward_steps(d_hidden_ref, active_ref, router_ref, cos_ref, sin_ref, gain_one, gain_two,
                   x_ref, a_ref, branch_ref, slope0, slope1, silu0, silu1, q_ref, kz_ref, vz_ref, p_ref,
                   qkv_hbm, out_hbm, *rest):
    feed_hbm, rest = rest[:6], rest[6:]
    (df_ref, dg0, dg1, dw0, dw1, d_attn_ref, du_ref, base_ref, state_ref, small_ref), rest = rest[:10], rest[10:]
    qkv_w, out_w, w0, w1, w2, w3, w4, w5, d_branch, total, do_ref, sems = rest
    step = pl.program_id(0)
    copies = load_all(list(zip(
        (feed_hbm[2], feed_hbm[0], feed_hbm[1], feed_hbm[5], feed_hbm[3], feed_hbm[4], out_hbm, qkv_hbm),
        (w2, w0, w1, w5, w3, w4, out_w, qkv_w))), sems)

    @pl.when(step == 0)
    def _():
        for copy in copies:
            copy.start()
        state_ref[...] = d_hidden_ref[...]
        small_ref[...] = jnp.zeros(small_ref.shape, F32)

    router_row = router_ref[pl.ds(RECURSIONS - 1 - step, 1), :]
    width = state_ref.shape[1]
    laps = state_ref.shape[0] // ROWS

    def enter(i, terms):
        rows = pl.ds(pl.multiple_of(i * ROWS, ROWS), ROWS)
        x = x_ref[0, rows, :]
        d_new = jnp.where(active_ref[0, rows, :] > 0, state_ref[rows, :], 0.0)
        gate = router_gate(x, router_row)
        d_gate = jnp.sum(d_new * branch_ref[0, rows, :], axis=-1, keepdims=True)
        d_logit = d_gate * gate * (1.0 - gate)
        spread = gate * d_new
        d_branch[rows, :] = spread
        df_ref[0, rows, :] = spread.astype(BF)
        base_ref[rows, :] = d_new + d_logit * router_row
        return terms + jnp.sum(d_logit * x, axis=0, keepdims=True)

    small_ref[pl.ds(2 + RECURSIONS - 1 - step, 1), :] = lax.fori_loop(0, laps, enter, jnp.zeros((1, width), F32))

    @pl.when(step == 0)
    def _():
        for copy in copies[:6]:
            copy.wait()

    feed_backward(df_ref.at[0], ((w0, w1, w2, slope0.at[0], silu0.at[0], dg0.at[0], dw0.at[0]),
                                 (w3, w4, w5, slope1.at[0], silu1.at[0], dg1.at[0], dw1.at[0])), total)

    def leave(i, terms):
        rows = pl.ds(pl.multiple_of(i * ROWS, ROWS), ROWS)
        d_after, term = norm_back(a_ref[0, rows, :], gain_two[...], total[rows, :].astype(BF).astype(F32))
        d_attn_ref[0, rows, :] = (d_branch[rows, :] + d_after).astype(BF)
        base_ref[rows, :] = base_ref[rows, :] + d_after
        return terms + term

    small_ref[1:2, :] = small_ref[1:2, :] + lax.fori_loop(0, laps, leave, jnp.zeros((1, width), F32))

    @pl.when(step == 0)
    def _():
        for copy in copies[6:]:
            copy.wait()

    @pl.when(step < RECURSIONS - 1)
    def _():
        attention_backward(d_attn_ref.at[0], out_w, qkv_w, cos_ref, sin_ref, q_ref.at[0], kz_ref.at[0], vz_ref.at[0],
                           p_ref.at[0], do_ref, du_ref.at[0])
        term = finish_attention_backward(x_ref.at[0], gain_one[...], active_ref.at[0], du_ref.at[0], qkv_w, base_ref, state_ref, total, state_ref)
        small_ref[0:1, :] = small_ref[0:1, :] + term


def last_attention(x_ref, active_ref, cos_ref, sin_ref, gain_one, q_ref, kz_ref, vz_ref, p_ref, d_attn_ref,
                   base_ref, state_ref, small_in, du_in, qkv_w, out_w, token, du_ref, d_input_ref, small_ref, do_ref, total):
    attention_backward(d_attn_ref.at[0], out_w, qkv_w, cos_ref, sin_ref, q_ref, kz_ref, vz_ref, p_ref, do_ref, du_ref.at[0])
    term = finish_attention_backward(x_ref.at[0], gain_one[...], active_ref.at[0], du_ref.at[0], qkv_w, base_ref, state_ref, total, d_input_ref)
    small_ref[...] = small_in[...]
    small_ref[0:1, :] = small_in[0:1, :] + term


def swap_dp(values_in, bit, n_dp):
    return lax.ppermute(values_in, "dp", [(i, i ^ (1 << bit)) for i in range(n_dp)])


def swap_mp(values_in):
    return lax.ppermute(values_in, "mp", [(0, 1), (1, 0)])


def halving(parts, order, n_dp, index):
    bits = n_dp.bit_length() - 1
    left = list(range(bits - 1, -1, -1))
    shape = parts.shape[1:]
    held = parts.reshape((2,) * bits + shape)
    for step, bit in enumerate(order):
        at = left.index(bit)
        upper = ((index >> bit) & 1) == 1
        low = lax.index_in_dim(held, 0, at, keepdims=False)
        high = lax.index_in_dim(held, 1, at, keepdims=False)
        keep, send = jnp.where(upper, high, low), jnp.where(upper, low, high)
        got = swap_dp(send, bit, n_dp)
        last = step == bits - 1
        total = keep.astype(F32) + got.astype(F32)
        held = total if last else total.astype(BF)
        left.remove(bit)
    return held


def orders_of(bits):
    rest = list(range(3, bits))
    if bits < 3:
        return [list(range(bits))] * 3
    return [[0, 1, 2] + rest, [1, 0, 2] + rest, [2, 0, 1] + rest]


PART = 2 * LANES
FFN_TILES = (4, 4, 2)
FFN_ORDERS = ((0, 1, 2, 3), (1, 0, 2, 3), (3, 2, 0, 1))
ATTN_ORDERS = ((0, 1, 3, 2), (2, 3, 1, 0))
SCHEDULE = (
    "T0", "T1", "T2", "A",
    "F0", "F1", "F2", "A0", "A1",
    "F0", "F1", "F2", "A0", "A1",
    "F0", "F1", "F2", "A0", "A1",
)
SMALL = 64


def halves(bit, outs, index):
    mine = (index >> bit) & 1
    inner = 1 << bit
    for out, which in zip(outs, (mine, 1 - mine)):
        for p in range(out.shape[0]):
            for q in range(inner):
                yield out, p, q, p * 2 * inner + which * inner + q


def ffn_terms(bit, tiles, n2_a, n2_b, df_a, df_b, dg_a, dg_b, dw_a, dw_b, m_a, m_b, token, keep_ref, send_ref, flat):
    width = n2_a.shape[1]
    part = tiles * LANES
    first = contract_rows(n2_a[...], jnp.concatenate([dg_a[...], dw_a[...]], axis=1))
    first = first + contract_rows(n2_b[...], jnp.concatenate([dg_b[...], dw_b[...]], axis=1))
    second = contract_rows(df_a[...], m_a[...]) + contract_rows(df_b[...], m_b[...])
    for matrix, (terms, at) in enumerate(((first, 0), (first, part), (second, 0))):
        for c in range(tiles):
            start = at + c * LANES
            flat[pl.ds(tiles * width * matrix + c, width, stride=tiles), :] = terms[:, start : start + LANES]
    rows = keep_ref.shape[2]
    for out, p, q, shard in halves(bit, (keep_ref, send_ref), lax.axis_index("dp")):
        out[p, q] = flat[pl.ds(pl.multiple_of(shard * rows, 8), rows), :].astype(BF)


def small_rows(small):
    rest = -small.shape[1] % LANES
    small = jnp.concatenate([small, jnp.zeros((small.shape[0], rest), F32)], axis=1)
    return jnp.concatenate([small[:, at : at + LANES] for at in range(0, small.shape[1], LANES)], axis=0)


def split_small(small, ref, start):
    high = small.astype(BF)
    ref[start : start + SMALL, :] = high
    ref[start + SMALL : start + 2 * SMALL, :] = (small - high.astype(F32)).astype(BF)


def rounded_small(small):
    high = small.astype(BF)
    return high.astype(F32) + (small - high.astype(F32)).astype(BF).astype(F32)


def joined_small(ref, start):
    return ref[start : start + SMALL, :].astype(F32) + ref[start + SMALL : start + 2 * SMALL, :].astype(F32)


def attn_terms(bits, cut, n1_a, n1_b, du_a, du_b, o_a, o_b, da_a, da_b, small_a, small_b, token,
               keep0, send0, keep1, send1, small_out, terms, flat):
    width = n1_a.shape[1]
    base = 0
    lower = lane_of(width // 2) < HEAD_DIM
    for lefts, rights in (((n1_a, n1_b), (du_a, du_b)), ((o_a, o_b), (da_a, da_b))):
        columns = rights[0].shape[1]
        half = columns // LANES
        for start in range(0, columns, PART):
            stop = min(columns, start + PART)
            block = sum(contract_rows(left[...], right[:, start:stop]) for left, right in zip(lefts, rights))
            if stop - start < PART:
                block = jnp.concatenate([block, jnp.zeros((width, PART - (stop - start)), F32)], axis=1)
            for part in range(0, stop - start, LANES):
                terms[(start + part) // LANES] = block[:, part : part + LANES]
        step = 2 * columns // LANES
        count = width // 2
        after = first_odd = None
        for c in range(half + 1):
            even = terms[c, pl.ds(0, count, stride=2), :]
            odd = other_half(terms[c, pl.ds(1, count, stride=2), :])
            if c < half:
                flat[pl.ds(base + c, count, stride=step), :] = even
            else:
                flat[pl.ds(base + c, count, stride=step), :] = jnp.where(lower, even, first_odd)
            if c == 0:
                first_odd = odd
            else:
                flat[pl.ds(base + half + c, count, stride=step), :] = jnp.where(lower, after, odd)
            after = odd
        base += width * columns // LANES
    index, core = lax.axis_index("dp"), lax.axis_index("mp")
    total = rounded_small(small_rows(small_a[...])) + rounded_small(small_rows(small_b[...]))
    small_out[...] = total
    shards, depth = 2 * keep0.shape[0] * keep0.shape[1], cut + keep1.shape[2]
    split_small(total, send0, shards // 2 * cut)

    def rows_of_shard(shard, low, high):
        start = pl.multiple_of((2 * shard + core) * depth + low, 8)
        return flat[pl.ds(start, high - low), :].astype(BF)

    mine = (index >> bits[0]) & 1
    inner = 1 << bits[0]
    for p in range(keep0.shape[0]):
        for q in range(inner):
            shard = 2 * p * inner + q
            keep0[p, q] = rows_of_shard(shard + mine * inner, 0, cut)
            at = (p * inner + q) * cut
            send0[at : at + cut, :] = rows_of_shard(shard + (1 - mine) * inner, 0, cut)
    for out, p, q, shard in halves(bits[1], (keep1, send1), index):
        out[p, q] = rows_of_shard(shard, cut, depth)


def fold(bit, kept, got, token, keep, send):
    mine = (lax.axis_index("dp") >> bit) & 1
    for p in range(kept.shape[0]):
        for q in range(kept.shape[2]):
            for out, which in ((keep, mine), (send, 1 - mine)):
                out[p, q] = (kept[p, which, q].astype(F32) + got[p, which, q].astype(F32)).astype(BF)


def fold_small(bit, kept, got, small, token, keep, send, small_out):
    mine = (lax.axis_index("dp") >> bit) & 1
    outer, _, inner, rows, _ = kept.shape
    for p in range(outer):
        for q in range(inner):
            totals = []
            for which in (mine, 1 - mine):
                start = pl.multiple_of(((2 * p + which) * inner + q) * rows, 16)
                totals.append((kept[p, which, q].astype(F32) + got[pl.ds(start, rows), :].astype(F32)).astype(BF))
            keep[p, q] = totals[0]
            at = (p * inner + q) * rows
            send[at : at + rows, :] = totals[1]
    total = rounded_small(small[...]) + joined_small(got, 2 * outer * inner * rows)
    small_out[...] = total
    split_small(total, send, outer * inner * rows)


def finish_streams(tiles, *refs):
    count = len(tiles)
    feeds, refs = refs[: 2 * count], refs[2 * count :]
    attn, refs = refs[:4], refs[4:]
    small, ffn_out, attn_out, small_out, flat = refs
    every = sum(tiles)
    rows = ffn_out.shape[0] // every
    base = 0
    for i, wide in enumerate(tiles):
        flat[: rows * wide, :] = feeds[2 * i][...].astype(F32) + feeds[2 * i + 1][...].astype(F32)
        for c in range(wide):
            ffn_out[pl.ds(base + c, rows, stride=every), :] = flat[pl.ds(c, rows, stride=wide), :]
        base += wide
    cut = attn[0].shape[0]
    attn_out[:cut, :] = attn[0][...].astype(F32) + attn[1][:cut, :].astype(F32)
    attn_out[cut:, :] = attn[2][...].astype(F32) + attn[3][...].astype(F32)
    total = rounded_small(small[...]) + joined_small(attn[1], cut)
    width = small_out.shape[1]
    for at in range(0, width, LANES):
        stop = min(width, at + LANES)
        small_out[:, at:stop] = total[at // LANES * 8 : at // LANES * 8 + 8, : stop - at]


class Stream:
    def __init__(self, order, bits):
        self.order, self.left, self.done = order, list(range(bits - 1, -1, -1)), 0
        self.kept = self.got = None

    def shape_for(self, array):
        at = self.left.index(self.order[self.done])
        rows, lanes = array.shape[-2:]
        return (1 << at, 2, 1 << (len(self.left) - 1 - at), rows, lanes)

    def sent(self, kept, send, n_dp):
        bit = self.order[self.done]
        self.kept, self.got = kept, swap_dp(send, bit, n_dp)
        self.left.remove(bit)
        self.done += 1


def on_device(
    hidden_in,
    sel_one,
    sel_two,
    sel_three,
    segment_ids,
    pad_mask,
    qkv_weight,
    out_weight,
    gate_weight,
    up_weight,
    down_weight,
    norm_one,
    norm_two,
    router_weight,
    d_hidden,
):
    seq_len, width = hidden_in.shape
    n_dp, n_mp = lax.axis_size("dp"), lax.axis_size("mp")
    dp_index, mp_index = lax.axis_index("dp"), lax.axis_index("mp")
    cosine, sine = rotary_tables(seq_len)
    weights = [(gate_weight, up_weight, down_weight)]
    weights.append(tuple(swap_mp(w) for w in weights[0]))
    gain_one, gain_two = norm_one.reshape(1, width), norm_two.reshape(1, width)
    padded = CHUNKS * LANES
    units = gate_weight.shape[1]
    feed_weights = (*weights[0], *weights[1])

    def shape(*dims, dtype=BF):
        return jax.ShapeDtypeStruct(dims, dtype)

    def whole(*dims, **kw):
        return pl.BlockSpec(dims, lambda *_: (0,) * len(dims), **kw)

    anywhere = pl.BlockSpec(memory_space=pl.ANY)
    one = pl.Buffered(1)
    stack = RECURSIONS, seq_len
    heads = (2 * KV_HEADS, seq_len, LANES)
    square = (HEADS, seq_len, seq_len)
    n1, q, kz, vz, p, o, attn, n2, bias, active = pl.pallas_call(
        first_attention,
        grid=(1,),
        in_specs=[
            whole(seq_len, width), *[whole(*ref.shape) for ref in (sel_one, sel_two, sel_three, segment_ids, pad_mask)],
            whole(seq_len, LANES), whole(seq_len, LANES), whole(1, width), whole(1, width), whole(*qkv_weight.shape), whole(*out_weight.shape),
        ],
        out_specs=[
            whole(1, seq_len, width), whole(seq_len, padded), whole(*heads), whole(*heads), whole(*square),
            whole(1, seq_len, width), whole(seq_len, width), whole(seq_len, width), whole(RECURSIONS, seq_len, seq_len), whole(*stack, 1),
        ],
        out_shape=[
            shape(*stack, width), shape(seq_len, padded), shape(*heads), shape(*heads), shape(*square),
            shape(*stack, width), shape(seq_len, width, dtype=F32), shape(seq_len, width),
            shape(*stack, seq_len, dtype=F32), shape(*stack, 1, dtype=F32),
        ],
        compiler_params=pltpu.CompilerParams(vmem_limit_bytes=VMEM_MIB * MIB),
        cost_estimate=pl.CostEstimate(flops=2 * 10**9, bytes_accessed=12 * 10**6, transcendentals=600000),
        name="first_attention",
    )(hidden_in, sel_one, sel_two, sel_three, segment_ids, pad_mask, cosine, sine, gain_one, gain_two, qkv_weight, out_weight)
    attention_0 = (q, kz, vz, p)

    def at_step(*dims):
        return pl.BlockSpec((1, *dims), lambda r: (r,) + (0,) * len(dims))

    def next_step(*dims):
        return pl.BlockSpec((1, *dims), lambda r: (jnp.minimum(r + 1, RECURSIONS - 1),) + (0,) * len(dims))

    def next_pair(*dims):
        return pl.BlockSpec((1, *dims), lambda r: (jnp.minimum(r, RECURSIONS - 2),) + (0,) * len(dims))

    weight_scratch = [pltpu.VMEM(w.shape, BF) for w in (qkv_weight, out_weight, *feed_weights)]
    results = pl.pallas_call(
        forward_steps,
        grid=(RECURSIONS,),
        in_specs=[
            whole(seq_len, width, pipeline_mode=one), whole(seq_len, width, pipeline_mode=one), whole(seq_len, width, pipeline_mode=one),
            next_step(seq_len, seq_len), at_step(seq_len, 1), whole(RECURSIONS, width),
            whole(seq_len, LANES), whole(seq_len, LANES), whole(1, width), whole(1, width),
            anywhere, anywhere, *[anywhere] * 8,
        ],
        out_specs=[
            next_step(seq_len, width), next_step(seq_len, width), next_pair(seq_len, padded), next_pair(*heads), next_pair(*heads),
            next_pair(*square), *[at_step(seq_len, width)] * 4, *[at_step(seq_len, units)] * 6, whole(seq_len, width),
        ],
        out_shape=[
            shape(*stack, width), shape(*stack, width), shape(RECURSIONS - 1, seq_len, padded), shape(RECURSIONS - 1, *heads), shape(RECURSIONS - 1, *heads),
            shape(RECURSIONS - 1, *square), *[shape(*stack, width, dtype=F32)] * 3, shape(*stack, width), *[shape(*stack, units)] * 6,
            shape(seq_len, width, dtype=F32),
        ],
        scratch_shapes=[
            *weight_scratch,
            pltpu.VMEM((seq_len, width), F32), pltpu.VMEM((seq_len, width), F32), pltpu.VMEM((seq_len, width), BF), pltpu.VMEM((seq_len, width), F32),
            pltpu.SemaphoreType.DMA((8,)),
        ],
        input_output_aliases={10: 0, 11: 1},
        compiler_params=pltpu.CompilerParams(vmem_limit_bytes=VMEM_MIB * MIB),
        cost_estimate=pl.CostEstimate(flops=12 * 10**9, bytes_accessed=50 * 10**6, transcendentals=4 * 10**6),
        name="forward_steps",
    )(hidden_in, attn, n2, bias, active, router_weight, cosine, sine, gain_one, gain_two, n1, o, qkv_weight, out_weight, *feed_weights)
    n1, o, q, kz, vz, p, x, a, branch, n2, m0, m1, slope0, slope1, silu0, silu1, state = results

    def back_step(*dims):
        return pl.BlockSpec((1, *dims), lambda i: (RECURSIONS - 1 - i,) + (0,) * len(dims))

    def back_pair(*dims):
        return pl.BlockSpec((1, *dims), lambda i: (jnp.maximum(RECURSIONS - 2 - i, 0),) + (0,) * len(dims))

    def back_next(*dims):
        return pl.BlockSpec((1, *dims), lambda i: (jnp.maximum(RECURSIONS - 1 - i, 1),) + (0,) * len(dims))

    results = pl.pallas_call(
        backward_steps,
        grid=(RECURSIONS,),
        in_specs=[
            whole(seq_len, width, pipeline_mode=one), back_step(seq_len, 1), whole(RECURSIONS, width),
            whole(seq_len, LANES), whole(seq_len, LANES), whole(1, width), whole(1, width),
            *[back_step(seq_len, width)] * 3, *[back_step(seq_len, units)] * 4,
            back_pair(seq_len, padded), back_pair(*heads), back_pair(*heads), back_pair(*square),
            *[anywhere] * 8,
        ],
        out_specs=[
            back_step(seq_len, width), *[back_step(seq_len, units)] * 4, back_step(seq_len, width), back_next(seq_len, qkv_weight.shape[1]),
            whole(seq_len, width), whole(seq_len, width), whole(8, width),
        ],
        out_shape=[
            shape(*stack, width), *[shape(*stack, units)] * 4, shape(*stack, width), shape(*stack, qkv_weight.shape[1]),
            shape(seq_len, width, dtype=F32), shape(seq_len, width, dtype=F32), shape(8, width, dtype=F32),
        ],
        scratch_shapes=[
            *weight_scratch,
            pltpu.VMEM((seq_len, width), F32), pltpu.VMEM((seq_len, width), F32), pltpu.VMEM((seq_len, padded), BF),
            pltpu.SemaphoreType.DMA((8,)),
        ],
        compiler_params=pltpu.CompilerParams(vmem_limit_bytes=VMEM_MIB * MIB),
        cost_estimate=pl.CostEstimate(flops=11 * 10**9, bytes_accessed=50 * 10**6, transcendentals=4 * 10**6),
        name="backward_steps",
    )(d_hidden, active, router_weight, cosine, sine, gain_one, gain_two, x, a, branch, slope0, slope1, silu0, silu1, q, kz, vz, p,
      qkv_weight, out_weight, *feed_weights)
    d_feed, dg0, dg1, dw0, dw1, d_attn, du, base, grad_state, small = results

    def run_last(token):
        return pl.pallas_call(
            last_attention,
            grid=(1,),
            in_specs=[
                whole(1, seq_len, width), whole(1, seq_len, 1), whole(seq_len, LANES), whole(seq_len, LANES), whole(1, width),
                whole(seq_len, padded), whole(*heads), whole(*heads), whole(*square), whole(1, seq_len, width),
                whole(seq_len, width), whole(seq_len, width), whole(8, width), anywhere, whole(*qkv_weight.shape), whole(*out_weight.shape), anywhere,
            ],
            out_specs=[whole(1, seq_len, qkv_weight.shape[1]), whole(seq_len, width), whole(8, width)],
            out_shape=[shape(*stack, qkv_weight.shape[1]), shape(seq_len, width, dtype=F32), shape(8, width, dtype=F32)],
            scratch_shapes=[pltpu.VMEM((seq_len, padded), BF), pltpu.VMEM((seq_len, width), F32)],
            input_output_aliases={13: 0},
            compiler_params=pltpu.CompilerParams(vmem_limit_bytes=VMEM_MIB * MIB),
            cost_estimate=pl.CostEstimate(flops=1, bytes_accessed=1, transcendentals=0),
            name="last_attention",
        )(x, active, cosine, sine, gain_one, *attention_0, d_attn, base, grad_state, small, du, qkv_weight, out_weight, token)

    def rows_of(stacked):
        return stacked.reshape(-1, stacked.shape[-1])

    two, feed = rows_of(n2), rows_of(d_feed)
    sides = ((dg0, dw0, m0), (dg1, dw1, m1))
    bits = n_dp.bit_length() - 1
    share = (qkv_weight.size + out_weight.size) // (n_dp * n_mp)
    if bits == 4 and 3 * width % n_dp == 0 and units == sum(FFN_TILES) * LANES and share % (8 * LANES) == 0:
        crossed = [(t, swap_mp(far)) for t, far in
                   ((n2, n2), (d_feed, d_feed), (dg0, dg1), (dw0, dw1), (m0, m1))]
        factors = [rows_of(t) for both in crossed for t in both]
        streams = [Stream(order, bits) for order in FFN_ORDERS]
        pair = [Stream(order, bits) for order in ATTN_ORDERS]
        depth = share // LANES
        cut = depth // 2 // 16 * 16
        common = dict(
            grid=(1,),
            compiler_params=pltpu.CompilerParams(vmem_limit_bytes=VMEM_MIB * MIB),
            cost_estimate=pl.CostEstimate(flops=1, bytes_accessed=1, transcendentals=0),
        )

        def wholes(arrays):
            return [whole(*t.shape) for t in arrays]

        def terms_of(j, token):
            stream, tiles = streams[j], FFN_TILES[j]
            at = sum(FFN_TILES[:j]) // tiles
            bit = stream.order[0]
            dims = (1 << (bits - 1 - bit), 1 << bit, 3 * width // n_dp * tiles, LANES)
            columns = pl.BlockSpec((factors[4].shape[0], tiles * LANES), lambda i: (0, at))
            keep, send = pl.pallas_call(
                functools.partial(ffn_terms, bit, tiles),
                in_specs=[*wholes(factors[:4]), *[columns] * 6, anywhere],
                out_specs=[whole(*dims)] * 2,
                out_shape=[shape(*dims)] * 2,
                scratch_shapes=[pltpu.VMEM((3 * width * tiles, LANES), F32)],
                name=f"ffn_terms_{j}",
                **common,
            )(*factors, token)
            stream.sent(keep, send, n_dp)
            return keep

        def fold_stream(stream, token, small_own=None):
            bit = stream.order[stream.done]
            dims = stream.shape_for(stream.kept)
            kept = stream.kept.reshape(dims)
            held = (dims[0], *dims[2:])
            if small_own is None:
                operands = (kept, stream.got.reshape(dims))
                outs = (shape(*held), shape(*held))
            else:
                operands = (kept, stream.got, small_own)
                outs = (shape(*held), shape(dims[0] * dims[2] * dims[3] + 2 * SMALL, LANES), shape(SMALL, LANES, dtype=F32))
            results = pl.pallas_call(
                functools.partial(fold if small_own is None else fold_small, bit),
                in_specs=[*wholes(operands), anywhere],
                out_specs=wholes(outs),
                out_shape=outs,
                name="fold_terms",
                **common,
            )(*operands, token)
            stream.sent(results[0], results[1], n_dp)
            return results

        du, grad_state, small = run_last(small)
        first_crossed = [(rows_of(n1), swap_mp(rows_of(n1))), (rows_of(du), swap_mp(rows_of(du)))]
        late_crossed = [(rows_of(o), swap_mp(rows_of(o))), (rows_of(d_attn), swap_mp(rows_of(d_attn))), (small, swap_mp(small))]
        token = small
        for item in SCHEDULE:
            if item[0] == "T":
                token = terms_of(int(item[1:]), token)
            elif item[0] == "F":
                token = fold_stream(streams[int(item[1:])], token)[0]
            elif item == "A":
                firsts = [t.order[0] for t in pair]
                dims = [(1 << (bits - 1 - bit), 1 << bit, rows, LANES) for bit, rows in zip(firsts, (cut, depth - cut))]
                operands = [t for both in (*first_crossed, *late_crossed) for t in both]
                outs = (shape(*dims[0]), shape(n_dp // 2 * cut + 2 * SMALL, LANES), shape(*dims[1]), shape(*dims[1]),
                        shape(SMALL, LANES, dtype=F32))
                keep0, send0, keep1, send1, small_own = pl.pallas_call(
                    functools.partial(attn_terms, tuple(firsts), cut),
                    in_specs=[*wholes(operands), anywhere],
                    out_specs=wholes(outs),
                    out_shape=outs,
                    scratch_shapes=[pltpu.VMEM((-(-du.shape[-1] // PART) * 2, width, LANES), F32),
                                    pltpu.VMEM((n_dp * 2 * depth, LANES), F32)],
                    name="attn_terms",
                    **common,
                )(*operands, token)
                pair[0].sent(keep0, send0, n_dp)
                pair[1].sent(keep1, send1, n_dp)
                token = small_own
            elif item == "A0":
                token, _, small_own = fold_stream(pair[0], token, small_own)
            else:
                token = fold_stream(pair[1], token)[0]
        ends = [t.reshape(t.shape[-2:]) for stream in (*streams, *pair) for t in (stream.kept, stream.got)]
        outs = (shape(3 * width // n_dp * sum(FFN_TILES), LANES, dtype=F32), shape(depth, LANES, dtype=F32), shape(*small.shape, dtype=F32))
        ffn_flat, attn_flat, small = pl.pallas_call(
            functools.partial(finish_streams, FFN_TILES),
            in_specs=wholes((*ends, small_own)),
            out_specs=wholes(outs),
            out_shape=outs,
            scratch_shapes=[pltpu.VMEM((3 * width // n_dp * max(FFN_TILES), LANES), F32)],
            name="finish_streams",
            **common,
        )(*ends, small_own)
        return (state, grad_state, attn_flat.reshape(-1), ffn_flat.reshape(1, -1), small[0], small[1], small[2 : 2 + RECURSIONS])

    du, grad_state, small = run_last(small)

    def side_terms(side, columns):
        return jnp.concatenate(
            [
                contract_rows(left, rows_of(sides[side][which])[:, columns]).astype(BF)
                for which, left in enumerate((two, two, feed))
            ],
            axis=0,
        )

    orders = orders_of(bits)
    if 3 * width % n_dp == 0 and units % 1280 == 0:
        fifth = units // 5
        streams = [(orders[i], slice(j * fifth, (j + 1) * fifth)) for i, j in ((0, 0), (1, 1), (2, 2), (0, 3), (1, 4))]
        done = []
        for order, columns in streams:
            terms = side_terms(0, columns).astype(F32) + swap_mp(side_terms(1, columns)).astype(F32)
            done.append(halving(terms.astype(BF).reshape(n_dp, 3 * width // n_dp, fifth), order, n_dp, dp_index))
        ffn_flat = jnp.concatenate(done, axis=1).reshape(1, -1)
    else:
        terms = side_terms(0, slice(None)).astype(F32) + swap_mp(side_terms(1, slice(None))).astype(F32)
        terms = terms.astype(BF).reshape(n_dp, 3 * width * units // n_dp // 128, 128)
        ffn_flat = halving(terms, orders[0], n_dp, dp_index).reshape(1, -1)

    grad_qkv = contract_rows(rows_of(n1), rows_of(du)).astype(BF)
    grad_out = contract_rows(rows_of(o), rows_of(d_attn)).astype(BF)
    attn = jnp.concatenate([grad_qkv.reshape(-1), grad_out.reshape(-1)]).reshape(n_dp, 2, share // 128, 128)
    keep = jnp.where(mp_index == 0, attn[:, 0], attn[:, 1])
    send = jnp.where(mp_index == 0, attn[:, 1], attn[:, 0])
    attn = (keep.astype(F32) + swap_mp(send).astype(F32)).astype(BF)
    cuts = [0, (share // 128) // 24 * 8, (share // 128) // 12 * 8, share // 128]
    attn_flat = jnp.concatenate(
        [halving(attn[:, a:b], order, n_dp, dp_index) for a, b, order in zip(cuts, cuts[1:], orders)], axis=0
    ).reshape(-1)

    small = small + swap_mp(small)
    for bit in range(bits):
        small = small + swap_dp(small, bit, n_dp)
    return (state, grad_state, attn_flat, ffn_flat, small[0], small[1], small[2 : 2 + RECURSIONS])


def solution(mesh):
    both = P(("dp", "mp"), None)
    in_specs = (
        both,
        both,
        both,
        both,
        both,
        both,
        P(),
        P(),
        P(None, "mp"),
        P(None, "mp"),
        P(None, "mp"),
        P(),
        P(),
        P(),
        both,
    )
    out_specs = (both, both, P(("dp", "mp")), P("mp", "dp"), P(), P(), P())
    return jax.shard_map(
        on_device, mesh=mesh, in_specs=in_specs, out_specs=out_specs, check_vma=False
    )
```

```python
import functools
import math

import jax
import jax.numpy as jnp
import numpy as np
from jax import lax
from jax.experimental import pallas as pl
from jax.experimental.pallas import tpu as pltpu
from jax.sharding import PartitionSpec as P

HEADS = 15
KV_HEADS = 5
HEAD_DIM = 64
RECURSIONS = 3
GROUPS = HEADS // KV_HEADS
EPS = 1e-05
BF = jnp.bfloat16
F32 = jnp.float32


LANES = 128
CHUNKS = -(-HEADS * HEAD_DIM // LANES)
ROWS = 32
BLOCK = 256
MIB = 1 << 20
VMEM_MIB = 63


def rotary_tables(seq_len):
    half = HEAD_DIM // 2
    frequency = np.float32(100000.0) ** (
        np.float32(-2.0) * np.arange(half, dtype=np.float32) / np.float32(HEAD_DIM)
    )
    angles = np.arange(seq_len, dtype=np.float32)[:, None] * frequency.astype(np.float32)
    cosine, sine = np.cos(angles), np.sin(angles)
    return (
        jnp.asarray(np.concatenate([cosine] * 4, axis=1), F32),
        jnp.asarray(np.concatenate([-sine, sine] * 2, axis=1), F32),
    )


def contract_rows(left, right):
    return lax.dot_general(left, right, (((0,), (0,)), ((), ())), preferred_element_type=F32)


def contract_last(left, right):
    return lax.dot_general(left, right, (((1,), (1,)), ((), ())), preferred_element_type=F32)


def plain(left, right):
    return jnp.dot(left, right, preferred_element_type=F32)


def inverse_rms(rows):
    return lax.rsqrt(jnp.mean(rows * rows, axis=-1, keepdims=True) + EPS)


def norm_back(rows, gain, d_out):
    inv = inverse_rms(rows)
    scaled = d_out * gain
    inner = jnp.mean(scaled * rows, axis=-1, keepdims=True)
    d_rows = inv * scaled - rows * (inv * inv * inv * inner)
    return d_rows, jnp.sum(d_out * rows * inv, axis=0, keepdims=True)


def lane_of(rows):
    return lax.broadcasted_iota(jnp.int32, (rows, LANES), 1)


def swapped(chunk):
    first = lane_of(chunk.shape[0]) % HEAD_DIM < HEAD_DIM // 2
    return jnp.where(first, pltpu.roll(chunk, LANES - 32, 1), pltpu.roll(chunk, 32, 1))


def other_half(chunk):
    return pltpu.roll(chunk, HEAD_DIM, 1)


def over_rows(count, body):
    def lap(i, carry):
        body(pl.ds(pl.multiple_of(i * ROWS, ROWS), ROWS))
        return carry

    lax.fori_loop(0, count // ROWS, lap, 0)


def attention_forward(x_ref, bias_ref, cos_ref, sin_ref, gain, qkv_w, n1_ref, q_ref, kz_ref, vz_ref, p_ref, o_ref):
    seq_len, width = x_ref.shape
    scale = 1.0 / math.sqrt(HEAD_DIM)

    def norm(rows):
        x = x_ref[rows, :]
        n1_ref[rows, :] = (x * inverse_rms(x) * gain).astype(BF)

    over_rows(seq_len, norm)
    lower = lane_of(seq_len) < HEAD_DIM
    n1 = n1_ref[...]

    def spread(ref, head, chunk, upper):
        flipped = other_half(chunk)
        here, there = (flipped, chunk) if upper else (chunk, flipped)
        ref[2 * head] = jnp.where(lower, here, 0.0).astype(BF)
        ref[2 * head + 1] = jnp.where(lower, 0.0, there).astype(BF)

    columns = qkv_w.shape[1]
    for start in range(0, columns, 2 * LANES):
        wide = plain(n1, qkv_w[:, start : min(start + 2 * LANES, columns)])
        for part in range(0, wide.shape[1], LANES):
            chunk = wide[:, part : part + LANES]
            if chunk.shape[1] < LANES:
                chunk = jnp.concatenate([chunk, jnp.zeros_like(chunk)], axis=1)
            at = (start + part) // LANES
            heads = (2 * at, 2 * at + 1)
            if heads[0] < HEADS + KV_HEADS:
                chunk = chunk * cos_ref[...] + swapped(chunk) * sin_ref[...]
                if heads[0] < HEADS:
                    q_ref[:, at * LANES : (at + 1) * LANES] = chunk.astype(BF)
            for upper, head in enumerate(heads):
                if HEADS <= head < HEADS + KV_HEADS:
                    spread(kz_ref, head - HEADS, chunk, upper)
                elif HEADS + KV_HEADS <= head < HEADS + 2 * KV_HEADS:
                    spread(vz_ref, head - HEADS - KV_HEADS, chunk, upper)

    for at in range(CHUNKS):
        query = q_ref[:, at * LANES : (at + 1) * LANES]
        total = None
        for upper in range(2):
            head = 2 * at + upper
            if head < HEADS:
                key = 2 * (head // GROUPS) + upper
                scores = contract_last(query, kz_ref[key]) * scale + bias_ref[...]
                top = jnp.max(scores, axis=-1, keepdims=True)
                exponent = jnp.exp(scores - top)
                share = pl.reciprocal(jnp.sum(exponent, axis=-1, keepdims=True))
                attend = (exponent * share).astype(BF)
                p_ref[head] = attend
                mixed = plain(attend, vz_ref[key])
                total = mixed if total is None else total + mixed
        stop = min(width, (at + 1) * LANES)
        o_ref[:, at * LANES : stop] = total[:, : stop - at * LANES].astype(BF)


def attention_out(x_ref, o_ref, out_w, gain, attn_ref, n2_ref):
    attn_ref[...] = plain(o_ref[...], out_w[...])

    def norm(rows):
        after = x_ref[rows, :] + attn_ref[rows, :]
        n2_ref[rows, :] = (after * inverse_rms(after) * gain).astype(BF)

    over_rows(x_ref.shape[0], norm)


def feed_forward(n2_ref, sides, f_ref, ready):
    n2 = n2_ref[...]
    for side, (gate_w, up_w, down_w, m_ref, slope_ref, silu_ref) in enumerate(sides):
        ready(3 * side, 3 * side + 1)
        for start in range(0, gate_w.shape[1], BLOCK):
            at = slice(start, start + BLOCK)
            g, u = plain(n2, gate_w[:, at]), plain(n2, up_w[:, at])
            s = jax.nn.sigmoid(g)
            silu = g * s
            m_ref[:, at] = (silu * u).astype(BF)
            slope_ref[:, at] = (u * s * (1.0 + g * (1.0 - s))).astype(BF)
            silu_ref[:, at] = silu.astype(BF)
        ready(3 * side + 2)
        part = contract_last(m_ref[...], down_w[...])
        f_ref[...] = part if side == 0 else f_ref[...] + part


def feed_backward(df_ref, sides, d_two_ref, ready):
    d_feed = df_ref[...]
    for side, (gate_w, up_w, down_w, slope_ref, silu_ref, dg_ref, du_ref) in enumerate(sides):
        ready(3 * side)
        for start in range(0, gate_w.shape[1], BLOCK):
            at = slice(start, start + BLOCK)
            d_hidden = plain(d_feed, down_w[:, at])
            dg_ref[:, at] = (d_hidden * slope_ref[:, at].astype(F32)).astype(BF)
            du_ref[:, at] = (d_hidden * silu_ref[:, at].astype(F32)).astype(BF)
        ready(3 * side + 1, 3 * side + 2)
        part = contract_last(dg_ref[...], gate_w[...]) + contract_last(du_ref[...], up_w[...])
        d_two_ref[...] = part if side == 0 else d_two_ref[...] + part


def attention_backward(d_attn_ref, out_w, qkv_w, cos_ref, sin_ref, q_ref, kz_ref, vz_ref, p_ref, do_ref, du_ref):
    seq_len, width = d_attn_ref.shape
    scale = 1.0 / math.sqrt(HEAD_DIM)
    do_ref[:, :width] = contract_last(d_attn_ref[...], out_w[...]).astype(BF)
    do_ref[:, width:] = jnp.zeros((seq_len, do_ref.shape[1] - width), BF)
    lower = lane_of(seq_len) < HEAD_DIM
    cosine, sine = cos_ref[...], sin_ref[...]

    def back(chunk):
        chunk = chunk * scale
        return chunk * cosine - swapped(chunk) * sine

    waiting, d_k, d_v = None, {}, {}
    sums = [[None, None], [None, None]]
    for at in range(CHUNKS):
        query, d_mixed = (ref[:, at * LANES : (at + 1) * LANES] for ref in (q_ref, do_ref))
        d_query = None
        for upper in range(2):
            head = 2 * at + upper
            if head >= HEADS:
                continue
            group = head // GROUPS
            key = 2 * group + upper
            attend = p_ref[head]
            d_attend = contract_last(d_mixed, vz_ref[key])
            soft = attend.astype(F32)
            weighted = soft * d_attend
            inner = jnp.sum(weighted, axis=-1, keepdims=True)
            d_scores = (weighted - soft * inner).astype(BF)
            part = plain(d_scores, kz_ref[key])
            d_query = part if d_query is None else d_query + part
            for which, term in ((0, contract_rows(d_scores, query)), (1, contract_rows(attend, d_mixed))):
                old = sums[which][upper]
                sums[which][upper] = term if old is None else old + term
            if head % GROUPS == GROUPS - 1:
                for which, store in ((0, d_k), (1, d_v)):
                    both = jnp.where(lower, sums[which][0], sums[which][1])
                    store[group] = both + other_half(both)
                sums = [[None, None], [None, None]]
        if at < CHUNKS - 1:
            du_ref[:, at * LANES : (at + 1) * LANES] = back(d_query).astype(BF)
        else:
            waiting = d_query
    tail = jnp.where(lower, waiting, d_k[0])
    du_ref[:, (CHUNKS - 1) * LANES : CHUNKS * LANES] = back(tail).astype(BF)
    for i in range(2):
        at = CHUNKS + i
        du_ref[:, at * LANES : (at + 1) * LANES] = back(jnp.where(lower, d_k[1 + 2 * i], d_k[2 + 2 * i])).astype(BF)
        at = CHUNKS + 2 + i
        du_ref[:, at * LANES : (at + 1) * LANES] = jnp.where(lower, d_v[2 * i], d_v[2 * i + 1]).astype(BF)
    at = CHUNKS + 4
    du_ref[:, at * LANES :] = d_v[4][:, : du_ref.shape[1] - at * LANES].astype(BF)


def router_gate(x, router_row):
    return jax.nn.sigmoid(jnp.sum(x * router_row, axis=-1, keepdims=True))


def masks(select_refs, segment_ref, pad_ref, bias_ref, active_ref):
    seq_len = segment_ref.shape[1]
    square = (seq_len, seq_len)
    query, key = (lax.broadcasted_iota(jnp.int32, square, axis) for axis in (0, 1))
    diagonal = query == key
    segment = segment_ref[...].astype(F32)
    own = jnp.sum(jnp.where(diagonal, segment, 0.0), axis=1, keepdims=True)
    near = (key <= query) & (segment == own)
    real = pad_ref[...] == 1
    for recursion, ref in enumerate(select_refs):
        place = lax.broadcasted_iota(jnp.int32, (seq_len, ref.shape[1]), 0)
        active = jnp.max(jnp.where(ref[...] == place, 1.0, 0.0), axis=1, keepdims=True)
        active_ref[recursion] = active
        along = jnp.sum(jnp.where(diagonal, active, 0.0), axis=0, keepdims=True)
        usable = (along > 0.0) & real
        bias_ref[recursion] = jnp.where(near & (usable | diagonal), 0.0, -1e30)


def first_attention(x_ref, sel_one, sel_two, sel_three, segment_ref, pad_ref, cos_ref, sin_ref, gain_one, gain_two, qkv_w, out_w,
                    n1_ref, q_ref, kz_ref, vz_ref, p_ref, o_ref, attn_ref, n2_ref, bias_ref, active_ref):
    n1, o = n1_ref.at[0], o_ref.at[0]
    masks((sel_one, sel_two, sel_three), segment_ref, pad_ref, bias_ref, active_ref)
    attention_forward(x_ref, bias_ref.at[0], cos_ref, sin_ref, gain_one[...], qkv_w, n1, q_ref, kz_ref, vz_ref, p_ref, o)
    attention_out(x_ref, o, out_w, gain_two[...], attn_ref, n2_ref)


def load_all(pairs, sems):
    return [pltpu.make_async_copy(src, dst, sems.at[i]) for i, (src, dst) in enumerate(pairs)]


def waits_at(condition, copies):
    def ready(*which):
        @pl.when(condition)
        def _():
            for i in which:
                copies[i].wait()

    return ready


def forward_steps(x0_ref, attn0_ref, n20_ref, bias_ref, active_ref, router_ref, cos_ref, sin_ref, gain_one, gain_two,
                  n1_in, o_in, qkv_hbm, out_hbm, *rest):
    feed_hbm, rest = rest[:6], rest[6:]
    (n1_ref, o_ref, q_ref, kz_ref, vz_ref, p_ref, x_ref, a_ref, branch_ref, n2_ref,
     m0, m1, slope0, slope1, silu0, silu1, final_ref), rest = rest[:17], rest[17:]
    qkv_w, out_w, w0, w1, w2, w3, w4, w5, state, attn, n2, total, sems = rest
    step = pl.program_id(0)
    copies = load_all(list(zip((*feed_hbm, qkv_hbm, out_hbm), (w0, w1, w2, w3, w4, w5, qkv_w, out_w))), sems)

    @pl.when(step == 0)
    def _():
        for copy in copies:
            copy.start()
        state[...] = x0_ref[...]
        attn[...] = attn0_ref[...]
        n2[...] = n20_ref[...]

    ready = waits_at(step == 0, copies)
    n2_ref[0] = n2[...]
    feed_forward(n2, ((w0, w1, w2, m0.at[0], slope0.at[0], silu0.at[0]), (w3, w4, w5, m1.at[0], slope1.at[0], silu1.at[0])), total, ready)
    router_row = router_ref[pl.ds(step, 1), :]

    def finish(rows):
        x, attn_rows = state[rows, :], attn[rows, :]
        x_ref[0, rows, :] = x
        a_ref[0, rows, :] = x + attn_rows
        branch = attn_rows + total[rows, :].astype(BF).astype(F32)
        branch_ref[0, rows, :] = branch
        new = jnp.where(active_ref[0, rows, :] > 0, x + router_gate(x, router_row) * branch, x)
        state[rows, :] = new
        final_ref[rows, :] = new

    over_rows(state.shape[0], finish)
    ready(6, 7)

    @pl.when(step < RECURSIONS - 1)
    def _():
        attention_forward(state, bias_ref.at[0], cos_ref, sin_ref, gain_one[...], qkv_w,
                          n1_ref.at[0], q_ref.at[0], kz_ref.at[0], vz_ref.at[0], p_ref.at[0], o_ref.at[0])
        attention_out(state, o_ref.at[0], out_w, gain_two[...], attn, n2)


def finish_attention_backward(x_ref, gain, active_ref, du_ref, qkv_w, base, state, total, out_ref):
    total[...] = contract_last(du_ref[...], qkv_w[...])
    terms = jnp.zeros((1, state.shape[1]), F32)

    def lap(i, terms):
        rows = pl.ds(pl.multiple_of(i * ROWS, ROWS), ROWS)
        d_rows, term = norm_back(x_ref[rows, :], gain, total[rows, :])
        new = jnp.where(active_ref[rows, :] > 0, base[rows, :] + d_rows, state[rows, :])
        out_ref[rows, :] = new
        return terms + term

    return lax.fori_loop(0, state.shape[0] // ROWS, lap, terms)


def backward_steps(d_hidden_ref, active_ref, router_ref, cos_ref, sin_ref, gain_one, gain_two,
                   x_ref, a_ref, branch_ref, slope0, slope1, silu0, silu1, q_ref, kz_ref, vz_ref, p_ref,
                   qkv_hbm, out_hbm, *rest):
    feed_hbm, rest = rest[:6], rest[6:]
    (df_ref, dg0, dg1, dw0, dw1, d_attn_ref, du_ref, base_ref, state_ref, small_ref), rest = rest[:10], rest[10:]
    qkv_w, out_w, w0, w1, w2, w3, w4, w5, d_branch, total, do_ref, sems = rest
    step = pl.program_id(0)
    copies = load_all(list(zip(
        (feed_hbm[2], feed_hbm[0], feed_hbm[1], feed_hbm[5], feed_hbm[3], feed_hbm[4], out_hbm, qkv_hbm),
        (w2, w0, w1, w5, w3, w4, out_w, qkv_w))), sems)

    @pl.when(step == 0)
    def _():
        for copy in copies:
            copy.start()
        state_ref[...] = d_hidden_ref[...]
        small_ref[...] = jnp.zeros(small_ref.shape, F32)

    router_row = router_ref[pl.ds(RECURSIONS - 1 - step, 1), :]
    width = state_ref.shape[1]
    laps = state_ref.shape[0] // ROWS

    def enter(i, terms):
        rows = pl.ds(pl.multiple_of(i * ROWS, ROWS), ROWS)
        x = x_ref[0, rows, :]
        d_new = jnp.where(active_ref[0, rows, :] > 0, state_ref[rows, :], 0.0)
        gate = router_gate(x, router_row)
        d_gate = jnp.sum(d_new * branch_ref[0, rows, :], axis=-1, keepdims=True)
        d_logit = d_gate * gate * (1.0 - gate)
        spread = gate * d_new
        d_branch[rows, :] = spread
        df_ref[0, rows, :] = spread.astype(BF)
        base_ref[rows, :] = d_new + d_logit * router_row
        return terms + jnp.sum(d_logit * x, axis=0, keepdims=True)

    small_ref[pl.ds(2 + RECURSIONS - 1 - step, 1), :] = lax.fori_loop(0, laps, enter, jnp.zeros((1, width), F32))

    ready = waits_at(step == 0, copies)
    feed_backward(df_ref.at[0], ((w0, w1, w2, slope0.at[0], silu0.at[0], dg0.at[0], dw0.at[0]),
                                 (w3, w4, w5, slope1.at[0], silu1.at[0], dg1.at[0], dw1.at[0])), total, ready)

    def leave(i, terms):
        rows = pl.ds(pl.multiple_of(i * ROWS, ROWS), ROWS)
        d_after, term = norm_back(a_ref[0, rows, :], gain_two[...], total[rows, :].astype(BF).astype(F32))
        d_attn_ref[0, rows, :] = (d_branch[rows, :] + d_after).astype(BF)
        base_ref[rows, :] = base_ref[rows, :] + d_after
        return terms + term

    small_ref[1:2, :] = small_ref[1:2, :] + lax.fori_loop(0, laps, leave, jnp.zeros((1, width), F32))
    ready(6, 7)

    @pl.when(step < RECURSIONS - 1)
    def _():
        attention_backward(d_attn_ref.at[0], out_w, qkv_w, cos_ref, sin_ref, q_ref.at[0], kz_ref.at[0], vz_ref.at[0],
                           p_ref.at[0], do_ref, du_ref.at[0])
        term = finish_attention_backward(x_ref.at[0], gain_one[...], active_ref.at[0], du_ref.at[0], qkv_w, base_ref, state_ref, total, state_ref)
        small_ref[0:1, :] = small_ref[0:1, :] + term


def last_attention(active_ref, cos_ref, sin_ref, gain_one, q_ref, kz_ref, vz_ref, p_ref, d_attn_ref, small_in, out_w,
                   x_hbm, base_hbm, state_hbm, qkv_hbm, du_in, token, du_ref, d_input_ref, small_ref,
                   do_ref, total, x, base, state, qkv_w, sems):
    copies = load_all([(qkv_hbm, qkv_w), (x_hbm.at[0], x), (base_hbm, base), (state_hbm, state)], sems)
    for copy in copies:
        copy.start()
    attention_backward(d_attn_ref.at[0], out_w, qkv_w, cos_ref, sin_ref, q_ref, kz_ref, vz_ref, p_ref, do_ref, du_ref.at[0])
    for copy in copies:
        copy.wait()
    term = finish_attention_backward(x, gain_one[...], active_ref.at[0], du_ref.at[0], qkv_w, base, state, total, d_input_ref)
    small_ref[...] = small_in[...]
    small_ref[0:1, :] = small_in[0:1, :] + term


def swap_dp(values_in, bit, n_dp):
    return lax.ppermute(values_in, "dp", [(i, i ^ (1 << bit)) for i in range(n_dp)])


def swap_mp(values_in):
    return lax.ppermute(values_in, "mp", [(0, 1), (1, 0)])


def halving(parts, order, n_dp, index):
    bits = n_dp.bit_length() - 1
    left = list(range(bits - 1, -1, -1))
    shape = parts.shape[1:]
    held = parts.reshape((2,) * bits + shape)
    for step, bit in enumerate(order):
        at = left.index(bit)
        upper = ((index >> bit) & 1) == 1
        low = lax.index_in_dim(held, 0, at, keepdims=False)
        high = lax.index_in_dim(held, 1, at, keepdims=False)
        keep, send = jnp.where(upper, high, low), jnp.where(upper, low, high)
        got = swap_dp(send, bit, n_dp)
        last = step == bits - 1
        total = keep.astype(F32) + got.astype(F32)
        held = total if last else total.astype(BF)
        left.remove(bit)
    return held


def orders_of(bits):
    rest = list(range(3, bits))
    if bits < 3:
        return [list(range(bits))] * 3
    return [[0, 1, 2] + rest, [1, 0, 2] + rest, [2, 0, 1] + rest]


PART = 2 * LANES
FFN_TILES = (4, 4, 2)
FFN_ORDERS = ((0, 1, 2, 3), (2, 0, 1, 3), (1, 2, 3, 0))
ATTN_ORDERS = ((0, 3, 2, 1), (3, 0, 1, 2))
SCHEDULE = (
    "T0", "T1", "T2", "A",
    "F0", "F1", "F2", "A0", "A1",
    "F0", "F1", "F2", "A0", "A1",
    "F0", "F1", "F2", "A0", "A1",
)
SMALL = 64


def halves(bit, outs, index):
    mine = (index >> bit) & 1
    inner = 1 << bit
    for out, which in zip(outs, (mine, 1 - mine)):
        for p in range(out.shape[0]):
            for q in range(inner):
                yield out, p, q, p * 2 * inner + which * inner + q


def stacked_copies(pairs, sems):
    flat_pairs = []
    for sources, target in pairs:
        rows = target.shape[0] // 2
        flat_pairs += [(source, target.at[pl.ds(i * rows, rows)]) for i, source in enumerate(sources)]
    copies = load_all(flat_pairs, sems)
    for copy in copies:
        copy.start()
    return [copies[i : i + 2] for i in range(0, len(copies), 2)]


def ffn_terms(bit, tiles, at, n2_a, n2_b, df_a, df_b, dg_a, dg_b, dw_a, dw_b, m_a, m_b, token, keep_ref, send_ref,
              left, right, flat, sems):
    width = left.shape[2]
    columns = pl.ds(at, tiles * LANES)
    parts = [tuple(ref.at[:, columns] for ref in both) for both in ((dg_a, dg_b), (dw_a, dw_b), (m_a, m_b))]
    n2, dg, dw, df, m = stacked_copies(
        [((n2_a, n2_b), left.at[0]), (parts[0], right.at[0]), (parts[1], right.at[1]),
         ((df_a, df_b), left.at[1]), (parts[2], right.at[2])], sems)
    for matrix, needed in enumerate((n2 + dg, dw, df + m)):
        for copy in needed:
            copy.wait()
        terms = contract_rows(left[matrix // 2], right[matrix])
        for c in range(tiles):
            flat[pl.ds(tiles * width * matrix + c, width, stride=tiles), :] = terms[:, c * LANES : (c + 1) * LANES]
    rows = keep_ref.shape[2]
    for out, p, q, shard in halves(bit, (keep_ref, send_ref), lax.axis_index("dp")):
        out[p, q] = flat[pl.ds(pl.multiple_of(shard * rows, 8), rows), :].astype(BF)


def small_rows(small):
    rest = -small.shape[1] % LANES
    small = jnp.concatenate([small, jnp.zeros((small.shape[0], rest), F32)], axis=1)
    return jnp.concatenate([small[:, at : at + LANES] for at in range(0, small.shape[1], LANES)], axis=0)


def split_small(small, ref, start):
    high = small.astype(BF)
    ref[start : start + SMALL, :] = high
    ref[start + SMALL : start + 2 * SMALL, :] = (small - high.astype(F32)).astype(BF)


def rounded_small(small):
    high = small.astype(BF)
    return high.astype(F32) + (small - high.astype(F32)).astype(BF).astype(F32)


def joined_small(ref, start):
    return ref[start : start + SMALL, :].astype(F32) + ref[start + SMALL : start + 2 * SMALL, :].astype(F32)


def attn_terms(bits, cut, n1_a, n1_b, du_a, du_b, o_a, o_b, da_a, da_b, small_a, small_b, token,
               keep0, send0, keep1, send1, small_out, left, du_rows, da_rows, terms, flat, sems):
    width = left.shape[2]
    base = 0
    lower = lane_of(width // 2) < HEAD_DIM
    n1, du, o, da = stacked_copies(
        [((n1_a, n1_b), left.at[0]), ((du_a, du_b), du_rows), ((o_a, o_b), left.at[1]), ((da_a, da_b), da_rows)], sems)
    for which, (right, needed) in enumerate(((du_rows, n1 + du), (da_rows, o + da))):
        for copy in needed:
            copy.wait()
        columns = right.shape[1]
        half = columns // LANES
        for start in range(0, columns, PART):
            stop = min(columns, start + PART)
            block = contract_rows(left[which], right[:, start:stop])
            if stop - start < PART:
                block = jnp.concatenate([block, jnp.zeros((width, PART - (stop - start)), F32)], axis=1)
            for part in range(0, stop - start, LANES):
                terms[(start + part) // LANES] = block[:, part : part + LANES]
        step = 2 * columns // LANES
        count = width // 2
        after = first_odd = None
        for c in range(half + 1):
            even = terms[c, pl.ds(0, count, stride=2), :]
            odd = other_half(terms[c, pl.ds(1, count, stride=2), :])
            if c < half:
                flat[pl.ds(base + c, count, stride=step), :] = even
            else:
                flat[pl.ds(base + c, count, stride=step), :] = jnp.where(lower, even, first_odd)
            if c == 0:
                first_odd = odd
            else:
                flat[pl.ds(base + half + c, count, stride=step), :] = jnp.where(lower, after, odd)
            after = odd
        base += width * columns // LANES
    index, core = lax.axis_index("dp"), lax.axis_index("mp")
    total = rounded_small(small_rows(small_a[...])) + rounded_small(small_rows(small_b[...]))
    small_out[...] = total
    shards, depth = 2 * keep0.shape[0] * keep0.shape[1], cut + keep1.shape[2]
    split_small(total, send0, shards // 2 * cut)

    def rows_of_shard(shard, low, high):
        start = pl.multiple_of((2 * shard + core) * depth + low, 8)
        return flat[pl.ds(start, high - low), :].astype(BF)

    mine = (index >> bits[0]) & 1
    inner = 1 << bits[0]
    for p in range(keep0.shape[0]):
        for q in range(inner):
            shard = 2 * p * inner + q
            keep0[p, q] = rows_of_shard(shard + mine * inner, 0, cut)
            at = (p * inner + q) * cut
            send0[at : at + cut, :] = rows_of_shard(shard + (1 - mine) * inner, 0, cut)
    for out, p, q, shard in halves(bits[1], (keep1, send1), index):
        out[p, q] = rows_of_shard(shard, cut, depth)


def fold(bit, kept, got, token, keep, send):
    mine = (lax.axis_index("dp") >> bit) & 1
    for p in range(kept.shape[0]):
        for q in range(kept.shape[2]):
            for out, which in ((keep, mine), (send, 1 - mine)):
                out[p, q] = (kept[p, which, q].astype(F32) + got[p, which, q].astype(F32)).astype(BF)


def fold_small(bit, kept, got, small, token, keep, send, small_out):
    mine = (lax.axis_index("dp") >> bit) & 1
    outer, _, inner, rows, _ = kept.shape
    for p in range(outer):
        for q in range(inner):
            totals = []
            for which in (mine, 1 - mine):
                start = pl.multiple_of(((2 * p + which) * inner + q) * rows, 16)
                totals.append((kept[p, which, q].astype(F32) + got[pl.ds(start, rows), :].astype(F32)).astype(BF))
            keep[p, q] = totals[0]
            at = (p * inner + q) * rows
            send[at : at + rows, :] = totals[1]
    total = rounded_small(small[...]) + joined_small(got, 2 * outer * inner * rows)
    small_out[...] = total
    split_small(total, send, outer * inner * rows)


def finish_streams(tiles, *refs):
    count = len(tiles)
    feeds, refs = refs[: 2 * count], refs[2 * count :]
    attn, refs = refs[:4], refs[4:]
    small, ffn_out, attn_out, one_out, two_out, router_out, flat = refs
    every = sum(tiles)
    rows = ffn_out.shape[0] // every
    base = 0
    for i, wide in enumerate(tiles):
        flat[: rows * wide, :] = feeds[2 * i][...].astype(F32) + feeds[2 * i + 1][...].astype(F32)
        for c in range(wide):
            ffn_out[pl.ds(base + c, rows, stride=every), :] = flat[pl.ds(c, rows, stride=wide), :]
        base += wide
    cut = attn[0].shape[0]
    attn_out[:cut, :] = attn[0][...].astype(F32) + attn[1][:cut, :].astype(F32)
    attn_out[cut:, :] = attn[2][...].astype(F32) + attn[3][...].astype(F32)
    total = rounded_small(small[...]) + joined_small(attn[1], cut)
    width = one_out.shape[1]
    for at in range(0, width, LANES):
        stop = min(width, at + LANES)
        tile = total[at // LANES * 8 : at // LANES * 8 + 8, : stop - at]
        one_out[:, at:stop] = tile[0:1]
        two_out[:, at:stop] = tile[1:2]
        router_out[:, at:stop] = tile[2 : 2 + RECURSIONS]


class Stream:
    def __init__(self, order, bits):
        self.order, self.left, self.done = order, list(range(bits - 1, -1, -1)), 0
        self.kept = self.got = None

    def shape_for(self, array):
        at = self.left.index(self.order[self.done])
        rows, lanes = array.shape[-2:]
        return (1 << at, 2, 1 << (len(self.left) - 1 - at), rows, lanes)

    def sent(self, kept, send, n_dp):
        bit = self.order[self.done]
        self.kept, self.got = kept, swap_dp(send, bit, n_dp)
        self.left.remove(bit)
        self.done += 1


def on_device(
    hidden_in,
    sel_one,
    sel_two,
    sel_three,
    segment_ids,
    pad_mask,
    qkv_weight,
    out_weight,
    gate_weight,
    up_weight,
    down_weight,
    norm_one,
    norm_two,
    router_weight,
    d_hidden,
):
    seq_len, width = hidden_in.shape
    n_dp, n_mp = lax.axis_size("dp"), lax.axis_size("mp")
    dp_index, mp_index = lax.axis_index("dp"), lax.axis_index("mp")
    cosine, sine = rotary_tables(seq_len)
    weights = [(gate_weight, up_weight, down_weight)]
    weights.append(tuple(swap_mp(w) for w in weights[0]))
    gain_one, gain_two = norm_one.reshape(1, width), norm_two.reshape(1, width)
    padded = CHUNKS * LANES
    units = gate_weight.shape[1]
    feed_weights = (*weights[0], *weights[1])

    def shape(*dims, dtype=BF):
        return jax.ShapeDtypeStruct(dims, dtype)

    def whole(*dims, **kw):
        return pl.BlockSpec(dims, lambda *_: (0,) * len(dims), **kw)

    anywhere = pl.BlockSpec(memory_space=pl.ANY)
    one = pl.Buffered(1)
    stack = RECURSIONS, seq_len
    heads = (2 * KV_HEADS, seq_len, LANES)
    square = (HEADS, seq_len, seq_len)
    n1, q, kz, vz, p, o, attn, n2, bias, active = pl.pallas_call(
        first_attention,
        grid=(1,),
        in_specs=[
            whole(seq_len, width), *[whole(*ref.shape) for ref in (sel_one, sel_two, sel_three, segment_ids, pad_mask)],
            whole(seq_len, LANES), whole(seq_len, LANES), whole(1, width), whole(1, width), whole(*qkv_weight.shape), whole(*out_weight.shape),
        ],
        out_specs=[
            whole(1, seq_len, width), whole(seq_len, padded), whole(*heads), whole(*heads), whole(*square),
            whole(1, seq_len, width), whole(seq_len, width), whole(seq_len, width), whole(RECURSIONS, seq_len, seq_len), whole(*stack, 1),
        ],
        out_shape=[
            shape(*stack, width), shape(seq_len, padded), shape(*heads), shape(*heads), shape(*square),
            shape(*stack, width), shape(seq_len, width, dtype=F32), shape(seq_len, width),
            shape(*stack, seq_len, dtype=F32), shape(*stack, 1, dtype=F32),
        ],
        compiler_params=pltpu.CompilerParams(vmem_limit_bytes=VMEM_MIB * MIB),
        cost_estimate=pl.CostEstimate(flops=2 * 10**9, bytes_accessed=12 * 10**6, transcendentals=600000),
        name="first_attention",
    )(hidden_in, sel_one, sel_two, sel_three, segment_ids, pad_mask, cosine, sine, gain_one, gain_two, qkv_weight, out_weight)
    attention_0 = (q, kz, vz, p)

    def at_step(*dims):
        return pl.BlockSpec((1, *dims), lambda r: (r,) + (0,) * len(dims))

    def next_step(*dims):
        return pl.BlockSpec((1, *dims), lambda r: (jnp.minimum(r + 1, RECURSIONS - 1),) + (0,) * len(dims))

    def next_pair(*dims):
        return pl.BlockSpec((1, *dims), lambda r: (jnp.minimum(r, RECURSIONS - 2),) + (0,) * len(dims))

    weight_scratch = [pltpu.VMEM(w.shape, BF) for w in (qkv_weight, out_weight, *feed_weights)]
    results = pl.pallas_call(
        forward_steps,
        grid=(RECURSIONS,),
        in_specs=[
            whole(seq_len, width, pipeline_mode=one), whole(seq_len, width, pipeline_mode=one), whole(seq_len, width, pipeline_mode=one),
            next_step(seq_len, seq_len), at_step(seq_len, 1), whole(RECURSIONS, width),
            whole(seq_len, LANES), whole(seq_len, LANES), whole(1, width), whole(1, width),
            anywhere, anywhere, *[anywhere] * 8,
        ],
        out_specs=[
            next_step(seq_len, width), next_step(seq_len, width), next_pair(seq_len, padded), next_pair(*heads), next_pair(*heads),
            next_pair(*square), *[at_step(seq_len, width)] * 4, *[at_step(seq_len, units)] * 6, whole(seq_len, width),
        ],
        out_shape=[
            shape(*stack, width), shape(*stack, width), shape(RECURSIONS - 1, seq_len, padded), shape(RECURSIONS - 1, *heads), shape(RECURSIONS - 1, *heads),
            shape(RECURSIONS - 1, *square), *[shape(*stack, width, dtype=F32)] * 3, shape(*stack, width), *[shape(*stack, units)] * 6,
            shape(seq_len, width, dtype=F32),
        ],
        scratch_shapes=[
            *weight_scratch,
            pltpu.VMEM((seq_len, width), F32), pltpu.VMEM((seq_len, width), F32), pltpu.VMEM((seq_len, width), BF), pltpu.VMEM((seq_len, width), F32),
            pltpu.SemaphoreType.DMA((8,)),
        ],
        input_output_aliases={10: 0, 11: 1},
        compiler_params=pltpu.CompilerParams(vmem_limit_bytes=VMEM_MIB * MIB),
        cost_estimate=pl.CostEstimate(flops=12 * 10**9, bytes_accessed=50 * 10**6, transcendentals=4 * 10**6),
        name="forward_steps",
    )(hidden_in, attn, n2, bias, active, router_weight, cosine, sine, gain_one, gain_two, n1, o, qkv_weight, out_weight, *feed_weights)
    n1, o, q, kz, vz, p, x, a, branch, n2, m0, m1, slope0, slope1, silu0, silu1, state = results

    def back_step(*dims):
        return pl.BlockSpec((1, *dims), lambda i: (RECURSIONS - 1 - i,) + (0,) * len(dims))

    def back_pair(*dims):
        return pl.BlockSpec((1, *dims), lambda i: (jnp.maximum(RECURSIONS - 2 - i, 0),) + (0,) * len(dims))

    def back_next(*dims):
        return pl.BlockSpec((1, *dims), lambda i: (jnp.maximum(RECURSIONS - 1 - i, 1),) + (0,) * len(dims))

    results = pl.pallas_call(
        backward_steps,
        grid=(RECURSIONS,),
        in_specs=[
            whole(seq_len, width, pipeline_mode=one), back_step(seq_len, 1), whole(RECURSIONS, width),
            whole(seq_len, LANES), whole(seq_len, LANES), whole(1, width), whole(1, width),
            *[back_step(seq_len, width)] * 3, *[back_step(seq_len, units)] * 4,
            back_pair(seq_len, padded), back_pair(*heads), back_pair(*heads), back_pair(*square),
            *[anywhere] * 8,
        ],
        out_specs=[
            back_step(seq_len, width), *[back_step(seq_len, units)] * 4, back_step(seq_len, width), back_next(seq_len, qkv_weight.shape[1]),
            whole(seq_len, width), whole(seq_len, width), whole(8, width),
        ],
        out_shape=[
            shape(*stack, width), *[shape(*stack, units)] * 4, shape(*stack, width), shape(*stack, qkv_weight.shape[1]),
            shape(seq_len, width, dtype=F32), shape(seq_len, width, dtype=F32), shape(8, width, dtype=F32),
        ],
        scratch_shapes=[
            *weight_scratch,
            pltpu.VMEM((seq_len, width), F32), pltpu.VMEM((seq_len, width), F32), pltpu.VMEM((seq_len, padded), BF),
            pltpu.SemaphoreType.DMA((8,)),
        ],
        compiler_params=pltpu.CompilerParams(vmem_limit_bytes=VMEM_MIB * MIB),
        cost_estimate=pl.CostEstimate(flops=11 * 10**9, bytes_accessed=50 * 10**6, transcendentals=4 * 10**6),
        name="backward_steps",
    )(d_hidden, active, router_weight, cosine, sine, gain_one, gain_two, x, a, branch, slope0, slope1, silu0, silu1, q, kz, vz, p,
      qkv_weight, out_weight, *feed_weights)
    d_feed, dg0, dg1, dw0, dw1, d_attn, du, base, grad_state, small = results

    def run_last(token):
        return pl.pallas_call(
            last_attention,
            grid=(1,),
            in_specs=[
                whole(1, seq_len, 1), whole(seq_len, LANES), whole(seq_len, LANES), whole(1, width),
                whole(seq_len, padded), whole(*heads), whole(*heads), whole(*square), whole(1, seq_len, width),
                whole(8, width), whole(*out_weight.shape), *[anywhere] * 6,
            ],
            out_specs=[whole(1, seq_len, qkv_weight.shape[1]), whole(seq_len, width), whole(8, width)],
            out_shape=[shape(*stack, qkv_weight.shape[1]), shape(seq_len, width, dtype=F32), shape(8, width, dtype=F32)],
            scratch_shapes=[
                pltpu.VMEM((seq_len, padded), BF), *[pltpu.VMEM((seq_len, width), F32)] * 4,
                pltpu.VMEM(qkv_weight.shape, BF), pltpu.SemaphoreType.DMA((4,)),
            ],
            input_output_aliases={15: 0},
            compiler_params=pltpu.CompilerParams(vmem_limit_bytes=VMEM_MIB * MIB),
            cost_estimate=pl.CostEstimate(flops=1, bytes_accessed=1, transcendentals=0),
            name="last_attention",
        )(active, cosine, sine, gain_one, *attention_0, d_attn, small, out_weight, x, base, grad_state, qkv_weight, du, token)

    def rows_of(stacked):
        return stacked.reshape(-1, stacked.shape[-1])

    two, feed = rows_of(n2), rows_of(d_feed)
    sides = ((dg0, dw0, m0), (dg1, dw1, m1))
    bits = n_dp.bit_length() - 1
    share = (qkv_weight.size + out_weight.size) // (n_dp * n_mp)
    if bits == 4 and 3 * width % n_dp == 0 and units == sum(FFN_TILES) * LANES and share % (8 * LANES) == 0:
        crossed = [(t, swap_mp(far)) for t, far in
                   ((n2, n2), (d_feed, d_feed), (dg0, dg1), (dw0, dw1), (m0, m1))]
        factors = [rows_of(t) for both in crossed for t in both]
        streams = [Stream(order, bits) for order in FFN_ORDERS]
        pair = [Stream(order, bits) for order in ATTN_ORDERS]
        depth = share // LANES
        cut = depth // 2 // 16 * 16
        common = dict(
            grid=(1,),
            compiler_params=pltpu.CompilerParams(vmem_limit_bytes=VMEM_MIB * MIB),
            cost_estimate=pl.CostEstimate(flops=1, bytes_accessed=1, transcendentals=0),
        )

        def wholes(arrays):
            return [whole(*t.shape) for t in arrays]

        def terms_of(j, token):
            stream, tiles = streams[j], FFN_TILES[j]
            at = sum(FFN_TILES[:j]) * LANES
            bit = stream.order[0]
            dims = (1 << (bits - 1 - bit), 1 << bit, 3 * width // n_dp * tiles, LANES)
            both = 2 * RECURSIONS * seq_len
            keep, send = pl.pallas_call(
                functools.partial(ffn_terms, bit, tiles, at),
                in_specs=[anywhere] * (len(factors) + 1),
                out_specs=[whole(*dims)] * 2,
                out_shape=[shape(*dims)] * 2,
                scratch_shapes=[pltpu.VMEM((2, both, width), BF), pltpu.VMEM((3, both, tiles * LANES), BF),
                                pltpu.VMEM((3 * width * tiles, LANES), F32), pltpu.SemaphoreType.DMA((10,))],
                name=f"ffn_terms_{j}",
                **common,
            )(*factors, token)
            stream.sent(keep, send, n_dp)
            return keep

        def fold_stream(stream, token, small_own=None):
            bit = stream.order[stream.done]
            dims = stream.shape_for(stream.kept)
            kept = stream.kept.reshape(dims)
            held = (dims[0], *dims[2:])
            if small_own is None:
                operands = (kept, stream.got.reshape(dims))
                outs = (shape(*held), shape(*held))
            else:
                operands = (kept, stream.got, small_own)
                outs = (shape(*held), shape(dims[0] * dims[2] * dims[3] + 2 * SMALL, LANES), shape(SMALL, LANES, dtype=F32))
            results = pl.pallas_call(
                functools.partial(fold if small_own is None else fold_small, bit),
                in_specs=[*wholes(operands), anywhere],
                out_specs=wholes(outs),
                out_shape=outs,
                name="fold_terms",
                **common,
            )(*operands, token)
            stream.sent(results[0], results[1], n_dp)
            return results

        du, grad_state, small = run_last(small)
        first_crossed = [(rows_of(n1), swap_mp(rows_of(n1))), (rows_of(du), swap_mp(rows_of(du)))]
        late_crossed = [(rows_of(o), swap_mp(rows_of(o))), (rows_of(d_attn), swap_mp(rows_of(d_attn))), (small, swap_mp(small))]
        token = small
        for item in SCHEDULE:
            if item[0] == "T":
                token = terms_of(int(item[1:]), token)
            elif item[0] == "F":
                token = fold_stream(streams[int(item[1:])], token)[0]
            elif item == "A":
                firsts = [t.order[0] for t in pair]
                dims = [(1 << (bits - 1 - bit), 1 << bit, rows, LANES) for bit, rows in zip(firsts, (cut, depth - cut))]
                operands = [t for both in (*first_crossed, *late_crossed) for t in both]
                outs = (shape(*dims[0]), shape(n_dp // 2 * cut + 2 * SMALL, LANES), shape(*dims[1]), shape(*dims[1]),
                        shape(SMALL, LANES, dtype=F32))
                keep0, send0, keep1, send1, small_own = pl.pallas_call(
                    functools.partial(attn_terms, tuple(firsts), cut),
                    in_specs=[*[anywhere] * 8, *wholes(operands[8:]), anywhere],
                    out_specs=wholes(outs),
                    out_shape=outs,
                    scratch_shapes=[pltpu.VMEM((2, 2 * RECURSIONS * seq_len, width), BF),
                                    *[pltpu.VMEM((2 * RECURSIONS * seq_len, t.shape[-1]), BF) for t in (du, d_attn)],
                                    pltpu.VMEM((-(-du.shape[-1] // PART) * 2, width, LANES), F32),
                                    pltpu.VMEM((n_dp * 2 * depth, LANES), F32), pltpu.SemaphoreType.DMA((8,))],
                    name="attn_terms",
                    **common,
                )(*operands, token)
                pair[0].sent(keep0, send0, n_dp)
                pair[1].sent(keep1, send1, n_dp)
                token = small_own
            elif item == "A0":
                token, _, small_own = fold_stream(pair[0], token, small_own)
            else:
                token = fold_stream(pair[1], token)[0]
        ends = [t.reshape(t.shape[-2:]) for stream in (*streams, *pair) for t in (stream.kept, stream.got)]
        outs = (shape(3 * width // n_dp * sum(FFN_TILES), LANES, dtype=F32), shape(depth, LANES, dtype=F32),
                shape(1, width, dtype=F32), shape(1, width, dtype=F32), shape(RECURSIONS, width, dtype=F32))
        ffn_flat, attn_flat, one, two, router = pl.pallas_call(
            functools.partial(finish_streams, FFN_TILES),
            in_specs=wholes((*ends, small_own)),
            out_specs=wholes(outs),
            out_shape=outs,
            scratch_shapes=[pltpu.VMEM((3 * width // n_dp * max(FFN_TILES), LANES), F32)],
            name="finish_streams",
            **common,
        )(*ends, small_own)
        return (state, grad_state, attn_flat.reshape(-1), ffn_flat.reshape(1, -1), one.reshape(-1), two.reshape(-1), router)

    du, grad_state, small = run_last(small)

    def side_terms(side, columns):
        return jnp.concatenate(
            [
                contract_rows(left, rows_of(sides[side][which])[:, columns]).astype(BF)
                for which, left in enumerate((two, two, feed))
            ],
            axis=0,
        )

    orders = orders_of(bits)
    if 3 * width % n_dp == 0 and units % 1280 == 0:
        fifth = units // 5
        streams = [(orders[i], slice(j * fifth, (j + 1) * fifth)) for i, j in ((0, 0), (1, 1), (2, 2), (0, 3), (1, 4))]
        done = []
        for order, columns in streams:
            terms = side_terms(0, columns).astype(F32) + swap_mp(side_terms(1, columns)).astype(F32)
            done.append(halving(terms.astype(BF).reshape(n_dp, 3 * width // n_dp, fifth), order, n_dp, dp_index))
        ffn_flat = jnp.concatenate(done, axis=1).reshape(1, -1)
    else:
        terms = side_terms(0, slice(None)).astype(F32) + swap_mp(side_terms(1, slice(None))).astype(F32)
        terms = terms.astype(BF).reshape(n_dp, 3 * width * units // n_dp // 128, 128)
        ffn_flat = halving(terms, orders[0], n_dp, dp_index).reshape(1, -1)

    grad_qkv = contract_rows(rows_of(n1), rows_of(du)).astype(BF)
    grad_out = contract_rows(rows_of(o), rows_of(d_attn)).astype(BF)
    attn = jnp.concatenate([grad_qkv.reshape(-1), grad_out.reshape(-1)]).reshape(n_dp, 2, share // 128, 128)
    keep = jnp.where(mp_index == 0, attn[:, 0], attn[:, 1])
    send = jnp.where(mp_index == 0, attn[:, 1], attn[:, 0])
    attn = (keep.astype(F32) + swap_mp(send).astype(F32)).astype(BF)
    cuts = [0, (share // 128) // 24 * 8, (share // 128) // 12 * 8, share // 128]
    attn_flat = jnp.concatenate(
        [halving(attn[:, a:b], order, n_dp, dp_index) for a, b, order in zip(cuts, cuts[1:], orders)], axis=0
    ).reshape(-1)

    small = small + swap_mp(small)
    for bit in range(bits):
        small = small + swap_dp(small, bit, n_dp)
    return (state, grad_state, attn_flat, ffn_flat, small[0], small[1], small[2 : 2 + RECURSIONS])


def solution(mesh):
    both = P(("dp", "mp"), None)
    in_specs = (
        both,
        both,
        both,
        both,
        both,
        both,
        P(),
        P(),
        P(None, "mp"),
        P(None, "mp"),
        P(None, "mp"),
        P(),
        P(),
        P(),
        both,
    )
    out_specs = (both, both, P(("dp", "mp")), P("mp", "dp"), P(), P(), P())
    return jax.shard_map(
        on_device, mesh=mesh, in_specs=in_specs, out_specs=out_specs, check_vma=False
    )
```

```python
import functools
import math

import jax
import jax.numpy as jnp
import numpy as np
from jax import lax
from jax.experimental import pallas as pl
from jax.experimental.pallas import tpu as pltpu
from jax.sharding import PartitionSpec as P

HEADS = 15
KV_HEADS = 5
HEAD_DIM = 64
RECURSIONS = 3
GROUPS = HEADS // KV_HEADS
EPS = 1e-05
BF = jnp.bfloat16
F32 = jnp.float32


LANES = 128
CHUNKS = -(-HEADS * HEAD_DIM // LANES)
ROWS = 32
BLOCK = 256
MIB = 1 << 20
VMEM_MIB = 63


def rotary_tables(seq_len):
    half = HEAD_DIM // 2
    frequency = np.float32(100000.0) ** (
        np.float32(-2.0) * np.arange(half, dtype=np.float32) / np.float32(HEAD_DIM)
    )
    angles = np.arange(seq_len, dtype=np.float32)[:, None] * frequency.astype(np.float32)
    cosine, sine = np.cos(angles), np.sin(angles)
    return (
        jnp.asarray(np.concatenate([cosine] * 4, axis=1), F32),
        jnp.asarray(np.concatenate([-sine, sine] * 2, axis=1), F32),
    )


def contract_rows(left, right):
    return lax.dot_general(left, right, (((0,), (0,)), ((), ())), preferred_element_type=F32)


def contract_last(left, right):
    return lax.dot_general(left, right, (((1,), (1,)), ((), ())), preferred_element_type=F32)


def plain(left, right):
    return jnp.dot(left, right, preferred_element_type=F32)


def inverse_rms(rows):
    return lax.rsqrt(jnp.mean(rows * rows, axis=-1, keepdims=True) + EPS)


def norm_back(rows, gain, d_out):
    inv = inverse_rms(rows)
    scaled = d_out * gain
    inner = jnp.mean(scaled * rows, axis=-1, keepdims=True)
    d_rows = inv * scaled - rows * (inv * inv * inv * inner)
    return d_rows, jnp.sum(d_out * rows * inv, axis=0, keepdims=True)


def lane_of(rows):
    return lax.broadcasted_iota(jnp.int32, (rows, LANES), 1)


def swapped(chunk):
    first = lane_of(chunk.shape[0]) % HEAD_DIM < HEAD_DIM // 2
    return jnp.where(first, pltpu.roll(chunk, LANES - 32, 1), pltpu.roll(chunk, 32, 1))


def other_half(chunk):
    return pltpu.roll(chunk, HEAD_DIM, 1)


def over_rows(count, body):
    def lap(i, carry):
        body(pl.ds(pl.multiple_of(i * ROWS, ROWS), ROWS))
        return carry

    lax.fori_loop(0, count // ROWS, lap, 0)


def attention_forward(x_ref, bias_ref, cos_ref, sin_ref, gain, qkv_w, n1_ref, q_ref, kz_ref, vz_ref, p_ref, o_ref):
    seq_len, width = x_ref.shape
    scale = 1.0 / math.sqrt(HEAD_DIM)

    def norm(rows):
        x = x_ref[rows, :]
        n1_ref[rows, :] = (x * inverse_rms(x) * gain).astype(BF)

    over_rows(seq_len, norm)
    lower = lane_of(seq_len) < HEAD_DIM
    n1 = n1_ref[...]

    def spread(ref, head, chunk, upper):
        flipped = other_half(chunk)
        here, there = (flipped, chunk) if upper else (chunk, flipped)
        ref[2 * head] = jnp.where(lower, here, 0.0).astype(BF)
        ref[2 * head + 1] = jnp.where(lower, 0.0, there).astype(BF)

    columns = qkv_w.shape[1]
    for start in range(0, columns, 2 * LANES):
        wide = plain(n1, qkv_w[:, start : min(start + 2 * LANES, columns)])
        for part in range(0, wide.shape[1], LANES):
            chunk = wide[:, part : part + LANES]
            if chunk.shape[1] < LANES:
                chunk = jnp.concatenate([chunk, jnp.zeros_like(chunk)], axis=1)
            at = (start + part) // LANES
            heads = (2 * at, 2 * at + 1)
            if heads[0] < HEADS + KV_HEADS:
                chunk = chunk * cos_ref[...] + swapped(chunk) * sin_ref[...]
                if heads[0] < HEADS:
                    q_ref[:, at * LANES : (at + 1) * LANES] = chunk.astype(BF)
            for upper, head in enumerate(heads):
                if HEADS <= head < HEADS + KV_HEADS:
                    spread(kz_ref, head - HEADS, chunk, upper)
                elif HEADS + KV_HEADS <= head < HEADS + 2 * KV_HEADS:
                    spread(vz_ref, head - HEADS - KV_HEADS, chunk, upper)

    for at in range(CHUNKS):
        query = q_ref[:, at * LANES : (at + 1) * LANES]
        total = None
        for upper in range(2):
            head = 2 * at + upper
            if head < HEADS:
                key = 2 * (head // GROUPS) + upper
                scores = contract_last(query, kz_ref[key]) * scale + bias_ref[...]
                top = jnp.max(scores, axis=-1, keepdims=True)
                exponent = jnp.exp(scores - top)
                share = pl.reciprocal(jnp.sum(exponent, axis=-1, keepdims=True))
                attend = (exponent * share).astype(BF)
                p_ref[head] = attend
                mixed = plain(attend, vz_ref[key])
                total = mixed if total is None else total + mixed
        stop = min(width, (at + 1) * LANES)
        o_ref[:, at * LANES : stop] = total[:, : stop - at * LANES].astype(BF)


def attention_out(x_ref, o_ref, out_w, gain, attn_ref, n2_ref):
    attn_ref[...] = plain(o_ref[...], out_w[...])

    def norm(rows):
        after = x_ref[rows, :] + attn_ref[rows, :]
        n2_ref[rows, :] = (after * inverse_rms(after) * gain).astype(BF)

    over_rows(x_ref.shape[0], norm)


def feed_forward(n2_ref, sides, f_ref, ready):
    n2 = n2_ref[...]
    for side, (gate_w, up_w, down_w, m_ref, slope_ref, silu_ref) in enumerate(sides):
        ready(3 * side, 3 * side + 1)
        for start in range(0, gate_w.shape[1], BLOCK):
            at = slice(start, start + BLOCK)
            g, u = plain(n2, gate_w[:, at]), plain(n2, up_w[:, at])
            s = jax.nn.sigmoid(g)
            silu = g * s
            m_ref[:, at] = (silu * u).astype(BF)
            slope_ref[:, at] = (u * s * (1.0 + g * (1.0 - s))).astype(BF)
            silu_ref[:, at] = silu.astype(BF)
        ready(3 * side + 2)
        part = contract_last(m_ref[...], down_w[...])
        f_ref[...] = part if side == 0 else f_ref[...] + part


def feed_backward(df_ref, sides, d_two_ref, ready):
    d_feed = df_ref[...]
    for side, (gate_w, up_w, down_w, slope_ref, silu_ref, dg_ref, du_ref) in enumerate(sides):
        ready(3 * side)
        for start in range(0, gate_w.shape[1], BLOCK):
            at = slice(start, start + BLOCK)
            d_hidden = plain(d_feed, down_w[:, at])
            dg_ref[:, at] = (d_hidden * slope_ref[:, at].astype(F32)).astype(BF)
            du_ref[:, at] = (d_hidden * silu_ref[:, at].astype(F32)).astype(BF)
        ready(3 * side + 1, 3 * side + 2)
        part = contract_last(dg_ref[...], gate_w[...]) + contract_last(du_ref[...], up_w[...])
        d_two_ref[...] = part if side == 0 else d_two_ref[...] + part


def attention_backward(d_attn_ref, out_w, qkv_w, cos_ref, sin_ref, q_ref, kz_ref, vz_ref, p_ref, do_ref, du_ref):
    seq_len, width = d_attn_ref.shape
    scale = 1.0 / math.sqrt(HEAD_DIM)
    do_ref[:, :width] = contract_last(d_attn_ref[...], out_w[...]).astype(BF)
    do_ref[:, width:] = jnp.zeros((seq_len, do_ref.shape[1] - width), BF)
    lower = lane_of(seq_len) < HEAD_DIM
    cosine, sine = cos_ref[...], sin_ref[...]

    def back(chunk):
        chunk = chunk * scale
        return chunk * cosine - swapped(chunk) * sine

    waiting, d_k, d_v = None, {}, {}
    sums = [[None, None], [None, None]]
    for at in range(CHUNKS):
        query, d_mixed = (ref[:, at * LANES : (at + 1) * LANES] for ref in (q_ref, do_ref))
        d_query = None
        for upper in range(2):
            head = 2 * at + upper
            if head >= HEADS:
                continue
            group = head // GROUPS
            key = 2 * group + upper
            attend = p_ref[head]
            d_attend = contract_last(d_mixed, vz_ref[key])
            soft = attend.astype(F32)
            weighted = soft * d_attend
            inner = jnp.sum(weighted, axis=-1, keepdims=True)
            d_scores = (weighted - soft * inner).astype(BF)
            part = plain(d_scores, kz_ref[key])
            d_query = part if d_query is None else d_query + part
            for which, term in ((0, contract_rows(d_scores, query)), (1, contract_rows(attend, d_mixed))):
                old = sums[which][upper]
                sums[which][upper] = term if old is None else old + term
            if head % GROUPS == GROUPS - 1:
                for which, store in ((0, d_k), (1, d_v)):
                    both = jnp.where(lower, sums[which][0], sums[which][1])
                    store[group] = both + other_half(both)
                sums = [[None, None], [None, None]]
        if at < CHUNKS - 1:
            du_ref[:, at * LANES : (at + 1) * LANES] = back(d_query).astype(BF)
        else:
            waiting = d_query
    tail = jnp.where(lower, waiting, d_k[0])
    du_ref[:, (CHUNKS - 1) * LANES : CHUNKS * LANES] = back(tail).astype(BF)
    for i in range(2):
        at = CHUNKS + i
        du_ref[:, at * LANES : (at + 1) * LANES] = back(jnp.where(lower, d_k[1 + 2 * i], d_k[2 + 2 * i])).astype(BF)
        at = CHUNKS + 2 + i
        du_ref[:, at * LANES : (at + 1) * LANES] = jnp.where(lower, d_v[2 * i], d_v[2 * i + 1]).astype(BF)
    at = CHUNKS + 4
    du_ref[:, at * LANES :] = d_v[4][:, : du_ref.shape[1] - at * LANES].astype(BF)


def router_gate(x, router_row):
    return jax.nn.sigmoid(jnp.sum(x * router_row, axis=-1, keepdims=True))


def masks(select_refs, segment_ref, pad_ref, bias_ref, active_ref):
    seq_len = segment_ref.shape[1]
    square = (seq_len, seq_len)
    query, key = (lax.broadcasted_iota(jnp.int32, square, axis) for axis in (0, 1))
    diagonal = query == key
    segment = segment_ref[...].astype(F32)
    own = jnp.sum(jnp.where(diagonal, segment, 0.0), axis=1, keepdims=True)
    near = (key <= query) & (segment == own)
    real = pad_ref[...] == 1
    for recursion, ref in enumerate(select_refs):
        place = lax.broadcasted_iota(jnp.int32, (seq_len, ref.shape[1]), 0)
        active = jnp.max(jnp.where(ref[...] == place, 1.0, 0.0), axis=1, keepdims=True)
        active_ref[recursion] = active
        along = jnp.sum(jnp.where(diagonal, active, 0.0), axis=0, keepdims=True)
        usable = (along > 0.0) & real
        bias_ref[recursion] = jnp.where(near & (usable | diagonal), 0.0, -1e30)


def first_attention(x_ref, sel_one, sel_two, sel_three, segment_ref, pad_ref, cos_ref, sin_ref, gain_one, gain_two, qkv_w, out_w,
                    n1_ref, q_ref, kz_ref, vz_ref, p_ref, o_ref, attn_ref, n2_ref, bias_ref, active_ref):
    n1, o = n1_ref.at[0], o_ref.at[0]
    masks((sel_one, sel_two, sel_three), segment_ref, pad_ref, bias_ref, active_ref)
    attention_forward(x_ref, bias_ref.at[0], cos_ref, sin_ref, gain_one[...], qkv_w, n1, q_ref, kz_ref, vz_ref, p_ref, o)
    attention_out(x_ref, o, out_w, gain_two[...], attn_ref, n2_ref)


def load_all(pairs, sems):
    return [pltpu.make_async_copy(src, dst, sems.at[i]) for i, (src, dst) in enumerate(pairs)]


def waits_at(condition, copies):
    def ready(*which):
        @pl.when(condition)
        def _():
            for i in which:
                copies[i].wait()

    return ready


def finish_attention_backward(x_ref, gain, active_ref, du_ref, qkv_w, base, state, total, out_ref):
    total[...] = contract_last(du_ref[...], qkv_w[...])
    terms = jnp.zeros((1, state.shape[1]), F32)

    def lap(i, terms):
        rows = pl.ds(pl.multiple_of(i * ROWS, ROWS), ROWS)
        d_rows, term = norm_back(x_ref[rows, :], gain, total[rows, :])
        new = jnp.where(active_ref[rows, :] > 0, base[rows, :] + d_rows, state[rows, :])
        out_ref[rows, :] = new
        return terms + term

    return lax.fori_loop(0, state.shape[0] // ROWS, lap, terms)


def all_steps(bias_ref, active_ref, router_ref, cos_ref, sin_ref, gain_one, gain_two,
              hidden_hbm, d_hidden_hbm, attn0_hbm, n20_hbm, n1_in, o_in, qkv_hbm, out_hbm, *rest):
    feed_hbm, rest = rest[:6], rest[6:]
    (n1_out, o_out, n2_out, m0_out, m1_out, df_out, dg0_out, dg1_out, dw0_out, dw1_out, da_out, du_out, final_out,
     base_ref, state_ref, small_ref), rest = rest[:16], rest[16:]
    qkv_w, out_w, *feed_w = rest[:8]
    (xs, attns, fs, slope0, slope1, silu0, silu1, qs, kzs, vzs, ps, n1, o, n2, m0, m1, df, dg0, dg1, dw0, dw1, da, du,
     total, d_branch, do_ref, load_sems, out_sems) = rest[8:]
    width = state_ref.shape[1]
    laps = state_ref.shape[0] // ROWS
    loads = load_all(
        [*zip(feed_hbm, feed_w), (qkv_hbm, qkv_w), (out_hbm, out_w),
         (n20_hbm, n2), (attn0_hbm, attns.at[0]), (hidden_hbm, xs.at[0]), (d_hidden_hbm, state_ref)], load_sems)
    for i in (8, 0, 1, 2, 3, 4, 5, 9, 10, 6, 7, 11):
        loads[i].start()
    loads[8].wait()

    places = dict(n2=(n2, n2_out, 0), m0=(m0, m0_out, 1), m1=(m1, m1_out, 2), n1=(n1, n1_out, 3), o=(o, o_out, 4),
                  df=(df, df_out, 5), dg0=(dg0, dg0_out, 6), dg1=(dg1, dg1_out, 7), dw0=(dw0, dw0_out, 8),
                  dw1=(dw1, dw1_out, 9), da=(da, da_out, 10), du=(du, du_out, 11))

    def leaving(name, recursion):
        source, target, sem = places[name]
        return pltpu.make_async_copy(source, target.at[recursion], out_sems.at[sem])

    def start(recursion, *names):
        for name in names:
            leaving(name, recursion).start()

    def wait(recursion, *names):
        for name in names:
            leaving(name, recursion).wait()

    def forward(r, carry):
        ready = waits_at(r == 0, loads)
        start(r, "n2")

        @pl.when(r > 0)
        def _():
            wait(r - 1, "m0", "m1")

        feed_forward(n2, ((*feed_w[:3], m0, slope0.at[r], silu0.at[r]), (*feed_w[3:], m1, slope1.at[r], silu1.at[r])), total, ready)
        start(r, "m0", "m1")
        ready(9, 10)
        router_row = router_ref[pl.ds(r, 1), :]

        def finish(rows):
            x = xs[r, rows, :]
            f = total[rows, :].astype(BF)
            fs[r, rows, :] = f
            branch = attns[r, rows, :] + f.astype(F32)
            xs[r + 1, rows, :] = jnp.where(active_ref[r, rows, :] > 0, x + router_gate(x, router_row) * branch, x)

        over_rows(total.shape[0], finish)
        ready(6, 7)
        wait(r, "n2")

        @pl.when(r < RECURSIONS - 1)
        def _():
            @pl.when(r > 0)
            def _():
                wait(r, "n1", "o")

            attention_forward(xs.at[r + 1], bias_ref.at[r + 1], cos_ref, sin_ref, gain_one[...], qkv_w,
                              n1, qs.at[r], kzs.at[r], vzs.at[r], ps.at[r], o)
            start(r + 1, "n1", "o")
            attention_out(xs.at[r + 1], o, out_w, gain_two[...], attns.at[r + 1], n2)

        return carry

    lax.fori_loop(0, RECURSIONS, forward, 0)
    final = pltpu.make_async_copy(xs.at[RECURSIONS], final_out, out_sems.at[12])
    final.start()
    loads[11].wait()
    small_ref[...] = jnp.zeros(small_ref.shape, F32)

    def backward(i, carry):
        r = RECURSIONS - 1 - i
        router_row = router_ref[pl.ds(r, 1), :]

        @pl.when(i > 0)
        def _():
            wait(r + 1, "df", "dg0", "dg1", "dw0", "dw1", "da")

        def enter(lap, terms):
            rows = pl.ds(pl.multiple_of(lap * ROWS, ROWS), ROWS)
            x = xs[r, rows, :]
            d_new = jnp.where(active_ref[r, rows, :] > 0, state_ref[rows, :], 0.0)
            gate = router_gate(x, router_row)
            branch = attns[r, rows, :] + fs[r, rows, :].astype(F32)
            d_gate = jnp.sum(d_new * branch, axis=-1, keepdims=True)
            d_logit = d_gate * gate * (1.0 - gate)
            spread = gate * d_new
            d_branch[rows, :] = spread
            df[rows, :] = spread.astype(BF)
            base_ref[rows, :] = d_new + d_logit * router_row
            return terms + jnp.sum(d_logit * x, axis=0, keepdims=True)

        small_ref[pl.ds(2 + r, 1), :] = lax.fori_loop(0, laps, enter, jnp.zeros((1, width), F32))
        start(r, "df")
        feed_backward(df, ((*feed_w[:3], slope0.at[r], silu0.at[r], dg0, dw0), (*feed_w[3:], slope1.at[r], silu1.at[r], dg1, dw1)),
                      total, lambda *which: None)
        start(r, "dg0", "dg1", "dw0", "dw1")

        def leave(lap, terms):
            rows = pl.ds(pl.multiple_of(lap * ROWS, ROWS), ROWS)
            after = xs[r, rows, :] + attns[r, rows, :]
            d_after, term = norm_back(after, gain_two[...], total[rows, :].astype(BF).astype(F32))
            da[rows, :] = (d_branch[rows, :] + d_after).astype(BF)
            base_ref[rows, :] = base_ref[rows, :] + d_after
            return terms + term

        small_ref[1:2, :] = small_ref[1:2, :] + lax.fori_loop(0, laps, leave, jnp.zeros((1, width), F32))
        start(r, "da")

        @pl.when(r > 0)
        def _():
            @pl.when(i > 0)
            def _():
                wait(r + 1, "du")

            attention_backward(da, out_w, qkv_w, cos_ref, sin_ref, qs.at[r - 1], kzs.at[r - 1], vzs.at[r - 1], ps.at[r - 1], do_ref, du)
            start(r, "du")
            term = finish_attention_backward(xs.at[r], gain_one[...], active_ref.at[r], du, qkv_w, base_ref, state_ref, total, state_ref)
            small_ref[0:1, :] = small_ref[0:1, :] + term

        return carry

    lax.fori_loop(0, RECURSIONS, backward, 0)
    wait(RECURSIONS - 1, "m0", "m1", "n1", "o")
    wait(0, "df", "dg0", "dg1", "dw0", "dw1", "da")
    wait(1, "du")
    final.wait()


def last_attention(active_ref, cos_ref, sin_ref, gain_one, q_ref, kz_ref, vz_ref, p_ref, d_attn_ref, small_in, out_w,
                   x_hbm, base_hbm, state_hbm, qkv_hbm, du_in, token, du_ref, d_input_ref, small_ref,
                   do_ref, total, x, base, state, qkv_w, sems):
    copies = load_all([(qkv_hbm, qkv_w), (x_hbm, x), (base_hbm, base), (state_hbm, state)], sems)
    for copy in copies:
        copy.start()
    attention_backward(d_attn_ref.at[0], out_w, qkv_w, cos_ref, sin_ref, q_ref, kz_ref, vz_ref, p_ref, do_ref, du_ref.at[0])
    for copy in copies:
        copy.wait()
    term = finish_attention_backward(x, gain_one[...], active_ref.at[0], du_ref.at[0], qkv_w, base, state, total, d_input_ref)
    small_ref[...] = small_in[...]
    small_ref[0:1, :] = small_in[0:1, :] + term


def swap_dp(values_in, bit, n_dp):
    return lax.ppermute(values_in, "dp", [(i, i ^ (1 << bit)) for i in range(n_dp)])


def swap_mp(values_in):
    return lax.ppermute(values_in, "mp", [(0, 1), (1, 0)])


def halving(parts, order, n_dp, index):
    bits = n_dp.bit_length() - 1
    left = list(range(bits - 1, -1, -1))
    shape = parts.shape[1:]
    held = parts.reshape((2,) * bits + shape)
    for step, bit in enumerate(order):
        at = left.index(bit)
        upper = ((index >> bit) & 1) == 1
        low = lax.index_in_dim(held, 0, at, keepdims=False)
        high = lax.index_in_dim(held, 1, at, keepdims=False)
        keep, send = jnp.where(upper, high, low), jnp.where(upper, low, high)
        got = swap_dp(send, bit, n_dp)
        last = step == bits - 1
        total = keep.astype(F32) + got.astype(F32)
        held = total if last else total.astype(BF)
        left.remove(bit)
    return held


def orders_of(bits):
    rest = list(range(3, bits))
    if bits < 3:
        return [list(range(bits))] * 3
    return [[0, 1, 2] + rest, [1, 0, 2] + rest, [2, 0, 1] + rest]


PART = 2 * LANES
FFN_TILES = (4, 4, 2)
FFN_ORDERS = ((0, 1, 2, 3), (2, 0, 1, 3), (1, 2, 3, 0))
ATTN_ORDERS = ((0, 3, 2, 1), (3, 0, 1, 2))
SCHEDULE = (
    "T0", "T1", "T2", "A",
    "F0", "F1", "F2", "A0", "A1",
    "F0", "F1", "F2", "A0", "A1",
    "F0", "F1", "F2", "A0", "A1",
)
SMALL = 64


def halves(bit, outs, index):
    mine = (index >> bit) & 1
    inner = 1 << bit
    for out, which in zip(outs, (mine, 1 - mine)):
        for p in range(out.shape[0]):
            for q in range(inner):
                yield out, p, q, p * 2 * inner + which * inner + q


def stacked_copies(pairs, sems):
    flat_pairs = []
    for sources, target in pairs:
        rows = target.shape[0] // 2
        flat_pairs += [(source, target.at[pl.ds(i * rows, rows)]) for i, source in enumerate(sources)]
    copies = load_all(flat_pairs, sems)
    for copy in copies:
        copy.start()
    return [copies[i : i + 2] for i in range(0, len(copies), 2)]


def ffn_terms(bit, tiles, at, n2_a, n2_b, df_a, df_b, dg_a, dg_b, dw_a, dw_b, m_a, m_b, token, keep_ref, send_ref,
              left, right, flat, sems):
    width = left.shape[2]
    columns = pl.ds(at, tiles * LANES)
    parts = [tuple(ref.at[:, columns] for ref in both) for both in ((dg_a, dg_b), (dw_a, dw_b), (m_a, m_b))]
    n2, dg, dw, df, m = stacked_copies(
        [((n2_a, n2_b), left.at[0]), (parts[0], right.at[0]), (parts[1], right.at[1]),
         ((df_a, df_b), left.at[1]), (parts[2], right.at[2])], sems)
    for matrix, needed in enumerate((n2 + dg, dw, df + m)):
        for copy in needed:
            copy.wait()
        terms = contract_rows(left[matrix // 2], right[matrix])
        for c in range(tiles):
            flat[pl.ds(tiles * width * matrix + c, width, stride=tiles), :] = terms[:, c * LANES : (c + 1) * LANES]
    rows = keep_ref.shape[2]
    for out, p, q, shard in halves(bit, (keep_ref, send_ref), lax.axis_index("dp")):
        out[p, q] = flat[pl.ds(pl.multiple_of(shard * rows, 8), rows), :].astype(BF)


def small_rows(small):
    rest = -small.shape[1] % LANES
    small = jnp.concatenate([small, jnp.zeros((small.shape[0], rest), F32)], axis=1)
    return jnp.concatenate([small[:, at : at + LANES] for at in range(0, small.shape[1], LANES)], axis=0)


def split_small(small, ref, start):
    high = small.astype(BF)
    ref[start : start + SMALL, :] = high
    ref[start + SMALL : start + 2 * SMALL, :] = (small - high.astype(F32)).astype(BF)


def rounded_small(small):
    high = small.astype(BF)
    return high.astype(F32) + (small - high.astype(F32)).astype(BF).astype(F32)


def joined_small(ref, start):
    return ref[start : start + SMALL, :].astype(F32) + ref[start + SMALL : start + 2 * SMALL, :].astype(F32)


def attn_terms(bits, cut, n1_a, n1_b, du_a, du_b, o_a, o_b, da_a, da_b, small_a, small_b, token,
               keep0, send0, keep1, send1, small_out, left, du_rows, da_rows, terms, flat, sems):
    width = left.shape[2]
    base = 0
    lower = lane_of(width // 2) < HEAD_DIM
    n1, du, o, da = stacked_copies(
        [((n1_a, n1_b), left.at[0]), ((du_a, du_b), du_rows), ((o_a, o_b), left.at[1]), ((da_a, da_b), da_rows)], sems)
    for which, (right, needed) in enumerate(((du_rows, n1 + du), (da_rows, o + da))):
        for copy in needed:
            copy.wait()
        columns = right.shape[1]
        half = columns // LANES
        for start in range(0, columns, PART):
            stop = min(columns, start + PART)
            block = contract_rows(left[which], right[:, start:stop])
            if stop - start < PART:
                block = jnp.concatenate([block, jnp.zeros((width, PART - (stop - start)), F32)], axis=1)
            for part in range(0, stop - start, LANES):
                terms[(start + part) // LANES] = block[:, part : part + LANES]
        step = 2 * columns // LANES
        count = width // 2
        after = first_odd = None
        for c in range(half + 1):
            even = terms[c, pl.ds(0, count, stride=2), :]
            odd = other_half(terms[c, pl.ds(1, count, stride=2), :])
            if c < half:
                flat[pl.ds(base + c, count, stride=step), :] = even
            else:
                flat[pl.ds(base + c, count, stride=step), :] = jnp.where(lower, even, first_odd)
            if c == 0:
                first_odd = odd
            else:
                flat[pl.ds(base + half + c, count, stride=step), :] = jnp.where(lower, after, odd)
            after = odd
        base += width * columns // LANES
    index, core = lax.axis_index("dp"), lax.axis_index("mp")
    total = rounded_small(small_rows(small_a[...])) + rounded_small(small_rows(small_b[...]))
    small_out[...] = total
    shards, depth = 2 * keep0.shape[0] * keep0.shape[1], cut + keep1.shape[2]
    split_small(total, send0, shards // 2 * cut)

    def rows_of_shard(shard, low, high):
        start = pl.multiple_of((2 * shard + core) * depth + low, 8)
        return flat[pl.ds(start, high - low), :].astype(BF)

    mine = (index >> bits[0]) & 1
    inner = 1 << bits[0]
    for p in range(keep0.shape[0]):
        for q in range(inner):
            shard = 2 * p * inner + q
            keep0[p, q] = rows_of_shard(shard + mine * inner, 0, cut)
            at = (p * inner + q) * cut
            send0[at : at + cut, :] = rows_of_shard(shard + (1 - mine) * inner, 0, cut)
    for out, p, q, shard in halves(bits[1], (keep1, send1), index):
        out[p, q] = rows_of_shard(shard, cut, depth)


def fold(bit, kept, got, token, keep, send):
    mine = (lax.axis_index("dp") >> bit) & 1
    for p in range(kept.shape[0]):
        for q in range(kept.shape[2]):
            for out, which in ((keep, mine), (send, 1 - mine)):
                out[p, q] = (kept[p, which, q].astype(F32) + got[p, which, q].astype(F32)).astype(BF)


def fold_small(bit, kept, got, small, token, keep, send, small_out):
    mine = (lax.axis_index("dp") >> bit) & 1
    outer, _, inner, rows, _ = kept.shape
    for p in range(outer):
        for q in range(inner):
            totals = []
            for which in (mine, 1 - mine):
                start = pl.multiple_of(((2 * p + which) * inner + q) * rows, 16)
                totals.append((kept[p, which, q].astype(F32) + got[pl.ds(start, rows), :].astype(F32)).astype(BF))
            keep[p, q] = totals[0]
            at = (p * inner + q) * rows
            send[at : at + rows, :] = totals[1]
    total = rounded_small(small[...]) + joined_small(got, 2 * outer * inner * rows)
    small_out[...] = total
    split_small(total, send, outer * inner * rows)


def finish_streams(tiles, *refs):
    count = len(tiles)
    feeds, refs = refs[: 2 * count], refs[2 * count :]
    attn, refs = refs[:4], refs[4:]
    small, ffn_out, attn_out, one_out, two_out, router_out, flat = refs
    every = sum(tiles)
    rows = ffn_out.shape[0] // every
    base = 0
    for i, wide in enumerate(tiles):
        flat[: rows * wide, :] = feeds[2 * i][...].astype(F32) + feeds[2 * i + 1][...].astype(F32)
        for c in range(wide):
            ffn_out[pl.ds(base + c, rows, stride=every), :] = flat[pl.ds(c, rows, stride=wide), :]
        base += wide
    cut = attn[0].shape[0]
    attn_out[:cut, :] = attn[0][...].astype(F32) + attn[1][:cut, :].astype(F32)
    attn_out[cut:, :] = attn[2][...].astype(F32) + attn[3][...].astype(F32)
    total = rounded_small(small[...]) + joined_small(attn[1], cut)
    width = one_out.shape[1]
    for at in range(0, width, LANES):
        stop = min(width, at + LANES)
        tile = total[at // LANES * 8 : at // LANES * 8 + 8, : stop - at]
        one_out[:, at:stop] = tile[0:1]
        two_out[:, at:stop] = tile[1:2]
        router_out[:, at:stop] = tile[2 : 2 + RECURSIONS]


class Stream:
    def __init__(self, order, bits):
        self.order, self.left, self.done = order, list(range(bits - 1, -1, -1)), 0
        self.kept = self.got = None

    def shape_for(self, array):
        at = self.left.index(self.order[self.done])
        rows, lanes = array.shape[-2:]
        return (1 << at, 2, 1 << (len(self.left) - 1 - at), rows, lanes)

    def sent(self, kept, send, n_dp):
        bit = self.order[self.done]
        self.kept, self.got = kept, swap_dp(send, bit, n_dp)
        self.left.remove(bit)
        self.done += 1


def on_device(
    hidden_in,
    sel_one,
    sel_two,
    sel_three,
    segment_ids,
    pad_mask,
    qkv_weight,
    out_weight,
    gate_weight,
    up_weight,
    down_weight,
    norm_one,
    norm_two,
    router_weight,
    d_hidden,
):
    seq_len, width = hidden_in.shape
    n_dp, n_mp = lax.axis_size("dp"), lax.axis_size("mp")
    dp_index, mp_index = lax.axis_index("dp"), lax.axis_index("mp")
    cosine, sine = rotary_tables(seq_len)
    weights = [(gate_weight, up_weight, down_weight)]
    weights.append(tuple(swap_mp(w) for w in weights[0]))
    gain_one, gain_two = norm_one.reshape(1, width), norm_two.reshape(1, width)
    padded = CHUNKS * LANES
    units = gate_weight.shape[1]
    feed_weights = (*weights[0], *weights[1])

    def shape(*dims, dtype=BF):
        return jax.ShapeDtypeStruct(dims, dtype)

    def whole(*dims, **kw):
        return pl.BlockSpec(dims, lambda *_: (0,) * len(dims), **kw)

    anywhere = pl.BlockSpec(memory_space=pl.ANY)
    one = pl.Buffered(1)
    stack = RECURSIONS, seq_len
    heads = (2 * KV_HEADS, seq_len, LANES)
    square = (HEADS, seq_len, seq_len)
    n1, q, kz, vz, p, o, attn, n2, bias, active = pl.pallas_call(
        first_attention,
        grid=(1,),
        in_specs=[
            whole(seq_len, width), *[whole(*ref.shape) for ref in (sel_one, sel_two, sel_three, segment_ids, pad_mask)],
            whole(seq_len, LANES), whole(seq_len, LANES), whole(1, width), whole(1, width), whole(*qkv_weight.shape), whole(*out_weight.shape),
        ],
        out_specs=[
            whole(1, seq_len, width), whole(seq_len, padded), whole(*heads), whole(*heads), whole(*square),
            whole(1, seq_len, width), whole(seq_len, width), whole(seq_len, width), whole(RECURSIONS, seq_len, seq_len), whole(*stack, 1),
        ],
        out_shape=[
            shape(*stack, width), shape(seq_len, padded), shape(*heads), shape(*heads), shape(*square),
            shape(*stack, width), shape(seq_len, width, dtype=F32), shape(seq_len, width),
            shape(*stack, seq_len, dtype=F32), shape(*stack, 1, dtype=F32),
        ],
        compiler_params=pltpu.CompilerParams(vmem_limit_bytes=VMEM_MIB * MIB),
        cost_estimate=pl.CostEstimate(flops=2 * 10**9, bytes_accessed=12 * 10**6, transcendentals=600000),
        name="first_attention",
    )(hidden_in, sel_one, sel_two, sel_three, segment_ids, pad_mask, cosine, sine, gain_one, gain_two, qkv_weight, out_weight)
    attention_0 = (q, kz, vz, p)
    wide = qkv_weight.shape[1]
    row = (seq_len, width)
    kept = RECURSIONS - 1
    vm = pltpu.VMEM
    results = pl.pallas_call(
        all_steps,
        grid=(1,),
        in_specs=[
            whole(RECURSIONS, seq_len, seq_len), whole(RECURSIONS, seq_len, 1), whole(RECURSIONS, width),
            whole(seq_len, LANES), whole(seq_len, LANES), whole(1, width), whole(1, width), *[anywhere] * 14,
        ],
        out_specs=[*[anywhere] * 13, whole(*row), whole(*row), whole(8, width)],
        out_shape=[
            *[shape(*stack, width)] * 3, *[shape(*stack, units)] * 2, shape(*stack, width), *[shape(*stack, units)] * 4,
            shape(*stack, width), shape(*stack, wide), *[shape(*row, dtype=F32)] * 3, shape(8, width, dtype=F32),
        ],
        scratch_shapes=[
            *[vm(w.shape, BF) for w in (qkv_weight, out_weight, *feed_weights)],
            vm((RECURSIONS + 1, *row), F32), vm((RECURSIONS, *row), F32), vm((RECURSIONS, *row), BF),
            *[vm((*stack, units), BF)] * 4, vm((kept, seq_len, padded), BF), vm((kept, *heads), BF), vm((kept, *heads), BF),
            vm((kept, *square), BF), *[vm(row, BF)] * 3, *[vm((seq_len, units), BF)] * 2, vm(row, BF), *[vm((seq_len, units), BF)] * 4,
            vm(row, BF), vm((seq_len, wide), BF), vm(row, F32), vm(row, F32), vm((seq_len, padded), BF),
            pltpu.SemaphoreType.DMA((12,)), pltpu.SemaphoreType.DMA((13,)),
        ],
        input_output_aliases={11: 0, 12: 1},
        compiler_params=pltpu.CompilerParams(vmem_limit_bytes=VMEM_MIB * MIB),
        cost_estimate=pl.CostEstimate(flops=23 * 10**9, bytes_accessed=50 * 10**6, transcendentals=4 * 10**6),
        name="all_steps",
    )(bias, active, router_weight, cosine, sine, gain_one, gain_two, hidden_in, d_hidden, attn, n2, n1, o,
      qkv_weight, out_weight, *feed_weights)
    n1, o, n2, m0, m1, d_feed, dg0, dg1, dw0, dw1, d_attn, du, state, base, grad_state, small = results

    def run_last(token):
        return pl.pallas_call(
            last_attention,
            grid=(1,),
            in_specs=[
                whole(1, seq_len, 1), whole(seq_len, LANES), whole(seq_len, LANES), whole(1, width),
                whole(seq_len, padded), whole(*heads), whole(*heads), whole(*square), whole(1, seq_len, width),
                whole(8, width), whole(*out_weight.shape), *[anywhere] * 6,
            ],
            out_specs=[whole(1, seq_len, qkv_weight.shape[1]), whole(seq_len, width), whole(8, width)],
            out_shape=[shape(*stack, qkv_weight.shape[1]), shape(seq_len, width, dtype=F32), shape(8, width, dtype=F32)],
            scratch_shapes=[
                pltpu.VMEM((seq_len, padded), BF), *[pltpu.VMEM((seq_len, width), F32)] * 4,
                pltpu.VMEM(qkv_weight.shape, BF), pltpu.SemaphoreType.DMA((4,)),
            ],
            input_output_aliases={15: 0},
            compiler_params=pltpu.CompilerParams(vmem_limit_bytes=VMEM_MIB * MIB),
            cost_estimate=pl.CostEstimate(flops=1, bytes_accessed=1, transcendentals=0),
            name="last_attention",
        )(active, cosine, sine, gain_one, *attention_0, d_attn, small, out_weight, hidden_in, base, grad_state, qkv_weight, du, token)

    def rows_of(stacked):
        return stacked.reshape(-1, stacked.shape[-1])

    two, feed = rows_of(n2), rows_of(d_feed)
    sides = ((dg0, dw0, m0), (dg1, dw1, m1))
    bits = n_dp.bit_length() - 1
    share = (qkv_weight.size + out_weight.size) // (n_dp * n_mp)
    if bits == 4 and 3 * width % n_dp == 0 and units == sum(FFN_TILES) * LANES and share % (8 * LANES) == 0:
        crossed = [(t, swap_mp(far)) for t, far in
                   ((n2, n2), (d_feed, d_feed), (dg0, dg1), (dw0, dw1), (m0, m1))]
        factors = [rows_of(t) for both in crossed for t in both]
        streams = [Stream(order, bits) for order in FFN_ORDERS]
        pair = [Stream(order, bits) for order in ATTN_ORDERS]
        depth = share // LANES
        cut = depth // 2 // 16 * 16
        common = dict(
            grid=(1,),
            compiler_params=pltpu.CompilerParams(vmem_limit_bytes=VMEM_MIB * MIB),
            cost_estimate=pl.CostEstimate(flops=1, bytes_accessed=1, transcendentals=0),
        )

        def wholes(arrays):
            return [whole(*t.shape) for t in arrays]

        def terms_of(j, token):
            stream, tiles = streams[j], FFN_TILES[j]
            at = sum(FFN_TILES[:j]) * LANES
            bit = stream.order[0]
            dims = (1 << (bits - 1 - bit), 1 << bit, 3 * width // n_dp * tiles, LANES)
            both = 2 * RECURSIONS * seq_len
            keep, send = pl.pallas_call(
                functools.partial(ffn_terms, bit, tiles, at),
                in_specs=[anywhere] * (len(factors) + 1),
                out_specs=[whole(*dims)] * 2,
                out_shape=[shape(*dims)] * 2,
                scratch_shapes=[pltpu.VMEM((2, both, width), BF), pltpu.VMEM((3, both, tiles * LANES), BF),
                                pltpu.VMEM((3 * width * tiles, LANES), F32), pltpu.SemaphoreType.DMA((10,))],
                name=f"ffn_terms_{j}",
                **common,
            )(*factors, token)
            stream.sent(keep, send, n_dp)
            return keep

        def fold_stream(stream, token, small_own=None):
            bit = stream.order[stream.done]
            dims = stream.shape_for(stream.kept)
            kept = stream.kept.reshape(dims)
            held = (dims[0], *dims[2:])
            if small_own is None:
                operands = (kept, stream.got.reshape(dims))
                outs = (shape(*held), shape(*held))
            else:
                operands = (kept, stream.got, small_own)
                outs = (shape(*held), shape(dims[0] * dims[2] * dims[3] + 2 * SMALL, LANES), shape(SMALL, LANES, dtype=F32))
            results = pl.pallas_call(
                functools.partial(fold if small_own is None else fold_small, bit),
                in_specs=[*wholes(operands), anywhere],
                out_specs=wholes(outs),
                out_shape=outs,
                name="fold_terms",
                **common,
            )(*operands, token)
            stream.sent(results[0], results[1], n_dp)
            return results

        du, grad_state, small = run_last(small)
        first_crossed = [(rows_of(n1), swap_mp(rows_of(n1))), (rows_of(du), swap_mp(rows_of(du)))]
        late_crossed = [(rows_of(o), swap_mp(rows_of(o))), (rows_of(d_attn), swap_mp(rows_of(d_attn))), (small, swap_mp(small))]
        token = small
        for item in SCHEDULE:
            if item[0] == "T":
                token = terms_of(int(item[1:]), token)
            elif item[0] == "F":
                token = fold_stream(streams[int(item[1:])], token)[0]
            elif item == "A":
                firsts = [t.order[0] for t in pair]
                dims = [(1 << (bits - 1 - bit), 1 << bit, rows, LANES) for bit, rows in zip(firsts, (cut, depth - cut))]
                operands = [t for both in (*first_crossed, *late_crossed) for t in both]
                outs = (shape(*dims[0]), shape(n_dp // 2 * cut + 2 * SMALL, LANES), shape(*dims[1]), shape(*dims[1]),
                        shape(SMALL, LANES, dtype=F32))
                keep0, send0, keep1, send1, small_own = pl.pallas_call(
                    functools.partial(attn_terms, tuple(firsts), cut),
                    in_specs=[*[anywhere] * 8, *wholes(operands[8:]), anywhere],
                    out_specs=wholes(outs),
                    out_shape=outs,
                    scratch_shapes=[pltpu.VMEM((2, 2 * RECURSIONS * seq_len, width), BF),
                                    *[pltpu.VMEM((2 * RECURSIONS * seq_len, t.shape[-1]), BF) for t in (du, d_attn)],
                                    pltpu.VMEM((-(-du.shape[-1] // PART) * 2, width, LANES), F32),
                                    pltpu.VMEM((n_dp * 2 * depth, LANES), F32), pltpu.SemaphoreType.DMA((8,))],
                    name="attn_terms",
                    **common,
                )(*operands, token)
                pair[0].sent(keep0, send0, n_dp)
                pair[1].sent(keep1, send1, n_dp)
                token = small_own
            elif item == "A0":
                token, _, small_own = fold_stream(pair[0], token, small_own)
            else:
                token = fold_stream(pair[1], token)[0]
        ends = [t.reshape(t.shape[-2:]) for stream in (*streams, *pair) for t in (stream.kept, stream.got)]
        outs = (shape(3 * width // n_dp * sum(FFN_TILES), LANES, dtype=F32), shape(depth, LANES, dtype=F32),
                shape(1, width, dtype=F32), shape(1, width, dtype=F32), shape(RECURSIONS, width, dtype=F32))
        ffn_flat, attn_flat, one, two, router = pl.pallas_call(
            functools.partial(finish_streams, FFN_TILES),
            in_specs=wholes((*ends, small_own)),
            out_specs=wholes(outs),
            out_shape=outs,
            scratch_shapes=[pltpu.VMEM((3 * width // n_dp * max(FFN_TILES), LANES), F32)],
            name="finish_streams",
            **common,
        )(*ends, small_own)
        return (state, grad_state, attn_flat.reshape(-1), ffn_flat.reshape(1, -1), one.reshape(-1), two.reshape(-1), router)

    du, grad_state, small = run_last(small)

    def side_terms(side, columns):
        return jnp.concatenate(
            [
                contract_rows(left, rows_of(sides[side][which])[:, columns]).astype(BF)
                for which, left in enumerate((two, two, feed))
            ],
            axis=0,
        )

    orders = orders_of(bits)
    if 3 * width % n_dp == 0 and units % 1280 == 0:
        fifth = units // 5
        streams = [(orders[i], slice(j * fifth, (j + 1) * fifth)) for i, j in ((0, 0), (1, 1), (2, 2), (0, 3), (1, 4))]
        done = []
        for order, columns in streams:
            terms = side_terms(0, columns).astype(F32) + swap_mp(side_terms(1, columns)).astype(F32)
            done.append(halving(terms.astype(BF).reshape(n_dp, 3 * width // n_dp, fifth), order, n_dp, dp_index))
        ffn_flat = jnp.concatenate(done, axis=1).reshape(1, -1)
    else:
        terms = side_terms(0, slice(None)).astype(F32) + swap_mp(side_terms(1, slice(None))).astype(F32)
        terms = terms.astype(BF).reshape(n_dp, 3 * width * units // n_dp // 128, 128)
        ffn_flat = halving(terms, orders[0], n_dp, dp_index).reshape(1, -1)

    grad_qkv = contract_rows(rows_of(n1), rows_of(du)).astype(BF)
    grad_out = contract_rows(rows_of(o), rows_of(d_attn)).astype(BF)
    attn = jnp.concatenate([grad_qkv.reshape(-1), grad_out.reshape(-1)]).reshape(n_dp, 2, share // 128, 128)
    keep = jnp.where(mp_index == 0, attn[:, 0], attn[:, 1])
    send = jnp.where(mp_index == 0, attn[:, 1], attn[:, 0])
    attn = (keep.astype(F32) + swap_mp(send).astype(F32)).astype(BF)
    cuts = [0, (share // 128) // 24 * 8, (share // 128) // 12 * 8, share // 128]
    attn_flat = jnp.concatenate(
        [halving(attn[:, a:b], order, n_dp, dp_index) for a, b, order in zip(cuts, cuts[1:], orders)], axis=0
    ).reshape(-1)

    small = small + swap_mp(small)
    for bit in range(bits):
        small = small + swap_dp(small, bit, n_dp)
    return (state, grad_state, attn_flat, ffn_flat, small[0], small[1], small[2 : 2 + RECURSIONS])


def solution(mesh):
    both = P(("dp", "mp"), None)
    in_specs = (
        both,
        both,
        both,
        both,
        both,
        both,
        P(),
        P(),
        P(None, "mp"),
        P(None, "mp"),
        P(None, "mp"),
        P(),
        P(),
        P(),
        both,
    )
    out_specs = (both, both, P(("dp", "mp")), P("mp", "dp"), P(), P(), P())
    return jax.shard_map(
        on_device, mesh=mesh, in_specs=in_specs, out_specs=out_specs, check_vma=False
    )
```

```python
import functools
import math

import jax
import jax.numpy as jnp
import numpy as np
from jax import lax
from jax.experimental import pallas as pl
from jax.experimental.pallas import tpu as pltpu
from jax.sharding import PartitionSpec as P

HEADS = 15
KV_HEADS = 5
HEAD_DIM = 64
RECURSIONS = 3
GROUPS = HEADS // KV_HEADS
EPS = 1e-05
BF = jnp.bfloat16
F32 = jnp.float32


LANES = 128
CHUNKS = -(-HEADS * HEAD_DIM // LANES)
ROWS = 32
BLOCK = 256
MIB = 1 << 20
VMEM_MIB = 63


def rotary_tables(seq_len):
    half = HEAD_DIM // 2
    frequency = np.float32(100000.0) ** (
        np.float32(-2.0) * np.arange(half, dtype=np.float32) / np.float32(HEAD_DIM)
    )
    angles = np.arange(seq_len, dtype=np.float32)[:, None] * frequency.astype(np.float32)
    cosine, sine = np.cos(angles), np.sin(angles)
    return (
        jnp.asarray(np.concatenate([cosine] * 4, axis=1), F32),
        jnp.asarray(np.concatenate([-sine, sine] * 2, axis=1), F32),
    )


def contract_rows(left, right):
    return lax.dot_general(left, right, (((0,), (0,)), ((), ())), preferred_element_type=F32)


def contract_last(left, right):
    return lax.dot_general(left, right, (((1,), (1,)), ((), ())), preferred_element_type=F32)


def plain(left, right):
    return jnp.dot(left, right, preferred_element_type=F32)


def inverse_rms(rows):
    return lax.rsqrt(jnp.mean(rows * rows, axis=-1, keepdims=True) + EPS)


def norm_back(rows, gain, d_out):
    inv = inverse_rms(rows)
    scaled = d_out * gain
    inner = jnp.mean(scaled * rows, axis=-1, keepdims=True)
    d_rows = inv * scaled - rows * (inv * inv * inv * inner)
    return d_rows, jnp.sum(d_out * rows * inv, axis=0, keepdims=True)


def lane_of(rows):
    return lax.broadcasted_iota(jnp.int32, (rows, LANES), 1)


def swapped(chunk):
    first = lane_of(chunk.shape[0]) % HEAD_DIM < HEAD_DIM // 2
    return jnp.where(first, pltpu.roll(chunk, LANES - 32, 1), pltpu.roll(chunk, 32, 1))


def other_half(chunk):
    return pltpu.roll(chunk, HEAD_DIM, 1)


def over_rows(count, body):
    def lap(i, carry):
        body(pl.ds(pl.multiple_of(i * ROWS, ROWS), ROWS))
        return carry

    lax.fori_loop(0, count // ROWS, lap, 0)


def attention_forward(x_ref, bias_ref, cos_ref, sin_ref, gain, qkv_w, n1_ref, q_ref, kz_ref, vz_ref, p_ref, o_ref):
    seq_len, width = x_ref.shape
    scale = 1.0 / math.sqrt(HEAD_DIM)

    def norm(rows):
        x = x_ref[rows, :]
        n1_ref[rows, :] = (x * inverse_rms(x) * gain).astype(BF)

    over_rows(seq_len, norm)
    lower = lane_of(seq_len) < HEAD_DIM
    n1 = n1_ref[...]

    def spread(ref, head, chunk, upper):
        flipped = other_half(chunk)
        here, there = (flipped, chunk) if upper else (chunk, flipped)
        ref[2 * head] = jnp.where(lower, here, 0.0).astype(BF)
        ref[2 * head + 1] = jnp.where(lower, 0.0, there).astype(BF)

    columns = qkv_w.shape[1]
    for start in range(0, columns, 2 * LANES):
        wide = plain(n1, qkv_w[:, start : min(start + 2 * LANES, columns)])
        for part in range(0, wide.shape[1], LANES):
            chunk = wide[:, part : part + LANES]
            if chunk.shape[1] < LANES:
                chunk = jnp.concatenate([chunk, jnp.zeros_like(chunk)], axis=1)
            at = (start + part) // LANES
            heads = (2 * at, 2 * at + 1)
            if heads[0] < HEADS + KV_HEADS:
                chunk = chunk * cos_ref[...] + swapped(chunk) * sin_ref[...]
                if heads[0] < HEADS:
                    q_ref[:, at * LANES : (at + 1) * LANES] = chunk.astype(BF)
            for upper, head in enumerate(heads):
                if HEADS <= head < HEADS + KV_HEADS:
                    spread(kz_ref, head - HEADS, chunk, upper)
                elif HEADS + KV_HEADS <= head < HEADS + 2 * KV_HEADS:
                    spread(vz_ref, head - HEADS - KV_HEADS, chunk, upper)

    for at in range(CHUNKS):
        query = q_ref[:, at * LANES : (at + 1) * LANES]
        total = None
        for upper in range(2):
            head = 2 * at + upper
            if head < HEADS:
                key = 2 * (head // GROUPS) + upper
                scores = contract_last(query, kz_ref[key]) * scale + bias_ref[...]
                top = jnp.max(scores, axis=-1, keepdims=True)
                exponent = jnp.exp(scores - top)
                share = pl.reciprocal(jnp.sum(exponent, axis=-1, keepdims=True))
                attend = (exponent * share).astype(BF)
                p_ref[head] = attend
                mixed = plain(attend, vz_ref[key])
                total = mixed if total is None else total + mixed
        stop = min(width, (at + 1) * LANES)
        o_ref[:, at * LANES : stop] = total[:, : stop - at * LANES].astype(BF)


def attention_out(x_ref, o_ref, out_w, gain, attn_ref, n2_ref):
    attn_ref[...] = plain(o_ref[...], out_w[...])

    def norm(rows):
        after = x_ref[rows, :] + attn_ref[rows, :]
        n2_ref[rows, :] = (after * inverse_rms(after) * gain).astype(BF)

    over_rows(x_ref.shape[0], norm)


def feed_forward(n2_ref, sides, f_ref, ready):
    n2 = n2_ref[...]
    for side, (gate_w, up_w, down_w, m_ref, slope_ref, silu_ref) in enumerate(sides):
        ready(3 * side, 3 * side + 1)
        for start in range(0, gate_w.shape[1], BLOCK):
            at = slice(start, start + BLOCK)
            g, u = plain(n2, gate_w[:, at]), plain(n2, up_w[:, at])
            s = jax.nn.sigmoid(g)
            silu = g * s
            m_ref[:, at] = (silu * u).astype(BF)
            slope_ref[:, at] = (u * s * (1.0 + g * (1.0 - s))).astype(BF)
            silu_ref[:, at] = silu.astype(BF)
        ready(3 * side + 2)
        part = contract_last(m_ref[...], down_w[...])
        f_ref[...] = part if side == 0 else f_ref[...] + part


def feed_backward(df_ref, sides, d_two_ref, ready):
    d_feed = df_ref[...]
    for side, (gate_w, up_w, down_w, slope_ref, silu_ref, dg_ref, du_ref) in enumerate(sides):
        ready(3 * side)
        for start in range(0, gate_w.shape[1], BLOCK):
            at = slice(start, start + BLOCK)
            d_hidden = plain(d_feed, down_w[:, at])
            dg_ref[:, at] = (d_hidden * slope_ref[:, at].astype(F32)).astype(BF)
            du_ref[:, at] = (d_hidden * silu_ref[:, at].astype(F32)).astype(BF)
        ready(3 * side + 1, 3 * side + 2)
        part = contract_last(dg_ref[...], gate_w[...]) + contract_last(du_ref[...], up_w[...])
        d_two_ref[...] = part if side == 0 else d_two_ref[...] + part


def attention_backward(d_attn_ref, out_w, qkv_w, cos_ref, sin_ref, q_ref, kz_ref, vz_ref, p_ref, do_ref, du_ref):
    seq_len, width = d_attn_ref.shape
    scale = 1.0 / math.sqrt(HEAD_DIM)
    do_ref[:, :width] = contract_last(d_attn_ref[...], out_w[...]).astype(BF)
    do_ref[:, width:] = jnp.zeros((seq_len, do_ref.shape[1] - width), BF)
    lower = lane_of(seq_len) < HEAD_DIM
    cosine, sine = cos_ref[...], sin_ref[...]

    def back(chunk):
        chunk = chunk * scale
        return chunk * cosine - swapped(chunk) * sine

    waiting, d_k, d_v = None, {}, {}
    sums = [[None, None], [None, None]]
    for at in range(CHUNKS):
        query, d_mixed = (ref[:, at * LANES : (at + 1) * LANES] for ref in (q_ref, do_ref))
        d_query = None
        for upper in range(2):
            head = 2 * at + upper
            if head >= HEADS:
                continue
            group = head // GROUPS
            key = 2 * group + upper
            attend = p_ref[head]
            d_attend = contract_last(d_mixed, vz_ref[key])
            soft = attend.astype(F32)
            weighted = soft * d_attend
            inner = jnp.sum(weighted, axis=-1, keepdims=True)
            d_scores = (weighted - soft * inner).astype(BF)
            part = plain(d_scores, kz_ref[key])
            d_query = part if d_query is None else d_query + part
            for which, term in ((0, contract_rows(d_scores, query)), (1, contract_rows(attend, d_mixed))):
                old = sums[which][upper]
                sums[which][upper] = term if old is None else old + term
            if head % GROUPS == GROUPS - 1:
                for which, store in ((0, d_k), (1, d_v)):
                    both = jnp.where(lower, sums[which][0], sums[which][1])
                    store[group] = both + other_half(both)
                sums = [[None, None], [None, None]]
        if at < CHUNKS - 1:
            du_ref[:, at * LANES : (at + 1) * LANES] = back(d_query).astype(BF)
        else:
            waiting = d_query
    tail = jnp.where(lower, waiting, d_k[0])
    du_ref[:, (CHUNKS - 1) * LANES : CHUNKS * LANES] = back(tail).astype(BF)
    for i in range(2):
        at = CHUNKS + i
        du_ref[:, at * LANES : (at + 1) * LANES] = back(jnp.where(lower, d_k[1 + 2 * i], d_k[2 + 2 * i])).astype(BF)
        at = CHUNKS + 2 + i
        du_ref[:, at * LANES : (at + 1) * LANES] = jnp.where(lower, d_v[2 * i], d_v[2 * i + 1]).astype(BF)
    at = CHUNKS + 4
    du_ref[:, at * LANES :] = d_v[4][:, : du_ref.shape[1] - at * LANES].astype(BF)


def router_gate(x, router_row):
    return jax.nn.sigmoid(jnp.sum(x * router_row, axis=-1, keepdims=True))


def masks(select_refs, segment_ref, pad_ref, bias_ref, active_ref):
    seq_len = segment_ref.shape[1]
    square = (seq_len, seq_len)
    query, key = (lax.broadcasted_iota(jnp.int32, square, axis) for axis in (0, 1))
    diagonal = query == key
    segment = segment_ref[...].astype(F32)
    own = jnp.sum(jnp.where(diagonal, segment, 0.0), axis=1, keepdims=True)
    near = (key <= query) & (segment == own)
    real = pad_ref[...] == 1
    for recursion, ref in enumerate(select_refs):
        place = lax.broadcasted_iota(jnp.int32, (seq_len, ref.shape[1]), 0)
        active = jnp.max(jnp.where(ref[...] == place, 1.0, 0.0), axis=1, keepdims=True)
        active_ref[recursion] = active
        along = jnp.sum(jnp.where(diagonal, active, 0.0), axis=0, keepdims=True)
        usable = (along > 0.0) & real
        bias_ref[recursion] = jnp.where(near & (usable | diagonal), 0.0, -1e30)


def first_attention(x_ref, sel_one, sel_two, sel_three, segment_ref, pad_ref, cos_ref, sin_ref, gain_one, gain_two, qkv_w, out_w,
                    n1_ref, q_ref, kz_ref, vz_ref, p_ref, o_ref, attn_ref, n2_ref, bias_ref, active_ref):
    n1, o = n1_ref.at[0], o_ref.at[0, 0]
    masks((sel_one, sel_two, sel_three), segment_ref, pad_ref, bias_ref, active_ref)
    attention_forward(x_ref, bias_ref.at[0], cos_ref, sin_ref, gain_one[...], qkv_w, n1, q_ref, kz_ref, vz_ref, p_ref, o)
    attention_out(x_ref, o, out_w, gain_two[...], attn_ref, n2_ref)


def load_all(pairs, sems):
    return [pltpu.make_async_copy(src, dst, sems.at[i]) for i, (src, dst) in enumerate(pairs)]


def waits_at(condition, copies):
    def ready(*which):
        @pl.when(condition)
        def _():
            for i in which:
                copies[i].wait()

    return ready


def finish_attention_backward(x_ref, gain, active_ref, du_ref, qkv_w, base, state, total, out_ref):
    total[...] = contract_last(du_ref[...], qkv_w[...])
    terms = jnp.zeros((1, state.shape[1]), F32)

    def lap(i, terms):
        rows = pl.ds(pl.multiple_of(i * ROWS, ROWS), ROWS)
        d_rows, term = norm_back(x_ref[rows, :], gain, total[rows, :])
        new = jnp.where(active_ref[rows, :] > 0, base[rows, :] + d_rows, state[rows, :])
        out_ref[rows, :] = new
        return terms + term

    return lax.fori_loop(0, state.shape[0] // ROWS, lap, terms)


def all_steps(bias_ref, active_ref, router_ref, cos_ref, sin_ref, gain_one, gain_two,
              hidden_hbm, d_hidden_hbm, attn0_hbm, n20_hbm, n1_in, o_da_in, qkv_hbm, out_hbm, *rest):
    feed_hbm, rest = rest[:6], rest[6:]
    (n1_out, o_da_out, n2_df_out, near_out, far_out, du_out, final_out, base_ref, state_ref, small_ref), rest = rest[:10], rest[10:]
    qkv_w, out_w, *feed_w = rest[:8]
    (xs, attns, fs, slope0, slope1, silu0, silu1, qs, kzs, vzs, ps, n1, o, n2, m0, m1, df, dg0, dg1, dw0, dw1, da, du,
     total, d_branch, do_ref, load_sems, out_sems) = rest[8:]
    width = state_ref.shape[1]
    laps = state_ref.shape[0] // ROWS
    loads = load_all(
        [*zip(feed_hbm, feed_w), (qkv_hbm, qkv_w), (out_hbm, out_w),
         (n20_hbm, n2), (attn0_hbm, attns.at[0]), (hidden_hbm, xs.at[0]), (d_hidden_hbm, state_ref)], load_sems)
    for i in (8, 0, 1, 2, 3, 4, 5, 9, 10, 6, 7, 11):
        loads[i].start()
    loads[8].wait()

    places = dict(n2=(n2, n2_df_out.at[0], 0), m0=(m0, near_out.at[0], 1), m1=(m1, far_out.at[0], 2), n1=(n1, n1_out, 3),
                  o=(o, o_da_out.at[0], 4), df=(df, n2_df_out.at[1], 5), dg0=(dg0, near_out.at[1], 6), dg1=(dg1, far_out.at[1], 7),
                  dw0=(dw0, near_out.at[2], 8), dw1=(dw1, far_out.at[2], 9), da=(da, o_da_out.at[1], 10), du=(du, du_out, 11))

    def leaving(name, recursion):
        source, target, sem = places[name]
        return pltpu.make_async_copy(source, target.at[recursion], out_sems.at[sem])

    def start(recursion, *names):
        for name in names:
            leaving(name, recursion).start()

    def wait(recursion, *names):
        for name in names:
            leaving(name, recursion).wait()

    def forward(r, carry):
        ready = waits_at(r == 0, loads)
        start(r, "n2")

        @pl.when(r > 0)
        def _():
            wait(r - 1, "m0", "m1")

        feed_forward(n2, ((*feed_w[:3], m0, slope0.at[r], silu0.at[r]), (*feed_w[3:], m1, slope1.at[r], silu1.at[r])), total, ready)
        start(r, "m0", "m1")
        ready(9, 10)
        router_row = router_ref[pl.ds(r, 1), :]

        def finish(rows):
            x = xs[r, rows, :]
            f = total[rows, :].astype(BF)
            fs[r, rows, :] = f
            branch = attns[r, rows, :] + f.astype(F32)
            xs[r + 1, rows, :] = jnp.where(active_ref[r, rows, :] > 0, x + router_gate(x, router_row) * branch, x)

        over_rows(total.shape[0], finish)
        ready(6, 7)
        wait(r, "n2")

        @pl.when(r < RECURSIONS - 1)
        def _():
            @pl.when(r > 0)
            def _():
                wait(r, "n1", "o")

            attention_forward(xs.at[r + 1], bias_ref.at[r + 1], cos_ref, sin_ref, gain_one[...], qkv_w,
                              n1, qs.at[r], kzs.at[r], vzs.at[r], ps.at[r], o)
            start(r + 1, "n1", "o")
            attention_out(xs.at[r + 1], o, out_w, gain_two[...], attns.at[r + 1], n2)

        return carry

    lax.fori_loop(0, RECURSIONS, forward, 0)
    final = pltpu.make_async_copy(xs.at[RECURSIONS], final_out, out_sems.at[12])
    final.start()
    loads[11].wait()
    small_ref[...] = jnp.zeros(small_ref.shape, F32)

    def backward(i, carry):
        r = RECURSIONS - 1 - i
        router_row = router_ref[pl.ds(r, 1), :]

        @pl.when(i > 0)
        def _():
            wait(r + 1, "df", "dg0", "dg1", "dw0", "dw1", "da")

        def enter(lap, terms):
            rows = pl.ds(pl.multiple_of(lap * ROWS, ROWS), ROWS)
            x = xs[r, rows, :]
            d_new = jnp.where(active_ref[r, rows, :] > 0, state_ref[rows, :], 0.0)
            gate = router_gate(x, router_row)
            branch = attns[r, rows, :] + fs[r, rows, :].astype(F32)
            d_gate = jnp.sum(d_new * branch, axis=-1, keepdims=True)
            d_logit = d_gate * gate * (1.0 - gate)
            spread = gate * d_new
            d_branch[rows, :] = spread
            df[rows, :] = spread.astype(BF)
            base_ref[rows, :] = d_new + d_logit * router_row
            return terms + jnp.sum(d_logit * x, axis=0, keepdims=True)

        small_ref[pl.ds(2 + r, 1), :] = lax.fori_loop(0, laps, enter, jnp.zeros((1, width), F32))
        start(r, "df")
        feed_backward(df, ((*feed_w[:3], slope0.at[r], silu0.at[r], dg0, dw0), (*feed_w[3:], slope1.at[r], silu1.at[r], dg1, dw1)),
                      total, lambda *which: None)
        start(r, "dg0", "dg1", "dw0", "dw1")

        def leave(lap, terms):
            rows = pl.ds(pl.multiple_of(lap * ROWS, ROWS), ROWS)
            after = xs[r, rows, :] + attns[r, rows, :]
            d_after, term = norm_back(after, gain_two[...], total[rows, :].astype(BF).astype(F32))
            da[rows, :] = (d_branch[rows, :] + d_after).astype(BF)
            base_ref[rows, :] = base_ref[rows, :] + d_after
            return terms + term

        small_ref[1:2, :] = small_ref[1:2, :] + lax.fori_loop(0, laps, leave, jnp.zeros((1, width), F32))
        start(r, "da")

        @pl.when(r > 0)
        def _():
            @pl.when(i > 0)
            def _():
                wait(r + 1, "du")

            attention_backward(da, out_w, qkv_w, cos_ref, sin_ref, qs.at[r - 1], kzs.at[r - 1], vzs.at[r - 1], ps.at[r - 1], do_ref, du)
            start(r, "du")
            term = finish_attention_backward(xs.at[r], gain_one[...], active_ref.at[r], du, qkv_w, base_ref, state_ref, total, state_ref)
            small_ref[0:1, :] = small_ref[0:1, :] + term

        return carry

    lax.fori_loop(0, RECURSIONS, backward, 0)
    wait(RECURSIONS - 1, "m0", "m1", "n1", "o")
    wait(0, "df", "dg0", "dg1", "dw0", "dw1", "da")
    wait(1, "du")
    final.wait()


def last_attention(active_ref, cos_ref, sin_ref, gain_one, q_ref, kz_ref, vz_ref, p_ref, d_attn_ref, small_in, out_w,
                   x_hbm, base_hbm, state_hbm, qkv_hbm, du_in, token, du_ref, d_input_ref, small_ref,
                   do_ref, total, x, base, state, qkv_w, sems):
    copies = load_all([(qkv_hbm, qkv_w), (x_hbm, x), (base_hbm, base), (state_hbm, state)], sems)
    for copy in copies:
        copy.start()
    attention_backward(d_attn_ref.at[0, 0], out_w, qkv_w, cos_ref, sin_ref, q_ref, kz_ref, vz_ref, p_ref, do_ref, du_ref.at[0])
    for copy in copies:
        copy.wait()
    term = finish_attention_backward(x, gain_one[...], active_ref.at[0], du_ref.at[0], qkv_w, base, state, total, d_input_ref)
    small_ref[...] = small_in[...]
    small_ref[0:1, :] = small_in[0:1, :] + term


def swap_dp(values_in, bit, n_dp):
    return lax.ppermute(values_in, "dp", [(i, i ^ (1 << bit)) for i in range(n_dp)])


def swap_mp(values_in):
    return lax.ppermute(values_in, "mp", [(0, 1), (1, 0)])


def halving(parts, order, n_dp, index):
    bits = n_dp.bit_length() - 1
    left = list(range(bits - 1, -1, -1))
    shape = parts.shape[1:]
    held = parts.reshape((2,) * bits + shape)
    for step, bit in enumerate(order):
        at = left.index(bit)
        upper = ((index >> bit) & 1) == 1
        low = lax.index_in_dim(held, 0, at, keepdims=False)
        high = lax.index_in_dim(held, 1, at, keepdims=False)
        keep, send = jnp.where(upper, high, low), jnp.where(upper, low, high)
        got = swap_dp(send, bit, n_dp)
        last = step == bits - 1
        total = keep.astype(F32) + got.astype(F32)
        held = total if last else total.astype(BF)
        left.remove(bit)
    return held


def orders_of(bits):
    rest = list(range(3, bits))
    if bits < 3:
        return [list(range(bits))] * 3
    return [[0, 1, 2] + rest, [1, 0, 2] + rest, [2, 0, 1] + rest]


PART = 2 * LANES
FFN_TILES = (4, 4, 2)
FFN_ORDERS = ((2, 1, 3, 0), (1, 0, 2, 3), (2, 0, 3, 1))
ATTN_ORDER = (0, 1, 2, 3)
SCHEDULE = (
    "T0", "T1", "A", "T2",
    "F0", "F1", "A0", "F2",
    "F0", "F1", "A0", "F2",
    "F0", "F1", "A0", "F2",
)
SMALL = 48


def halves(bit, outs, index):
    mine = (index >> bit) & 1
    inner = 1 << bit
    for out, which in zip(outs, (mine, 1 - mine)):
        for p in range(out.shape[0]):
            for q in range(inner):
                yield out, p, q, p * 2 * inner + which * inner + q


def stacked_copies(pairs, sems):
    flat_pairs = []
    for sources, target in pairs:
        rows = target.shape[0] // 2
        flat_pairs += [(source, target.at[pl.ds(i * rows, rows)]) for i, source in enumerate(sources)]
    copies = load_all(flat_pairs, sems)
    for copy in copies:
        copy.start()
    return [copies[i : i + 2] for i in range(0, len(copies), 2)]


def ffn_terms(bit, tiles, at, n2_df_a, n2_df_b, units_a, units_b, token, keep_ref, send_ref, left, right, flat, sems):
    width = left.shape[2]
    columns = pl.ds(at, tiles * LANES)
    lefts = [(n2_df_a.at[i], n2_df_b.at[i]) for i in range(2)]
    m, dg, dw = [(units_a.at[i, :, columns], units_b.at[i, :, columns]) for i in range(3)]
    n2, dg, dw, df, m = stacked_copies(
        [(lefts[0], left.at[0]), (dg, right.at[0]), (dw, right.at[1]), (lefts[1], left.at[1]), (m, right.at[2])], sems)
    for matrix, needed in enumerate((n2 + dg, dw, df + m)):
        for copy in needed:
            copy.wait()
        terms = contract_rows(left[matrix // 2], right[matrix])
        for c in range(tiles):
            flat[pl.ds(tiles * width * matrix + c, width, stride=tiles), :] = terms[:, c * LANES : (c + 1) * LANES]
    rows = keep_ref.shape[2]
    for out, p, q, shard in halves(bit, (keep_ref, send_ref), lax.axis_index("dp")):
        out[p, q] = flat[pl.ds(pl.multiple_of(shard * rows, 8), rows), :].astype(BF)


def small_rows(small, packed):
    packed[...] = jnp.zeros(packed.shape, F32)
    width = small.shape[1]
    for i in range(2 + RECURSIONS):
        for c in range(CHUNKS):
            stop = min(width, (c + 1) * LANES)
            packed[i * CHUNKS + c : i * CHUNKS + c + 1, : stop - c * LANES] = small[i : i + 1, c * LANES : stop]
    return packed[...]


def split_small(small, ref, start):
    high = small.astype(BF)
    ref[start : start + SMALL, :] = high
    ref[start + SMALL : start + 2 * SMALL, :] = (small - high.astype(F32)).astype(BF)


def rounded_small(small):
    high = small.astype(BF)
    return high.astype(F32) + (small - high.astype(F32)).astype(BF).astype(F32)


def joined_small(ref, start):
    return ref[start : start + SMALL, :].astype(F32) + ref[start + SMALL : start + 2 * SMALL, :].astype(F32)


def attn_terms(bit, depth, n1_a, n1_b, du_a, du_b, o_da_a, o_da_b, small_a, small_b, token,
               keep, send, small_out, left, du_rows, da_rows, terms, flat, packed, sems):
    width = left.shape[2]
    base = 0
    lower = lane_of(width // 2) < HEAD_DIM
    n1, du, o, da = stacked_copies(
        [((n1_a, n1_b), left.at[0]), ((du_a, du_b), du_rows), ((o_da_a.at[0], o_da_b.at[0]), left.at[1]),
         ((o_da_a.at[1], o_da_b.at[1]), da_rows)], sems)
    for which, (right, needed) in enumerate(((du_rows, n1 + du), (da_rows, o + da))):
        for copy in needed:
            copy.wait()
        columns = right.shape[1]
        half = columns // LANES
        for start in range(0, columns, PART):
            stop = min(columns, start + PART)
            block = contract_rows(left[which], right[:, start:stop])
            if stop - start < PART:
                block = jnp.concatenate([block, jnp.zeros((width, PART - (stop - start)), F32)], axis=1)
            for part in range(0, stop - start, LANES):
                terms[(start + part) // LANES] = block[:, part : part + LANES]
        step = 2 * columns // LANES
        count = width // 2
        after = first_odd = None
        for c in range(half + 1):
            even = terms[c, pl.ds(0, count, stride=2), :]
            odd = other_half(terms[c, pl.ds(1, count, stride=2), :])
            if c < half:
                flat[pl.ds(base + c, count, stride=step), :] = even
            else:
                flat[pl.ds(base + c, count, stride=step), :] = jnp.where(lower, even, first_odd)
            if c == 0:
                first_odd = odd
            else:
                flat[pl.ds(base + half + c, count, stride=step), :] = jnp.where(lower, after, odd)
            after = odd
        base += width * columns // LANES
    index, core = lax.axis_index("dp"), lax.axis_index("mp")
    total = rounded_small(small_rows(small_a, packed.at[0])) + rounded_small(small_rows(small_b, packed.at[1]))
    small_out[...] = total
    outer, inner, rows = keep.shape[:3]
    split_small(total, send, outer * inner * rows)

    def rows_of_shard(shard):
        start = pl.multiple_of((2 * shard + core) * depth, 8)
        return flat[pl.ds(start, rows), :].astype(BF)

    mine = (index >> bit) & 1
    for p in range(outer):
        for q in range(inner):
            shard = 2 * p * inner + q
            keep[p, q] = rows_of_shard(shard + mine * inner)
            at = (p * inner + q) * rows
            send[at : at + rows, :] = rows_of_shard(shard + (1 - mine) * inner)


def fold(bit, kept, got, token, keep, send):
    mine = (lax.axis_index("dp") >> bit) & 1
    for p in range(kept.shape[0]):
        for q in range(kept.shape[2]):
            for out, which in ((keep, mine), (send, 1 - mine)):
                out[p, q] = (kept[p, which, q].astype(F32) + got[p, which, q].astype(F32)).astype(BF)


def fold_small(bit, kept, got, small, token, keep, send, small_out):
    mine = (lax.axis_index("dp") >> bit) & 1
    outer, _, inner, rows, _ = kept.shape
    for p in range(outer):
        for q in range(inner):
            totals = []
            for which in (mine, 1 - mine):
                start = pl.multiple_of(((2 * p + which) * inner + q) * rows, 16)
                totals.append((kept[p, which, q].astype(F32) + got[pl.ds(start, rows), :].astype(F32)).astype(BF))
            keep[p, q] = totals[0]
            at = (p * inner + q) * rows
            send[at : at + rows, :] = totals[1]
    total = rounded_small(small[...]) + joined_small(got, 2 * outer * inner * rows)
    small_out[...] = total
    split_small(total, send, outer * inner * rows)


def finish_streams(tiles, *refs):
    count = len(tiles)
    feeds, refs = refs[: 2 * count], refs[2 * count :]
    attn, refs = refs[:2], refs[2:]
    small, ffn_out, attn_out, one_out, two_out, router_out, flat, packed = refs
    every = sum(tiles)
    rows = ffn_out.shape[0] // every
    base = 0
    for i, wide in enumerate(tiles):
        flat[: rows * wide, :] = feeds[2 * i][...].astype(F32) + feeds[2 * i + 1][...].astype(F32)
        for c in range(wide):
            ffn_out[pl.ds(base + c, rows, stride=every), :] = flat[pl.ds(c, rows, stride=wide), :]
        base += wide
    padded = attn[0].shape[0]
    both = attn[0][...].astype(F32) + attn[1][:padded, :].astype(F32)
    attn_out[...] = both[: attn_out.shape[0]]
    total = rounded_small(small[...]) + joined_small(attn[1], padded)
    packed[...] = total
    width = one_out.shape[1]
    outs = [(one_out, 0), (two_out, 0), *[(router_out, i) for i in range(RECURSIONS)]]
    for i, (out, row) in enumerate(outs):
        for c in range(CHUNKS):
            stop = min(width, (c + 1) * LANES)
            out[row : row + 1, c * LANES : stop] = packed[i * CHUNKS + c : i * CHUNKS + c + 1, : stop - c * LANES]


class Stream:
    def __init__(self, order, bits):
        self.order, self.left, self.done = order, list(range(bits - 1, -1, -1)), 0
        self.kept = self.got = None

    def shape_for(self, array):
        at = self.left.index(self.order[self.done])
        rows, lanes = array.shape[-2:]
        return (1 << at, 2, 1 << (len(self.left) - 1 - at), rows, lanes)

    def sent(self, kept, send, n_dp):
        bit = self.order[self.done]
        self.kept, self.got = kept, swap_dp(send, bit, n_dp)
        self.left.remove(bit)
        self.done += 1


def on_device(
    hidden_in,
    sel_one,
    sel_two,
    sel_three,
    segment_ids,
    pad_mask,
    qkv_weight,
    out_weight,
    gate_weight,
    up_weight,
    down_weight,
    norm_one,
    norm_two,
    router_weight,
    d_hidden,
):
    seq_len, width = hidden_in.shape
    n_dp, n_mp = lax.axis_size("dp"), lax.axis_size("mp")
    dp_index, mp_index = lax.axis_index("dp"), lax.axis_index("mp")
    cosine, sine = rotary_tables(seq_len)
    weights = [(gate_weight, up_weight, down_weight)]
    weights.append(tuple(swap_mp(w) for w in weights[0]))
    gain_one, gain_two = norm_one.reshape(1, width), norm_two.reshape(1, width)
    padded = CHUNKS * LANES
    units = gate_weight.shape[1]
    feed_weights = (*weights[0], *weights[1])

    def shape(*dims, dtype=BF):
        return jax.ShapeDtypeStruct(dims, dtype)

    def whole(*dims, **kw):
        return pl.BlockSpec(dims, lambda *_: (0,) * len(dims), **kw)

    anywhere = pl.BlockSpec(memory_space=pl.ANY)
    one = pl.Buffered(1)
    stack = RECURSIONS, seq_len
    heads = (2 * KV_HEADS, seq_len, LANES)
    square = (HEADS, seq_len, seq_len)
    n1, q, kz, vz, p, o_da, attn, n2, bias, active = pl.pallas_call(
        first_attention,
        grid=(1,),
        in_specs=[
            whole(seq_len, width), *[whole(*ref.shape) for ref in (sel_one, sel_two, sel_three, segment_ids, pad_mask)],
            whole(seq_len, LANES), whole(seq_len, LANES), whole(1, width), whole(1, width), whole(*qkv_weight.shape), whole(*out_weight.shape),
        ],
        out_specs=[
            whole(1, seq_len, width), whole(seq_len, padded), whole(*heads), whole(*heads), whole(*square),
            whole(1, 1, seq_len, width), whole(seq_len, width), whole(seq_len, width), whole(RECURSIONS, seq_len, seq_len), whole(*stack, 1),
        ],
        out_shape=[
            shape(*stack, width), shape(seq_len, padded), shape(*heads), shape(*heads), shape(*square),
            shape(2, *stack, width), shape(seq_len, width, dtype=F32), shape(seq_len, width),
            shape(*stack, seq_len, dtype=F32), shape(*stack, 1, dtype=F32),
        ],
        compiler_params=pltpu.CompilerParams(vmem_limit_bytes=VMEM_MIB * MIB),
        cost_estimate=pl.CostEstimate(flops=2 * 10**9, bytes_accessed=12 * 10**6, transcendentals=600000),
        name="first_attention",
    )(hidden_in, sel_one, sel_two, sel_three, segment_ids, pad_mask, cosine, sine, gain_one, gain_two, qkv_weight, out_weight)
    attention_0 = (q, kz, vz, p)
    wide = qkv_weight.shape[1]
    row = (seq_len, width)
    kept = RECURSIONS - 1
    vm = pltpu.VMEM
    results = pl.pallas_call(
        all_steps,
        grid=(1,),
        in_specs=[
            whole(RECURSIONS, seq_len, seq_len), whole(RECURSIONS, seq_len, 1), whole(RECURSIONS, width),
            whole(seq_len, LANES), whole(seq_len, LANES), whole(1, width), whole(1, width), *[anywhere] * 14,
        ],
        out_specs=[*[anywhere] * 7, whole(*row), whole(*row), whole(8, width)],
        out_shape=[
            shape(*stack, width), *[shape(2, *stack, width)] * 2, *[shape(3, *stack, units)] * 2, shape(*stack, wide),
            *[shape(*row, dtype=F32)] * 3, shape(8, width, dtype=F32),
        ],
        scratch_shapes=[
            *[vm(w.shape, BF) for w in (qkv_weight, out_weight, *feed_weights)],
            vm((RECURSIONS + 1, *row), F32), vm((RECURSIONS, *row), F32), vm((RECURSIONS, *row), BF),
            *[vm((*stack, units), BF)] * 4, vm((kept, seq_len, padded), BF), vm((kept, *heads), BF), vm((kept, *heads), BF),
            vm((kept, *square), BF), *[vm(row, BF)] * 3, *[vm((seq_len, units), BF)] * 2, vm(row, BF), *[vm((seq_len, units), BF)] * 4,
            vm(row, BF), vm((seq_len, wide), BF), vm(row, F32), vm(row, F32), vm((seq_len, padded), BF),
            pltpu.SemaphoreType.DMA((12,)), pltpu.SemaphoreType.DMA((13,)),
        ],
        input_output_aliases={11: 0, 12: 1},
        compiler_params=pltpu.CompilerParams(vmem_limit_bytes=VMEM_MIB * MIB),
        cost_estimate=pl.CostEstimate(flops=23 * 10**9, bytes_accessed=50 * 10**6, transcendentals=4 * 10**6),
        name="all_steps",
    )(bias, active, router_weight, cosine, sine, gain_one, gain_two, hidden_in, d_hidden, attn, n2, n1, o_da,
      qkv_weight, out_weight, *feed_weights)
    n1, o_da, n2_df, near, far, du, state, base, grad_state, small = results

    def run_last(token):
        return pl.pallas_call(
            last_attention,
            grid=(1,),
            in_specs=[
                whole(1, seq_len, 1), whole(seq_len, LANES), whole(seq_len, LANES), whole(1, width),
                whole(seq_len, padded), whole(*heads), whole(*heads), whole(*square),
                pl.BlockSpec((1, 1, seq_len, width), lambda i: (1, 0, 0, 0)), whole(8, width), whole(*out_weight.shape), *[anywhere] * 6,
            ],
            out_specs=[whole(1, seq_len, qkv_weight.shape[1]), whole(seq_len, width), whole(8, width)],
            out_shape=[shape(*stack, qkv_weight.shape[1]), shape(seq_len, width, dtype=F32), shape(8, width, dtype=F32)],
            scratch_shapes=[
                pltpu.VMEM((seq_len, padded), BF), *[pltpu.VMEM((seq_len, width), F32)] * 4,
                pltpu.VMEM(qkv_weight.shape, BF), pltpu.SemaphoreType.DMA((4,)),
            ],
            input_output_aliases={15: 0},
            compiler_params=pltpu.CompilerParams(vmem_limit_bytes=VMEM_MIB * MIB),
            cost_estimate=pl.CostEstimate(flops=1, bytes_accessed=1, transcendentals=0),
            name="last_attention",
        )(active, cosine, sine, gain_one, *attention_0, o_da, small, out_weight, hidden_in, base, grad_state, qkv_weight, du, token)

    def rows_of(stacked):
        return stacked.reshape(*stacked.shape[:-3], -1, stacked.shape[-1])

    bits = n_dp.bit_length() - 1
    share = (qkv_weight.size + out_weight.size) // (n_dp * n_mp)
    if bits == 4 and 3 * width % n_dp == 0 and units == sum(FFN_TILES) * LANES and share % (8 * LANES) == 0:
        factors = [rows_of(t) for t in (n2_df, swap_mp(n2_df), near, swap_mp(far))]
        streams = [Stream(order, bits) for order in FFN_ORDERS]
        attn_stream = Stream(ATTN_ORDER, bits)
        depth = share // LANES
        tiled = -(-depth // 16) * 16
        common = dict(
            grid=(1,),
            compiler_params=pltpu.CompilerParams(vmem_limit_bytes=VMEM_MIB * MIB),
            cost_estimate=pl.CostEstimate(flops=1, bytes_accessed=1, transcendentals=0),
        )

        def wholes(arrays):
            return [whole(*t.shape) for t in arrays]

        def terms_of(j, token):
            stream, tiles = streams[j], FFN_TILES[j]
            at = sum(FFN_TILES[:j]) * LANES
            bit = stream.order[0]
            dims = (1 << (bits - 1 - bit), 1 << bit, 3 * width // n_dp * tiles, LANES)
            both = 2 * RECURSIONS * seq_len
            keep, send = pl.pallas_call(
                functools.partial(ffn_terms, bit, tiles, at),
                in_specs=[anywhere] * (len(factors) + 1),
                out_specs=[whole(*dims)] * 2,
                out_shape=[shape(*dims)] * 2,
                scratch_shapes=[pltpu.VMEM((2, both, width), BF), pltpu.VMEM((3, both, tiles * LANES), BF),
                                pltpu.VMEM((3 * width * tiles, LANES), F32), pltpu.SemaphoreType.DMA((10,))],
                name=f"ffn_terms_{j}",
                **common,
            )(*factors, token)
            stream.sent(keep, send, n_dp)
            return keep

        def fold_stream(stream, token, small_own=None):
            bit = stream.order[stream.done]
            dims = stream.shape_for(stream.kept)
            kept = stream.kept.reshape(dims)
            held = (dims[0], *dims[2:])
            if small_own is None:
                operands = (kept, stream.got.reshape(dims))
                outs = (shape(*held), shape(*held))
            else:
                operands = (kept, stream.got, small_own)
                outs = (shape(*held), shape(dims[0] * dims[2] * dims[3] + 2 * SMALL, LANES), shape(SMALL, LANES, dtype=F32))
            results = pl.pallas_call(
                functools.partial(fold if small_own is None else fold_small, bit),
                in_specs=[*wholes(operands), anywhere],
                out_specs=wholes(outs),
                out_shape=outs,
                name="fold_terms",
                **common,
            )(*operands, token)
            stream.sent(results[0], results[1], n_dp)
            return results

        du, grad_state, small = run_last(small)
        n1, o_da, small = lax.optimization_barrier((n1, o_da, small))
        operands = [t for mine in (rows_of(n1), rows_of(du), rows_of(o_da), small) for t in (mine, swap_mp(mine))]
        token = small
        for item in SCHEDULE:
            if item[0] == "T":
                token = terms_of(int(item[1:]), token)
            elif item[0] == "F":
                token = fold_stream(streams[int(item[1:])], token)[0]
            elif item == "A":
                bit = attn_stream.order[0]
                dims = (1 << (bits - 1 - bit), 1 << bit, tiled, LANES)
                outs = (shape(*dims), shape(n_dp // 2 * tiled + 2 * SMALL, LANES), shape(SMALL, LANES, dtype=F32))
                keep, send, small_own = pl.pallas_call(
                    functools.partial(attn_terms, bit, depth),
                    in_specs=[*[anywhere] * 6, *wholes(operands[6:]), anywhere],
                    out_specs=wholes(outs),
                    out_shape=outs,
                    scratch_shapes=[pltpu.VMEM((2, 2 * RECURSIONS * seq_len, width), BF),
                                    *[pltpu.VMEM((2 * RECURSIONS * seq_len, t.shape[-1]), BF) for t in (du, o_da)],
                                    pltpu.VMEM((-(-du.shape[-1] // PART) * 2, width, LANES), F32),
                                    pltpu.VMEM((n_dp * 2 * depth + tiled - depth, LANES), F32), pltpu.VMEM((2, SMALL, LANES), F32),
                                    pltpu.SemaphoreType.DMA((8,))],
                    name="attn_terms",
                    **common,
                )(*operands, token)
                attn_stream.sent(keep, send, n_dp)
                token = small_own
            else:
                token, _, small_own = fold_stream(attn_stream, token, small_own)
        ends = [t.reshape(t.shape[-2:]) for stream in (*streams, attn_stream) for t in (stream.kept, stream.got)]
        outs = (shape(3 * width // n_dp * sum(FFN_TILES), LANES, dtype=F32), shape(depth, LANES, dtype=F32),
                shape(1, width, dtype=F32), shape(1, width, dtype=F32), shape(RECURSIONS, width, dtype=F32))
        ffn_flat, attn_flat, one, two, router = pl.pallas_call(
            functools.partial(finish_streams, FFN_TILES),
            in_specs=wholes((*ends, small_own)),
            out_specs=wholes(outs),
            out_shape=outs,
            scratch_shapes=[pltpu.VMEM((3 * width // n_dp * max(FFN_TILES), LANES), F32), pltpu.VMEM((SMALL, LANES), F32)],
            name="finish_streams",
            **common,
        )(*ends, small_own)
        return (state, grad_state, attn_flat.reshape(-1), ffn_flat.reshape(1, -1), one.reshape(-1), two.reshape(-1), router)

    du, grad_state, small = run_last(small)
    two, feed = rows_of(n2_df)
    o, d_attn = rows_of(o_da)
    sides = [[t[i] for i in (1, 2, 0)] for t in (rows_of(near), rows_of(far))]

    def side_terms(side, columns):
        return jnp.concatenate(
            [
                contract_rows(left, sides[side][which][:, columns]).astype(BF)
                for which, left in enumerate((two, two, feed))
            ],
            axis=0,
        )

    orders = orders_of(bits)
    if 3 * width % n_dp == 0 and units % 1280 == 0:
        fifth = units // 5
        streams = [(orders[i], slice(j * fifth, (j + 1) * fifth)) for i, j in ((0, 0), (1, 1), (2, 2), (0, 3), (1, 4))]
        done = []
        for order, columns in streams:
            terms = side_terms(0, columns).astype(F32) + swap_mp(side_terms(1, columns)).astype(F32)
            done.append(halving(terms.astype(BF).reshape(n_dp, 3 * width // n_dp, fifth), order, n_dp, dp_index))
        ffn_flat = jnp.concatenate(done, axis=1).reshape(1, -1)
    else:
        terms = side_terms(0, slice(None)).astype(F32) + swap_mp(side_terms(1, slice(None))).astype(F32)
        terms = terms.astype(BF).reshape(n_dp, 3 * width * units // n_dp // 128, 128)
        ffn_flat = halving(terms, orders[0], n_dp, dp_index).reshape(1, -1)

    grad_qkv = contract_rows(rows_of(n1), rows_of(du)).astype(BF)
    grad_out = contract_rows(o, d_attn).astype(BF)
    attn = jnp.concatenate([grad_qkv.reshape(-1), grad_out.reshape(-1)]).reshape(n_dp, 2, share // 128, 128)
    keep = jnp.where(mp_index == 0, attn[:, 0], attn[:, 1])
    send = jnp.where(mp_index == 0, attn[:, 1], attn[:, 0])
    attn = (keep.astype(F32) + swap_mp(send).astype(F32)).astype(BF)
    cuts = [0, (share // 128) // 24 * 8, (share // 128) // 12 * 8, share // 128]
    attn_flat = jnp.concatenate(
        [halving(attn[:, a:b], order, n_dp, dp_index) for a, b, order in zip(cuts, cuts[1:], orders)], axis=0
    ).reshape(-1)

    small = small + swap_mp(small)
    for bit in range(bits):
        small = small + swap_dp(small, bit, n_dp)
    return (state, grad_state, attn_flat, ffn_flat, small[0], small[1], small[2 : 2 + RECURSIONS])


def solution(mesh):
    both = P(("dp", "mp"), None)
    in_specs = (
        both,
        both,
        both,
        both,
        both,
        both,
        P(),
        P(),
        P(None, "mp"),
        P(None, "mp"),
        P(None, "mp"),
        P(),
        P(),
        P(),
        both,
    )
    out_specs = (both, both, P(("dp", "mp")), P("mp", "dp"), P(), P(), P())
    return jax.shard_map(
        on_device, mesh=mesh, in_specs=in_specs, out_specs=out_specs, check_vma=False
    )
```

```python
import functools
import math

import jax
import jax.numpy as jnp
import numpy as np
from jax import lax
from jax.experimental import pallas as pl
from jax.experimental.pallas import tpu as pltpu
from jax.sharding import PartitionSpec as P

HEADS = 15
KV_HEADS = 5
HEAD_DIM = 64
RECURSIONS = 3
GROUPS = HEADS // KV_HEADS
EPS = 1e-05
BF = jnp.bfloat16
F32 = jnp.float32


LANES = 128
CHUNKS = -(-HEADS * HEAD_DIM // LANES)
ROWS = 192
BLOCK = 256
MIB = 1 << 20
VMEM_MIB = 63


def rotary_tables(seq_len):
    half = HEAD_DIM // 2
    frequency = np.float32(100000.0) ** (
        np.float32(-2.0) * np.arange(half, dtype=np.float32) / np.float32(HEAD_DIM)
    )
    angles = np.arange(seq_len, dtype=np.float32)[:, None] * frequency.astype(np.float32)
    cosine, sine = np.cos(angles), np.sin(angles)
    return (
        jnp.asarray(np.concatenate([cosine] * 4, axis=1), F32),
        jnp.asarray(np.concatenate([-sine, sine] * 2, axis=1), F32),
    )


def contract_rows(left, right):
    return lax.dot_general(left, right, (((0,), (0,)), ((), ())), preferred_element_type=F32)


def contract_last(left, right):
    return lax.dot_general(left, right, (((1,), (1,)), ((), ())), preferred_element_type=F32)


def plain(left, right):
    return jnp.dot(left, right, preferred_element_type=F32)


def inverse_rms(rows):
    return lax.rsqrt(jnp.mean(rows * rows, axis=-1, keepdims=True) + EPS)


def norm_back(rows, gain, d_out):
    inv = inverse_rms(rows)
    scaled = d_out * gain
    inner = jnp.mean(scaled * rows, axis=-1, keepdims=True)
    d_rows = inv * scaled - rows * (inv * inv * inv * inner)
    return d_rows, jnp.sum(d_out * rows * inv, axis=0, keepdims=True)


def lane_of(rows):
    return lax.broadcasted_iota(jnp.int32, (rows, LANES), 1)


def swapped(chunk):
    first = lane_of(chunk.shape[0]) % HEAD_DIM < HEAD_DIM // 2
    return jnp.where(first, pltpu.roll(chunk, LANES - 32, 1), pltpu.roll(chunk, 32, 1))


def other_half(chunk):
    return pltpu.roll(chunk, HEAD_DIM, 1)


def over_rows(count, body):
    def lap(i, carry):
        body(pl.ds(pl.multiple_of(i * ROWS, ROWS), ROWS))
        return carry

    lax.fori_loop(0, count // ROWS, lap, 0)


def attention_forward(x_ref, bias_ref, cos_ref, sin_ref, gain, qkv_w, n1_ref, q_ref, kz_ref, vz_ref, p_ref, o_ref):
    seq_len, width = x_ref.shape
    scale = 1.0 / math.sqrt(HEAD_DIM)

    def norm(rows):
        x = x_ref[rows, :]
        n1_ref[rows, :] = (x * inverse_rms(x) * gain).astype(BF)

    over_rows(seq_len, norm)
    lower = lane_of(seq_len) < HEAD_DIM
    n1 = n1_ref[...]

    def spread(ref, head, chunk, upper):
        flipped = other_half(chunk)
        here, there = (flipped, chunk) if upper else (chunk, flipped)
        ref[2 * head] = jnp.where(lower, here, 0.0).astype(BF)
        ref[2 * head + 1] = jnp.where(lower, 0.0, there).astype(BF)

    columns = qkv_w.shape[1]
    for start in range(0, columns, 2 * LANES):
        wide = plain(n1, qkv_w[:, start : min(start + 2 * LANES, columns)])
        for part in range(0, wide.shape[1], LANES):
            chunk = wide[:, part : part + LANES]
            if chunk.shape[1] < LANES:
                chunk = jnp.concatenate([chunk, jnp.zeros_like(chunk)], axis=1)
            at = (start + part) // LANES
            heads = (2 * at, 2 * at + 1)
            if heads[0] < HEADS + KV_HEADS:
                chunk = chunk * cos_ref[...] + swapped(chunk) * sin_ref[...]
                if heads[0] < HEADS:
                    q_ref[:, at * LANES : (at + 1) * LANES] = chunk.astype(BF)
            for upper, head in enumerate(heads):
                if HEADS <= head < HEADS + KV_HEADS:
                    spread(kz_ref, head - HEADS, chunk, upper)
                elif HEADS + KV_HEADS <= head < HEADS + 2 * KV_HEADS:
                    spread(vz_ref, head - HEADS - KV_HEADS, chunk, upper)

    for at in range(CHUNKS):
        query = q_ref[:, at * LANES : (at + 1) * LANES]
        total = None
        for upper in range(2):
            head = 2 * at + upper
            if head < HEADS:
                key = 2 * (head // GROUPS) + upper
                scores = contract_last(query, kz_ref[key]) * scale + bias_ref[...]
                top = jnp.max(scores, axis=-1, keepdims=True)
                exponent = jnp.exp(scores - top)
                share = pl.reciprocal(jnp.sum(exponent, axis=-1, keepdims=True))
                attend = (exponent * share).astype(BF)
                p_ref[head] = attend
                mixed = plain(attend, vz_ref[key])
                total = mixed if total is None else total + mixed
        stop = min(width, (at + 1) * LANES)
        o_ref[:, at * LANES : stop] = total[:, : stop - at * LANES].astype(BF)


def attention_out(x_ref, o_ref, out_w, gain, attn_ref, n2_ref):
    attn_ref[...] = plain(o_ref[...], out_w[...])

    def norm(rows):
        after = x_ref[rows, :] + attn_ref[rows, :]
        n2_ref[rows, :] = (after * inverse_rms(after) * gain).astype(BF)

    over_rows(x_ref.shape[0], norm)


def feed_forward(n2_ref, sides, f_ref, ready):
    n2 = n2_ref[...]
    for side, (gate_w, up_w, down_w, m_ref, slope_ref, silu_ref) in enumerate(sides):
        ready(3 * side, 3 * side + 1)
        for start in range(0, gate_w.shape[1], BLOCK):
            at = slice(start, start + BLOCK)
            g, u = plain(n2, gate_w[:, at]), plain(n2, up_w[:, at])
            s = jax.nn.sigmoid(g)
            silu = g * s
            m_ref[:, at] = (silu * u).astype(BF)
            slope_ref[:, at] = (u * s * (1.0 + g * (1.0 - s))).astype(BF)
            silu_ref[:, at] = silu.astype(BF)
        ready(3 * side + 2)
        part = contract_last(m_ref[...], down_w[...])
        f_ref[...] = part if side == 0 else f_ref[...] + part


def feed_backward(df_ref, sides, d_two_ref, ready):
    d_feed = df_ref[...]
    for side, (gate_w, up_w, down_w, slope_ref, silu_ref, dg_ref, du_ref) in enumerate(sides):
        ready(3 * side)
        for start in range(0, gate_w.shape[1], BLOCK):
            at = slice(start, start + BLOCK)
            d_hidden = plain(d_feed, down_w[:, at])
            dg_ref[:, at] = (d_hidden * slope_ref[:, at].astype(F32)).astype(BF)
            du_ref[:, at] = (d_hidden * silu_ref[:, at].astype(F32)).astype(BF)
        ready(3 * side + 1, 3 * side + 2)
        part = contract_last(dg_ref[...], gate_w[...]) + contract_last(du_ref[...], up_w[...])
        d_two_ref[...] = part if side == 0 else d_two_ref[...] + part


def attention_backward(d_attn_ref, out_w, qkv_w, cos_ref, sin_ref, q_ref, kz_ref, vz_ref, p_ref, do_ref, du_ref):
    seq_len, width = d_attn_ref.shape
    scale = 1.0 / math.sqrt(HEAD_DIM)
    do_ref[:, :width] = contract_last(d_attn_ref[...], out_w[...]).astype(BF)
    do_ref[:, width:] = jnp.zeros((seq_len, do_ref.shape[1] - width), BF)
    lower = lane_of(seq_len) < HEAD_DIM
    cosine, sine = cos_ref[...], sin_ref[...]

    def back(chunk):
        chunk = chunk * scale
        return chunk * cosine - swapped(chunk) * sine

    waiting, d_k, d_v = None, {}, {}
    for at in range(CHUNKS):
        query, d_mixed = (ref[:, at * LANES : (at + 1) * LANES] for ref in (q_ref, do_ref))
        query_t, d_mixed_t = query.T, d_mixed.T
        d_query = None
        for upper in range(2):
            head = 2 * at + upper
            if head >= HEADS:
                continue
            group = head // GROUPS
            key = 2 * group + upper
            rows = slice(upper * HEAD_DIM, (upper + 1) * HEAD_DIM)
            attend = p_ref[head]
            d_attend = contract_last(d_mixed, vz_ref[key])
            soft = attend.astype(F32)
            weighted = soft * d_attend
            inner = jnp.sum(weighted, axis=-1, keepdims=True)
            d_scores = (weighted - soft * inner).astype(BF)
            part = plain(d_scores, kz_ref[key])
            d_query = part if d_query is None else d_query + part
            for store, term in ((d_k, plain(query_t[rows], d_scores)), (d_v, plain(d_mixed_t[rows], attend))):
                store[group] = term if group not in store else store[group] + term
        if at < CHUNKS - 1:
            du_ref[:, at * LANES : (at + 1) * LANES] = back(d_query).astype(BF)
        else:
            waiting = d_query

    def two_heads(store, first, second):
        return jnp.concatenate([store[first], store[second]], axis=0).T

    tail = jnp.where(lower, waiting, two_heads(d_k, 0, 0))
    du_ref[:, (CHUNKS - 1) * LANES : CHUNKS * LANES] = back(tail).astype(BF)
    for i in range(2):
        at = CHUNKS + i
        du_ref[:, at * LANES : (at + 1) * LANES] = back(two_heads(d_k, 1 + 2 * i, 2 + 2 * i)).astype(BF)
        at = CHUNKS + 2 + i
        du_ref[:, at * LANES : (at + 1) * LANES] = two_heads(d_v, 2 * i, 2 * i + 1).astype(BF)
    at = CHUNKS + 4
    du_ref[:, at * LANES :] = two_heads(d_v, 4, 4)[:, : du_ref.shape[1] - at * LANES].astype(BF)


def router_gate(x, router_row):
    return jax.nn.sigmoid(jnp.sum(x * router_row, axis=-1, keepdims=True))


def masks(select_refs, segment_ref, pad_ref, bias_ref, active_ref):
    seq_len = segment_ref.shape[1]
    square = (seq_len, seq_len)
    query, key = (lax.broadcasted_iota(jnp.int32, square, axis) for axis in (0, 1))
    diagonal = query == key
    segment = segment_ref[...].astype(F32)
    own = jnp.sum(jnp.where(diagonal, segment, 0.0), axis=1, keepdims=True)
    near = (key <= query) & (segment == own)
    real = pad_ref[...] == 1
    for recursion, ref in enumerate(select_refs):
        place = lax.broadcasted_iota(jnp.int32, (seq_len, ref.shape[1]), 0)
        active = jnp.max(jnp.where(ref[...] == place, 1.0, 0.0), axis=1, keepdims=True)
        active_ref[recursion] = active
        along = jnp.sum(jnp.where(diagonal, active, 0.0), axis=0, keepdims=True)
        usable = (along > 0.0) & real
        bias_ref[recursion] = jnp.where(near & (usable | diagonal), 0.0, -1e30)


def first_attention(x_ref, sel_one, sel_two, sel_three, segment_ref, pad_ref, cos_ref, sin_ref, gain_one, gain_two, qkv_w, out_w,
                    n1_ref, q_ref, kz_ref, vz_ref, p_ref, o_ref, attn_ref, n2_ref, bias_ref, active_ref):
    n1, o = n1_ref.at[0], o_ref.at[0, 0]
    masks((sel_one, sel_two, sel_three), segment_ref, pad_ref, bias_ref, active_ref)
    attention_forward(x_ref, bias_ref.at[0], cos_ref, sin_ref, gain_one[...], qkv_w, n1, q_ref, kz_ref, vz_ref, p_ref, o)
    attention_out(x_ref, o, out_w, gain_two[...], attn_ref, n2_ref)


def load_all(pairs, sems):
    return [pltpu.make_async_copy(src, dst, sems.at[i]) for i, (src, dst) in enumerate(pairs)]


def waits_at(condition, copies):
    def ready(*which):
        @pl.when(condition)
        def _():
            for i in which:
                copies[i].wait()

    return ready


def finish_attention_backward(x_ref, gain, active_ref, du_ref, qkv_w, base, state, total, out_ref):
    total[...] = contract_last(du_ref[...], qkv_w[...])
    terms = jnp.zeros((1, state.shape[1]), F32)

    def lap(i, terms):
        rows = pl.ds(pl.multiple_of(i * ROWS, ROWS), ROWS)
        d_rows, term = norm_back(x_ref[rows, :], gain, total[rows, :])
        new = jnp.where(active_ref[rows, :] > 0, base[rows, :] + d_rows, state[rows, :])
        out_ref[rows, :] = new
        return terms + term

    return lax.fori_loop(0, state.shape[0] // ROWS, lap, terms)


def all_steps(bias_ref, active_ref, router_ref, cos_ref, sin_ref, gain_one, gain_two,
              hidden_hbm, d_hidden_hbm, attn0_hbm, n20_hbm, n1_in, o_da_in, qkv_hbm, out_hbm, *rest):
    feed_hbm, rest = rest[:6], rest[6:]
    (n1_out, o_da_out, n2_df_out, near_out, far_out, late_out, du_out, final_out, base_ref, state_ref, small_ref), rest = rest[:11], rest[11:]
    qkv_w, out_w, *feed_w = rest[:8]
    (xs, attns, fs, slope0, slope1, silu0, silu1, qs, kzs, vzs, ps, n1, o, n2, m0, m1, df, dg0, dg1, dw0, dw1, da, du,
     total, d_branch, do_ref, load_sems, out_sems) = rest[8:]
    width = state_ref.shape[1]
    first_part = far_out.shape[3]
    laps = state_ref.shape[0] // ROWS
    loads = load_all(
        [*zip(feed_hbm, feed_w), (qkv_hbm, qkv_w), (out_hbm, out_w),
         (n20_hbm, n2), (attn0_hbm, attns.at[0]), (hidden_hbm, xs.at[0]), (d_hidden_hbm, state_ref)], load_sems)
    for i in (8, 0, 1, 2, 3, 4, 5, 9, 10, 6, 7, 11):
        loads[i].start()
    loads[8].wait()

    places = dict(n2=[(n2, n2_df_out.at[0])], m0=[(m0, near_out.at[0])], n1=[(n1, n1_out)], o=[(o, o_da_out.at[0])],
                  df=[(df, n2_df_out.at[1])], dg0=[(dg0, near_out.at[1])], dw0=[(dw0, near_out.at[2])],
                  da=[(da, o_da_out.at[1])], du=[(du, du_out)])
    for i, (name, ref) in enumerate((("m1", m1), ("dg1", dg1), ("dw1", dw1))):
        places[name] = [(ref.at[:, :first_part], far_out.at[i]), (ref.at[:, first_part:], late_out.at[i])]
    numbers = {}
    for pairs in places.values():
        for source, target in pairs:
            numbers[id(target)] = len(numbers)

    def leaving(recursion, names):
        return [pltpu.make_async_copy(source, target.at[recursion], out_sems.at[numbers[id(target)]])
                for name in names for source, target in places[name]]

    def start(recursion, *names):
        for copy in leaving(recursion, names):
            copy.start()

    def wait(recursion, *names):
        for copy in leaving(recursion, names):
            copy.wait()

    def forward(r, carry):
        ready = waits_at(r == 0, loads)
        start(r, "n2")

        @pl.when(r > 0)
        def _():
            wait(r - 1, "m0", "m1")

        feed_forward(n2, ((*feed_w[:3], m0, slope0.at[r], silu0.at[r]), (*feed_w[3:], m1, slope1.at[r], silu1.at[r])), total, ready)
        start(r, "m0", "m1")
        ready(9, 10)
        router_row = router_ref[pl.ds(r, 1), :]

        def finish(rows):
            x = xs[r, rows, :]
            f = total[rows, :].astype(BF)
            fs[r, rows, :] = f
            branch = attns[r, rows, :] + f.astype(F32)
            xs[r + 1, rows, :] = jnp.where(active_ref[r, rows, :] > 0, x + router_gate(x, router_row) * branch, x)

        over_rows(total.shape[0], finish)
        ready(6, 7)
        wait(r, "n2")

        @pl.when(r < RECURSIONS - 1)
        def _():
            @pl.when(r > 0)
            def _():
                wait(r, "n1", "o")

            attention_forward(xs.at[r + 1], bias_ref.at[r + 1], cos_ref, sin_ref, gain_one[...], qkv_w,
                              n1, qs.at[r], kzs.at[r], vzs.at[r], ps.at[r], o)
            start(r + 1, "n1", "o")
            attention_out(xs.at[r + 1], o, out_w, gain_two[...], attns.at[r + 1], n2)

        return carry

    lax.fori_loop(0, RECURSIONS, forward, 0)
    final = pltpu.make_async_copy(xs.at[RECURSIONS], final_out, out_sems.at[15])
    final.start()
    loads[11].wait()
    small_ref[...] = jnp.zeros(small_ref.shape, F32)

    def backward(i, carry):
        r = RECURSIONS - 1 - i
        router_row = router_ref[pl.ds(r, 1), :]

        @pl.when(i > 0)
        def _():
            wait(r + 1, "df", "dg0", "dg1", "dw0", "dw1", "da")

        def enter(lap, terms):
            rows = pl.ds(pl.multiple_of(lap * ROWS, ROWS), ROWS)
            x = xs[r, rows, :]
            d_new = jnp.where(active_ref[r, rows, :] > 0, state_ref[rows, :], 0.0)
            gate = router_gate(x, router_row)
            branch = attns[r, rows, :] + fs[r, rows, :].astype(F32)
            d_gate = jnp.sum(d_new * branch, axis=-1, keepdims=True)
            d_logit = d_gate * gate * (1.0 - gate)
            spread = gate * d_new
            d_branch[rows, :] = spread
            df[rows, :] = spread.astype(BF)
            base_ref[rows, :] = d_new + d_logit * router_row
            return terms + jnp.sum(d_logit * x, axis=0, keepdims=True)

        small_ref[pl.ds(2 + r, 1), :] = lax.fori_loop(0, laps, enter, jnp.zeros((1, width), F32))
        start(r, "df")
        feed_backward(df, ((*feed_w[:3], slope0.at[r], silu0.at[r], dg0, dw0), (*feed_w[3:], slope1.at[r], silu1.at[r], dg1, dw1)),
                      total, lambda *which: None)
        start(r, "dg0", "dg1", "dw0", "dw1")

        def leave(lap, terms):
            rows = pl.ds(pl.multiple_of(lap * ROWS, ROWS), ROWS)
            after = xs[r, rows, :] + attns[r, rows, :]
            d_after, term = norm_back(after, gain_two[...], total[rows, :].astype(BF).astype(F32))
            da[rows, :] = (d_branch[rows, :] + d_after).astype(BF)
            base_ref[rows, :] = base_ref[rows, :] + d_after
            return terms + term

        small_ref[1:2, :] = small_ref[1:2, :] + lax.fori_loop(0, laps, leave, jnp.zeros((1, width), F32))
        start(r, "da")

        @pl.when(r > 0)
        def _():
            @pl.when(i > 0)
            def _():
                wait(r + 1, "du")

            attention_backward(da, out_w, qkv_w, cos_ref, sin_ref, qs.at[r - 1], kzs.at[r - 1], vzs.at[r - 1], ps.at[r - 1], do_ref, du)
            start(r, "du")
            term = finish_attention_backward(xs.at[r], gain_one[...], active_ref.at[r], du, qkv_w, base_ref, state_ref, total, state_ref)
            small_ref[0:1, :] = small_ref[0:1, :] + term

        return carry

    lax.fori_loop(0, RECURSIONS, backward, 0)
    wait(RECURSIONS - 1, "m0", "m1", "n1", "o")
    wait(0, "df", "dg0", "dg1", "dw0", "dw1", "da")
    wait(1, "du")
    final.wait()


def last_attention(active_ref, cos_ref, sin_ref, gain_one, q_ref, kz_ref, vz_ref, p_ref, d_attn_ref, small_in, out_w,
                   x_hbm, base_hbm, state_hbm, qkv_hbm, du_in, token, du_ref, d_input_ref, small_ref,
                   do_ref, total, x, base, state, qkv_w, sems):
    copies = load_all([(qkv_hbm, qkv_w), (x_hbm, x), (base_hbm, base), (state_hbm, state)], sems)
    for copy in copies:
        copy.start()
    attention_backward(d_attn_ref.at[0, 0], out_w, qkv_w, cos_ref, sin_ref, q_ref, kz_ref, vz_ref, p_ref, do_ref, du_ref.at[0])
    for copy in copies:
        copy.wait()
    term = finish_attention_backward(x, gain_one[...], active_ref.at[0], du_ref.at[0], qkv_w, base, state, total, d_input_ref)
    small_ref[...] = small_in[...]
    small_ref[0:1, :] = small_in[0:1, :] + term


def swap_dp(values_in, bit, n_dp):
    return lax.ppermute(values_in, "dp", [(i, i ^ (1 << bit)) for i in range(n_dp)])


def swap_mp(values_in):
    return lax.ppermute(values_in, "mp", [(0, 1), (1, 0)])


def halving(parts, order, n_dp, index):
    bits = n_dp.bit_length() - 1
    left = list(range(bits - 1, -1, -1))
    shape = parts.shape[1:]
    held = parts.reshape((2,) * bits + shape)
    for step, bit in enumerate(order):
        at = left.index(bit)
        upper = ((index >> bit) & 1) == 1
        low = lax.index_in_dim(held, 0, at, keepdims=False)
        high = lax.index_in_dim(held, 1, at, keepdims=False)
        keep, send = jnp.where(upper, high, low), jnp.where(upper, low, high)
        got = swap_dp(send, bit, n_dp)
        last = step == bits - 1
        total = keep.astype(F32) + got.astype(F32)
        held = total if last else total.astype(BF)
        left.remove(bit)
    return held


def orders_of(bits):
    rest = list(range(3, bits))
    if bits < 3:
        return [list(range(bits))] * 3
    return [[0, 1, 2] + rest, [1, 0, 2] + rest, [2, 0, 1] + rest]


PART = 2 * LANES
FFN_TILES = (4, 4, 2)
FFN_ORDERS = ((2, 1, 3, 0), (1, 0, 2, 3), (2, 0, 3, 1))
ATTN_ORDER = (0, 1, 2, 3)
SCHEDULE = (
    "T0", "T1", "A", "T2",
    "F0", "F1", "A0", "F2",
    "F0", "F1", "A0", "F2",
    "F0", "F1", "A0", "F2",
)
SMALL = 48


def halves(bit, outs, index):
    mine = (index >> bit) & 1
    inner = 1 << bit
    for out, which in zip(outs, (mine, 1 - mine)):
        for p in range(out.shape[0]):
            for q in range(inner):
                yield out, p, q, p * 2 * inner + which * inner + q


def stacked_copies(pairs, sems):
    flat_pairs = []
    for sources, target in pairs:
        rows = target.shape[0] // 2
        flat_pairs += [(source, target.at[pl.ds(i * rows, rows)]) for i, source in enumerate(sources)]
    copies = load_all(flat_pairs, sems)
    for copy in copies:
        copy.start()
    return [copies[i : i + 2] for i in range(0, len(copies), 2)]


def ffn_terms(bit, tiles, at, at_b, n2_df_a, n2_df_b, units_a, units_b, token, keep_ref, send_ref, left, right, flat, sems):
    width = left.shape[2]
    columns, columns_b = (pl.ds(start, tiles * LANES) for start in (at, at_b))
    lefts = [(n2_df_a.at[i], n2_df_b.at[i]) for i in range(2)]
    m, dg, dw = [(units_a.at[i, :, columns], units_b.at[i, :, columns_b]) for i in range(3)]
    n2, dg, dw, df, m = stacked_copies(
        [(lefts[0], left.at[0]), (dg, right.at[0]), (dw, right.at[1]), (lefts[1], left.at[1]), (m, right.at[2])], sems)
    for matrix, needed in enumerate((n2 + dg, dw, df + m)):
        for copy in needed:
            copy.wait()
        terms = contract_rows(left[matrix // 2], right[matrix])
        for c in range(tiles):
            flat[pl.ds(tiles * width * matrix + c, width, stride=tiles), :] = terms[:, c * LANES : (c + 1) * LANES]
    rows = keep_ref.shape[2]
    for out, p, q, shard in halves(bit, (keep_ref, send_ref), lax.axis_index("dp")):
        out[p, q] = flat[pl.ds(pl.multiple_of(shard * rows, 8), rows), :].astype(BF)


def small_rows(small, packed):
    packed[...] = jnp.zeros(packed.shape, F32)
    width = small.shape[1]
    for i in range(2 + RECURSIONS):
        for c in range(CHUNKS):
            stop = min(width, (c + 1) * LANES)
            packed[i * CHUNKS + c : i * CHUNKS + c + 1, : stop - c * LANES] = small[i : i + 1, c * LANES : stop]
    return packed[...]


def split_small(small, ref, start):
    high = small.astype(BF)
    ref[start : start + SMALL, :] = high
    ref[start + SMALL : start + 2 * SMALL, :] = (small - high.astype(F32)).astype(BF)


def rounded_small(small):
    high = small.astype(BF)
    return high.astype(F32) + (small - high.astype(F32)).astype(BF).astype(F32)


def joined_small(ref, start):
    return ref[start : start + SMALL, :].astype(F32) + ref[start + SMALL : start + 2 * SMALL, :].astype(F32)


def attn_terms(bit, depth, n1_a, n1_b, du_a, du_b, o_da_a, o_da_b, small_a, small_b, token,
               keep, send, small_out, left, du_rows, da_rows, terms, flat, packed, sems):
    width = left.shape[2]
    base = 0
    lower = lane_of(width // 2) < HEAD_DIM
    n1, du, o, da = stacked_copies(
        [((n1_a, n1_b), left.at[0]), ((du_a, du_b), du_rows), ((o_da_a.at[0], o_da_b.at[0]), left.at[1]),
         ((o_da_a.at[1], o_da_b.at[1]), da_rows)], sems)
    for which, (right, needed) in enumerate(((du_rows, n1 + du), (da_rows, o + da))):
        for copy in needed:
            copy.wait()
        columns = right.shape[1]
        half = columns // LANES
        for start in range(0, columns, PART):
            stop = min(columns, start + PART)
            block = contract_rows(left[which], right[:, start:stop])
            if stop - start < PART:
                block = jnp.concatenate([block, jnp.zeros((width, PART - (stop - start)), F32)], axis=1)
            for part in range(0, stop - start, LANES):
                terms[(start + part) // LANES] = block[:, part : part + LANES]
        step = 2 * columns // LANES
        count = width // 2
        after = first_odd = None
        for c in range(half + 1):
            even = terms[c, pl.ds(0, count, stride=2), :]
            odd = other_half(terms[c, pl.ds(1, count, stride=2), :])
            if c < half:
                flat[pl.ds(base + c, count, stride=step), :] = even
            else:
                flat[pl.ds(base + c, count, stride=step), :] = jnp.where(lower, even, first_odd)
            if c == 0:
                first_odd = odd
            else:
                flat[pl.ds(base + half + c, count, stride=step), :] = jnp.where(lower, after, odd)
            after = odd
        base += width * columns // LANES
    index, core = lax.axis_index("dp"), lax.axis_index("mp")
    total = rounded_small(small_rows(small_a, packed.at[0])) + rounded_small(small_rows(small_b, packed.at[1]))
    small_out[...] = total
    outer, inner, rows = keep.shape[:3]
    split_small(total, send, outer * inner * rows)

    def rows_of_shard(shard):
        start = pl.multiple_of((2 * shard + core) * depth, 8)
        return flat[pl.ds(start, rows), :].astype(BF)

    mine = (index >> bit) & 1
    for p in range(outer):
        for q in range(inner):
            shard = 2 * p * inner + q
            keep[p, q] = rows_of_shard(shard + mine * inner)
            at = (p * inner + q) * rows
            send[at : at + rows, :] = rows_of_shard(shard + (1 - mine) * inner)


def fold(bit, kept, got, token, keep, send):
    mine = (lax.axis_index("dp") >> bit) & 1
    for p in range(kept.shape[0]):
        for q in range(kept.shape[2]):
            for out, which in ((keep, mine), (send, 1 - mine)):
                out[p, q] = (kept[p, which, q].astype(F32) + got[p, which, q].astype(F32)).astype(BF)


def fold_small(bit, kept, got, small, token, keep, send, small_out):
    mine = (lax.axis_index("dp") >> bit) & 1
    outer, _, inner, rows, _ = kept.shape
    for p in range(outer):
        for q in range(inner):
            totals = []
            for which in (mine, 1 - mine):
                start = pl.multiple_of(((2 * p + which) * inner + q) * rows, 16)
                totals.append((kept[p, which, q].astype(F32) + got[pl.ds(start, rows), :].astype(F32)).astype(BF))
            keep[p, q] = totals[0]
            at = (p * inner + q) * rows
            send[at : at + rows, :] = totals[1]
    total = rounded_small(small[...]) + joined_small(got, 2 * outer * inner * rows)
    small_out[...] = total
    split_small(total, send, outer * inner * rows)


def finish_streams(tiles, *refs):
    count = len(tiles)
    feeds, refs = refs[: 2 * count], refs[2 * count :]
    attn, refs = refs[:2], refs[2:]
    small, ffn_out, attn_out, one_out, two_out, router_out, flat, packed = refs
    every = sum(tiles)
    rows = ffn_out.shape[0] // every
    base = 0
    for i, wide in enumerate(tiles):
        flat[: rows * wide, :] = feeds[2 * i][...].astype(F32) + feeds[2 * i + 1][...].astype(F32)
        for c in range(wide):
            ffn_out[pl.ds(base + c, rows, stride=every), :] = flat[pl.ds(c, rows, stride=wide), :]
        base += wide
    padded = attn[0].shape[0]
    both = attn[0][...].astype(F32) + attn[1][:padded, :].astype(F32)
    attn_out[...] = both[: attn_out.shape[0]]
    total = rounded_small(small[...]) + joined_small(attn[1], padded)
    packed[...] = total
    width = one_out.shape[1]
    outs = [(one_out, 0), (two_out, 0), *[(router_out, i) for i in range(RECURSIONS)]]
    for i, (out, row) in enumerate(outs):
        for c in range(CHUNKS):
            stop = min(width, (c + 1) * LANES)
            out[row : row + 1, c * LANES : stop] = packed[i * CHUNKS + c : i * CHUNKS + c + 1, : stop - c * LANES]


class Stream:
    def __init__(self, order, bits):
        self.order, self.left, self.done = order, list(range(bits - 1, -1, -1)), 0
        self.kept = self.got = None

    def shape_for(self, array):
        at = self.left.index(self.order[self.done])
        rows, lanes = array.shape[-2:]
        return (1 << at, 2, 1 << (len(self.left) - 1 - at), rows, lanes)

    def sent(self, kept, send, n_dp):
        bit = self.order[self.done]
        self.kept, self.got = kept, swap_dp(send, bit, n_dp)
        self.left.remove(bit)
        self.done += 1


def on_device(
    hidden_in,
    sel_one,
    sel_two,
    sel_three,
    segment_ids,
    pad_mask,
    qkv_weight,
    out_weight,
    gate_weight,
    up_weight,
    down_weight,
    norm_one,
    norm_two,
    router_weight,
    d_hidden,
):
    seq_len, width = hidden_in.shape
    n_dp, n_mp = lax.axis_size("dp"), lax.axis_size("mp")
    dp_index, mp_index = lax.axis_index("dp"), lax.axis_index("mp")
    cosine, sine = rotary_tables(seq_len)
    weights = [(gate_weight, up_weight, down_weight)]
    weights.append(tuple(swap_mp(w) for w in weights[0]))
    gain_one, gain_two = norm_one.reshape(1, width), norm_two.reshape(1, width)
    padded = CHUNKS * LANES
    units = gate_weight.shape[1]
    feed_weights = (*weights[0], *weights[1])

    def shape(*dims, dtype=BF):
        return jax.ShapeDtypeStruct(dims, dtype)

    def whole(*dims, **kw):
        return pl.BlockSpec(dims, lambda *_: (0,) * len(dims), **kw)

    anywhere = pl.BlockSpec(memory_space=pl.ANY)
    one = pl.Buffered(1)
    stack = RECURSIONS, seq_len
    heads = (2 * KV_HEADS, seq_len, LANES)
    square = (HEADS, seq_len, seq_len)
    n1, q, kz, vz, p, o_da, attn, n2, bias, active = pl.pallas_call(
        first_attention,
        grid=(1,),
        in_specs=[
            whole(seq_len, width), *[whole(*ref.shape) for ref in (sel_one, sel_two, sel_three, segment_ids, pad_mask)],
            whole(seq_len, LANES), whole(seq_len, LANES), whole(1, width), whole(1, width), whole(*qkv_weight.shape), whole(*out_weight.shape),
        ],
        out_specs=[
            whole(1, seq_len, width), whole(seq_len, padded), whole(*heads), whole(*heads), whole(*square),
            whole(1, 1, seq_len, width), whole(seq_len, width), whole(seq_len, width), whole(RECURSIONS, seq_len, seq_len), whole(*stack, 1),
        ],
        out_shape=[
            shape(*stack, width), shape(seq_len, padded), shape(*heads), shape(*heads), shape(*square),
            shape(2, *stack, width), shape(seq_len, width, dtype=F32), shape(seq_len, width),
            shape(*stack, seq_len, dtype=F32), shape(*stack, 1, dtype=F32),
        ],
        compiler_params=pltpu.CompilerParams(vmem_limit_bytes=VMEM_MIB * MIB),
        cost_estimate=pl.CostEstimate(flops=2 * 10**9, bytes_accessed=12 * 10**6, transcendentals=600000),
        name="first_attention",
    )(hidden_in, sel_one, sel_two, sel_three, segment_ids, pad_mask, cosine, sine, gain_one, gain_two, qkv_weight, out_weight)
    attention_0 = (q, kz, vz, p)
    wide = qkv_weight.shape[1]
    row = (seq_len, width)
    kept = RECURSIONS - 1
    first_part = FFN_TILES[0] * LANES
    vm = pltpu.VMEM
    results = pl.pallas_call(
        all_steps,
        grid=(1,),
        in_specs=[
            whole(RECURSIONS, seq_len, seq_len), whole(RECURSIONS, seq_len, 1), whole(RECURSIONS, width),
            whole(seq_len, LANES), whole(seq_len, LANES), whole(1, width), whole(1, width), *[anywhere] * 14,
        ],
        out_specs=[*[anywhere] * 8, whole(*row), whole(*row), whole(8, width)],
        out_shape=[
            shape(*stack, width), *[shape(2, *stack, width)] * 2, shape(3, *stack, units), shape(3, *stack, first_part), shape(3, *stack, units - first_part), shape(*stack, wide),
            *[shape(*row, dtype=F32)] * 3, shape(8, width, dtype=F32),
        ],
        scratch_shapes=[
            *[vm(w.shape, BF) for w in (qkv_weight, out_weight, *feed_weights)],
            vm((RECURSIONS + 1, *row), F32), vm((RECURSIONS, *row), F32), vm((RECURSIONS, *row), BF),
            *[vm((*stack, units), BF)] * 4, vm((kept, seq_len, padded), BF), vm((kept, *heads), BF), vm((kept, *heads), BF),
            vm((kept, *square), BF), *[vm(row, BF)] * 3, *[vm((seq_len, units), BF)] * 2, vm(row, BF), *[vm((seq_len, units), BF)] * 4,
            vm(row, BF), vm((seq_len, wide), BF), vm(row, F32), vm(row, F32), vm((seq_len, padded), BF),
            pltpu.SemaphoreType.DMA((12,)), pltpu.SemaphoreType.DMA((16,)),
        ],
        input_output_aliases={11: 0, 12: 1},
        compiler_params=pltpu.CompilerParams(vmem_limit_bytes=VMEM_MIB * MIB),
        cost_estimate=pl.CostEstimate(flops=23 * 10**9, bytes_accessed=50 * 10**6, transcendentals=4 * 10**6),
        name="all_steps",
    )(bias, active, router_weight, cosine, sine, gain_one, gain_two, hidden_in, d_hidden, attn, n2, n1, o_da,
      qkv_weight, out_weight, *feed_weights)
    n1, o_da, n2_df, near, far, late, du, state, base, grad_state, small = results

    def run_last(token):
        return pl.pallas_call(
            last_attention,
            grid=(1,),
            in_specs=[
                whole(1, seq_len, 1), whole(seq_len, LANES), whole(seq_len, LANES), whole(1, width),
                whole(seq_len, padded), whole(*heads), whole(*heads), whole(*square),
                pl.BlockSpec((1, 1, seq_len, width), lambda i: (1, 0, 0, 0)), whole(8, width), whole(*out_weight.shape), *[anywhere] * 6,
            ],
            out_specs=[whole(1, seq_len, qkv_weight.shape[1]), whole(seq_len, width), whole(8, width)],
            out_shape=[shape(*stack, qkv_weight.shape[1]), shape(seq_len, width, dtype=F32), shape(8, width, dtype=F32)],
            scratch_shapes=[
                pltpu.VMEM((seq_len, padded), BF), *[pltpu.VMEM((seq_len, width), F32)] * 4,
                pltpu.VMEM(qkv_weight.shape, BF), pltpu.SemaphoreType.DMA((4,)),
            ],
            input_output_aliases={15: 0},
            compiler_params=pltpu.CompilerParams(vmem_limit_bytes=VMEM_MIB * MIB),
            cost_estimate=pl.CostEstimate(flops=1, bytes_accessed=1, transcendentals=0),
            name="last_attention",
        )(active, cosine, sine, gain_one, *attention_0, o_da, small, out_weight, hidden_in, base, grad_state, qkv_weight, du, token)

    def rows_of(stacked):
        return stacked.reshape(*stacked.shape[:-3], -1, stacked.shape[-1])

    bits = n_dp.bit_length() - 1
    share = (qkv_weight.size + out_weight.size) // (n_dp * n_mp)
    if bits == 4 and 3 * width % n_dp == 0 and units == sum(FFN_TILES) * LANES and share % (8 * LANES) == 0:
        n2_df_rows = [rows_of(t) for t in (n2_df, swap_mp(n2_df))]
        near, far_b = rows_of(near), rows_of(swap_mp(far))
        n1_b = rows_of(swap_mp(n1))
        streams = [Stream(order, bits) for order in FFN_ORDERS]
        attn_stream = Stream(ATTN_ORDER, bits)
        depth = share // LANES
        tiled = -(-depth // 16) * 16
        common = dict(
            grid=(1,),
            compiler_params=pltpu.CompilerParams(vmem_limit_bytes=VMEM_MIB * MIB),
            cost_estimate=pl.CostEstimate(flops=1, bytes_accessed=1, transcendentals=0),
        )

        def wholes(arrays):
            return [whole(*t.shape) for t in arrays]

        def terms_of(j, token):
            stream, tiles = streams[j], FFN_TILES[j]
            at = sum(FFN_TILES[:j]) * LANES
            factors = (*n2_df_rows, near, far_b if j == 0 else late_b)
            bit = stream.order[0]
            dims = (1 << (bits - 1 - bit), 1 << bit, 3 * width // n_dp * tiles, LANES)
            both = 2 * RECURSIONS * seq_len
            keep, send = pl.pallas_call(
                functools.partial(ffn_terms, bit, tiles, at, 0 if j == 0 else at - first_part),
                in_specs=[anywhere] * (len(factors) + 1),
                out_specs=[whole(*dims)] * 2,
                out_shape=[shape(*dims)] * 2,
                scratch_shapes=[pltpu.VMEM((2, both, width), BF), pltpu.VMEM((3, both, tiles * LANES), BF),
                                pltpu.VMEM((3 * width * tiles, LANES), F32), pltpu.SemaphoreType.DMA((10,))],
                name=f"ffn_terms_{j}",
                **common,
            )(*factors, token)
            stream.sent(keep, send, n_dp)
            return keep

        def fold_stream(stream, token, small_own=None):
            bit = stream.order[stream.done]
            dims = stream.shape_for(stream.kept)
            kept = stream.kept.reshape(dims)
            held = (dims[0], *dims[2:])
            if small_own is None:
                operands = (kept, stream.got.reshape(dims))
                outs = (shape(*held), shape(*held))
            else:
                operands = (kept, stream.got, small_own)
                outs = (shape(*held), shape(dims[0] * dims[2] * dims[3] + 2 * SMALL, LANES), shape(SMALL, LANES, dtype=F32))
            results = pl.pallas_call(
                functools.partial(fold if small_own is None else fold_small, bit),
                in_specs=[*wholes(operands), anywhere],
                out_specs=wholes(outs),
                out_shape=outs,
                name="fold_terms",
                **common,
            )(*operands, token)
            stream.sent(results[0], results[1], n_dp)
            return results

        du, grad_state, small = run_last(small)
        late, du, small = lax.optimization_barrier((late, du, small))
        late_b, du_b = rows_of(swap_mp(late)), rows_of(swap_mp(du))
        token = small
        for item in SCHEDULE:
            if item[0] == "T":
                token = terms_of(int(item[1:]), token)
                if item == "T0":
                    o_da, small, token = lax.optimization_barrier((o_da, small, token))
                    o_da_b, small_b = rows_of(swap_mp(o_da)), swap_mp(small)
            elif item[0] == "F":
                token = fold_stream(streams[int(item[1:])], token)[0]
            elif item == "A":
                bit = attn_stream.order[0]
                dims = (1 << (bits - 1 - bit), 1 << bit, tiled, LANES)
                operands = (rows_of(n1), n1_b, rows_of(du), du_b, rows_of(o_da), o_da_b, small, small_b)
                outs = (shape(*dims), shape(n_dp // 2 * tiled + 2 * SMALL, LANES), shape(SMALL, LANES, dtype=F32))
                keep, send, small_own = pl.pallas_call(
                    functools.partial(attn_terms, bit, depth),
                    in_specs=[*[anywhere] * 6, *wholes(operands[6:]), anywhere],
                    out_specs=wholes(outs),
                    out_shape=outs,
                    scratch_shapes=[pltpu.VMEM((2, 2 * RECURSIONS * seq_len, width), BF),
                                    *[pltpu.VMEM((2 * RECURSIONS * seq_len, t.shape[-1]), BF) for t in (du, o_da)],
                                    pltpu.VMEM((-(-du.shape[-1] // PART) * 2, width, LANES), F32),
                                    pltpu.VMEM((n_dp * 2 * depth + tiled - depth, LANES), F32), pltpu.VMEM((2, SMALL, LANES), F32),
                                    pltpu.SemaphoreType.DMA((8,))],
                    name="attn_terms",
                    **common,
                )(*operands, token)
                attn_stream.sent(keep, send, n_dp)
                token = small_own
            else:
                token, _, small_own = fold_stream(attn_stream, token, small_own)
        ends = [t.reshape(t.shape[-2:]) for stream in (*streams, attn_stream) for t in (stream.kept, stream.got)]
        outs = (shape(3 * width // n_dp * sum(FFN_TILES), LANES, dtype=F32), shape(depth, LANES, dtype=F32),
                shape(1, width, dtype=F32), shape(1, width, dtype=F32), shape(RECURSIONS, width, dtype=F32))
        ffn_flat, attn_flat, one, two, router = pl.pallas_call(
            functools.partial(finish_streams, FFN_TILES),
            in_specs=wholes((*ends, small_own)),
            out_specs=wholes(outs),
            out_shape=outs,
            scratch_shapes=[pltpu.VMEM((3 * width // n_dp * max(FFN_TILES), LANES), F32), pltpu.VMEM((SMALL, LANES), F32)],
            name="finish_streams",
            **common,
        )(*ends, small_own)
        return (state, grad_state, attn_flat.reshape(-1), ffn_flat.reshape(1, -1), one.reshape(-1), two.reshape(-1), router)

    du, grad_state, small = run_last(small)
    two, feed = rows_of(n2_df)
    o, d_attn = rows_of(o_da)
    far = jnp.concatenate([far, late], axis=-1)
    sides = [[t[i] for i in (1, 2, 0)] for t in (rows_of(near), rows_of(far))]

    def side_terms(side, columns):
        return jnp.concatenate(
            [
                contract_rows(left, sides[side][which][:, columns]).astype(BF)
                for which, left in enumerate((two, two, feed))
            ],
            axis=0,
        )

    orders = orders_of(bits)
    if 3 * width % n_dp == 0 and units % 1280 == 0:
        fifth = units // 5
        streams = [(orders[i], slice(j * fifth, (j + 1) * fifth)) for i, j in ((0, 0), (1, 1), (2, 2), (0, 3), (1, 4))]
        done = []
        for order, columns in streams:
            terms = side_terms(0, columns).astype(F32) + swap_mp(side_terms(1, columns)).astype(F32)
            done.append(halving(terms.astype(BF).reshape(n_dp, 3 * width // n_dp, fifth), order, n_dp, dp_index))
        ffn_flat = jnp.concatenate(done, axis=1).reshape(1, -1)
    else:
        terms = side_terms(0, slice(None)).astype(F32) + swap_mp(side_terms(1, slice(None))).astype(F32)
        terms = terms.astype(BF).reshape(n_dp, 3 * width * units // n_dp // 128, 128)
        ffn_flat = halving(terms, orders[0], n_dp, dp_index).reshape(1, -1)

    grad_qkv = contract_rows(rows_of(n1), rows_of(du)).astype(BF)
    grad_out = contract_rows(o, d_attn).astype(BF)
    attn = jnp.concatenate([grad_qkv.reshape(-1), grad_out.reshape(-1)]).reshape(n_dp, 2, share // 128, 128)
    keep = jnp.where(mp_index == 0, attn[:, 0], attn[:, 1])
    send = jnp.where(mp_index == 0, attn[:, 1], attn[:, 0])
    attn = (keep.astype(F32) + swap_mp(send).astype(F32)).astype(BF)
    cuts = [0, (share // 128) // 24 * 8, (share // 128) // 12 * 8, share // 128]
    attn_flat = jnp.concatenate(
        [halving(attn[:, a:b], order, n_dp, dp_index) for a, b, order in zip(cuts, cuts[1:], orders)], axis=0
    ).reshape(-1)

    small = small + swap_mp(small)
    for bit in range(bits):
        small = small + swap_dp(small, bit, n_dp)
    return (state, grad_state, attn_flat, ffn_flat, small[0], small[1], small[2 : 2 + RECURSIONS])


def solution(mesh):
    both = P(("dp", "mp"), None)
    in_specs = (
        both,
        both,
        both,
        both,
        both,
        both,
        P(),
        P(),
        P(None, "mp"),
        P(None, "mp"),
        P(None, "mp"),
        P(),
        P(),
        P(),
        both,
    )
    out_specs = (both, both, P(("dp", "mp")), P("mp", "dp"), P(), P(), P())
    return jax.shard_map(
        on_device, mesh=mesh, in_specs=in_specs, out_specs=out_specs, check_vma=False
    )
```

```python
import functools
import math

import jax
import jax.numpy as jnp
import numpy as np
from jax import lax
from jax.experimental import pallas as pl
from jax.experimental.pallas import tpu as pltpu
from jax.sharding import PartitionSpec as P

HEADS = 15
KV_HEADS = 5
HEAD_DIM = 64
RECURSIONS = 3
GROUPS = HEADS // KV_HEADS
EPS = 1e-05
BF = jnp.bfloat16
F32 = jnp.float32


LANES = 128
CHUNKS = -(-HEADS * HEAD_DIM // LANES)
ROWS = 192
BLOCK = 256
MIB = 1 << 20
VMEM_MIB = 63


def rotary_tables(seq_len):
    half = HEAD_DIM // 2
    frequency = np.float32(100000.0) ** (
        np.float32(-2.0) * np.arange(half, dtype=np.float32) / np.float32(HEAD_DIM)
    )
    angles = np.arange(seq_len, dtype=np.float32)[:, None] * frequency.astype(np.float32)
    cosine, sine = np.cos(angles), np.sin(angles)
    return (
        jnp.asarray(np.concatenate([cosine] * 4, axis=1), F32),
        jnp.asarray(np.concatenate([-sine, sine] * 2, axis=1), F32),
    )


def contract_rows(left, right):
    return lax.dot_general(left, right, (((0,), (0,)), ((), ())), preferred_element_type=F32)


def contract_last(left, right):
    return lax.dot_general(left, right, (((1,), (1,)), ((), ())), preferred_element_type=F32)


def plain(left, right):
    return jnp.dot(left, right, preferred_element_type=F32)


def inverse_rms(rows):
    return lax.rsqrt(jnp.mean(rows * rows, axis=-1, keepdims=True) + EPS)


def norm_back(rows, gain, d_out):
    inv = inverse_rms(rows)
    scaled = d_out * gain
    inner = jnp.mean(scaled * rows, axis=-1, keepdims=True)
    d_rows = inv * scaled - rows * (inv * inv * inv * inner)
    return d_rows, jnp.sum(d_out * rows * inv, axis=0, keepdims=True)


def lane_of(rows):
    return lax.broadcasted_iota(jnp.int32, (rows, LANES), 1)


def swapped(chunk):
    first = lane_of(chunk.shape[0]) % HEAD_DIM < HEAD_DIM // 2
    return jnp.where(first, pltpu.roll(chunk, LANES - 32, 1), pltpu.roll(chunk, 32, 1))


def other_half(chunk):
    return pltpu.roll(chunk, HEAD_DIM, 1)


def over_rows(count, body):
    def lap(i, carry):
        body(pl.ds(pl.multiple_of(i * ROWS, ROWS), ROWS))
        return carry

    lax.fori_loop(0, count // ROWS, lap, 0)


def attention_forward(x_ref, bias_ref, cos_ref, sin_ref, gain, qkv_w, n1_ref, q_ref, kz_ref, vz_ref, p_ref, o_ref):
    seq_len, width = x_ref.shape
    scale = 1.0 / math.sqrt(HEAD_DIM)

    def norm(rows):
        x = x_ref[rows, :]
        n1_ref[rows, :] = (x * inverse_rms(x) * gain).astype(BF)

    over_rows(seq_len, norm)
    lower = lane_of(seq_len) < HEAD_DIM
    n1 = n1_ref[...]

    def spread(ref, head, chunk, upper):
        flipped = other_half(chunk)
        here, there = (flipped, chunk) if upper else (chunk, flipped)
        ref[2 * head] = jnp.where(lower, here, 0.0).astype(BF)
        ref[2 * head + 1] = jnp.where(lower, 0.0, there).astype(BF)

    columns = qkv_w.shape[1]
    for start in range(0, columns, 2 * LANES):
        wide = plain(n1, qkv_w[:, start : min(start + 2 * LANES, columns)])
        for part in range(0, wide.shape[1], LANES):
            chunk = wide[:, part : part + LANES]
            if chunk.shape[1] < LANES:
                chunk = jnp.concatenate([chunk, jnp.zeros_like(chunk)], axis=1)
            at = (start + part) // LANES
            heads = (2 * at, 2 * at + 1)
            if heads[0] < HEADS + KV_HEADS:
                chunk = chunk * cos_ref[...] + swapped(chunk) * sin_ref[...]
                if heads[0] < HEADS:
                    q_ref[:, at * LANES : (at + 1) * LANES] = chunk.astype(BF)
            for upper, head in enumerate(heads):
                if HEADS <= head < HEADS + KV_HEADS:
                    spread(kz_ref, head - HEADS, chunk, upper)
                elif HEADS + KV_HEADS <= head < HEADS + 2 * KV_HEADS:
                    spread(vz_ref, head - HEADS - KV_HEADS, chunk, upper)

    for at in range(CHUNKS):
        query = q_ref[:, at * LANES : (at + 1) * LANES]
        total = None
        for upper in range(2):
            head = 2 * at + upper
            if head < HEADS:
                key = 2 * (head // GROUPS) + upper
                scores = contract_last(query, kz_ref[key]) * scale + bias_ref[...]
                top = jnp.max(scores, axis=-1, keepdims=True)
                exponent = jnp.exp(scores - top)
                share = pl.reciprocal(jnp.sum(exponent, axis=-1, keepdims=True))
                attend = (exponent * share).astype(BF)
                p_ref[head] = attend
                mixed = plain(attend, vz_ref[key])
                total = mixed if total is None else total + mixed
        stop = min(width, (at + 1) * LANES)
        o_ref[:, at * LANES : stop] = total[:, : stop - at * LANES].astype(BF)


def attention_out(x_ref, o_ref, out_w, gain, attn_ref, n2_ref):
    attn_ref[...] = plain(o_ref[...], out_w[...])

    def norm(rows):
        after = x_ref[rows, :] + attn_ref[rows, :]
        n2_ref[rows, :] = (after * inverse_rms(after) * gain).astype(BF)

    over_rows(x_ref.shape[0], norm)


def feed_side(n2_ref, weights, results, ready):
    n2 = n2_ref[...]
    gate_w, up_w, down_w = weights
    m_ref, slope_ref, silu_ref = results
    ready(0, 1)
    for start in range(0, gate_w.shape[1], BLOCK):
        at = slice(start, start + BLOCK)
        g, u = plain(n2, gate_w[:, at]), plain(n2, up_w[:, at])
        s = jax.nn.sigmoid(g)
        silu = g * s
        m_ref[:, at] = (silu * u).astype(BF)
        slope_ref[:, at] = (u * s * (1.0 + g * (1.0 - s))).astype(BF)
        silu_ref[:, at] = silu.astype(BF)
    ready(2)
    return contract_last(m_ref[...], down_w[...])


def feed_backward(df_ref, sides, d_two_ref, ready):
    d_feed = df_ref[...]
    for side, (gate_w, up_w, down_w, slope_ref, silu_ref, dg_ref, du_ref) in enumerate(sides):
        ready(3 * side)
        for start in range(0, gate_w.shape[1], BLOCK):
            at = slice(start, start + BLOCK)
            d_hidden = plain(d_feed, down_w[:, at])
            dg_ref[:, at] = (d_hidden * slope_ref[:, at].astype(F32)).astype(BF)
            du_ref[:, at] = (d_hidden * silu_ref[:, at].astype(F32)).astype(BF)
        ready(3 * side + 1, 3 * side + 2)
        part = contract_last(dg_ref[...], gate_w[...]) + contract_last(du_ref[...], up_w[...])
        d_two_ref[...] = part if side == 0 else d_two_ref[...] + part


def attention_backward(d_attn_ref, out_w, qkv_w, cos_ref, sin_ref, q_ref, kz_ref, vz_ref, p_ref, do_ref, du_ref):
    seq_len, width = d_attn_ref.shape
    scale = 1.0 / math.sqrt(HEAD_DIM)
    do_ref[:, :width] = contract_last(d_attn_ref[...], out_w[...]).astype(BF)
    do_ref[:, width:] = jnp.zeros((seq_len, do_ref.shape[1] - width), BF)
    lower = lane_of(seq_len) < HEAD_DIM
    cosine, sine = cos_ref[...], sin_ref[...]

    def back(chunk):
        chunk = chunk * scale
        return chunk * cosine - swapped(chunk) * sine

    waiting, d_k, d_v = None, {}, {}
    for at in range(CHUNKS):
        query, d_mixed = (ref[:, at * LANES : (at + 1) * LANES] for ref in (q_ref, do_ref))
        query_t, d_mixed_t = query.T, d_mixed.T
        d_query = None
        for upper in range(2):
            head = 2 * at + upper
            if head >= HEADS:
                continue
            group = head // GROUPS
            key = 2 * group + upper
            rows = slice(upper * HEAD_DIM, (upper + 1) * HEAD_DIM)
            attend = p_ref[head]
            d_attend = contract_last(d_mixed, vz_ref[key])
            soft = attend.astype(F32)
            weighted = soft * d_attend
            inner = jnp.sum(weighted, axis=-1, keepdims=True)
            d_scores = (weighted - soft * inner).astype(BF)
            part = plain(d_scores, kz_ref[key])
            d_query = part if d_query is None else d_query + part
            for store, term in ((d_k, plain(query_t[rows], d_scores)), (d_v, plain(d_mixed_t[rows], attend))):
                store[group] = term if group not in store else store[group] + term
        if at < CHUNKS - 1:
            du_ref[:, at * LANES : (at + 1) * LANES] = back(d_query).astype(BF)
        else:
            waiting = d_query

    def two_heads(store, first, second):
        return jnp.concatenate([store[first], store[second]], axis=0).T

    tail = jnp.where(lower, waiting, two_heads(d_k, 0, 0))
    du_ref[:, (CHUNKS - 1) * LANES : CHUNKS * LANES] = back(tail).astype(BF)
    for i in range(2):
        at = CHUNKS + i
        du_ref[:, at * LANES : (at + 1) * LANES] = back(two_heads(d_k, 1 + 2 * i, 2 + 2 * i)).astype(BF)
        at = CHUNKS + 2 + i
        du_ref[:, at * LANES : (at + 1) * LANES] = two_heads(d_v, 2 * i, 2 * i + 1).astype(BF)
    at = CHUNKS + 4
    du_ref[:, at * LANES :] = two_heads(d_v, 4, 4)[:, : du_ref.shape[1] - at * LANES].astype(BF)


def router_gate(x, router_row):
    return jax.nn.sigmoid(jnp.sum(x * router_row, axis=-1, keepdims=True))


def masks(select_refs, segment_ref, pad_ref, bias_ref, active_ref):
    seq_len = segment_ref.shape[1]
    square = (seq_len, seq_len)
    query, key = (lax.broadcasted_iota(jnp.int32, square, axis) for axis in (0, 1))
    diagonal = query == key
    segment = segment_ref[...].astype(F32)
    own = jnp.sum(jnp.where(diagonal, segment, 0.0), axis=1, keepdims=True)
    near = (key <= query) & (segment == own)
    real = pad_ref[...] == 1
    for recursion, ref in enumerate(select_refs):
        place = lax.broadcasted_iota(jnp.int32, (seq_len, ref.shape[1]), 0)
        active = jnp.max(jnp.where(ref[...] == place, 1.0, 0.0), axis=1, keepdims=True)
        active_ref[recursion] = active
        along = jnp.sum(jnp.where(diagonal, active, 0.0), axis=0, keepdims=True)
        usable = (along > 0.0) & real
        bias_ref[recursion] = jnp.where(near & (usable | diagonal), 0.0, -1e30)


def first_attention(x_ref, sel_one, sel_two, sel_three, segment_ref, pad_ref, cos_ref, sin_ref, gain_one, gain_two, qkv_w, out_w,
                    gate_hbm, up_hbm, down_hbm, n1_ref, q_ref, kz_ref, vz_ref, p_ref, o_ref, attn_ref, n2_ref, bias_ref, active_ref,
                    m_ref, slope_ref, silu_ref, f_ref, gate_w, up_w, down_w, sems):
    copies = load_all([(gate_hbm, gate_w), (up_hbm, up_w), (down_hbm, down_w)], sems)
    for copy in copies:
        copy.start()
    n1, o = n1_ref.at[0], o_ref.at[0, 0]
    masks((sel_one, sel_two, sel_three), segment_ref, pad_ref, bias_ref, active_ref)
    attention_forward(x_ref, bias_ref.at[0], cos_ref, sin_ref, gain_one[...], qkv_w, n1, q_ref, kz_ref, vz_ref, p_ref, o)
    attention_out(x_ref, o, out_w, gain_two[...], attn_ref, n2_ref)

    def ready(*which):
        for i in which:
            copies[i].wait()

    f_ref[...] = feed_side(n2_ref, (gate_w, up_w, down_w), (m_ref.at[0, 0], slope_ref, silu_ref), ready)


def load_all(pairs, sems):
    return [pltpu.make_async_copy(src, dst, sems.at[i]) for i, (src, dst) in enumerate(pairs)]


def waits_at(condition, copies):
    def ready(*which):
        @pl.when(condition)
        def _():
            for i in which:
                copies[i].wait()

    return ready


def finish_attention_backward(x_ref, gain, active_ref, du_ref, qkv_w, base, state, total, out_ref):
    total[...] = contract_last(du_ref[...], qkv_w[...])
    terms = jnp.zeros((1, state.shape[1]), F32)

    def lap(i, terms):
        rows = pl.ds(pl.multiple_of(i * ROWS, ROWS), ROWS)
        d_rows, term = norm_back(x_ref[rows, :], gain, total[rows, :])
        new = jnp.where(active_ref[rows, :] > 0, base[rows, :] + d_rows, state[rows, :])
        out_ref[rows, :] = new
        return terms + term

    return lax.fori_loop(0, state.shape[0] // ROWS, lap, terms)


def all_steps(bias_ref, active_ref, router_ref, cos_ref, sin_ref, gain_one, gain_two,
              hidden_hbm, d_hidden_hbm, attn0_hbm, n20_hbm, slope_hbm, silu_hbm, f_hbm, n1_in, o_da_in, near_in,
              qkv_hbm, out_hbm, *rest):
    feed_hbm, rest = rest[:6], rest[6:]
    (n1_out, o_da_out, n2_df_out, near_out, far_out, late_out, du_out, final_out, base_ref, state_ref, small_ref), rest = rest[:11], rest[11:]
    qkv_w, out_w, *feed_w = rest[:8]
    (xs, attns, fs, slope0, slope1, silu0, silu1, qs, kzs, vzs, ps, n1, o, n2, m0, m1, df, dg0, dg1, dw0, dw1, da, du,
     total, d_branch, do_ref, load_sems, out_sems) = rest[8:]
    width = state_ref.shape[1]
    first_part = far_out.shape[3]
    laps = state_ref.shape[0] // ROWS
    loads = load_all(
        [*zip(feed_hbm, feed_w), (qkv_hbm, qkv_w), (out_hbm, out_w),
         (n20_hbm, n2), (attn0_hbm, attns.at[0]), (hidden_hbm, xs.at[0]), (d_hidden_hbm, state_ref),
         (f_hbm, total), (slope_hbm, slope0.at[0]), (silu_hbm, silu0.at[0])], load_sems)
    for i in (8, 3, 4, 5, 12, 9, 10, 6, 7, 0, 1, 2, 13, 14, 11):
        loads[i].start()
    loads[8].wait()

    places = dict(n2=[(n2, n2_df_out.at[0])], m0=[(m0, near_out.at[0])], n1=[(n1, n1_out)], o=[(o, o_da_out.at[0])],
                  df=[(df, n2_df_out.at[1])], dg0=[(dg0, near_out.at[1])], dw0=[(dw0, near_out.at[2])],
                  da=[(da, o_da_out.at[1])], du=[(du, du_out)])
    for i, (name, ref) in enumerate((("m1", m1), ("dg1", dg1), ("dw1", dw1))):
        places[name] = [(ref.at[:, :first_part], far_out.at[i]), (ref.at[:, first_part:], late_out.at[i])]
    numbers = {}
    for pairs in places.values():
        for source, target in pairs:
            numbers[id(target)] = len(numbers)

    def leaving(recursion, names):
        return [pltpu.make_async_copy(source, target.at[recursion], out_sems.at[numbers[id(target)]])
                for name in names for source, target in places[name]]

    def start(recursion, *names):
        for copy in leaving(recursion, names):
            copy.start()

    def wait(recursion, *names):
        for copy in leaving(recursion, names):
            copy.wait()

    def forward(r, carry):
        ready, later = (waits_at(r == step, loads) for step in range(2))
        start(r, "n2")

        @pl.when(r > 0)
        def _():
            @pl.when(r > 1)
            def _():
                wait(r - 1, "m0")

            total[...] = feed_side(n2, feed_w[:3], (m0, slope0.at[r], silu0.at[r]), later)
            start(r, "m0")
            wait(r - 1, "m1")

        part = feed_side(n2, feed_w[3:], (m1, slope1.at[r], silu1.at[r]), lambda *which: ready(*[3 + i for i in which]))
        ready(12)
        total[...] = total[...] + part
        start(r, "m1")
        ready(9, 10)
        router_row = router_ref[pl.ds(r, 1), :]

        def finish(rows):
            x = xs[r, rows, :]
            f = total[rows, :].astype(BF)
            fs[r, rows, :] = f
            branch = attns[r, rows, :] + f.astype(F32)
            xs[r + 1, rows, :] = jnp.where(active_ref[r, rows, :] > 0, x + router_gate(x, router_row) * branch, x)

        over_rows(total.shape[0], finish)
        ready(6, 7)
        wait(r, "n2")

        @pl.when(r < RECURSIONS - 1)
        def _():
            @pl.when(r > 0)
            def _():
                wait(r, "n1", "o")

            attention_forward(xs.at[r + 1], bias_ref.at[r + 1], cos_ref, sin_ref, gain_one[...], qkv_w,
                              n1, qs.at[r], kzs.at[r], vzs.at[r], ps.at[r], o)
            start(r + 1, "n1", "o")
            attention_out(xs.at[r + 1], o, out_w, gain_two[...], attns.at[r + 1], n2)

        return carry

    lax.fori_loop(0, RECURSIONS, forward, 0)
    final = pltpu.make_async_copy(xs.at[RECURSIONS], final_out, out_sems.at[15])
    final.start()
    for i in (11, 13, 14):
        loads[i].wait()
    small_ref[...] = jnp.zeros(small_ref.shape, F32)

    def backward(i, carry):
        r = RECURSIONS - 1 - i
        router_row = router_ref[pl.ds(r, 1), :]

        @pl.when(i > 0)
        def _():
            wait(r + 1, "df", "dg0", "dg1", "dw0", "dw1", "da")

        def enter(lap, terms):
            rows = pl.ds(pl.multiple_of(lap * ROWS, ROWS), ROWS)
            x = xs[r, rows, :]
            d_new = jnp.where(active_ref[r, rows, :] > 0, state_ref[rows, :], 0.0)
            gate = router_gate(x, router_row)
            branch = attns[r, rows, :] + fs[r, rows, :].astype(F32)
            d_gate = jnp.sum(d_new * branch, axis=-1, keepdims=True)
            d_logit = d_gate * gate * (1.0 - gate)
            spread = gate * d_new
            d_branch[rows, :] = spread
            df[rows, :] = spread.astype(BF)
            base_ref[rows, :] = d_new + d_logit * router_row
            return terms + jnp.sum(d_logit * x, axis=0, keepdims=True)

        small_ref[pl.ds(2 + r, 1), :] = lax.fori_loop(0, laps, enter, jnp.zeros((1, width), F32))
        start(r, "df")
        feed_backward(df, ((*feed_w[:3], slope0.at[r], silu0.at[r], dg0, dw0), (*feed_w[3:], slope1.at[r], silu1.at[r], dg1, dw1)),
                      total, lambda *which: None)
        start(r, "dg0", "dg1", "dw0", "dw1")

        def leave(lap, terms):
            rows = pl.ds(pl.multiple_of(lap * ROWS, ROWS), ROWS)
            after = xs[r, rows, :] + attns[r, rows, :]
            d_after, term = norm_back(after, gain_two[...], total[rows, :].astype(BF).astype(F32))
            da[rows, :] = (d_branch[rows, :] + d_after).astype(BF)
            base_ref[rows, :] = base_ref[rows, :] + d_after
            return terms + term

        small_ref[1:2, :] = small_ref[1:2, :] + lax.fori_loop(0, laps, leave, jnp.zeros((1, width), F32))
        start(r, "da")

        @pl.when(r > 0)
        def _():
            @pl.when(i > 0)
            def _():
                wait(r + 1, "du")

            attention_backward(da, out_w, qkv_w, cos_ref, sin_ref, qs.at[r - 1], kzs.at[r - 1], vzs.at[r - 1], ps.at[r - 1], do_ref, du)
            start(r, "du")
            term = finish_attention_backward(xs.at[r], gain_one[...], active_ref.at[r], du, qkv_w, base_ref, state_ref, total, state_ref)
            small_ref[0:1, :] = small_ref[0:1, :] + term

        return carry

    lax.fori_loop(0, RECURSIONS, backward, 0)
    wait(RECURSIONS - 1, "m0", "m1", "n1", "o")
    wait(0, "df", "dg0", "dg1", "dw0", "dw1", "da")
    wait(1, "du")
    final.wait()


def last_attention(active_ref, cos_ref, sin_ref, gain_one, q_ref, kz_ref, vz_ref, p_ref, d_attn_ref, small_in, out_w,
                   x_hbm, base_hbm, state_hbm, qkv_hbm, du_in, token, du_ref, d_input_ref, small_ref,
                   do_ref, total, x, base, state, qkv_w, sems):
    copies = load_all([(qkv_hbm, qkv_w), (x_hbm, x), (base_hbm, base), (state_hbm, state)], sems)
    for copy in copies:
        copy.start()
    attention_backward(d_attn_ref.at[0, 0], out_w, qkv_w, cos_ref, sin_ref, q_ref, kz_ref, vz_ref, p_ref, do_ref, du_ref.at[0])
    for copy in copies:
        copy.wait()
    term = finish_attention_backward(x, gain_one[...], active_ref.at[0], du_ref.at[0], qkv_w, base, state, total, d_input_ref)
    small_ref[...] = small_in[...]
    small_ref[0:1, :] = small_in[0:1, :] + term


def swap_dp(values_in, bit, n_dp):
    return lax.ppermute(values_in, "dp", [(i, i ^ (1 << bit)) for i in range(n_dp)])


def swap_mp(values_in):
    return lax.ppermute(values_in, "mp", [(0, 1), (1, 0)])


def halving(parts, order, n_dp, index):
    bits = n_dp.bit_length() - 1
    left = list(range(bits - 1, -1, -1))
    shape = parts.shape[1:]
    held = parts.reshape((2,) * bits + shape)
    for step, bit in enumerate(order):
        at = left.index(bit)
        upper = ((index >> bit) & 1) == 1
        low = lax.index_in_dim(held, 0, at, keepdims=False)
        high = lax.index_in_dim(held, 1, at, keepdims=False)
        keep, send = jnp.where(upper, high, low), jnp.where(upper, low, high)
        got = swap_dp(send, bit, n_dp)
        last = step == bits - 1
        total = keep.astype(F32) + got.astype(F32)
        held = total if last else total.astype(BF)
        left.remove(bit)
    return held


def orders_of(bits):
    rest = list(range(3, bits))
    if bits < 3:
        return [list(range(bits))] * 3
    return [[0, 1, 2] + rest, [1, 0, 2] + rest, [2, 0, 1] + rest]


PART = 2 * LANES
FFN_TILES = (4, 4, 2)
FFN_ORDERS = ((2, 1, 0, 3), (1, 2, 3, 0), (3, 0, 1, 2))
ATTN_ORDER = (0, 1, 2, 3)
SCHEDULE = (
    "T0", "T1", "A", "T2",
    "F0", "F1", "A0", "F2",
    "F0", "F1", "A0", "F2",
    "F0", "F1", "A0", "F2",
)
SMALL = 48


def halves(bit, outs, index):
    mine = (index >> bit) & 1
    inner = 1 << bit
    for out, which in zip(outs, (mine, 1 - mine)):
        for p in range(out.shape[0]):
            for q in range(inner):
                yield out, p, q, p * 2 * inner + which * inner + q


def stacked_copies(pairs, sems):
    flat_pairs = []
    for sources, target in pairs:
        rows = target.shape[0] // 2
        flat_pairs += [(source, target.at[pl.ds(i * rows, rows)]) for i, source in enumerate(sources)]
    copies = load_all(flat_pairs, sems)
    for copy in copies:
        copy.start()
    return [copies[i : i + 2] for i in range(0, len(copies), 2)]


def ffn_terms(bit, tiles, at, at_b, n2_df_a, n2_df_b, units_a, units_b, token, keep_ref, send_ref, left, gate_up, down, flat, sems):
    width, part = left.shape[2], down.shape[1]
    columns, columns_b = (pl.ds(start, tiles * LANES) for start in (at, at_b))
    lefts = [(n2_df_a.at[i], n2_df_b.at[i]) for i in range(2)]
    m, dg, dw = [(units_a.at[i, :, columns], units_b.at[i, :, columns_b]) for i in range(3)]
    n2, dg, dw, df, m = stacked_copies(
        [(lefts[0], left.at[0]), (dg, gate_up.at[:, :part]), (dw, gate_up.at[:, part:]), (lefts[1], left.at[1]), (m, down)], sems)
    for which, (right, needed) in enumerate(((gate_up, n2 + dg + dw), (down, df + m))):
        for copy in needed:
            copy.wait()
        terms = contract_rows(left[which], right[...])
        for at_lane in range(0, right.shape[1], LANES):
            matrix, c = divmod(at_lane // LANES, tiles)
            start = tiles * width * (2 * which + matrix) + c
            flat[pl.ds(start, width, stride=tiles), :] = terms[:, at_lane : at_lane + LANES]
    rows = keep_ref.shape[2]
    for out, p, q, shard in halves(bit, (keep_ref, send_ref), lax.axis_index("dp")):
        out[p, q] = flat[pl.ds(pl.multiple_of(shard * rows, 8), rows), :].astype(BF)


def small_rows(small, packed):
    packed[...] = jnp.zeros(packed.shape, F32)
    width = small.shape[1]
    for i in range(2 + RECURSIONS):
        for c in range(CHUNKS):
            stop = min(width, (c + 1) * LANES)
            packed[i * CHUNKS + c : i * CHUNKS + c + 1, : stop - c * LANES] = small[i : i + 1, c * LANES : stop]
    return packed[...]


def split_small(small, ref, start):
    high = small.astype(BF)
    ref[start : start + SMALL, :] = high
    ref[start + SMALL : start + 2 * SMALL, :] = (small - high.astype(F32)).astype(BF)


def rounded_small(small):
    high = small.astype(BF)
    return high.astype(F32) + (small - high.astype(F32)).astype(BF).astype(F32)


def joined_small(ref, start):
    return ref[start : start + SMALL, :].astype(F32) + ref[start + SMALL : start + 2 * SMALL, :].astype(F32)


def attn_terms(bit, depth, n1_a, n1_b, du_a, du_b, o_da_a, o_da_b, small_a, small_b, token,
               keep, send, small_out, left, du_rows, da_rows, turned, own, terms, flat, packed, sems):
    base, count = 0, own.shape[0] // 2
    lower = lane_of(count) < HEAD_DIM
    core = lax.axis_index("mp")
    n1, du, o, da = stacked_copies(
        [((n1_a, n1_b), left.at[0]), ((du_a, du_b), du_rows), ((o_da_a.at[0], o_da_b.at[0]), left.at[1]),
         ((o_da_a.at[1], o_da_b.at[1]), da_rows)], sems)
    for which, (right, needed) in enumerate(((du_rows, n1 + du), (da_rows, o + da))):
        for copy in needed:
            copy.wait()
        columns = right.shape[1]
        half = columns // LANES
        turned[...] = left[which].T
        group = depth * LANES // columns
        for i in range(own.shape[0] // group):
            own[i * group : (i + 1) * group, :] = turned[pl.ds(pl.multiple_of((2 * i + core) * group, 16), group), :]
        for start in range(0, columns, PART):
            stop = min(columns, start + PART)
            block = plain(own[...], right[:, start:stop])
            if stop - start < PART:
                block = jnp.concatenate([block, jnp.zeros((2 * count, PART - (stop - start)), F32)], axis=1)
            for part in range(0, stop - start, LANES):
                terms[(start + part) // LANES] = block[:, part : part + LANES]
        step = 2 * columns // LANES
        after = first_odd = None
        for c in range(half + 1):
            even = terms[c, pl.ds(0, count, stride=2), :]
            odd = other_half(terms[c, pl.ds(1, count, stride=2), :])
            if c < half:
                flat[pl.ds(base + c, count, stride=step), :] = even
            else:
                flat[pl.ds(base + c, count, stride=step), :] = jnp.where(lower, even, first_odd)
            if c == 0:
                first_odd = odd
            else:
                flat[pl.ds(base + half + c, count, stride=step), :] = jnp.where(lower, after, odd)
            after = odd
        base += 2 * count * columns // LANES
    index = lax.axis_index("dp")
    total = rounded_small(small_rows(small_a, packed.at[0])) + rounded_small(small_rows(small_b, packed.at[1]))
    small_out[...] = total
    outer, inner, rows = keep.shape[:3]
    split_small(total, send, outer * inner * rows)

    def rows_of_shard(shard):
        start = pl.multiple_of(shard * depth, 8)
        return flat[pl.ds(start, rows), :].astype(BF)

    mine = (index >> bit) & 1
    for p in range(outer):
        for q in range(inner):
            shard = 2 * p * inner + q
            keep[p, q] = rows_of_shard(shard + mine * inner)
            at = (p * inner + q) * rows
            send[at : at + rows, :] = rows_of_shard(shard + (1 - mine) * inner)


def fold(bit, kept, got, token, keep, send):
    mine = (lax.axis_index("dp") >> bit) & 1
    for p in range(kept.shape[0]):
        for q in range(kept.shape[2]):
            for out, which in ((keep, mine), (send, 1 - mine)):
                out[p, q] = (kept[p, which, q].astype(F32) + got[p, which, q].astype(F32)).astype(BF)


def fold_small(bit, kept, got, small, token, keep, send, small_out):
    mine = (lax.axis_index("dp") >> bit) & 1
    outer, _, inner, rows, _ = kept.shape
    for p in range(outer):
        for q in range(inner):
            totals = []
            for which in (mine, 1 - mine):
                start = pl.multiple_of(((2 * p + which) * inner + q) * rows, 16)
                totals.append((kept[p, which, q].astype(F32) + got[pl.ds(start, rows), :].astype(F32)).astype(BF))
            keep[p, q] = totals[0]
            at = (p * inner + q) * rows
            send[at : at + rows, :] = totals[1]
    total = rounded_small(small[...]) + joined_small(got, 2 * outer * inner * rows)
    small_out[...] = total
    split_small(total, send, outer * inner * rows)


def finish_streams(tiles, *refs):
    count = len(tiles)
    feeds, refs = refs[: 2 * count], refs[2 * count :]
    attn, refs = refs[:2], refs[2:]
    small, ffn_out, attn_out, one_out, two_out, router_out, flat, packed = refs
    every = sum(tiles)
    rows = ffn_out.shape[0] // every
    base = 0
    for i, wide in enumerate(tiles):
        flat[: rows * wide, :] = feeds[2 * i][...].astype(F32) + feeds[2 * i + 1][...].astype(F32)
        for c in range(wide):
            ffn_out[pl.ds(base + c, rows, stride=every), :] = flat[pl.ds(c, rows, stride=wide), :]
        base += wide
    padded = attn[0].shape[0]
    both = attn[0][...].astype(F32) + attn[1][:padded, :].astype(F32)
    attn_out[...] = both[: attn_out.shape[0]]
    total = rounded_small(small[...]) + joined_small(attn[1], padded)
    packed[...] = total
    width = one_out.shape[1]
    outs = [(one_out, 0), (two_out, 0), *[(router_out, i) for i in range(RECURSIONS)]]
    for i, (out, row) in enumerate(outs):
        for c in range(CHUNKS):
            stop = min(width, (c + 1) * LANES)
            out[row : row + 1, c * LANES : stop] = packed[i * CHUNKS + c : i * CHUNKS + c + 1, : stop - c * LANES]


class Stream:
    def __init__(self, order, bits):
        self.order, self.left, self.done = order, list(range(bits - 1, -1, -1)), 0
        self.kept = self.got = None

    def shape_for(self, array):
        at = self.left.index(self.order[self.done])
        rows, lanes = array.shape[-2:]
        return (1 << at, 2, 1 << (len(self.left) - 1 - at), rows, lanes)

    def sent(self, kept, send, n_dp):
        bit = self.order[self.done]
        self.kept, self.got = kept, swap_dp(send, bit, n_dp)
        self.left.remove(bit)
        self.done += 1


def on_device(
    hidden_in,
    sel_one,
    sel_two,
    sel_three,
    segment_ids,
    pad_mask,
    qkv_weight,
    out_weight,
    gate_weight,
    up_weight,
    down_weight,
    norm_one,
    norm_two,
    router_weight,
    d_hidden,
):
    seq_len, width = hidden_in.shape
    n_dp, n_mp = lax.axis_size("dp"), lax.axis_size("mp")
    dp_index, mp_index = lax.axis_index("dp"), lax.axis_index("mp")
    cosine, sine = rotary_tables(seq_len)
    weights = [(gate_weight, up_weight, down_weight)]
    weights.append(tuple(swap_mp(w) for w in weights[0]))
    gain_one, gain_two = norm_one.reshape(1, width), norm_two.reshape(1, width)
    padded = CHUNKS * LANES
    units = gate_weight.shape[1]
    feed_weights = (*weights[0], *weights[1])

    def shape(*dims, dtype=BF):
        return jax.ShapeDtypeStruct(dims, dtype)

    def whole(*dims, **kw):
        return pl.BlockSpec(dims, lambda *_: (0,) * len(dims), **kw)

    anywhere = pl.BlockSpec(memory_space=pl.ANY)
    one = pl.Buffered(1)
    stack = RECURSIONS, seq_len
    heads = (2 * KV_HEADS, seq_len, LANES)
    square = (HEADS, seq_len, seq_len)
    n1, q, kz, vz, p, o_da, attn, n2, bias, active, near, slope_first, silu_first, f_first = pl.pallas_call(
        first_attention,
        grid=(1,),
        in_specs=[
            whole(seq_len, width), *[whole(*ref.shape) for ref in (sel_one, sel_two, sel_three, segment_ids, pad_mask)],
            whole(seq_len, LANES), whole(seq_len, LANES), whole(1, width), whole(1, width), whole(*qkv_weight.shape), whole(*out_weight.shape),
            *[anywhere] * 3,
        ],
        out_specs=[
            whole(1, seq_len, width), whole(seq_len, padded), whole(*heads), whole(*heads), whole(*square),
            whole(1, 1, seq_len, width), whole(seq_len, width), whole(seq_len, width), whole(RECURSIONS, seq_len, seq_len), whole(*stack, 1),
            whole(1, 1, seq_len, units), whole(seq_len, units), whole(seq_len, units), whole(seq_len, width),
        ],
        out_shape=[
            shape(*stack, width), shape(seq_len, padded), shape(*heads), shape(*heads), shape(*square),
            shape(2, *stack, width), shape(seq_len, width, dtype=F32), shape(seq_len, width),
            shape(*stack, seq_len, dtype=F32), shape(*stack, 1, dtype=F32),
            shape(3, *stack, units), shape(seq_len, units), shape(seq_len, units), shape(seq_len, width, dtype=F32),
        ],
        scratch_shapes=[*[pltpu.VMEM(w.shape, BF) for w in weights[0]], pltpu.SemaphoreType.DMA((3,))],
        compiler_params=pltpu.CompilerParams(vmem_limit_bytes=VMEM_MIB * MIB),
        cost_estimate=pl.CostEstimate(flops=2 * 10**9, bytes_accessed=12 * 10**6, transcendentals=600000),
        name="first_attention",
    )(hidden_in, sel_one, sel_two, sel_three, segment_ids, pad_mask, cosine, sine, gain_one, gain_two, qkv_weight, out_weight,
      *weights[0])
    attention_0 = (q, kz, vz, p)
    wide = qkv_weight.shape[1]
    row = (seq_len, width)
    kept = RECURSIONS - 1
    first_part = FFN_TILES[0] * LANES
    vm = pltpu.VMEM
    results = pl.pallas_call(
        all_steps,
        grid=(1,),
        in_specs=[
            whole(RECURSIONS, seq_len, seq_len), whole(RECURSIONS, seq_len, 1), whole(RECURSIONS, width),
            whole(seq_len, LANES), whole(seq_len, LANES), whole(1, width), whole(1, width), *[anywhere] * 18,
        ],
        out_specs=[*[anywhere] * 8, whole(*row), whole(*row), whole(8, width)],
        out_shape=[
            shape(*stack, width), *[shape(2, *stack, width)] * 2, shape(3, *stack, units), shape(3, *stack, first_part), shape(3, *stack, units - first_part), shape(*stack, wide),
            *[shape(*row, dtype=F32)] * 3, shape(8, width, dtype=F32),
        ],
        scratch_shapes=[
            *[vm(w.shape, BF) for w in (qkv_weight, out_weight, *feed_weights)],
            vm((RECURSIONS + 1, *row), F32), vm((RECURSIONS, *row), F32), vm((RECURSIONS, *row), BF),
            *[vm((*stack, units), BF)] * 4, vm((kept, seq_len, padded), BF), vm((kept, *heads), BF), vm((kept, *heads), BF),
            vm((kept, *square), BF), *[vm(row, BF)] * 3, *[vm((seq_len, units), BF)] * 2, vm(row, BF), *[vm((seq_len, units), BF)] * 4,
            vm(row, BF), vm((seq_len, wide), BF), vm(row, F32), vm(row, F32), vm((seq_len, padded), BF),
            pltpu.SemaphoreType.DMA((15,)), pltpu.SemaphoreType.DMA((16,)),
        ],
        input_output_aliases={14: 0, 15: 1, 16: 3},
        compiler_params=pltpu.CompilerParams(vmem_limit_bytes=VMEM_MIB * MIB),
        cost_estimate=pl.CostEstimate(flops=23 * 10**9, bytes_accessed=50 * 10**6, transcendentals=4 * 10**6),
        name="all_steps",
    )(bias, active, router_weight, cosine, sine, gain_one, gain_two, hidden_in, d_hidden, attn, n2,
      slope_first, silu_first, f_first, n1, o_da, near,
      qkv_weight, out_weight, *feed_weights)
    n1, o_da, n2_df, near, far, late, du, state, base, grad_state, small = results

    def run_last(token):
        return pl.pallas_call(
            last_attention,
            grid=(1,),
            in_specs=[
                whole(1, seq_len, 1), whole(seq_len, LANES), whole(seq_len, LANES), whole(1, width),
                whole(seq_len, padded), whole(*heads), whole(*heads), whole(*square),
                pl.BlockSpec((1, 1, seq_len, width), lambda i: (1, 0, 0, 0)), whole(8, width), whole(*out_weight.shape), *[anywhere] * 6,
            ],
            out_specs=[whole(1, seq_len, qkv_weight.shape[1]), whole(seq_len, width), whole(8, width)],
            out_shape=[shape(*stack, qkv_weight.shape[1]), shape(seq_len, width, dtype=F32), shape(8, width, dtype=F32)],
            scratch_shapes=[
                pltpu.VMEM((seq_len, padded), BF), *[pltpu.VMEM((seq_len, width), F32)] * 4,
                pltpu.VMEM(qkv_weight.shape, BF), pltpu.SemaphoreType.DMA((4,)),
            ],
            input_output_aliases={15: 0},
            compiler_params=pltpu.CompilerParams(vmem_limit_bytes=VMEM_MIB * MIB),
            cost_estimate=pl.CostEstimate(flops=1, bytes_accessed=1, transcendentals=0),
            name="last_attention",
        )(active, cosine, sine, gain_one, *attention_0, o_da, small, out_weight, hidden_in, base, grad_state, qkv_weight, du, token)

    def rows_of(stacked):
        return stacked.reshape(*stacked.shape[:-3], -1, stacked.shape[-1])

    bits = n_dp.bit_length() - 1
    share = (qkv_weight.size + out_weight.size) // (n_dp * n_mp)
    if bits == 4 and 3 * width % n_dp == 0 and units == sum(FFN_TILES) * LANES and share % (16 * qkv_weight.shape[1]) == share % (16 * width) == 0:
        n2_df_rows = [rows_of(t) for t in (n2_df, swap_mp(n2_df))]
        near, far_b = rows_of(near), rows_of(swap_mp(far))
        n1_b = rows_of(swap_mp(n1))
        streams = [Stream(order, bits) for order in FFN_ORDERS]
        attn_stream = Stream(ATTN_ORDER, bits)
        depth = share // LANES
        tiled = -(-depth // 16) * 16
        common = dict(
            grid=(1,),
            compiler_params=pltpu.CompilerParams(vmem_limit_bytes=VMEM_MIB * MIB),
            cost_estimate=pl.CostEstimate(flops=1, bytes_accessed=1, transcendentals=0),
        )

        def wholes(arrays):
            return [whole(*t.shape) for t in arrays]

        def terms_of(j, token):
            stream, tiles = streams[j], FFN_TILES[j]
            at = sum(FFN_TILES[:j]) * LANES
            factors = (*n2_df_rows, near, far_b if j == 0 else late_b)
            bit = stream.order[0]
            dims = (1 << (bits - 1 - bit), 1 << bit, 3 * width // n_dp * tiles, LANES)
            both = 2 * RECURSIONS * seq_len
            keep, send = pl.pallas_call(
                functools.partial(ffn_terms, bit, tiles, at, 0 if j == 0 else at - first_part),
                in_specs=[anywhere] * (len(factors) + 1),
                out_specs=[whole(*dims)] * 2,
                out_shape=[shape(*dims)] * 2,
                scratch_shapes=[pltpu.VMEM((2, both, width), BF), *[pltpu.VMEM((both, n * tiles * LANES), BF) for n in (2, 1)],
                                pltpu.VMEM((3 * width * tiles, LANES), F32), pltpu.SemaphoreType.DMA((10,))],
                name=f"ffn_terms_{j}",
                **common,
            )(*factors, token)
            stream.sent(keep, send, n_dp)
            return keep

        def fold_stream(stream, token, small_own=None):
            bit = stream.order[stream.done]
            dims = stream.shape_for(stream.kept)
            kept = stream.kept.reshape(dims)
            held = (dims[0], *dims[2:])
            if small_own is None:
                operands = (kept, stream.got.reshape(dims))
                outs = (shape(*held), shape(*held))
            else:
                operands = (kept, stream.got, small_own)
                outs = (shape(*held), shape(dims[0] * dims[2] * dims[3] + 2 * SMALL, LANES), shape(SMALL, LANES, dtype=F32))
            results = pl.pallas_call(
                functools.partial(fold if small_own is None else fold_small, bit),
                in_specs=[*wholes(operands), anywhere],
                out_specs=wholes(outs),
                out_shape=outs,
                name="fold_terms",
                **common,
            )(*operands, token)
            stream.sent(results[0], results[1], n_dp)
            return results

        du, grad_state, small = run_last(small)
        late, du, small = lax.optimization_barrier((late, du, small))
        late_b, du_b = rows_of(swap_mp(late)), rows_of(swap_mp(du))
        token = small
        for item in SCHEDULE:
            if item[0] == "T":
                token = terms_of(int(item[1:]), token)
                if item == "T0":
                    o_da, small, token = lax.optimization_barrier((o_da, small, token))
                    o_da_b, small_b = rows_of(swap_mp(o_da)), swap_mp(small)
            elif item[0] == "F":
                token = fold_stream(streams[int(item[1:])], token)[0]
            elif item == "A":
                bit = attn_stream.order[0]
                dims = (1 << (bits - 1 - bit), 1 << bit, tiled, LANES)
                operands = (rows_of(n1), n1_b, rows_of(du), du_b, rows_of(o_da), o_da_b, small, small_b)
                outs = (shape(*dims), shape(n_dp // 2 * tiled + 2 * SMALL, LANES), shape(SMALL, LANES, dtype=F32))
                keep, send, small_own = pl.pallas_call(
                    functools.partial(attn_terms, bit, depth),
                    in_specs=[*[anywhere] * 6, *wholes(operands[6:]), anywhere],
                    out_specs=wholes(outs),
                    out_shape=outs,
                    scratch_shapes=[pltpu.VMEM((2, 2 * RECURSIONS * seq_len, width), BF),
                                    *[pltpu.VMEM((2 * RECURSIONS * seq_len, t.shape[-1]), BF) for t in (du, o_da)],
                                    pltpu.VMEM((width, 2 * RECURSIONS * seq_len), BF),
                                    pltpu.VMEM((width // 2, 2 * RECURSIONS * seq_len), BF),
                                    pltpu.VMEM((-(-du.shape[-1] // PART) * 2, width // 2, LANES), F32),
                                    pltpu.VMEM((n_dp * depth + tiled - depth, LANES), F32), pltpu.VMEM((2, SMALL, LANES), F32),
                                    pltpu.SemaphoreType.DMA((8,))],
                    name="attn_terms",
                    **common,
                )(*operands, token)
                attn_stream.sent(keep, send, n_dp)
                token = small_own
            else:
                token, _, small_own = fold_stream(attn_stream, token, small_own)
        ends = [t.reshape(t.shape[-2:]) for stream in (*streams, attn_stream) for t in (stream.kept, stream.got)]
        outs = (shape(3 * width // n_dp * sum(FFN_TILES), LANES, dtype=F32), shape(depth, LANES, dtype=F32),
                shape(1, width, dtype=F32), shape(1, width, dtype=F32), shape(RECURSIONS, width, dtype=F32))
        ffn_flat, attn_flat, one, two, router = pl.pallas_call(
            functools.partial(finish_streams, FFN_TILES),
            in_specs=wholes((*ends, small_own)),
            out_specs=wholes(outs),
            out_shape=outs,
            scratch_shapes=[pltpu.VMEM((3 * width // n_dp * max(FFN_TILES), LANES), F32), pltpu.VMEM((SMALL, LANES), F32)],
            name="finish_streams",
            **common,
        )(*ends, small_own)
        return (state, grad_state, attn_flat.reshape(-1), ffn_flat.reshape(1, -1), one.reshape(-1), two.reshape(-1), router)

    du, grad_state, small = run_last(small)
    two, feed = rows_of(n2_df)
    o, d_attn = rows_of(o_da)
    far = jnp.concatenate([far, late], axis=-1)
    sides = [[t[i] for i in (1, 2, 0)] for t in (rows_of(near), rows_of(far))]

    def side_terms(side, columns):
        return jnp.concatenate(
            [
                contract_rows(left, sides[side][which][:, columns]).astype(BF)
                for which, left in enumerate((two, two, feed))
            ],
            axis=0,
        )

    orders = orders_of(bits)
    if 3 * width % n_dp == 0 and units % 1280 == 0:
        fifth = units // 5
        streams = [(orders[i], slice(j * fifth, (j + 1) * fifth)) for i, j in ((0, 0), (1, 1), (2, 2), (0, 3), (1, 4))]
        done = []
        for order, columns in streams:
            terms = side_terms(0, columns).astype(F32) + swap_mp(side_terms(1, columns)).astype(F32)
            done.append(halving(terms.astype(BF).reshape(n_dp, 3 * width // n_dp, fifth), order, n_dp, dp_index))
        ffn_flat = jnp.concatenate(done, axis=1).reshape(1, -1)
    else:
        terms = side_terms(0, slice(None)).astype(F32) + swap_mp(side_terms(1, slice(None))).astype(F32)
        terms = terms.astype(BF).reshape(n_dp, 3 * width * units // n_dp // 128, 128)
        ffn_flat = halving(terms, orders[0], n_dp, dp_index).reshape(1, -1)

    grad_qkv = contract_rows(rows_of(n1), rows_of(du)).astype(BF)
    grad_out = contract_rows(o, d_attn).astype(BF)
    attn = jnp.concatenate([grad_qkv.reshape(-1), grad_out.reshape(-1)]).reshape(n_dp, 2, share // 128, 128)
    keep = jnp.where(mp_index == 0, attn[:, 0], attn[:, 1])
    send = jnp.where(mp_index == 0, attn[:, 1], attn[:, 0])
    attn = (keep.astype(F32) + swap_mp(send).astype(F32)).astype(BF)
    cuts = [0, (share // 128) // 24 * 8, (share // 128) // 12 * 8, share // 128]
    attn_flat = jnp.concatenate(
        [halving(attn[:, a:b], order, n_dp, dp_index) for a, b, order in zip(cuts, cuts[1:], orders)], axis=0
    ).reshape(-1)

    small = small + swap_mp(small)
    for bit in range(bits):
        small = small + swap_dp(small, bit, n_dp)
    return (state, grad_state, attn_flat, ffn_flat, small[0], small[1], small[2 : 2 + RECURSIONS])


def solution(mesh):
    both = P(("dp", "mp"), None)
    in_specs = (
        both,
        both,
        both,
        both,
        both,
        both,
        P(),
        P(),
        P(None, "mp"),
        P(None, "mp"),
        P(None, "mp"),
        P(),
        P(),
        P(),
        both,
    )
    out_specs = (both, both, P(("dp", "mp")), P("mp", "dp"), P(), P(), P())
    return jax.shard_map(
        on_device, mesh=mesh, in_specs=in_specs, out_specs=out_specs, check_vma=False
    )
```

```python
import functools
import math

import jax
import jax.numpy as jnp
import numpy as np
from jax import lax
from jax.experimental import pallas as pl
from jax.experimental.pallas import tpu as pltpu
from jax.sharding import PartitionSpec as P

HEADS = 15
KV_HEADS = 5
HEAD_DIM = 64
RECURSIONS = 3
GROUPS = HEADS // KV_HEADS
EPS = 1e-05
BF = jnp.bfloat16
F32 = jnp.float32


LANES = 128
CHUNKS = -(-HEADS * HEAD_DIM // LANES)
ROWS = 192
BLOCK = 256
MIB = 1 << 20
VMEM_BYTES = 64 * MIB - 65536


def rotary_tables(seq_len):
    half = HEAD_DIM // 2
    frequency = np.float32(100000.0) ** (
        np.float32(-2.0) * np.arange(half, dtype=np.float32) / np.float32(HEAD_DIM)
    )
    angles = np.arange(seq_len, dtype=np.float32)[:, None] * frequency.astype(np.float32)
    cosine, sine = np.cos(angles), np.sin(angles)
    return (
        jnp.asarray(np.concatenate([cosine] * 4, axis=1), F32),
        jnp.asarray(np.concatenate([-sine, sine] * 2, axis=1), F32),
    )


def contract_rows(left, right):
    return lax.dot_general(left, right, (((0,), (0,)), ((), ())), preferred_element_type=F32)


def contract_last(left, right):
    return lax.dot_general(left, right, (((1,), (1,)), ((), ())), preferred_element_type=F32)


def plain(left, right):
    return jnp.dot(left, right, preferred_element_type=F32)


def inverse_rms(rows):
    return lax.rsqrt(jnp.mean(rows * rows, axis=-1, keepdims=True) + EPS)


def norm_back(rows, gain, d_out):
    inv = inverse_rms(rows)
    scaled = d_out * gain
    inner = jnp.mean(scaled * rows, axis=-1, keepdims=True)
    d_rows = inv * scaled - rows * (inv * inv * inv * inner)
    return d_rows, jnp.sum(d_out * rows * inv, axis=0, keepdims=True)


def lane_of(rows):
    return lax.broadcasted_iota(jnp.int32, (rows, LANES), 1)


def swapped(chunk):
    first = lane_of(chunk.shape[0]) % HEAD_DIM < HEAD_DIM // 2
    return jnp.where(first, pltpu.roll(chunk, LANES - 32, 1), pltpu.roll(chunk, 32, 1))


def other_half(chunk):
    return pltpu.roll(chunk, HEAD_DIM, 1)


def over_rows(count, body):
    def lap(i, carry):
        body(pl.ds(pl.multiple_of(i * ROWS, ROWS), ROWS))
        return carry

    lax.fori_loop(0, count // ROWS, lap, 0)


def attention_forward(x_ref, bias_ref, cos_ref, sin_ref, gain, qkv_w, n1_ref, q_ref, kz_ref, vz_ref, p_ref, o_ref):
    seq_len, width = x_ref.shape
    scale = 1.0 / math.sqrt(HEAD_DIM)

    def norm(rows):
        x = x_ref[rows, :]
        n1_ref[rows, :] = (x * inverse_rms(x) * gain).astype(BF)

    over_rows(seq_len, norm)
    lower = lane_of(seq_len) < HEAD_DIM
    n1 = n1_ref[...]

    def spread(ref, head, chunk, upper):
        flipped = other_half(chunk)
        here, there = (flipped, chunk) if upper else (chunk, flipped)
        ref[2 * head] = jnp.where(lower, here, 0.0).astype(BF)
        ref[2 * head + 1] = jnp.where(lower, 0.0, there).astype(BF)

    columns = qkv_w.shape[1]
    for start in range(0, columns, 2 * LANES):
        wide = plain(n1, qkv_w[:, start : min(start + 2 * LANES, columns)])
        for part in range(0, wide.shape[1], LANES):
            chunk = wide[:, part : part + LANES]
            if chunk.shape[1] < LANES:
                chunk = jnp.concatenate([chunk, jnp.zeros_like(chunk)], axis=1)
            at = (start + part) // LANES
            heads = (2 * at, 2 * at + 1)
            if heads[0] < HEADS + KV_HEADS:
                chunk = chunk * cos_ref[...] + swapped(chunk) * sin_ref[...]
                if heads[0] < HEADS:
                    q_ref[:, at * LANES : (at + 1) * LANES] = chunk.astype(BF)
            for upper, head in enumerate(heads):
                if HEADS <= head < HEADS + KV_HEADS:
                    spread(kz_ref, head - HEADS, chunk, upper)
                elif HEADS + KV_HEADS <= head < HEADS + 2 * KV_HEADS:
                    spread(vz_ref, head - HEADS - KV_HEADS, chunk, upper)

    for at in range(CHUNKS):
        query = q_ref[:, at * LANES : (at + 1) * LANES]
        total = None
        for upper in range(2):
            head = 2 * at + upper
            if head < HEADS:
                key = 2 * (head // GROUPS) + upper
                scores = contract_last(query, kz_ref[key]) * scale + bias_ref[...]
                top = jnp.max(scores, axis=-1, keepdims=True)
                exponent = jnp.exp(scores - top)
                share = pl.reciprocal(jnp.sum(exponent, axis=-1, keepdims=True))
                attend = (exponent * share).astype(BF)
                p_ref[head] = attend
                mixed = plain(attend, vz_ref[key])
                total = mixed if total is None else total + mixed
        stop = min(width, (at + 1) * LANES)
        o_ref[:, at * LANES : stop] = total[:, : stop - at * LANES].astype(BF)


def attention_out(x_ref, o_ref, out_w, gain, attn_ref, n2_ref):
    attn_ref[...] = plain(o_ref[...], out_w[...])

    def norm(rows):
        after = x_ref[rows, :] + attn_ref[rows, :]
        n2_ref[rows, :] = (after * inverse_rms(after) * gain).astype(BF)

    over_rows(x_ref.shape[0], norm)


def feed_side(n2_ref, weights, results, ready):
    n2 = n2_ref[...]
    gate_w, up_w, down_w = weights
    m_ref, slope_ref, silu_ref = results
    ready(0, 1)
    for start in range(0, gate_w.shape[1], BLOCK):
        at = slice(start, start + BLOCK)
        g, u = plain(n2, gate_w[:, at]), plain(n2, up_w[:, at])
        s = jax.nn.sigmoid(g)
        silu = g * s
        m_ref[:, at] = (silu * u).astype(BF)
        slope_ref[:, at] = (u * s * (1.0 + g * (1.0 - s))).astype(BF)
        silu_ref[:, at] = silu.astype(BF)
    ready(2)
    return contract_last(m_ref[...], down_w[...])


def feed_backward(df_ref, sides, d_two_ref, ready):
    d_feed = df_ref[...]
    for side, (gate_w, up_w, down_w, slope_ref, silu_ref, dg_ref, du_ref) in enumerate(sides):
        ready(3 * side)
        for start in range(0, gate_w.shape[1], BLOCK):
            at = slice(start, start + BLOCK)
            d_hidden = plain(d_feed, down_w[:, at])
            dg_ref[:, at] = (d_hidden * slope_ref[:, at].astype(F32)).astype(BF)
            du_ref[:, at] = (d_hidden * silu_ref[:, at].astype(F32)).astype(BF)
        ready(3 * side + 1, 3 * side + 2)
        part = contract_last(dg_ref[...], gate_w[...]) + contract_last(du_ref[...], up_w[...])
        d_two_ref[...] = part if side == 0 else d_two_ref[...] + part


def attention_backward(d_attn_ref, out_w, qkv_w, cos_ref, sin_ref, q_ref, kz_ref, vz_ref, p_ref, do_ref, du_ref):
    seq_len, width = d_attn_ref.shape
    scale = 1.0 / math.sqrt(HEAD_DIM)
    do_ref[:, :width] = contract_last(d_attn_ref[...], out_w[...]).astype(BF)
    do_ref[:, width:] = jnp.zeros((seq_len, do_ref.shape[1] - width), BF)
    lower = lane_of(seq_len) < HEAD_DIM
    cosine, sine = cos_ref[...], sin_ref[...]

    def back(chunk):
        chunk = chunk * scale
        return chunk * cosine - swapped(chunk) * sine

    waiting, d_k, d_v = None, {}, {}
    for at in range(CHUNKS):
        query, d_mixed = (ref[:, at * LANES : (at + 1) * LANES] for ref in (q_ref, do_ref))
        query_t, d_mixed_t = query.T, d_mixed.T
        d_query = None
        for upper in range(2):
            head = 2 * at + upper
            if head >= HEADS:
                continue
            group = head // GROUPS
            key = 2 * group + upper
            rows = slice(upper * HEAD_DIM, (upper + 1) * HEAD_DIM)
            attend = p_ref[head]
            d_attend = contract_last(d_mixed, vz_ref[key])
            soft = attend.astype(F32)
            weighted = soft * d_attend
            inner = jnp.sum(weighted, axis=-1, keepdims=True)
            d_scores = (weighted - soft * inner).astype(BF)
            part = plain(d_scores, kz_ref[key])
            d_query = part if d_query is None else d_query + part
            for store, term in ((d_k, plain(query_t[rows], d_scores)), (d_v, plain(d_mixed_t[rows], attend))):
                store[group] = term if group not in store else store[group] + term
        if at < CHUNKS - 1:
            du_ref[:, at * LANES : (at + 1) * LANES] = back(d_query).astype(BF)
        else:
            waiting = d_query

    def two_heads(store, first, second):
        return jnp.concatenate([store[first], store[second]], axis=0).T

    tail = jnp.where(lower, waiting, two_heads(d_k, 0, 0))
    du_ref[:, (CHUNKS - 1) * LANES : CHUNKS * LANES] = back(tail).astype(BF)
    for i in range(2):
        at = CHUNKS + i
        du_ref[:, at * LANES : (at + 1) * LANES] = back(two_heads(d_k, 1 + 2 * i, 2 + 2 * i)).astype(BF)
        at = CHUNKS + 2 + i
        du_ref[:, at * LANES : (at + 1) * LANES] = two_heads(d_v, 2 * i, 2 * i + 1).astype(BF)
    at = CHUNKS + 4
    du_ref[:, at * LANES :] = two_heads(d_v, 4, 4)[:, : du_ref.shape[1] - at * LANES].astype(BF)


def router_gate(x, router_row):
    return jax.nn.sigmoid(jnp.sum(x * router_row, axis=-1, keepdims=True))


def masks(select_refs, segment_ref, pad_ref, bias_ref, active_ref):
    seq_len = segment_ref.shape[1]
    square = (seq_len, seq_len)
    query, key = (lax.broadcasted_iota(jnp.int32, square, axis) for axis in (0, 1))
    diagonal = query == key
    segment = segment_ref[...].astype(F32)
    own = jnp.sum(jnp.where(diagonal, segment, 0.0), axis=1, keepdims=True)
    near = (key <= query) & (segment == own)
    real = pad_ref[...] == 1
    for recursion, ref in enumerate(select_refs):
        place = lax.broadcasted_iota(jnp.int32, (seq_len, ref.shape[1]), 0)
        active = jnp.max(jnp.where(ref[...] == place, 1.0, 0.0), axis=1, keepdims=True)
        active_ref[recursion] = active
        along = jnp.sum(jnp.where(diagonal, active, 0.0), axis=0, keepdims=True)
        usable = (along > 0.0) & real
        bias_ref[recursion] = jnp.where(near & (usable | diagonal), 0.0, -1e30)


def first_attention(x_ref, sel_one, sel_two, sel_three, segment_ref, pad_ref, cos_ref, sin_ref, gain_one, gain_two, qkv_w, out_w,
                    gate_hbm, up_hbm, down_hbm, n1_ref, q_ref, kz_ref, vz_ref, p_ref, o_ref, attn_ref, n2_ref, bias_ref, active_ref,
                    m_ref, slope_ref, silu_ref, f_ref, gate_w, up_w, down_w, sems):
    copies = load_all([(gate_hbm, gate_w), (up_hbm, up_w), (down_hbm, down_w)], sems)
    for copy in copies:
        copy.start()
    n1, o = n1_ref.at[0], o_ref.at[0, 0]
    masks((sel_one, sel_two, sel_three), segment_ref, pad_ref, bias_ref, active_ref)
    attention_forward(x_ref, bias_ref.at[0], cos_ref, sin_ref, gain_one[...], qkv_w, n1, q_ref, kz_ref, vz_ref, p_ref, o)
    attention_out(x_ref, o, out_w, gain_two[...], attn_ref, n2_ref)

    def ready(*which):
        for i in which:
            copies[i].wait()

    f_ref[...] = feed_side(n2_ref, (gate_w, up_w, down_w), (m_ref.at[0, 0], slope_ref, silu_ref), ready)


def load_all(pairs, sems):
    return [pltpu.make_async_copy(src, dst, sems.at[i]) for i, (src, dst) in enumerate(pairs)]


def waits_at(condition, copies):
    def ready(*which):
        @pl.when(condition)
        def _():
            for i in which:
                copies[i].wait()

    return ready


def finish_attention_backward(x_ref, gain, active_ref, du_ref, qkv_w, base, state, total, out_ref):
    total[...] = contract_last(du_ref[...], qkv_w[...])
    terms = jnp.zeros((1, state.shape[1]), F32)

    def lap(i, terms):
        rows = pl.ds(pl.multiple_of(i * ROWS, ROWS), ROWS)
        d_rows, term = norm_back(x_ref[rows, :], gain, total[rows, :])
        new = jnp.where(active_ref[rows, :] > 0, base[rows, :] + d_rows, state[rows, :])
        out_ref[rows, :] = new
        return terms + term

    return lax.fori_loop(0, state.shape[0] // ROWS, lap, terms)


def all_steps(bias_ref, active_ref, router_ref, cos_ref, sin_ref, gain_one, gain_two,
              hidden_hbm, d_hidden_hbm, attn0_hbm, n20_hbm, slope_hbm, silu_hbm, f_hbm, n1_in, o_da_in, near_in,
              qkv_hbm, out_hbm, *rest):
    feed_hbm, rest = rest[:6], rest[6:]
    (n1_out, o_da_out, n2_df_out, near_out, far_out, late_out, du_out, final_out, base_ref, state_ref, small_ref), rest = rest[:11], rest[11:]
    qkv_w, out_w, *feed_w = rest[:8]
    (xs, attns, fs, slope0, slope1, silu0, silu1, qs, kzs, vzs, ps, n1, o, n2, m0, m1, df, dg0, dg1, dw0, dw1, da, du,
     total, d_branch, do_ref, load_sems, out_sems) = rest[8:]
    width = state_ref.shape[1]
    first_part = far_out.shape[3]
    laps = state_ref.shape[0] // ROWS
    loads = load_all(
        [*zip(feed_hbm, feed_w), (qkv_hbm, qkv_w), (out_hbm, out_w),
         (n20_hbm, n2), (attn0_hbm, attns.at[0]), (hidden_hbm, xs.at[0]), (d_hidden_hbm, state_ref),
         (f_hbm, total), (slope_hbm, slope0.at[0]), (silu_hbm, silu0.at[0])], load_sems)
    for i in (8, 3, 4, 5, 12, 9, 10, 6, 7, 0, 1, 2, 13, 14, 11):
        loads[i].start()
    loads[8].wait()

    places = dict(n2=[(n2, n2_df_out.at[0])], m0=[(m0, near_out.at[0])], n1=[(n1, n1_out)], o=[(o, o_da_out.at[0])],
                  df=[(df, n2_df_out.at[1])], dg0=[(dg0, near_out.at[1])], dw0=[(dw0, near_out.at[2])],
                  da=[(da, o_da_out.at[1])], du=[(du, du_out)])
    for i, (name, ref) in enumerate((("m1", m1), ("dg1", dg1), ("dw1", dw1))):
        places[name] = [(ref.at[:, :first_part], far_out.at[i]), (ref.at[:, first_part:], late_out.at[i])]
    numbers = {}
    for pairs in places.values():
        for source, target in pairs:
            numbers[id(target)] = len(numbers)

    def leaving(recursion, names):
        return [pltpu.make_async_copy(source, target.at[recursion], out_sems.at[numbers[id(target)]])
                for name in names for source, target in places[name]]

    def start(recursion, *names):
        for copy in leaving(recursion, names):
            copy.start()

    def wait(recursion, *names):
        for copy in leaving(recursion, names):
            copy.wait()

    def forward(r, carry):
        ready, later = (waits_at(r == step, loads) for step in range(2))
        start(r, "n2")

        @pl.when(r > 0)
        def _():
            @pl.when(r > 1)
            def _():
                wait(r - 1, "m0")

            total[...] = feed_side(n2, feed_w[:3], (m0, slope0.at[r], silu0.at[r]), later)
            start(r, "m0")
            wait(r - 1, "m1")

        part = feed_side(n2, feed_w[3:], (m1, slope1.at[r], silu1.at[r]), lambda *which: ready(*[3 + i for i in which]))
        ready(12)
        total[...] = total[...] + part
        start(r, "m1")
        ready(9, 10)
        router_row = router_ref[pl.ds(r, 1), :]

        def finish(rows):
            x = xs[r, rows, :]
            f = total[rows, :].astype(BF)
            fs[r, rows, :] = f
            branch = attns[r, rows, :] + f.astype(F32)
            xs[r + 1, rows, :] = jnp.where(active_ref[r, rows, :] > 0, x + router_gate(x, router_row) * branch, x)

        over_rows(total.shape[0], finish)
        ready(6, 7)
        wait(r, "n2")

        @pl.when(r < RECURSIONS - 1)
        def _():
            @pl.when(r > 0)
            def _():
                wait(r, "n1", "o")

            attention_forward(xs.at[r + 1], bias_ref.at[r + 1], cos_ref, sin_ref, gain_one[...], qkv_w,
                              n1, qs.at[r], kzs.at[r], vzs.at[r], ps.at[r], o)
            start(r + 1, "n1", "o")
            attention_out(xs.at[r + 1], o, out_w, gain_two[...], attns.at[r + 1], n2)

        return carry

    lax.fori_loop(0, RECURSIONS, forward, 0)
    final = pltpu.make_async_copy(xs.at[RECURSIONS], final_out, out_sems.at[15])
    final.start()
    for i in (11, 13, 14):
        loads[i].wait()
    small_ref[...] = jnp.zeros(small_ref.shape, F32)

    def backward(i, carry):
        r = RECURSIONS - 1 - i
        router_row = router_ref[pl.ds(r, 1), :]

        @pl.when(i > 0)
        def _():
            wait(r + 1, "df", "dg0", "dg1", "dw0", "dw1", "da")

        def enter(lap, terms):
            rows = pl.ds(pl.multiple_of(lap * ROWS, ROWS), ROWS)
            x = xs[r, rows, :]
            d_new = jnp.where(active_ref[r, rows, :] > 0, state_ref[rows, :], 0.0)
            gate = router_gate(x, router_row)
            branch = attns[r, rows, :] + fs[r, rows, :].astype(F32)
            d_gate = jnp.sum(d_new * branch, axis=-1, keepdims=True)
            d_logit = d_gate * gate * (1.0 - gate)
            spread = gate * d_new
            d_branch[rows, :] = spread
            df[rows, :] = spread.astype(BF)
            base_ref[rows, :] = d_new + d_logit * router_row
            return terms + jnp.sum(d_logit * x, axis=0, keepdims=True)

        small_ref[pl.ds(2 + r, 1), :] = lax.fori_loop(0, laps, enter, jnp.zeros((1, width), F32))
        start(r, "df")
        feed_backward(df, ((*feed_w[:3], slope0.at[r], silu0.at[r], dg0, dw0), (*feed_w[3:], slope1.at[r], silu1.at[r], dg1, dw1)),
                      total, lambda *which: None)
        start(r, "dg0", "dg1", "dw0", "dw1")

        def leave(lap, terms):
            rows = pl.ds(pl.multiple_of(lap * ROWS, ROWS), ROWS)
            after = xs[r, rows, :] + attns[r, rows, :]
            d_after, term = norm_back(after, gain_two[...], total[rows, :].astype(BF).astype(F32))
            da[rows, :] = (d_branch[rows, :] + d_after).astype(BF)
            base_ref[rows, :] = base_ref[rows, :] + d_after
            return terms + term

        small_ref[1:2, :] = small_ref[1:2, :] + lax.fori_loop(0, laps, leave, jnp.zeros((1, width), F32))
        start(r, "da")

        @pl.when(r > 0)
        def _():
            @pl.when(i > 0)
            def _():
                wait(r + 1, "du")

            attention_backward(da, out_w, qkv_w, cos_ref, sin_ref, qs.at[r - 1], kzs.at[r - 1], vzs.at[r - 1], ps.at[r - 1], do_ref, du)
            start(r, "du")
            term = finish_attention_backward(xs.at[r], gain_one[...], active_ref.at[r], du, qkv_w, base_ref, state_ref, total, state_ref)
            small_ref[0:1, :] = small_ref[0:1, :] + term

        return carry

    lax.fori_loop(0, RECURSIONS, backward, 0)
    wait(RECURSIONS - 1, "m0", "m1", "n1", "o")
    wait(0, "df", "dg0", "dg1", "dw0", "dw1", "da")
    wait(1, "du")
    final.wait()


def last_attention(active_ref, cos_ref, sin_ref, gain_one, q_ref, kz_ref, vz_ref, p_ref, d_attn_ref, small_in, out_w,
                   x_hbm, base_hbm, state_hbm, qkv_hbm, du_in, token, du_ref, d_input_ref, small_ref,
                   do_ref, total, x, base, state, qkv_w, sems):
    copies = load_all([(qkv_hbm, qkv_w), (x_hbm, x), (base_hbm, base), (state_hbm, state)], sems)
    for copy in copies:
        copy.start()
    attention_backward(d_attn_ref.at[0, 0], out_w, qkv_w, cos_ref, sin_ref, q_ref, kz_ref, vz_ref, p_ref, do_ref, du_ref.at[0])
    for copy in copies:
        copy.wait()
    term = finish_attention_backward(x, gain_one[...], active_ref.at[0], du_ref.at[0], qkv_w, base, state, total, d_input_ref)
    small_ref[...] = small_in[...]
    small_ref[0:1, :] = small_in[0:1, :] + term


def swap_dp(values_in, bit, n_dp):
    return lax.ppermute(values_in, "dp", [(i, i ^ (1 << bit)) for i in range(n_dp)])


def swap_mp(values_in):
    return lax.ppermute(values_in, "mp", [(0, 1), (1, 0)])


def halving(parts, order, n_dp, index):
    bits = n_dp.bit_length() - 1
    left = list(range(bits - 1, -1, -1))
    shape = parts.shape[1:]
    held = parts.reshape((2,) * bits + shape)
    for step, bit in enumerate(order):
        at = left.index(bit)
        upper = ((index >> bit) & 1) == 1
        low = lax.index_in_dim(held, 0, at, keepdims=False)
        high = lax.index_in_dim(held, 1, at, keepdims=False)
        keep, send = jnp.where(upper, high, low), jnp.where(upper, low, high)
        got = swap_dp(send, bit, n_dp)
        last = step == bits - 1
        total = keep.astype(F32) + got.astype(F32)
        held = total if last else total.astype(BF)
        left.remove(bit)
    return held


def orders_of(bits):
    rest = list(range(3, bits))
    if bits < 3:
        return [list(range(bits))] * 3
    return [[0, 1, 2] + rest, [1, 0, 2] + rest, [2, 0, 1] + rest]


PART = 2 * LANES
FFN_TILES = (4, 4, 2)
FFN_ORDERS = ((2, 1, 3, 0), (1, 2, 0, 3), (2, 0, 3, 1))
ATTN_ORDER = (0, 1, 2, 3)
SCHEDULE = (
    "T0", "T1", "A", "T2",
    "F0", "F1", "A0", "F2",
    "F0", "F1", "A0", "F2",
    "F0 F1", "A0 F2",
)
SMALL = 48


def halves(bit, outs, index):
    mine = (index >> bit) & 1
    inner = 1 << bit
    for out, which in zip(outs, (mine, 1 - mine)):
        for p in range(out.shape[0]):
            for q in range(inner):
                yield out, p, q, p * 2 * inner + which * inner + q


def stacked_copies(pairs, sems):
    flat_pairs = []
    for sources, target in pairs:
        rows = target.shape[0] // 2
        flat_pairs += [(source, target.at[pl.ds(i * rows, rows)]) for i, source in enumerate(sources)]
    copies = load_all(flat_pairs, sems)
    for copy in copies:
        copy.start()
    return [copies[i : i + 2] for i in range(0, len(copies), 2)]


def ffn_terms(bit, tiles, at, at_b, n2_df_a, n2_df_b, units_a, units_b, token, keep_ref, send_ref, left, gate_up, down, flat, sems):
    width, part = left.shape[2], down.shape[1]
    columns, columns_b = (pl.ds(start, tiles * LANES) for start in (at, at_b))
    lefts = [(n2_df_a.at[i], n2_df_b.at[i]) for i in range(2)]
    m, dg, dw = [(units_a.at[i, :, columns], units_b.at[i, :, columns_b]) for i in range(3)]
    n2, dg, dw, df, m = stacked_copies(
        [(lefts[0], left.at[0]), (dg, gate_up.at[:, :part]), (dw, gate_up.at[:, part:]), (lefts[1], left.at[1]), (m, down)], sems)
    for which, (right, needed) in enumerate(((gate_up, n2 + dg + dw), (down, df + m))):
        for copy in needed:
            copy.wait()
        terms = contract_rows(left[which], right[...])
        for at_lane in range(0, right.shape[1], LANES):
            matrix, c = divmod(at_lane // LANES, tiles)
            start = tiles * width * (2 * which + matrix) + c
            flat[pl.ds(start, width, stride=tiles), :] = terms[:, at_lane : at_lane + LANES]
    rows = keep_ref.shape[2]
    for out, p, q, shard in halves(bit, (keep_ref, send_ref), lax.axis_index("dp")):
        out[p, q] = flat[pl.ds(pl.multiple_of(shard * rows, 8), rows), :].astype(BF)


def small_rows(small, packed):
    packed[...] = jnp.zeros(packed.shape, F32)
    width = small.shape[1]
    for i in range(2 + RECURSIONS):
        for c in range(CHUNKS):
            stop = min(width, (c + 1) * LANES)
            packed[i * CHUNKS + c : i * CHUNKS + c + 1, : stop - c * LANES] = small[i : i + 1, c * LANES : stop]
    return packed[...]


def split_small(small, ref, start):
    high = small.astype(BF)
    ref[start : start + SMALL, :] = high
    ref[start + SMALL : start + 2 * SMALL, :] = (small - high.astype(F32)).astype(BF)


def rounded_small(small):
    high = small.astype(BF)
    return high.astype(F32) + (small - high.astype(F32)).astype(BF).astype(F32)


def joined_small(ref, start):
    return ref[start : start + SMALL, :].astype(F32) + ref[start + SMALL : start + 2 * SMALL, :].astype(F32)


def attn_terms(bit, depth, n1_a, n1_b, du_a, du_b, o_da_a, o_da_b, small_a, small_b, token,
               keep, send, small_out, left, du_rows, da_rows, turned, own, terms, flat, packed, sems):
    base, count = 0, own.shape[0] // 2
    lower = lane_of(count) < HEAD_DIM
    core = lax.axis_index("mp")
    n1, du, o, da = stacked_copies(
        [((n1_a, n1_b), left.at[0]), ((du_a, du_b), du_rows), ((o_da_a.at[0], o_da_b.at[0]), left.at[1]),
         ((o_da_a.at[1], o_da_b.at[1]), da_rows)], sems)
    for which, (right, needed) in enumerate(((du_rows, n1 + du), (da_rows, o + da))):
        for copy in needed:
            copy.wait()
        columns = right.shape[1]
        half = columns // LANES
        turned[...] = left[which].T
        group = depth * LANES // columns
        for i in range(own.shape[0] // group):
            own[i * group : (i + 1) * group, :] = turned[pl.ds(pl.multiple_of((2 * i + core) * group, 16), group), :]
        for start in range(0, columns, PART):
            stop = min(columns, start + PART)
            block = plain(own[...], right[:, start:stop])
            if stop - start < PART:
                block = jnp.concatenate([block, jnp.zeros((2 * count, PART - (stop - start)), F32)], axis=1)
            for part in range(0, stop - start, LANES):
                terms[(start + part) // LANES] = block[:, part : part + LANES]
        step = 2 * columns // LANES
        after = first_odd = None
        for c in range(half + 1):
            even = terms[c, pl.ds(0, count, stride=2), :]
            odd = other_half(terms[c, pl.ds(1, count, stride=2), :])
            if c < half:
                flat[pl.ds(base + c, count, stride=step), :] = even
            else:
                flat[pl.ds(base + c, count, stride=step), :] = jnp.where(lower, even, first_odd)
            if c == 0:
                first_odd = odd
            else:
                flat[pl.ds(base + half + c, count, stride=step), :] = jnp.where(lower, after, odd)
            after = odd
        base += 2 * count * columns // LANES
    index = lax.axis_index("dp")
    total = rounded_small(small_rows(small_a, packed.at[0])) + rounded_small(small_rows(small_b, packed.at[1]))
    small_out[...] = total
    outer, inner, rows = keep.shape[:3]
    split_small(total, send, outer * inner * rows)

    def rows_of_shard(shard):
        start = pl.multiple_of(shard * depth, 8)
        return flat[pl.ds(start, rows), :].astype(BF)

    mine = (index >> bit) & 1
    for p in range(outer):
        for q in range(inner):
            shard = 2 * p * inner + q
            keep[p, q] = rows_of_shard(shard + mine * inner)
            at = (p * inner + q) * rows
            send[at : at + rows, :] = rows_of_shard(shard + (1 - mine) * inner)


def fold(bit, kept, got, token, keep, send):
    mine = (lax.axis_index("dp") >> bit) & 1
    for p in range(kept.shape[0]):
        for q in range(kept.shape[2]):
            for out, which in ((keep, mine), (send, 1 - mine)):
                out[p, q] = (kept[p, which, q].astype(F32) + got[p, which, q].astype(F32)).astype(BF)


def fold_small(bit, kept, got, small, token, keep, send, small_out):
    mine = (lax.axis_index("dp") >> bit) & 1
    outer, _, inner, rows, _ = kept.shape
    for p in range(outer):
        for q in range(inner):
            totals = []
            for which in (mine, 1 - mine):
                start = pl.multiple_of(((2 * p + which) * inner + q) * rows, 16)
                totals.append((kept[p, which, q].astype(F32) + got[pl.ds(start, rows), :].astype(F32)).astype(BF))
            keep[p, q] = totals[0]
            at = (p * inner + q) * rows
            send[at : at + rows, :] = totals[1]
    total = rounded_small(small[...]) + joined_small(got, 2 * outer * inner * rows)
    small_out[...] = total
    split_small(total, send, outer * inner * rows)


def fold_group(folds, *refs):
    inputs, results = refs, refs[sum(n for _, n, _ in folds) + 1 :]
    token = refs[sum(n for _, n, _ in folds)]
    for function, n_in, n_out in folds:
        function(*inputs[:n_in], token, *results[:n_out])
        inputs, results = inputs[n_in:], results[n_out:]


def finish_streams(tiles, *refs):
    count = len(tiles)
    feeds, refs = refs[: 2 * count], refs[2 * count :]
    attn, refs = refs[:2], refs[2:]
    small, ffn_out, attn_out, one_out, two_out, router_out, flat, packed = refs
    every = sum(tiles)
    rows = ffn_out.shape[0] // every
    base = 0
    for i, wide in enumerate(tiles):
        flat[: rows * wide, :] = feeds[2 * i][...].astype(F32) + feeds[2 * i + 1][...].astype(F32)
        for c in range(wide):
            ffn_out[pl.ds(base + c, rows, stride=every), :] = flat[pl.ds(c, rows, stride=wide), :]
        base += wide
    padded = attn[0].shape[0]
    both = attn[0][...].astype(F32) + attn[1][:padded, :].astype(F32)
    attn_out[...] = both[: attn_out.shape[0]]
    total = rounded_small(small[...]) + joined_small(attn[1], padded)
    packed[...] = total
    width = one_out.shape[1]
    outs = [(one_out, 0), (two_out, 0), *[(router_out, i) for i in range(RECURSIONS)]]
    for i, (out, row) in enumerate(outs):
        for c in range(CHUNKS):
            stop = min(width, (c + 1) * LANES)
            out[row : row + 1, c * LANES : stop] = packed[i * CHUNKS + c : i * CHUNKS + c + 1, : stop - c * LANES]


class Stream:
    def __init__(self, order, bits):
        self.order, self.left, self.done = order, list(range(bits - 1, -1, -1)), 0
        self.kept = self.got = None

    def shape_for(self, array):
        at = self.left.index(self.order[self.done])
        rows, lanes = array.shape[-2:]
        return (1 << at, 2, 1 << (len(self.left) - 1 - at), rows, lanes)

    def sent(self, kept, send, n_dp):
        bit = self.order[self.done]
        self.kept, self.got = kept, swap_dp(send, bit, n_dp)
        self.left.remove(bit)
        self.done += 1


def on_device(
    hidden_in,
    sel_one,
    sel_two,
    sel_three,
    segment_ids,
    pad_mask,
    qkv_weight,
    out_weight,
    gate_weight,
    up_weight,
    down_weight,
    norm_one,
    norm_two,
    router_weight,
    d_hidden,
):
    seq_len, width = hidden_in.shape
    n_dp, n_mp = lax.axis_size("dp"), lax.axis_size("mp")
    dp_index, mp_index = lax.axis_index("dp"), lax.axis_index("mp")
    cosine, sine = rotary_tables(seq_len)
    weights = [(gate_weight, up_weight, down_weight)]
    weights.append(tuple(swap_mp(w) for w in weights[0]))
    gain_one, gain_two = norm_one.reshape(1, width), norm_two.reshape(1, width)
    padded = CHUNKS * LANES
    units = gate_weight.shape[1]
    feed_weights = (*weights[0], *weights[1])

    def shape(*dims, dtype=BF):
        return jax.ShapeDtypeStruct(dims, dtype)

    def whole(*dims, **kw):
        return pl.BlockSpec(dims, lambda *_: (0,) * len(dims), **kw)

    anywhere = pl.BlockSpec(memory_space=pl.ANY)
    one = pl.Buffered(1)
    stack = RECURSIONS, seq_len
    heads = (2 * KV_HEADS, seq_len, LANES)
    square = (HEADS, seq_len, seq_len)
    n1, q, kz, vz, p, o_da, attn, n2, bias, active, near, slope_first, silu_first, f_first = pl.pallas_call(
        first_attention,
        grid=(1,),
        in_specs=[
            whole(seq_len, width), *[whole(*ref.shape) for ref in (sel_one, sel_two, sel_three, segment_ids, pad_mask)],
            whole(seq_len, LANES), whole(seq_len, LANES), whole(1, width), whole(1, width), whole(*qkv_weight.shape), whole(*out_weight.shape),
            *[anywhere] * 3,
        ],
        out_specs=[
            whole(1, seq_len, width), whole(seq_len, padded), whole(*heads), whole(*heads), whole(*square),
            whole(1, 1, seq_len, width), whole(seq_len, width), whole(seq_len, width), whole(RECURSIONS, seq_len, seq_len), whole(*stack, 1),
            whole(1, 1, seq_len, units), whole(seq_len, units), whole(seq_len, units), whole(seq_len, width),
        ],
        out_shape=[
            shape(*stack, width), shape(seq_len, padded), shape(*heads), shape(*heads), shape(*square),
            shape(2, *stack, width), shape(seq_len, width, dtype=F32), shape(seq_len, width),
            shape(*stack, seq_len, dtype=F32), shape(*stack, 1, dtype=F32),
            shape(3, *stack, units), shape(seq_len, units), shape(seq_len, units), shape(seq_len, width, dtype=F32),
        ],
        scratch_shapes=[*[pltpu.VMEM(w.shape, BF) for w in weights[0]], pltpu.SemaphoreType.DMA((3,))],
        compiler_params=pltpu.CompilerParams(vmem_limit_bytes=VMEM_BYTES),
        cost_estimate=pl.CostEstimate(flops=2 * 10**9, bytes_accessed=12 * 10**6, transcendentals=600000),
        name="first_attention",
    )(hidden_in, sel_one, sel_two, sel_three, segment_ids, pad_mask, cosine, sine, gain_one, gain_two, qkv_weight, out_weight,
      *weights[0])
    attention_0 = (q, kz, vz, p)
    wide = qkv_weight.shape[1]
    row = (seq_len, width)
    kept = RECURSIONS - 1
    first_part = FFN_TILES[0] * LANES
    vm = pltpu.VMEM
    results = pl.pallas_call(
        all_steps,
        grid=(1,),
        in_specs=[
            whole(RECURSIONS, seq_len, seq_len), whole(RECURSIONS, seq_len, 1), whole(RECURSIONS, width),
            whole(seq_len, LANES), whole(seq_len, LANES), whole(1, width), whole(1, width), *[anywhere] * 18,
        ],
        out_specs=[*[anywhere] * 8, whole(*row), whole(*row), whole(8, width)],
        out_shape=[
            shape(*stack, width), *[shape(2, *stack, width)] * 2, shape(3, *stack, units), shape(3, *stack, first_part), shape(3, *stack, units - first_part), shape(*stack, wide),
            *[shape(*row, dtype=F32)] * 3, shape(8, width, dtype=F32),
        ],
        scratch_shapes=[
            *[vm(w.shape, BF) for w in (qkv_weight, out_weight, *feed_weights)],
            vm((RECURSIONS + 1, *row), F32), vm((RECURSIONS, *row), F32), vm((RECURSIONS, *row), BF),
            *[vm((*stack, units), BF)] * 4, vm((kept, seq_len, padded), BF), vm((kept, *heads), BF), vm((kept, *heads), BF),
            vm((kept, *square), BF), *[vm(row, BF)] * 3, *[vm((seq_len, units), BF)] * 2, vm(row, BF), *[vm((seq_len, units), BF)] * 4,
            vm(row, BF), vm((seq_len, wide), BF), vm(row, F32), vm(row, F32), vm((seq_len, padded), BF),
            pltpu.SemaphoreType.DMA((15,)), pltpu.SemaphoreType.DMA((16,)),
        ],
        input_output_aliases={14: 0, 15: 1, 16: 3},
        compiler_params=pltpu.CompilerParams(vmem_limit_bytes=VMEM_BYTES),
        cost_estimate=pl.CostEstimate(flops=23 * 10**9, bytes_accessed=50 * 10**6, transcendentals=4 * 10**6),
        name="all_steps",
    )(bias, active, router_weight, cosine, sine, gain_one, gain_two, hidden_in, d_hidden, attn, n2,
      slope_first, silu_first, f_first, n1, o_da, near,
      qkv_weight, out_weight, *feed_weights)
    n1, o_da, n2_df, near, far, late, du, state, base, grad_state, small = results

    def run_last(token):
        return pl.pallas_call(
            last_attention,
            grid=(1,),
            in_specs=[
                whole(1, seq_len, 1), whole(seq_len, LANES), whole(seq_len, LANES), whole(1, width),
                whole(seq_len, padded), whole(*heads), whole(*heads), whole(*square),
                pl.BlockSpec((1, 1, seq_len, width), lambda i: (1, 0, 0, 0)), whole(8, width), whole(*out_weight.shape), *[anywhere] * 6,
            ],
            out_specs=[whole(1, seq_len, qkv_weight.shape[1]), whole(seq_len, width), whole(8, width)],
            out_shape=[shape(*stack, qkv_weight.shape[1]), shape(seq_len, width, dtype=F32), shape(8, width, dtype=F32)],
            scratch_shapes=[
                pltpu.VMEM((seq_len, padded), BF), *[pltpu.VMEM((seq_len, width), F32)] * 4,
                pltpu.VMEM(qkv_weight.shape, BF), pltpu.SemaphoreType.DMA((4,)),
            ],
            input_output_aliases={15: 0},
            compiler_params=pltpu.CompilerParams(vmem_limit_bytes=VMEM_BYTES),
            cost_estimate=pl.CostEstimate(flops=1, bytes_accessed=1, transcendentals=0),
            name="last_attention",
        )(active, cosine, sine, gain_one, *attention_0, o_da, small, out_weight, hidden_in, base, grad_state, qkv_weight, du, token)

    def rows_of(stacked):
        return stacked.reshape(*stacked.shape[:-3], -1, stacked.shape[-1])

    bits = n_dp.bit_length() - 1
    share = (qkv_weight.size + out_weight.size) // (n_dp * n_mp)
    if bits == 4 and 3 * width % n_dp == 0 and units == sum(FFN_TILES) * LANES and share % (16 * qkv_weight.shape[1]) == share % (16 * width) == 0:
        n2_df_rows = [rows_of(t) for t in (n2_df, swap_mp(n2_df))]
        near, far_b = rows_of(near), rows_of(swap_mp(far))
        n1_b = rows_of(swap_mp(n1))
        streams = [Stream(order, bits) for order in FFN_ORDERS]
        attn_stream = Stream(ATTN_ORDER, bits)
        depth = share // LANES
        tiled = -(-depth // 16) * 16
        common = dict(
            grid=(1,),
            compiler_params=pltpu.CompilerParams(vmem_limit_bytes=VMEM_BYTES),
            cost_estimate=pl.CostEstimate(flops=1, bytes_accessed=1, transcendentals=0),
        )

        def wholes(arrays):
            return [whole(*t.shape) for t in arrays]

        def terms_of(j, token):
            stream, tiles = streams[j], FFN_TILES[j]
            at = sum(FFN_TILES[:j]) * LANES
            factors = (*n2_df_rows, near, far_b if j == 0 else late_b)
            bit = stream.order[0]
            dims = (1 << (bits - 1 - bit), 1 << bit, 3 * width // n_dp * tiles, LANES)
            both = 2 * RECURSIONS * seq_len
            keep, send = pl.pallas_call(
                functools.partial(ffn_terms, bit, tiles, at, 0 if j == 0 else at - first_part),
                in_specs=[anywhere] * (len(factors) + 1),
                out_specs=[whole(*dims)] * 2,
                out_shape=[shape(*dims)] * 2,
                scratch_shapes=[pltpu.VMEM((2, both, width), BF), *[pltpu.VMEM((both, n * tiles * LANES), BF) for n in (2, 1)],
                                pltpu.VMEM((3 * width * tiles, LANES), F32), pltpu.SemaphoreType.DMA((10,))],
                name=f"ffn_terms_{j}",
                **common,
            )(*factors, token)
            stream.sent(keep, send, n_dp)
            return keep

        def fold_streams(group, token, small_own):
            folds, operands, outs = [], [], []
            for stream in group:
                bit = stream.order[stream.done]
                dims = stream.shape_for(stream.kept)
                kept = stream.kept.reshape(dims)
                held = (dims[0], *dims[2:])
                if stream is attn_stream:
                    operands += [kept, stream.got, small_own]
                    outs += [shape(*held), shape(dims[0] * dims[2] * dims[3] + 2 * SMALL, LANES), shape(SMALL, LANES, dtype=F32)]
                    folds.append((functools.partial(fold_small, bit), 3, 3))
                else:
                    operands += [kept, stream.got.reshape(dims)]
                    outs += [shape(*held), shape(*held)]
                    folds.append((functools.partial(fold, bit), 2, 2))
            results = pl.pallas_call(
                functools.partial(fold_group, folds),
                in_specs=[*wholes(operands), anywhere],
                out_specs=wholes(outs),
                out_shape=outs,
                name="fold_terms",
                **common,
            )(*operands, token)
            token = results[0]
            for stream, (_, _, n_out) in zip(group, folds):
                stream.sent(results[0], results[1], n_dp)
                small_own = results[2] if n_out == 3 else small_own
                results = results[n_out:]
            return token, small_own

        du, grad_state, small = run_last(small)
        late, du, small = lax.optimization_barrier((late, du, small))
        late_b, du_b = rows_of(swap_mp(late)), rows_of(swap_mp(du))
        token, small_own = small, None
        for item in SCHEDULE:
            if item[0] == "T":
                token = terms_of(int(item[1:]), token)
                if item == "T0":
                    o_da, small, token = lax.optimization_barrier((o_da, small, token))
                    o_da_b, small_b = rows_of(swap_mp(o_da)), swap_mp(small)
            elif item == "A":
                bit = attn_stream.order[0]
                dims = (1 << (bits - 1 - bit), 1 << bit, tiled, LANES)
                operands = (rows_of(n1), n1_b, rows_of(du), du_b, rows_of(o_da), o_da_b, small, small_b)
                outs = (shape(*dims), shape(n_dp // 2 * tiled + 2 * SMALL, LANES), shape(SMALL, LANES, dtype=F32))
                keep, send, small_own = pl.pallas_call(
                    functools.partial(attn_terms, bit, depth),
                    in_specs=[*[anywhere] * 6, *wholes(operands[6:]), anywhere],
                    out_specs=wholes(outs),
                    out_shape=outs,
                    scratch_shapes=[pltpu.VMEM((2, 2 * RECURSIONS * seq_len, width), BF),
                                    *[pltpu.VMEM((2 * RECURSIONS * seq_len, t.shape[-1]), BF) for t in (du, o_da)],
                                    pltpu.VMEM((width, 2 * RECURSIONS * seq_len), BF),
                                    pltpu.VMEM((width // 2, 2 * RECURSIONS * seq_len), BF),
                                    pltpu.VMEM((-(-du.shape[-1] // PART) * 2, width // 2, LANES), F32),
                                    pltpu.VMEM((n_dp * depth + tiled - depth, LANES), F32), pltpu.VMEM((2, SMALL, LANES), F32),
                                    pltpu.SemaphoreType.DMA((8,))],
                    name="attn_terms",
                    **common,
                )(*operands, token)
                attn_stream.sent(keep, send, n_dp)
                token = small_own
            else:
                group = [attn_stream if name == "A0" else streams[int(name[1:])] for name in item.split()]
                token, small_own = fold_streams(group, token, small_own)
        ends = [t.reshape(t.shape[-2:]) for stream in (*streams, attn_stream) for t in (stream.kept, stream.got)]
        outs = (shape(3 * width // n_dp * sum(FFN_TILES), LANES, dtype=F32), shape(depth, LANES, dtype=F32),
                shape(1, width, dtype=F32), shape(1, width, dtype=F32), shape(RECURSIONS, width, dtype=F32))
        ffn_flat, attn_flat, one, two, router = pl.pallas_call(
            functools.partial(finish_streams, FFN_TILES),
            in_specs=wholes((*ends, small_own)),
            out_specs=wholes(outs),
            out_shape=outs,
            scratch_shapes=[pltpu.VMEM((3 * width // n_dp * max(FFN_TILES), LANES), F32), pltpu.VMEM((SMALL, LANES), F32)],
            name="finish_streams",
            **common,
        )(*ends, small_own)
        return (state, grad_state, attn_flat.reshape(-1), ffn_flat.reshape(1, -1), one.reshape(-1), two.reshape(-1), router)

    du, grad_state, small = run_last(small)
    two, feed = rows_of(n2_df)
    o, d_attn = rows_of(o_da)
    far = jnp.concatenate([far, late], axis=-1)
    sides = [[t[i] for i in (1, 2, 0)] for t in (rows_of(near), rows_of(far))]

    def side_terms(side, columns):
        return jnp.concatenate(
            [
                contract_rows(left, sides[side][which][:, columns]).astype(BF)
                for which, left in enumerate((two, two, feed))
            ],
            axis=0,
        )

    orders = orders_of(bits)
    if 3 * width % n_dp == 0 and units % 1280 == 0:
        fifth = units // 5
        streams = [(orders[i], slice(j * fifth, (j + 1) * fifth)) for i, j in ((0, 0), (1, 1), (2, 2), (0, 3), (1, 4))]
        done = []
        for order, columns in streams:
            terms = side_terms(0, columns).astype(F32) + swap_mp(side_terms(1, columns)).astype(F32)
            done.append(halving(terms.astype(BF).reshape(n_dp, 3 * width // n_dp, fifth), order, n_dp, dp_index))
        ffn_flat = jnp.concatenate(done, axis=1).reshape(1, -1)
    else:
        terms = side_terms(0, slice(None)).astype(F32) + swap_mp(side_terms(1, slice(None))).astype(F32)
        terms = terms.astype(BF).reshape(n_dp, 3 * width * units // n_dp // 128, 128)
        ffn_flat = halving(terms, orders[0], n_dp, dp_index).reshape(1, -1)

    grad_qkv = contract_rows(rows_of(n1), rows_of(du)).astype(BF)
    grad_out = contract_rows(o, d_attn).astype(BF)
    attn = jnp.concatenate([grad_qkv.reshape(-1), grad_out.reshape(-1)]).reshape(n_dp, 2, share // 128, 128)
    keep = jnp.where(mp_index == 0, attn[:, 0], attn[:, 1])
    send = jnp.where(mp_index == 0, attn[:, 1], attn[:, 0])
    attn = (keep.astype(F32) + swap_mp(send).astype(F32)).astype(BF)
    cuts = [0, (share // 128) // 24 * 8, (share // 128) // 12 * 8, share // 128]
    attn_flat = jnp.concatenate(
        [halving(attn[:, a:b], order, n_dp, dp_index) for a, b, order in zip(cuts, cuts[1:], orders)], axis=0
    ).reshape(-1)

    small = small + swap_mp(small)
    for bit in range(bits):
        small = small + swap_dp(small, bit, n_dp)
    return (state, grad_state, attn_flat, ffn_flat, small[0], small[1], small[2 : 2 + RECURSIONS])


def solution(mesh):
    both = P(("dp", "mp"), None)
    in_specs = (
        both,
        both,
        both,
        both,
        both,
        both,
        P(),
        P(),
        P(None, "mp"),
        P(None, "mp"),
        P(None, "mp"),
        P(),
        P(),
        P(),
        both,
    )
    out_specs = (both, both, P(("dp", "mp")), P("mp", "dp"), P(), P(), P())
    return jax.shard_map(
        on_device, mesh=mesh, in_specs=in_specs, out_specs=out_specs, check_vma=False
    )
```

```python
import functools
import math

import jax
import jax.numpy as jnp
import numpy as np
from jax import lax
from jax.experimental import pallas as pl
from jax.experimental.pallas import tpu as pltpu
from jax.sharding import PartitionSpec as P

HEADS = 15
KV_HEADS = 5
HEAD_DIM = 64
RECURSIONS = 3
GROUPS = HEADS // KV_HEADS
EPS = 1e-05
BF = jnp.bfloat16
F32 = jnp.float32


LANES = 128
CHUNKS = -(-HEADS * HEAD_DIM // LANES)
ROWS = 192
BLOCK = 256
MIB = 1 << 20
VMEM_BYTES = 64 * MIB - 65536


def rotary_tables(seq_len):
    half = HEAD_DIM // 2
    frequency = np.float32(100000.0) ** (
        np.float32(-2.0) * np.arange(half, dtype=np.float32) / np.float32(HEAD_DIM)
    )
    angles = np.arange(seq_len, dtype=np.float32)[:, None] * frequency.astype(np.float32)
    cosine, sine = np.cos(angles), np.sin(angles)
    return (
        jnp.asarray(np.concatenate([cosine] * 4, axis=1), F32),
        jnp.asarray(np.concatenate([-sine, sine] * 2, axis=1), F32),
    )


def contract_rows(left, right):
    return lax.dot_general(left, right, (((0,), (0,)), ((), ())), preferred_element_type=F32)


def contract_last(left, right):
    return lax.dot_general(left, right, (((1,), (1,)), ((), ())), preferred_element_type=F32)


def plain(left, right):
    return jnp.dot(left, right, preferred_element_type=F32)


def inverse_rms(rows):
    return lax.rsqrt(jnp.mean(rows * rows, axis=-1, keepdims=True) + EPS)


def norm_back(rows, gain, d_out):
    inv = inverse_rms(rows)
    scaled = d_out * gain
    inner = jnp.mean(scaled * rows, axis=-1, keepdims=True)
    d_rows = inv * scaled - rows * (inv * inv * inv * inner)
    return d_rows, jnp.sum(d_out * rows * inv, axis=0, keepdims=True)


def lane_of(rows):
    return lax.broadcasted_iota(jnp.int32, (rows, LANES), 1)


def swapped(chunk):
    first = lane_of(chunk.shape[0]) % HEAD_DIM < HEAD_DIM // 2
    return jnp.where(first, pltpu.roll(chunk, LANES - 32, 1), pltpu.roll(chunk, 32, 1))


def other_half(chunk):
    return pltpu.roll(chunk, HEAD_DIM, 1)


def over_rows(count, body):
    def lap(i, carry):
        body(pl.ds(pl.multiple_of(i * ROWS, ROWS), ROWS))
        return carry

    lax.fori_loop(0, count // ROWS, lap, 0)


def attention_forward(x_ref, bias_ref, cos_ref, sin_ref, gain, qkv_w, n1_ref, q_ref, kz_ref, vz_ref, p_ref, o_ref):
    seq_len, width = x_ref.shape
    scale = 1.0 / math.sqrt(HEAD_DIM)

    def norm(rows):
        x = x_ref[rows, :]
        n1_ref[rows, :] = (x * inverse_rms(x) * gain).astype(BF)

    over_rows(seq_len, norm)
    lower = lane_of(seq_len) < HEAD_DIM
    n1 = n1_ref[...]

    def spread(ref, head, chunk, upper):
        flipped = other_half(chunk)
        here, there = (flipped, chunk) if upper else (chunk, flipped)
        ref[2 * head] = jnp.where(lower, here, 0.0).astype(BF)
        ref[2 * head + 1] = jnp.where(lower, 0.0, there).astype(BF)

    columns = qkv_w.shape[1]
    for start in range(0, columns, 2 * LANES):
        wide = plain(n1, qkv_w[:, start : min(start + 2 * LANES, columns)])
        for part in range(0, wide.shape[1], LANES):
            chunk = wide[:, part : part + LANES]
            if chunk.shape[1] < LANES:
                chunk = jnp.concatenate([chunk, jnp.zeros_like(chunk)], axis=1)
            at = (start + part) // LANES
            heads = (2 * at, 2 * at + 1)
            if heads[0] < HEADS + KV_HEADS:
                chunk = chunk * cos_ref[...] + swapped(chunk) * sin_ref[...]
                if heads[0] < HEADS:
                    q_ref[:, at * LANES : (at + 1) * LANES] = chunk.astype(BF)
            for upper, head in enumerate(heads):
                if HEADS <= head < HEADS + KV_HEADS:
                    spread(kz_ref, head - HEADS, chunk, upper)
                elif HEADS + KV_HEADS <= head < HEADS + 2 * KV_HEADS:
                    spread(vz_ref, head - HEADS - KV_HEADS, chunk, upper)

    for at in range(CHUNKS):
        query = q_ref[:, at * LANES : (at + 1) * LANES]
        total = None
        for upper in range(2):
            head = 2 * at + upper
            if head < HEADS:
                key = 2 * (head // GROUPS) + upper
                scores = contract_last(query, kz_ref[key]) * scale + bias_ref[...]
                top = jnp.max(scores, axis=-1, keepdims=True)
                exponent = jnp.exp(scores - top)
                share = pl.reciprocal(jnp.sum(exponent, axis=-1, keepdims=True))
                attend = (exponent * share).astype(BF)
                p_ref[head] = attend
                mixed = plain(attend, vz_ref[key])
                total = mixed if total is None else total + mixed
        stop = min(width, (at + 1) * LANES)
        o_ref[:, at * LANES : stop] = total[:, : stop - at * LANES].astype(BF)


def attention_out(x_ref, o_ref, out_w, gain, attn_ref, n2_ref):
    attn_ref[...] = plain(o_ref[...], out_w[...])

    def norm(rows):
        after = x_ref[rows, :] + attn_ref[rows, :]
        n2_ref[rows, :] = (after * inverse_rms(after) * gain).astype(BF)

    over_rows(x_ref.shape[0], norm)


def feed_side(n2_ref, weights, results, ready):
    n2 = n2_ref[...]
    gate_w, up_w, down_w = weights
    m_ref, slope_ref, silu_ref = results
    ready(0, 1)
    for start in range(0, gate_w.shape[1], BLOCK):
        at = slice(start, start + BLOCK)
        g, u = plain(n2, gate_w[:, at]), plain(n2, up_w[:, at])
        s = jax.nn.sigmoid(g)
        silu = g * s
        m_ref[:, at] = (silu * u).astype(BF)
        slope_ref[:, at] = (u * s * (1.0 + g * (1.0 - s))).astype(BF)
        silu_ref[:, at] = silu.astype(BF)
    ready(2)
    return contract_last(m_ref[...], down_w[...])


def feed_backward(df_ref, sides, d_two_ref, ready):
    d_feed = df_ref[...]
    for side, (gate_w, up_w, down_w, slope_ref, silu_ref, dg_ref, du_ref) in enumerate(sides):
        ready(3 * side)
        for start in range(0, gate_w.shape[1], BLOCK):
            at = slice(start, start + BLOCK)
            d_hidden = plain(d_feed, down_w[:, at])
            dg_ref[:, at] = (d_hidden * slope_ref[:, at].astype(F32)).astype(BF)
            du_ref[:, at] = (d_hidden * silu_ref[:, at].astype(F32)).astype(BF)
        ready(3 * side + 1, 3 * side + 2)
        part = contract_last(dg_ref[...], gate_w[...]) + contract_last(du_ref[...], up_w[...])
        d_two_ref[...] = part if side == 0 else d_two_ref[...] + part


def attention_backward(d_attn_ref, out_w, qkv_w, cos_ref, sin_ref, q_ref, kz_ref, vz_ref, p_ref, do_ref, du_ref):
    seq_len, width = d_attn_ref.shape
    scale = 1.0 / math.sqrt(HEAD_DIM)
    do_ref[:, :width] = contract_last(d_attn_ref[...], out_w[...]).astype(BF)
    do_ref[:, width:] = jnp.zeros((seq_len, do_ref.shape[1] - width), BF)
    lower = lane_of(seq_len) < HEAD_DIM
    cosine, sine = cos_ref[...], sin_ref[...]

    def back(chunk):
        chunk = chunk * scale
        return chunk * cosine - swapped(chunk) * sine

    waiting, d_k, d_v = None, {}, {}
    for at in range(CHUNKS):
        query, d_mixed = (ref[:, at * LANES : (at + 1) * LANES] for ref in (q_ref, do_ref))
        query_t, d_mixed_t = query.T, d_mixed.T
        d_query = None
        for upper in range(2):
            head = 2 * at + upper
            if head >= HEADS:
                continue
            group = head // GROUPS
            key = 2 * group + upper
            rows = slice(upper * HEAD_DIM, (upper + 1) * HEAD_DIM)
            attend = p_ref[head]
            d_attend = contract_last(d_mixed, vz_ref[key])
            soft = attend.astype(F32)
            weighted = soft * d_attend
            inner = jnp.sum(weighted, axis=-1, keepdims=True)
            d_scores = (weighted - soft * inner).astype(BF)
            part = plain(d_scores, kz_ref[key])
            d_query = part if d_query is None else d_query + part
            for store, term in ((d_k, plain(query_t[rows], d_scores)), (d_v, plain(d_mixed_t[rows], attend))):
                store[group] = term if group not in store else store[group] + term
        if at < CHUNKS - 1:
            du_ref[:, at * LANES : (at + 1) * LANES] = back(d_query).astype(BF)
        else:
            waiting = d_query

    def two_heads(store, first, second):
        return jnp.concatenate([store[first], store[second]], axis=0).T

    tail = jnp.where(lower, waiting, two_heads(d_k, 0, 0))
    du_ref[:, (CHUNKS - 1) * LANES : CHUNKS * LANES] = back(tail).astype(BF)
    for i in range(2):
        at = CHUNKS + i
        du_ref[:, at * LANES : (at + 1) * LANES] = back(two_heads(d_k, 1 + 2 * i, 2 + 2 * i)).astype(BF)
        at = CHUNKS + 2 + i
        du_ref[:, at * LANES : (at + 1) * LANES] = two_heads(d_v, 2 * i, 2 * i + 1).astype(BF)
    at = CHUNKS + 4
    du_ref[:, at * LANES :] = two_heads(d_v, 4, 4)[:, : du_ref.shape[1] - at * LANES].astype(BF)


def router_gate(x, router_row):
    return jax.nn.sigmoid(jnp.sum(x * router_row, axis=-1, keepdims=True))


def masks(select_refs, segment_ref, pad_ref, bias_ref, active_ref):
    seq_len = segment_ref.shape[1]
    square = (seq_len, seq_len)
    query, key = (lax.broadcasted_iota(jnp.int32, square, axis) for axis in (0, 1))
    diagonal = query == key
    segment = segment_ref[...].astype(F32)
    own = jnp.sum(jnp.where(diagonal, segment, 0.0), axis=1, keepdims=True)
    near = (key <= query) & (segment == own)
    real = pad_ref[...] == 1
    for recursion, ref in enumerate(select_refs):
        place = lax.broadcasted_iota(jnp.int32, (seq_len, ref.shape[1]), 0)
        active = jnp.max(jnp.where(ref[...] == place, 1.0, 0.0), axis=1, keepdims=True)
        active_ref[recursion] = active
        along = jnp.sum(jnp.where(diagonal, active, 0.0), axis=0, keepdims=True)
        usable = (along > 0.0) & real
        bias_ref[recursion] = jnp.where(near & (usable | diagonal), 0.0, -1e30)


def first_attention(x_ref, sel_one, sel_two, sel_three, segment_ref, pad_ref, cos_ref, sin_ref, gain_one, gain_two, qkv_w, out_w,
                    gate_hbm, up_hbm, down_hbm, n1_ref, q_out, kz_out, vz_out, p_out, o_ref, attn_ref, n2_ref, bias_ref, active_ref,
                    m_ref, slope_ref, silu_ref, f_ref, gate_w, up_w, down_w, q_ref, kz_ref, vz_ref, p_ref, sems):
    copies = load_all([(gate_hbm, gate_w), (up_hbm, up_w), (down_hbm, down_w),
                       (q_ref, q_out), (kz_ref, kz_out), (vz_ref, vz_out), (p_ref, p_out)], sems)
    for copy in copies[:3]:
        copy.start()
    n1, o = n1_ref.at[0], o_ref.at[0, 0]
    masks((sel_one, sel_two, sel_three), segment_ref, pad_ref, bias_ref, active_ref)
    attention_forward(x_ref, bias_ref.at[0], cos_ref, sin_ref, gain_one[...], qkv_w, n1, q_ref, kz_ref, vz_ref, p_ref, o)
    for copy in copies[3:]:
        copy.start()
    attention_out(x_ref, o, out_w, gain_two[...], attn_ref, n2_ref)

    def ready(*which):
        for i in which:
            copies[i].wait()

    f_ref[...] = feed_side(n2_ref, (gate_w, up_w, down_w), (m_ref.at[0, 0], slope_ref, silu_ref), ready)
    for copy in copies[3:]:
        copy.wait()


def load_all(pairs, sems):
    return [pltpu.make_async_copy(src, dst, sems.at[i]) for i, (src, dst) in enumerate(pairs)]


def waits_at(condition, copies):
    def ready(*which):
        @pl.when(condition)
        def _():
            for i in which:
                copies[i].wait()

    return ready


def finish_attention_backward(x_ref, gain, active_ref, du_ref, qkv_w, base, state, total, out_ref):
    total[...] = contract_last(du_ref[...], qkv_w[...])
    terms = jnp.zeros((1, state.shape[1]), F32)

    def lap(i, terms):
        rows = pl.ds(pl.multiple_of(i * ROWS, ROWS), ROWS)
        d_rows, term = norm_back(x_ref[rows, :], gain, total[rows, :])
        new = jnp.where(active_ref[rows, :] > 0, base[rows, :] + d_rows, state[rows, :])
        out_ref[rows, :] = new
        return terms + term

    return lax.fori_loop(0, state.shape[0] // ROWS, lap, terms)


def all_steps(bias_ref, active_ref, router_ref, cos_ref, sin_ref, gain_one, gain_two,
              hidden_hbm, d_hidden_hbm, attn0_hbm, n20_hbm, slope_hbm, silu_hbm, f_hbm, n1_in, o_da_in, near_in,
              qkv_hbm, out_hbm, *rest):
    feed_hbm, rest = rest[:6], rest[6:]
    (n1_out, o_da_out, n2_df_out, near_out, far_out, late_out, du_out, final_out, base_ref, state_ref, small_ref), rest = rest[:11], rest[11:]
    qkv_w, out_w, *feed_w = rest[:8]
    (xs, attns, fs, slope0, slope1, silu0, silu1, qs, kzs, vzs, ps, n1, o, n2, m0, m1, df, dgw0, dgw1, da, du,
     total, d_branch, do_ref, load_sems, out_sems) = rest[8:]
    width = state_ref.shape[1]
    first_part = far_out.shape[3]
    laps = state_ref.shape[0] // ROWS
    loads = load_all(
        [*zip(feed_hbm, feed_w), (qkv_hbm, qkv_w), (out_hbm, out_w),
         (n20_hbm, n2), (attn0_hbm, attns.at[0]), (hidden_hbm, xs.at[0]), (d_hidden_hbm, state_ref),
         (f_hbm, total), (slope_hbm, slope0.at[0]), (silu_hbm, silu0.at[0])], load_sems)
    for i in (8, 3, 4, 5, 12, 9, 10, 6, 7, 0, 1, 2, 13, 14, 11):
        loads[i].start()
    loads[8].wait()

    places = dict(
        n2=[(n2, n2_df_out, 0)], m0=[(m0, near_out, 0)], m1=[(m1.at[:, :first_part], far_out, 0), (m1.at[:, first_part:], late_out, 0)],
        n1=[(n1, n1_out, None)], o=[(o, o_da_out, 0)], df=[(df, n2_df_out, 1)], dgw0=[(dgw0, near_out, pl.ds(1, 2))],
        dgw1=[(dgw1.at[:, :, :first_part], far_out, pl.ds(1, 2)), (dgw1.at[:, :, first_part:], late_out, pl.ds(1, 2))],
        da=[(da, o_da_out, 1)], du=[(du, du_out, None)])
    firsts = dict(zip(places, np.cumsum([0] + [len(pairs) for pairs in places.values()]).tolist()))

    def leaving(recursion, names):
        return [pltpu.make_async_copy(source, target.at[recursion] if which is None else target.at[which, recursion],
                                      out_sems.at[firsts[name] + i])
                for name in names for i, (source, target, which) in enumerate(places[name])]

    def start(recursion, *names):
        for copy in leaving(recursion, names):
            copy.start()

    def wait(recursion, *names):
        for copy in leaving(recursion, names):
            copy.wait()

    def forward(r, carry):
        ready, later = (waits_at(r == step, loads) for step in range(2))
        start(r, "n2")

        @pl.when(r > 0)
        def _():
            @pl.when(r > 1)
            def _():
                wait(r - 1, "m0")

            total[...] = feed_side(n2, feed_w[:3], (m0, slope0.at[r], silu0.at[r]), later)
            start(r, "m0")
            wait(r - 1, "m1")

        part = feed_side(n2, feed_w[3:], (m1, slope1.at[r], silu1.at[r]), lambda *which: ready(*[3 + i for i in which]))
        ready(12)
        total[...] = total[...] + part
        start(r, "m1")
        ready(9, 10)
        router_row = router_ref[pl.ds(r, 1), :]

        def finish(rows):
            x = xs[r, rows, :]
            f = total[rows, :].astype(BF)
            fs[r, rows, :] = f
            branch = attns[r, rows, :] + f.astype(F32)
            xs[r + 1, rows, :] = jnp.where(active_ref[r, rows, :] > 0, x + router_gate(x, router_row) * branch, x)

        over_rows(total.shape[0], finish)
        ready(6, 7)
        wait(r, "n2")

        @pl.when(r < RECURSIONS - 1)
        def _():
            @pl.when(r > 0)
            def _():
                wait(r, "n1", "o")

            attention_forward(xs.at[r + 1], bias_ref.at[r + 1], cos_ref, sin_ref, gain_one[...], qkv_w,
                              n1, qs.at[r], kzs.at[r], vzs.at[r], ps.at[r], o)
            start(r + 1, "n1", "o")
            attention_out(xs.at[r + 1], o, out_w, gain_two[...], attns.at[r + 1], n2)

        return carry

    lax.fori_loop(0, RECURSIONS, forward, 0)
    final = pltpu.make_async_copy(xs.at[RECURSIONS], final_out, out_sems.at[12])
    final.start()
    for i in (11, 13, 14):
        loads[i].wait()
    small_ref[...] = jnp.zeros(small_ref.shape, F32)

    def backward(i, carry):
        r = RECURSIONS - 1 - i
        router_row = router_ref[pl.ds(r, 1), :]

        @pl.when(i > 0)
        def _():
            wait(r + 1, "df", "dgw0", "dgw1", "da")

        def enter(lap, terms):
            rows = pl.ds(pl.multiple_of(lap * ROWS, ROWS), ROWS)
            x = xs[r, rows, :]
            d_new = jnp.where(active_ref[r, rows, :] > 0, state_ref[rows, :], 0.0)
            gate = router_gate(x, router_row)
            branch = attns[r, rows, :] + fs[r, rows, :].astype(F32)
            d_gate = jnp.sum(d_new * branch, axis=-1, keepdims=True)
            d_logit = d_gate * gate * (1.0 - gate)
            spread = gate * d_new
            d_branch[rows, :] = spread
            df[rows, :] = spread.astype(BF)
            base_ref[rows, :] = d_new + d_logit * router_row
            return terms + jnp.sum(d_logit * x, axis=0, keepdims=True)

        small_ref[pl.ds(2 + r, 1), :] = lax.fori_loop(0, laps, enter, jnp.zeros((1, width), F32))
        start(r, "df")
        feed_backward(df, ((*feed_w[:3], slope0.at[r], silu0.at[r], dgw0.at[0], dgw0.at[1]),
                           (*feed_w[3:], slope1.at[r], silu1.at[r], dgw1.at[0], dgw1.at[1])),
                      total, lambda *which: None)
        start(r, "dgw0", "dgw1")

        def leave(lap, terms):
            rows = pl.ds(pl.multiple_of(lap * ROWS, ROWS), ROWS)
            after = xs[r, rows, :] + attns[r, rows, :]
            d_after, term = norm_back(after, gain_two[...], total[rows, :].astype(BF).astype(F32))
            da[rows, :] = (d_branch[rows, :] + d_after).astype(BF)
            base_ref[rows, :] = base_ref[rows, :] + d_after
            return terms + term

        small_ref[1:2, :] = small_ref[1:2, :] + lax.fori_loop(0, laps, leave, jnp.zeros((1, width), F32))
        start(r, "da")

        @pl.when(r > 0)
        def _():
            @pl.when(i > 0)
            def _():
                wait(r + 1, "du")

            attention_backward(da, out_w, qkv_w, cos_ref, sin_ref, qs.at[r - 1], kzs.at[r - 1], vzs.at[r - 1], ps.at[r - 1], do_ref, du)
            start(r, "du")
            term = finish_attention_backward(xs.at[r], gain_one[...], active_ref.at[r], du, qkv_w, base_ref, state_ref, total, state_ref)
            small_ref[0:1, :] = small_ref[0:1, :] + term

        return carry

    lax.fori_loop(0, RECURSIONS, backward, 0)
    wait(RECURSIONS - 1, "m0", "m1", "n1", "o")
    wait(0, "df", "dgw0", "dgw1", "da")
    wait(1, "du")
    final.wait()


def last_attention(active_ref, cos_ref, sin_ref, gain_one, q_ref, kz_ref, vz_ref, p_ref, d_attn_ref, small_in, out_w,
                   x_hbm, base_hbm, state_hbm, qkv_hbm, du_in, token, du_ref, d_input_ref, small_ref,
                   do_ref, total, x, base, state, qkv_w, sems):
    copies = load_all([(qkv_hbm, qkv_w), (x_hbm, x), (base_hbm, base), (state_hbm, state)], sems)
    for copy in copies:
        copy.start()
    attention_backward(d_attn_ref.at[0, 0], out_w, qkv_w, cos_ref, sin_ref, q_ref, kz_ref, vz_ref, p_ref, do_ref, du_ref.at[0])
    for copy in copies:
        copy.wait()
    term = finish_attention_backward(x, gain_one[...], active_ref.at[0], du_ref.at[0], qkv_w, base, state, total, d_input_ref)
    small_ref[...] = small_in[...]
    small_ref[0:1, :] = small_in[0:1, :] + term


def swap_dp(values_in, bit, n_dp):
    return lax.ppermute(values_in, "dp", [(i, i ^ (1 << bit)) for i in range(n_dp)])


def swap_mp(values_in):
    return lax.ppermute(values_in, "mp", [(0, 1), (1, 0)])


def halving(parts, order, n_dp, index):
    bits = n_dp.bit_length() - 1
    left = list(range(bits - 1, -1, -1))
    shape = parts.shape[1:]
    held = parts.reshape((2,) * bits + shape)
    for step, bit in enumerate(order):
        at = left.index(bit)
        upper = ((index >> bit) & 1) == 1
        low = lax.index_in_dim(held, 0, at, keepdims=False)
        high = lax.index_in_dim(held, 1, at, keepdims=False)
        keep, send = jnp.where(upper, high, low), jnp.where(upper, low, high)
        got = swap_dp(send, bit, n_dp)
        last = step == bits - 1
        total = keep.astype(F32) + got.astype(F32)
        held = total if last else total.astype(BF)
        left.remove(bit)
    return held


def orders_of(bits):
    rest = list(range(3, bits))
    if bits < 3:
        return [list(range(bits))] * 3
    return [[0, 1, 2] + rest, [1, 0, 2] + rest, [2, 0, 1] + rest]


PART = 2 * LANES
FFN_TILES = (4, 4, 2)
FFN_ORDERS = ((2, 1, 3, 0), (1, 2, 0, 3), (2, 0, 3, 1))
ATTN_ORDER = (0, 1, 2, 3)
SCHEDULE = (
    "T0", "T1", "A", "T2",
    "F0", "F1", "A0", "F2",
    "F0", "F1", "A0", "F2",
    "F0 F1", "A0 F2",
)
SMALL = 48


def halves(bit, outs, index):
    mine = (index >> bit) & 1
    inner = 1 << bit
    for out, which in zip(outs, (mine, 1 - mine)):
        for p in range(out.shape[0]):
            for q in range(inner):
                yield out, p, q, p * 2 * inner + which * inner + q


def stacked_copies(pairs, sems):
    flat_pairs = []
    for sources, target in pairs:
        rows = target.shape[0] // 2
        flat_pairs += [(source, target.at[pl.ds(i * rows, rows)]) for i, source in enumerate(sources)]
    copies = load_all(flat_pairs, sems)
    for copy in copies:
        copy.start()
    return [copies[i : i + 2] for i in range(0, len(copies), 2)]


def ffn_terms(bit, tiles, at, at_b, n2_df_a, n2_df_b, units_a, units_b, token, keep_ref, send_ref, left, gate_up, down, flat, sems):
    width, part = left.shape[2], down.shape[1]
    columns, columns_b = (pl.ds(start, tiles * LANES) for start in (at, at_b))
    lefts = [(n2_df_a.at[i], n2_df_b.at[i]) for i in range(2)]
    m, dg, dw = [(units_a.at[i, :, columns], units_b.at[i, :, columns_b]) for i in range(3)]
    n2, dg, dw, df, m = stacked_copies(
        [(lefts[0], left.at[0]), (dg, gate_up.at[:, :part]), (dw, gate_up.at[:, part:]), (lefts[1], left.at[1]), (m, down)], sems)
    for which, (right, needed) in enumerate(((gate_up, n2 + dg + dw), (down, df + m))):
        for copy in needed:
            copy.wait()
        terms = contract_rows(left[which], right[...])
        for at_lane in range(0, right.shape[1], LANES):
            matrix, c = divmod(at_lane // LANES, tiles)
            start = tiles * width * (2 * which + matrix) + c
            flat[pl.ds(start, width, stride=tiles), :] = terms[:, at_lane : at_lane + LANES]
    rows = keep_ref.shape[2]
    for out, p, q, shard in halves(bit, (keep_ref, send_ref), lax.axis_index("dp")):
        out[p, q] = flat[pl.ds(pl.multiple_of(shard * rows, 8), rows), :].astype(BF)


def small_rows(small, packed):
    packed[...] = jnp.zeros(packed.shape, F32)
    width = small.shape[1]
    for i in range(2 + RECURSIONS):
        for c in range(CHUNKS):
            stop = min(width, (c + 1) * LANES)
            packed[i * CHUNKS + c : i * CHUNKS + c + 1, : stop - c * LANES] = small[i : i + 1, c * LANES : stop]
    return packed[...]


def split_small(small, ref, start):
    high = small.astype(BF)
    ref[start : start + SMALL, :] = high
    ref[start + SMALL : start + 2 * SMALL, :] = (small - high.astype(F32)).astype(BF)


def rounded_small(small):
    high = small.astype(BF)
    return high.astype(F32) + (small - high.astype(F32)).astype(BF).astype(F32)


def joined_small(ref, start):
    return ref[start : start + SMALL, :].astype(F32) + ref[start + SMALL : start + 2 * SMALL, :].astype(F32)


def attn_terms(bit, depth, n1_a, n1_b, du_a, du_b, o_da_a, o_da_b, small_a, small_b, token,
               keep, send, small_out, left, du_rows, da_rows, turned, own, terms, flat, packed, sems):
    base, count = 0, own.shape[0] // 2
    lower = lane_of(count) < HEAD_DIM
    core = lax.axis_index("mp")
    n1, du, o, da = stacked_copies(
        [((n1_a, n1_b), left.at[0]), ((du_a, du_b), du_rows), ((o_da_a.at[0], o_da_b.at[0]), left.at[1]),
         ((o_da_a.at[1], o_da_b.at[1]), da_rows)], sems)
    for which, (right, needed) in enumerate(((du_rows, n1 + du), (da_rows, o + da))):
        for copy in needed:
            copy.wait()
        columns = right.shape[1]
        half = columns // LANES
        turned[...] = left[which].T
        group = depth * LANES // columns
        for i in range(own.shape[0] // group):
            own[i * group : (i + 1) * group, :] = turned[pl.ds(pl.multiple_of((2 * i + core) * group, 16), group), :]
        for start in range(0, columns, PART):
            stop = min(columns, start + PART)
            block = plain(own[...], right[:, start:stop])
            if stop - start < PART:
                block = jnp.concatenate([block, jnp.zeros((2 * count, PART - (stop - start)), F32)], axis=1)
            for part in range(0, stop - start, LANES):
                terms[(start + part) // LANES] = block[:, part : part + LANES]
        step = 2 * columns // LANES
        after = first_odd = None
        for c in range(half + 1):
            even = terms[c, pl.ds(0, count, stride=2), :]
            odd = other_half(terms[c, pl.ds(1, count, stride=2), :])
            if c < half:
                flat[pl.ds(base + c, count, stride=step), :] = even
            else:
                flat[pl.ds(base + c, count, stride=step), :] = jnp.where(lower, even, first_odd)
            if c == 0:
                first_odd = odd
            else:
                flat[pl.ds(base + half + c, count, stride=step), :] = jnp.where(lower, after, odd)
            after = odd
        base += 2 * count * columns // LANES
    index = lax.axis_index("dp")
    total = rounded_small(small_rows(small_a, packed.at[0])) + rounded_small(small_rows(small_b, packed.at[1]))
    small_out[...] = total
    outer, inner, rows = keep.shape[:3]
    split_small(total, send, outer * inner * rows)

    def rows_of_shard(shard):
        start = pl.multiple_of(shard * depth, 8)
        return flat[pl.ds(start, rows), :].astype(BF)

    mine = (index >> bit) & 1
    for p in range(outer):
        for q in range(inner):
            shard = 2 * p * inner + q
            keep[p, q] = rows_of_shard(shard + mine * inner)
            at = (p * inner + q) * rows
            send[at : at + rows, :] = rows_of_shard(shard + (1 - mine) * inner)


def fold(bit, kept, got, token, keep, send):
    mine = (lax.axis_index("dp") >> bit) & 1
    for p in range(kept.shape[0]):
        for q in range(kept.shape[2]):
            for out, which in ((keep, mine), (send, 1 - mine)):
                out[p, q] = (kept[p, which, q].astype(F32) + got[p, which, q].astype(F32)).astype(BF)


def fold_small(bit, kept, got, small, token, keep, send, small_out):
    mine = (lax.axis_index("dp") >> bit) & 1
    outer, _, inner, rows, _ = kept.shape
    for p in range(outer):
        for q in range(inner):
            totals = []
            for which in (mine, 1 - mine):
                start = pl.multiple_of(((2 * p + which) * inner + q) * rows, 16)
                totals.append((kept[p, which, q].astype(F32) + got[pl.ds(start, rows), :].astype(F32)).astype(BF))
            keep[p, q] = totals[0]
            at = (p * inner + q) * rows
            send[at : at + rows, :] = totals[1]
    total = rounded_small(small[...]) + joined_small(got, 2 * outer * inner * rows)
    small_out[...] = total
    split_small(total, send, outer * inner * rows)


def fold_group(folds, *refs):
    inputs, results = refs, refs[sum(n for _, n, _ in folds) + 1 :]
    token = refs[sum(n for _, n, _ in folds)]
    for function, n_in, n_out in folds:
        function(*inputs[:n_in], token, *results[:n_out])
        inputs, results = inputs[n_in:], results[n_out:]


def finish_streams(tiles, *refs):
    count = len(tiles)
    feeds, refs = refs[: 2 * count], refs[2 * count :]
    attn, refs = refs[:2], refs[2:]
    small, ffn_out, attn_out, one_out, two_out, router_out, flat, packed = refs
    every = sum(tiles)
    rows = ffn_out.shape[0] // every
    base = 0
    for i, wide in enumerate(tiles):
        flat[: rows * wide, :] = feeds[2 * i][...].astype(F32) + feeds[2 * i + 1][...].astype(F32)
        for c in range(wide):
            ffn_out[pl.ds(base + c, rows, stride=every), :] = flat[pl.ds(c, rows, stride=wide), :]
        base += wide
    padded = attn[0].shape[0]
    both = attn[0][...].astype(F32) + attn[1][:padded, :].astype(F32)
    attn_out[...] = both[: attn_out.shape[0]]
    total = rounded_small(small[...]) + joined_small(attn[1], padded)
    packed[...] = total
    width = one_out.shape[1]
    outs = [(one_out, 0), (two_out, 0), *[(router_out, i) for i in range(RECURSIONS)]]
    for i, (out, row) in enumerate(outs):
        for c in range(CHUNKS):
            stop = min(width, (c + 1) * LANES)
            out[row : row + 1, c * LANES : stop] = packed[i * CHUNKS + c : i * CHUNKS + c + 1, : stop - c * LANES]


class Stream:
    def __init__(self, order, bits):
        self.order, self.left, self.done = order, list(range(bits - 1, -1, -1)), 0
        self.kept = self.got = None

    def shape_for(self, array):
        at = self.left.index(self.order[self.done])
        rows, lanes = array.shape[-2:]
        return (1 << at, 2, 1 << (len(self.left) - 1 - at), rows, lanes)

    def sent(self, kept, send, n_dp):
        bit = self.order[self.done]
        self.kept, self.got = kept, swap_dp(send, bit, n_dp)
        self.left.remove(bit)
        self.done += 1


def on_device(
    hidden_in,
    sel_one,
    sel_two,
    sel_three,
    segment_ids,
    pad_mask,
    qkv_weight,
    out_weight,
    gate_weight,
    up_weight,
    down_weight,
    norm_one,
    norm_two,
    router_weight,
    d_hidden,
):
    seq_len, width = hidden_in.shape
    n_dp, n_mp = lax.axis_size("dp"), lax.axis_size("mp")
    dp_index, mp_index = lax.axis_index("dp"), lax.axis_index("mp")
    cosine, sine = rotary_tables(seq_len)
    weights = [(gate_weight, up_weight, down_weight)]
    weights.append(tuple(swap_mp(w) for w in weights[0]))
    gain_one, gain_two = norm_one.reshape(1, width), norm_two.reshape(1, width)
    padded = CHUNKS * LANES
    units = gate_weight.shape[1]
    feed_weights = (*weights[0], *weights[1])

    def shape(*dims, dtype=BF):
        return jax.ShapeDtypeStruct(dims, dtype)

    def whole(*dims, **kw):
        return pl.BlockSpec(dims, lambda *_: (0,) * len(dims), **kw)

    anywhere = pl.BlockSpec(memory_space=pl.ANY)
    one = pl.Buffered(1)
    stack = RECURSIONS, seq_len
    heads = (2 * KV_HEADS, seq_len, LANES)
    square = (HEADS, seq_len, seq_len)
    n1, q, kz, vz, p, o_da, attn, n2, bias, active, near, slope_first, silu_first, f_first = pl.pallas_call(
        first_attention,
        grid=(1,),
        in_specs=[
            whole(seq_len, width), *[whole(*ref.shape) for ref in (sel_one, sel_two, sel_three, segment_ids, pad_mask)],
            whole(seq_len, LANES), whole(seq_len, LANES), whole(1, width), whole(1, width), whole(*qkv_weight.shape), whole(*out_weight.shape),
            *[anywhere] * 3,
        ],
        out_specs=[
            whole(1, seq_len, width), *[anywhere] * 4, whole(1, 1, seq_len, width), whole(seq_len, width), whole(seq_len, width), whole(RECURSIONS, seq_len, seq_len), whole(*stack, 1),
            whole(1, 1, seq_len, units), whole(seq_len, units), whole(seq_len, units), whole(seq_len, width),
        ],
        out_shape=[
            shape(*stack, width), shape(seq_len, padded), shape(*heads), shape(*heads), shape(*square),
            shape(2, *stack, width), shape(seq_len, width, dtype=F32), shape(seq_len, width),
            shape(*stack, seq_len, dtype=F32), shape(*stack, 1, dtype=F32),
            shape(3, *stack, units), shape(seq_len, units), shape(seq_len, units), shape(seq_len, width, dtype=F32),
        ],
        scratch_shapes=[*[pltpu.VMEM(w.shape, BF) for w in weights[0]],
                        *[pltpu.VMEM(dims, BF) for dims in ((seq_len, padded), heads, heads, square)], pltpu.SemaphoreType.DMA((7,))],
        compiler_params=pltpu.CompilerParams(vmem_limit_bytes=VMEM_BYTES),
        cost_estimate=pl.CostEstimate(flops=2 * 10**9, bytes_accessed=12 * 10**6, transcendentals=600000),
        name="first_attention",
    )(hidden_in, sel_one, sel_two, sel_three, segment_ids, pad_mask, cosine, sine, gain_one, gain_two, qkv_weight, out_weight,
      *weights[0])
    attention_0 = (q, kz, vz, p)
    wide = qkv_weight.shape[1]
    row = (seq_len, width)
    kept = RECURSIONS - 1
    first_part = FFN_TILES[0] * LANES
    vm = pltpu.VMEM
    results = pl.pallas_call(
        all_steps,
        grid=(1,),
        in_specs=[
            whole(RECURSIONS, seq_len, seq_len), whole(RECURSIONS, seq_len, 1), whole(RECURSIONS, width),
            whole(seq_len, LANES), whole(seq_len, LANES), whole(1, width), whole(1, width), *[anywhere] * 18,
        ],
        out_specs=[*[anywhere] * 8, whole(*row), whole(*row), whole(8, width)],
        out_shape=[
            shape(*stack, width), *[shape(2, *stack, width)] * 2, shape(3, *stack, units), shape(3, *stack, first_part), shape(3, *stack, units - first_part), shape(*stack, wide),
            *[shape(*row, dtype=F32)] * 3, shape(8, width, dtype=F32),
        ],
        scratch_shapes=[
            *[vm(w.shape, BF) for w in (qkv_weight, out_weight, *feed_weights)],
            vm((RECURSIONS + 1, *row), F32), vm((RECURSIONS, *row), F32), vm((RECURSIONS, *row), BF),
            *[vm((*stack, units), BF)] * 4, vm((kept, seq_len, padded), BF), vm((kept, *heads), BF), vm((kept, *heads), BF),
            vm((kept, *square), BF), *[vm(row, BF)] * 3, *[vm((seq_len, units), BF)] * 2, vm(row, BF), *[vm((2, seq_len, units), BF)] * 2,
            vm(row, BF), vm((seq_len, wide), BF), vm(row, F32), vm(row, F32), vm((seq_len, padded), BF),
            pltpu.SemaphoreType.DMA((15,)), pltpu.SemaphoreType.DMA((13,)),
        ],
        input_output_aliases={14: 0, 15: 1, 16: 3},
        compiler_params=pltpu.CompilerParams(vmem_limit_bytes=VMEM_BYTES),
        cost_estimate=pl.CostEstimate(flops=23 * 10**9, bytes_accessed=50 * 10**6, transcendentals=4 * 10**6),
        name="all_steps",
    )(bias, active, router_weight, cosine, sine, gain_one, gain_two, hidden_in, d_hidden, attn, n2,
      slope_first, silu_first, f_first, n1, o_da, near,
      qkv_weight, out_weight, *feed_weights)
    n1, o_da, n2_df, near, far, late, du, state, base, grad_state, small = results

    def run_last(token):
        return pl.pallas_call(
            last_attention,
            grid=(1,),
            in_specs=[
                whole(1, seq_len, 1), whole(seq_len, LANES), whole(seq_len, LANES), whole(1, width),
                whole(seq_len, padded), whole(*heads), whole(*heads), whole(*square),
                pl.BlockSpec((1, 1, seq_len, width), lambda i: (1, 0, 0, 0)), whole(8, width), whole(*out_weight.shape), *[anywhere] * 6,
            ],
            out_specs=[whole(1, seq_len, qkv_weight.shape[1]), whole(seq_len, width), whole(8, width)],
            out_shape=[shape(*stack, qkv_weight.shape[1]), shape(seq_len, width, dtype=F32), shape(8, width, dtype=F32)],
            scratch_shapes=[
                pltpu.VMEM((seq_len, padded), BF), *[pltpu.VMEM((seq_len, width), F32)] * 4,
                pltpu.VMEM(qkv_weight.shape, BF), pltpu.SemaphoreType.DMA((4,)),
            ],
            input_output_aliases={15: 0},
            compiler_params=pltpu.CompilerParams(vmem_limit_bytes=VMEM_BYTES),
            cost_estimate=pl.CostEstimate(flops=1, bytes_accessed=1, transcendentals=0),
            name="last_attention",
        )(active, cosine, sine, gain_one, *attention_0, o_da, small, out_weight, hidden_in, base, grad_state, qkv_weight, du, token)

    def rows_of(stacked):
        return stacked.reshape(*stacked.shape[:-3], -1, stacked.shape[-1])

    bits = n_dp.bit_length() - 1
    share = (qkv_weight.size + out_weight.size) // (n_dp * n_mp)
    if bits == 4 and 3 * width % n_dp == 0 and units == sum(FFN_TILES) * LANES and share % (16 * qkv_weight.shape[1]) == share % (16 * width) == 0:
        n2_df_rows = [rows_of(t) for t in (n2_df, swap_mp(n2_df))]
        near, far_b = rows_of(near), rows_of(swap_mp(far))
        n1_b = rows_of(swap_mp(n1))
        streams = [Stream(order, bits) for order in FFN_ORDERS]
        attn_stream = Stream(ATTN_ORDER, bits)
        depth = share // LANES
        tiled = -(-depth // 16) * 16
        common = dict(
            grid=(1,),
            compiler_params=pltpu.CompilerParams(vmem_limit_bytes=VMEM_BYTES),
            cost_estimate=pl.CostEstimate(flops=1, bytes_accessed=1, transcendentals=0),
        )

        def wholes(arrays):
            return [whole(*t.shape) for t in arrays]

        def terms_of(j, token):
            stream, tiles = streams[j], FFN_TILES[j]
            at = sum(FFN_TILES[:j]) * LANES
            factors = (*n2_df_rows, near, far_b if j == 0 else late_b)
            bit = stream.order[0]
            dims = (1 << (bits - 1 - bit), 1 << bit, 3 * width // n_dp * tiles, LANES)
            both = 2 * RECURSIONS * seq_len
            keep, send = pl.pallas_call(
                functools.partial(ffn_terms, bit, tiles, at, 0 if j == 0 else at - first_part),
                in_specs=[anywhere] * (len(factors) + 1),
                out_specs=[whole(*dims)] * 2,
                out_shape=[shape(*dims)] * 2,
                scratch_shapes=[pltpu.VMEM((2, both, width), BF), *[pltpu.VMEM((both, n * tiles * LANES), BF) for n in (2, 1)],
                                pltpu.VMEM((3 * width * tiles, LANES), F32), pltpu.SemaphoreType.DMA((10,))],
                name=f"ffn_terms_{j}",
                **common,
            )(*factors, token)
            stream.sent(keep, send, n_dp)
            return keep

        def fold_streams(group, token, small_own):
            folds, operands, outs = [], [], []
            for stream in group:
                bit = stream.order[stream.done]
                dims = stream.shape_for(stream.kept)
                kept = stream.kept.reshape(dims)
                held = (dims[0], *dims[2:])
                if stream is attn_stream:
                    operands += [kept, stream.got, small_own]
                    outs += [shape(*held), shape(dims[0] * dims[2] * dims[3] + 2 * SMALL, LANES), shape(SMALL, LANES, dtype=F32)]
                    folds.append((functools.partial(fold_small, bit), 3, 3))
                else:
                    operands += [kept, stream.got.reshape(dims)]
                    outs += [shape(*held), shape(*held)]
                    folds.append((functools.partial(fold, bit), 2, 2))
            results = pl.pallas_call(
                functools.partial(fold_group, folds),
                in_specs=[*wholes(operands), anywhere],
                out_specs=wholes(outs),
                out_shape=outs,
                name="fold_terms",
                **common,
            )(*operands, token)
            token = results[0]
            for stream, (_, _, n_out) in zip(group, folds):
                stream.sent(results[0], results[1], n_dp)
                small_own = results[2] if n_out == 3 else small_own
                results = results[n_out:]
            return token, small_own

        du, grad_state, small = run_last(small)
        late, du, small = lax.optimization_barrier((late, du, small))
        late_b, du_b = rows_of(swap_mp(late)), rows_of(swap_mp(du))
        token, small_own = small, None
        for item in SCHEDULE:
            if item[0] == "T":
                token = terms_of(int(item[1:]), token)
                if item == "T0":
                    o_da, small, token = lax.optimization_barrier((o_da, small, token))
                    o_da_b, small_b = rows_of(swap_mp(o_da)), swap_mp(small)
            elif item == "A":
                bit = attn_stream.order[0]
                dims = (1 << (bits - 1 - bit), 1 << bit, tiled, LANES)
                operands = (rows_of(n1), n1_b, rows_of(du), du_b, rows_of(o_da), o_da_b, small, small_b)
                outs = (shape(*dims), shape(n_dp // 2 * tiled + 2 * SMALL, LANES), shape(SMALL, LANES, dtype=F32))
                keep, send, small_own = pl.pallas_call(
                    functools.partial(attn_terms, bit, depth),
                    in_specs=[*[anywhere] * 6, *wholes(operands[6:]), anywhere],
                    out_specs=wholes(outs),
                    out_shape=outs,
                    scratch_shapes=[pltpu.VMEM((2, 2 * RECURSIONS * seq_len, width), BF),
                                    *[pltpu.VMEM((2 * RECURSIONS * seq_len, t.shape[-1]), BF) for t in (du, o_da)],
                                    pltpu.VMEM((width, 2 * RECURSIONS * seq_len), BF),
                                    pltpu.VMEM((width // 2, 2 * RECURSIONS * seq_len), BF),
                                    pltpu.VMEM((-(-du.shape[-1] // PART) * 2, width // 2, LANES), F32),
                                    pltpu.VMEM((n_dp * depth + tiled - depth, LANES), F32), pltpu.VMEM((2, SMALL, LANES), F32),
                                    pltpu.SemaphoreType.DMA((8,))],
                    name="attn_terms",
                    **common,
                )(*operands, token)
                attn_stream.sent(keep, send, n_dp)
                token = small_own
            else:
                group = [attn_stream if name == "A0" else streams[int(name[1:])] for name in item.split()]
                token, small_own = fold_streams(group, token, small_own)
        ends = [t.reshape(t.shape[-2:]) for stream in (*streams, attn_stream) for t in (stream.kept, stream.got)]
        outs = (shape(3 * width // n_dp * sum(FFN_TILES), LANES, dtype=F32), shape(depth, LANES, dtype=F32),
                shape(1, width, dtype=F32), shape(1, width, dtype=F32), shape(RECURSIONS, width, dtype=F32))
        ffn_flat, attn_flat, one, two, router = pl.pallas_call(
            functools.partial(finish_streams, FFN_TILES),
            in_specs=wholes((*ends, small_own)),
            out_specs=wholes(outs),
            out_shape=outs,
            scratch_shapes=[pltpu.VMEM((3 * width // n_dp * max(FFN_TILES), LANES), F32), pltpu.VMEM((SMALL, LANES), F32)],
            name="finish_streams",
            **common,
        )(*ends, small_own)
        return (state, grad_state, attn_flat.reshape(-1), ffn_flat.reshape(1, -1), one.reshape(-1), two.reshape(-1), router)

    du, grad_state, small = run_last(small)
    two, feed = rows_of(n2_df)
    o, d_attn = rows_of(o_da)
    far = jnp.concatenate([far, late], axis=-1)
    sides = [[t[i] for i in (1, 2, 0)] for t in (rows_of(near), rows_of(far))]

    def side_terms(side, columns):
        return jnp.concatenate(
            [
                contract_rows(left, sides[side][which][:, columns]).astype(BF)
                for which, left in enumerate((two, two, feed))
            ],
            axis=0,
        )

    orders = orders_of(bits)
    if 3 * width % n_dp == 0 and units % 1280 == 0:
        fifth = units // 5
        streams = [(orders[i], slice(j * fifth, (j + 1) * fifth)) for i, j in ((0, 0), (1, 1), (2, 2), (0, 3), (1, 4))]
        done = []
        for order, columns in streams:
            terms = side_terms(0, columns).astype(F32) + swap_mp(side_terms(1, columns)).astype(F32)
            done.append(halving(terms.astype(BF).reshape(n_dp, 3 * width // n_dp, fifth), order, n_dp, dp_index))
        ffn_flat = jnp.concatenate(done, axis=1).reshape(1, -1)
    else:
        terms = side_terms(0, slice(None)).astype(F32) + swap_mp(side_terms(1, slice(None))).astype(F32)
        terms = terms.astype(BF).reshape(n_dp, 3 * width * units // n_dp // 128, 128)
        ffn_flat = halving(terms, orders[0], n_dp, dp_index).reshape(1, -1)

    grad_qkv = contract_rows(rows_of(n1), rows_of(du)).astype(BF)
    grad_out = contract_rows(o, d_attn).astype(BF)
    attn = jnp.concatenate([grad_qkv.reshape(-1), grad_out.reshape(-1)]).reshape(n_dp, 2, share // 128, 128)
    keep = jnp.where(mp_index == 0, attn[:, 0], attn[:, 1])
    send = jnp.where(mp_index == 0, attn[:, 1], attn[:, 0])
    attn = (keep.astype(F32) + swap_mp(send).astype(F32)).astype(BF)
    cuts = [0, (share // 128) // 24 * 8, (share // 128) // 12 * 8, share // 128]
    attn_flat = jnp.concatenate(
        [halving(attn[:, a:b], order, n_dp, dp_index) for a, b, order in zip(cuts, cuts[1:], orders)], axis=0
    ).reshape(-1)

    small = small + swap_mp(small)
    for bit in range(bits):
        small = small + swap_dp(small, bit, n_dp)
    return (state, grad_state, attn_flat, ffn_flat, small[0], small[1], small[2 : 2 + RECURSIONS])


def solution(mesh):
    both = P(("dp", "mp"), None)
    in_specs = (
        both,
        both,
        both,
        both,
        both,
        both,
        P(),
        P(),
        P(None, "mp"),
        P(None, "mp"),
        P(None, "mp"),
        P(),
        P(),
        P(),
        both,
    )
    out_specs = (both, both, P(("dp", "mp")), P("mp", "dp"), P(), P(), P())
    return jax.shard_map(
        on_device, mesh=mesh, in_specs=in_specs, out_specs=out_specs, check_vma=False
    )
```

```python
import functools
import math

import jax
import jax.numpy as jnp
import numpy as np
from jax import lax
from jax.experimental import pallas as pl
from jax.experimental.pallas import tpu as pltpu
from jax.sharding import PartitionSpec as P

HEADS = 15
KV_HEADS = 5
HEAD_DIM = 64
RECURSIONS = 3
GROUPS = HEADS // KV_HEADS
EPS = 1e-05
BF = jnp.bfloat16
F32 = jnp.float32


LANES = 128
CHUNKS = -(-HEADS * HEAD_DIM // LANES)
ROWS = 192
BLOCK = 256
MIB = 1 << 20
VMEM_BYTES = 64 * MIB - 65536


def rotary_tables(seq_len):
    half = HEAD_DIM // 2
    frequency = np.float32(100000.0) ** (
        np.float32(-2.0) * np.arange(half, dtype=np.float32) / np.float32(HEAD_DIM)
    )
    angles = np.arange(seq_len, dtype=np.float32)[:, None] * frequency.astype(np.float32)
    cosine, sine = np.cos(angles), np.sin(angles)
    return (
        jnp.asarray(np.concatenate([cosine] * 4, axis=1), F32),
        jnp.asarray(np.concatenate([-sine, sine] * 2, axis=1), F32),
    )


def contract_rows(left, right):
    return lax.dot_general(left, right, (((0,), (0,)), ((), ())), preferred_element_type=F32)


def contract_last(left, right):
    return lax.dot_general(left, right, (((1,), (1,)), ((), ())), preferred_element_type=F32)


def plain(left, right):
    return jnp.dot(left, right, preferred_element_type=F32)


def inverse_rms(rows):
    return lax.rsqrt(jnp.mean(rows * rows, axis=-1, keepdims=True) + EPS)


def norm_back(rows, gain, d_out):
    inv = inverse_rms(rows)
    scaled = d_out * gain
    inner = jnp.mean(scaled * rows, axis=-1, keepdims=True)
    d_rows = inv * scaled - rows * (inv * inv * inv * inner)
    return d_rows, jnp.sum(d_out * rows * inv, axis=0, keepdims=True)


def lane_of(rows):
    return lax.broadcasted_iota(jnp.int32, (rows, LANES), 1)


def swapped(chunk):
    first = lane_of(chunk.shape[0]) % HEAD_DIM < HEAD_DIM // 2
    return jnp.where(first, pltpu.roll(chunk, LANES - 32, 1), pltpu.roll(chunk, 32, 1))


def other_half(chunk):
    return pltpu.roll(chunk, HEAD_DIM, 1)


def over_rows(count, body):
    def lap(i, carry):
        body(pl.ds(pl.multiple_of(i * ROWS, ROWS), ROWS))
        return carry

    lax.fori_loop(0, count // ROWS, lap, 0)


def attention_forward(x_ref, bias_ref, cos_ref, sin_ref, gain, qkv_w, n1_ref, q_ref, kz_ref, vz_ref, p_ref, o_ref):
    seq_len, width = x_ref.shape
    scale = 1.0 / math.sqrt(HEAD_DIM)

    def norm(rows):
        x = x_ref[rows, :]
        n1_ref[rows, :] = (x * inverse_rms(x) * gain).astype(BF)

    over_rows(seq_len, norm)
    lower = lane_of(seq_len) < HEAD_DIM
    n1 = n1_ref[...]

    def spread(ref, head, chunk, upper):
        flipped = other_half(chunk)
        here, there = (flipped, chunk) if upper else (chunk, flipped)
        ref[2 * head] = jnp.where(lower, here, 0.0).astype(BF)
        ref[2 * head + 1] = jnp.where(lower, 0.0, there).astype(BF)

    columns = qkv_w.shape[1]
    for start in range(0, columns, 2 * LANES):
        wide = plain(n1, qkv_w[:, start : min(start + 2 * LANES, columns)])
        for part in range(0, wide.shape[1], LANES):
            chunk = wide[:, part : part + LANES]
            if chunk.shape[1] < LANES:
                chunk = jnp.concatenate([chunk, jnp.zeros_like(chunk)], axis=1)
            at = (start + part) // LANES
            heads = (2 * at, 2 * at + 1)
            if heads[0] < HEADS + KV_HEADS:
                chunk = chunk * cos_ref[...] + swapped(chunk) * sin_ref[...]
                if heads[0] < HEADS:
                    q_ref[:, at * LANES : (at + 1) * LANES] = chunk.astype(BF)
            for upper, head in enumerate(heads):
                if HEADS <= head < HEADS + KV_HEADS:
                    spread(kz_ref, head - HEADS, chunk, upper)
                elif HEADS + KV_HEADS <= head < HEADS + 2 * KV_HEADS:
                    spread(vz_ref, head - HEADS - KV_HEADS, chunk, upper)

    for at in range(CHUNKS):
        query = q_ref[:, at * LANES : (at + 1) * LANES]
        total = None
        for upper in range(2):
            head = 2 * at + upper
            if head < HEADS:
                key = 2 * (head // GROUPS) + upper
                scores = contract_last(query, kz_ref[key]) * scale + bias_ref[...]
                top = jnp.max(scores, axis=-1, keepdims=True)
                exponent = jnp.exp(scores - top)
                share = pl.reciprocal(jnp.sum(exponent, axis=-1, keepdims=True))
                attend = (exponent * share).astype(BF)
                p_ref[head] = attend
                mixed = plain(attend, vz_ref[key])
                total = mixed if total is None else total + mixed
        stop = min(width, (at + 1) * LANES)
        o_ref[:, at * LANES : stop] = total[:, : stop - at * LANES].astype(BF)


def attention_out(x_ref, o_ref, out_w, gain, attn_ref, n2_ref):
    attn_ref[...] = plain(o_ref[...], out_w[...])

    def norm(rows):
        after = x_ref[rows, :] + attn_ref[rows, :]
        n2_ref[rows, :] = (after * inverse_rms(after) * gain).astype(BF)

    over_rows(x_ref.shape[0], norm)


def feed_side(n2_ref, weights, results, ready):
    n2 = n2_ref[...]
    gate_w, up_w, down_w = weights
    m_ref, slope_ref, silu_ref = results
    ready(0, 1)
    for start in range(0, gate_w.shape[1], BLOCK):
        at = slice(start, start + BLOCK)
        g, u = plain(n2, gate_w[:, at]), plain(n2, up_w[:, at])
        s = jax.nn.sigmoid(g)
        silu = g * s
        m_ref[:, at] = (silu * u).astype(BF)
        slope_ref[:, at] = (u * s * (1.0 + g * (1.0 - s))).astype(BF)
        silu_ref[:, at] = silu.astype(BF)
    ready(2)
    return contract_last(m_ref[...], down_w[...])


def feed_backward(df_ref, sides, d_two_ref, ready):
    d_feed = df_ref[...]
    for side, (gate_w, up_w, down_w, slope_ref, silu_ref, dg_ref, du_ref) in enumerate(sides):
        ready(3 * side)
        for start in range(0, gate_w.shape[1], BLOCK):
            at = slice(start, start + BLOCK)
            d_hidden = plain(d_feed, down_w[:, at])
            dg_ref[:, at] = (d_hidden * slope_ref[:, at].astype(F32)).astype(BF)
            du_ref[:, at] = (d_hidden * silu_ref[:, at].astype(F32)).astype(BF)
        ready(3 * side + 1, 3 * side + 2)
        part = contract_last(dg_ref[...], gate_w[...]) + contract_last(du_ref[...], up_w[...])
        d_two_ref[...] = part if side == 0 else d_two_ref[...] + part


def attention_backward(d_attn_ref, out_w, qkv_w, cos_ref, sin_ref, q_ref, kz_ref, vz_ref, p_ref, do_ref, du_ref):
    seq_len, width = d_attn_ref.shape
    scale = 1.0 / math.sqrt(HEAD_DIM)
    do_ref[:, :width] = contract_last(d_attn_ref[...], out_w[...]).astype(BF)
    do_ref[:, width:] = jnp.zeros((seq_len, do_ref.shape[1] - width), BF)
    lower = lane_of(seq_len) < HEAD_DIM
    cosine, sine = cos_ref[...], sin_ref[...]

    def back(chunk):
        chunk = chunk * scale
        return chunk * cosine - swapped(chunk) * sine

    waiting, d_k, d_v = None, {}, {}
    for at in range(CHUNKS):
        query, d_mixed = (ref[:, at * LANES : (at + 1) * LANES] for ref in (q_ref, do_ref))
        query_t, d_mixed_t = query.T, d_mixed.T
        d_query = None
        for upper in range(2):
            head = 2 * at + upper
            if head >= HEADS:
                continue
            group = head // GROUPS
            key = 2 * group + upper
            rows = slice(upper * HEAD_DIM, (upper + 1) * HEAD_DIM)
            attend = p_ref[head]
            d_attend = contract_last(d_mixed, vz_ref[key])
            soft = attend.astype(F32)
            weighted = soft * d_attend
            inner = jnp.sum(weighted, axis=-1, keepdims=True)
            d_scores = (weighted - soft * inner).astype(BF)
            part = plain(d_scores, kz_ref[key])
            d_query = part if d_query is None else d_query + part
            for store, term in ((d_k, plain(query_t[rows], d_scores)), (d_v, plain(d_mixed_t[rows], attend))):
                store[group] = term if group not in store else store[group] + term
        if at < CHUNKS - 1:
            du_ref[:, at * LANES : (at + 1) * LANES] = back(d_query).astype(BF)
        else:
            waiting = d_query

    def two_heads(store, first, second):
        return jnp.concatenate([store[first], store[second]], axis=0).T

    tail = jnp.where(lower, waiting, two_heads(d_k, 0, 0))
    du_ref[:, (CHUNKS - 1) * LANES : CHUNKS * LANES] = back(tail).astype(BF)
    for i in range(2):
        at = CHUNKS + i
        du_ref[:, at * LANES : (at + 1) * LANES] = back(two_heads(d_k, 1 + 2 * i, 2 + 2 * i)).astype(BF)
        at = CHUNKS + 2 + i
        du_ref[:, at * LANES : (at + 1) * LANES] = two_heads(d_v, 2 * i, 2 * i + 1).astype(BF)
    at = CHUNKS + 4
    du_ref[:, at * LANES :] = two_heads(d_v, 4, 4)[:, : du_ref.shape[1] - at * LANES].astype(BF)


def router_gate(x, router_row):
    return jax.nn.sigmoid(jnp.sum(x * router_row, axis=-1, keepdims=True))


def masks(select_refs, segment_ref, pad_ref, bias_ref, active_ref):
    seq_len = segment_ref.shape[1]
    square = (seq_len, seq_len)
    query, key = (lax.broadcasted_iota(jnp.int32, square, axis) for axis in (0, 1))
    diagonal = query == key
    segment = segment_ref[...].astype(F32)
    own = jnp.sum(jnp.where(diagonal, segment, 0.0), axis=1, keepdims=True)
    near = (key <= query) & (segment == own)
    real = pad_ref[...] == 1
    for recursion, ref in enumerate(select_refs):
        place = lax.broadcasted_iota(jnp.int32, (seq_len, ref.shape[1]), 0)
        active = jnp.max(jnp.where(ref[...] == place, 1.0, 0.0), axis=1, keepdims=True)
        active_ref[recursion] = active
        along = jnp.sum(jnp.where(diagonal, active, 0.0), axis=0, keepdims=True)
        usable = (along > 0.0) & real
        bias_ref[recursion] = jnp.where(near & (usable | diagonal), 0.0, -1e30)


def first_attention(x_ref, sel_one, sel_two, sel_three, segment_ref, pad_ref, cos_ref, sin_ref, gain_one, gain_two, qkv_w, out_w,
                    gate_hbm, up_hbm, down_hbm, n1_ref, q_ref, kz_ref, vz_ref, p_ref, o_ref, attn_ref, n2_ref, bias_ref, active_ref,
                    m_ref, slope_ref, silu_ref, f_ref, gate_w, up_w, down_w, sems):
    copies = load_all([(gate_hbm, gate_w), (up_hbm, up_w), (down_hbm, down_w)], sems)
    for copy in copies:
        copy.start()
    n1, o = n1_ref.at[0], o_ref.at[0, 0]
    masks((sel_one, sel_two, sel_three), segment_ref, pad_ref, bias_ref, active_ref)
    attention_forward(x_ref, bias_ref.at[0], cos_ref, sin_ref, gain_one[...], qkv_w, n1, q_ref, kz_ref, vz_ref, p_ref, o)
    attention_out(x_ref, o, out_w, gain_two[...], attn_ref, n2_ref)

    def ready(*which):
        for i in which:
            copies[i].wait()

    f_ref[...] = feed_side(n2_ref, (gate_w, up_w, down_w), (m_ref.at[0, 0], slope_ref, silu_ref), ready)


def load_all(pairs, sems):
    return [pltpu.make_async_copy(src, dst, sems.at[i]) for i, (src, dst) in enumerate(pairs)]


def waits_at(condition, copies):
    def ready(*which):
        @pl.when(condition)
        def _():
            for i in which:
                copies[i].wait()

    return ready


def finish_attention_backward(x_ref, gain, active_ref, du_ref, qkv_w, base, state, total, out_ref):
    total[...] = contract_last(du_ref[...], qkv_w[...])
    terms = jnp.zeros((1, state.shape[1]), F32)

    def lap(i, terms):
        rows = pl.ds(pl.multiple_of(i * ROWS, ROWS), ROWS)
        d_rows, term = norm_back(x_ref[rows, :], gain, total[rows, :])
        new = jnp.where(active_ref[rows, :] > 0, base[rows, :] + d_rows, state[rows, :])
        out_ref[rows, :] = new
        return terms + term

    return lax.fori_loop(0, state.shape[0] // ROWS, lap, terms)


def all_steps(bias_ref, active_ref, router_ref, cos_ref, sin_ref, gain_one, gain_two,
              hidden_hbm, d_hidden_hbm, attn0_hbm, n20_hbm, slope_hbm, silu_hbm, f_hbm, n1_in, o_da_in, near_in,
              qkv_hbm, out_hbm, *rest):
    feed_hbm, rest = rest[:6], rest[6:]
    (n1_out, o_da_out, n2_df_out, near_out, far_out, late_out, du_out, final_out, base_ref, state_ref, small_ref), rest = rest[:11], rest[11:]
    qkv_w, out_w, *feed_w = rest[:8]
    (xs, attns, fs, slope0, slope1, silu0, silu1, qs, kzs, vzs, ps, n1, o, n2, m0, m1, df, dg0, dg1, dw0, dw1, da, du,
     total, d_branch, do_ref, load_sems, out_sems) = rest[8:]
    width = state_ref.shape[1]
    first_part = far_out.shape[3]
    laps = state_ref.shape[0] // ROWS
    loads = load_all(
        [*zip(feed_hbm, feed_w), (qkv_hbm, qkv_w), (out_hbm, out_w),
         (n20_hbm, n2), (attn0_hbm, attns.at[0]), (hidden_hbm, xs.at[0]), (d_hidden_hbm, state_ref),
         (f_hbm, total), (slope_hbm, slope0.at[0]), (silu_hbm, silu0.at[0])], load_sems)
    for i in (8, 3, 4, 5, 12, 9, 10, 6, 7, 0, 1, 2, 13, 14, 11):
        loads[i].start()
    loads[8].wait()

    places = dict(n2=[(n2, n2_df_out.at[0])], m0=[(m0, near_out.at[0])], n1=[(n1, n1_out)], o=[(o, o_da_out.at[0])],
                  df=[(df, n2_df_out.at[1])], dg0=[(dg0, near_out.at[1])], dw0=[(dw0, near_out.at[2])],
                  da=[(da, o_da_out.at[1])], du=[(du, du_out)])
    for i, (name, ref) in enumerate((("m1", m1), ("dg1", dg1), ("dw1", dw1))):
        places[name] = [(ref.at[:, :first_part], far_out.at[i]), (ref.at[:, first_part:], late_out.at[i])]
    numbers = {}
    for pairs in places.values():
        for source, target in pairs:
            numbers[id(target)] = len(numbers)

    def leaving(recursion, names):
        return [pltpu.make_async_copy(source, target.at[recursion], out_sems.at[numbers[id(target)]])
                for name in names for source, target in places[name]]

    def start(recursion, *names):
        for copy in leaving(recursion, names):
            copy.start()

    def wait(recursion, *names):
        for copy in leaving(recursion, names):
            copy.wait()

    def forward(r, carry):
        ready, later = (waits_at(r == step, loads) for step in range(2))
        start(r, "n2")

        @pl.when(r > 0)
        def _():
            @pl.when(r > 1)
            def _():
                wait(r - 1, "m0")

            total[...] = feed_side(n2, feed_w[:3], (m0, slope0.at[r], silu0.at[r]), later)
            start(r, "m0")
            wait(r - 1, "m1")

        part = feed_side(n2, feed_w[3:], (m1, slope1.at[r], silu1.at[r]), lambda *which: ready(*[3 + i for i in which]))
        ready(12)
        total[...] = total[...] + part
        start(r, "m1")
        ready(9, 10)
        router_row = router_ref[pl.ds(r, 1), :]

        def finish(rows):
            x = xs[r, rows, :]
            f = total[rows, :].astype(BF)
            fs[r, rows, :] = f
            branch = attns[r, rows, :] + f.astype(F32)
            xs[r + 1, rows, :] = jnp.where(active_ref[r, rows, :] > 0, x + router_gate(x, router_row) * branch, x)

        over_rows(total.shape[0], finish)
        ready(6, 7)
        wait(r, "n2")

        @pl.when(r < RECURSIONS - 1)
        def _():
            @pl.when(r > 0)
            def _():
                wait(r, "n1", "o")

            attention_forward(xs.at[r + 1], bias_ref.at[r + 1], cos_ref, sin_ref, gain_one[...], qkv_w,
                              n1, qs.at[r], kzs.at[r], vzs.at[r], ps.at[r], o)
            start(r + 1, "n1", "o")
            attention_out(xs.at[r + 1], o, out_w, gain_two[...], attns.at[r + 1], n2)

        return carry

    lax.fori_loop(0, RECURSIONS, forward, 0)
    final = pltpu.make_async_copy(xs.at[RECURSIONS], final_out, out_sems.at[15])
    final.start()
    for i in (11, 13, 14):
        loads[i].wait()
    small_ref[...] = jnp.zeros(small_ref.shape, F32)

    def backward(i, carry):
        r = RECURSIONS - 1 - i
        router_row = router_ref[pl.ds(r, 1), :]

        @pl.when(i > 0)
        def _():
            wait(r + 1, "df", "dg0", "dg1", "dw0", "dw1", "da")

        def enter(lap, terms):
            rows = pl.ds(pl.multiple_of(lap * ROWS, ROWS), ROWS)
            x = xs[r, rows, :]
            d_new = jnp.where(active_ref[r, rows, :] > 0, state_ref[rows, :], 0.0)
            gate = router_gate(x, router_row)
            branch = attns[r, rows, :] + fs[r, rows, :].astype(F32)
            d_gate = jnp.sum(d_new * branch, axis=-1, keepdims=True)
            d_logit = d_gate * gate * (1.0 - gate)
            spread = gate * d_new
            d_branch[rows, :] = spread
            df[rows, :] = spread.astype(BF)
            base_ref[rows, :] = d_new + d_logit * router_row
            return terms + jnp.sum(d_logit * x, axis=0, keepdims=True)

        small_ref[pl.ds(2 + r, 1), :] = lax.fori_loop(0, laps, enter, jnp.zeros((1, width), F32))
        start(r, "df")
        feed_backward(df, ((*feed_w[:3], slope0.at[r], silu0.at[r], dg0, dw0), (*feed_w[3:], slope1.at[r], silu1.at[r], dg1, dw1)),
                      total, lambda *which: None)
        start(r, "dg0", "dg1", "dw0", "dw1")

        def leave(lap, terms):
            rows = pl.ds(pl.multiple_of(lap * ROWS, ROWS), ROWS)
            after = xs[r, rows, :] + attns[r, rows, :]
            d_after, term = norm_back(after, gain_two[...], total[rows, :].astype(BF).astype(F32))
            da[rows, :] = (d_branch[rows, :] + d_after).astype(BF)
            base_ref[rows, :] = base_ref[rows, :] + d_after
            return terms + term

        small_ref[1:2, :] = small_ref[1:2, :] + lax.fori_loop(0, laps, leave, jnp.zeros((1, width), F32))
        start(r, "da")

        @pl.when(r > 0)
        def _():
            @pl.when(i > 0)
            def _():
                wait(r + 1, "du")

            attention_backward(da, out_w, qkv_w, cos_ref, sin_ref, qs.at[r - 1], kzs.at[r - 1], vzs.at[r - 1], ps.at[r - 1], do_ref, du)
            start(r, "du")
            term = finish_attention_backward(xs.at[r], gain_one[...], active_ref.at[r], du, qkv_w, base_ref, state_ref, total, state_ref)
            small_ref[0:1, :] = small_ref[0:1, :] + term

        return carry

    lax.fori_loop(0, RECURSIONS, backward, 0)
    wait(RECURSIONS - 1, "m0", "m1", "n1", "o")
    wait(0, "df", "dg0", "dg1", "dw0", "dw1", "da")
    wait(1, "du")
    final.wait()


def last_attention(active_ref, cos_ref, sin_ref, gain_one, q_ref, kz_ref, vz_ref, p_ref, d_attn_ref, small_in, out_w,
                   x_hbm, base_hbm, state_hbm, qkv_hbm, du_in, token, du_ref, d_input_ref, small_ref,
                   do_ref, total, x, base, state, qkv_w, sems):
    copies = load_all([(qkv_hbm, qkv_w), (x_hbm, x), (base_hbm, base), (state_hbm, state)], sems)
    for copy in copies:
        copy.start()
    attention_backward(d_attn_ref.at[0, 0], out_w, qkv_w, cos_ref, sin_ref, q_ref, kz_ref, vz_ref, p_ref, do_ref, du_ref.at[0])
    for copy in copies:
        copy.wait()
    term = finish_attention_backward(x, gain_one[...], active_ref.at[0], du_ref.at[0], qkv_w, base, state, total, d_input_ref)
    small_ref[...] = small_in[...]
    small_ref[0:1, :] = small_in[0:1, :] + term


def swap_dp(values_in, bit, n_dp):
    return lax.ppermute(values_in, "dp", [(i, i ^ (1 << bit)) for i in range(n_dp)])


def swap_mp(values_in):
    return lax.ppermute(values_in, "mp", [(0, 1), (1, 0)])


def halving(parts, order, n_dp, index):
    bits = n_dp.bit_length() - 1
    left = list(range(bits - 1, -1, -1))
    shape = parts.shape[1:]
    held = parts.reshape((2,) * bits + shape)
    for step, bit in enumerate(order):
        at = left.index(bit)
        upper = ((index >> bit) & 1) == 1
        low = lax.index_in_dim(held, 0, at, keepdims=False)
        high = lax.index_in_dim(held, 1, at, keepdims=False)
        keep, send = jnp.where(upper, high, low), jnp.where(upper, low, high)
        got = swap_dp(send, bit, n_dp)
        last = step == bits - 1
        total = keep.astype(F32) + got.astype(F32)
        held = total if last else total.astype(BF)
        left.remove(bit)
    return held


def orders_of(bits):
    rest = list(range(3, bits))
    if bits < 3:
        return [list(range(bits))] * 3
    return [[0, 1, 2] + rest, [1, 0, 2] + rest, [2, 0, 1] + rest]


PART = 2 * LANES
FFN_TILES = (4, 4, 2)
FFN_ORDERS = (((1, 3, 0, 2), (2, 0, 1, 3)), ((0, 2, 1, 3), (2, 1, 0, 3)), ((1, 0, 2, 3), (2, 0, 3, 1)))
ATTN_ORDER = ((0, 1, 3, 2), (1, 0, 2, 3))
SCHEDULE = (
    "T0", "T1", "A", "T2",
    "F0", "F1", "A0", "F2",
    "F0", "F1", "A0", "F2",
    "A0", "F0 F1", "F2",
)
SMALL = 64


def of_core(pair):
    first, second = pair
    return first if first == second else jnp.where(lax.axis_index("mp") == 0, first, second)


def halves(bits, places, count):
    mine = (lax.axis_index("dp") >> of_core(bits)) & 1
    place = of_core(places)
    for i in range(count):
        base = ((i >> place) << (place + 1)) | (i & ((1 << place) - 1))
        yield i, base | (mine << place), base | ((1 - mine) << place)


def stacked_copies(pairs, sems):
    flat_pairs = []
    for sources, target in pairs:
        rows = target.shape[0] // 2
        flat_pairs += [(source, target.at[pl.ds(i * rows, rows)]) for i, source in enumerate(sources)]
    copies = load_all(flat_pairs, sems)
    for copy in copies:
        copy.start()
    return [copies[i : i + 2] for i in range(0, len(copies), 2)]


def ffn_terms(split, tiles, at, at_b, n2_df_a, n2_df_b, units_a, units_b, token, keep_ref, send_ref, left, gate_up, down, flat, sems):
    width, part = left.shape[2], down.shape[1]
    columns, columns_b = (pl.ds(start, tiles * LANES) for start in (at, at_b))
    lefts = [(n2_df_a.at[i], n2_df_b.at[i]) for i in range(2)]
    m, dg, dw = [(units_a.at[i, :, columns], units_b.at[i, :, columns_b]) for i in range(3)]
    n2, dg, dw, df, m = stacked_copies(
        [(lefts[0], left.at[0]), (dg, gate_up.at[:, :part]), (dw, gate_up.at[:, part:]), (lefts[1], left.at[1]), (m, down)], sems)
    for which, (right, needed) in enumerate(((gate_up, n2 + dg + dw), (down, df + m))):
        for copy in needed:
            copy.wait()
        terms = contract_rows(left[which], right[...])
        for at_lane in range(0, right.shape[1], LANES):
            matrix, c = divmod(at_lane // LANES, tiles)
            start = tiles * width * (2 * which + matrix) + c
            flat[pl.ds(start, width, stride=tiles), :] = terms[:, at_lane : at_lane + LANES]
    count, rows, _ = keep_ref.shape
    for i, kept, sent in halves(*split, count):
        for out, shard in ((keep_ref, kept), (send_ref, sent)):
            out[i] = flat[pl.ds(pl.multiple_of(shard * rows, 8), rows), :].astype(BF)


def small_rows(small, packed):
    packed[...] = jnp.zeros(packed.shape, F32)
    width = small.shape[1]
    for i in range(2 + RECURSIONS):
        for c in range(CHUNKS):
            stop = min(width, (c + 1) * LANES)
            packed[i * CHUNKS + c : i * CHUNKS + c + 1, : stop - c * LANES] = small[i : i + 1, c * LANES : stop]
    return packed[...]


def split_small(small, ref, start):
    high = small.astype(BF)
    ref[start : start + SMALL, :] = high
    ref[start + SMALL : start + 2 * SMALL, :] = (small - high.astype(F32)).astype(BF)


def rounded_small(small):
    high = small.astype(BF)
    return high.astype(F32) + (small - high.astype(F32)).astype(BF).astype(F32)


def joined_small(ref, start):
    return ref[start : start + SMALL, :].astype(F32) + ref[start + SMALL : start + 2 * SMALL, :].astype(F32)


def attn_terms(split, depth, n1_a, n1_b, du_a, du_b, o_da_a, o_da_b, small, token,
               keep, send, small_out, left, du_rows, da_rows, turned, own, terms, flat, packed, sems):
    base, count = 0, own.shape[0] // 2
    lower = lane_of(count) < HEAD_DIM
    core = lax.axis_index("mp")
    n1, du, o, da = stacked_copies(
        [((n1_a, n1_b), left.at[0]), ((du_a, du_b), du_rows), ((o_da_a.at[0], o_da_b.at[0]), left.at[1]),
         ((o_da_a.at[1], o_da_b.at[1]), da_rows)], sems)
    for which, (right, needed) in enumerate(((du_rows, n1 + du), (da_rows, o + da))):
        for copy in needed:
            copy.wait()
        columns = right.shape[1]
        half = columns // LANES
        turned[...] = left[which].T
        group = depth * LANES // columns
        for i in range(own.shape[0] // group):
            own[i * group : (i + 1) * group, :] = turned[pl.ds(pl.multiple_of((2 * i + core) * group, 16), group), :]
        for start in range(0, columns, PART):
            stop = min(columns, start + PART)
            block = plain(own[...], right[:, start:stop])
            if stop - start < PART:
                block = jnp.concatenate([block, jnp.zeros((2 * count, PART - (stop - start)), F32)], axis=1)
            for part in range(0, stop - start, LANES):
                terms[(start + part) // LANES] = block[:, part : part + LANES]
        step = 2 * columns // LANES
        after = first_odd = None
        for c in range(half + 1):
            even = terms[c, pl.ds(0, count, stride=2), :]
            odd = other_half(terms[c, pl.ds(1, count, stride=2), :])
            if c < half:
                flat[pl.ds(base + c, count, stride=step), :] = even
            else:
                flat[pl.ds(base + c, count, stride=step), :] = jnp.where(lower, even, first_odd)
            if c == 0:
                first_odd = odd
            else:
                flat[pl.ds(base + half + c, count, stride=step), :] = jnp.where(lower, after, odd)
            after = odd
        base += 2 * count * columns // LANES
    total = rounded_small(small_rows(small, packed))
    small_out[...] = total
    shards, rows, _ = keep.shape
    split_small(total, send, shards * rows)

    def rows_of_shard(shard):
        return flat[pl.ds(pl.multiple_of(shard * depth, 8), rows), :].astype(BF)

    for i, kept, sent in halves(*split, shards):
        keep[i] = rows_of_shard(kept)
        send[i * rows : (i + 1) * rows, :] = rows_of_shard(sent)


def fold(split, kept, got, token, keep, send):
    for i, *shards in halves(*split, keep.shape[0]):
        for out, shard in zip((keep, send), shards):
            out[i] = (kept[shard].astype(F32) + got[shard].astype(F32)).astype(BF)


def fold_small(split, kept, got, small, token, keep, send, small_out):
    held, rows, _ = kept.shape
    for i, *shards in halves(*split, held // 2):
        totals = [(kept[shard].astype(F32) + got[pl.ds(pl.multiple_of(shard * rows, 16), rows), :].astype(F32)).astype(BF)
                  for shard in shards]
        keep[i] = totals[0]
        send[i * rows : (i + 1) * rows, :] = totals[1]
    total = rounded_small(small[...]) + joined_small(got, held * rows)
    small_out[...] = total
    split_small(total, send, held // 2 * rows)


def fold_group(folds, *refs):
    inputs, results = refs, refs[sum(n for _, n, _ in folds) + 1 :]
    token = refs[sum(n for _, n, _ in folds)]
    for function, n_in, n_out in folds:
        function(*inputs[:n_in], token, *results[:n_out])
        inputs, results = inputs[n_in:], results[n_out:]


def finish_small(got, small, token, total_ref, send):
    total = rounded_small(small[...]) + joined_small(got, got.shape[0] - 2 * SMALL)
    total_ref[...] = total
    split_small(total, send, 0)


def finish_attn(kept, got, small, far, token, attn_out, one_out, two_out, router_out, packed):
    padded = kept.shape[0]
    both = kept[...].astype(F32) + got[:padded, :].astype(F32)
    attn_out[...] = both[: attn_out.shape[0]]
    packed[...] = rounded_small(small[...]) + joined_small(far, 0)
    width = one_out.shape[1]
    outs = [(one_out, 0), (two_out, 0), *[(router_out, i) for i in range(RECURSIONS)]]
    for i, (out, row) in enumerate(outs):
        for c in range(CHUNKS):
            stop = min(width, (c + 1) * LANES)
            out[row : row + 1, c * LANES : stop] = packed[i * CHUNKS + c : i * CHUNKS + c + 1, : stop - c * LANES]


def finish_ffn(tiles, *refs):
    feeds, (_, ffn_out, flat) = refs[:-3], refs[-3:]
    every = sum(tiles)
    rows = ffn_out.shape[0] // every
    base = 0
    for i, wide in enumerate(tiles):
        flat[: rows * wide, :] = feeds[2 * i][...].astype(F32) + feeds[2 * i + 1][...].astype(F32)
        for c in range(wide):
            ffn_out[pl.ds(base + c, rows, stride=every), :] = flat[pl.ds(c, rows, stride=wide), :]
        base += wide


class Stream:
    def __init__(self, orders, bits):
        self.orders, self.left, self.done = orders, [list(range(bits - 1, -1, -1)) for _ in orders], 0
        self.kept = self.got = None

    def split(self):
        bits = tuple(order[self.done] for order in self.orders)
        return bits, tuple(len(left) - 1 - left.index(bit) for left, bit in zip(self.left, bits))

    def sent(self, kept, send, n_dp):
        bits = self.split()[0]
        pairs = [(2 * d + core, 2 * (d ^ (1 << bit)) + core) for d in range(n_dp) for core, bit in enumerate(bits)]
        self.kept, self.got = kept, lax.ppermute(send, ("dp", "mp"), pairs)
        for left, bit in zip(self.left, bits):
            left.remove(bit)
        self.done += 1


def on_device(
    hidden_in,
    sel_one,
    sel_two,
    sel_three,
    segment_ids,
    pad_mask,
    qkv_weight,
    out_weight,
    gate_weight,
    up_weight,
    down_weight,
    norm_one,
    norm_two,
    router_weight,
    d_hidden,
):
    seq_len, width = hidden_in.shape
    n_dp, n_mp = lax.axis_size("dp"), lax.axis_size("mp")
    dp_index, mp_index = lax.axis_index("dp"), lax.axis_index("mp")
    cosine, sine = rotary_tables(seq_len)
    weights = [(gate_weight, up_weight, down_weight)]
    weights.append(tuple(swap_mp(w) for w in weights[0]))
    gain_one, gain_two = norm_one.reshape(1, width), norm_two.reshape(1, width)
    padded = CHUNKS * LANES
    units = gate_weight.shape[1]
    feed_weights = (*weights[0], *weights[1])

    def shape(*dims, dtype=BF):
        return jax.ShapeDtypeStruct(dims, dtype)

    def whole(*dims, **kw):
        return pl.BlockSpec(dims, lambda *_: (0,) * len(dims), **kw)

    anywhere = pl.BlockSpec(memory_space=pl.ANY)
    one = pl.Buffered(1)
    stack = RECURSIONS, seq_len
    heads = (2 * KV_HEADS, seq_len, LANES)
    square = (HEADS, seq_len, seq_len)
    n1, q, kz, vz, p, o_da, attn, n2, bias, active, near, slope_first, silu_first, f_first = pl.pallas_call(
        first_attention,
        grid=(1,),
        in_specs=[
            whole(seq_len, width), *[whole(*ref.shape) for ref in (sel_one, sel_two, sel_three, segment_ids, pad_mask)],
            whole(seq_len, LANES), whole(seq_len, LANES), whole(1, width), whole(1, width), whole(*qkv_weight.shape), whole(*out_weight.shape),
            *[anywhere] * 3,
        ],
        out_specs=[
            whole(1, seq_len, width), whole(seq_len, padded), whole(*heads), whole(*heads), whole(*square),
            whole(1, 1, seq_len, width), whole(seq_len, width), whole(seq_len, width), whole(RECURSIONS, seq_len, seq_len), whole(*stack, 1),
            whole(1, 1, seq_len, units), whole(seq_len, units), whole(seq_len, units), whole(seq_len, width),
        ],
        out_shape=[
            shape(*stack, width), shape(seq_len, padded), shape(*heads), shape(*heads), shape(*square),
            shape(2, *stack, width), shape(seq_len, width, dtype=F32), shape(seq_len, width),
            shape(*stack, seq_len, dtype=F32), shape(*stack, 1, dtype=F32),
            shape(3, *stack, units), shape(seq_len, units), shape(seq_len, units), shape(seq_len, width, dtype=F32),
        ],
        scratch_shapes=[*[pltpu.VMEM(w.shape, BF) for w in weights[0]], pltpu.SemaphoreType.DMA((3,))],
        compiler_params=pltpu.CompilerParams(vmem_limit_bytes=VMEM_BYTES),
        cost_estimate=pl.CostEstimate(flops=2 * 10**9, bytes_accessed=12 * 10**6, transcendentals=600000),
        name="first_attention",
    )(hidden_in, sel_one, sel_two, sel_three, segment_ids, pad_mask, cosine, sine, gain_one, gain_two, qkv_weight, out_weight,
      *weights[0])
    attention_0 = (q, kz, vz, p)
    wide = qkv_weight.shape[1]
    row = (seq_len, width)
    kept = RECURSIONS - 1
    first_part = FFN_TILES[0] * LANES
    vm = pltpu.VMEM
    results = pl.pallas_call(
        all_steps,
        grid=(1,),
        in_specs=[
            whole(RECURSIONS, seq_len, seq_len), whole(RECURSIONS, seq_len, 1), whole(RECURSIONS, width),
            whole(seq_len, LANES), whole(seq_len, LANES), whole(1, width), whole(1, width), *[anywhere] * 18,
        ],
        out_specs=[*[anywhere] * 8, whole(*row), whole(*row), whole(8, width)],
        out_shape=[
            shape(*stack, width), *[shape(2, *stack, width)] * 2, shape(3, *stack, units), shape(3, *stack, first_part), shape(3, *stack, units - first_part), shape(*stack, wide),
            *[shape(*row, dtype=F32)] * 3, shape(8, width, dtype=F32),
        ],
        scratch_shapes=[
            *[vm(w.shape, BF) for w in (qkv_weight, out_weight, *feed_weights)],
            vm((RECURSIONS + 1, *row), F32), vm((RECURSIONS, *row), F32), vm((RECURSIONS, *row), BF),
            *[vm((*stack, units), BF)] * 4, vm((kept, seq_len, padded), BF), vm((kept, *heads), BF), vm((kept, *heads), BF),
            vm((kept, *square), BF), *[vm(row, BF)] * 3, *[vm((seq_len, units), BF)] * 2, vm(row, BF), *[vm((seq_len, units), BF)] * 4,
            vm(row, BF), vm((seq_len, wide), BF), vm(row, F32), vm(row, F32), vm((seq_len, padded), BF),
            pltpu.SemaphoreType.DMA((15,)), pltpu.SemaphoreType.DMA((16,)),
        ],
        input_output_aliases={14: 0, 15: 1, 16: 3},
        compiler_params=pltpu.CompilerParams(vmem_limit_bytes=VMEM_BYTES),
        cost_estimate=pl.CostEstimate(flops=23 * 10**9, bytes_accessed=50 * 10**6, transcendentals=4 * 10**6),
        name="all_steps",
    )(bias, active, router_weight, cosine, sine, gain_one, gain_two, hidden_in, d_hidden, attn, n2,
      slope_first, silu_first, f_first, n1, o_da, near,
      qkv_weight, out_weight, *feed_weights)
    n1, o_da, n2_df, near, far, late, du, state, base, grad_state, small = results

    def run_last(token):
        return pl.pallas_call(
            last_attention,
            grid=(1,),
            in_specs=[
                whole(1, seq_len, 1), whole(seq_len, LANES), whole(seq_len, LANES), whole(1, width),
                whole(seq_len, padded), whole(*heads), whole(*heads), whole(*square),
                pl.BlockSpec((1, 1, seq_len, width), lambda i: (1, 0, 0, 0)), whole(8, width), whole(*out_weight.shape), *[anywhere] * 6,
            ],
            out_specs=[whole(1, seq_len, qkv_weight.shape[1]), whole(seq_len, width), whole(8, width)],
            out_shape=[shape(*stack, qkv_weight.shape[1]), shape(seq_len, width, dtype=F32), shape(8, width, dtype=F32)],
            scratch_shapes=[
                pltpu.VMEM((seq_len, padded), BF), *[pltpu.VMEM((seq_len, width), F32)] * 4,
                pltpu.VMEM(qkv_weight.shape, BF), pltpu.SemaphoreType.DMA((4,)),
            ],
            input_output_aliases={15: 0},
            compiler_params=pltpu.CompilerParams(vmem_limit_bytes=VMEM_BYTES),
            cost_estimate=pl.CostEstimate(flops=1, bytes_accessed=1, transcendentals=0),
            name="last_attention",
        )(active, cosine, sine, gain_one, *attention_0, o_da, small, out_weight, hidden_in, base, grad_state, qkv_weight, du, token)

    def rows_of(stacked):
        return stacked.reshape(*stacked.shape[:-3], -1, stacked.shape[-1])

    bits = n_dp.bit_length() - 1
    share = (qkv_weight.size + out_weight.size) // (n_dp * n_mp)
    if bits == 4 and 3 * width % n_dp == 0 and units == sum(FFN_TILES) * LANES and share % (16 * qkv_weight.shape[1]) == share % (16 * width) == 0:
        n2_df_rows = [rows_of(t) for t in (n2_df, swap_mp(n2_df))]
        near, far_b = rows_of(near), rows_of(swap_mp(far))
        n1_b = rows_of(swap_mp(n1))
        streams = [Stream(order, bits) for order in FFN_ORDERS]
        attn_stream = Stream(ATTN_ORDER, bits)
        depth = share // LANES
        tiled = -(-depth // 16) * 16
        common = dict(
            grid=(1,),
            compiler_params=pltpu.CompilerParams(vmem_limit_bytes=VMEM_BYTES),
            cost_estimate=pl.CostEstimate(flops=1, bytes_accessed=1, transcendentals=0),
        )

        def wholes(arrays):
            return [whole(*t.shape) for t in arrays]

        def terms_of(j, token):
            stream, tiles = streams[j], FFN_TILES[j]
            at = sum(FFN_TILES[:j]) * LANES
            factors = (*n2_df_rows, near, far_b if j == 0 else late_b)
            dims = (n_dp // 2, 3 * width // n_dp * tiles, LANES)
            both = 2 * RECURSIONS * seq_len
            keep, send = pl.pallas_call(
                functools.partial(ffn_terms, stream.split(), tiles, at, 0 if j == 0 else at - first_part),
                in_specs=[anywhere] * (len(factors) + 1),
                out_specs=[whole(*dims)] * 2,
                out_shape=[shape(*dims)] * 2,
                scratch_shapes=[pltpu.VMEM((2, both, width), BF), *[pltpu.VMEM((both, n * tiles * LANES), BF) for n in (2, 1)],
                                pltpu.VMEM((3 * width * tiles, LANES), F32), pltpu.SemaphoreType.DMA((10,))],
                name=f"ffn_terms_{j}",
                **common,
            )(*factors, token)
            stream.sent(keep, send, n_dp)
            return keep

        def fold_streams(group, token, small_own):
            folds, operands, outs = [], [], []
            for stream in group:
                count, rows, _ = stream.kept.shape
                held = (count // 2, rows, LANES)
                operands += [stream.kept, stream.got]
                if stream is attn_stream:
                    operands.append(small_own)
                    outs += [shape(*held), shape(count // 2 * rows + 2 * SMALL, LANES), shape(SMALL, LANES, dtype=F32)]
                    folds.append((functools.partial(fold_small, stream.split()), 3, 3))
                else:
                    outs += [shape(*held), shape(*held)]
                    folds.append((functools.partial(fold, stream.split()), 2, 2))
            results = pl.pallas_call(
                functools.partial(fold_group, folds),
                in_specs=[*wholes(operands), anywhere],
                out_specs=wholes(outs),
                out_shape=outs,
                name="fold_terms",
                **common,
            )(*operands, token)
            token = results[0]
            for stream, (_, _, n_out) in zip(group, folds):
                stream.sent(results[0], results[1], n_dp)
                small_own = results[2] if n_out == 3 else small_own
                results = results[n_out:]
            return token, small_own

        du, grad_state, small = run_last(small)
        late, du, small = lax.optimization_barrier((late, du, small))
        late_b, du_b = rows_of(swap_mp(late)), rows_of(swap_mp(du))
        token, small_own = small, None
        for item in SCHEDULE:
            if item[0] == "T":
                token = terms_of(int(item[1:]), token)
                if item == "T0":
                    o_da, token = lax.optimization_barrier((o_da, token))
                    o_da_b = rows_of(swap_mp(o_da))
            elif item == "A":
                dims = (n_dp // 2, tiled, LANES)
                operands = (rows_of(n1), n1_b, rows_of(du), du_b, rows_of(o_da), o_da_b, small)
                outs = (shape(*dims), shape(n_dp // 2 * tiled + 2 * SMALL, LANES), shape(SMALL, LANES, dtype=F32))
                keep, send, small_own = pl.pallas_call(
                    functools.partial(attn_terms, attn_stream.split(), depth),
                    in_specs=[*[anywhere] * 6, *wholes(operands[6:]), anywhere],
                    out_specs=wholes(outs),
                    out_shape=outs,
                    scratch_shapes=[pltpu.VMEM((2, 2 * RECURSIONS * seq_len, width), BF),
                                    *[pltpu.VMEM((2 * RECURSIONS * seq_len, t.shape[-1]), BF) for t in (du, o_da)],
                                    pltpu.VMEM((width, 2 * RECURSIONS * seq_len), BF),
                                    pltpu.VMEM((width // 2, 2 * RECURSIONS * seq_len), BF),
                                    pltpu.VMEM((-(-du.shape[-1] // PART) * 2, width // 2, LANES), F32),
                                    pltpu.VMEM((n_dp * depth + tiled - depth, LANES), F32), pltpu.VMEM((SMALL, LANES), F32),
                                    pltpu.SemaphoreType.DMA((8,))],
                    name="attn_terms",
                    **common,
                )(*operands, token)
                attn_stream.sent(keep, send, n_dp)
                token = small_own
            else:
                group = [attn_stream if name == "A0" else streams[int(name[1:])] for name in item.split()]
                token, small_own = fold_streams(group, token, small_own)
        attn_kept = attn_stream.kept.reshape(tiled, LANES)
        outs = (shape(SMALL, LANES, dtype=F32), shape(2 * SMALL, LANES))
        small_own, small_send = pl.pallas_call(
            finish_small,
            in_specs=[*wholes((attn_stream.got, small_own)), anywhere],
            out_specs=wholes(outs),
            out_shape=outs,
            name="finish_small",
            **common,
        )(attn_stream.got, small_own, token)
        operands = (attn_kept, attn_stream.got, small_own, swap_mp(small_send))
        outs = (shape(depth, LANES, dtype=F32), shape(1, width, dtype=F32), shape(1, width, dtype=F32),
                shape(RECURSIONS, width, dtype=F32))
        attn_flat, one, two, router = pl.pallas_call(
            finish_attn,
            in_specs=[*wholes(operands), anywhere],
            out_specs=wholes(outs),
            out_shape=outs,
            scratch_shapes=[pltpu.VMEM((SMALL, LANES), F32)],
            name="finish_attn",
            **common,
        )(*operands, small_own)
        ends = [t.reshape(t.shape[-2:]) for stream in streams for t in (stream.kept, stream.got)]
        ffn_rows = (3 * width // n_dp * sum(FFN_TILES), LANES)
        ffn_flat = pl.pallas_call(
            functools.partial(finish_ffn, FFN_TILES),
            in_specs=[*wholes(ends), anywhere],
            out_specs=whole(*ffn_rows),
            out_shape=shape(*ffn_rows, dtype=F32),
            scratch_shapes=[pltpu.VMEM((3 * width // n_dp * max(FFN_TILES), LANES), F32)],
            name="finish_ffn",
            **common,
        )(*ends, attn_flat)
        return (state, grad_state, attn_flat.reshape(-1), ffn_flat.reshape(1, -1), one.reshape(-1), two.reshape(-1), router)

    du, grad_state, small = run_last(small)
    two, feed = rows_of(n2_df)
    o, d_attn = rows_of(o_da)
    far = jnp.concatenate([far, late], axis=-1)
    sides = [[t[i] for i in (1, 2, 0)] for t in (rows_of(near), rows_of(far))]

    def side_terms(side, columns):
        return jnp.concatenate(
            [
                contract_rows(left, sides[side][which][:, columns]).astype(BF)
                for which, left in enumerate((two, two, feed))
            ],
            axis=0,
        )

    orders = orders_of(bits)
    if 3 * width % n_dp == 0 and units % 1280 == 0:
        fifth = units // 5
        streams = [(orders[i], slice(j * fifth, (j + 1) * fifth)) for i, j in ((0, 0), (1, 1), (2, 2), (0, 3), (1, 4))]
        done = []
        for order, columns in streams:
            terms = side_terms(0, columns).astype(F32) + swap_mp(side_terms(1, columns)).astype(F32)
            done.append(halving(terms.astype(BF).reshape(n_dp, 3 * width // n_dp, fifth), order, n_dp, dp_index))
        ffn_flat = jnp.concatenate(done, axis=1).reshape(1, -1)
    else:
        terms = side_terms(0, slice(None)).astype(F32) + swap_mp(side_terms(1, slice(None))).astype(F32)
        terms = terms.astype(BF).reshape(n_dp, 3 * width * units // n_dp // 128, 128)
        ffn_flat = halving(terms, orders[0], n_dp, dp_index).reshape(1, -1)

    grad_qkv = contract_rows(rows_of(n1), rows_of(du)).astype(BF)
    grad_out = contract_rows(o, d_attn).astype(BF)
    attn = jnp.concatenate([grad_qkv.reshape(-1), grad_out.reshape(-1)]).reshape(n_dp, 2, share // 128, 128)
    keep = jnp.where(mp_index == 0, attn[:, 0], attn[:, 1])
    send = jnp.where(mp_index == 0, attn[:, 1], attn[:, 0])
    attn = (keep.astype(F32) + swap_mp(send).astype(F32)).astype(BF)
    cuts = [0, (share // 128) // 24 * 8, (share // 128) // 12 * 8, share // 128]
    attn_flat = jnp.concatenate(
        [halving(attn[:, a:b], order, n_dp, dp_index) for a, b, order in zip(cuts, cuts[1:], orders)], axis=0
    ).reshape(-1)

    small = small + swap_mp(small)
    for bit in range(bits):
        small = small + swap_dp(small, bit, n_dp)
    return (state, grad_state, attn_flat, ffn_flat, small[0], small[1], small[2 : 2 + RECURSIONS])


def solution(mesh):
    both = P(("dp", "mp"), None)
    in_specs = (
        both,
        both,
        both,
        both,
        both,
        both,
        P(),
        P(),
        P(None, "mp"),
        P(None, "mp"),
        P(None, "mp"),
        P(),
        P(),
        P(),
        both,
    )
    out_specs = (both, both, P(("dp", "mp")), P("mp", "dp"), P(), P(), P())
    return jax.shard_map(
        on_device, mesh=mesh, in_specs=in_specs, out_specs=out_specs, check_vma=False
    )
```

```python
import functools
import math

import jax
import jax.numpy as jnp
import numpy as np
from jax import lax
from jax.experimental import pallas as pl
from jax.experimental.pallas import tpu as pltpu
from jax.sharding import PartitionSpec as P

HEADS = 15
KV_HEADS = 5
HEAD_DIM = 64
RECURSIONS = 3
GROUPS = HEADS // KV_HEADS
EPS = 1e-05
BF = jnp.bfloat16
F32 = jnp.float32


LANES = 128
CHUNKS = -(-HEADS * HEAD_DIM // LANES)
ROWS = 192
BLOCK = 256
MIB = 1 << 20
VMEM_BYTES = 64 * MIB - 65536


def rotary_tables(seq_len):
    half = HEAD_DIM // 2
    frequency = np.float32(100000.0) ** (
        np.float32(-2.0) * np.arange(half, dtype=np.float32) / np.float32(HEAD_DIM)
    )
    angles = np.arange(seq_len, dtype=np.float32)[:, None] * frequency.astype(np.float32)
    cosine, sine = np.cos(angles), np.sin(angles)
    return (
        jnp.asarray(np.concatenate([cosine] * 4, axis=1), F32),
        jnp.asarray(np.concatenate([-sine, sine] * 2, axis=1), F32),
    )


def contract_rows(left, right):
    return lax.dot_general(left, right, (((0,), (0,)), ((), ())), preferred_element_type=F32)


def contract_last(left, right):
    return lax.dot_general(left, right, (((1,), (1,)), ((), ())), preferred_element_type=F32)


def plain(left, right):
    return jnp.dot(left, right, preferred_element_type=F32)


def inverse_rms(rows):
    return lax.rsqrt(jnp.mean(rows * rows, axis=-1, keepdims=True) + EPS)


def norm_back(rows, gain, d_out):
    inv = inverse_rms(rows)
    scaled = d_out * gain
    inner = jnp.mean(scaled * rows, axis=-1, keepdims=True)
    d_rows = inv * scaled - rows * (inv * inv * inv * inner)
    return d_rows, jnp.sum(d_out * rows * inv, axis=0, keepdims=True)


def lane_of(rows):
    return lax.broadcasted_iota(jnp.int32, (rows, LANES), 1)


def swapped(chunk):
    first = lane_of(chunk.shape[0]) % HEAD_DIM < HEAD_DIM // 2
    return jnp.where(first, pltpu.roll(chunk, LANES - 32, 1), pltpu.roll(chunk, 32, 1))


def other_half(chunk):
    return pltpu.roll(chunk, HEAD_DIM, 1)


def over_rows(count, body):
    def lap(i, carry):
        body(pl.ds(pl.multiple_of(i * ROWS, ROWS), ROWS))
        return carry

    lax.fori_loop(0, count // ROWS, lap, 0)


def attention_forward(x_ref, bias_ref, cos_ref, sin_ref, gain, qkv_w, n1_ref, q_ref, kz_ref, vz_ref, p_ref, o_ref):
    seq_len, width = x_ref.shape
    scale = 1.0 / math.sqrt(HEAD_DIM)

    def norm(rows):
        x = x_ref[rows, :]
        n1_ref[rows, :] = (x * inverse_rms(x) * gain).astype(BF)

    over_rows(seq_len, norm)
    lower = lane_of(seq_len) < HEAD_DIM
    n1 = n1_ref[...]

    def spread(ref, head, chunk, upper):
        flipped = other_half(chunk)
        here, there = (flipped, chunk) if upper else (chunk, flipped)
        ref[2 * head] = jnp.where(lower, here, 0.0).astype(BF)
        ref[2 * head + 1] = jnp.where(lower, 0.0, there).astype(BF)

    columns = qkv_w.shape[1]
    for start in range(0, columns, 2 * LANES):
        wide = plain(n1, qkv_w[:, start : min(start + 2 * LANES, columns)])
        for part in range(0, wide.shape[1], LANES):
            chunk = wide[:, part : part + LANES]
            if chunk.shape[1] < LANES:
                chunk = jnp.concatenate([chunk, jnp.zeros_like(chunk)], axis=1)
            at = (start + part) // LANES
            heads = (2 * at, 2 * at + 1)
            if heads[0] < HEADS + KV_HEADS:
                chunk = chunk * cos_ref[...] + swapped(chunk) * sin_ref[...]
                if heads[0] < HEADS:
                    q_ref[:, at * LANES : (at + 1) * LANES] = chunk.astype(BF)
            for upper, head in enumerate(heads):
                if HEADS <= head < HEADS + KV_HEADS:
                    spread(kz_ref, head - HEADS, chunk, upper)
                elif HEADS + KV_HEADS <= head < HEADS + 2 * KV_HEADS:
                    spread(vz_ref, head - HEADS - KV_HEADS, chunk, upper)

    for at in range(CHUNKS):
        query = q_ref[:, at * LANES : (at + 1) * LANES]
        total = None
        for upper in range(2):
            head = 2 * at + upper
            if head < HEADS:
                key = 2 * (head // GROUPS) + upper
                scores = contract_last(query, kz_ref[key]) * scale + bias_ref[...]
                top = jnp.max(scores, axis=-1, keepdims=True)
                exponent = jnp.exp(scores - top)
                share = pl.reciprocal(jnp.sum(exponent, axis=-1, keepdims=True))
                attend = (exponent * share).astype(BF)
                p_ref[head] = attend
                mixed = plain(attend, vz_ref[key])
                total = mixed if total is None else total + mixed
        stop = min(width, (at + 1) * LANES)
        o_ref[:, at * LANES : stop] = total[:, : stop - at * LANES].astype(BF)


def attention_out(x_ref, o_ref, out_w, gain, attn_ref, n2_ref):
    attn_ref[...] = plain(o_ref[...], out_w[...])

    def norm(rows):
        after = x_ref[rows, :] + attn_ref[rows, :]
        n2_ref[rows, :] = (after * inverse_rms(after) * gain).astype(BF)

    over_rows(x_ref.shape[0], norm)


def feed_side(n2_ref, weights, results, ready):
    n2 = n2_ref[...]
    gate_w, up_w, down_w = weights
    m_ref, slope_ref, silu_ref = results
    ready(0, 1)
    for start in range(0, gate_w.shape[1], BLOCK):
        at = slice(start, start + BLOCK)
        g, u = plain(n2, gate_w[:, at]), plain(n2, up_w[:, at])
        s = jax.nn.sigmoid(g)
        silu = g * s
        m_ref[:, at] = (silu * u).astype(BF)
        slope_ref[:, at] = (u * s * (1.0 + g * (1.0 - s))).astype(BF)
        silu_ref[:, at] = silu.astype(BF)
    ready(2)
    return contract_last(m_ref[...], down_w[...])


def feed_backward(df_ref, sides, d_two_ref, ready):
    d_feed = df_ref[...]
    for side, (gate_w, up_w, down_w, slope_ref, silu_ref, dg_ref, du_ref) in enumerate(sides):
        ready(3 * side)
        for start in range(0, gate_w.shape[1], BLOCK):
            at = slice(start, start + BLOCK)
            d_hidden = plain(d_feed, down_w[:, at])
            dg_ref[:, at] = (d_hidden * slope_ref[:, at].astype(F32)).astype(BF)
            du_ref[:, at] = (d_hidden * silu_ref[:, at].astype(F32)).astype(BF)
        ready(3 * side + 1, 3 * side + 2)
        part = contract_last(dg_ref[...], gate_w[...]) + contract_last(du_ref[...], up_w[...])
        d_two_ref[...] = part if side == 0 else d_two_ref[...] + part


def attention_backward(d_attn_ref, out_w, qkv_w, cos_ref, sin_ref, q_ref, kz_ref, vz_ref, p_ref, do_ref, du_ref):
    seq_len, width = d_attn_ref.shape
    scale = 1.0 / math.sqrt(HEAD_DIM)
    do_ref[:, :width] = contract_last(d_attn_ref[...], out_w[...]).astype(BF)
    do_ref[:, width:] = jnp.zeros((seq_len, do_ref.shape[1] - width), BF)
    lower = lane_of(seq_len) < HEAD_DIM
    cosine, sine = cos_ref[...], sin_ref[...]

    def back(chunk):
        chunk = chunk * scale
        return chunk * cosine - swapped(chunk) * sine

    waiting, d_k, d_v = None, {}, {}
    for at in range(CHUNKS):
        query, d_mixed = (ref[:, at * LANES : (at + 1) * LANES] for ref in (q_ref, do_ref))
        query_t, d_mixed_t = query.T, d_mixed.T
        d_query = None
        for upper in range(2):
            head = 2 * at + upper
            if head >= HEADS:
                continue
            group = head // GROUPS
            key = 2 * group + upper
            rows = slice(upper * HEAD_DIM, (upper + 1) * HEAD_DIM)
            attend = p_ref[head]
            d_attend = contract_last(d_mixed, vz_ref[key])
            soft = attend.astype(F32)
            weighted = soft * d_attend
            inner = jnp.sum(weighted, axis=-1, keepdims=True)
            d_scores = (weighted - soft * inner).astype(BF)
            part = plain(d_scores, kz_ref[key])
            d_query = part if d_query is None else d_query + part
            for store, term in ((d_k, plain(query_t[rows], d_scores)), (d_v, plain(d_mixed_t[rows], attend))):
                store[group] = term if group not in store else store[group] + term
        if at < CHUNKS - 1:
            du_ref[:, at * LANES : (at + 1) * LANES] = back(d_query).astype(BF)
        else:
            waiting = d_query

    def two_heads(store, first, second):
        return jnp.concatenate([store[first], store[second]], axis=0).T

    tail = jnp.where(lower, waiting, two_heads(d_k, 0, 0))
    du_ref[:, (CHUNKS - 1) * LANES : CHUNKS * LANES] = back(tail).astype(BF)
    for i in range(2):
        at = CHUNKS + i
        du_ref[:, at * LANES : (at + 1) * LANES] = back(two_heads(d_k, 1 + 2 * i, 2 + 2 * i)).astype(BF)
        at = CHUNKS + 2 + i
        du_ref[:, at * LANES : (at + 1) * LANES] = two_heads(d_v, 2 * i, 2 * i + 1).astype(BF)
    at = CHUNKS + 4
    du_ref[:, at * LANES :] = two_heads(d_v, 4, 4)[:, : du_ref.shape[1] - at * LANES].astype(BF)


def router_gate(x, router_row):
    return jax.nn.sigmoid(jnp.sum(x * router_row, axis=-1, keepdims=True))


def masks(select_refs, segment_ref, pad_ref, bias_ref, active_ref):
    seq_len = segment_ref.shape[1]
    square = (seq_len, seq_len)
    query, key = (lax.broadcasted_iota(jnp.int32, square, axis) for axis in (0, 1))
    diagonal = query == key
    segment = segment_ref[...].astype(F32)
    own = jnp.sum(jnp.where(diagonal, segment, 0.0), axis=1, keepdims=True)
    near = (key <= query) & (segment == own)
    real = pad_ref[...] == 1
    for recursion, ref in enumerate(select_refs):
        place = lax.broadcasted_iota(jnp.int32, (seq_len, ref.shape[1]), 0)
        active = jnp.max(jnp.where(ref[...] == place, 1.0, 0.0), axis=1, keepdims=True)
        active_ref[recursion] = active
        along = jnp.sum(jnp.where(diagonal, active, 0.0), axis=0, keepdims=True)
        usable = (along > 0.0) & real
        bias_ref[recursion] = jnp.where(near & (usable | diagonal), 0.0, -1e30)


def first_attention(x_ref, sel_one, sel_two, sel_three, segment_ref, pad_ref, cos_ref, sin_ref, gain_one, gain_two, qkv_w, out_w,
                    gate_hbm, up_hbm, down_hbm, n1_ref, q_ref, kz_ref, vz_ref, p_ref, o_ref, attn_ref, n2_ref, bias_ref, active_ref,
                    m_ref, slope_ref, silu_ref, f_ref, gate_w, up_w, down_w, sems):
    copies = load_all([(gate_hbm, gate_w), (up_hbm, up_w), (down_hbm, down_w)], sems)
    for copy in copies:
        copy.start()
    n1, o = n1_ref.at[0], o_ref.at[0, 0]
    masks((sel_one, sel_two, sel_three), segment_ref, pad_ref, bias_ref, active_ref)
    attention_forward(x_ref, bias_ref.at[0], cos_ref, sin_ref, gain_one[...], qkv_w, n1, q_ref, kz_ref, vz_ref, p_ref, o)
    attention_out(x_ref, o, out_w, gain_two[...], attn_ref, n2_ref)

    def ready(*which):
        for i in which:
            copies[i].wait()

    f_ref[...] = feed_side(n2_ref, (gate_w, up_w, down_w), (m_ref.at[0, 0], slope_ref, silu_ref), ready)


def load_all(pairs, sems):
    return [pltpu.make_async_copy(src, dst, sems.at[i]) for i, (src, dst) in enumerate(pairs)]


def waits_at(condition, copies):
    def ready(*which):
        @pl.when(condition)
        def _():
            for i in which:
                copies[i].wait()

    return ready


def finish_attention_backward(x_ref, gain, active_ref, du_ref, qkv_w, base, state, total, out_ref):
    total[...] = contract_last(du_ref[...], qkv_w[...])
    terms = jnp.zeros((1, state.shape[1]), F32)

    def lap(i, terms):
        rows = pl.ds(pl.multiple_of(i * ROWS, ROWS), ROWS)
        d_rows, term = norm_back(x_ref[rows, :], gain, total[rows, :])
        new = jnp.where(active_ref[rows, :] > 0, base[rows, :] + d_rows, state[rows, :])
        out_ref[rows, :] = new
        return terms + term

    return lax.fori_loop(0, state.shape[0] // ROWS, lap, terms)


def all_steps(bias_ref, active_ref, router_ref, cos_ref, sin_ref, gain_one, gain_two,
              hidden_hbm, d_hidden_hbm, attn0_hbm, n20_hbm, slope_hbm, silu_hbm, f_hbm, n1_in, o_da_in, near_in,
              qkv_hbm, out_hbm, *rest):
    feed_hbm, rest = rest[:6], rest[6:]
    (n1_out, o_da_out, n2_df_out, near_out, far_out, late_out, du_out, final_out, base_ref, state_ref, small_ref), rest = rest[:11], rest[11:]
    qkv_w, out_w, *feed_w = rest[:8]
    (xs, attns, fs, slope0, slope1, silu0, silu1, qs, kzs, vzs, ps, n1, o, n2, m0, m1, df, dg0, dg1, dw0, dw1, da, du,
     total, d_branch, do_ref, load_sems, out_sems) = rest[8:]
    width = state_ref.shape[1]
    first_part = far_out.shape[3]
    laps = state_ref.shape[0] // ROWS
    loads = load_all(
        [*zip(feed_hbm, feed_w), (qkv_hbm, qkv_w), (out_hbm, out_w),
         (n20_hbm, n2), (attn0_hbm, attns.at[0]), (hidden_hbm, xs.at[0]), (d_hidden_hbm, state_ref),
         (f_hbm, total), (slope_hbm, slope0.at[0]), (silu_hbm, silu0.at[0])], load_sems)
    for i in (8, 3, 4, 5, 12, 9, 10, 6, 7, 0, 1, 2, 13, 14, 11):
        loads[i].start()
    loads[8].wait()

    places = dict(n2=[(n2, n2_df_out.at[0])], m0=[(m0, near_out.at[0])], n1=[(n1, n1_out)], o=[(o, o_da_out.at[0])],
                  df=[(df, n2_df_out.at[1])], dg0=[(dg0, near_out.at[1])], dw0=[(dw0, near_out.at[2])],
                  da=[(da, o_da_out.at[1])], du=[(du, du_out)])
    for i, (name, ref) in enumerate((("m1", m1), ("dg1", dg1), ("dw1", dw1))):
        places[name] = [(ref.at[:, :first_part], far_out.at[i]), (ref.at[:, first_part:], late_out.at[i])]
    numbers = {}
    for pairs in places.values():
        for source, target in pairs:
            numbers[id(target)] = len(numbers)

    def leaving(recursion, names):
        return [pltpu.make_async_copy(source, target.at[recursion], out_sems.at[numbers[id(target)]])
                for name in names for source, target in places[name]]

    def start(recursion, *names):
        for copy in leaving(recursion, names):
            copy.start()

    def wait(recursion, *names):
        for copy in leaving(recursion, names):
            copy.wait()

    def forward(r, carry):
        ready, later = (waits_at(r == step, loads) for step in range(2))
        start(r, "n2")

        @pl.when(r > 0)
        def _():
            @pl.when(r > 1)
            def _():
                wait(r - 1, "m0")

            total[...] = feed_side(n2, feed_w[:3], (m0, slope0.at[r], silu0.at[r]), later)
            start(r, "m0")
            wait(r - 1, "m1")

        part = feed_side(n2, feed_w[3:], (m1, slope1.at[r], silu1.at[r]), lambda *which: ready(*[3 + i for i in which]))
        ready(12)
        total[...] = total[...] + part
        start(r, "m1")
        ready(9, 10)
        router_row = router_ref[pl.ds(r, 1), :]

        def finish(rows):
            x = xs[r, rows, :]
            f = total[rows, :].astype(BF)
            fs[r, rows, :] = f
            branch = attns[r, rows, :] + f.astype(F32)
            xs[r + 1, rows, :] = jnp.where(active_ref[r, rows, :] > 0, x + router_gate(x, router_row) * branch, x)

        over_rows(total.shape[0], finish)
        ready(6, 7)
        wait(r, "n2")

        @pl.when(r < RECURSIONS - 1)
        def _():
            @pl.when(r > 0)
            def _():
                wait(r, "n1", "o")

            attention_forward(xs.at[r + 1], bias_ref.at[r + 1], cos_ref, sin_ref, gain_one[...], qkv_w,
                              n1, qs.at[r], kzs.at[r], vzs.at[r], ps.at[r], o)
            start(r + 1, "n1", "o")
            attention_out(xs.at[r + 1], o, out_w, gain_two[...], attns.at[r + 1], n2)

        return carry

    lax.fori_loop(0, RECURSIONS, forward, 0)
    final = pltpu.make_async_copy(xs.at[RECURSIONS], final_out, out_sems.at[15])
    final.start()
    for i in (11, 13, 14):
        loads[i].wait()
    small_ref[...] = jnp.zeros(small_ref.shape, F32)

    def backward(i, carry):
        r = RECURSIONS - 1 - i
        router_row = router_ref[pl.ds(r, 1), :]

        @pl.when(i > 0)
        def _():
            wait(r + 1, "df", "dg0", "dg1", "dw0", "dw1", "da")

        def enter(lap, terms):
            rows = pl.ds(pl.multiple_of(lap * ROWS, ROWS), ROWS)
            x = xs[r, rows, :]
            d_new = jnp.where(active_ref[r, rows, :] > 0, state_ref[rows, :], 0.0)
            gate = router_gate(x, router_row)
            branch = attns[r, rows, :] + fs[r, rows, :].astype(F32)
            d_gate = jnp.sum(d_new * branch, axis=-1, keepdims=True)
            d_logit = d_gate * gate * (1.0 - gate)
            spread = gate * d_new
            d_branch[rows, :] = spread
            df[rows, :] = spread.astype(BF)
            base_ref[rows, :] = d_new + d_logit * router_row
            return terms + jnp.sum(d_logit * x, axis=0, keepdims=True)

        small_ref[pl.ds(2 + r, 1), :] = lax.fori_loop(0, laps, enter, jnp.zeros((1, width), F32))
        start(r, "df")
        feed_backward(df, ((*feed_w[:3], slope0.at[r], silu0.at[r], dg0, dw0), (*feed_w[3:], slope1.at[r], silu1.at[r], dg1, dw1)),
                      total, lambda *which: None)
        start(r, "dg0", "dg1", "dw0", "dw1")

        def leave(lap, terms):
            rows = pl.ds(pl.multiple_of(lap * ROWS, ROWS), ROWS)
            after = xs[r, rows, :] + attns[r, rows, :]
            d_after, term = norm_back(after, gain_two[...], total[rows, :].astype(BF).astype(F32))
            da[rows, :] = (d_branch[rows, :] + d_after).astype(BF)
            base_ref[rows, :] = base_ref[rows, :] + d_after
            return terms + term

        small_ref[1:2, :] = small_ref[1:2, :] + lax.fori_loop(0, laps, leave, jnp.zeros((1, width), F32))
        start(r, "da")

        @pl.when(r > 0)
        def _():
            @pl.when(i > 0)
            def _():
                wait(r + 1, "du")

            attention_backward(da, out_w, qkv_w, cos_ref, sin_ref, qs.at[r - 1], kzs.at[r - 1], vzs.at[r - 1], ps.at[r - 1], do_ref, du)
            start(r, "du")
            term = finish_attention_backward(xs.at[r], gain_one[...], active_ref.at[r], du, qkv_w, base_ref, state_ref, total, state_ref)
            small_ref[0:1, :] = small_ref[0:1, :] + term

        return carry

    lax.fori_loop(0, RECURSIONS, backward, 0)
    wait(RECURSIONS - 1, "m0", "m1", "n1", "o")
    wait(0, "df", "dg0", "dg1", "dw0", "dw1", "da")
    wait(1, "du")
    final.wait()


def last_attention(active_ref, cos_ref, sin_ref, gain_one, q_ref, kz_ref, vz_ref, p_ref, d_attn_ref, small_in, out_w,
                   x_hbm, base_hbm, state_hbm, qkv_hbm, du_in, token, du_ref, d_input_ref, small_ref,
                   do_ref, total, x, base, state, qkv_w, sems):
    copies = load_all([(qkv_hbm, qkv_w), (x_hbm, x), (base_hbm, base), (state_hbm, state)], sems)
    for copy in copies:
        copy.start()
    attention_backward(d_attn_ref.at[0, 0], out_w, qkv_w, cos_ref, sin_ref, q_ref, kz_ref, vz_ref, p_ref, do_ref, du_ref.at[0])
    for copy in copies:
        copy.wait()
    term = finish_attention_backward(x, gain_one[...], active_ref.at[0], du_ref.at[0], qkv_w, base, state, total, d_input_ref)
    small_ref[...] = small_in[...]
    small_ref[0:1, :] = small_in[0:1, :] + term


def swap_dp(values_in, bit, n_dp):
    return lax.ppermute(values_in, "dp", [(i, i ^ (1 << bit)) for i in range(n_dp)])


def swap_mp(values_in):
    return lax.ppermute(values_in, "mp", [(0, 1), (1, 0)])


def halving(parts, order, n_dp, index):
    bits = n_dp.bit_length() - 1
    left = list(range(bits - 1, -1, -1))
    shape = parts.shape[1:]
    held = parts.reshape((2,) * bits + shape)
    for step, bit in enumerate(order):
        at = left.index(bit)
        upper = ((index >> bit) & 1) == 1
        low = lax.index_in_dim(held, 0, at, keepdims=False)
        high = lax.index_in_dim(held, 1, at, keepdims=False)
        keep, send = jnp.where(upper, high, low), jnp.where(upper, low, high)
        got = swap_dp(send, bit, n_dp)
        last = step == bits - 1
        total = keep.astype(F32) + got.astype(F32)
        held = total if last else total.astype(BF)
        left.remove(bit)
    return held


def orders_of(bits):
    rest = list(range(3, bits))
    if bits < 3:
        return [list(range(bits))] * 3
    return [[0, 1, 2] + rest, [1, 0, 2] + rest, [2, 0, 1] + rest]


PART = 2 * LANES
FFN_TILES = (4, 4, 2)
FFN_ORDERS = (((2, 1, 3, 0), (2, 0, 3, 1)), ((1, 2, 0, 3), (0, 2, 1, 3)), ((2, 0, 3, 1), (2, 1, 3, 0)))
ATTN_ORDER = ((0, 1, 2, 3), (1, 0, 2, 3))
SCHEDULE = (
    "T0", "T1", "A", "T2",
    "F0", "F1", "A0", "F2",
    "F0", "F1", "A0", "F2",
    "A0", "F0 F1", "F2",
)
SMALL = 64


def of_core(pair):
    first, second = pair
    return first if first == second else jnp.where(lax.axis_index("mp") == 0, first, second)


def halves(bits, places, count):
    mine = (lax.axis_index("dp") >> of_core(bits)) & 1
    place = of_core(places)
    for i in range(count):
        base = ((i >> place) << (place + 1)) | (i & ((1 << place) - 1))
        yield i, base | (mine << place), base | ((1 - mine) << place)


def stacked_copies(pairs, sems):
    flat_pairs = []
    for sources, target in pairs:
        rows = target.shape[0] // 2
        flat_pairs += [(source, target.at[pl.ds(i * rows, rows)]) for i, source in enumerate(sources)]
    copies = load_all(flat_pairs, sems)
    for copy in copies:
        copy.start()
    return [copies[i : i + 2] for i in range(0, len(copies), 2)]


def ffn_terms(split, tiles, at, at_b, n2_df_a, n2_df_b, units_a, units_b, token, keep_ref, send_ref, left, gate_up, down, flat, sems):
    width, part = left.shape[2], down.shape[1]
    columns, columns_b = (pl.ds(start, tiles * LANES) for start in (at, at_b))
    lefts = [(n2_df_a.at[i], n2_df_b.at[i]) for i in range(2)]
    m, dg, dw = [(units_a.at[i, :, columns], units_b.at[i, :, columns_b]) for i in range(3)]
    n2, dg, dw, df, m = stacked_copies(
        [(lefts[0], left.at[0]), (dg, gate_up.at[:, :part]), (dw, gate_up.at[:, part:]), (lefts[1], left.at[1]), (m, down)], sems)
    for which, (right, needed) in enumerate(((gate_up, n2 + dg + dw), (down, df + m))):
        for copy in needed:
            copy.wait()
        terms = contract_rows(left[which], right[...])
        for at_lane in range(0, right.shape[1], LANES):
            matrix, c = divmod(at_lane // LANES, tiles)
            start = tiles * width * (2 * which + matrix) + c
            flat[pl.ds(start, width, stride=tiles), :] = terms[:, at_lane : at_lane + LANES]
    count, rows, _ = keep_ref.shape
    for i, kept, sent in halves(*split, count):
        for out, shard in ((keep_ref, kept), (send_ref, sent)):
            out[i] = flat[pl.ds(pl.multiple_of(shard * rows, 8), rows), :].astype(BF)


def small_rows(small, packed):
    packed[...] = jnp.zeros(packed.shape, F32)
    width = small.shape[1]
    for i in range(2 + RECURSIONS):
        for c in range(CHUNKS):
            stop = min(width, (c + 1) * LANES)
            packed[i * CHUNKS + c : i * CHUNKS + c + 1, : stop - c * LANES] = small[i : i + 1, c * LANES : stop]
    return packed[...]


def split_small(small, ref, start):
    high = small.astype(BF)
    ref[start : start + SMALL, :] = high
    ref[start + SMALL : start + 2 * SMALL, :] = (small - high.astype(F32)).astype(BF)


def rounded_small(small):
    high = small.astype(BF)
    return high.astype(F32) + (small - high.astype(F32)).astype(BF).astype(F32)


def joined_small(ref, start):
    return ref[start : start + SMALL, :].astype(F32) + ref[start + SMALL : start + 2 * SMALL, :].astype(F32)


def attn_terms(split, depth, n1_a, n1_b, du_a, du_b, o_da_a, o_da_b, small, token,
               keep, send, small_out, left, du_rows, da_rows, turned, own, terms, flat, packed, sems):
    base, count = 0, own.shape[0] // 2
    lower = lane_of(count) < HEAD_DIM
    core = lax.axis_index("mp")
    n1, du, o, da = stacked_copies(
        [((n1_a, n1_b), left.at[0]), ((du_a, du_b), du_rows), ((o_da_a.at[0], o_da_b.at[0]), left.at[1]),
         ((o_da_a.at[1], o_da_b.at[1]), da_rows)], sems)
    for which, (right, needed) in enumerate(((du_rows, n1 + du), (da_rows, o + da))):
        for copy in needed:
            copy.wait()
        columns = right.shape[1]
        half = columns // LANES
        turned[...] = left[which].T
        group = depth * LANES // columns
        for i in range(own.shape[0] // group):
            own[i * group : (i + 1) * group, :] = turned[pl.ds(pl.multiple_of((2 * i + core) * group, 16), group), :]
        for start in range(0, columns, PART):
            stop = min(columns, start + PART)
            block = plain(own[...], right[:, start:stop])
            if stop - start < PART:
                block = jnp.concatenate([block, jnp.zeros((2 * count, PART - (stop - start)), F32)], axis=1)
            for part in range(0, stop - start, LANES):
                terms[(start + part) // LANES] = block[:, part : part + LANES]
        step = 2 * columns // LANES
        after = first_odd = None
        for c in range(half + 1):
            even = terms[c, pl.ds(0, count, stride=2), :]
            odd = other_half(terms[c, pl.ds(1, count, stride=2), :])
            if c < half:
                flat[pl.ds(base + c, count, stride=step), :] = even
            else:
                flat[pl.ds(base + c, count, stride=step), :] = jnp.where(lower, even, first_odd)
            if c == 0:
                first_odd = odd
            else:
                flat[pl.ds(base + half + c, count, stride=step), :] = jnp.where(lower, after, odd)
            after = odd
        base += 2 * count * columns // LANES
    total = rounded_small(small_rows(small, packed))
    small_out[...] = total
    shards, rows, _ = keep.shape
    split_small(total, send, shards * rows)

    def rows_of_shard(shard):
        return flat[pl.ds(pl.multiple_of(shard * depth, 8), rows), :].astype(BF)

    for i, kept, sent in halves(*split, shards):
        keep[i] = rows_of_shard(kept)
        send[i * rows : (i + 1) * rows, :] = rows_of_shard(sent)


def fold(split, kept, got, token, keep, send):
    for i, *shards in halves(*split, keep.shape[0]):
        for out, shard in zip((keep, send), shards):
            out[i] = (kept[shard].astype(F32) + got[shard].astype(F32)).astype(BF)


def fold_small(split, kept, got, small, token, keep, send, small_out):
    held, rows, _ = kept.shape
    for i, *shards in halves(*split, held // 2):
        totals = [(kept[shard].astype(F32) + got[pl.ds(pl.multiple_of(shard * rows, 16), rows), :].astype(F32)).astype(BF)
                  for shard in shards]
        keep[i] = totals[0]
        send[i * rows : (i + 1) * rows, :] = totals[1]
    total = rounded_small(small[...]) + joined_small(got, held * rows)
    small_out[...] = total
    split_small(total, send, held // 2 * rows)


def fold_group(folds, *refs):
    inputs, results = refs, refs[sum(n for _, n, _ in folds) + 1 :]
    token = refs[sum(n for _, n, _ in folds)]
    for function, n_in, n_out in folds:
        function(*inputs[:n_in], token, *results[:n_out])
        inputs, results = inputs[n_in:], results[n_out:]


def finish_small(got, small, token, total_ref, send):
    total = rounded_small(small[...]) + joined_small(got, got.shape[0] - 2 * SMALL)
    total_ref[...] = total
    split_small(total, send, 0)


def finish_attn(kept, got, small, far, token, attn_out, one_out, two_out, router_out, packed):
    padded = kept.shape[0]
    both = kept[...].astype(F32) + got[:padded, :].astype(F32)
    attn_out[...] = both[: attn_out.shape[0]]
    packed[...] = rounded_small(small[...]) + joined_small(far, 0)
    width = one_out.shape[1]
    outs = [(one_out, 0), (two_out, 0), *[(router_out, i) for i in range(RECURSIONS)]]
    for i, (out, row) in enumerate(outs):
        for c in range(CHUNKS):
            stop = min(width, (c + 1) * LANES)
            out[row : row + 1, c * LANES : stop] = packed[i * CHUNKS + c : i * CHUNKS + c + 1, : stop - c * LANES]


def finish_ffn(tiles, *refs):
    feeds, (_, ffn_out, flat) = refs[:-3], refs[-3:]
    every = sum(tiles)
    rows = ffn_out.shape[0] // every
    base = 0
    for i, wide in enumerate(tiles):
        flat[: rows * wide, :] = feeds[2 * i][...].astype(F32) + feeds[2 * i + 1][...].astype(F32)
        for c in range(wide):
            ffn_out[pl.ds(base + c, rows, stride=every), :] = flat[pl.ds(c, rows, stride=wide), :]
        base += wide


class Stream:
    def __init__(self, orders, bits):
        self.orders, self.left, self.done = orders, [list(range(bits - 1, -1, -1)) for _ in orders], 0
        self.kept = self.got = None

    def split(self):
        bits = tuple(order[self.done] for order in self.orders)
        return bits, tuple(len(left) - 1 - left.index(bit) for left, bit in zip(self.left, bits))

    def sent(self, kept, send, n_dp):
        bits = self.split()[0]
        pairs = [(2 * d + core, 2 * (d ^ (1 << bit)) + core) for d in range(n_dp) for core, bit in enumerate(bits)]
        self.kept, self.got = kept, lax.ppermute(send, ("dp", "mp"), pairs)
        for left, bit in zip(self.left, bits):
            left.remove(bit)
        self.done += 1


def on_device(
    hidden_in,
    sel_one,
    sel_two,
    sel_three,
    segment_ids,
    pad_mask,
    qkv_weight,
    out_weight,
    gate_weight,
    up_weight,
    down_weight,
    norm_one,
    norm_two,
    router_weight,
    d_hidden,
):
    seq_len, width = hidden_in.shape
    n_dp, n_mp = lax.axis_size("dp"), lax.axis_size("mp")
    dp_index, mp_index = lax.axis_index("dp"), lax.axis_index("mp")
    cosine, sine = rotary_tables(seq_len)
    weights = [(gate_weight, up_weight, down_weight)]
    weights.append(tuple(swap_mp(w) for w in weights[0]))
    gain_one, gain_two = norm_one.reshape(1, width), norm_two.reshape(1, width)
    padded = CHUNKS * LANES
    units = gate_weight.shape[1]
    feed_weights = (*weights[0], *weights[1])

    def shape(*dims, dtype=BF):
        return jax.ShapeDtypeStruct(dims, dtype)

    def whole(*dims, **kw):
        return pl.BlockSpec(dims, lambda *_: (0,) * len(dims), **kw)

    anywhere = pl.BlockSpec(memory_space=pl.ANY)
    one = pl.Buffered(1)
    stack = RECURSIONS, seq_len
    heads = (2 * KV_HEADS, seq_len, LANES)
    square = (HEADS, seq_len, seq_len)
    n1, q, kz, vz, p, o_da, attn, n2, bias, active, near, slope_first, silu_first, f_first = pl.pallas_call(
        first_attention,
        grid=(1,),
        in_specs=[
            whole(seq_len, width), *[whole(*ref.shape) for ref in (sel_one, sel_two, sel_three, segment_ids, pad_mask)],
            whole(seq_len, LANES), whole(seq_len, LANES), whole(1, width), whole(1, width), whole(*qkv_weight.shape), whole(*out_weight.shape),
            *[anywhere] * 3,
        ],
        out_specs=[
            whole(1, seq_len, width), whole(seq_len, padded), whole(*heads), whole(*heads), whole(*square),
            whole(1, 1, seq_len, width), whole(seq_len, width), whole(seq_len, width), whole(RECURSIONS, seq_len, seq_len), whole(*stack, 1),
            whole(1, 1, seq_len, units), whole(seq_len, units), whole(seq_len, units), whole(seq_len, width),
        ],
        out_shape=[
            shape(*stack, width), shape(seq_len, padded), shape(*heads), shape(*heads), shape(*square),
            shape(2, *stack, width), shape(seq_len, width, dtype=F32), shape(seq_len, width),
            shape(*stack, seq_len, dtype=F32), shape(*stack, 1, dtype=F32),
            shape(3, *stack, units), shape(seq_len, units), shape(seq_len, units), shape(seq_len, width, dtype=F32),
        ],
        scratch_shapes=[*[pltpu.VMEM(w.shape, BF) for w in weights[0]], pltpu.SemaphoreType.DMA((3,))],
        compiler_params=pltpu.CompilerParams(vmem_limit_bytes=VMEM_BYTES),
        cost_estimate=pl.CostEstimate(flops=2 * 10**9, bytes_accessed=12 * 10**6, transcendentals=600000),
        name="first_attention",
    )(hidden_in, sel_one, sel_two, sel_three, segment_ids, pad_mask, cosine, sine, gain_one, gain_two, qkv_weight, out_weight,
      *weights[0])
    attention_0 = (q, kz, vz, p)
    wide = qkv_weight.shape[1]
    row = (seq_len, width)
    kept = RECURSIONS - 1
    first_part = FFN_TILES[0] * LANES
    vm = pltpu.VMEM
    results = pl.pallas_call(
        all_steps,
        grid=(1,),
        in_specs=[
            whole(RECURSIONS, seq_len, seq_len), whole(RECURSIONS, seq_len, 1), whole(RECURSIONS, width),
            whole(seq_len, LANES), whole(seq_len, LANES), whole(1, width), whole(1, width), *[anywhere] * 18,
        ],
        out_specs=[*[anywhere] * 8, whole(*row), whole(*row), whole(8, width)],
        out_shape=[
            shape(*stack, width), *[shape(2, *stack, width)] * 2, shape(3, *stack, units), shape(3, *stack, first_part), shape(3, *stack, units - first_part), shape(*stack, wide),
            *[shape(*row, dtype=F32)] * 3, shape(8, width, dtype=F32),
        ],
        scratch_shapes=[
            *[vm(w.shape, BF) for w in (qkv_weight, out_weight, *feed_weights)],
            vm((RECURSIONS + 1, *row), F32), vm((RECURSIONS, *row), F32), vm((RECURSIONS, *row), BF),
            *[vm((*stack, units), BF)] * 4, vm((kept, seq_len, padded), BF), vm((kept, *heads), BF), vm((kept, *heads), BF),
            vm((kept, *square), BF), *[vm(row, BF)] * 3, *[vm((seq_len, units), BF)] * 2, vm(row, BF), *[vm((seq_len, units), BF)] * 4,
            vm(row, BF), vm((seq_len, wide), BF), vm(row, F32), vm(row, F32), vm((seq_len, padded), BF),
            pltpu.SemaphoreType.DMA((15,)), pltpu.SemaphoreType.DMA((16,)),
        ],
        input_output_aliases={14: 0, 15: 1, 16: 3},
        compiler_params=pltpu.CompilerParams(vmem_limit_bytes=VMEM_BYTES),
        cost_estimate=pl.CostEstimate(flops=23 * 10**9, bytes_accessed=50 * 10**6, transcendentals=4 * 10**6),
        name="all_steps",
    )(bias, active, router_weight, cosine, sine, gain_one, gain_two, hidden_in, d_hidden, attn, n2,
      slope_first, silu_first, f_first, n1, o_da, near,
      qkv_weight, out_weight, *feed_weights)
    n1, o_da, n2_df, near, far, late, du, state, base, grad_state, small = results

    def run_last(token):
        return pl.pallas_call(
            last_attention,
            grid=(1,),
            in_specs=[
                whole(1, seq_len, 1), whole(seq_len, LANES), whole(seq_len, LANES), whole(1, width),
                whole(seq_len, padded), whole(*heads), whole(*heads), whole(*square),
                pl.BlockSpec((1, 1, seq_len, width), lambda i: (1, 0, 0, 0)), whole(8, width), whole(*out_weight.shape), *[anywhere] * 6,
            ],
            out_specs=[whole(1, seq_len, qkv_weight.shape[1]), whole(seq_len, width), whole(8, width)],
            out_shape=[shape(*stack, qkv_weight.shape[1]), shape(seq_len, width, dtype=F32), shape(8, width, dtype=F32)],
            scratch_shapes=[
                pltpu.VMEM((seq_len, padded), BF), *[pltpu.VMEM((seq_len, width), F32)] * 4,
                pltpu.VMEM(qkv_weight.shape, BF), pltpu.SemaphoreType.DMA((4,)),
            ],
            input_output_aliases={15: 0},
            compiler_params=pltpu.CompilerParams(vmem_limit_bytes=VMEM_BYTES),
            cost_estimate=pl.CostEstimate(flops=1, bytes_accessed=1, transcendentals=0),
            name="last_attention",
        )(active, cosine, sine, gain_one, *attention_0, o_da, small, out_weight, hidden_in, base, grad_state, qkv_weight, du, token)

    def rows_of(stacked):
        return stacked.reshape(*stacked.shape[:-3], -1, stacked.shape[-1])

    bits = n_dp.bit_length() - 1
    share = (qkv_weight.size + out_weight.size) // (n_dp * n_mp)
    if bits == 4 and 3 * width % n_dp == 0 and units == sum(FFN_TILES) * LANES and share % (16 * qkv_weight.shape[1]) == share % (16 * width) == 0:
        n2_df_rows = [rows_of(t) for t in (n2_df, swap_mp(n2_df))]
        near, far_b = rows_of(near), rows_of(swap_mp(far))
        n1_b = rows_of(swap_mp(n1))
        streams = [Stream(order, bits) for order in FFN_ORDERS]
        attn_stream = Stream(ATTN_ORDER, bits)
        depth = share // LANES
        tiled = -(-depth // 16) * 16
        common = dict(
            grid=(1,),
            compiler_params=pltpu.CompilerParams(vmem_limit_bytes=VMEM_BYTES),
            cost_estimate=pl.CostEstimate(flops=1, bytes_accessed=1, transcendentals=0),
        )

        def wholes(arrays):
            return [whole(*t.shape) for t in arrays]

        def terms_of(j, token):
            stream, tiles = streams[j], FFN_TILES[j]
            at = sum(FFN_TILES[:j]) * LANES
            factors = (*n2_df_rows, near, far_b if j == 0 else late_b)
            dims = (n_dp // 2, 3 * width // n_dp * tiles, LANES)
            both = 2 * RECURSIONS * seq_len
            keep, send = pl.pallas_call(
                functools.partial(ffn_terms, stream.split(), tiles, at, 0 if j == 0 else at - first_part),
                in_specs=[anywhere] * (len(factors) + 1),
                out_specs=[whole(*dims)] * 2,
                out_shape=[shape(*dims)] * 2,
                scratch_shapes=[pltpu.VMEM((2, both, width), BF), *[pltpu.VMEM((both, n * tiles * LANES), BF) for n in (2, 1)],
                                pltpu.VMEM((3 * width * tiles, LANES), F32), pltpu.SemaphoreType.DMA((10,))],
                name=f"ffn_terms_{j}",
                **common,
            )(*factors, token)
            stream.sent(keep, send, n_dp)
            return keep

        def fold_streams(group, token, small_own):
            folds, operands, outs = [], [], []
            for stream in group:
                count, rows, _ = stream.kept.shape
                held = (count // 2, rows, LANES)
                operands += [stream.kept, stream.got]
                if stream is attn_stream:
                    operands.append(small_own)
                    outs += [shape(*held), shape(count // 2 * rows + 2 * SMALL, LANES), shape(SMALL, LANES, dtype=F32)]
                    folds.append((functools.partial(fold_small, stream.split()), 3, 3))
                else:
                    outs += [shape(*held), shape(*held)]
                    folds.append((functools.partial(fold, stream.split()), 2, 2))
            results = pl.pallas_call(
                functools.partial(fold_group, folds),
                in_specs=[*wholes(operands), anywhere],
                out_specs=wholes(outs),
                out_shape=outs,
                name="fold_terms",
                **common,
            )(*operands, token)
            token = results[0]
            for stream, (_, _, n_out) in zip(group, folds):
                stream.sent(results[0], results[1], n_dp)
                small_own = results[2] if n_out == 3 else small_own
                results = results[n_out:]
            return token, small_own

        du, grad_state, small = run_last(small)
        late, du, small = lax.optimization_barrier((late, du, small))
        late_b, du_b = rows_of(swap_mp(late)), rows_of(swap_mp(du))
        token, small_own = small, None
        for item in SCHEDULE:
            if item[0] == "T":
                token = terms_of(int(item[1:]), token)
                if item == "T0":
                    o_da, token = lax.optimization_barrier((o_da, token))
                    o_da_b = rows_of(swap_mp(o_da))
            elif item == "A":
                dims = (n_dp // 2, tiled, LANES)
                operands = (rows_of(n1), n1_b, rows_of(du), du_b, rows_of(o_da), o_da_b, small)
                outs = (shape(*dims), shape(n_dp // 2 * tiled + 2 * SMALL, LANES), shape(SMALL, LANES, dtype=F32))
                keep, send, small_own = pl.pallas_call(
                    functools.partial(attn_terms, attn_stream.split(), depth),
                    in_specs=[*[anywhere] * 6, *wholes(operands[6:]), anywhere],
                    out_specs=wholes(outs),
                    out_shape=outs,
                    scratch_shapes=[pltpu.VMEM((2, 2 * RECURSIONS * seq_len, width), BF),
                                    *[pltpu.VMEM((2 * RECURSIONS * seq_len, t.shape[-1]), BF) for t in (du, o_da)],
                                    pltpu.VMEM((width, 2 * RECURSIONS * seq_len), BF),
                                    pltpu.VMEM((width // 2, 2 * RECURSIONS * seq_len), BF),
                                    pltpu.VMEM((-(-du.shape[-1] // PART) * 2, width // 2, LANES), F32),
                                    pltpu.VMEM((n_dp * depth + tiled - depth, LANES), F32), pltpu.VMEM((SMALL, LANES), F32),
                                    pltpu.SemaphoreType.DMA((8,))],
                    name="attn_terms",
                    **common,
                )(*operands, token)
                attn_stream.sent(keep, send, n_dp)
                token = small_own
            else:
                group = [attn_stream if name == "A0" else streams[int(name[1:])] for name in item.split()]
                token, small_own = fold_streams(group, token, small_own)
        attn_kept = attn_stream.kept.reshape(tiled, LANES)
        outs = (shape(SMALL, LANES, dtype=F32), shape(2 * SMALL, LANES))
        small_own, small_send = pl.pallas_call(
            finish_small,
            in_specs=[*wholes((attn_stream.got, small_own)), anywhere],
            out_specs=wholes(outs),
            out_shape=outs,
            name="finish_small",
            **common,
        )(attn_stream.got, small_own, token)
        operands = (attn_kept, attn_stream.got, small_own, swap_mp(small_send))
        outs = (shape(depth, LANES, dtype=F32), shape(1, width, dtype=F32), shape(1, width, dtype=F32),
                shape(RECURSIONS, width, dtype=F32))
        attn_flat, one, two, router = pl.pallas_call(
            finish_attn,
            in_specs=[*wholes(operands), anywhere],
            out_specs=wholes(outs),
            out_shape=outs,
            scratch_shapes=[pltpu.VMEM((SMALL, LANES), F32)],
            name="finish_attn",
            **common,
        )(*operands, small_own)
        ends = [t.reshape(t.shape[-2:]) for stream in streams for t in (stream.kept, stream.got)]
        ffn_rows = (3 * width // n_dp * sum(FFN_TILES), LANES)
        ffn_flat = pl.pallas_call(
            functools.partial(finish_ffn, FFN_TILES),
            in_specs=[*wholes(ends), anywhere],
            out_specs=whole(*ffn_rows),
            out_shape=shape(*ffn_rows, dtype=F32),
            scratch_shapes=[pltpu.VMEM((3 * width // n_dp * max(FFN_TILES), LANES), F32)],
            name="finish_ffn",
            **common,
        )(*ends, attn_flat)
        return (state, grad_state, attn_flat.reshape(-1), ffn_flat.reshape(1, -1), one.reshape(-1), two.reshape(-1), router)

    du, grad_state, small = run_last(small)
    two, feed = rows_of(n2_df)
    o, d_attn = rows_of(o_da)
    far = jnp.concatenate([far, late], axis=-1)
    sides = [[t[i] for i in (1, 2, 0)] for t in (rows_of(near), rows_of(far))]

    def side_terms(side, columns):
        return jnp.concatenate(
            [
                contract_rows(left, sides[side][which][:, columns]).astype(BF)
                for which, left in enumerate((two, two, feed))
            ],
            axis=0,
        )

    orders = orders_of(bits)
    if 3 * width % n_dp == 0 and units % 1280 == 0:
        fifth = units // 5
        streams = [(orders[i], slice(j * fifth, (j + 1) * fifth)) for i, j in ((0, 0), (1, 1), (2, 2), (0, 3), (1, 4))]
        done = []
        for order, columns in streams:
            terms = side_terms(0, columns).astype(F32) + swap_mp(side_terms(1, columns)).astype(F32)
            done.append(halving(terms.astype(BF).reshape(n_dp, 3 * width // n_dp, fifth), order, n_dp, dp_index))
        ffn_flat = jnp.concatenate(done, axis=1).reshape(1, -1)
    else:
        terms = side_terms(0, slice(None)).astype(F32) + swap_mp(side_terms(1, slice(None))).astype(F32)
        terms = terms.astype(BF).reshape(n_dp, 3 * width * units // n_dp // 128, 128)
        ffn_flat = halving(terms, orders[0], n_dp, dp_index).reshape(1, -1)

    grad_qkv = contract_rows(rows_of(n1), rows_of(du)).astype(BF)
    grad_out = contract_rows(o, d_attn).astype(BF)
    attn = jnp.concatenate([grad_qkv.reshape(-1), grad_out.reshape(-1)]).reshape(n_dp, 2, share // 128, 128)
    keep = jnp.where(mp_index == 0, attn[:, 0], attn[:, 1])
    send = jnp.where(mp_index == 0, attn[:, 1], attn[:, 0])
    attn = (keep.astype(F32) + swap_mp(send).astype(F32)).astype(BF)
    cuts = [0, (share // 128) // 24 * 8, (share // 128) // 12 * 8, share // 128]
    attn_flat = jnp.concatenate(
        [halving(attn[:, a:b], order, n_dp, dp_index) for a, b, order in zip(cuts, cuts[1:], orders)], axis=0
    ).reshape(-1)

    small = small + swap_mp(small)
    for bit in range(bits):
        small = small + swap_dp(small, bit, n_dp)
    return (state, grad_state, attn_flat, ffn_flat, small[0], small[1], small[2 : 2 + RECURSIONS])


def solution(mesh):
    both = P(("dp", "mp"), None)
    in_specs = (
        both,
        both,
        both,
        both,
        both,
        both,
        P(),
        P(),
        P(None, "mp"),
        P(None, "mp"),
        P(None, "mp"),
        P(),
        P(),
        P(),
        both,
    )
    out_specs = (both, both, P(("dp", "mp")), P("mp", "dp"), P(), P(), P())
    return jax.shard_map(
        on_device, mesh=mesh, in_specs=in_specs, out_specs=out_specs, check_vma=False
    )
```

```python
import functools
import math

import jax
import jax.numpy as jnp
import numpy as np
from jax import lax
from jax.experimental import pallas as pl
from jax.experimental.pallas import tpu as pltpu
from jax.sharding import PartitionSpec as P

HEADS = 15
KV_HEADS = 5
HEAD_DIM = 64
RECURSIONS = 3
GROUPS = HEADS // KV_HEADS
EPS = 1e-05
BF = jnp.bfloat16
F32 = jnp.float32


LANES = 128
CHUNKS = -(-HEADS * HEAD_DIM // LANES)
ROWS = 192
BLOCK = 256
MIB = 1 << 20
VMEM_BYTES = 64 * MIB - 65536


def rotary_tables(seq_len):
    half = HEAD_DIM // 2
    frequency = np.float32(100000.0) ** (
        np.float32(-2.0) * np.arange(half, dtype=np.float32) / np.float32(HEAD_DIM)
    )
    angles = np.arange(seq_len, dtype=np.float32)[:, None] * frequency.astype(np.float32)
    cosine, sine = np.cos(angles), np.sin(angles)
    return (
        jnp.asarray(np.concatenate([cosine] * 4, axis=1), F32),
        jnp.asarray(np.concatenate([-sine, sine] * 2, axis=1), F32),
    )


def contract_rows(left, right):
    return lax.dot_general(left, right, (((0,), (0,)), ((), ())), preferred_element_type=F32)


def contract_last(left, right):
    return lax.dot_general(left, right, (((1,), (1,)), ((), ())), preferred_element_type=F32)


def plain(left, right):
    return jnp.dot(left, right, preferred_element_type=F32)


def inverse_rms(rows):
    return lax.rsqrt(jnp.mean(rows * rows, axis=-1, keepdims=True) + EPS)


def norm_back(rows, gain, d_out):
    inv = inverse_rms(rows)
    scaled = d_out * gain
    inner = jnp.mean(scaled * rows, axis=-1, keepdims=True)
    d_rows = inv * scaled - rows * (inv * inv * inv * inner)
    return d_rows, jnp.sum(d_out * rows * inv, axis=0, keepdims=True)


def lane_of(rows):
    return lax.broadcasted_iota(jnp.int32, (rows, LANES), 1)


def swapped(chunk):
    first = lane_of(chunk.shape[0]) % HEAD_DIM < HEAD_DIM // 2
    return jnp.where(first, pltpu.roll(chunk, LANES - 32, 1), pltpu.roll(chunk, 32, 1))


def other_half(chunk):
    return pltpu.roll(chunk, HEAD_DIM, 1)


def over_rows(count, body):
    def lap(i, carry):
        body(pl.ds(pl.multiple_of(i * ROWS, ROWS), ROWS))
        return carry

    lax.fori_loop(0, count // ROWS, lap, 0)


def attention_forward(x_ref, bias_ref, cos_ref, sin_ref, gain, qkv_w, n1_ref, q_ref, kz_ref, vz_ref, p_ref, o_ref):
    seq_len, width = x_ref.shape
    scale = 1.0 / math.sqrt(HEAD_DIM)

    def norm(rows):
        x = x_ref[rows, :]
        n1_ref[rows, :] = (x * inverse_rms(x) * gain).astype(BF)

    over_rows(seq_len, norm)
    lower = lane_of(seq_len) < HEAD_DIM
    n1 = n1_ref[...]

    def spread(ref, head, chunk, upper):
        flipped = other_half(chunk)
        here, there = (flipped, chunk) if upper else (chunk, flipped)
        ref[2 * head] = jnp.where(lower, here, 0.0).astype(BF)
        ref[2 * head + 1] = jnp.where(lower, 0.0, there).astype(BF)

    columns = qkv_w.shape[1]
    for start in range(0, columns, 2 * LANES):
        wide = plain(n1, qkv_w[:, start : min(start + 2 * LANES, columns)])
        for part in range(0, wide.shape[1], LANES):
            chunk = wide[:, part : part + LANES]
            if chunk.shape[1] < LANES:
                chunk = jnp.concatenate([chunk, jnp.zeros_like(chunk)], axis=1)
            at = (start + part) // LANES
            heads = (2 * at, 2 * at + 1)
            if heads[0] < HEADS + KV_HEADS:
                chunk = chunk * cos_ref[...] + swapped(chunk) * sin_ref[...]
                if heads[0] < HEADS:
                    q_ref[:, at * LANES : (at + 1) * LANES] = chunk.astype(BF)
            for upper, head in enumerate(heads):
                if HEADS <= head < HEADS + KV_HEADS:
                    spread(kz_ref, head - HEADS, chunk, upper)
                elif HEADS + KV_HEADS <= head < HEADS + 2 * KV_HEADS:
                    spread(vz_ref, head - HEADS - KV_HEADS, chunk, upper)

    for at in range(CHUNKS):
        query = q_ref[:, at * LANES : (at + 1) * LANES]
        total = None
        for upper in range(2):
            head = 2 * at + upper
            if head < HEADS:
                key = 2 * (head // GROUPS) + upper
                scores = contract_last(query, kz_ref[key]) * scale + bias_ref[...]
                top = jnp.max(scores, axis=-1, keepdims=True)
                exponent = jnp.exp(scores - top)
                share = pl.reciprocal(jnp.sum(exponent, axis=-1, keepdims=True))
                attend = (exponent * share).astype(BF)
                p_ref[head] = attend
                mixed = plain(attend, vz_ref[key])
                total = mixed if total is None else total + mixed
        stop = min(width, (at + 1) * LANES)
        o_ref[:, at * LANES : stop] = total[:, : stop - at * LANES].astype(BF)


def attention_out(x_ref, o_ref, out_w, gain, attn_ref, n2_ref):
    attn_ref[...] = plain(o_ref[...], out_w[...])

    def norm(rows):
        after = x_ref[rows, :] + attn_ref[rows, :]
        n2_ref[rows, :] = (after * inverse_rms(after) * gain).astype(BF)

    over_rows(x_ref.shape[0], norm)


def feed_side(n2_ref, weights, results, ready):
    n2 = n2_ref[...]
    gate_w, up_w, down_w = weights
    m_ref, slope_ref, silu_ref = results
    ready(0, 1)
    for start in range(0, gate_w.shape[1], BLOCK):
        at = slice(start, start + BLOCK)
        g, u = plain(n2, gate_w[:, at]), plain(n2, up_w[:, at])
        s = jax.nn.sigmoid(g)
        silu = g * s
        m_ref[:, at] = (silu * u).astype(BF)
        slope_ref[:, at] = (u * s * (1.0 + g * (1.0 - s))).astype(BF)
        silu_ref[:, at] = silu.astype(BF)
    ready(2)
    return contract_last(m_ref[...], down_w[...])


def feed_backward(df_ref, sides, d_two_ref, ready):
    d_feed = df_ref[...]
    for side, (gate_w, up_w, down_w, slope_ref, silu_ref, dg_ref, du_ref) in enumerate(sides):
        ready(3 * side)
        for start in range(0, gate_w.shape[1], BLOCK):
            at = slice(start, start + BLOCK)
            d_hidden = plain(d_feed, down_w[:, at])
            dg_ref[:, at] = (d_hidden * slope_ref[:, at].astype(F32)).astype(BF)
            du_ref[:, at] = (d_hidden * silu_ref[:, at].astype(F32)).astype(BF)
        ready(3 * side + 1, 3 * side + 2)
        part = contract_last(dg_ref[...], gate_w[...]) + contract_last(du_ref[...], up_w[...])
        d_two_ref[...] = part if side == 0 else d_two_ref[...] + part


def attention_backward(d_attn_ref, out_w, qkv_w, cos_ref, sin_ref, q_ref, kz_ref, vz_ref, p_ref, do_ref, du_ref):
    seq_len, width = d_attn_ref.shape
    scale = 1.0 / math.sqrt(HEAD_DIM)
    do_ref[:, :width] = contract_last(d_attn_ref[...], out_w[...]).astype(BF)
    do_ref[:, width:] = jnp.zeros((seq_len, do_ref.shape[1] - width), BF)
    lower = lane_of(seq_len) < HEAD_DIM
    cosine, sine = cos_ref[...], sin_ref[...]

    def back(chunk):
        chunk = chunk * scale
        return chunk * cosine - swapped(chunk) * sine

    waiting, d_k, d_v = None, {}, {}
    for at in range(CHUNKS):
        query, d_mixed = (ref[:, at * LANES : (at + 1) * LANES] for ref in (q_ref, do_ref))
        query_t, d_mixed_t = query.T, d_mixed.T
        d_query = None
        for upper in range(2):
            head = 2 * at + upper
            if head >= HEADS:
                continue
            group = head // GROUPS
            key = 2 * group + upper
            rows = slice(upper * HEAD_DIM, (upper + 1) * HEAD_DIM)
            attend = p_ref[head]
            d_attend = contract_last(d_mixed, vz_ref[key])
            soft = attend.astype(F32)
            weighted = soft * d_attend
            inner = jnp.sum(weighted, axis=-1, keepdims=True)
            d_scores = (weighted - soft * inner).astype(BF)
            part = plain(d_scores, kz_ref[key])
            d_query = part if d_query is None else d_query + part
            for store, term in ((d_k, plain(query_t[rows], d_scores)), (d_v, plain(d_mixed_t[rows], attend))):
                store[group] = term if group not in store else store[group] + term
        if at < CHUNKS - 1:
            du_ref[:, at * LANES : (at + 1) * LANES] = back(d_query).astype(BF)
        else:
            waiting = d_query

    def two_heads(store, first, second):
        return jnp.concatenate([store[first], store[second]], axis=0).T

    tail = jnp.where(lower, waiting, two_heads(d_k, 0, 0))
    du_ref[:, (CHUNKS - 1) * LANES : CHUNKS * LANES] = back(tail).astype(BF)
    for i in range(2):
        at = CHUNKS + i
        du_ref[:, at * LANES : (at + 1) * LANES] = back(two_heads(d_k, 1 + 2 * i, 2 + 2 * i)).astype(BF)
        at = CHUNKS + 2 + i
        du_ref[:, at * LANES : (at + 1) * LANES] = two_heads(d_v, 2 * i, 2 * i + 1).astype(BF)
    at = CHUNKS + 4
    du_ref[:, at * LANES :] = two_heads(d_v, 4, 4)[:, : du_ref.shape[1] - at * LANES].astype(BF)


def router_gate(x, router_row):
    return jax.nn.sigmoid(jnp.sum(x * router_row, axis=-1, keepdims=True))


def masks(select_refs, segment_ref, pad_ref, bias_ref, active_ref):
    seq_len = segment_ref.shape[1]
    square = (seq_len, seq_len)
    query, key = (lax.broadcasted_iota(jnp.int32, square, axis) for axis in (0, 1))
    diagonal = query == key
    segment = segment_ref[...].astype(F32)
    own = jnp.sum(jnp.where(diagonal, segment, 0.0), axis=1, keepdims=True)
    near = (key <= query) & (segment == own)
    real = pad_ref[...] == 1
    for recursion, ref in enumerate(select_refs):
        place = lax.broadcasted_iota(jnp.int32, (seq_len, ref.shape[1]), 0)
        active = jnp.max(jnp.where(ref[...] == place, 1.0, 0.0), axis=1, keepdims=True)
        active_ref[recursion] = active
        along = jnp.sum(jnp.where(diagonal, active, 0.0), axis=0, keepdims=True)
        usable = (along > 0.0) & real
        bias_ref[recursion] = jnp.where(near & (usable | diagonal), 0.0, -1e30)


def first_attention(x_ref, sel_one, sel_two, sel_three, segment_ref, pad_ref, cos_ref, sin_ref, gain_one, gain_two, qkv_w, out_w,
                    gate_hbm, up_hbm, down_hbm, n1_ref, q_ref, kz_ref, vz_ref, p_ref, o_ref, attn_ref, n2_ref, bias_ref, active_ref,
                    m_ref, slope_ref, silu_ref, f_ref, gate_w, up_w, down_w, sems):
    copies = load_all([(gate_hbm, gate_w), (up_hbm, up_w), (down_hbm, down_w)], sems)
    for copy in copies:
        copy.start()
    n1, o = n1_ref.at[0], o_ref.at[0, 0]
    masks((sel_one, sel_two, sel_three), segment_ref, pad_ref, bias_ref, active_ref)
    attention_forward(x_ref, bias_ref.at[0], cos_ref, sin_ref, gain_one[...], qkv_w, n1, q_ref, kz_ref, vz_ref, p_ref, o)
    attention_out(x_ref, o, out_w, gain_two[...], attn_ref, n2_ref)

    def ready(*which):
        for i in which:
            copies[i].wait()

    f_ref[...] = feed_side(n2_ref, (gate_w, up_w, down_w), (m_ref.at[0, 0], slope_ref, silu_ref), ready)


def load_all(pairs, sems):
    return [pltpu.make_async_copy(src, dst, sems.at[i]) for i, (src, dst) in enumerate(pairs)]


def waits_at(condition, copies):
    def ready(*which):
        @pl.when(condition)
        def _():
            for i in which:
                copies[i].wait()

    return ready


def finish_attention_backward(x_ref, gain, active_ref, du_ref, qkv_w, base, state, total, out_ref):
    total[...] = contract_last(du_ref[...], qkv_w[...])
    terms = jnp.zeros((1, state.shape[1]), F32)

    def lap(i, terms):
        rows = pl.ds(pl.multiple_of(i * ROWS, ROWS), ROWS)
        d_rows, term = norm_back(x_ref[rows, :], gain, total[rows, :])
        new = jnp.where(active_ref[rows, :] > 0, base[rows, :] + d_rows, state[rows, :])
        out_ref[rows, :] = new
        return terms + term

    return lax.fori_loop(0, state.shape[0] // ROWS, lap, terms)


def all_steps(bias_ref, active_ref, router_ref, cos_ref, sin_ref, gain_one, gain_two,
              hidden_hbm, d_hidden_hbm, attn0_hbm, n20_hbm, slope_hbm, silu_hbm, f_hbm, n1_in, o_da_in, near_in,
              qkv_hbm, out_hbm, *rest):
    feed_hbm, rest = rest[:6], rest[6:]
    (n1_out, o_da_out, n2_df_out, near_out, far_out, late_out, du_out, final_out, base_ref, state_ref, small_ref), rest = rest[:11], rest[11:]
    qkv_w, out_w, *feed_w = rest[:8]
    (xs, attns, fs, slope0, slope1, silu0, silu1, qs, kzs, vzs, ps, n1, o, n2, m0, m1, df, dg0, dg1, dw0, dw1, da, du,
     total, d_branch, do_ref, load_sems, out_sems) = rest[8:]
    width = state_ref.shape[1]
    first_part = far_out.shape[3]
    laps = state_ref.shape[0] // ROWS
    loads = load_all(
        [*zip(feed_hbm, feed_w), (qkv_hbm, qkv_w), (out_hbm, out_w),
         (n20_hbm, n2), (attn0_hbm, attns.at[0]), (hidden_hbm, xs.at[0]), (d_hidden_hbm, state_ref),
         (f_hbm, total), (slope_hbm, slope0.at[0]), (silu_hbm, silu0.at[0])], load_sems)
    for i in (8, 3, 4, 5, 12, 9, 10, 6, 7, 0, 1, 2, 13, 14, 11):
        loads[i].start()
    loads[8].wait()

    places = dict(n2=[(n2, n2_df_out.at[0])], m0=[(m0, near_out.at[0])], n1=[(n1, n1_out)], o=[(o, o_da_out.at[0])],
                  df=[(df, n2_df_out.at[1])], dg0=[(dg0, near_out.at[1])], dw0=[(dw0, near_out.at[2])],
                  da=[(da, o_da_out.at[1])], du=[(du, du_out)])
    for i, (name, ref) in enumerate((("m1", m1), ("dg1", dg1), ("dw1", dw1))):
        places[name] = [(ref.at[:, :first_part], far_out.at[i]), (ref.at[:, first_part:], late_out.at[i])]
    numbers = {}
    for pairs in places.values():
        for source, target in pairs:
            numbers[id(target)] = len(numbers)

    def leaving(recursion, names):
        return [pltpu.make_async_copy(source, target.at[recursion], out_sems.at[numbers[id(target)]])
                for name in names for source, target in places[name]]

    def start(recursion, *names):
        for copy in leaving(recursion, names):
            copy.start()

    def wait(recursion, *names):
        for copy in leaving(recursion, names):
            copy.wait()

    def forward(r, carry):
        ready, later = (waits_at(r == step, loads) for step in range(2))
        start(r, "n2")

        @pl.when(r > 0)
        def _():
            @pl.when(r > 1)
            def _():
                wait(r - 1, "m0")

            total[...] = feed_side(n2, feed_w[:3], (m0, slope0.at[r], silu0.at[r]), later)
            start(r, "m0")
            wait(r - 1, "m1")

        part = feed_side(n2, feed_w[3:], (m1, slope1.at[r], silu1.at[r]), lambda *which: ready(*[3 + i for i in which]))
        ready(12)
        total[...] = total[...] + part
        start(r, "m1")
        ready(9, 10)
        router_row = router_ref[pl.ds(r, 1), :]

        def finish(rows):
            x = xs[r, rows, :]
            f = total[rows, :].astype(BF)
            fs[r, rows, :] = f
            branch = attns[r, rows, :] + f.astype(F32)
            xs[r + 1, rows, :] = jnp.where(active_ref[r, rows, :] > 0, x + router_gate(x, router_row) * branch, x)

        over_rows(total.shape[0], finish)
        ready(6, 7)
        wait(r, "n2")

        @pl.when(r < RECURSIONS - 1)
        def _():
            @pl.when(r > 0)
            def _():
                wait(r, "n1", "o")

            attention_forward(xs.at[r + 1], bias_ref.at[r + 1], cos_ref, sin_ref, gain_one[...], qkv_w,
                              n1, qs.at[r], kzs.at[r], vzs.at[r], ps.at[r], o)
            start(r + 1, "n1", "o")
            attention_out(xs.at[r + 1], o, out_w, gain_two[...], attns.at[r + 1], n2)

        return carry

    lax.fori_loop(0, RECURSIONS, forward, 0)
    final = pltpu.make_async_copy(xs.at[RECURSIONS], final_out, out_sems.at[15])
    final.start()
    for i in (11, 13, 14):
        loads[i].wait()
    small_ref[...] = jnp.zeros(small_ref.shape, F32)

    def backward(i, carry):
        r = RECURSIONS - 1 - i
        router_row = router_ref[pl.ds(r, 1), :]

        @pl.when(i > 0)
        def _():
            wait(r + 1, "df", "dg0", "dg1", "dw0", "dw1", "da")

        def enter(lap, terms):
            rows = pl.ds(pl.multiple_of(lap * ROWS, ROWS), ROWS)
            x = xs[r, rows, :]
            d_new = jnp.where(active_ref[r, rows, :] > 0, state_ref[rows, :], 0.0)
            gate = router_gate(x, router_row)
            branch = attns[r, rows, :] + fs[r, rows, :].astype(F32)
            d_gate = jnp.sum(d_new * branch, axis=-1, keepdims=True)
            d_logit = d_gate * gate * (1.0 - gate)
            spread = gate * d_new
            d_branch[rows, :] = spread
            df[rows, :] = spread.astype(BF)
            base_ref[rows, :] = d_new + d_logit * router_row
            return terms + jnp.sum(d_logit * x, axis=0, keepdims=True)

        small_ref[pl.ds(2 + r, 1), :] = lax.fori_loop(0, laps, enter, jnp.zeros((1, width), F32))
        start(r, "df")
        feed_backward(df, ((*feed_w[:3], slope0.at[r], silu0.at[r], dg0, dw0), (*feed_w[3:], slope1.at[r], silu1.at[r], dg1, dw1)),
                      total, lambda *which: None)
        start(r, "dg0", "dg1", "dw0", "dw1")

        def leave(lap, terms):
            rows = pl.ds(pl.multiple_of(lap * ROWS, ROWS), ROWS)
            after = xs[r, rows, :] + attns[r, rows, :]
            d_after, term = norm_back(after, gain_two[...], total[rows, :].astype(BF).astype(F32))
            da[rows, :] = (d_branch[rows, :] + d_after).astype(BF)
            base_ref[rows, :] = base_ref[rows, :] + d_after
            return terms + term

        small_ref[1:2, :] = small_ref[1:2, :] + lax.fori_loop(0, laps, leave, jnp.zeros((1, width), F32))
        start(r, "da")

        @pl.when(r > 0)
        def _():
            @pl.when(i > 0)
            def _():
                wait(r + 1, "du")

            attention_backward(da, out_w, qkv_w, cos_ref, sin_ref, qs.at[r - 1], kzs.at[r - 1], vzs.at[r - 1], ps.at[r - 1], do_ref, du)
            start(r, "du")
            term = finish_attention_backward(xs.at[r], gain_one[...], active_ref.at[r], du, qkv_w, base_ref, state_ref, total, state_ref)
            small_ref[0:1, :] = small_ref[0:1, :] + term

        return carry

    lax.fori_loop(0, RECURSIONS, backward, 0)
    wait(RECURSIONS - 1, "m0", "m1", "n1", "o")
    wait(0, "df", "dg0", "dg1", "dw0", "dw1", "da")
    wait(1, "du")
    final.wait()


def last_attention(active_ref, cos_ref, sin_ref, gain_one, q_ref, kz_ref, vz_ref, p_ref, d_attn_ref, small_in, out_w,
                   x_hbm, base_hbm, state_hbm, qkv_hbm, du_in, token, du_ref, d_input_ref, small_ref,
                   do_ref, total, x, base, state, qkv_w, sems):
    copies = load_all([(qkv_hbm, qkv_w), (x_hbm, x), (base_hbm, base), (state_hbm, state)], sems)
    for copy in copies:
        copy.start()
    attention_backward(d_attn_ref.at[0, 0], out_w, qkv_w, cos_ref, sin_ref, q_ref, kz_ref, vz_ref, p_ref, do_ref, du_ref.at[0])
    for copy in copies:
        copy.wait()
    term = finish_attention_backward(x, gain_one[...], active_ref.at[0], du_ref.at[0], qkv_w, base, state, total, d_input_ref)
    small_ref[...] = small_in[...]
    small_ref[0:1, :] = small_in[0:1, :] + term


def swap_dp(values_in, bit, n_dp):
    return lax.ppermute(values_in, "dp", [(i, i ^ (1 << bit)) for i in range(n_dp)])


def swap_mp(values_in):
    return lax.ppermute(values_in, "mp", [(0, 1), (1, 0)])


def halving(parts, order, n_dp, index):
    bits = n_dp.bit_length() - 1
    left = list(range(bits - 1, -1, -1))
    shape = parts.shape[1:]
    held = parts.reshape((2,) * bits + shape)
    for step, bit in enumerate(order):
        at = left.index(bit)
        upper = ((index >> bit) & 1) == 1
        low = lax.index_in_dim(held, 0, at, keepdims=False)
        high = lax.index_in_dim(held, 1, at, keepdims=False)
        keep, send = jnp.where(upper, high, low), jnp.where(upper, low, high)
        got = swap_dp(send, bit, n_dp)
        last = step == bits - 1
        total = keep.astype(F32) + got.astype(F32)
        held = total if last else total.astype(BF)
        left.remove(bit)
    return held


def orders_of(bits):
    rest = list(range(3, bits))
    if bits < 3:
        return [list(range(bits))] * 3
    return [[0, 1, 2] + rest, [1, 0, 2] + rest, [2, 0, 1] + rest]


PART = 2 * LANES
FFN_TILES = (4, 4, 2)
FFN_ORDERS = (((2, 0, 1, 3), (0, 2, 1, 3)), ((1, 0, 2, 3), (0, 2, 1, 3)), ((0, 1, 2, 3), (1, 2, 0, 3)))
ATTN_ORDER = ((1, 2, 0, 3), (2, 1, 0, 3))
SCHEDULE = (
    "T0", "T1", "A", "T2",
    "F0", "F1", "A0", "F2",
    "F0", "F1", "A0", "F2",
    "A0", "F0 F1", "F2",
)
SMALL = 64


def of_core(pair):
    first, second = pair
    return first if first == second else jnp.where(lax.axis_index("mp") == 0, first, second)


def halves(bits, places, count):
    mine = (lax.axis_index("dp") >> of_core(bits)) & 1
    place = of_core(places)
    for i in range(count):
        base = ((i >> place) << (place + 1)) | (i & ((1 << place) - 1))
        yield i, base | (mine << place), base | ((1 - mine) << place)


def stacked_copies(pairs, sems):
    flat_pairs = []
    for sources, target in pairs:
        rows = target.shape[0] // 2
        flat_pairs += [(source, target.at[pl.ds(i * rows, rows)]) for i, source in enumerate(sources)]
    copies = load_all(flat_pairs, sems)
    for copy in copies:
        copy.start()
    return [copies[i : i + 2] for i in range(0, len(copies), 2)]


def ffn_terms(split, tiles, at, at_b, n2_df_a, n2_df_b, units_a, units_b, token, keep_ref, send_ref, left, gate_up, down, flat, sems):
    width, part = left.shape[2], down.shape[1]
    columns, columns_b = (pl.ds(start, tiles * LANES) for start in (at, at_b))
    lefts = [(n2_df_a.at[i], n2_df_b.at[i]) for i in range(2)]
    m, dg, dw = [(units_a.at[i, :, columns], units_b.at[i, :, columns_b]) for i in range(3)]
    n2, dg, dw, df, m = stacked_copies(
        [(lefts[0], left.at[0]), (dg, gate_up.at[:, :part]), (dw, gate_up.at[:, part:]), (lefts[1], left.at[1]), (m, down)], sems)
    for which, (right, needed) in enumerate(((gate_up, n2 + dg + dw), (down, df + m))):
        for copy in needed:
            copy.wait()
        terms = contract_rows(left[which], right[...])
        for at_lane in range(0, right.shape[1], LANES):
            matrix, c = divmod(at_lane // LANES, tiles)
            start = tiles * width * (2 * which + matrix) + c
            flat[pl.ds(start, width, stride=tiles), :] = terms[:, at_lane : at_lane + LANES]
    count, rows, _ = keep_ref.shape
    for i, kept, sent in halves(*split, count):
        for out, shard in ((keep_ref, kept), (send_ref, sent)):
            out[i] = flat[pl.ds(pl.multiple_of(shard * rows, 8), rows), :].astype(BF)


def small_rows(small, packed):
    packed[...] = jnp.zeros(packed.shape, F32)
    width = small.shape[1]
    for i in range(2 + RECURSIONS):
        for c in range(CHUNKS):
            stop = min(width, (c + 1) * LANES)
            packed[i * CHUNKS + c : i * CHUNKS + c + 1, : stop - c * LANES] = small[i : i + 1, c * LANES : stop]
    return packed[...]


def split_small(small, ref, start):
    high = small.astype(BF)
    ref[start : start + SMALL, :] = high
    ref[start + SMALL : start + 2 * SMALL, :] = (small - high.astype(F32)).astype(BF)


def rounded_small(small):
    high = small.astype(BF)
    return high.astype(F32) + (small - high.astype(F32)).astype(BF).astype(F32)


def joined_small(ref, start):
    return ref[start : start + SMALL, :].astype(F32) + ref[start + SMALL : start + 2 * SMALL, :].astype(F32)


def attn_terms(split, depth, n1_a, n1_b, du_a, du_b, o_da_a, o_da_b, small, token,
               keep, send, small_out, left, du_rows, da_rows, turned, own, terms, flat, packed, sems):
    base, count = 0, own.shape[0] // 2
    lower = lane_of(count) < HEAD_DIM
    core = lax.axis_index("mp")
    n1, du, o, da = stacked_copies(
        [((n1_a, n1_b), left.at[0]), ((du_a, du_b), du_rows), ((o_da_a.at[0], o_da_b.at[0]), left.at[1]),
         ((o_da_a.at[1], o_da_b.at[1]), da_rows)], sems)
    for which, (right, needed) in enumerate(((du_rows, n1 + du), (da_rows, o + da))):
        for copy in needed:
            copy.wait()
        columns = right.shape[1]
        half = columns // LANES
        turned[...] = left[which].T
        group = depth * LANES // columns
        for i in range(own.shape[0] // group):
            own[i * group : (i + 1) * group, :] = turned[pl.ds(pl.multiple_of((2 * i + core) * group, 16), group), :]
        for start in range(0, columns, PART):
            stop = min(columns, start + PART)
            block = plain(own[...], right[:, start:stop])
            if stop - start < PART:
                block = jnp.concatenate([block, jnp.zeros((2 * count, PART - (stop - start)), F32)], axis=1)
            for part in range(0, stop - start, LANES):
                terms[(start + part) // LANES] = block[:, part : part + LANES]
        step = 2 * columns // LANES
        after = first_odd = None
        for c in range(half + 1):
            even = terms[c, pl.ds(0, count, stride=2), :]
            odd = other_half(terms[c, pl.ds(1, count, stride=2), :])
            if c < half:
                flat[pl.ds(base + c, count, stride=step), :] = even
            else:
                flat[pl.ds(base + c, count, stride=step), :] = jnp.where(lower, even, first_odd)
            if c == 0:
                first_odd = odd
            else:
                flat[pl.ds(base + half + c, count, stride=step), :] = jnp.where(lower, after, odd)
            after = odd
        base += 2 * count * columns // LANES
    total = rounded_small(small_rows(small, packed))
    small_out[...] = total
    shards, rows, _ = keep.shape
    split_small(total, send, shards * rows)

    def rows_of_shard(shard):
        return flat[pl.ds(pl.multiple_of(shard * depth, 8), rows), :].astype(BF)

    for i, kept, sent in halves(*split, shards):
        keep[i] = rows_of_shard(kept)
        send[i * rows : (i + 1) * rows, :] = rows_of_shard(sent)


def fold(split, kept, got, token, keep, send):
    for i, *shards in halves(*split, keep.shape[0]):
        for out, shard in zip((keep, send), shards):
            out[i] = (kept[shard].astype(F32) + got[shard].astype(F32)).astype(BF)


def fold_small(split, kept, got, small, token, keep, send, small_out):
    held, rows, _ = kept.shape
    for i, *shards in halves(*split, held // 2):
        totals = [(kept[shard].astype(F32) + got[pl.ds(pl.multiple_of(shard * rows, 16), rows), :].astype(F32)).astype(BF)
                  for shard in shards]
        keep[i] = totals[0]
        send[i * rows : (i + 1) * rows, :] = totals[1]
    total = rounded_small(small[...]) + joined_small(got, held * rows)
    small_out[...] = total
    split_small(total, send, held // 2 * rows)


def fold_group(folds, *refs):
    inputs, results = refs, refs[sum(n for _, n, _ in folds) + 1 :]
    token = refs[sum(n for _, n, _ in folds)]
    for function, n_in, n_out in folds:
        function(*inputs[:n_in], token, *results[:n_out])
        inputs, results = inputs[n_in:], results[n_out:]


def finish_small(got, small, token, total_ref, send):
    total = rounded_small(small[...]) + joined_small(got, got.shape[0] - 2 * SMALL)
    total_ref[...] = total
    split_small(total, send, 0)


def finish_attn(kept, got, small, far, token, attn_out, one_out, two_out, router_out, packed):
    padded = kept.shape[0]
    both = kept[...].astype(F32) + got[:padded, :].astype(F32)
    attn_out[...] = both[: attn_out.shape[0]]
    packed[...] = rounded_small(small[...]) + joined_small(far, 0)
    width = one_out.shape[1]
    outs = [(one_out, 0), (two_out, 0), *[(router_out, i) for i in range(RECURSIONS)]]
    for i, (out, row) in enumerate(outs):
        for c in range(CHUNKS):
            stop = min(width, (c + 1) * LANES)
            out[row : row + 1, c * LANES : stop] = packed[i * CHUNKS + c : i * CHUNKS + c + 1, : stop - c * LANES]


def finish_ffn(tiles, *refs):
    feeds, (_, ffn_out, flat) = refs[:-3], refs[-3:]
    every = sum(tiles)
    rows = ffn_out.shape[0] // every
    base = 0
    for i, wide in enumerate(tiles):
        flat[: rows * wide, :] = feeds[2 * i][...].astype(F32) + feeds[2 * i + 1][...].astype(F32)
        for c in range(wide):
            ffn_out[pl.ds(base + c, rows, stride=every), :] = flat[pl.ds(c, rows, stride=wide), :]
        base += wide


class Stream:
    def __init__(self, orders, bits):
        self.orders, self.left, self.done = orders, [list(range(bits - 1, -1, -1)) for _ in orders], 0
        self.kept = self.got = None

    def split(self):
        bits = tuple(order[self.done] for order in self.orders)
        return bits, tuple(len(left) - 1 - left.index(bit) for left, bit in zip(self.left, bits))

    def sent(self, kept, send, n_dp):
        bits = self.split()[0]
        pairs = [(2 * d + core, 2 * (d ^ (1 << bit)) + core) for d in range(n_dp) for core, bit in enumerate(bits)]
        self.kept, self.got = kept, lax.ppermute(send, ("dp", "mp"), pairs)
        for left, bit in zip(self.left, bits):
            left.remove(bit)
        self.done += 1


def on_device(
    hidden_in,
    sel_one,
    sel_two,
    sel_three,
    segment_ids,
    pad_mask,
    qkv_weight,
    out_weight,
    gate_weight,
    up_weight,
    down_weight,
    norm_one,
    norm_two,
    router_weight,
    d_hidden,
):
    seq_len, width = hidden_in.shape
    n_dp, n_mp = lax.axis_size("dp"), lax.axis_size("mp")
    dp_index, mp_index = lax.axis_index("dp"), lax.axis_index("mp")
    cosine, sine = rotary_tables(seq_len)
    weights = [(gate_weight, up_weight, down_weight)]
    weights.append(tuple(swap_mp(w) for w in weights[0]))
    gain_one, gain_two = norm_one.reshape(1, width), norm_two.reshape(1, width)
    padded = CHUNKS * LANES
    units = gate_weight.shape[1]
    feed_weights = (*weights[0], *weights[1])

    def shape(*dims, dtype=BF):
        return jax.ShapeDtypeStruct(dims, dtype)

    def whole(*dims, **kw):
        return pl.BlockSpec(dims, lambda *_: (0,) * len(dims), **kw)

    anywhere = pl.BlockSpec(memory_space=pl.ANY)
    one = pl.Buffered(1)
    stack = RECURSIONS, seq_len
    heads = (2 * KV_HEADS, seq_len, LANES)
    square = (HEADS, seq_len, seq_len)
    n1, q, kz, vz, p, o_da, attn, n2, bias, active, near, slope_first, silu_first, f_first = pl.pallas_call(
        first_attention,
        grid=(1,),
        in_specs=[
            whole(seq_len, width), *[whole(*ref.shape) for ref in (sel_one, sel_two, sel_three, segment_ids, pad_mask)],
            whole(seq_len, LANES), whole(seq_len, LANES), whole(1, width), whole(1, width), whole(*qkv_weight.shape), whole(*out_weight.shape),
            *[anywhere] * 3,
        ],
        out_specs=[
            whole(1, seq_len, width), whole(seq_len, padded), whole(*heads), whole(*heads), whole(*square),
            whole(1, 1, seq_len, width), whole(seq_len, width), whole(seq_len, width), whole(RECURSIONS, seq_len, seq_len), whole(*stack, 1),
            whole(1, 1, seq_len, units), whole(seq_len, units), whole(seq_len, units), whole(seq_len, width),
        ],
        out_shape=[
            shape(*stack, width), shape(seq_len, padded), shape(*heads), shape(*heads), shape(*square),
            shape(2, *stack, width), shape(seq_len, width, dtype=F32), shape(seq_len, width),
            shape(*stack, seq_len, dtype=F32), shape(*stack, 1, dtype=F32),
            shape(3, *stack, units), shape(seq_len, units), shape(seq_len, units), shape(seq_len, width, dtype=F32),
        ],
        scratch_shapes=[*[pltpu.VMEM(w.shape, BF) for w in weights[0]], pltpu.SemaphoreType.DMA((3,))],
        compiler_params=pltpu.CompilerParams(vmem_limit_bytes=VMEM_BYTES),
        cost_estimate=pl.CostEstimate(flops=2 * 10**9, bytes_accessed=12 * 10**6, transcendentals=600000),
        name="first_attention",
    )(hidden_in, sel_one, sel_two, sel_three, segment_ids, pad_mask, cosine, sine, gain_one, gain_two, qkv_weight, out_weight,
      *weights[0])
    attention_0 = (q, kz, vz, p)
    wide = qkv_weight.shape[1]
    row = (seq_len, width)
    kept = RECURSIONS - 1
    first_part = FFN_TILES[0] * LANES
    vm = pltpu.VMEM
    results = pl.pallas_call(
        all_steps,
        grid=(1,),
        in_specs=[
            whole(RECURSIONS, seq_len, seq_len), whole(RECURSIONS, seq_len, 1), whole(RECURSIONS, width),
            whole(seq_len, LANES), whole(seq_len, LANES), whole(1, width), whole(1, width), *[anywhere] * 18,
        ],
        out_specs=[*[anywhere] * 8, whole(*row), whole(*row), whole(8, width)],
        out_shape=[
            shape(*stack, width), *[shape(2, *stack, width)] * 2, shape(3, *stack, units), shape(3, *stack, first_part), shape(3, *stack, units - first_part), shape(*stack, wide),
            *[shape(*row, dtype=F32)] * 3, shape(8, width, dtype=F32),
        ],
        scratch_shapes=[
            *[vm(w.shape, BF) for w in (qkv_weight, out_weight, *feed_weights)],
            vm((RECURSIONS + 1, *row), F32), vm((RECURSIONS, *row), F32), vm((RECURSIONS, *row), BF),
            *[vm((*stack, units), BF)] * 4, vm((kept, seq_len, padded), BF), vm((kept, *heads), BF), vm((kept, *heads), BF),
            vm((kept, *square), BF), *[vm(row, BF)] * 3, *[vm((seq_len, units), BF)] * 2, vm(row, BF), *[vm((seq_len, units), BF)] * 4,
            vm(row, BF), vm((seq_len, wide), BF), vm(row, F32), vm(row, F32), vm((seq_len, padded), BF),
            pltpu.SemaphoreType.DMA((15,)), pltpu.SemaphoreType.DMA((16,)),
        ],
        input_output_aliases={14: 0, 15: 1, 16: 3},
        compiler_params=pltpu.CompilerParams(vmem_limit_bytes=VMEM_BYTES),
        cost_estimate=pl.CostEstimate(flops=23 * 10**9, bytes_accessed=50 * 10**6, transcendentals=4 * 10**6),
        name="all_steps",
    )(bias, active, router_weight, cosine, sine, gain_one, gain_two, hidden_in, d_hidden, attn, n2,
      slope_first, silu_first, f_first, n1, o_da, near,
      qkv_weight, out_weight, *feed_weights)
    n1, o_da, n2_df, near, far, late, du, state, base, grad_state, small = results

    def run_last(token):
        return pl.pallas_call(
            last_attention,
            grid=(1,),
            in_specs=[
                whole(1, seq_len, 1), whole(seq_len, LANES), whole(seq_len, LANES), whole(1, width),
                whole(seq_len, padded), whole(*heads), whole(*heads), whole(*square),
                pl.BlockSpec((1, 1, seq_len, width), lambda i: (1, 0, 0, 0)), whole(8, width), whole(*out_weight.shape), *[anywhere] * 6,
            ],
            out_specs=[whole(1, seq_len, qkv_weight.shape[1]), whole(seq_len, width), whole(8, width)],
            out_shape=[shape(*stack, qkv_weight.shape[1]), shape(seq_len, width, dtype=F32), shape(8, width, dtype=F32)],
            scratch_shapes=[
                pltpu.VMEM((seq_len, padded), BF), *[pltpu.VMEM((seq_len, width), F32)] * 4,
                pltpu.VMEM(qkv_weight.shape, BF), pltpu.SemaphoreType.DMA((4,)),
            ],
            input_output_aliases={15: 0},
            compiler_params=pltpu.CompilerParams(vmem_limit_bytes=VMEM_BYTES),
            cost_estimate=pl.CostEstimate(flops=1, bytes_accessed=1, transcendentals=0),
            name="last_attention",
        )(active, cosine, sine, gain_one, *attention_0, o_da, small, out_weight, hidden_in, base, grad_state, qkv_weight, du, token)

    def rows_of(stacked):
        return stacked.reshape(*stacked.shape[:-3], -1, stacked.shape[-1])

    bits = n_dp.bit_length() - 1
    share = (qkv_weight.size + out_weight.size) // (n_dp * n_mp)
    if bits == 4 and 3 * width % n_dp == 0 and units == sum(FFN_TILES) * LANES and share % (16 * qkv_weight.shape[1]) == share % (16 * width) == 0:
        n2_df_rows = [rows_of(t) for t in (n2_df, swap_mp(n2_df))]
        near, far_b = rows_of(near), rows_of(swap_mp(far))
        n1_b = rows_of(swap_mp(n1))
        streams = [Stream(order, bits) for order in FFN_ORDERS]
        attn_stream = Stream(ATTN_ORDER, bits)
        depth = share // LANES
        tiled = -(-depth // 16) * 16
        common = dict(
            grid=(1,),
            compiler_params=pltpu.CompilerParams(vmem_limit_bytes=VMEM_BYTES),
            cost_estimate=pl.CostEstimate(flops=1, bytes_accessed=1, transcendentals=0),
        )

        def wholes(arrays):
            return [whole(*t.shape) for t in arrays]

        def terms_of(j, token):
            stream, tiles = streams[j], FFN_TILES[j]
            at = sum(FFN_TILES[:j]) * LANES
            factors = (*n2_df_rows, near, far_b if j == 0 else late_b)
            dims = (n_dp // 2, 3 * width // n_dp * tiles, LANES)
            both = 2 * RECURSIONS * seq_len
            keep, send = pl.pallas_call(
                functools.partial(ffn_terms, stream.split(), tiles, at, 0 if j == 0 else at - first_part),
                in_specs=[anywhere] * (len(factors) + 1),
                out_specs=[whole(*dims)] * 2,
                out_shape=[shape(*dims)] * 2,
                scratch_shapes=[pltpu.VMEM((2, both, width), BF), *[pltpu.VMEM((both, n * tiles * LANES), BF) for n in (2, 1)],
                                pltpu.VMEM((3 * width * tiles, LANES), F32), pltpu.SemaphoreType.DMA((10,))],
                name=f"ffn_terms_{j}",
                **common,
            )(*factors, token)
            stream.sent(keep, send, n_dp)
            return keep

        def fold_streams(group, token, small_own):
            folds, operands, outs = [], [], []
            for stream in group:
                count, rows, _ = stream.kept.shape
                held = (count // 2, rows, LANES)
                operands += [stream.kept, stream.got]
                if stream is attn_stream:
                    operands.append(small_own)
                    outs += [shape(*held), shape(count // 2 * rows + 2 * SMALL, LANES), shape(SMALL, LANES, dtype=F32)]
                    folds.append((functools.partial(fold_small, stream.split()), 3, 3))
                else:
                    outs += [shape(*held), shape(*held)]
                    folds.append((functools.partial(fold, stream.split()), 2, 2))
            results = pl.pallas_call(
                functools.partial(fold_group, folds),
                in_specs=[*wholes(operands), anywhere],
                out_specs=wholes(outs),
                out_shape=outs,
                name="fold_terms",
                **common,
            )(*operands, token)
            token = results[0]
            for stream, (_, _, n_out) in zip(group, folds):
                stream.sent(results[0], results[1], n_dp)
                small_own = results[2] if n_out == 3 else small_own
                results = results[n_out:]
            return token, small_own

        du, grad_state, small = run_last(small)
        late, du, small = lax.optimization_barrier((late, du, small))
        late_b, du_b = rows_of(swap_mp(late)), rows_of(swap_mp(du))
        token, small_own = small, None
        for item in SCHEDULE:
            if item[0] == "T":
                token = terms_of(int(item[1:]), token)
                if item == "T0":
                    o_da, token = lax.optimization_barrier((o_da, token))
                    o_da_b = rows_of(swap_mp(o_da))
            elif item == "A":
                dims = (n_dp // 2, tiled, LANES)
                operands = (rows_of(n1), n1_b, rows_of(du), du_b, rows_of(o_da), o_da_b, small)
                outs = (shape(*dims), shape(n_dp // 2 * tiled + 2 * SMALL, LANES), shape(SMALL, LANES, dtype=F32))
                keep, send, small_own = pl.pallas_call(
                    functools.partial(attn_terms, attn_stream.split(), depth),
                    in_specs=[*[anywhere] * 6, *wholes(operands[6:]), anywhere],
                    out_specs=wholes(outs),
                    out_shape=outs,
                    scratch_shapes=[pltpu.VMEM((2, 2 * RECURSIONS * seq_len, width), BF),
                                    *[pltpu.VMEM((2 * RECURSIONS * seq_len, t.shape[-1]), BF) for t in (du, o_da)],
                                    pltpu.VMEM((width, 2 * RECURSIONS * seq_len), BF),
                                    pltpu.VMEM((width // 2, 2 * RECURSIONS * seq_len), BF),
                                    pltpu.VMEM((-(-du.shape[-1] // PART) * 2, width // 2, LANES), F32),
                                    pltpu.VMEM((n_dp * depth + tiled - depth, LANES), F32), pltpu.VMEM((SMALL, LANES), F32),
                                    pltpu.SemaphoreType.DMA((8,))],
                    name="attn_terms",
                    **common,
                )(*operands, token)
                attn_stream.sent(keep, send, n_dp)
                token = small_own
            else:
                group = [attn_stream if name == "A0" else streams[int(name[1:])] for name in item.split()]
                token, small_own = fold_streams(group, token, small_own)
        attn_kept = attn_stream.kept.reshape(tiled, LANES)
        outs = (shape(SMALL, LANES, dtype=F32), shape(2 * SMALL, LANES))
        small_own, small_send = pl.pallas_call(
            finish_small,
            in_specs=[*wholes((attn_stream.got, small_own)), anywhere],
            out_specs=wholes(outs),
            out_shape=outs,
            name="finish_small",
            **common,
        )(attn_stream.got, small_own, token)
        operands = (attn_kept, attn_stream.got, small_own, swap_mp(small_send))
        outs = (shape(depth, LANES, dtype=F32), shape(1, width, dtype=F32), shape(1, width, dtype=F32),
                shape(RECURSIONS, width, dtype=F32))
        attn_flat, one, two, router = pl.pallas_call(
            finish_attn,
            in_specs=[*wholes(operands), anywhere],
            out_specs=wholes(outs),
            out_shape=outs,
            scratch_shapes=[pltpu.VMEM((SMALL, LANES), F32)],
            name="finish_attn",
            **common,
        )(*operands, small_own)
        ends = [t.reshape(t.shape[-2:]) for stream in streams for t in (stream.kept, stream.got)]
        ffn_rows = (3 * width // n_dp * sum(FFN_TILES), LANES)
        ffn_flat = pl.pallas_call(
            functools.partial(finish_ffn, FFN_TILES),
            in_specs=[*wholes(ends), anywhere],
            out_specs=whole(*ffn_rows),
            out_shape=shape(*ffn_rows, dtype=F32),
            scratch_shapes=[pltpu.VMEM((3 * width // n_dp * max(FFN_TILES), LANES), F32)],
            name="finish_ffn",
            **common,
        )(*ends, attn_flat)
        return (state, grad_state, attn_flat.reshape(-1), ffn_flat.reshape(1, -1), one.reshape(-1), two.reshape(-1), router)

    du, grad_state, small = run_last(small)
    two, feed = rows_of(n2_df)
    o, d_attn = rows_of(o_da)
    far = jnp.concatenate([far, late], axis=-1)
    sides = [[t[i] for i in (1, 2, 0)] for t in (rows_of(near), rows_of(far))]

    def side_terms(side, columns):
        return jnp.concatenate(
            [
                contract_rows(left, sides[side][which][:, columns]).astype(BF)
                for which, left in enumerate((two, two, feed))
            ],
            axis=0,
        )

    orders = orders_of(bits)
    if 3 * width % n_dp == 0 and units % 1280 == 0:
        fifth = units // 5
        streams = [(orders[i], slice(j * fifth, (j + 1) * fifth)) for i, j in ((0, 0), (1, 1), (2, 2), (0, 3), (1, 4))]
        done = []
        for order, columns in streams:
            terms = side_terms(0, columns).astype(F32) + swap_mp(side_terms(1, columns)).astype(F32)
            done.append(halving(terms.astype(BF).reshape(n_dp, 3 * width // n_dp, fifth), order, n_dp, dp_index))
        ffn_flat = jnp.concatenate(done, axis=1).reshape(1, -1)
    else:
        terms = side_terms(0, slice(None)).astype(F32) + swap_mp(side_terms(1, slice(None))).astype(F32)
        terms = terms.astype(BF).reshape(n_dp, 3 * width * units // n_dp // 128, 128)
        ffn_flat = halving(terms, orders[0], n_dp, dp_index).reshape(1, -1)

    grad_qkv = contract_rows(rows_of(n1), rows_of(du)).astype(BF)
    grad_out = contract_rows(o, d_attn).astype(BF)
    attn = jnp.concatenate([grad_qkv.reshape(-1), grad_out.reshape(-1)]).reshape(n_dp, 2, share // 128, 128)
    keep = jnp.where(mp_index == 0, attn[:, 0], attn[:, 1])
    send = jnp.where(mp_index == 0, attn[:, 1], attn[:, 0])
    attn = (keep.astype(F32) + swap_mp(send).astype(F32)).astype(BF)
    cuts = [0, (share // 128) // 24 * 8, (share // 128) // 12 * 8, share // 128]
    attn_flat = jnp.concatenate(
        [halving(attn[:, a:b], order, n_dp, dp_index) for a, b, order in zip(cuts, cuts[1:], orders)], axis=0
    ).reshape(-1)

    small = small + swap_mp(small)
    for bit in range(bits):
        small = small + swap_dp(small, bit, n_dp)
    return (state, grad_state, attn_flat, ffn_flat, small[0], small[1], small[2 : 2 + RECURSIONS])


def solution(mesh):
    both = P(("dp", "mp"), None)
    in_specs = (
        both,
        both,
        both,
        both,
        both,
        both,
        P(),
        P(),
        P(None, "mp"),
        P(None, "mp"),
        P(None, "mp"),
        P(),
        P(),
        P(),
        both,
    )
    out_specs = (both, both, P(("dp", "mp")), P("mp", "dp"), P(), P(), P())
    return jax.shard_map(
        on_device, mesh=mesh, in_specs=in_specs, out_specs=out_specs, check_vma=False
    )
```

```python
import functools
import math

import jax
import jax.numpy as jnp
import numpy as np
from jax import lax
from jax.experimental import pallas as pl
from jax.experimental.pallas import tpu as pltpu
from jax.sharding import PartitionSpec as P

HEADS = 15
KV_HEADS = 5
HEAD_DIM = 64
RECURSIONS = 3
GROUPS = HEADS // KV_HEADS
EPS = 1e-05
BF = jnp.bfloat16
F32 = jnp.float32


LANES = 128
CHUNKS = -(-HEADS * HEAD_DIM // LANES)
ROWS = 192
BLOCK = 256
MIB = 1 << 20
VMEM_BYTES = 64 * MIB - 65536


def rotary_tables(seq_len):
    half = HEAD_DIM // 2
    frequency = np.float32(100000.0) ** (
        np.float32(-2.0) * np.arange(half, dtype=np.float32) / np.float32(HEAD_DIM)
    )
    angles = np.arange(seq_len, dtype=np.float32)[:, None] * frequency.astype(np.float32)
    cosine, sine = np.cos(angles), np.sin(angles)
    return (
        jnp.asarray(np.concatenate([cosine] * 4, axis=1), F32),
        jnp.asarray(np.concatenate([-sine, sine] * 2, axis=1), F32),
    )


def contract_rows(left, right):
    return lax.dot_general(left, right, (((0,), (0,)), ((), ())), preferred_element_type=F32)


def contract_last(left, right):
    return lax.dot_general(left, right, (((1,), (1,)), ((), ())), preferred_element_type=F32)


def plain(left, right):
    return jnp.dot(left, right, preferred_element_type=F32)


def inverse_rms(rows):
    return lax.rsqrt(jnp.mean(rows * rows, axis=-1, keepdims=True) + EPS)


def norm_back(rows, gain, d_out):
    inv = inverse_rms(rows)
    scaled = d_out * gain
    inner = jnp.mean(scaled * rows, axis=-1, keepdims=True)
    d_rows = inv * scaled - rows * (inv * inv * inv * inner)
    return d_rows, jnp.sum(d_out * rows * inv, axis=0, keepdims=True)


def lane_of(rows):
    return lax.broadcasted_iota(jnp.int32, (rows, LANES), 1)


def swapped(chunk):
    first = lane_of(chunk.shape[0]) % HEAD_DIM < HEAD_DIM // 2
    return jnp.where(first, pltpu.roll(chunk, LANES - 32, 1), pltpu.roll(chunk, 32, 1))


def other_half(chunk):
    return pltpu.roll(chunk, HEAD_DIM, 1)


def over_rows(count, body):
    def lap(i, carry):
        body(pl.ds(pl.multiple_of(i * ROWS, ROWS), ROWS))
        return carry

    lax.fori_loop(0, count // ROWS, lap, 0)


def attention_forward(x_ref, bias_ref, cos_ref, sin_ref, gain, qkv_w, n1_ref, q_ref, kz_ref, vz_ref, p_ref, o_ref):
    seq_len, width = x_ref.shape
    scale = 1.0 / math.sqrt(HEAD_DIM)

    def norm(rows):
        x = x_ref[rows, :]
        n1_ref[rows, :] = (x * inverse_rms(x) * gain).astype(BF)

    over_rows(seq_len, norm)
    lower = lane_of(seq_len) < HEAD_DIM
    n1 = n1_ref[...]

    def spread(ref, head, chunk, upper):
        flipped = other_half(chunk)
        here, there = (flipped, chunk) if upper else (chunk, flipped)
        ref[2 * head] = jnp.where(lower, here, 0.0).astype(BF)
        ref[2 * head + 1] = jnp.where(lower, 0.0, there).astype(BF)

    columns = qkv_w.shape[1]
    for start in range(0, columns, 2 * LANES):
        wide = plain(n1, qkv_w[:, start : min(start + 2 * LANES, columns)])
        for part in range(0, wide.shape[1], LANES):
            chunk = wide[:, part : part + LANES]
            if chunk.shape[1] < LANES:
                chunk = jnp.concatenate([chunk, jnp.zeros_like(chunk)], axis=1)
            at = (start + part) // LANES
            heads = (2 * at, 2 * at + 1)
            if heads[0] < HEADS + KV_HEADS:
                chunk = chunk * cos_ref[...] + swapped(chunk) * sin_ref[...]
                if heads[0] < HEADS:
                    q_ref[:, at * LANES : (at + 1) * LANES] = chunk.astype(BF)
            for upper, head in enumerate(heads):
                if HEADS <= head < HEADS + KV_HEADS:
                    spread(kz_ref, head - HEADS, chunk, upper)
                elif HEADS + KV_HEADS <= head < HEADS + 2 * KV_HEADS:
                    spread(vz_ref, head - HEADS - KV_HEADS, chunk, upper)

    for at in range(CHUNKS):
        query = q_ref[:, at * LANES : (at + 1) * LANES]
        total = None
        for upper in range(2):
            head = 2 * at + upper
            if head < HEADS:
                key = 2 * (head // GROUPS) + upper
                scores = contract_last(query, kz_ref[key]) * scale + bias_ref[...]
                top = jnp.max(scores, axis=-1, keepdims=True)
                exponent = jnp.exp(scores - top)
                share = pl.reciprocal(jnp.sum(exponent, axis=-1, keepdims=True))
                attend = (exponent * share).astype(BF)
                p_ref[head] = attend
                mixed = plain(attend, vz_ref[key])
                total = mixed if total is None else total + mixed
        stop = min(width, (at + 1) * LANES)
        o_ref[:, at * LANES : stop] = total[:, : stop - at * LANES].astype(BF)


def attention_out(x_ref, o_ref, out_w, gain, attn_ref, n2_ref):
    attn_ref[...] = plain(o_ref[...], out_w[...])

    def norm(rows):
        after = x_ref[rows, :] + attn_ref[rows, :]
        n2_ref[rows, :] = (after * inverse_rms(after) * gain).astype(BF)

    over_rows(x_ref.shape[0], norm)


def feed_side(n2_ref, weights, results, ready):
    n2 = n2_ref[...]
    gate_w, up_w, down_w = weights
    m_ref, slope_ref, silu_ref = results
    ready(0, 1)
    for start in range(0, gate_w.shape[1], BLOCK):
        at = slice(start, start + BLOCK)
        g, u = plain(n2, gate_w[:, at]), plain(n2, up_w[:, at])
        s = jax.nn.sigmoid(g)
        silu = g * s
        m_ref[:, at] = (silu * u).astype(BF)
        slope_ref[:, at] = (u * s * (1.0 + g * (1.0 - s))).astype(BF)
        silu_ref[:, at] = silu.astype(BF)
    ready(2)
    return contract_last(m_ref[...], down_w[...])


def feed_backward(df_ref, sides, d_two_ref, ready):
    d_feed = df_ref[...]
    for side, (gate_w, up_w, down_w, slope_ref, silu_ref, dg_ref, du_ref) in enumerate(sides):
        ready(3 * side)
        for start in range(0, gate_w.shape[1], BLOCK):
            at = slice(start, start + BLOCK)
            d_hidden = plain(d_feed, down_w[:, at])
            dg_ref[:, at] = (d_hidden * slope_ref[:, at].astype(F32)).astype(BF)
            du_ref[:, at] = (d_hidden * silu_ref[:, at].astype(F32)).astype(BF)
        ready(3 * side + 1, 3 * side + 2)
        part = contract_last(dg_ref[...], gate_w[...]) + contract_last(du_ref[...], up_w[...])
        d_two_ref[...] = part if side == 0 else d_two_ref[...] + part


def attention_backward(d_attn_ref, out_w, qkv_w, cos_ref, sin_ref, q_ref, kz_ref, vz_ref, p_ref, do_ref, du_ref):
    seq_len, width = d_attn_ref.shape
    scale = 1.0 / math.sqrt(HEAD_DIM)
    do_ref[:, :width] = contract_last(d_attn_ref[...], out_w[...]).astype(BF)
    do_ref[:, width:] = jnp.zeros((seq_len, do_ref.shape[1] - width), BF)
    lower = lane_of(seq_len) < HEAD_DIM
    cosine, sine = cos_ref[...], sin_ref[...]

    def back(chunk):
        chunk = chunk * scale
        return chunk * cosine - swapped(chunk) * sine

    waiting, d_k, d_v = None, {}, {}
    for at in range(CHUNKS):
        query, d_mixed = (ref[:, at * LANES : (at + 1) * LANES] for ref in (q_ref, do_ref))
        query_t, d_mixed_t = query.T, d_mixed.T
        d_query = None
        for upper in range(2):
            head = 2 * at + upper
            if head >= HEADS:
                continue
            group = head // GROUPS
            key = 2 * group + upper
            rows = slice(upper * HEAD_DIM, (upper + 1) * HEAD_DIM)
            attend = p_ref[head]
            d_attend = contract_last(d_mixed, vz_ref[key])
            soft = attend.astype(F32)
            weighted = soft * d_attend
            inner = jnp.sum(weighted, axis=-1, keepdims=True)
            d_scores = (weighted - soft * inner).astype(BF)
            part = plain(d_scores, kz_ref[key])
            d_query = part if d_query is None else d_query + part
            for store, term in ((d_k, plain(query_t[rows], d_scores)), (d_v, plain(d_mixed_t[rows], attend))):
                store[group] = term if group not in store else store[group] + term
        if at < CHUNKS - 1:
            du_ref[:, at * LANES : (at + 1) * LANES] = back(d_query).astype(BF)
        else:
            waiting = d_query

    def two_heads(store, first, second):
        return jnp.concatenate([store[first], store[second]], axis=0).T

    tail = jnp.where(lower, waiting, two_heads(d_k, 0, 0))
    du_ref[:, (CHUNKS - 1) * LANES : CHUNKS * LANES] = back(tail).astype(BF)
    for i in range(2):
        at = CHUNKS + i
        du_ref[:, at * LANES : (at + 1) * LANES] = back(two_heads(d_k, 1 + 2 * i, 2 + 2 * i)).astype(BF)
        at = CHUNKS + 2 + i
        du_ref[:, at * LANES : (at + 1) * LANES] = two_heads(d_v, 2 * i, 2 * i + 1).astype(BF)
    at = CHUNKS + 4
    du_ref[:, at * LANES :] = two_heads(d_v, 4, 4)[:, : du_ref.shape[1] - at * LANES].astype(BF)


def router_gate(x, router_row):
    return jax.nn.sigmoid(jnp.sum(x * router_row, axis=-1, keepdims=True))


def masks(select_refs, segment_ref, pad_ref, bias_ref, active_ref):
    seq_len = segment_ref.shape[1]
    square = (seq_len, seq_len)
    query, key = (lax.broadcasted_iota(jnp.int32, square, axis) for axis in (0, 1))
    diagonal = query == key
    segment = segment_ref[...].astype(F32)
    own = jnp.sum(jnp.where(diagonal, segment, 0.0), axis=1, keepdims=True)
    near = (key <= query) & (segment == own)
    real = pad_ref[...] == 1
    for recursion, ref in enumerate(select_refs):
        place = lax.broadcasted_iota(jnp.int32, (seq_len, ref.shape[1]), 0)
        active = jnp.max(jnp.where(ref[...] == place, 1.0, 0.0), axis=1, keepdims=True)
        active_ref[recursion] = active
        along = jnp.sum(jnp.where(diagonal, active, 0.0), axis=0, keepdims=True)
        usable = (along > 0.0) & real
        bias_ref[recursion] = jnp.where(near & (usable | diagonal), 0.0, -1e30)


def first_attention(x_ref, sel_one, sel_two, sel_three, segment_ref, pad_ref, cos_ref, sin_ref, gain_one, gain_two, qkv_w, out_w,
                    gate_hbm, up_hbm, down_hbm, n1_ref, q_ref, kz_ref, vz_ref, p_ref, o_ref, attn_ref, n2_ref, bias_ref, active_ref,
                    m_ref, slope_ref, silu_ref, f_ref, gate_w, up_w, down_w, sems):
    copies = load_all([(gate_hbm, gate_w), (up_hbm, up_w), (down_hbm, down_w)], sems)
    for copy in copies:
        copy.start()
    n1, o = n1_ref.at[0], o_ref.at[0, 0]
    masks((sel_one, sel_two, sel_three), segment_ref, pad_ref, bias_ref, active_ref)
    attention_forward(x_ref, bias_ref.at[0], cos_ref, sin_ref, gain_one[...], qkv_w, n1, q_ref, kz_ref, vz_ref, p_ref, o)
    attention_out(x_ref, o, out_w, gain_two[...], attn_ref, n2_ref)

    def ready(*which):
        for i in which:
            copies[i].wait()

    f_ref[...] = feed_side(n2_ref, (gate_w, up_w, down_w), (m_ref.at[0, 0], slope_ref, silu_ref), ready)


def load_all(pairs, sems):
    return [pltpu.make_async_copy(src, dst, sems.at[i]) for i, (src, dst) in enumerate(pairs)]


def waits_at(condition, copies):
    def ready(*which):
        @pl.when(condition)
        def _():
            for i in which:
                copies[i].wait()

    return ready


def finish_attention_backward(x_ref, gain, active_ref, du_ref, qkv_w, base, state, total, out_ref):
    total[...] = contract_last(du_ref[...], qkv_w[...])
    terms = jnp.zeros((1, state.shape[1]), F32)

    def lap(i, terms):
        rows = pl.ds(pl.multiple_of(i * ROWS, ROWS), ROWS)
        d_rows, term = norm_back(x_ref[rows, :], gain, total[rows, :])
        new = jnp.where(active_ref[rows, :] > 0, base[rows, :] + d_rows, state[rows, :])
        out_ref[rows, :] = new
        return terms + term

    return lax.fori_loop(0, state.shape[0] // ROWS, lap, terms)


def all_steps(bias_ref, active_ref, router_ref, cos_ref, sin_ref, gain_one, gain_two,
              hidden_hbm, d_hidden_hbm, attn0_hbm, n20_hbm, slope_hbm, silu_hbm, f_hbm, n1_in, o_da_in, near_in,
              qkv_hbm, out_hbm, *rest):
    feed_hbm, rest = rest[:6], rest[6:]
    (n1_out, o_da_out, n2_df_out, near_out, far_out, late_out, du_out, final_out, base_ref, state_ref, small_ref), rest = rest[:11], rest[11:]
    qkv_w, out_w, *feed_w = rest[:8]
    (xs, attns, fs, slope0, slope1, silu0, silu1, qs, kzs, vzs, ps, n1, o, n2, m0, m1, df, dg0, dg1, dw0, dw1, da, du,
     total, d_branch, do_ref, load_sems, out_sems) = rest[8:]
    width = state_ref.shape[1]
    first_part = far_out.shape[3]
    laps = state_ref.shape[0] // ROWS
    loads = load_all(
        [*zip(feed_hbm, feed_w), (qkv_hbm, qkv_w), (out_hbm, out_w),
         (n20_hbm, n2), (attn0_hbm, attns.at[0]), (hidden_hbm, xs.at[0]), (d_hidden_hbm, state_ref),
         (f_hbm, total), (slope_hbm, slope0.at[0]), (silu_hbm, silu0.at[0])], load_sems)
    for i in (8, 3, 4, 5, 12, 9, 10, 6, 7, 0, 1, 2, 13, 14, 11):
        loads[i].start()
    loads[8].wait()

    places = dict(n2=[(n2, n2_df_out.at[0])], m0=[(m0, near_out.at[0])], n1=[(n1, n1_out)], o=[(o, o_da_out.at[0])],
                  df=[(df, n2_df_out.at[1])], dg0=[(dg0, near_out.at[1])], dw0=[(dw0, near_out.at[2])],
                  da=[(da, o_da_out.at[1])], du=[(du, du_out)])
    for i, (name, ref) in enumerate((("m1", m1), ("dg1", dg1), ("dw1", dw1))):
        places[name] = [(ref.at[:, :first_part], far_out.at[i]), (ref.at[:, first_part:], late_out.at[i])]
    numbers = {}
    for pairs in places.values():
        for source, target in pairs:
            numbers[id(target)] = len(numbers)

    def leaving(recursion, names):
        return [pltpu.make_async_copy(source, target.at[recursion], out_sems.at[numbers[id(target)]])
                for name in names for source, target in places[name]]

    def start(recursion, *names):
        for copy in leaving(recursion, names):
            copy.start()

    def wait(recursion, *names):
        for copy in leaving(recursion, names):
            copy.wait()

    def forward(r, carry):
        ready, later = (waits_at(r == step, loads) for step in range(2))
        start(r, "n2")

        @pl.when(r > 0)
        def _():
            @pl.when(r > 1)
            def _():
                wait(r - 1, "m0")

            total[...] = feed_side(n2, feed_w[:3], (m0, slope0.at[r], silu0.at[r]), later)
            start(r, "m0")
            wait(r - 1, "m1")

        part = feed_side(n2, feed_w[3:], (m1, slope1.at[r], silu1.at[r]), lambda *which: ready(*[3 + i for i in which]))
        ready(12)
        total[...] = total[...] + part
        start(r, "m1")
        ready(9, 10)
        router_row = router_ref[pl.ds(r, 1), :]

        def finish(rows):
            x = xs[r, rows, :]
            f = total[rows, :].astype(BF)
            fs[r, rows, :] = f
            branch = attns[r, rows, :] + f.astype(F32)
            xs[r + 1, rows, :] = jnp.where(active_ref[r, rows, :] > 0, x + router_gate(x, router_row) * branch, x)

        over_rows(total.shape[0], finish)
        ready(6, 7)
        wait(r, "n2")

        @pl.when(r < RECURSIONS - 1)
        def _():
            @pl.when(r > 0)
            def _():
                wait(r, "n1", "o")

            attention_forward(xs.at[r + 1], bias_ref.at[r + 1], cos_ref, sin_ref, gain_one[...], qkv_w,
                              n1, qs.at[r], kzs.at[r], vzs.at[r], ps.at[r], o)
            start(r + 1, "n1", "o")
            attention_out(xs.at[r + 1], o, out_w, gain_two[...], attns.at[r + 1], n2)

        return carry

    lax.fori_loop(0, RECURSIONS, forward, 0)
    final = pltpu.make_async_copy(xs.at[RECURSIONS], final_out, out_sems.at[15])
    final.start()
    for i in (11, 13, 14):
        loads[i].wait()
    small_ref[...] = jnp.zeros(small_ref.shape, F32)

    def backward(i, carry):
        r = RECURSIONS - 1 - i
        router_row = router_ref[pl.ds(r, 1), :]

        @pl.when(i > 0)
        def _():
            wait(r + 1, "df", "dg0", "dg1", "dw0", "dw1", "da")

        def enter(lap, terms):
            rows = pl.ds(pl.multiple_of(lap * ROWS, ROWS), ROWS)
            x = xs[r, rows, :]
            d_new = jnp.where(active_ref[r, rows, :] > 0, state_ref[rows, :], 0.0)
            gate = router_gate(x, router_row)
            branch = attns[r, rows, :] + fs[r, rows, :].astype(F32)
            d_gate = jnp.sum(d_new * branch, axis=-1, keepdims=True)
            d_logit = d_gate * gate * (1.0 - gate)
            spread = gate * d_new
            d_branch[rows, :] = spread
            df[rows, :] = spread.astype(BF)
            base_ref[rows, :] = d_new + d_logit * router_row
            return terms + jnp.sum(d_logit * x, axis=0, keepdims=True)

        small_ref[pl.ds(2 + r, 1), :] = lax.fori_loop(0, laps, enter, jnp.zeros((1, width), F32))
        start(r, "df")
        feed_backward(df, ((*feed_w[:3], slope0.at[r], silu0.at[r], dg0, dw0), (*feed_w[3:], slope1.at[r], silu1.at[r], dg1, dw1)),
                      total, lambda *which: None)
        start(r, "dg0", "dg1", "dw0", "dw1")

        def leave(lap, terms):
            rows = pl.ds(pl.multiple_of(lap * ROWS, ROWS), ROWS)
            after = xs[r, rows, :] + attns[r, rows, :]
            d_after, term = norm_back(after, gain_two[...], total[rows, :].astype(BF).astype(F32))
            da[rows, :] = (d_branch[rows, :] + d_after).astype(BF)
            base_ref[rows, :] = base_ref[rows, :] + d_after
            return terms + term

        small_ref[1:2, :] = small_ref[1:2, :] + lax.fori_loop(0, laps, leave, jnp.zeros((1, width), F32))
        start(r, "da")

        @pl.when(r > 0)
        def _():
            @pl.when(i > 0)
            def _():
                wait(r + 1, "du")

            attention_backward(da, out_w, qkv_w, cos_ref, sin_ref, qs.at[r - 1], kzs.at[r - 1], vzs.at[r - 1], ps.at[r - 1], do_ref, du)
            start(r, "du")
            term = finish_attention_backward(xs.at[r], gain_one[...], active_ref.at[r], du, qkv_w, base_ref, state_ref, total, state_ref)
            small_ref[0:1, :] = small_ref[0:1, :] + term

        return carry

    lax.fori_loop(0, RECURSIONS, backward, 0)
    wait(RECURSIONS - 1, "m0", "m1", "n1", "o")
    wait(0, "df", "dg0", "dg1", "dw0", "dw1", "da")
    wait(1, "du")
    final.wait()


def last_attention(active_ref, cos_ref, sin_ref, gain_one, q_ref, kz_ref, vz_ref, p_ref, d_attn_ref, small_in, out_w,
                   x_hbm, base_hbm, state_hbm, qkv_hbm, du_in, token, du_ref, d_input_ref, small_ref,
                   do_ref, total, x, base, state, qkv_w, sems):
    copies = load_all([(qkv_hbm, qkv_w), (x_hbm, x), (base_hbm, base), (state_hbm, state)], sems)
    for copy in copies:
        copy.start()
    attention_backward(d_attn_ref.at[0, 0], out_w, qkv_w, cos_ref, sin_ref, q_ref, kz_ref, vz_ref, p_ref, do_ref, du_ref.at[0])
    for copy in copies:
        copy.wait()
    term = finish_attention_backward(x, gain_one[...], active_ref.at[0], du_ref.at[0], qkv_w, base, state, total, d_input_ref)
    small_ref[...] = small_in[...]
    small_ref[0:1, :] = small_in[0:1, :] + term


def swap_dp(values_in, bit, n_dp):
    return lax.ppermute(values_in, "dp", [(i, i ^ (1 << bit)) for i in range(n_dp)])


def swap_mp(values_in):
    return lax.ppermute(values_in, "mp", [(0, 1), (1, 0)])


def halving(parts, order, n_dp, index):
    bits = n_dp.bit_length() - 1
    left = list(range(bits - 1, -1, -1))
    shape = parts.shape[1:]
    held = parts.reshape((2,) * bits + shape)
    for step, bit in enumerate(order):
        at = left.index(bit)
        upper = ((index >> bit) & 1) == 1
        low = lax.index_in_dim(held, 0, at, keepdims=False)
        high = lax.index_in_dim(held, 1, at, keepdims=False)
        keep, send = jnp.where(upper, high, low), jnp.where(upper, low, high)
        got = swap_dp(send, bit, n_dp)
        last = step == bits - 1
        total = keep.astype(F32) + got.astype(F32)
        held = total if last else total.astype(BF)
        left.remove(bit)
    return held


def orders_of(bits):
    rest = list(range(3, bits))
    if bits < 3:
        return [list(range(bits))] * 3
    return [[0, 1, 2] + rest, [1, 0, 2] + rest, [2, 0, 1] + rest]


PART = 2 * LANES
FFN_TILES = (4, 4, 2)
FFN_ORDERS = (((2, 1, 0, 3), (1, 0, 3, 2)), ((1, 3, 0, 2), (0, 1, 2, 3)), ((2, 0, 1, 3), (1, 0, 2, 3)))
ATTN_ORDER = ((0, 2, 1, 3), (2, 0, 1, 3))
SCHEDULE = (
    "T0", "T1", "A", "T2",
    "F0", "F1", "A0", "F2",
    "F0", "F1", "A0", "F2",
    "A0", "F0 F1", "F2",
)
SMALL = 64


def of_core(pair):
    first, second = pair
    return first if first == second else jnp.where(lax.axis_index("mp") == 0, first, second)


def halves(bits, places, count):
    mine = (lax.axis_index("dp") >> of_core(bits)) & 1
    place = of_core(places)
    for i in range(count):
        base = ((i >> place) << (place + 1)) | (i & ((1 << place) - 1))
        yield i, base | (mine << place), base | ((1 - mine) << place)


def stacked_copies(pairs, sems):
    flat_pairs = []
    for sources, target in pairs:
        rows = target.shape[0] // 2
        flat_pairs += [(source, target.at[pl.ds(i * rows, rows)]) for i, source in enumerate(sources)]
    copies = load_all(flat_pairs, sems)
    for copy in copies:
        copy.start()
    return [copies[i : i + 2] for i in range(0, len(copies), 2)]


def ffn_terms(split, tiles, at, at_b, n2_df_a, n2_df_b, units_a, units_b, token, keep_ref, send_ref, left, gate_up, down, flat, sems):
    width, part = left.shape[2], down.shape[1]
    columns, columns_b = (pl.ds(start, tiles * LANES) for start in (at, at_b))
    lefts = [(n2_df_a.at[i], n2_df_b.at[i]) for i in range(2)]
    m, dg, dw = [(units_a.at[i, :, columns], units_b.at[i, :, columns_b]) for i in range(3)]
    n2, dg, dw, df, m = stacked_copies(
        [(lefts[0], left.at[0]), (dg, gate_up.at[:, :part]), (dw, gate_up.at[:, part:]), (lefts[1], left.at[1]), (m, down)], sems)
    for which, (right, needed) in enumerate(((gate_up, n2 + dg + dw), (down, df + m))):
        for copy in needed:
            copy.wait()
        terms = contract_rows(left[which], right[...])
        for at_lane in range(0, right.shape[1], LANES):
            matrix, c = divmod(at_lane // LANES, tiles)
            start = tiles * width * (2 * which + matrix) + c
            flat[pl.ds(start, width, stride=tiles), :] = terms[:, at_lane : at_lane + LANES]
    count, rows, _ = keep_ref.shape
    for i, kept, sent in halves(*split, count):
        for out, shard in ((keep_ref, kept), (send_ref, sent)):
            out[i] = flat[pl.ds(pl.multiple_of(shard * rows, 8), rows), :].astype(BF)


def small_rows(small, packed):
    packed[...] = jnp.zeros(packed.shape, F32)
    width = small.shape[1]
    for i in range(2 + RECURSIONS):
        for c in range(CHUNKS):
            stop = min(width, (c + 1) * LANES)
            packed[i * CHUNKS + c : i * CHUNKS + c + 1, : stop - c * LANES] = small[i : i + 1, c * LANES : stop]
    return packed[...]


def split_small(small, ref, start):
    high = small.astype(BF)
    ref[start : start + SMALL, :] = high
    ref[start + SMALL : start + 2 * SMALL, :] = (small - high.astype(F32)).astype(BF)


def rounded_small(small):
    high = small.astype(BF)
    return high.astype(F32) + (small - high.astype(F32)).astype(BF).astype(F32)


def joined_small(ref, start):
    return ref[start : start + SMALL, :].astype(F32) + ref[start + SMALL : start + 2 * SMALL, :].astype(F32)


def attn_terms(split, depth, n1_a, n1_b, du_a, du_b, o_da_a, o_da_b, small, token,
               keep, send, small_out, left, du_rows, da_rows, turned, own, terms, flat, packed, sems):
    base, count = 0, own.shape[0] // 2
    lower = lane_of(count) < HEAD_DIM
    core = lax.axis_index("mp")
    n1, du, o, da = stacked_copies(
        [((n1_a, n1_b), left.at[0]), ((du_a, du_b), du_rows), ((o_da_a.at[0], o_da_b.at[0]), left.at[1]),
         ((o_da_a.at[1], o_da_b.at[1]), da_rows)], sems)
    for which, (right, needed) in enumerate(((du_rows, n1 + du), (da_rows, o + da))):
        for copy in needed:
            copy.wait()
        columns = right.shape[1]
        half = columns // LANES
        turned[...] = left[which].T
        group = depth * LANES // columns
        for i in range(own.shape[0] // group):
            own[i * group : (i + 1) * group, :] = turned[pl.ds(pl.multiple_of((2 * i + core) * group, 16), group), :]
        for start in range(0, columns, PART):
            stop = min(columns, start + PART)
            block = plain(own[...], right[:, start:stop])
            if stop - start < PART:
                block = jnp.concatenate([block, jnp.zeros((2 * count, PART - (stop - start)), F32)], axis=1)
            for part in range(0, stop - start, LANES):
                terms[(start + part) // LANES] = block[:, part : part + LANES]
        step = 2 * columns // LANES
        after = first_odd = None
        for c in range(half + 1):
            even = terms[c, pl.ds(0, count, stride=2), :]
            odd = other_half(terms[c, pl.ds(1, count, stride=2), :])
            if c < half:
                flat[pl.ds(base + c, count, stride=step), :] = even
            else:
                flat[pl.ds(base + c, count, stride=step), :] = jnp.where(lower, even, first_odd)
            if c == 0:
                first_odd = odd
            else:
                flat[pl.ds(base + half + c, count, stride=step), :] = jnp.where(lower, after, odd)
            after = odd
        base += 2 * count * columns // LANES
    total = rounded_small(small_rows(small, packed))
    small_out[...] = total
    shards, rows, _ = keep.shape
    split_small(total, send, shards * rows)

    def rows_of_shard(shard):
        return flat[pl.ds(pl.multiple_of(shard * depth, 8), rows), :].astype(BF)

    for i, kept, sent in halves(*split, shards):
        keep[i] = rows_of_shard(kept)
        send[i * rows : (i + 1) * rows, :] = rows_of_shard(sent)


def fold(split, kept, got, token, keep, send):
    for i, *shards in halves(*split, keep.shape[0]):
        for out, shard in zip((keep, send), shards):
            out[i] = (kept[shard].astype(F32) + got[shard].astype(F32)).astype(BF)


def fold_small(split, kept, got, small, token, keep, send, small_out):
    held, rows, _ = kept.shape
    for i, *shards in halves(*split, held // 2):
        totals = [(kept[shard].astype(F32) + got[pl.ds(pl.multiple_of(shard * rows, 16), rows), :].astype(F32)).astype(BF)
                  for shard in shards]
        keep[i] = totals[0]
        send[i * rows : (i + 1) * rows, :] = totals[1]
    total = rounded_small(small[...]) + joined_small(got, held * rows)
    small_out[...] = total
    split_small(total, send, held // 2 * rows)


def fold_group(folds, *refs):
    inputs, results = refs, refs[sum(n for _, n, _ in folds) + 1 :]
    token = refs[sum(n for _, n, _ in folds)]
    for function, n_in, n_out in folds:
        function(*inputs[:n_in], token, *results[:n_out])
        inputs, results = inputs[n_in:], results[n_out:]


def finish_small(got, small, token, total_ref, send):
    total = rounded_small(small[...]) + joined_small(got, got.shape[0] - 2 * SMALL)
    total_ref[...] = total
    split_small(total, send, 0)


def finish_attn(kept, got, small, far, token, attn_out, one_out, two_out, router_out, packed):
    padded = kept.shape[0]
    both = kept[...].astype(F32) + got[:padded, :].astype(F32)
    attn_out[...] = both[: attn_out.shape[0]]
    packed[...] = rounded_small(small[...]) + joined_small(far, 0)
    width = one_out.shape[1]
    outs = [(one_out, 0), (two_out, 0), *[(router_out, i) for i in range(RECURSIONS)]]
    for i, (out, row) in enumerate(outs):
        for c in range(CHUNKS):
            stop = min(width, (c + 1) * LANES)
            out[row : row + 1, c * LANES : stop] = packed[i * CHUNKS + c : i * CHUNKS + c + 1, : stop - c * LANES]


def finish_ffn(tiles, *refs):
    feeds, (_, ffn_out, flat) = refs[:-3], refs[-3:]
    every = sum(tiles)
    rows = ffn_out.shape[0] // every
    base = 0
    for i, wide in enumerate(tiles):
        flat[: rows * wide, :] = feeds[2 * i][...].astype(F32) + feeds[2 * i + 1][...].astype(F32)
        for c in range(wide):
            ffn_out[pl.ds(base + c, rows, stride=every), :] = flat[pl.ds(c, rows, stride=wide), :]
        base += wide


class Stream:
    def __init__(self, orders, bits):
        self.orders, self.left, self.done = orders, [list(range(bits - 1, -1, -1)) for _ in orders], 0
        self.kept = self.got = None

    def split(self):
        bits = tuple(order[self.done] for order in self.orders)
        return bits, tuple(len(left) - 1 - left.index(bit) for left, bit in zip(self.left, bits))

    def sent(self, kept, send, n_dp):
        bits = self.split()[0]
        pairs = [(2 * d + core, 2 * (d ^ (1 << bit)) + core) for d in range(n_dp) for core, bit in enumerate(bits)]
        self.kept, self.got = kept, lax.ppermute(send, ("dp", "mp"), pairs)
        for left, bit in zip(self.left, bits):
            left.remove(bit)
        self.done += 1


def on_device(
    hidden_in,
    sel_one,
    sel_two,
    sel_three,
    segment_ids,
    pad_mask,
    qkv_weight,
    out_weight,
    gate_weight,
    up_weight,
    down_weight,
    norm_one,
    norm_two,
    router_weight,
    d_hidden,
):
    seq_len, width = hidden_in.shape
    n_dp, n_mp = lax.axis_size("dp"), lax.axis_size("mp")
    dp_index, mp_index = lax.axis_index("dp"), lax.axis_index("mp")
    cosine, sine = rotary_tables(seq_len)
    weights = [(gate_weight, up_weight, down_weight)]
    weights.append(tuple(swap_mp(w) for w in weights[0]))
    gain_one, gain_two = norm_one.reshape(1, width), norm_two.reshape(1, width)
    padded = CHUNKS * LANES
    units = gate_weight.shape[1]
    feed_weights = (*weights[0], *weights[1])

    def shape(*dims, dtype=BF):
        return jax.ShapeDtypeStruct(dims, dtype)

    def whole(*dims, **kw):
        return pl.BlockSpec(dims, lambda *_: (0,) * len(dims), **kw)

    anywhere = pl.BlockSpec(memory_space=pl.ANY)
    one = pl.Buffered(1)
    stack = RECURSIONS, seq_len
    heads = (2 * KV_HEADS, seq_len, LANES)
    square = (HEADS, seq_len, seq_len)
    n1, q, kz, vz, p, o_da, attn, n2, bias, active, near, slope_first, silu_first, f_first = pl.pallas_call(
        first_attention,
        grid=(1,),
        in_specs=[
            whole(seq_len, width), *[whole(*ref.shape) for ref in (sel_one, sel_two, sel_three, segment_ids, pad_mask)],
            whole(seq_len, LANES), whole(seq_len, LANES), whole(1, width), whole(1, width), whole(*qkv_weight.shape), whole(*out_weight.shape),
            *[anywhere] * 3,
        ],
        out_specs=[
            whole(1, seq_len, width), whole(seq_len, padded), whole(*heads), whole(*heads), whole(*square),
            whole(1, 1, seq_len, width), whole(seq_len, width), whole(seq_len, width), whole(RECURSIONS, seq_len, seq_len), whole(*stack, 1),
            whole(1, 1, seq_len, units), whole(seq_len, units), whole(seq_len, units), whole(seq_len, width),
        ],
        out_shape=[
            shape(*stack, width), shape(seq_len, padded), shape(*heads), shape(*heads), shape(*square),
            shape(2, *stack, width), shape(seq_len, width, dtype=F32), shape(seq_len, width),
            shape(*stack, seq_len, dtype=F32), shape(*stack, 1, dtype=F32),
            shape(3, *stack, units), shape(seq_len, units), shape(seq_len, units), shape(seq_len, width, dtype=F32),
        ],
        scratch_shapes=[*[pltpu.VMEM(w.shape, BF) for w in weights[0]], pltpu.SemaphoreType.DMA((3,))],
        compiler_params=pltpu.CompilerParams(vmem_limit_bytes=VMEM_BYTES),
        cost_estimate=pl.CostEstimate(flops=2 * 10**9, bytes_accessed=12 * 10**6, transcendentals=600000),
        name="first_attention",
    )(hidden_in, sel_one, sel_two, sel_three, segment_ids, pad_mask, cosine, sine, gain_one, gain_two, qkv_weight, out_weight,
      *weights[0])
    attention_0 = (q, kz, vz, p)
    wide = qkv_weight.shape[1]
    row = (seq_len, width)
    kept = RECURSIONS - 1
    first_part = FFN_TILES[0] * LANES
    vm = pltpu.VMEM
    results = pl.pallas_call(
        all_steps,
        grid=(1,),
        in_specs=[
            whole(RECURSIONS, seq_len, seq_len), whole(RECURSIONS, seq_len, 1), whole(RECURSIONS, width),
            whole(seq_len, LANES), whole(seq_len, LANES), whole(1, width), whole(1, width), *[anywhere] * 18,
        ],
        out_specs=[*[anywhere] * 8, whole(*row), whole(*row), whole(8, width)],
        out_shape=[
            shape(*stack, width), *[shape(2, *stack, width)] * 2, shape(3, *stack, units), shape(3, *stack, first_part), shape(3, *stack, units - first_part), shape(*stack, wide),
            *[shape(*row, dtype=F32)] * 3, shape(8, width, dtype=F32),
        ],
        scratch_shapes=[
            *[vm(w.shape, BF) for w in (qkv_weight, out_weight, *feed_weights)],
            vm((RECURSIONS + 1, *row), F32), vm((RECURSIONS, *row), F32), vm((RECURSIONS, *row), BF),
            *[vm((*stack, units), BF)] * 4, vm((kept, seq_len, padded), BF), vm((kept, *heads), BF), vm((kept, *heads), BF),
            vm((kept, *square), BF), *[vm(row, BF)] * 3, *[vm((seq_len, units), BF)] * 2, vm(row, BF), *[vm((seq_len, units), BF)] * 4,
            vm(row, BF), vm((seq_len, wide), BF), vm(row, F32), vm(row, F32), vm((seq_len, padded), BF),
            pltpu.SemaphoreType.DMA((15,)), pltpu.SemaphoreType.DMA((16,)),
        ],
        input_output_aliases={14: 0, 15: 1, 16: 3},
        compiler_params=pltpu.CompilerParams(vmem_limit_bytes=VMEM_BYTES),
        cost_estimate=pl.CostEstimate(flops=23 * 10**9, bytes_accessed=50 * 10**6, transcendentals=4 * 10**6),
        name="all_steps",
    )(bias, active, router_weight, cosine, sine, gain_one, gain_two, hidden_in, d_hidden, attn, n2,
      slope_first, silu_first, f_first, n1, o_da, near,
      qkv_weight, out_weight, *feed_weights)
    n1, o_da, n2_df, near, far, late, du, state, base, grad_state, small = results

    def run_last(token):
        return pl.pallas_call(
            last_attention,
            grid=(1,),
            in_specs=[
                whole(1, seq_len, 1), whole(seq_len, LANES), whole(seq_len, LANES), whole(1, width),
                whole(seq_len, padded), whole(*heads), whole(*heads), whole(*square),
                pl.BlockSpec((1, 1, seq_len, width), lambda i: (1, 0, 0, 0)), whole(8, width), whole(*out_weight.shape), *[anywhere] * 6,
            ],
            out_specs=[whole(1, seq_len, qkv_weight.shape[1]), whole(seq_len, width), whole(8, width)],
            out_shape=[shape(*stack, qkv_weight.shape[1]), shape(seq_len, width, dtype=F32), shape(8, width, dtype=F32)],
            scratch_shapes=[
                pltpu.VMEM((seq_len, padded), BF), *[pltpu.VMEM((seq_len, width), F32)] * 4,
                pltpu.VMEM(qkv_weight.shape, BF), pltpu.SemaphoreType.DMA((4,)),
            ],
            input_output_aliases={15: 0},
            compiler_params=pltpu.CompilerParams(vmem_limit_bytes=VMEM_BYTES),
            cost_estimate=pl.CostEstimate(flops=1, bytes_accessed=1, transcendentals=0),
            name="last_attention",
        )(active, cosine, sine, gain_one, *attention_0, o_da, small, out_weight, hidden_in, base, grad_state, qkv_weight, du, token)

    def rows_of(stacked):
        return stacked.reshape(*stacked.shape[:-3], -1, stacked.shape[-1])

    bits = n_dp.bit_length() - 1
    share = (qkv_weight.size + out_weight.size) // (n_dp * n_mp)
    if bits == 4 and 3 * width % n_dp == 0 and units == sum(FFN_TILES) * LANES and share % (16 * qkv_weight.shape[1]) == share % (16 * width) == 0:
        n2_df_rows = [rows_of(t) for t in (n2_df, swap_mp(n2_df))]
        near, far_b = rows_of(near), rows_of(swap_mp(far))
        n1_b = rows_of(swap_mp(n1))
        streams = [Stream(order, bits) for order in FFN_ORDERS]
        attn_stream = Stream(ATTN_ORDER, bits)
        depth = share // LANES
        tiled = -(-depth // 16) * 16
        common = dict(
            grid=(1,),
            compiler_params=pltpu.CompilerParams(vmem_limit_bytes=VMEM_BYTES),
            cost_estimate=pl.CostEstimate(flops=1, bytes_accessed=1, transcendentals=0),
        )

        def wholes(arrays):
            return [whole(*t.shape) for t in arrays]

        def terms_of(j, token):
            stream, tiles = streams[j], FFN_TILES[j]
            at = sum(FFN_TILES[:j]) * LANES
            factors = (*n2_df_rows, near, far_b if j == 0 else late_b)
            dims = (n_dp // 2, 3 * width // n_dp * tiles, LANES)
            both = 2 * RECURSIONS * seq_len
            keep, send = pl.pallas_call(
                functools.partial(ffn_terms, stream.split(), tiles, at, 0 if j == 0 else at - first_part),
                in_specs=[anywhere] * (len(factors) + 1),
                out_specs=[whole(*dims)] * 2,
                out_shape=[shape(*dims)] * 2,
                scratch_shapes=[pltpu.VMEM((2, both, width), BF), *[pltpu.VMEM((both, n * tiles * LANES), BF) for n in (2, 1)],
                                pltpu.VMEM((3 * width * tiles, LANES), F32), pltpu.SemaphoreType.DMA((10,))],
                name=f"ffn_terms_{j}",
                **common,
            )(*factors, token)
            stream.sent(keep, send, n_dp)
            return keep

        def fold_streams(group, token, small_own):
            folds, operands, outs = [], [], []
            for stream in group:
                count, rows, _ = stream.kept.shape
                held = (count // 2, rows, LANES)
                operands += [stream.kept, stream.got]
                if stream is attn_stream:
                    operands.append(small_own)
                    outs += [shape(*held), shape(count // 2 * rows + 2 * SMALL, LANES), shape(SMALL, LANES, dtype=F32)]
                    folds.append((functools.partial(fold_small, stream.split()), 3, 3))
                else:
                    outs += [shape(*held), shape(*held)]
                    folds.append((functools.partial(fold, stream.split()), 2, 2))
            results = pl.pallas_call(
                functools.partial(fold_group, folds),
                in_specs=[*wholes(operands), anywhere],
                out_specs=wholes(outs),
                out_shape=outs,
                name="fold_terms",
                **common,
            )(*operands, token)
            token = results[0]
            for stream, (_, _, n_out) in zip(group, folds):
                stream.sent(results[0], results[1], n_dp)
                small_own = results[2] if n_out == 3 else small_own
                results = results[n_out:]
            return token, small_own

        du, grad_state, small = run_last(small)
        late, du, small = lax.optimization_barrier((late, du, small))
        late_b, du_b = rows_of(swap_mp(late)), rows_of(swap_mp(du))
        token, small_own = small, None
        for item in SCHEDULE:
            if item[0] == "T":
                token = terms_of(int(item[1:]), token)
                if item == "T0":
                    o_da, token = lax.optimization_barrier((o_da, token))
                    o_da_b = rows_of(swap_mp(o_da))
            elif item == "A":
                dims = (n_dp // 2, tiled, LANES)
                operands = (rows_of(n1), n1_b, rows_of(du), du_b, rows_of(o_da), o_da_b, small)
                outs = (shape(*dims), shape(n_dp // 2 * tiled + 2 * SMALL, LANES), shape(SMALL, LANES, dtype=F32))
                keep, send, small_own = pl.pallas_call(
                    functools.partial(attn_terms, attn_stream.split(), depth),
                    in_specs=[*[anywhere] * 6, *wholes(operands[6:]), anywhere],
                    out_specs=wholes(outs),
                    out_shape=outs,
                    scratch_shapes=[pltpu.VMEM((2, 2 * RECURSIONS * seq_len, width), BF),
                                    *[pltpu.VMEM((2 * RECURSIONS * seq_len, t.shape[-1]), BF) for t in (du, o_da)],
                                    pltpu.VMEM((width, 2 * RECURSIONS * seq_len), BF),
                                    pltpu.VMEM((width // 2, 2 * RECURSIONS * seq_len), BF),
                                    pltpu.VMEM((-(-du.shape[-1] // PART) * 2, width // 2, LANES), F32),
                                    pltpu.VMEM((n_dp * depth + tiled - depth, LANES), F32), pltpu.VMEM((SMALL, LANES), F32),
                                    pltpu.SemaphoreType.DMA((8,))],
                    name="attn_terms",
                    **common,
                )(*operands, token)
                attn_stream.sent(keep, send, n_dp)
                token = small_own
            else:
                group = [attn_stream if name == "A0" else streams[int(name[1:])] for name in item.split()]
                token, small_own = fold_streams(group, token, small_own)
        attn_kept = attn_stream.kept.reshape(tiled, LANES)
        outs = (shape(SMALL, LANES, dtype=F32), shape(2 * SMALL, LANES))
        small_own, small_send = pl.pallas_call(
            finish_small,
            in_specs=[*wholes((attn_stream.got, small_own)), anywhere],
            out_specs=wholes(outs),
            out_shape=outs,
            name="finish_small",
            **common,
        )(attn_stream.got, small_own, token)
        operands = (attn_kept, attn_stream.got, small_own, swap_mp(small_send))
        outs = (shape(depth, LANES, dtype=F32), shape(1, width, dtype=F32), shape(1, width, dtype=F32),
                shape(RECURSIONS, width, dtype=F32))
        attn_flat, one, two, router = pl.pallas_call(
            finish_attn,
            in_specs=[*wholes(operands), anywhere],
            out_specs=wholes(outs),
            out_shape=outs,
            scratch_shapes=[pltpu.VMEM((SMALL, LANES), F32)],
            name="finish_attn",
            **common,
        )(*operands, small_own)
        ends = [t.reshape(t.shape[-2:]) for stream in streams for t in (stream.kept, stream.got)]
        ffn_rows = (3 * width // n_dp * sum(FFN_TILES), LANES)
        ffn_flat = pl.pallas_call(
            functools.partial(finish_ffn, FFN_TILES),
            in_specs=[*wholes(ends), anywhere],
            out_specs=whole(*ffn_rows),
            out_shape=shape(*ffn_rows, dtype=F32),
            scratch_shapes=[pltpu.VMEM((3 * width // n_dp * max(FFN_TILES), LANES), F32)],
            name="finish_ffn",
            **common,
        )(*ends, attn_flat)
        return (state, grad_state, attn_flat.reshape(-1), ffn_flat.reshape(1, -1), one.reshape(-1), two.reshape(-1), router)

    du, grad_state, small = run_last(small)
    two, feed = rows_of(n2_df)
    o, d_attn = rows_of(o_da)
    far = jnp.concatenate([far, late], axis=-1)
    sides = [[t[i] for i in (1, 2, 0)] for t in (rows_of(near), rows_of(far))]

    def side_terms(side, columns):
        return jnp.concatenate(
            [
                contract_rows(left, sides[side][which][:, columns]).astype(BF)
                for which, left in enumerate((two, two, feed))
            ],
            axis=0,
        )

    orders = orders_of(bits)
    if 3 * width % n_dp == 0 and units % 1280 == 0:
        fifth = units // 5
        streams = [(orders[i], slice(j * fifth, (j + 1) * fifth)) for i, j in ((0, 0), (1, 1), (2, 2), (0, 3), (1, 4))]
        done = []
        for order, columns in streams:
            terms = side_terms(0, columns).astype(F32) + swap_mp(side_terms(1, columns)).astype(F32)
            done.append(halving(terms.astype(BF).reshape(n_dp, 3 * width // n_dp, fifth), order, n_dp, dp_index))
        ffn_flat = jnp.concatenate(done, axis=1).reshape(1, -1)
    else:
        terms = side_terms(0, slice(None)).astype(F32) + swap_mp(side_terms(1, slice(None))).astype(F32)
        terms = terms.astype(BF).reshape(n_dp, 3 * width * units // n_dp // 128, 128)
        ffn_flat = halving(terms, orders[0], n_dp, dp_index).reshape(1, -1)

    grad_qkv = contract_rows(rows_of(n1), rows_of(du)).astype(BF)
    grad_out = contract_rows(o, d_attn).astype(BF)
    attn = jnp.concatenate([grad_qkv.reshape(-1), grad_out.reshape(-1)]).reshape(n_dp, 2, share // 128, 128)
    keep = jnp.where(mp_index == 0, attn[:, 0], attn[:, 1])
    send = jnp.where(mp_index == 0, attn[:, 1], attn[:, 0])
    attn = (keep.astype(F32) + swap_mp(send).astype(F32)).astype(BF)
    cuts = [0, (share // 128) // 24 * 8, (share // 128) // 12 * 8, share // 128]
    attn_flat = jnp.concatenate(
        [halving(attn[:, a:b], order, n_dp, dp_index) for a, b, order in zip(cuts, cuts[1:], orders)], axis=0
    ).reshape(-1)

    small = small + swap_mp(small)
    for bit in range(bits):
        small = small + swap_dp(small, bit, n_dp)
    return (state, grad_state, attn_flat, ffn_flat, small[0], small[1], small[2 : 2 + RECURSIONS])


def solution(mesh):
    both = P(("dp", "mp"), None)
    in_specs = (
        both,
        both,
        both,
        both,
        both,
        both,
        P(),
        P(),
        P(None, "mp"),
        P(None, "mp"),
        P(None, "mp"),
        P(),
        P(),
        P(),
        both,
    )
    out_specs = (both, both, P(("dp", "mp")), P("mp", "dp"), P(), P(), P())
    return jax.shard_map(
        on_device, mesh=mesh, in_specs=in_specs, out_specs=out_specs, check_vma=False
    )
```

```python
import functools
import math

import jax
import jax.numpy as jnp
import numpy as np
from jax import lax
from jax.experimental import pallas as pl
from jax.experimental.pallas import tpu as pltpu
from jax.sharding import PartitionSpec as P

HEADS = 15
KV_HEADS = 5
HEAD_DIM = 64
RECURSIONS = 3
GROUPS = HEADS // KV_HEADS
EPS = 1e-05
BF = jnp.bfloat16
F32 = jnp.float32


LANES = 128
CHUNKS = -(-HEADS * HEAD_DIM // LANES)
ROWS = 192
BLOCK = 256
MIB = 1 << 20
VMEM_BYTES = 64 * MIB - 65536


def rotary_tables(seq_len):
    half = HEAD_DIM // 2
    frequency = np.float32(100000.0) ** (
        np.float32(-2.0) * np.arange(half, dtype=np.float32) / np.float32(HEAD_DIM)
    )
    angles = np.arange(seq_len, dtype=np.float32)[:, None] * frequency.astype(np.float32)
    cosine, sine = np.cos(angles), np.sin(angles)
    return (
        jnp.asarray(np.concatenate([cosine] * 4, axis=1), F32),
        jnp.asarray(np.concatenate([-sine, sine] * 2, axis=1), F32),
    )


def contract_rows(left, right):
    return lax.dot_general(left, right, (((0,), (0,)), ((), ())), preferred_element_type=F32)


def contract_last(left, right):
    return lax.dot_general(left, right, (((1,), (1,)), ((), ())), preferred_element_type=F32)


def plain(left, right):
    return jnp.dot(left, right, preferred_element_type=F32)


def inverse_rms(rows):
    return lax.rsqrt(jnp.mean(rows * rows, axis=-1, keepdims=True) + EPS)


def norm_back(rows, gain, d_out):
    inv = inverse_rms(rows)
    scaled = d_out * gain
    inner = jnp.mean(scaled * rows, axis=-1, keepdims=True)
    d_rows = inv * scaled - rows * (inv * inv * inv * inner)
    return d_rows, jnp.sum(d_out * rows * inv, axis=0, keepdims=True)


def lane_of(rows):
    return lax.broadcasted_iota(jnp.int32, (rows, LANES), 1)


def swapped(chunk):
    first = lane_of(chunk.shape[0]) % HEAD_DIM < HEAD_DIM // 2
    return jnp.where(first, pltpu.roll(chunk, LANES - 32, 1), pltpu.roll(chunk, 32, 1))


def other_half(chunk):
    return pltpu.roll(chunk, HEAD_DIM, 1)


def over_rows(count, body):
    def lap(i, carry):
        body(pl.ds(pl.multiple_of(i * ROWS, ROWS), ROWS))
        return carry

    lax.fori_loop(0, count // ROWS, lap, 0)


def attention_forward(x_ref, bias_ref, cos_ref, sin_ref, gain, qkv_w, n1_ref, q_ref, kz_ref, vz_ref, p_ref, o_ref):
    seq_len, width = x_ref.shape
    scale = 1.0 / math.sqrt(HEAD_DIM)

    def norm(rows):
        x = x_ref[rows, :]
        n1_ref[rows, :] = (x * inverse_rms(x) * gain).astype(BF)

    over_rows(seq_len, norm)
    lower = lane_of(seq_len) < HEAD_DIM
    n1 = n1_ref[...]

    def spread(ref, head, chunk, upper):
        flipped = other_half(chunk)
        here, there = (flipped, chunk) if upper else (chunk, flipped)
        ref[2 * head] = jnp.where(lower, here, 0.0).astype(BF)
        ref[2 * head + 1] = jnp.where(lower, 0.0, there).astype(BF)

    columns = qkv_w.shape[1]
    for start in range(0, columns, 2 * LANES):
        wide = plain(n1, qkv_w[:, start : min(start + 2 * LANES, columns)])
        for part in range(0, wide.shape[1], LANES):
            chunk = wide[:, part : part + LANES]
            if chunk.shape[1] < LANES:
                chunk = jnp.concatenate([chunk, jnp.zeros_like(chunk)], axis=1)
            at = (start + part) // LANES
            heads = (2 * at, 2 * at + 1)
            if heads[0] < HEADS + KV_HEADS:
                chunk = chunk * cos_ref[...] + swapped(chunk) * sin_ref[...]
                if heads[0] < HEADS:
                    q_ref[:, at * LANES : (at + 1) * LANES] = chunk.astype(BF)
            for upper, head in enumerate(heads):
                if HEADS <= head < HEADS + KV_HEADS:
                    spread(kz_ref, head - HEADS, chunk, upper)
                elif HEADS + KV_HEADS <= head < HEADS + 2 * KV_HEADS:
                    spread(vz_ref, head - HEADS - KV_HEADS, chunk, upper)

    for at in range(CHUNKS):
        query = q_ref[:, at * LANES : (at + 1) * LANES]
        total = None
        for upper in range(2):
            head = 2 * at + upper
            if head < HEADS:
                key = 2 * (head // GROUPS) + upper
                scores = contract_last(query, kz_ref[key]) * scale + bias_ref[...]
                top = jnp.max(scores, axis=-1, keepdims=True)
                exponent = jnp.exp(scores - top)
                share = pl.reciprocal(jnp.sum(exponent, axis=-1, keepdims=True))
                attend = (exponent * share).astype(BF)
                p_ref[head] = attend
                mixed = plain(attend, vz_ref[key])
                total = mixed if total is None else total + mixed
        stop = min(width, (at + 1) * LANES)
        o_ref[:, at * LANES : stop] = total[:, : stop - at * LANES].astype(BF)


def attention_out(x_ref, o_ref, out_w, gain, attn_ref, n2_ref):
    attn_ref[...] = plain(o_ref[...], out_w[...])

    def norm(rows):
        after = x_ref[rows, :] + attn_ref[rows, :]
        n2_ref[rows, :] = (after * inverse_rms(after) * gain).astype(BF)

    over_rows(x_ref.shape[0], norm)


def feed_side(n2_ref, weights, results, ready):
    n2 = n2_ref[...]
    gate_w, up_w, down_w = weights
    m_ref, slope_ref, silu_ref = results
    ready(0, 1)
    for start in range(0, gate_w.shape[1], BLOCK):
        at = slice(start, start + BLOCK)
        g, u = plain(n2, gate_w[:, at]), plain(n2, up_w[:, at])
        s = jax.nn.sigmoid(g)
        silu = g * s
        m_ref[:, at] = (silu * u).astype(BF)
        slope_ref[:, at] = (u * s * (1.0 + g * (1.0 - s))).astype(BF)
        silu_ref[:, at] = silu.astype(BF)
    ready(2)
    return contract_last(m_ref[...], down_w[...])


def feed_backward(df_ref, sides, d_two_ref, ready):
    d_feed = df_ref[...]
    for side, (gate_w, up_w, down_w, slope_ref, silu_ref, dg_ref, du_ref) in enumerate(sides):
        ready(3 * side)
        for start in range(0, gate_w.shape[1], BLOCK):
            at = slice(start, start + BLOCK)
            d_hidden = plain(d_feed, down_w[:, at])
            dg_ref[:, at] = (d_hidden * slope_ref[:, at].astype(F32)).astype(BF)
            du_ref[:, at] = (d_hidden * silu_ref[:, at].astype(F32)).astype(BF)
        ready(3 * side + 1, 3 * side + 2)
        part = contract_last(dg_ref[...], gate_w[...]) + contract_last(du_ref[...], up_w[...])
        d_two_ref[...] = part if side == 0 else d_two_ref[...] + part


def attention_backward(d_attn_ref, out_w, qkv_w, cos_ref, sin_ref, q_ref, kz_ref, vz_ref, p_ref, do_ref, du_ref):
    seq_len, width = d_attn_ref.shape
    scale = 1.0 / math.sqrt(HEAD_DIM)
    do_ref[:, :width] = contract_last(d_attn_ref[...], out_w[...]).astype(BF)
    do_ref[:, width:] = jnp.zeros((seq_len, do_ref.shape[1] - width), BF)
    lower = lane_of(seq_len) < HEAD_DIM
    cosine, sine = cos_ref[...], sin_ref[...]

    def back(chunk):
        chunk = chunk * scale
        return chunk * cosine - swapped(chunk) * sine

    waiting, d_k, d_v = None, {}, {}
    for at in range(CHUNKS):
        query, d_mixed = (ref[:, at * LANES : (at + 1) * LANES] for ref in (q_ref, do_ref))
        query_t, d_mixed_t = query.T, d_mixed.T
        d_query = None
        for upper in range(2):
            head = 2 * at + upper
            if head >= HEADS:
                continue
            group = head // GROUPS
            key = 2 * group + upper
            rows = slice(upper * HEAD_DIM, (upper + 1) * HEAD_DIM)
            attend = p_ref[head]
            d_attend = contract_last(d_mixed, vz_ref[key])
            soft = attend.astype(F32)
            weighted = soft * d_attend
            inner = jnp.sum(weighted, axis=-1, keepdims=True)
            d_scores = (weighted - soft * inner).astype(BF)
            part = plain(d_scores, kz_ref[key])
            d_query = part if d_query is None else d_query + part
            for store, term in ((d_k, plain(query_t[rows], d_scores)), (d_v, plain(d_mixed_t[rows], attend))):
                store[group] = term if group not in store else store[group] + term
        if at < CHUNKS - 1:
            du_ref[:, at * LANES : (at + 1) * LANES] = back(d_query).astype(BF)
        else:
            waiting = d_query

    def two_heads(store, first, second):
        return jnp.concatenate([store[first], store[second]], axis=0).T

    tail = jnp.where(lower, waiting, two_heads(d_k, 0, 0))
    du_ref[:, (CHUNKS - 1) * LANES : CHUNKS * LANES] = back(tail).astype(BF)
    for i in range(2):
        at = CHUNKS + i
        du_ref[:, at * LANES : (at + 1) * LANES] = back(two_heads(d_k, 1 + 2 * i, 2 + 2 * i)).astype(BF)
        at = CHUNKS + 2 + i
        du_ref[:, at * LANES : (at + 1) * LANES] = two_heads(d_v, 2 * i, 2 * i + 1).astype(BF)
    at = CHUNKS + 4
    du_ref[:, at * LANES :] = two_heads(d_v, 4, 4)[:, : du_ref.shape[1] - at * LANES].astype(BF)


def router_gate(x, router_row):
    return jax.nn.sigmoid(jnp.sum(x * router_row, axis=-1, keepdims=True))


def masks(select_refs, segment_ref, pad_ref, bias_ref, active_ref):
    seq_len = segment_ref.shape[1]
    square = (seq_len, seq_len)
    query, key = (lax.broadcasted_iota(jnp.int32, square, axis) for axis in (0, 1))
    diagonal = query == key
    segment = segment_ref[...].astype(F32)
    own = jnp.sum(jnp.where(diagonal, segment, 0.0), axis=1, keepdims=True)
    near = (key <= query) & (segment == own)
    real = pad_ref[...] == 1
    for recursion, ref in enumerate(select_refs):
        place = lax.broadcasted_iota(jnp.int32, (seq_len, ref.shape[1]), 0)
        active = jnp.max(jnp.where(ref[...] == place, 1.0, 0.0), axis=1, keepdims=True)
        active_ref[recursion] = active
        along = jnp.sum(jnp.where(diagonal, active, 0.0), axis=0, keepdims=True)
        usable = (along > 0.0) & real
        bias_ref[recursion] = jnp.where(near & (usable | diagonal), 0.0, -1e30)


def first_attention(x_ref, sel_one, sel_two, sel_three, segment_ref, pad_ref, cos_ref, sin_ref, gain_one, gain_two, qkv_w, out_w,
                    gate_hbm, up_hbm, down_hbm, n1_ref, q_ref, kz_ref, vz_ref, p_ref, o_ref, attn_ref, n2_ref, bias_ref, active_ref,
                    m_ref, slope_ref, silu_ref, f_ref, gate_w, up_w, down_w, sems):
    copies = load_all([(gate_hbm, gate_w), (up_hbm, up_w), (down_hbm, down_w)], sems)
    for copy in copies:
        copy.start()
    n1, o = n1_ref.at[0], o_ref.at[0, 0]
    masks((sel_one, sel_two, sel_three), segment_ref, pad_ref, bias_ref, active_ref)
    attention_forward(x_ref, bias_ref.at[0], cos_ref, sin_ref, gain_one[...], qkv_w, n1, q_ref, kz_ref, vz_ref, p_ref, o)
    attention_out(x_ref, o, out_w, gain_two[...], attn_ref, n2_ref)

    def ready(*which):
        for i in which:
            copies[i].wait()

    f_ref[...] = feed_side(n2_ref, (gate_w, up_w, down_w), (m_ref.at[0, 0], slope_ref, silu_ref), ready)


def load_all(pairs, sems):
    return [pltpu.make_async_copy(src, dst, sems.at[i]) for i, (src, dst) in enumerate(pairs)]


def waits_at(condition, copies):
    def ready(*which):
        @pl.when(condition)
        def _():
            for i in which:
                copies[i].wait()

    return ready


def finish_attention_backward(x_ref, gain, active_ref, du_ref, qkv_w, base, state, total, out_ref):
    total[...] = contract_last(du_ref[...], qkv_w[...])
    terms = jnp.zeros((1, state.shape[1]), F32)

    def lap(i, terms):
        rows = pl.ds(pl.multiple_of(i * ROWS, ROWS), ROWS)
        d_rows, term = norm_back(x_ref[rows, :], gain, total[rows, :])
        new = jnp.where(active_ref[rows, :] > 0, base[rows, :] + d_rows, state[rows, :])
        out_ref[rows, :] = new
        return terms + term

    return lax.fori_loop(0, state.shape[0] // ROWS, lap, terms)


def all_steps(bias_ref, active_ref, router_ref, cos_ref, sin_ref, gain_one, gain_two,
              hidden_hbm, d_hidden_hbm, attn0_hbm, n20_hbm, slope_hbm, silu_hbm, f_hbm, n1_in, o_da_in, near_in,
              qkv_hbm, out_hbm, *rest):
    feed_hbm, rest = rest[:6], rest[6:]
    (n1_out, o_da_out, n2_df_out, near_out, far_out, late_out, du_out, final_out, base_ref, state_ref, small_ref), rest = rest[:11], rest[11:]
    qkv_w, out_w, *feed_w = rest[:8]
    (xs, attns, fs, slope0, slope1, silu0, silu1, qs, kzs, vzs, ps, n1, o, n2, m0, m1, df, dg0, dg1, dw0, dw1, da, du,
     total, d_branch, do_ref, load_sems, out_sems) = rest[8:]
    width = state_ref.shape[1]
    first_part = far_out.shape[3]
    laps = state_ref.shape[0] // ROWS
    loads = load_all(
        [*zip(feed_hbm, feed_w), (qkv_hbm, qkv_w), (out_hbm, out_w),
         (n20_hbm, n2), (attn0_hbm, attns.at[0]), (hidden_hbm, xs.at[0]), (d_hidden_hbm, state_ref),
         (f_hbm, total), (slope_hbm, slope0.at[0]), (silu_hbm, silu0.at[0])], load_sems)
    for i in (8, 3, 4, 5, 12, 9, 10, 6, 7, 0, 1, 2, 13, 14, 11):
        loads[i].start()
    loads[8].wait()

    places = dict(n2=[(n2, n2_df_out.at[0])], m0=[(m0, near_out.at[0])], n1=[(n1, n1_out)], o=[(o, o_da_out.at[0])],
                  df=[(df, n2_df_out.at[1])], dg0=[(dg0, near_out.at[1])], dw0=[(dw0, near_out.at[2])],
                  da=[(da, o_da_out.at[1])], du=[(du, du_out)])
    for i, (name, ref) in enumerate((("m1", m1), ("dg1", dg1), ("dw1", dw1))):
        places[name] = [(ref.at[:, :first_part], far_out.at[i]), (ref.at[:, first_part:], late_out.at[i])]
    numbers = {}
    for pairs in places.values():
        for source, target in pairs:
            numbers[id(target)] = len(numbers)

    def leaving(recursion, names):
        return [pltpu.make_async_copy(source, target.at[recursion], out_sems.at[numbers[id(target)]])
                for name in names for source, target in places[name]]

    def start(recursion, *names):
        for copy in leaving(recursion, names):
            copy.start()

    def wait(recursion, *names):
        for copy in leaving(recursion, names):
            copy.wait()

    def forward(r, carry):
        ready, later = (waits_at(r == step, loads) for step in range(2))
        start(r, "n2")

        @pl.when(r > 0)
        def _():
            @pl.when(r > 1)
            def _():
                wait(r - 1, "m0")

            total[...] = feed_side(n2, feed_w[:3], (m0, slope0.at[r], silu0.at[r]), later)
            start(r, "m0")
            wait(r - 1, "m1")

        part = feed_side(n2, feed_w[3:], (m1, slope1.at[r], silu1.at[r]), lambda *which: ready(*[3 + i for i in which]))
        ready(12)
        total[...] = total[...] + part
        start(r, "m1")
        ready(9, 10)
        router_row = router_ref[pl.ds(r, 1), :]

        def finish(rows):
            x = xs[r, rows, :]
            f = total[rows, :].astype(BF)
            fs[r, rows, :] = f
            branch = attns[r, rows, :] + f.astype(F32)
            xs[r + 1, rows, :] = jnp.where(active_ref[r, rows, :] > 0, x + router_gate(x, router_row) * branch, x)

        over_rows(total.shape[0], finish)
        ready(6, 7)
        wait(r, "n2")

        @pl.when(r < RECURSIONS - 1)
        def _():
            @pl.when(r > 0)
            def _():
                wait(r, "n1", "o")

            attention_forward(xs.at[r + 1], bias_ref.at[r + 1], cos_ref, sin_ref, gain_one[...], qkv_w,
                              n1, qs.at[r], kzs.at[r], vzs.at[r], ps.at[r], o)
            start(r + 1, "n1", "o")
            attention_out(xs.at[r + 1], o, out_w, gain_two[...], attns.at[r + 1], n2)

        return carry

    lax.fori_loop(0, RECURSIONS, forward, 0)
    final = pltpu.make_async_copy(xs.at[RECURSIONS], final_out, out_sems.at[15])
    final.start()
    for i in (11, 13, 14):
        loads[i].wait()
    small_ref[...] = jnp.zeros(small_ref.shape, F32)

    def backward(i, carry):
        r = RECURSIONS - 1 - i
        router_row = router_ref[pl.ds(r, 1), :]

        @pl.when(i > 0)
        def _():
            wait(r + 1, "df", "dg0", "dg1", "dw0", "dw1", "da")

        def enter(lap, terms):
            rows = pl.ds(pl.multiple_of(lap * ROWS, ROWS), ROWS)
            x = xs[r, rows, :]
            d_new = jnp.where(active_ref[r, rows, :] > 0, state_ref[rows, :], 0.0)
            gate = router_gate(x, router_row)
            branch = attns[r, rows, :] + fs[r, rows, :].astype(F32)
            d_gate = jnp.sum(d_new * branch, axis=-1, keepdims=True)
            d_logit = d_gate * gate * (1.0 - gate)
            spread = gate * d_new
            d_branch[rows, :] = spread
            df[rows, :] = spread.astype(BF)
            base_ref[rows, :] = d_new + d_logit * router_row
            return terms + jnp.sum(d_logit * x, axis=0, keepdims=True)

        small_ref[pl.ds(2 + r, 1), :] = lax.fori_loop(0, laps, enter, jnp.zeros((1, width), F32))
        start(r, "df")
        feed_backward(df, ((*feed_w[:3], slope0.at[r], silu0.at[r], dg0, dw0), (*feed_w[3:], slope1.at[r], silu1.at[r], dg1, dw1)),
                      total, lambda *which: None)
        start(r, "dg0", "dg1", "dw0", "dw1")

        def leave(lap, terms):
            rows = pl.ds(pl.multiple_of(lap * ROWS, ROWS), ROWS)
            after = xs[r, rows, :] + attns[r, rows, :]
            d_after, term = norm_back(after, gain_two[...], total[rows, :].astype(BF).astype(F32))
            da[rows, :] = (d_branch[rows, :] + d_after).astype(BF)
            base_ref[rows, :] = base_ref[rows, :] + d_after
            return terms + term

        small_ref[1:2, :] = small_ref[1:2, :] + lax.fori_loop(0, laps, leave, jnp.zeros((1, width), F32))
        start(r, "da")

        @pl.when(r > 0)
        def _():
            @pl.when(i > 0)
            def _():
                wait(r + 1, "du")

            attention_backward(da, out_w, qkv_w, cos_ref, sin_ref, qs.at[r - 1], kzs.at[r - 1], vzs.at[r - 1], ps.at[r - 1], do_ref, du)
            start(r, "du")
            term = finish_attention_backward(xs.at[r], gain_one[...], active_ref.at[r], du, qkv_w, base_ref, state_ref, total, state_ref)
            small_ref[0:1, :] = small_ref[0:1, :] + term

        return carry

    lax.fori_loop(0, RECURSIONS, backward, 0)
    wait(RECURSIONS - 1, "m0", "m1", "n1", "o")
    wait(0, "df", "dg0", "dg1", "dw0", "dw1", "da")
    wait(1, "du")
    final.wait()


def last_attention(active_ref, cos_ref, sin_ref, gain_one, q_ref, kz_ref, vz_ref, p_ref, d_attn_ref, small_in, out_w,
                   x_hbm, base_hbm, state_hbm, qkv_hbm, du_in, token, du_ref, d_input_ref, small_ref,
                   do_ref, total, x, base, state, qkv_w, sems):
    copies = load_all([(qkv_hbm, qkv_w), (x_hbm, x), (base_hbm, base), (state_hbm, state)], sems)
    for copy in copies:
        copy.start()
    attention_backward(d_attn_ref.at[0, 0], out_w, qkv_w, cos_ref, sin_ref, q_ref, kz_ref, vz_ref, p_ref, do_ref, du_ref.at[0])
    for copy in copies:
        copy.wait()
    term = finish_attention_backward(x, gain_one[...], active_ref.at[0], du_ref.at[0], qkv_w, base, state, total, d_input_ref)
    small_ref[...] = small_in[...]
    small_ref[0:1, :] = small_in[0:1, :] + term


def swap_dp(values_in, bit, n_dp):
    return lax.ppermute(values_in, "dp", [(i, i ^ (1 << bit)) for i in range(n_dp)])


def swap_mp(values_in):
    return lax.ppermute(values_in, "mp", [(0, 1), (1, 0)])


def halving(parts, order, n_dp, index):
    bits = n_dp.bit_length() - 1
    left = list(range(bits - 1, -1, -1))
    shape = parts.shape[1:]
    held = parts.reshape((2,) * bits + shape)
    for step, bit in enumerate(order):
        at = left.index(bit)
        upper = ((index >> bit) & 1) == 1
        low = lax.index_in_dim(held, 0, at, keepdims=False)
        high = lax.index_in_dim(held, 1, at, keepdims=False)
        keep, send = jnp.where(upper, high, low), jnp.where(upper, low, high)
        got = swap_dp(send, bit, n_dp)
        last = step == bits - 1
        total = keep.astype(F32) + got.astype(F32)
        held = total if last else total.astype(BF)
        left.remove(bit)
    return held


def orders_of(bits):
    rest = list(range(3, bits))
    if bits < 3:
        return [list(range(bits))] * 3
    return [[0, 1, 2] + rest, [1, 0, 2] + rest, [2, 0, 1] + rest]


PART = 2 * LANES
FFN_TILES = (4, 4, 2)
FFN_ORDERS = (((2, 1, 0, 3), (1, 0, 3, 2)), ((1, 3, 0, 2), (0, 1, 2, 3)), ((1, 0, 2, 3), (2, 0, 1, 3)))
ATTN_ORDER = ((0, 2, 1, 3), (2, 0, 1, 3))
SCHEDULE = (
    "T0", "T1", "A", "T2",
    "F0", "F1", "A0", "F2",
    "F0", "F1", "A0", "F2",
    "A0", "F0 F1", "F2",
)
SMALL = 64


def of_core(pair):
    first, second = pair
    return first if first == second else jnp.where(lax.axis_index("mp") == 0, first, second)


def halves(bits, places, count):
    mine = (lax.axis_index("dp") >> of_core(bits)) & 1
    place = of_core(places)
    for i in range(count):
        base = ((i >> place) << (place + 1)) | (i & ((1 << place) - 1))
        yield i, base | (mine << place), base | ((1 - mine) << place)


def stacked_copies(pairs, sems):
    flat_pairs = []
    for sources, target in pairs:
        rows = target.shape[0] // 2
        flat_pairs += [(source, target.at[pl.ds(i * rows, rows)]) for i, source in enumerate(sources)]
    copies = load_all(flat_pairs, sems)
    for copy in copies:
        copy.start()
    return [copies[i : i + 2] for i in range(0, len(copies), 2)]


def ffn_terms(split, tiles, at, at_b, n2_df_a, n2_df_b, units_a, units_b, token, keep_ref, send_ref, left, gate_up, down, flat, sems):
    width, part = left.shape[2], down.shape[1]
    columns, columns_b = (pl.ds(start, tiles * LANES) for start in (at, at_b))
    lefts = [(n2_df_a.at[i], n2_df_b.at[i]) for i in range(2)]
    m, dg, dw = [(units_a.at[i, :, columns], units_b.at[i, :, columns_b]) for i in range(3)]
    n2, dg, dw, df, m = stacked_copies(
        [(lefts[0], left.at[0]), (dg, gate_up.at[:, :part]), (dw, gate_up.at[:, part:]), (lefts[1], left.at[1]), (m, down)], sems)
    for which, (right, needed) in enumerate(((gate_up, n2 + dg + dw), (down, df + m))):
        for copy in needed:
            copy.wait()
        terms = contract_rows(left[which], right[...])
        for at_lane in range(0, right.shape[1], LANES):
            matrix, c = divmod(at_lane // LANES, tiles)
            start = tiles * width * (2 * which + matrix) + c
            flat[pl.ds(start, width, stride=tiles), :] = terms[:, at_lane : at_lane + LANES]
    count, rows, _ = keep_ref.shape
    for i, kept, sent in halves(*split, count):
        for out, shard in ((keep_ref, kept), (send_ref, sent)):
            out[i] = flat[pl.ds(pl.multiple_of(shard * rows, 8), rows), :].astype(BF)


def small_rows(small, packed):
    packed[...] = jnp.zeros(packed.shape, F32)
    width = small.shape[1]
    for i in range(2 + RECURSIONS):
        for c in range(CHUNKS):
            stop = min(width, (c + 1) * LANES)
            packed[i * CHUNKS + c : i * CHUNKS + c + 1, : stop - c * LANES] = small[i : i + 1, c * LANES : stop]
    return packed[...]


def split_small(small, ref, start):
    high = small.astype(BF)
    ref[start : start + SMALL, :] = high
    ref[start + SMALL : start + 2 * SMALL, :] = (small - high.astype(F32)).astype(BF)


def rounded_small(small):
    high = small.astype(BF)
    return high.astype(F32) + (small - high.astype(F32)).astype(BF).astype(F32)


def joined_small(ref, start):
    return ref[start : start + SMALL, :].astype(F32) + ref[start + SMALL : start + 2 * SMALL, :].astype(F32)


def attn_terms(split, depth, n1_a, n1_b, du_a, du_b, o_da_a, o_da_b, small, token,
               keep, send, small_out, left, du_rows, da_rows, turned, own, terms, flat, packed, sems):
    base, count = 0, own.shape[0] // 2
    lower = lane_of(count) < HEAD_DIM
    core = lax.axis_index("mp")
    n1, du, o, da = stacked_copies(
        [((n1_a, n1_b), left.at[0]), ((du_a, du_b), du_rows), ((o_da_a.at[0], o_da_b.at[0]), left.at[1]),
         ((o_da_a.at[1], o_da_b.at[1]), da_rows)], sems)
    for which, (right, needed) in enumerate(((du_rows, n1 + du), (da_rows, o + da))):
        for copy in needed:
            copy.wait()
        columns = right.shape[1]
        half = columns // LANES
        turned[...] = left[which].T
        group = depth * LANES // columns
        for i in range(own.shape[0] // group):
            own[i * group : (i + 1) * group, :] = turned[pl.ds(pl.multiple_of((2 * i + core) * group, 16), group), :]
        for start in range(0, columns, PART):
            stop = min(columns, start + PART)
            block = plain(own[...], right[:, start:stop])
            if stop - start < PART:
                block = jnp.concatenate([block, jnp.zeros((2 * count, PART - (stop - start)), F32)], axis=1)
            for part in range(0, stop - start, LANES):
                terms[(start + part) // LANES] = block[:, part : part + LANES]
        step = 2 * columns // LANES
        after = first_odd = None
        for c in range(half + 1):
            even = terms[c, pl.ds(0, count, stride=2), :]
            odd = other_half(terms[c, pl.ds(1, count, stride=2), :])
            if c < half:
                flat[pl.ds(base + c, count, stride=step), :] = even
            else:
                flat[pl.ds(base + c, count, stride=step), :] = jnp.where(lower, even, first_odd)
            if c == 0:
                first_odd = odd
            else:
                flat[pl.ds(base + half + c, count, stride=step), :] = jnp.where(lower, after, odd)
            after = odd
        base += 2 * count * columns // LANES
    total = rounded_small(small_rows(small, packed))
    small_out[...] = total
    shards, rows, _ = keep.shape
    split_small(total, send, shards * rows)

    def rows_of_shard(shard):
        return flat[pl.ds(pl.multiple_of(shard * depth, 8), rows), :].astype(BF)

    for i, kept, sent in halves(*split, shards):
        keep[i] = rows_of_shard(kept)
        send[i * rows : (i + 1) * rows, :] = rows_of_shard(sent)


def fold(split, kept, got, token, keep, send):
    for i, *shards in halves(*split, keep.shape[0]):
        for out, shard in zip((keep, send), shards):
            out[i] = (kept[shard].astype(F32) + got[shard].astype(F32)).astype(BF)


def fold_small(split, kept, got, small, token, keep, send, small_out):
    held, rows, _ = kept.shape
    for i, *shards in halves(*split, held // 2):
        totals = [(kept[shard].astype(F32) + got[pl.ds(pl.multiple_of(shard * rows, 16), rows), :].astype(F32)).astype(BF)
                  for shard in shards]
        keep[i] = totals[0]
        send[i * rows : (i + 1) * rows, :] = totals[1]
    total = rounded_small(small[...]) + joined_small(got, held * rows)
    small_out[...] = total
    split_small(total, send, held // 2 * rows)


def fold_group(folds, *refs):
    inputs, results = refs, refs[sum(n for _, n, _ in folds) + 1 :]
    token = refs[sum(n for _, n, _ in folds)]
    for function, n_in, n_out in folds:
        function(*inputs[:n_in], token, *results[:n_out])
        inputs, results = inputs[n_in:], results[n_out:]


def finish_small(got, small, token, total_ref, send):
    total = rounded_small(small[...]) + joined_small(got, got.shape[0] - 2 * SMALL)
    total_ref[...] = total
    split_small(total, send, 0)


def finish_attn(kept, got, small, far, token, attn_out, one_out, two_out, router_out, packed):
    padded = kept.shape[0]
    both = kept[...].astype(F32) + got[:padded, :].astype(F32)
    attn_out[...] = both[: attn_out.shape[0]]
    packed[...] = rounded_small(small[...]) + joined_small(far, 0)
    width = one_out.shape[1]
    outs = [(one_out, 0), (two_out, 0), *[(router_out, i) for i in range(RECURSIONS)]]
    for i, (out, row) in enumerate(outs):
        for c in range(CHUNKS):
            stop = min(width, (c + 1) * LANES)
            out[row : row + 1, c * LANES : stop] = packed[i * CHUNKS + c : i * CHUNKS + c + 1, : stop - c * LANES]


def finish_ffn(tiles, *refs):
    feeds, (_, ffn_out, flat) = refs[:-3], refs[-3:]
    every = sum(tiles)
    rows = ffn_out.shape[0] // every
    base = 0
    for i, wide in enumerate(tiles):
        flat[: rows * wide, :] = feeds[2 * i][...].astype(F32) + feeds[2 * i + 1][...].astype(F32)
        for c in range(wide):
            ffn_out[pl.ds(base + c, rows, stride=every), :] = flat[pl.ds(c, rows, stride=wide), :]
        base += wide


class Stream:
    def __init__(self, orders, bits):
        self.orders, self.left, self.done = orders, [list(range(bits - 1, -1, -1)) for _ in orders], 0
        self.kept = self.got = None

    def split(self):
        bits = tuple(order[self.done] for order in self.orders)
        return bits, tuple(len(left) - 1 - left.index(bit) for left, bit in zip(self.left, bits))

    def sent(self, kept, send, n_dp):
        bits = self.split()[0]
        pairs = [(2 * d + core, 2 * (d ^ (1 << bit)) + core) for d in range(n_dp) for core, bit in enumerate(bits)]
        self.kept, self.got = kept, lax.ppermute(send, ("dp", "mp"), pairs)
        for left, bit in zip(self.left, bits):
            left.remove(bit)
        self.done += 1


def on_device(
    hidden_in,
    sel_one,
    sel_two,
    sel_three,
    segment_ids,
    pad_mask,
    qkv_weight,
    out_weight,
    gate_weight,
    up_weight,
    down_weight,
    norm_one,
    norm_two,
    router_weight,
    d_hidden,
):
    seq_len, width = hidden_in.shape
    n_dp, n_mp = lax.axis_size("dp"), lax.axis_size("mp")
    dp_index, mp_index = lax.axis_index("dp"), lax.axis_index("mp")
    cosine, sine = rotary_tables(seq_len)
    weights = [(gate_weight, up_weight, down_weight)]
    weights.append(tuple(swap_mp(w) for w in weights[0]))
    gain_one, gain_two = norm_one.reshape(1, width), norm_two.reshape(1, width)
    padded = CHUNKS * LANES
    units = gate_weight.shape[1]
    feed_weights = (*weights[0], *weights[1])

    def shape(*dims, dtype=BF):
        return jax.ShapeDtypeStruct(dims, dtype)

    def whole(*dims, **kw):
        return pl.BlockSpec(dims, lambda *_: (0,) * len(dims), **kw)

    anywhere = pl.BlockSpec(memory_space=pl.ANY)
    one = pl.Buffered(1)
    stack = RECURSIONS, seq_len
    heads = (2 * KV_HEADS, seq_len, LANES)
    square = (HEADS, seq_len, seq_len)
    n1, q, kz, vz, p, o_da, attn, n2, bias, active, near, slope_first, silu_first, f_first = pl.pallas_call(
        first_attention,
        grid=(1,),
        in_specs=[
            whole(seq_len, width), *[whole(*ref.shape) for ref in (sel_one, sel_two, sel_three, segment_ids, pad_mask)],
            whole(seq_len, LANES), whole(seq_len, LANES), whole(1, width), whole(1, width), whole(*qkv_weight.shape), whole(*out_weight.shape),
            *[anywhere] * 3,
        ],
        out_specs=[
            whole(1, seq_len, width), whole(seq_len, padded), whole(*heads), whole(*heads), whole(*square),
            whole(1, 1, seq_len, width), whole(seq_len, width), whole(seq_len, width), whole(RECURSIONS, seq_len, seq_len), whole(*stack, 1),
            whole(1, 1, seq_len, units), whole(seq_len, units), whole(seq_len, units), whole(seq_len, width),
        ],
        out_shape=[
            shape(*stack, width), shape(seq_len, padded), shape(*heads), shape(*heads), shape(*square),
            shape(2, *stack, width), shape(seq_len, width, dtype=F32), shape(seq_len, width),
            shape(*stack, seq_len, dtype=F32), shape(*stack, 1, dtype=F32),
            shape(3, *stack, units), shape(seq_len, units), shape(seq_len, units), shape(seq_len, width, dtype=F32),
        ],
        scratch_shapes=[*[pltpu.VMEM(w.shape, BF) for w in weights[0]], pltpu.SemaphoreType.DMA((3,))],
        compiler_params=pltpu.CompilerParams(vmem_limit_bytes=VMEM_BYTES),
        cost_estimate=pl.CostEstimate(flops=2 * 10**9, bytes_accessed=12 * 10**6, transcendentals=600000),
        name="first_attention",
    )(hidden_in, sel_one, sel_two, sel_three, segment_ids, pad_mask, cosine, sine, gain_one, gain_two, qkv_weight, out_weight,
      *weights[0])
    attention_0 = (q, kz, vz, p)
    wide = qkv_weight.shape[1]
    row = (seq_len, width)
    kept = RECURSIONS - 1
    first_part = FFN_TILES[0] * LANES
    vm = pltpu.VMEM
    results = pl.pallas_call(
        all_steps,
        grid=(1,),
        in_specs=[
            whole(RECURSIONS, seq_len, seq_len), whole(RECURSIONS, seq_len, 1), whole(RECURSIONS, width),
            whole(seq_len, LANES), whole(seq_len, LANES), whole(1, width), whole(1, width), *[anywhere] * 18,
        ],
        out_specs=[*[anywhere] * 8, whole(*row), whole(*row), whole(8, width)],
        out_shape=[
            shape(*stack, width), *[shape(2, *stack, width)] * 2, shape(3, *stack, units), shape(3, *stack, first_part), shape(3, *stack, units - first_part), shape(*stack, wide),
            *[shape(*row, dtype=F32)] * 3, shape(8, width, dtype=F32),
        ],
        scratch_shapes=[
            *[vm(w.shape, BF) for w in (qkv_weight, out_weight, *feed_weights)],
            vm((RECURSIONS + 1, *row), F32), vm((RECURSIONS, *row), F32), vm((RECURSIONS, *row), BF),
            *[vm((*stack, units), BF)] * 4, vm((kept, seq_len, padded), BF), vm((kept, *heads), BF), vm((kept, *heads), BF),
            vm((kept, *square), BF), *[vm(row, BF)] * 3, *[vm((seq_len, units), BF)] * 2, vm(row, BF), *[vm((seq_len, units), BF)] * 4,
            vm(row, BF), vm((seq_len, wide), BF), vm(row, F32), vm(row, F32), vm((seq_len, padded), BF),
            pltpu.SemaphoreType.DMA((15,)), pltpu.SemaphoreType.DMA((16,)),
        ],
        input_output_aliases={14: 0, 15: 1, 16: 3},
        compiler_params=pltpu.CompilerParams(vmem_limit_bytes=VMEM_BYTES),
        cost_estimate=pl.CostEstimate(flops=23 * 10**9, bytes_accessed=50 * 10**6, transcendentals=4 * 10**6),
        name="all_steps",
    )(bias, active, router_weight, cosine, sine, gain_one, gain_two, hidden_in, d_hidden, attn, n2,
      slope_first, silu_first, f_first, n1, o_da, near,
      qkv_weight, out_weight, *feed_weights)
    n1, o_da, n2_df, near, far, late, du, state, base, grad_state, small = results

    def run_last(token):
        return pl.pallas_call(
            last_attention,
            grid=(1,),
            in_specs=[
                whole(1, seq_len, 1), whole(seq_len, LANES), whole(seq_len, LANES), whole(1, width),
                whole(seq_len, padded), whole(*heads), whole(*heads), whole(*square),
                pl.BlockSpec((1, 1, seq_len, width), lambda i: (1, 0, 0, 0)), whole(8, width), whole(*out_weight.shape), *[anywhere] * 6,
            ],
            out_specs=[whole(1, seq_len, qkv_weight.shape[1]), whole(seq_len, width), whole(8, width)],
            out_shape=[shape(*stack, qkv_weight.shape[1]), shape(seq_len, width, dtype=F32), shape(8, width, dtype=F32)],
            scratch_shapes=[
                pltpu.VMEM((seq_len, padded), BF), *[pltpu.VMEM((seq_len, width), F32)] * 4,
                pltpu.VMEM(qkv_weight.shape, BF), pltpu.SemaphoreType.DMA((4,)),
            ],
            input_output_aliases={15: 0},
            compiler_params=pltpu.CompilerParams(vmem_limit_bytes=VMEM_BYTES),
            cost_estimate=pl.CostEstimate(flops=1, bytes_accessed=1, transcendentals=0),
            name="last_attention",
        )(active, cosine, sine, gain_one, *attention_0, o_da, small, out_weight, hidden_in, base, grad_state, qkv_weight, du, token)

    def rows_of(stacked):
        return stacked.reshape(*stacked.shape[:-3], -1, stacked.shape[-1])

    bits = n_dp.bit_length() - 1
    share = (qkv_weight.size + out_weight.size) // (n_dp * n_mp)
    if bits == 4 and 3 * width % n_dp == 0 and units == sum(FFN_TILES) * LANES and share % (16 * qkv_weight.shape[1]) == share % (16 * width) == 0:
        n2_df_rows = [rows_of(t) for t in (n2_df, swap_mp(n2_df))]
        near, far_b = rows_of(near), rows_of(swap_mp(far))
        n1_b = rows_of(swap_mp(n1))
        streams = [Stream(order, bits) for order in FFN_ORDERS]
        attn_stream = Stream(ATTN_ORDER, bits)
        depth = share // LANES
        tiled = -(-depth // 16) * 16
        common = dict(
            grid=(1,),
            compiler_params=pltpu.CompilerParams(vmem_limit_bytes=VMEM_BYTES),
            cost_estimate=pl.CostEstimate(flops=1, bytes_accessed=1, transcendentals=0),
        )

        def wholes(arrays):
            return [whole(*t.shape) for t in arrays]

        def terms_of(j, token):
            stream, tiles = streams[j], FFN_TILES[j]
            at = sum(FFN_TILES[:j]) * LANES
            factors = (*n2_df_rows, near, far_b if j == 0 else late_b)
            dims = (n_dp // 2, 3 * width // n_dp * tiles, LANES)
            both = 2 * RECURSIONS * seq_len
            keep, send = pl.pallas_call(
                functools.partial(ffn_terms, stream.split(), tiles, at, 0 if j == 0 else at - first_part),
                in_specs=[anywhere] * (len(factors) + 1),
                out_specs=[whole(*dims)] * 2,
                out_shape=[shape(*dims)] * 2,
                scratch_shapes=[pltpu.VMEM((2, both, width), BF), *[pltpu.VMEM((both, n * tiles * LANES), BF) for n in (2, 1)],
                                pltpu.VMEM((3 * width * tiles, LANES), F32), pltpu.SemaphoreType.DMA((10,))],
                name=f"ffn_terms_{j}",
                **common,
            )(*factors, token)
            stream.sent(keep, send, n_dp)
            return keep

        def fold_streams(group, token, small_own):
            folds, operands, outs = [], [], []
            for stream in group:
                count, rows, _ = stream.kept.shape
                held = (count // 2, rows, LANES)
                operands += [stream.kept, stream.got]
                if stream is attn_stream:
                    operands.append(small_own)
                    outs += [shape(*held), shape(count // 2 * rows + 2 * SMALL, LANES), shape(SMALL, LANES, dtype=F32)]
                    folds.append((functools.partial(fold_small, stream.split()), 3, 3))
                else:
                    outs += [shape(*held), shape(*held)]
                    folds.append((functools.partial(fold, stream.split()), 2, 2))
            results = pl.pallas_call(
                functools.partial(fold_group, folds),
                in_specs=[*wholes(operands), anywhere],
                out_specs=wholes(outs),
                out_shape=outs,
                name="fold_terms",
                **common,
            )(*operands, token)
            token = results[0]
            for stream, (_, _, n_out) in zip(group, folds):
                stream.sent(results[0], results[1], n_dp)
                small_own = results[2] if n_out == 3 else small_own
                results = results[n_out:]
            return token, small_own

        du, grad_state, small = run_last(small)
        late, du, small = lax.optimization_barrier((late, du, small))
        late_b, du_b = rows_of(swap_mp(late)), rows_of(swap_mp(du))
        token, small_own = small, None
        for item in SCHEDULE:
            if item[0] == "T":
                token = terms_of(int(item[1:]), token)
                if item == "T0":
                    o_da, token = lax.optimization_barrier((o_da, token))
                    o_da_b = rows_of(swap_mp(o_da))
            elif item == "A":
                dims = (n_dp // 2, tiled, LANES)
                operands = (rows_of(n1), n1_b, rows_of(du), du_b, rows_of(o_da), o_da_b, small)
                outs = (shape(*dims), shape(n_dp // 2 * tiled + 2 * SMALL, LANES), shape(SMALL, LANES, dtype=F32))
                keep, send, small_own = pl.pallas_call(
                    functools.partial(attn_terms, attn_stream.split(), depth),
                    in_specs=[*[anywhere] * 6, *wholes(operands[6:]), anywhere],
                    out_specs=wholes(outs),
                    out_shape=outs,
                    scratch_shapes=[pltpu.VMEM((2, 2 * RECURSIONS * seq_len, width), BF),
                                    *[pltpu.VMEM((2 * RECURSIONS * seq_len, t.shape[-1]), BF) for t in (du, o_da)],
                                    pltpu.VMEM((width, 2 * RECURSIONS * seq_len), BF),
                                    pltpu.VMEM((width // 2, 2 * RECURSIONS * seq_len), BF),
                                    pltpu.VMEM((-(-du.shape[-1] // PART) * 2, width // 2, LANES), F32),
                                    pltpu.VMEM((n_dp * depth + tiled - depth, LANES), F32), pltpu.VMEM((SMALL, LANES), F32),
                                    pltpu.SemaphoreType.DMA((8,))],
                    name="attn_terms",
                    **common,
                )(*operands, token)
                attn_stream.sent(keep, send, n_dp)
                token = small_own
            else:
                group = [attn_stream if name == "A0" else streams[int(name[1:])] for name in item.split()]
                token, small_own = fold_streams(group, token, small_own)
        attn_kept = attn_stream.kept.reshape(tiled, LANES)
        outs = (shape(SMALL, LANES, dtype=F32), shape(2 * SMALL, LANES))
        small_own, small_send = pl.pallas_call(
            finish_small,
            in_specs=[*wholes((attn_stream.got, small_own)), anywhere],
            out_specs=wholes(outs),
            out_shape=outs,
            name="finish_small",
            **common,
        )(attn_stream.got, small_own, token)
        operands = (attn_kept, attn_stream.got, small_own, swap_mp(small_send))
        outs = (shape(depth, LANES, dtype=F32), shape(1, width, dtype=F32), shape(1, width, dtype=F32),
                shape(RECURSIONS, width, dtype=F32))
        attn_flat, one, two, router = pl.pallas_call(
            finish_attn,
            in_specs=[*wholes(operands), anywhere],
            out_specs=wholes(outs),
            out_shape=outs,
            scratch_shapes=[pltpu.VMEM((SMALL, LANES), F32)],
            name="finish_attn",
            **common,
        )(*operands, small_own)
        ends = [t.reshape(t.shape[-2:]) for stream in streams for t in (stream.kept, stream.got)]
        ffn_rows = (3 * width // n_dp * sum(FFN_TILES), LANES)
        ffn_flat = pl.pallas_call(
            functools.partial(finish_ffn, FFN_TILES),
            in_specs=[*wholes(ends), anywhere],
            out_specs=whole(*ffn_rows),
            out_shape=shape(*ffn_rows, dtype=F32),
            scratch_shapes=[pltpu.VMEM((3 * width // n_dp * max(FFN_TILES), LANES), F32)],
            name="finish_ffn",
            **common,
        )(*ends, attn_flat)
        return (state, grad_state, attn_flat.reshape(-1), ffn_flat.reshape(1, -1), one.reshape(-1), two.reshape(-1), router)

    du, grad_state, small = run_last(small)
    two, feed = rows_of(n2_df)
    o, d_attn = rows_of(o_da)
    far = jnp.concatenate([far, late], axis=-1)
    sides = [[t[i] for i in (1, 2, 0)] for t in (rows_of(near), rows_of(far))]

    def side_terms(side, columns):
        return jnp.concatenate(
            [
                contract_rows(left, sides[side][which][:, columns]).astype(BF)
                for which, left in enumerate((two, two, feed))
            ],
            axis=0,
        )

    orders = orders_of(bits)
    if 3 * width % n_dp == 0 and units % 1280 == 0:
        fifth = units // 5
        streams = [(orders[i], slice(j * fifth, (j + 1) * fifth)) for i, j in ((0, 0), (1, 1), (2, 2), (0, 3), (1, 4))]
        done = []
        for order, columns in streams:
            terms = side_terms(0, columns).astype(F32) + swap_mp(side_terms(1, columns)).astype(F32)
            done.append(halving(terms.astype(BF).reshape(n_dp, 3 * width // n_dp, fifth), order, n_dp, dp_index))
        ffn_flat = jnp.concatenate(done, axis=1).reshape(1, -1)
    else:
        terms = side_terms(0, slice(None)).astype(F32) + swap_mp(side_terms(1, slice(None))).astype(F32)
        terms = terms.astype(BF).reshape(n_dp, 3 * width * units // n_dp // 128, 128)
        ffn_flat = halving(terms, orders[0], n_dp, dp_index).reshape(1, -1)

    grad_qkv = contract_rows(rows_of(n1), rows_of(du)).astype(BF)
    grad_out = contract_rows(o, d_attn).astype(BF)
    attn = jnp.concatenate([grad_qkv.reshape(-1), grad_out.reshape(-1)]).reshape(n_dp, 2, share // 128, 128)
    keep = jnp.where(mp_index == 0, attn[:, 0], attn[:, 1])
    send = jnp.where(mp_index == 0, attn[:, 1], attn[:, 0])
    attn = (keep.astype(F32) + swap_mp(send).astype(F32)).astype(BF)
    cuts = [0, (share // 128) // 24 * 8, (share // 128) // 12 * 8, share // 128]
    attn_flat = jnp.concatenate(
        [halving(attn[:, a:b], order, n_dp, dp_index) for a, b, order in zip(cuts, cuts[1:], orders)], axis=0
    ).reshape(-1)

    small = small + swap_mp(small)
    for bit in range(bits):
        small = small + swap_dp(small, bit, n_dp)
    return (state, grad_state, attn_flat, ffn_flat, small[0], small[1], small[2 : 2 + RECURSIONS])


def solution(mesh):
    both = P(("dp", "mp"), None)
    in_specs = (
        both,
        both,
        both,
        both,
        both,
        both,
        P(),
        P(),
        P(None, "mp"),
        P(None, "mp"),
        P(None, "mp"),
        P(),
        P(),
        P(),
        both,
    )
    out_specs = (both, both, P(("dp", "mp")), P("mp", "dp"), P(), P(), P())
    return jax.shard_map(
        on_device, mesh=mesh, in_specs=in_specs, out_specs=out_specs, check_vma=False
    )
```

```python
import functools
import math

import jax
import jax.numpy as jnp
import numpy as np
from jax import lax
from jax.experimental import pallas as pl
from jax.experimental.pallas import tpu as pltpu
from jax.sharding import PartitionSpec as P

HEADS = 15
KV_HEADS = 5
HEAD_DIM = 64
RECURSIONS = 3
GROUPS = HEADS // KV_HEADS
EPS = 1e-05
BF = jnp.bfloat16
F32 = jnp.float32


LANES = 128
CHUNKS = -(-HEADS * HEAD_DIM // LANES)
ROWS = 192
BLOCK = 256
MIB = 1 << 20
VMEM_BYTES = 64 * MIB - 65536


def rotary_tables(seq_len):
    half = HEAD_DIM // 2
    frequency = np.float32(100000.0) ** (
        np.float32(-2.0) * np.arange(half, dtype=np.float32) / np.float32(HEAD_DIM)
    )
    angles = np.arange(seq_len, dtype=np.float32)[:, None] * frequency.astype(np.float32)
    cosine, sine = np.cos(angles), np.sin(angles)
    return (
        jnp.asarray(np.concatenate([cosine] * 4, axis=1), F32),
        jnp.asarray(np.concatenate([-sine, sine] * 2, axis=1), F32),
    )


def contract_rows(left, right):
    return lax.dot_general(left, right, (((0,), (0,)), ((), ())), preferred_element_type=F32)


def contract_last(left, right):
    return lax.dot_general(left, right, (((1,), (1,)), ((), ())), preferred_element_type=F32)


def plain(left, right):
    return jnp.dot(left, right, preferred_element_type=F32)


def inverse_rms(rows):
    return lax.rsqrt(jnp.mean(rows * rows, axis=-1, keepdims=True) + EPS)


def norm_back(rows, gain, d_out):
    inv = inverse_rms(rows)
    scaled = d_out * gain
    inner = jnp.mean(scaled * rows, axis=-1, keepdims=True)
    d_rows = inv * scaled - rows * (inv * inv * inv * inner)
    return d_rows, jnp.sum(d_out * rows * inv, axis=0, keepdims=True)


def lane_of(rows):
    return lax.broadcasted_iota(jnp.int32, (rows, LANES), 1)


def swapped(chunk):
    first = lane_of(chunk.shape[0]) % HEAD_DIM < HEAD_DIM // 2
    return jnp.where(first, pltpu.roll(chunk, LANES - 32, 1), pltpu.roll(chunk, 32, 1))


def other_half(chunk):
    return pltpu.roll(chunk, HEAD_DIM, 1)


def over_rows(count, body):
    def lap(i, carry):
        body(pl.ds(pl.multiple_of(i * ROWS, ROWS), ROWS))
        return carry

    lax.fori_loop(0, count // ROWS, lap, 0)


def attention_forward(x_ref, bias_ref, cos_ref, sin_ref, gain, qkv_w, n1_ref, q_ref, kz_ref, vz_ref, p_ref, o_ref):
    seq_len, width = x_ref.shape
    scale = 1.0 / math.sqrt(HEAD_DIM)

    def norm(rows):
        x = x_ref[rows, :]
        n1_ref[rows, :] = (x * inverse_rms(x) * gain).astype(BF)

    over_rows(seq_len, norm)
    lower = lane_of(seq_len) < HEAD_DIM
    n1 = n1_ref[...]

    def spread(ref, head, chunk, upper):
        flipped = other_half(chunk)
        here, there = (flipped, chunk) if upper else (chunk, flipped)
        ref[2 * head] = jnp.where(lower, here, 0.0).astype(BF)
        ref[2 * head + 1] = jnp.where(lower, 0.0, there).astype(BF)

    columns = qkv_w.shape[1]
    for start in range(0, columns, 2 * LANES):
        wide = plain(n1, qkv_w[:, start : min(start + 2 * LANES, columns)])
        for part in range(0, wide.shape[1], LANES):
            chunk = wide[:, part : part + LANES]
            if chunk.shape[1] < LANES:
                chunk = jnp.concatenate([chunk, jnp.zeros_like(chunk)], axis=1)
            at = (start + part) // LANES
            heads = (2 * at, 2 * at + 1)
            if heads[0] < HEADS + KV_HEADS:
                chunk = chunk * cos_ref[...] + swapped(chunk) * sin_ref[...]
                if heads[0] < HEADS:
                    q_ref[:, at * LANES : (at + 1) * LANES] = chunk.astype(BF)
            for upper, head in enumerate(heads):
                if HEADS <= head < HEADS + KV_HEADS:
                    spread(kz_ref, head - HEADS, chunk, upper)
                elif HEADS + KV_HEADS <= head < HEADS + 2 * KV_HEADS:
                    spread(vz_ref, head - HEADS - KV_HEADS, chunk, upper)

    for at in range(CHUNKS):
        query = q_ref[:, at * LANES : (at + 1) * LANES]
        total = None
        for upper in range(2):
            head = 2 * at + upper
            if head < HEADS:
                key = 2 * (head // GROUPS) + upper
                scores = contract_last(query, kz_ref[key]) * scale + bias_ref[...]
                top = jnp.max(scores, axis=-1, keepdims=True)
                exponent = jnp.exp(scores - top)
                share = pl.reciprocal(jnp.sum(exponent, axis=-1, keepdims=True))
                attend = (exponent * share).astype(BF)
                p_ref[head] = attend
                mixed = plain(attend, vz_ref[key])
                total = mixed if total is None else total + mixed
        stop = min(width, (at + 1) * LANES)
        o_ref[:, at * LANES : stop] = total[:, : stop - at * LANES].astype(BF)


def attention_out(x_ref, o_ref, out_w, gain, attn_ref, n2_ref):
    attn_ref[...] = plain(o_ref[...], out_w[...])

    def norm(rows):
        after = x_ref[rows, :] + attn_ref[rows, :]
        n2_ref[rows, :] = (after * inverse_rms(after) * gain).astype(BF)

    over_rows(x_ref.shape[0], norm)


def feed_side(n2_ref, weights, results, ready):
    n2 = n2_ref[...]
    gate_w, up_w, down_w = weights
    m_ref, slope_ref, silu_ref = results
    ready(0, 1)
    for start in range(0, gate_w.shape[1], BLOCK):
        at = slice(start, start + BLOCK)
        g, u = plain(n2, gate_w[:, at]), plain(n2, up_w[:, at])
        s = jax.nn.sigmoid(g)
        silu = g * s
        m_ref[:, at] = (silu * u).astype(BF)
        slope_ref[:, at] = (u * s * (1.0 + g * (1.0 - s))).astype(BF)
        silu_ref[:, at] = silu.astype(BF)
    ready(2)
    return contract_last(m_ref[...], down_w[...])


def feed_backward(df_ref, sides, d_two_ref, ready):
    d_feed = df_ref[...]
    for side, (gate_w, up_w, down_w, slope_ref, silu_ref, dg_ref, du_ref) in enumerate(sides):
        ready(3 * side)
        for start in range(0, gate_w.shape[1], BLOCK):
            at = slice(start, start + BLOCK)
            d_hidden = plain(d_feed, down_w[:, at])
            dg_ref[:, at] = (d_hidden * slope_ref[:, at].astype(F32)).astype(BF)
            du_ref[:, at] = (d_hidden * silu_ref[:, at].astype(F32)).astype(BF)
        ready(3 * side + 1, 3 * side + 2)
        part = contract_last(dg_ref[...], gate_w[...]) + contract_last(du_ref[...], up_w[...])
        d_two_ref[...] = part if side == 0 else d_two_ref[...] + part


def attention_backward(d_attn_ref, out_w, qkv_w, cos_ref, sin_ref, q_ref, kz_ref, vz_ref, p_ref, do_ref, du_ref):
    seq_len, width = d_attn_ref.shape
    scale = 1.0 / math.sqrt(HEAD_DIM)
    do_ref[:, :width] = contract_last(d_attn_ref[...], out_w[...]).astype(BF)
    do_ref[:, width:] = jnp.zeros((seq_len, do_ref.shape[1] - width), BF)
    lower = lane_of(seq_len) < HEAD_DIM
    cosine, sine = cos_ref[...], sin_ref[...]

    def back(chunk):
        chunk = chunk * scale
        return chunk * cosine - swapped(chunk) * sine

    waiting, d_k, d_v = None, {}, {}
    for at in range(CHUNKS):
        query, d_mixed = (ref[:, at * LANES : (at + 1) * LANES] for ref in (q_ref, do_ref))
        query_t, d_mixed_t = query.T, d_mixed.T
        d_query = None
        for upper in range(2):
            head = 2 * at + upper
            if head >= HEADS:
                continue
            group = head // GROUPS
            key = 2 * group + upper
            rows = slice(upper * HEAD_DIM, (upper + 1) * HEAD_DIM)
            attend = p_ref[head]
            d_attend = contract_last(d_mixed, vz_ref[key])
            soft = attend.astype(F32)
            weighted = soft * d_attend
            inner = jnp.sum(weighted, axis=-1, keepdims=True)
            d_scores = (weighted - soft * inner).astype(BF)
            part = plain(d_scores, kz_ref[key])
            d_query = part if d_query is None else d_query + part
            for store, term in ((d_k, plain(query_t[rows], d_scores)), (d_v, plain(d_mixed_t[rows], attend))):
                store[group] = term if group not in store else store[group] + term
        if at < CHUNKS - 1:
            du_ref[:, at * LANES : (at + 1) * LANES] = back(d_query).astype(BF)
        else:
            waiting = d_query

    def two_heads(store, first, second):
        return jnp.concatenate([store[first], store[second]], axis=0).T

    tail = jnp.where(lower, waiting, two_heads(d_k, 0, 0))
    du_ref[:, (CHUNKS - 1) * LANES : CHUNKS * LANES] = back(tail).astype(BF)
    for i in range(2):
        at = CHUNKS + i
        du_ref[:, at * LANES : (at + 1) * LANES] = back(two_heads(d_k, 1 + 2 * i, 2 + 2 * i)).astype(BF)
        at = CHUNKS + 2 + i
        du_ref[:, at * LANES : (at + 1) * LANES] = two_heads(d_v, 2 * i, 2 * i + 1).astype(BF)
    at = CHUNKS + 4
    du_ref[:, at * LANES :] = two_heads(d_v, 4, 4)[:, : du_ref.shape[1] - at * LANES].astype(BF)


def router_gate(x, router_row):
    return jax.nn.sigmoid(jnp.sum(x * router_row, axis=-1, keepdims=True))


def masks(select_refs, segment_ref, pad_ref, bias_ref, active_ref):
    seq_len = segment_ref.shape[1]
    square = (seq_len, seq_len)
    query, key = (lax.broadcasted_iota(jnp.int32, square, axis) for axis in (0, 1))
    diagonal = query == key
    segment = segment_ref[...].astype(F32)
    own = jnp.sum(jnp.where(diagonal, segment, 0.0), axis=1, keepdims=True)
    near = (key <= query) & (segment == own)
    real = pad_ref[...] == 1
    for recursion, ref in enumerate(select_refs):
        place = lax.broadcasted_iota(jnp.int32, (seq_len, ref.shape[1]), 0)
        active = jnp.max(jnp.where(ref[...] == place, 1.0, 0.0), axis=1, keepdims=True)
        active_ref[recursion] = active
        along = jnp.sum(jnp.where(diagonal, active, 0.0), axis=0, keepdims=True)
        usable = (along > 0.0) & real
        bias_ref[recursion] = jnp.where(near & (usable | diagonal), 0.0, -1e30)


def first_attention(x_ref, sel_one, sel_two, sel_three, segment_ref, pad_ref, cos_ref, sin_ref, gain_one, gain_two, qkv_w, out_w,
                    gate_hbm, up_hbm, down_hbm, n1_ref, q_ref, kz_ref, vz_ref, p_ref, o_ref, attn_ref, n2_ref, bias_ref, active_ref,
                    m_ref, slope_ref, silu_ref, f_ref, gate_w, up_w, down_w, sems):
    copies = load_all([(gate_hbm, gate_w), (up_hbm, up_w), (down_hbm, down_w)], sems)
    for copy in copies:
        copy.start()
    n1, o = n1_ref.at[0], o_ref.at[0, 0]
    masks((sel_one, sel_two, sel_three), segment_ref, pad_ref, bias_ref, active_ref)
    attention_forward(x_ref, bias_ref.at[0], cos_ref, sin_ref, gain_one[...], qkv_w, n1, q_ref, kz_ref, vz_ref, p_ref, o)
    attention_out(x_ref, o, out_w, gain_two[...], attn_ref, n2_ref)

    def ready(*which):
        for i in which:
            copies[i].wait()

    f_ref[...] = feed_side(n2_ref, (gate_w, up_w, down_w), (m_ref.at[0, 0], slope_ref, silu_ref), ready)


def load_all(pairs, sems):
    return [pltpu.make_async_copy(src, dst, sems.at[i]) for i, (src, dst) in enumerate(pairs)]


def waits_at(condition, copies):
    def ready(*which):
        @pl.when(condition)
        def _():
            for i in which:
                copies[i].wait()

    return ready


def finish_attention_backward(x_ref, gain, active_ref, du_ref, qkv_w, base, state, total, out_ref):
    total[...] = contract_last(du_ref[...], qkv_w[...])
    terms = jnp.zeros((1, state.shape[1]), F32)

    def lap(i, terms):
        rows = pl.ds(pl.multiple_of(i * ROWS, ROWS), ROWS)
        d_rows, term = norm_back(x_ref[rows, :], gain, total[rows, :])
        new = jnp.where(active_ref[rows, :] > 0, base[rows, :] + d_rows, state[rows, :])
        out_ref[rows, :] = new
        return terms + term

    return lax.fori_loop(0, state.shape[0] // ROWS, lap, terms)


def all_steps(bias_ref, active_ref, router_ref, cos_ref, sin_ref, gain_one, gain_two,
              hidden_hbm, d_hidden_hbm, attn0_hbm, n20_hbm, slope_hbm, silu_hbm, f_hbm, n1_in, o_da_in, near_in,
              qkv_hbm, out_hbm, *rest):
    feed_hbm, rest = rest[:6], rest[6:]
    (n1_out, o_da_out, n2_df_out, near_out, far_out, late_out, du_out, final_out, base_ref, state_ref, small_ref), rest = rest[:11], rest[11:]
    qkv_w, out_w, *feed_w = rest[:8]
    (xs, attns, fs, slope0, slope1, silu0, silu1, qs, kzs, vzs, ps, n1, o, n2, m0, m1, df, dg0, dg1, dw0, dw1, da, du,
     total, d_branch, do_ref, load_sems, out_sems) = rest[8:]
    width = state_ref.shape[1]
    first_part = far_out.shape[3]
    laps = state_ref.shape[0] // ROWS
    loads = load_all(
        [*zip(feed_hbm, feed_w), (qkv_hbm, qkv_w), (out_hbm, out_w),
         (n20_hbm, n2), (attn0_hbm, attns.at[0]), (hidden_hbm, xs.at[0]), (d_hidden_hbm, state_ref),
         (f_hbm, total), (slope_hbm, slope0.at[0]), (silu_hbm, silu0.at[0])], load_sems)
    for i in (8, 3, 4, 5, 12, 9, 10, 6, 7, 0, 1, 2, 13, 14, 11):
        loads[i].start()
    loads[8].wait()

    places = dict(n2=[(n2, n2_df_out.at[0])], m0=[(m0, near_out.at[0])], n1=[(n1, n1_out)], o=[(o, o_da_out.at[0])],
                  df=[(df, n2_df_out.at[1])], dg0=[(dg0, near_out.at[1])], dw0=[(dw0, near_out.at[2])],
                  da=[(da, o_da_out.at[1])], du=[(du, du_out)])
    for i, (name, ref) in enumerate((("m1", m1), ("dg1", dg1), ("dw1", dw1))):
        places[name] = [(ref.at[:, :first_part], far_out.at[i]), (ref.at[:, first_part:], late_out.at[i])]
    numbers = {}
    for pairs in places.values():
        for source, target in pairs:
            numbers[id(target)] = len(numbers)

    def leaving(recursion, names):
        return [pltpu.make_async_copy(source, target.at[recursion], out_sems.at[numbers[id(target)]])
                for name in names for source, target in places[name]]

    def start(recursion, *names):
        for copy in leaving(recursion, names):
            copy.start()

    def wait(recursion, *names):
        for copy in leaving(recursion, names):
            copy.wait()

    def forward(r, carry):
        ready, later = (waits_at(r == step, loads) for step in range(2))
        start(r, "n2")

        @pl.when(r > 0)
        def _():
            @pl.when(r > 1)
            def _():
                wait(r - 1, "m0")

            total[...] = feed_side(n2, feed_w[:3], (m0, slope0.at[r], silu0.at[r]), later)
            start(r, "m0")
            wait(r - 1, "m1")

        part = feed_side(n2, feed_w[3:], (m1, slope1.at[r], silu1.at[r]), lambda *which: ready(*[3 + i for i in which]))
        ready(12)
        total[...] = total[...] + part
        start(r, "m1")
        ready(9, 10)
        router_row = router_ref[pl.ds(r, 1), :]

        def finish(rows):
            x = xs[r, rows, :]
            f = total[rows, :].astype(BF)
            fs[r, rows, :] = f
            branch = attns[r, rows, :] + f.astype(F32)
            xs[r + 1, rows, :] = jnp.where(active_ref[r, rows, :] > 0, x + router_gate(x, router_row) * branch, x)

        over_rows(total.shape[0], finish)
        ready(6, 7)
        wait(r, "n2")

        @pl.when(r < RECURSIONS - 1)
        def _():
            @pl.when(r > 0)
            def _():
                wait(r, "n1", "o")

            attention_forward(xs.at[r + 1], bias_ref.at[r + 1], cos_ref, sin_ref, gain_one[...], qkv_w,
                              n1, qs.at[r], kzs.at[r], vzs.at[r], ps.at[r], o)
            start(r + 1, "n1", "o")
            attention_out(xs.at[r + 1], o, out_w, gain_two[...], attns.at[r + 1], n2)

        return carry

    lax.fori_loop(0, RECURSIONS, forward, 0)
    final = pltpu.make_async_copy(xs.at[RECURSIONS], final_out, out_sems.at[15])
    final.start()
    for i in (11, 13, 14):
        loads[i].wait()
    small_ref[...] = jnp.zeros(small_ref.shape, F32)

    def backward(i, carry):
        r = RECURSIONS - 1 - i
        router_row = router_ref[pl.ds(r, 1), :]

        @pl.when(i > 0)
        def _():
            wait(r + 1, "df", "dg0", "dg1", "dw0", "dw1", "da")

        def enter(lap, terms):
            rows = pl.ds(pl.multiple_of(lap * ROWS, ROWS), ROWS)
            x = xs[r, rows, :]
            d_new = jnp.where(active_ref[r, rows, :] > 0, state_ref[rows, :], 0.0)
            gate = router_gate(x, router_row)
            branch = attns[r, rows, :] + fs[r, rows, :].astype(F32)
            d_gate = jnp.sum(d_new * branch, axis=-1, keepdims=True)
            d_logit = d_gate * gate * (1.0 - gate)
            spread = gate * d_new
            d_branch[rows, :] = spread
            df[rows, :] = spread.astype(BF)
            base_ref[rows, :] = d_new + d_logit * router_row
            return terms + jnp.sum(d_logit * x, axis=0, keepdims=True)

        small_ref[pl.ds(2 + r, 1), :] = lax.fori_loop(0, laps, enter, jnp.zeros((1, width), F32))
        start(r, "df")
        feed_backward(df, ((*feed_w[:3], slope0.at[r], silu0.at[r], dg0, dw0), (*feed_w[3:], slope1.at[r], silu1.at[r], dg1, dw1)),
                      total, lambda *which: None)
        start(r, "dg0", "dg1", "dw0", "dw1")

        def leave(lap, terms):
            rows = pl.ds(pl.multiple_of(lap * ROWS, ROWS), ROWS)
            after = xs[r, rows, :] + attns[r, rows, :]
            d_after, term = norm_back(after, gain_two[...], total[rows, :].astype(BF).astype(F32))
            da[rows, :] = (d_branch[rows, :] + d_after).astype(BF)
            base_ref[rows, :] = base_ref[rows, :] + d_after
            return terms + term

        small_ref[1:2, :] = small_ref[1:2, :] + lax.fori_loop(0, laps, leave, jnp.zeros((1, width), F32))
        start(r, "da")

        @pl.when(r > 0)
        def _():
            @pl.when(i > 0)
            def _():
                wait(r + 1, "du")

            attention_backward(da, out_w, qkv_w, cos_ref, sin_ref, qs.at[r - 1], kzs.at[r - 1], vzs.at[r - 1], ps.at[r - 1], do_ref, du)
            start(r, "du")
            term = finish_attention_backward(xs.at[r], gain_one[...], active_ref.at[r], du, qkv_w, base_ref, state_ref, total, state_ref)
            small_ref[0:1, :] = small_ref[0:1, :] + term

        return carry

    lax.fori_loop(0, RECURSIONS, backward, 0)
    wait(RECURSIONS - 1, "m0", "m1", "n1", "o")
    wait(0, "df", "dg0", "dg1", "dw0", "dw1", "da")
    wait(1, "du")
    final.wait()


def last_attention(active_ref, cos_ref, sin_ref, gain_one, q_ref, kz_ref, vz_ref, p_ref, d_attn_ref, small_in, out_w,
                   x_hbm, base_hbm, state_hbm, qkv_hbm, du_in, token, du_ref, d_input_ref, small_ref,
                   do_ref, total, x, base, state, qkv_w, sems):
    copies = load_all([(qkv_hbm, qkv_w), (x_hbm, x), (base_hbm, base), (state_hbm, state)], sems)
    for copy in copies:
        copy.start()
    attention_backward(d_attn_ref.at[0, 0], out_w, qkv_w, cos_ref, sin_ref, q_ref, kz_ref, vz_ref, p_ref, do_ref, du_ref.at[0])
    for copy in copies:
        copy.wait()
    term = finish_attention_backward(x, gain_one[...], active_ref.at[0], du_ref.at[0], qkv_w, base, state, total, d_input_ref)
    small_ref[...] = small_in[...]
    small_ref[0:1, :] = small_in[0:1, :] + term


def swap_dp(values_in, bit, n_dp):
    return lax.ppermute(values_in, "dp", [(i, i ^ (1 << bit)) for i in range(n_dp)])


def swap_mp(values_in):
    return lax.ppermute(values_in, "mp", [(0, 1), (1, 0)])


def halving(parts, order, n_dp, index):
    bits = n_dp.bit_length() - 1
    left = list(range(bits - 1, -1, -1))
    shape = parts.shape[1:]
    held = parts.reshape((2,) * bits + shape)
    for step, bit in enumerate(order):
        at = left.index(bit)
        upper = ((index >> bit) & 1) == 1
        low = lax.index_in_dim(held, 0, at, keepdims=False)
        high = lax.index_in_dim(held, 1, at, keepdims=False)
        keep, send = jnp.where(upper, high, low), jnp.where(upper, low, high)
        got = swap_dp(send, bit, n_dp)
        last = step == bits - 1
        total = keep.astype(F32) + got.astype(F32)
        held = total if last else total.astype(BF)
        left.remove(bit)
    return held


def orders_of(bits):
    rest = list(range(3, bits))
    if bits < 3:
        return [list(range(bits))] * 3
    return [[0, 1, 2] + rest, [1, 0, 2] + rest, [2, 0, 1] + rest]


PART = 2 * LANES
FFN_TILES = (4, 4, 2)
FFN_ORDERS = (((1, 2, 0, 3), (2, 1, 0, 3)), ((1, 3, 0, 2), (0, 1, 3, 2)), ((0, 1, 2, 3), (1, 0, 2, 3)))
ATTN_ORDER = ((0, 2, 1, 3), (2, 0, 1, 3))
SCHEDULE = (
    "T0", "T1", "A", "T2",
    "F0", "F1", "A0", "F2",
    "F0", "F1", "A0", "F2",
    "A0", "F0 F1", "F2",
)
SMALL = 64


def of_core(pair):
    first, second = pair
    return first if first == second else jnp.where(lax.axis_index("mp") == 0, first, second)


def halves(bits, places, count):
    mine = (lax.axis_index("dp") >> of_core(bits)) & 1
    place = of_core(places)
    for i in range(count):
        base = ((i >> place) << (place + 1)) | (i & ((1 << place) - 1))
        yield i, base | (mine << place), base | ((1 - mine) << place)


def stacked_copies(pairs, sems):
    flat_pairs = []
    for sources, target in pairs:
        rows = target.shape[0] // 2
        flat_pairs += [(source, target.at[pl.ds(i * rows, rows)]) for i, source in enumerate(sources)]
    copies = load_all(flat_pairs, sems)
    for copy in copies:
        copy.start()
    return [copies[i : i + 2] for i in range(0, len(copies), 2)]


def ffn_terms(split, tiles, at, at_b, n2_df_a, n2_df_b, units_a, units_b, token, keep_ref, send_ref, left, gate_up, down, flat, sems):
    width, part = left.shape[2], down.shape[1]
    columns, columns_b = (pl.ds(start, tiles * LANES) for start in (at, at_b))
    lefts = [(n2_df_a.at[i], n2_df_b.at[i]) for i in range(2)]
    m, dg, dw = [(units_a.at[i, :, columns], units_b.at[i, :, columns_b]) for i in range(3)]
    n2, dg, dw, df, m = stacked_copies(
        [(lefts[0], left.at[0]), (dg, gate_up.at[:, :part]), (dw, gate_up.at[:, part:]), (lefts[1], left.at[1]), (m, down)], sems)
    for which, (right, needed) in enumerate(((gate_up, n2 + dg + dw), (down, df + m))):
        for copy in needed:
            copy.wait()
        terms = contract_rows(left[which], right[...])
        for at_lane in range(0, right.shape[1], LANES):
            matrix, c = divmod(at_lane // LANES, tiles)
            start = tiles * width * (2 * which + matrix) + c
            flat[pl.ds(start, width, stride=tiles), :] = terms[:, at_lane : at_lane + LANES]
    count, rows, _ = keep_ref.shape
    for i, kept, sent in halves(*split, count):
        for out, shard in ((keep_ref, kept), (send_ref, sent)):
            out[i] = flat[pl.ds(pl.multiple_of(shard * rows, 8), rows), :].astype(BF)


def small_rows(small, packed):
    packed[...] = jnp.zeros(packed.shape, F32)
    width = small.shape[1]
    for i in range(2 + RECURSIONS):
        for c in range(CHUNKS):
            stop = min(width, (c + 1) * LANES)
            packed[i * CHUNKS + c : i * CHUNKS + c + 1, : stop - c * LANES] = small[i : i + 1, c * LANES : stop]
    return packed[...]


def split_small(small, ref, start):
    high = small.astype(BF)
    ref[start : start + SMALL, :] = high
    ref[start + SMALL : start + 2 * SMALL, :] = (small - high.astype(F32)).astype(BF)


def rounded_small(small):
    high = small.astype(BF)
    return high.astype(F32) + (small - high.astype(F32)).astype(BF).astype(F32)


def joined_small(ref, start):
    return ref[start : start + SMALL, :].astype(F32) + ref[start + SMALL : start + 2 * SMALL, :].astype(F32)


def attn_terms(split, depth, n1_a, n1_b, du_a, du_b, o_da_a, o_da_b, small, token,
               keep, send, small_out, left, du_rows, da_rows, turned, own, terms, flat, packed, sems):
    base, count = 0, own.shape[0] // 2
    lower = lane_of(count) < HEAD_DIM
    core = lax.axis_index("mp")
    n1, du, o, da = stacked_copies(
        [((n1_a, n1_b), left.at[0]), ((du_a, du_b), du_rows), ((o_da_a.at[0], o_da_b.at[0]), left.at[1]),
         ((o_da_a.at[1], o_da_b.at[1]), da_rows)], sems)
    for which, (right, needed) in enumerate(((du_rows, n1 + du), (da_rows, o + da))):
        for copy in needed:
            copy.wait()
        columns = right.shape[1]
        half = columns // LANES
        turned[...] = left[which].T
        group = depth * LANES // columns
        for i in range(own.shape[0] // group):
            own[i * group : (i + 1) * group, :] = turned[pl.ds(pl.multiple_of((2 * i + core) * group, 16), group), :]
        for start in range(0, columns, PART):
            stop = min(columns, start + PART)
            block = plain(own[...], right[:, start:stop])
            if stop - start < PART:
                block = jnp.concatenate([block, jnp.zeros((2 * count, PART - (stop - start)), F32)], axis=1)
            for part in range(0, stop - start, LANES):
                terms[(start + part) // LANES] = block[:, part : part + LANES]
        step = 2 * columns // LANES
        after = first_odd = None
        for c in range(half + 1):
            even = terms[c, pl.ds(0, count, stride=2), :]
            odd = other_half(terms[c, pl.ds(1, count, stride=2), :])
            if c < half:
                flat[pl.ds(base + c, count, stride=step), :] = even
            else:
                flat[pl.ds(base + c, count, stride=step), :] = jnp.where(lower, even, first_odd)
            if c == 0:
                first_odd = odd
            else:
                flat[pl.ds(base + half + c, count, stride=step), :] = jnp.where(lower, after, odd)
            after = odd
        base += 2 * count * columns // LANES
    total = rounded_small(small_rows(small, packed))
    small_out[...] = total
    shards, rows, _ = keep.shape
    split_small(total, send, shards * rows)

    def rows_of_shard(shard):
        return flat[pl.ds(pl.multiple_of(shard * depth, 8), rows), :].astype(BF)

    for i, kept, sent in halves(*split, shards):
        keep[i] = rows_of_shard(kept)
        send[i * rows : (i + 1) * rows, :] = rows_of_shard(sent)


def fold(split, kept, got, token, keep, send):
    for i, *shards in halves(*split, keep.shape[0]):
        for out, shard in zip((keep, send), shards):
            out[i] = (kept[shard].astype(F32) + got[shard].astype(F32)).astype(BF)


def fold_small(split, kept, got, small, token, keep, send, small_out):
    held, rows, _ = kept.shape
    for i, *shards in halves(*split, held // 2):
        totals = [(kept[shard].astype(F32) + got[pl.ds(pl.multiple_of(shard * rows, 16), rows), :].astype(F32)).astype(BF)
                  for shard in shards]
        keep[i] = totals[0]
        send[i * rows : (i + 1) * rows, :] = totals[1]
    total = rounded_small(small[...]) + joined_small(got, held * rows)
    small_out[...] = total
    split_small(total, send, held // 2 * rows)


def fold_group(folds, *refs):
    inputs, results = refs, refs[sum(n for _, n, _ in folds) + 1 :]
    token = refs[sum(n for _, n, _ in folds)]
    for function, n_in, n_out in folds:
        function(*inputs[:n_in], token, *results[:n_out])
        inputs, results = inputs[n_in:], results[n_out:]


def finish_small(got, small, token, total_ref, send):
    total = rounded_small(small[...]) + joined_small(got, got.shape[0] - 2 * SMALL)
    total_ref[...] = total
    split_small(total, send, 0)


def finish_attn(kept, got, small, far, token, attn_out, one_out, two_out, router_out, packed):
    padded = kept.shape[0]
    both = kept[...].astype(F32) + got[:padded, :].astype(F32)
    attn_out[...] = both[: attn_out.shape[0]]
    packed[...] = rounded_small(small[...]) + joined_small(far, 0)
    width = one_out.shape[1]
    outs = [(one_out, 0), (two_out, 0), *[(router_out, i) for i in range(RECURSIONS)]]
    for i, (out, row) in enumerate(outs):
        for c in range(CHUNKS):
            stop = min(width, (c + 1) * LANES)
            out[row : row + 1, c * LANES : stop] = packed[i * CHUNKS + c : i * CHUNKS + c + 1, : stop - c * LANES]


def finish_ffn(tiles, *refs):
    feeds, (_, ffn_out, flat) = refs[:-3], refs[-3:]
    every = sum(tiles)
    rows = ffn_out.shape[0] // every
    base = 0
    for i, wide in enumerate(tiles):
        flat[: rows * wide, :] = feeds[2 * i][...].astype(F32) + feeds[2 * i + 1][...].astype(F32)
        for c in range(wide):
            ffn_out[pl.ds(base + c, rows, stride=every), :] = flat[pl.ds(c, rows, stride=wide), :]
        base += wide


class Stream:
    def __init__(self, orders, bits):
        self.orders, self.left, self.done = orders, [list(range(bits - 1, -1, -1)) for _ in orders], 0
        self.kept = self.got = None

    def split(self):
        bits = tuple(order[self.done] for order in self.orders)
        return bits, tuple(len(left) - 1 - left.index(bit) for left, bit in zip(self.left, bits))

    def sent(self, kept, send, n_dp):
        bits = self.split()[0]
        pairs = [(2 * d + core, 2 * (d ^ (1 << bit)) + core) for d in range(n_dp) for core, bit in enumerate(bits)]
        self.kept, self.got = kept, lax.ppermute(send, ("dp", "mp"), pairs)
        for left, bit in zip(self.left, bits):
            left.remove(bit)
        self.done += 1


def on_device(
    hidden_in,
    sel_one,
    sel_two,
    sel_three,
    segment_ids,
    pad_mask,
    qkv_weight,
    out_weight,
    gate_weight,
    up_weight,
    down_weight,
    norm_one,
    norm_two,
    router_weight,
    d_hidden,
):
    seq_len, width = hidden_in.shape
    n_dp, n_mp = lax.axis_size("dp"), lax.axis_size("mp")
    dp_index, mp_index = lax.axis_index("dp"), lax.axis_index("mp")
    cosine, sine = rotary_tables(seq_len)
    weights = [(gate_weight, up_weight, down_weight)]
    weights.append(tuple(swap_mp(w) for w in weights[0]))
    gain_one, gain_two = norm_one.reshape(1, width), norm_two.reshape(1, width)
    padded = CHUNKS * LANES
    units = gate_weight.shape[1]
    feed_weights = (*weights[0], *weights[1])

    def shape(*dims, dtype=BF):
        return jax.ShapeDtypeStruct(dims, dtype)

    def whole(*dims, **kw):
        return pl.BlockSpec(dims, lambda *_: (0,) * len(dims), **kw)

    anywhere = pl.BlockSpec(memory_space=pl.ANY)
    one = pl.Buffered(1)
    stack = RECURSIONS, seq_len
    heads = (2 * KV_HEADS, seq_len, LANES)
    square = (HEADS, seq_len, seq_len)
    n1, q, kz, vz, p, o_da, attn, n2, bias, active, near, slope_first, silu_first, f_first = pl.pallas_call(
        first_attention,
        grid=(1,),
        in_specs=[
            whole(seq_len, width), *[whole(*ref.shape) for ref in (sel_one, sel_two, sel_three, segment_ids, pad_mask)],
            whole(seq_len, LANES), whole(seq_len, LANES), whole(1, width), whole(1, width), whole(*qkv_weight.shape), whole(*out_weight.shape),
            *[anywhere] * 3,
        ],
        out_specs=[
            whole(1, seq_len, width), whole(seq_len, padded), whole(*heads), whole(*heads), whole(*square),
            whole(1, 1, seq_len, width), whole(seq_len, width), whole(seq_len, width), whole(RECURSIONS, seq_len, seq_len), whole(*stack, 1),
            whole(1, 1, seq_len, units), whole(seq_len, units), whole(seq_len, units), whole(seq_len, width),
        ],
        out_shape=[
            shape(*stack, width), shape(seq_len, padded), shape(*heads), shape(*heads), shape(*square),
            shape(2, *stack, width), shape(seq_len, width, dtype=F32), shape(seq_len, width),
            shape(*stack, seq_len, dtype=F32), shape(*stack, 1, dtype=F32),
            shape(3, *stack, units), shape(seq_len, units), shape(seq_len, units), shape(seq_len, width, dtype=F32),
        ],
        scratch_shapes=[*[pltpu.VMEM(w.shape, BF) for w in weights[0]], pltpu.SemaphoreType.DMA((3,))],
        compiler_params=pltpu.CompilerParams(vmem_limit_bytes=VMEM_BYTES),
        cost_estimate=pl.CostEstimate(flops=2 * 10**9, bytes_accessed=12 * 10**6, transcendentals=600000),
        name="first_attention",
    )(hidden_in, sel_one, sel_two, sel_three, segment_ids, pad_mask, cosine, sine, gain_one, gain_two, qkv_weight, out_weight,
      *weights[0])
    attention_0 = (q, kz, vz, p)
    wide = qkv_weight.shape[1]
    row = (seq_len, width)
    kept = RECURSIONS - 1
    first_part = FFN_TILES[0] * LANES
    vm = pltpu.VMEM
    results = pl.pallas_call(
        all_steps,
        grid=(1,),
        in_specs=[
            whole(RECURSIONS, seq_len, seq_len), whole(RECURSIONS, seq_len, 1), whole(RECURSIONS, width),
            whole(seq_len, LANES), whole(seq_len, LANES), whole(1, width), whole(1, width), *[anywhere] * 18,
        ],
        out_specs=[*[anywhere] * 8, whole(*row), whole(*row), whole(8, width)],
        out_shape=[
            shape(*stack, width), *[shape(2, *stack, width)] * 2, shape(3, *stack, units), shape(3, *stack, first_part), shape(3, *stack, units - first_part), shape(*stack, wide),
            *[shape(*row, dtype=F32)] * 3, shape(8, width, dtype=F32),
        ],
        scratch_shapes=[
            *[vm(w.shape, BF) for w in (qkv_weight, out_weight, *feed_weights)],
            vm((RECURSIONS + 1, *row), F32), vm((RECURSIONS, *row), F32), vm((RECURSIONS, *row), BF),
            *[vm((*stack, units), BF)] * 4, vm((kept, seq_len, padded), BF), vm((kept, *heads), BF), vm((kept, *heads), BF),
            vm((kept, *square), BF), *[vm(row, BF)] * 3, *[vm((seq_len, units), BF)] * 2, vm(row, BF), *[vm((seq_len, units), BF)] * 4,
            vm(row, BF), vm((seq_len, wide), BF), vm(row, F32), vm(row, F32), vm((seq_len, padded), BF),
            pltpu.SemaphoreType.DMA((15,)), pltpu.SemaphoreType.DMA((16,)),
        ],
        input_output_aliases={14: 0, 15: 1, 16: 3},
        compiler_params=pltpu.CompilerParams(vmem_limit_bytes=VMEM_BYTES),
        cost_estimate=pl.CostEstimate(flops=23 * 10**9, bytes_accessed=50 * 10**6, transcendentals=4 * 10**6),
        name="all_steps",
    )(bias, active, router_weight, cosine, sine, gain_one, gain_two, hidden_in, d_hidden, attn, n2,
      slope_first, silu_first, f_first, n1, o_da, near,
      qkv_weight, out_weight, *feed_weights)
    n1, o_da, n2_df, near, far, late, du, state, base, grad_state, small = results

    def run_last(token):
        return pl.pallas_call(
            last_attention,
            grid=(1,),
            in_specs=[
                whole(1, seq_len, 1), whole(seq_len, LANES), whole(seq_len, LANES), whole(1, width),
                whole(seq_len, padded), whole(*heads), whole(*heads), whole(*square),
                pl.BlockSpec((1, 1, seq_len, width), lambda i: (1, 0, 0, 0)), whole(8, width), whole(*out_weight.shape), *[anywhere] * 6,
            ],
            out_specs=[whole(1, seq_len, qkv_weight.shape[1]), whole(seq_len, width), whole(8, width)],
            out_shape=[shape(*stack, qkv_weight.shape[1]), shape(seq_len, width, dtype=F32), shape(8, width, dtype=F32)],
            scratch_shapes=[
                pltpu.VMEM((seq_len, padded), BF), *[pltpu.VMEM((seq_len, width), F32)] * 4,
                pltpu.VMEM(qkv_weight.shape, BF), pltpu.SemaphoreType.DMA((4,)),
            ],
            input_output_aliases={15: 0},
            compiler_params=pltpu.CompilerParams(vmem_limit_bytes=VMEM_BYTES),
            cost_estimate=pl.CostEstimate(flops=1, bytes_accessed=1, transcendentals=0),
            name="last_attention",
        )(active, cosine, sine, gain_one, *attention_0, o_da, small, out_weight, hidden_in, base, grad_state, qkv_weight, du, token)

    def rows_of(stacked):
        return stacked.reshape(*stacked.shape[:-3], -1, stacked.shape[-1])

    bits = n_dp.bit_length() - 1
    share = (qkv_weight.size + out_weight.size) // (n_dp * n_mp)
    if bits == 4 and 3 * width % n_dp == 0 and units == sum(FFN_TILES) * LANES and share % (16 * qkv_weight.shape[1]) == share % (16 * width) == 0:
        n2_df_rows = [rows_of(t) for t in (n2_df, swap_mp(n2_df))]
        near, far_b = rows_of(near), rows_of(swap_mp(far))
        n1_b = rows_of(swap_mp(n1))
        streams = [Stream(order, bits) for order in FFN_ORDERS]
        attn_stream = Stream(ATTN_ORDER, bits)
        depth = share // LANES
        tiled = -(-depth // 16) * 16
        common = dict(
            grid=(1,),
            compiler_params=pltpu.CompilerParams(vmem_limit_bytes=VMEM_BYTES),
            cost_estimate=pl.CostEstimate(flops=1, bytes_accessed=1, transcendentals=0),
        )

        def wholes(arrays):
            return [whole(*t.shape) for t in arrays]

        def terms_of(j, token):
            stream, tiles = streams[j], FFN_TILES[j]
            at = sum(FFN_TILES[:j]) * LANES
            factors = (*n2_df_rows, near, far_b if j == 0 else late_b)
            dims = (n_dp // 2, 3 * width // n_dp * tiles, LANES)
            both = 2 * RECURSIONS * seq_len
            keep, send = pl.pallas_call(
                functools.partial(ffn_terms, stream.split(), tiles, at, 0 if j == 0 else at - first_part),
                in_specs=[anywhere] * (len(factors) + 1),
                out_specs=[whole(*dims)] * 2,
                out_shape=[shape(*dims)] * 2,
                scratch_shapes=[pltpu.VMEM((2, both, width), BF), *[pltpu.VMEM((both, n * tiles * LANES), BF) for n in (2, 1)],
                                pltpu.VMEM((3 * width * tiles, LANES), F32), pltpu.SemaphoreType.DMA((10,))],
                name=f"ffn_terms_{j}",
                **common,
            )(*factors, token)
            stream.sent(keep, send, n_dp)
            return keep

        def fold_streams(group, token, small_own):
            folds, operands, outs = [], [], []
            for stream in group:
                count, rows, _ = stream.kept.shape
                held = (count // 2, rows, LANES)
                operands += [stream.kept, stream.got]
                if stream is attn_stream:
                    operands.append(small_own)
                    outs += [shape(*held), shape(count // 2 * rows + 2 * SMALL, LANES), shape(SMALL, LANES, dtype=F32)]
                    folds.append((functools.partial(fold_small, stream.split()), 3, 3))
                else:
                    outs += [shape(*held), shape(*held)]
                    folds.append((functools.partial(fold, stream.split()), 2, 2))
            results = pl.pallas_call(
                functools.partial(fold_group, folds),
                in_specs=[*wholes(operands), anywhere],
                out_specs=wholes(outs),
                out_shape=outs,
                name="fold_terms",
                **common,
            )(*operands, token)
            token = results[0]
            for stream, (_, _, n_out) in zip(group, folds):
                stream.sent(results[0], results[1], n_dp)
                small_own = results[2] if n_out == 3 else small_own
                results = results[n_out:]
            return token, small_own

        du, grad_state, small = run_last(small)
        late, du, small = lax.optimization_barrier((late, du, small))
        late_b, du_b = rows_of(swap_mp(late)), rows_of(swap_mp(du))
        token, small_own = small, None
        for item in SCHEDULE:
            if item[0] == "T":
                token = terms_of(int(item[1:]), token)
                if item == "T0":
                    o_da, token = lax.optimization_barrier((o_da, token))
                    o_da_b = rows_of(swap_mp(o_da))
            elif item == "A":
                dims = (n_dp // 2, tiled, LANES)
                operands = (rows_of(n1), n1_b, rows_of(du), du_b, rows_of(o_da), o_da_b, small)
                outs = (shape(*dims), shape(n_dp // 2 * tiled + 2 * SMALL, LANES), shape(SMALL, LANES, dtype=F32))
                keep, send, small_own = pl.pallas_call(
                    functools.partial(attn_terms, attn_stream.split(), depth),
                    in_specs=[*[anywhere] * 6, *wholes(operands[6:]), anywhere],
                    out_specs=wholes(outs),
                    out_shape=outs,
                    scratch_shapes=[pltpu.VMEM((2, 2 * RECURSIONS * seq_len, width), BF),
                                    *[pltpu.VMEM((2 * RECURSIONS * seq_len, t.shape[-1]), BF) for t in (du, o_da)],
                                    pltpu.VMEM((width, 2 * RECURSIONS * seq_len), BF),
                                    pltpu.VMEM((width // 2, 2 * RECURSIONS * seq_len), BF),
                                    pltpu.VMEM((-(-du.shape[-1] // PART) * 2, width // 2, LANES), F32),
                                    pltpu.VMEM((n_dp * depth + tiled - depth, LANES), F32), pltpu.VMEM((SMALL, LANES), F32),
                                    pltpu.SemaphoreType.DMA((8,))],
                    name="attn_terms",
                    **common,
                )(*operands, token)
                attn_stream.sent(keep, send, n_dp)
                token = small_own
            else:
                group = [attn_stream if name == "A0" else streams[int(name[1:])] for name in item.split()]
                token, small_own = fold_streams(group, token, small_own)
        attn_kept = attn_stream.kept.reshape(tiled, LANES)
        outs = (shape(SMALL, LANES, dtype=F32), shape(2 * SMALL, LANES))
        small_own, small_send = pl.pallas_call(
            finish_small,
            in_specs=[*wholes((attn_stream.got, small_own)), anywhere],
            out_specs=wholes(outs),
            out_shape=outs,
            name="finish_small",
            **common,
        )(attn_stream.got, small_own, token)
        operands = (attn_kept, attn_stream.got, small_own, swap_mp(small_send))
        outs = (shape(depth, LANES, dtype=F32), shape(1, width, dtype=F32), shape(1, width, dtype=F32),
                shape(RECURSIONS, width, dtype=F32))
        attn_flat, one, two, router = pl.pallas_call(
            finish_attn,
            in_specs=[*wholes(operands), anywhere],
            out_specs=wholes(outs),
            out_shape=outs,
            scratch_shapes=[pltpu.VMEM((SMALL, LANES), F32)],
            name="finish_attn",
            **common,
        )(*operands, small_own)
        ends = [t.reshape(t.shape[-2:]) for stream in streams for t in (stream.kept, stream.got)]
        ffn_rows = (3 * width // n_dp * sum(FFN_TILES), LANES)
        ffn_flat = pl.pallas_call(
            functools.partial(finish_ffn, FFN_TILES),
            in_specs=[*wholes(ends), anywhere],
            out_specs=whole(*ffn_rows),
            out_shape=shape(*ffn_rows, dtype=F32),
            scratch_shapes=[pltpu.VMEM((3 * width // n_dp * max(FFN_TILES), LANES), F32)],
            name="finish_ffn",
            **common,
        )(*ends, attn_flat)
        return (state, grad_state, attn_flat.reshape(-1), ffn_flat.reshape(1, -1), one.reshape(-1), two.reshape(-1), router)

    du, grad_state, small = run_last(small)
    two, feed = rows_of(n2_df)
    o, d_attn = rows_of(o_da)
    far = jnp.concatenate([far, late], axis=-1)
    sides = [[t[i] for i in (1, 2, 0)] for t in (rows_of(near), rows_of(far))]

    def side_terms(side, columns):
        return jnp.concatenate(
            [
                contract_rows(left, sides[side][which][:, columns]).astype(BF)
                for which, left in enumerate((two, two, feed))
            ],
            axis=0,
        )

    orders = orders_of(bits)
    if 3 * width % n_dp == 0 and units % 1280 == 0:
        fifth = units // 5
        streams = [(orders[i], slice(j * fifth, (j + 1) * fifth)) for i, j in ((0, 0), (1, 1), (2, 2), (0, 3), (1, 4))]
        done = []
        for order, columns in streams:
            terms = side_terms(0, columns).astype(F32) + swap_mp(side_terms(1, columns)).astype(F32)
            done.append(halving(terms.astype(BF).reshape(n_dp, 3 * width // n_dp, fifth), order, n_dp, dp_index))
        ffn_flat = jnp.concatenate(done, axis=1).reshape(1, -1)
    else:
        terms = side_terms(0, slice(None)).astype(F32) + swap_mp(side_terms(1, slice(None))).astype(F32)
        terms = terms.astype(BF).reshape(n_dp, 3 * width * units // n_dp // 128, 128)
        ffn_flat = halving(terms, orders[0], n_dp, dp_index).reshape(1, -1)

    grad_qkv = contract_rows(rows_of(n1), rows_of(du)).astype(BF)
    grad_out = contract_rows(o, d_attn).astype(BF)
    attn = jnp.concatenate([grad_qkv.reshape(-1), grad_out.reshape(-1)]).reshape(n_dp, 2, share // 128, 128)
    keep = jnp.where(mp_index == 0, attn[:, 0], attn[:, 1])
    send = jnp.where(mp_index == 0, attn[:, 1], attn[:, 0])
    attn = (keep.astype(F32) + swap_mp(send).astype(F32)).astype(BF)
    cuts = [0, (share // 128) // 24 * 8, (share // 128) // 12 * 8, share // 128]
    attn_flat = jnp.concatenate(
        [halving(attn[:, a:b], order, n_dp, dp_index) for a, b, order in zip(cuts, cuts[1:], orders)], axis=0
    ).reshape(-1)

    small = small + swap_mp(small)
    for bit in range(bits):
        small = small + swap_dp(small, bit, n_dp)
    return (state, grad_state, attn_flat, ffn_flat, small[0], small[1], small[2 : 2 + RECURSIONS])


def solution(mesh):
    both = P(("dp", "mp"), None)
    in_specs = (
        both,
        both,
        both,
        both,
        both,
        both,
        P(),
        P(),
        P(None, "mp"),
        P(None, "mp"),
        P(None, "mp"),
        P(),
        P(),
        P(),
        both,
    )
    out_specs = (both, both, P(("dp", "mp")), P("mp", "dp"), P(), P(), P())
    return jax.shard_map(
        on_device, mesh=mesh, in_specs=in_specs, out_specs=out_specs, check_vma=False
    )
```
